32 devices in a mesh: dp: 8 (over z, y), ns: 4 (over x, core).
Axes of the slice: x: 2, y: 2, z: 4, core: 2. Of those that a mesh axis runs over, the one named last changes fastest.
Arguments:
- tokens: bfloat16 [65536, 384], P(('dp', 'ns')), may hold values from -6 to 6
- cotangent: bfloat16 [65536, 384], P(('dp', 'ns')), may hold values from -6 to 6
- segment: int32 [65536], P(('dp', 'ns')), may hold values from 0 to 109, as said below
- valid_rows: int32 [65536], P(('dp', 'ns')), may hold values from 0 to 1, as said below
- qkv_weight: float32 [1152, 384], P('ns', 'dp'), may hold values from -0.3125 to 0.3125
- proj_weight: float32 [384, 384], P('ns', 'dp'), may hold values from -0.875 to 0.875
- fc1_weight: float32 [1536, 384], P('ns', 'dp'), may hold values from -0.3125 to 0.3125
- fc2_weight: float32 [1536, 384], P('ns', 'dp'), may hold values from -0.15625 to 0.15625
- qkv_moment: float32 [1152, 384], P('ns', 'dp')
- proj_moment: float32 [384, 384], P('ns', 'dp')
- fc1_moment: float32 [1536, 384], P('ns', 'dp')
- fc2_moment: float32 [1536, 384], P('ns', 'dp')
- vectors: float32 [12, 384], P('ns', 'dp')
- vector_moment: float32 [12, 384], P('ns', 'dp')
- vector_square: float32 [12, 384], P('ns', 'dp'), may hold values from 32 to 524
Outputs:
- output: bfloat16 [65536, 384], P(('dp', 'ns'))
- input_grad: bfloat16 [65536, 384], P(('dp', 'ns'))
- qkv_new: float32 [1152, 384], P('ns', 'dp')
- proj_new: float32 [384, 384], P('ns', 'dp')
- fc1_new: float32 [1536, 384], P('ns', 'dp')
- fc2_new: float32 [1536, 384], P('ns', 'dp')
- qkv_moment_new: float32 [1152, 384], P('ns', 'dp')
- proj_moment_new: float32 [384, 384], P('ns', 'dp')
- fc1_moment_new: float32 [1536, 384], P('ns', 'dp')
- fc2_moment_new: float32 [1536, 384], P('ns', 'dp')
- vector_moment_new: float32 [12, 384], P('ns', 'dp')
- vector_square_new: float32 [12, 384], P('ns', 'dp')
- vectors_new: float32 [12, 384], P('ns', 'dp')
- qkv_copy: bfloat16 [1152, 384], P('ns', 'dp')
- proj_copy: bfloat16 [384, 384], P('ns', 'dp')
- fc1_copy: bfloat16 [1536, 384], P('ns', 'dp')
- fc2_copy: bfloat16 [1536, 384], P('ns', 'dp')
The draws below stay inside these ranges and needn't reach their ends.
Inputs may be any that keep to these rules, and one draw needn't show every extreme that they name: `segment`: each pack of 2048 rows holds whole images of 18 to 102 rows, numbered 0, 1, 2, ... in order; the first image of every pack has 102 rows; the padding rows at a pack's end, if any, share the next number; some pack holds as many images as fit. `valid_rows`: 1 on the rows of images, 0 on a pack's padding rows.
All inputs are finite; a program needn't handle non-finite values.
Results may differ from the reference program's by a relative error of at most 0.022.
Values may be sent and summed in bfloat16 or wider, within the bound.
No kernel may reach another device: no remote copies, remote signals or barrier semaphores. Data moves between devices by JAX's collectives and lax.ppermute only.
A program may use at most 192 MiB of HBM per device.

```python
import math
import jax
import jax.numpy as jnp
from jax import lax

D = 384
HEADS = 6
HD = 64
FF = 1536
PACK = 2048
PATCH_MIN = 16
PATCH_MAX = 100
MARGIN = 128
NS_STEPS = 5
STEP = 10
BLOCK = 512
NVEC = 12
TOTAL_ROWS = 65536


def image_layout(key):
    packs = TOTAL_ROWS // PACK
    most_images = PACK // (PATCH_MIN + 2) + 1
    lengths = jax.random.randint(key, (packs, most_images), PATCH_MIN + 2, PATCH_MAX + 3)
    fullest = jax.random.randint(jax.random.fold_in(key, 7), (), 0, packs)
    pack_number = jnp.arange(packs, dtype=jnp.int32)[:, None]
    lengths = jnp.where(pack_number == fullest, PATCH_MIN + 2, lengths)
    lengths = lengths.at[:, 0].set(PATCH_MAX + 2)
    endings = jnp.cumsum(lengths, axis=1).astype(jnp.int32)
    positions = jnp.arange(PACK, dtype=jnp.int32)
    numbers = jax.vmap(lambda ending: jnp.searchsorted(ending, positions, side='right'))(endings)
    filled = jnp.max(jnp.where(endings <= PACK, endings, 0), axis=1)
    living = (positions[None, :] < filled[:, None]).astype(jnp.int32)
    return (numbers.astype(jnp.int32).reshape(-1), living.reshape(-1))


def draw_segment(key, part):
    return image_layout(key)[0]


def draw_valid_rows(key, part):
    return image_layout(key)[1]


def rising(base, low_end, high_end):
    height, breadth = base.shape
    along_rows = low_end + (high_end - low_end) * jnp.arange(height, dtype=jnp.float32) / height
    along_cols = low_end + (high_end - low_end) * jnp.arange(breadth, dtype=jnp.float32) / breadth
    return base * along_rows[:, None] * along_cols[None, :]


def draw_qkv_moment(key, part):
    key = jax.random.fold_in(key, 31)
    return rising(jax.random.normal(key, (3 * D, D), jnp.float32), 0.6, 1.8) * (0.5 * TOTAL_ROWS ** 0.5)


def draw_proj_moment(key, part):
    key = jax.random.fold_in(key, 32)
    return rising(jax.random.normal(key, (D, D), jnp.float32), 0.6, 1.8) * (0.5 * TOTAL_ROWS ** 0.5)


def draw_fc1_moment(key, part):
    key = jax.random.fold_in(key, 33)
    return rising(jax.random.normal(key, (FF, D), jnp.float32), 0.6, 1.8) * (0.5 * TOTAL_ROWS ** 0.5)


def draw_fc2_moment(key, part):
    key = jax.random.fold_in(key, 34)
    return rising(jax.random.normal(key, (FF, D), jnp.float32), 0.6, 1.8) * (0.5 * TOTAL_ROWS ** 0.5)


def draw_vectors(key, part):
    key = jax.random.fold_in(key, 41)
    noise = jax.random.normal(key, (NVEC, D), jnp.float32)
    slope = 0.6 + 1.2 * jnp.arange(D, dtype=jnp.float32) / D
    row_number = jnp.arange(NVEC, dtype=jnp.int32)[:, None]
    gains = slope[None, :] * (1.0 + 0.1 * noise)
    return jnp.where((row_number == 0) | (row_number == 5), gains, 0.2 * noise)


def draw_vector_moment(key, part):
    key = jax.random.fold_in(key, 42)
    return jax.random.normal(key, (NVEC, D), jnp.float32) * (0.11 * TOTAL_ROWS ** 0.5)


def steps_of(key, dims, shards, smallest, high):
    def one(position, blocks):
        heights = jax.random.uniform(jax.random.fold_in(jax.random.fold_in(key, 6), position), (blocks,), jnp.float32, smallest / len(shards), high / len(shards))
        return jnp.repeat(jnp.exp(heights), dims[position] // blocks).reshape((-1,) + (1,) * (len(dims) - position - 1))

    level = one(*shards[0])
    for cut in shards[1:]:
        level = level * one(*cut)
    return level


def gaussian(rng, shape, deviation, most, shards=(), kind=jnp.bfloat16):
    entries = jax.random.normal(rng, shape, jnp.float32) * deviation
    if len(shards) > 0:
        entries = steps_of(rng, shape, shards, -0.22, 0.18) * entries
    return jnp.clip(entries, min=-most, max=most).astype(kind)


def setup_inputs(seed: int = 0) -> dict:
    splits = jax.random.split(jax.random.key(seed), 16)
    return {
        "tokens": gaussian(splits[0], (TOTAL_ROWS, D), 1.0, 6.0, ((0, 32),)),
        "cotangent": gaussian(splits[1], (TOTAL_ROWS, D), 1.0, 6.0, ((0, 32),)),
        "segment": draw_segment(jax.random.fold_in(splits[15], 71), 0),
        "valid_rows": draw_valid_rows(jax.random.fold_in(splits[15], 71), 0),
        "qkv_weight": gaussian(splits[4], (3 * D, D), D ** -0.5, 0.3125, ((0, 4), (1, 8)), jnp.float32),
        "proj_weight": gaussian(splits[5], (D, D), (D // 8) ** -0.5, 0.875, ((0, 4), (1, 8)), jnp.float32),
        "fc1_weight": gaussian(splits[6], (FF, D), D ** -0.5, 0.3125, ((0, 4), (1, 8)), jnp.float32),
        "fc2_weight": gaussian(splits[7], (FF, D), FF ** -0.5, 0.15625, ((0, 4), (1, 8)), jnp.float32),
        "qkv_moment": draw_qkv_moment(jax.random.fold_in(splits[15], 71), 0),
        "proj_moment": draw_proj_moment(jax.random.fold_in(splits[15], 71), 0),
        "fc1_moment": draw_fc1_moment(jax.random.fold_in(splits[15], 71), 0),
        "fc2_moment": draw_fc2_moment(jax.random.fold_in(splits[15], 71), 0),
        "vectors": draw_vectors(jax.random.fold_in(splits[15], 71), 0),
        "vector_moment": draw_vector_moment(jax.random.fold_in(splits[15], 71), 0),
        "vector_square": jnp.clip(jnp.exp(math.log(524.0) - 2.7957558 * jax.random.uniform(splits[14], (NVEC, D), jnp.float32) ** steps_of(splits[14], (NVEC, D), ((0, 4), (1, 8)), -0.2, 0.2)), 32.0, 524.0),
    }


@jax.custom_vjp
def low(v):
    return lax.optimization_barrier(v.astype(jnp.bfloat16)).astype(jnp.float32)

@jax.custom_vjp
def low_back(v):
    return v

def low_keep(v):
    return (low(v), None)

def low_pass(kept, grad):
    return (grad,)

def back_keep(v):
    return (v, None)

def back_low(kept, grad):
    return (low(grad),)
low.defvjp(low_keep, low_pass)
low_back.defvjp(back_keep, back_low)
EPS_NORM = 1e-06
NEWTON_A = 3.4445
NEWTON_B = -4.775
NEWTON_C = 2.0315
MUON_RATE = 0.2
MUON_DECAY = 0.1
ADAM_RATE = 0.4
BETA_ONE = 0.9
BETA_TWO = 0.999
ADAM_EPS = 1e-08
HIGHEST = lax.Precision.HIGHEST

def layer_norm(value, gain, shift):
    center = value - lax.optimization_barrier(jnp.mean(value, axis=-1, keepdims=True))
    spread = lax.optimization_barrier(jnp.mean(center * center, axis=-1, keepdims=True))
    return center * lax.rsqrt(spread + EPS_NORM) * gain + shift

def matmul(left, right):
    return jnp.dot(left, right, precision=HIGHEST, preferred_element_type=jnp.float32)

def allowed_mask(segment_ids, segment_padded, live_padded, offset, span):
    own_ids = lax.dynamic_slice_in_dim(segment_ids, offset, BLOCK, 0)
    near_ids = lax.dynamic_slice_in_dim(segment_padded, offset, span, 0)
    near_live = lax.dynamic_slice_in_dim(live_padded, offset, span, 0)
    query_pos = offset + jnp.arange(BLOCK, dtype=jnp.int32)
    key_pos = offset - MARGIN + jnp.arange(span, dtype=jnp.int32)
    same_image = own_ids[:, None] == near_ids[None, :]
    return same_image & ((near_live[None, :] > 0) | (query_pos[:, None] == key_pos[None, :]))

def attend(query_heads, key_heads, value_heads, segment_ids, live_rows):
    total_rows = query_heads.shape[0]
    span = BLOCK + 2 * MARGIN
    key_padded = jnp.pad(key_heads, ((MARGIN, MARGIN), (0, 0), (0, 0)))
    value_padded = jnp.pad(value_heads, ((MARGIN, MARGIN), (0, 0), (0, 0)))
    segment_padded = jnp.pad(segment_ids, (MARGIN, MARGIN), constant_values=-1)
    live_padded = jnp.pad(live_rows, (MARGIN, MARGIN))
    score_scale = HD ** (-0.5)

    def one_block(block_index):
        offset = block_index * BLOCK
        queries = lax.dynamic_slice_in_dim(query_heads, offset, BLOCK, 0)
        keys_near = lax.dynamic_slice_in_dim(key_padded, offset, span, 0)
        values_near = lax.dynamic_slice_in_dim(value_padded, offset, span, 0)
        allowed = allowed_mask(segment_ids, segment_padded, live_padded, offset, span)
        scores = low_back(jnp.einsum('qhd,khd->hqk', queries, keys_near, precision=HIGHEST) * score_scale)
        scores = jnp.where(allowed[None], scores, -1e+30)
        largest = lax.optimization_barrier(jnp.max(scores, axis=-1, keepdims=True))
        expo = jnp.exp(scores - largest)
        attn_probs = expo / lax.optimization_barrier(jnp.sum(expo, axis=-1, keepdims=True))
        return jnp.einsum('hqk,khd->qhd', low(attn_probs), values_near, precision=HIGHEST)
    blocks = lax.map(jax.checkpoint(one_block), jnp.arange(total_rows // BLOCK, dtype=jnp.int32))
    return blocks.reshape(total_rows, HEADS * HD)

def one_pack(weights, tokens_f, segment_ids, live_rows):
    qkv_w, proj_w, fc1_w, fc2_w, vector_full = weights
    total_rows = tokens_f.shape[0]
    first_in = low(layer_norm(tokens_f, vector_full[0], vector_full[1]))
    qkv_bias = jnp.concatenate([vector_full[2], jnp.zeros_like(vector_full[2]), vector_full[3]])
    qkv_rows = low(low_back(matmul(first_in, qkv_w.T) + qkv_bias))
    head_split = qkv_rows.reshape(total_rows, 3, HEADS, HD)
    attn_mixed = low(low_back(attend(head_split[:, 0], head_split[:, 1], head_split[:, 2], segment_ids, live_rows)))
    residual = tokens_f + low_back(matmul(attn_mixed, proj_w) + vector_full[4])
    second_in = low(layer_norm(residual, vector_full[5], vector_full[6]))
    hidden = low_back(matmul(second_in, fc1_w.T) + vector_full[8:].reshape(-1))
    activated = low(jax.nn.gelu(hidden, approximate=False))
    return residual + low_back(matmul(activated, fc2_w) + vector_full[7])

def orthogonal(moment_new):
    current = moment_new / (jnp.sqrt(jnp.sum(moment_new * moment_new)) + 1e-07)
    for repeat in range(NS_STEPS):
        gram = matmul(current.T, current)
        current = NEWTON_A * current + matmul(current, NEWTON_B * gram + NEWTON_C * matmul(gram, gram))
    return current

def reference(tokens, cotangent, segment, valid_rows, qkv_weight, proj_weight, fc1_weight, fc2_weight, qkv_moment, proj_moment, fc1_moment, fc2_moment, vectors, vector_moment, vector_square):
    packs = tokens.shape[0] // PACK
    inputs = tokens.astype(jnp.float32).reshape(packs, PACK, D)
    segment_packs = segment.reshape(packs, PACK)
    live_packs = valid_rows.reshape(packs, PACK)

    def forward(params, pack_inputs):
        weights = tuple((low(member) for member in params))

        def run_pack(element):
            return jax.checkpoint(one_pack)(weights, element[0], element[1], element[2])
        return lax.map(run_pack, (pack_inputs, segment_packs, live_packs))
    params = (qkv_weight, proj_weight, fc1_weight, fc2_weight, vectors)
    result, pullback = jax.vjp(forward, params, inputs)
    grads, input_grads = pullback(cotangent.astype(jnp.float32).reshape(packs, PACK, D))
    output = result.reshape(-1, D).astype(jnp.bfloat16)
    input_grad = input_grads.reshape(-1, D).astype(jnp.bfloat16)
    masters = (qkv_weight, proj_weight, fc1_weight, fc2_weight)
    moments = (qkv_moment, proj_moment, fc1_moment, fc2_moment)
    moments_new = []
    weights_new = []
    for number in range(4):
        momentum_new = grads[number] + 0.5 * moments[number]
        ortho = orthogonal(momentum_new)
        height = masters[number].shape[0]
        weights_new.append(masters[number] * (1.0 - MUON_RATE * MUON_DECAY) - MUON_RATE * 0.2 * math.sqrt(height) * ortho)
        moments_new.append(momentum_new)
    vector_grad = grads[4]
    first_new = BETA_ONE * vector_moment + (1.0 - BETA_ONE) * vector_grad
    second_new = BETA_TWO * vector_square + (1.0 - BETA_TWO) * vector_grad * vector_grad
    first_hat = first_new / (1.0 - BETA_ONE ** STEP)
    second_hat = second_new / (1.0 - BETA_TWO ** STEP)
    vectors_new = vectors - ADAM_RATE * first_hat / (jnp.sqrt(second_hat) + ADAM_EPS)
    return (output, input_grad, weights_new[0], weights_new[1], weights_new[2], weights_new[3], moments_new[0], moments_new[1], moments_new[2], moments_new[3], first_new, second_new, vectors_new, weights_new[0].astype(jnp.bfloat16), weights_new[1].astype(jnp.bfloat16), weights_new[2].astype(jnp.bfloat16), weights_new[3].astype(jnp.bfloat16))
```

```python
import math

import jax
import jax.numpy as jnp
from jax import lax
from jax.sharding import PartitionSpec as P

HEADS = 6
MARGIN = 128
NS_STEPS = 5
STEP = 10
BLOCK = 512


EPS_NORM = 1e-06
NEWTON_A = 3.4445
NEWTON_B = -4.775
NEWTON_C = 2.0315
MUON_RATE = 0.2
MUON_DECAY = 0.1
ADAM_RATE = 0.4
BETA_ONE = 0.9
BETA_TWO = 0.999
ADAM_EPS = 1e-08
HIGHEST = lax.Precision.HIGHEST
ROWS_DIMS = (((0,), (0,)), ((), ()))
COLS_DIMS = (((1,), (1,)), ((), ()))
PLAIN_DIMS = (((1,), (0,)), ((), ()))


def exchange(x, axis, mask):
    size = lax.axis_size(axis)
    return lax.ppermute(x, axis, [(i, i ^ mask) for i in range(size)])


def xor_order(blocks, axis):
    size = blocks.shape[0]
    index = lax.axis_index(axis)
    bit = 1
    while bit < size:
        paired = blocks.reshape(size // (2 * bit), 2, bit, *blocks.shape[1:])
        turned = jnp.flip(paired, axis=1)
        blocks = jnp.where((index & bit) != 0, turned, paired).reshape(blocks.shape)
        bit *= 2
    return blocks


def spread(own, axis):
    size = lax.axis_size(axis)
    if size <= 8:
        return jnp.stack([own] + [exchange(own, axis, mask) for mask in range(1, size)])
    held = own[None]
    bit = 1
    while bit < size:
        held = jnp.concatenate([held, exchange(held, axis, bit)])
        bit *= 2
    return held


def spread_ns(own):
    size = lax.axis_size("ns")
    held = own[None]
    bit = size // 2
    while bit >= 1:
        held = jnp.concatenate([held, exchange(held, "ns", bit)])
        bit //= 2
    return held


def ns_order(blocks):
    size = blocks.shape[0]
    bits = size.bit_length() - 1
    back = [int(format(i, "0" + str(bits) + "b")[::-1], 2) for i in range(size)]
    return xor_order(jnp.stack([blocks[back[i]] for i in range(size)]), "ns")


def sum_owned(grad):
    low = jnp.bfloat16
    size = grad.shape[0]
    held = grad
    index = lax.axis_index("ns")
    bit = 1
    while bit < size:
        pairs = held.reshape(-1, 2, *held.shape[1:])
        mine = (index & bit) != 0
        keep = jnp.where(mine, pairs[:, 1], pairs[:, 0])
        send = jnp.where(mine, pairs[:, 0], pairs[:, 1])
        got = exchange(send, "ns", bit)
        held = (keep.astype(jnp.float32) + got.astype(jnp.float32)).astype(low)
        bit *= 2
    held = held[0]
    dp = lax.axis_size("dp")
    blocks = xor_order(held.reshape(dp, -1, held.shape[-1]), "dp")
    if dp <= 8:
        got = [exchange(blocks[mask], "dp", mask) for mask in range(1, dp)]
        total = blocks[0].astype(jnp.float32)
        for part in got:
            total = total + part.astype(jnp.float32)
        return total
    bit = dp // 2
    while bit >= 1:
        got = exchange(blocks[bit:], "dp", bit)
        total = blocks[:bit].astype(jnp.float32) + got.astype(jnp.float32)
        blocks = total.astype(low)
        bit //= 2
    return total[0]


def layer_norm(value, gain, shift):
    center = value - jnp.mean(value, axis=-1, keepdims=True)
    spread_of = jnp.mean(center * center, axis=-1, keepdims=True)
    return center * lax.rsqrt(spread_of + EPS_NORM) * gain + shift


def gelu_exact(value):
    return jax.nn.gelu(value, approximate=False)


def allowed_mask(segment_ids, segment_padded, live_padded, offset, span):
    own_ids = lax.dynamic_slice_in_dim(segment_ids, offset, BLOCK, 0)
    near_ids = lax.dynamic_slice_in_dim(segment_padded, offset, span, 0)
    near_live = lax.dynamic_slice_in_dim(live_padded, offset, span, 0)
    query_pos = offset + jnp.arange(BLOCK, dtype=jnp.int32)
    key_pos = offset - MARGIN + jnp.arange(span, dtype=jnp.int32)
    same_image = own_ids[:, None] == near_ids[None, :]
    return same_image & ((near_live[None, :] > 0) | (query_pos[:, None] == key_pos[None, :]))


def padded_inputs(key_heads, value_heads, segment_ids, live_rows):
    key_padded = jnp.pad(key_heads, ((MARGIN, MARGIN), (0, 0), (0, 0)))
    value_padded = jnp.pad(value_heads, ((MARGIN, MARGIN), (0, 0), (0, 0)))
    segment_padded = jnp.pad(segment_ids, (MARGIN, MARGIN), constant_values=-1)
    live_padded = jnp.pad(live_rows, (MARGIN, MARGIN))
    return (key_padded, value_padded, segment_padded, live_padded)


def block_scores(query_heads, key_padded, segment_ids, segment_padded, live_padded, offset, span):
    score_scale = query_heads.shape[-1] ** (-0.5)
    queries = lax.dynamic_slice_in_dim(query_heads, offset, BLOCK, 0)
    keys_near = lax.dynamic_slice_in_dim(key_padded, offset, span, 0)
    allowed = allowed_mask(segment_ids, segment_padded, live_padded, offset, span)
    raw_scores = (
        jnp.einsum("qhd,khd->hqk", queries, keys_near, preferred_element_type=jnp.float32)
        * score_scale
    )
    return (queries, keys_near, jnp.where(allowed[None], raw_scores, -1e30))


def attend_forward(query_heads, key_heads, value_heads, segment_ids, live_rows):
    total_rows = query_heads.shape[0]
    span = BLOCK + 2 * MARGIN
    key_padded, value_padded, segment_padded, live_padded = padded_inputs(
        key_heads, value_heads, segment_ids, live_rows
    )

    def one_block(block_index):
        offset = block_index * BLOCK
        queries, keys_near, scores = block_scores(
            query_heads, key_padded, segment_ids, segment_padded, live_padded, offset, span
        )
        values_near = lax.dynamic_slice_in_dim(value_padded, offset, span, 0)
        largest = jnp.max(scores, axis=-1, keepdims=True)
        expo = jnp.exp(scores - largest)
        summed = jnp.sum(expo, axis=-1, keepdims=True)
        attn_probs = (expo / summed).astype(jnp.bfloat16)
        attn_mixed = jnp.einsum(
            "hqk,khd->qhd", attn_probs, values_near, preferred_element_type=jnp.float32
        )
        return (attn_mixed.astype(jnp.bfloat16), largest[..., 0], summed[..., 0])

    attn_mixed, largest_all, summed_all = lax.map(
        one_block, jnp.arange(total_rows // BLOCK, dtype=jnp.int32)
    )
    return (attn_mixed.reshape(total_rows, -1), largest_all, summed_all)


def attend_backward(
    query_heads, key_heads, value_heads, segment_ids, live_rows, largest_all, summed_all, grad_mixed
):
    total_rows = query_heads.shape[0]
    span = BLOCK + 2 * MARGIN
    score_scale = query_heads.shape[-1] ** (-0.5)
    grad_heads = grad_mixed.reshape(query_heads.shape)
    key_padded, value_padded, segment_padded, live_padded = padded_inputs(
        key_heads, value_heads, segment_ids, live_rows
    )
    empty = jnp.zeros(key_padded.shape, jnp.float32)

    def one_block(carried, block_index):
        key_acc, value_acc = carried
        offset = block_index * BLOCK
        queries, keys_near, scores = block_scores(
            query_heads, key_padded, segment_ids, segment_padded, live_padded, offset, span
        )
        values_near = lax.dynamic_slice_in_dim(value_padded, offset, span, 0)
        attn_probs = (
            jnp.exp(scores - largest_all[block_index][..., None])
            / summed_all[block_index][..., None]
        )
        low_probs = attn_probs.astype(jnp.bfloat16)
        grad_out = lax.dynamic_slice_in_dim(grad_heads, offset, BLOCK, 0)
        grad_values = jnp.einsum(
            "hqk,qhd->khd", low_probs, grad_out, preferred_element_type=jnp.float32
        )
        grad_probs = jnp.einsum(
            "qhd,khd->hqk", grad_out, values_near, preferred_element_type=jnp.float32
        )
        inner = jnp.sum(attn_probs * grad_probs, axis=-1, keepdims=True)
        grad_scores = (attn_probs * (grad_probs - inner)).astype(jnp.bfloat16)
        grad_query = score_scale * jnp.einsum(
            "hqk,khd->qhd", grad_scores, keys_near, preferred_element_type=jnp.float32
        )
        grad_keys = score_scale * jnp.einsum(
            "hqk,qhd->khd", grad_scores, queries, preferred_element_type=jnp.float32
        )
        key_acc = lax.dynamic_update_slice_in_dim(
            key_acc, lax.dynamic_slice_in_dim(key_acc, offset, span, 0) + grad_keys, offset, 0
        )
        value_acc = lax.dynamic_update_slice_in_dim(
            value_acc, lax.dynamic_slice_in_dim(value_acc, offset, span, 0) + grad_values, offset, 0
        )
        return ((key_acc, value_acc), grad_query)

    (key_acc, value_acc), grad_query = lax.scan(
        one_block, (empty, empty), jnp.arange(total_rows // BLOCK, dtype=jnp.int32)
    )
    grad_keys_all = key_acc[MARGIN : MARGIN + total_rows].reshape(total_rows, -1)
    grad_values_all = value_acc[MARGIN : MARGIN + total_rows].reshape(total_rows, -1)
    return jnp.concatenate(
        [grad_query.reshape(total_rows, -1), grad_keys_all, grad_values_all], axis=1
    )


def matmul_high(left, right, dims=PLAIN_DIMS):
    return lax.dot_general(left, right, dims, precision=HIGHEST, preferred_element_type=jnp.float32)


def orthogonal_rows(blocks, rows):
    ns, depth, _ = blocks.shape
    gram = None
    for block in range(ns):
        part = lax.dot_general(
            blocks[block], blocks[block], COLS_DIMS, preferred_element_type=jnp.float32
        )
        gram = part if gram is None else gram + part
    eye = jnp.eye(depth, dtype=jnp.float32)
    norm = 1.0 / (jnp.sqrt(jnp.sum(gram * eye)) + 1e-07)
    gram = gram * (norm * norm)
    left = eye[:rows] * norm
    for step in range(NS_STEPS):
        once = matmul_high(left, gram)
        if step < NS_STEPS - 1:
            square = matmul_high(gram, gram)
            poly = NEWTON_A * eye + NEWTON_B * gram + NEWTON_C * square
            left = NEWTON_A * left + NEWTON_B * once + NEWTON_C * matmul_high(left, square)
            gram = matmul_high(matmul_high(gram, poly), poly)
        else:
            left = NEWTON_A * left + NEWTON_B * once + NEWTON_C * matmul_high(once, gram)
    return matmul_high(left, blocks[0].astype(jnp.float32))


def per_device(
    tokens,
    cotangent,
    segment,
    valid_rows,
    qkv_weight,
    proj_weight,
    fc1_weight,
    fc2_weight,
    qkv_moment,
    proj_moment,
    fc1_moment,
    fc2_moment,
    vectors,
    vector_moment,
    vector_square,
):
    low = jnp.bfloat16
    total_rows, model_width = tokens.shape
    head_size = model_width // HEADS
    ns = lax.axis_size("ns")
    weights = tuple(w.T for w in (qkv_weight, proj_weight, fc1_weight, fc2_weight))
    moments = tuple(w.T for w in (qkv_moment, proj_moment, fc1_moment, fc2_moment))
    share = weights[0].shape[0]
    heights = tuple(w.shape[1] for w in weights)
    vec_rows = vectors.shape[0]

    first_shard = jnp.concatenate([weights[0], vectors.T], axis=1).astype(low)
    later_shard = jnp.concatenate(weights[1:], axis=1).astype(low)

    def whole_of(shard):
        columns = xor_order(spread(shard, "dp"), "dp").reshape(model_width, -1)
        return ns_order(spread_ns(columns))

    def side(blocks, at, height):
        return jnp.moveaxis(blocks[:, :, at : at + height], 0, 1).reshape(model_width, -1)

    first_all = whole_of(first_shard)
    later_all = whole_of(later_shard)
    qkv_t = side(first_all, 0, heights[0])
    vector_full = side(first_all, heights[0], vec_rows).T.astype(jnp.float32)
    proj_t = side(later_all, 0, heights[1])
    fc1_t = side(later_all, heights[1], heights[2])
    fc2_t = side(later_all, heights[1] + heights[2], heights[3])

    tokens_f = tokens.astype(jnp.float32)
    normed_one, back_one = jax.vjp(layer_norm, tokens_f, vector_full[0], vector_full[1])
    first_in = normed_one.astype(low)
    qkv_bias = jnp.concatenate([vector_full[2], jnp.zeros_like(vector_full[2]), vector_full[3]])
    qkv_rows = (jnp.dot(first_in, qkv_t, preferred_element_type=jnp.float32) + qkv_bias).astype(low)
    head_split = qkv_rows.reshape(total_rows, 3, HEADS, head_size)
    query_heads = head_split[:, 0]
    key_heads = head_split[:, 1]
    value_heads = head_split[:, 2]
    attn_mixed, largest_all, summed_all = attend_forward(
        query_heads, key_heads, value_heads, segment, valid_rows
    )
    residual = (
        tokens_f
        + lax.dot_general(attn_mixed, proj_t, COLS_DIMS, preferred_element_type=jnp.float32)
        + vector_full[4]
    )
    normed_two, back_two = jax.vjp(layer_norm, residual, vector_full[5], vector_full[6])
    second_in = normed_two.astype(low)
    hidden = jnp.dot(
        second_in, fc1_t, preferred_element_type=jnp.float32
    ) + vector_full[8:].reshape(-1)
    activated_f, back_act = jax.vjp(gelu_exact, hidden)
    activated = activated_f.astype(low)
    output = (
        residual
        + lax.dot_general(activated, fc2_t, COLS_DIMS, preferred_element_type=jnp.float32)
        + vector_full[7]
    ).astype(low)
    grad_out = cotangent.astype(jnp.float32)
    grad_fc2 = lax.dot_general(cotangent, activated, ROWS_DIMS, preferred_element_type=jnp.float32)
    grad_act = jnp.dot(cotangent, fc2_t, preferred_element_type=jnp.float32)
    grad_hidden = back_act(grad_act)[0].astype(low)
    grad_fc1 = lax.dot_general(
        second_in, grad_hidden, ROWS_DIMS, preferred_element_type=jnp.float32
    )
    grad_second = lax.dot_general(grad_hidden, fc1_t, COLS_DIMS, preferred_element_type=jnp.float32)
    grad_norm_two, grad_gain_two, grad_shift_two = back_two(grad_second)
    grad_residual = grad_out + grad_norm_two
    grad_branch = grad_residual.astype(low)
    grad_proj = lax.dot_general(
        grad_branch, attn_mixed, ROWS_DIMS, preferred_element_type=jnp.float32
    )

    def blocked(grad, rows):
        return jnp.moveaxis(grad.reshape(model_width, ns, rows), 1, 0)

    later_grad = jnp.concatenate(
        [
            blocked(grad_proj.astype(low), heights[1]),
            blocked(grad_fc1.astype(low), heights[2]),
            blocked(grad_fc2.astype(low), heights[3]),
        ],
        axis=2,
    )
    later_owned = sum_owned(later_grad)

    grad_mixed = jnp.dot(
        grad_branch, proj_t, preferred_element_type=jnp.float32
    ).astype(low)
    grad_qkv = attend_backward(
        query_heads,
        key_heads,
        value_heads,
        segment,
        valid_rows,
        largest_all,
        summed_all,
        grad_mixed,
    ).astype(low)
    grad_qkvw = lax.dot_general(first_in, grad_qkv, ROWS_DIMS, preferred_element_type=jnp.float32)
    grad_first = lax.dot_general(grad_qkv, qkv_t, COLS_DIMS, preferred_element_type=jnp.float32)
    grad_norm_one, grad_gain_one, grad_shift_one = back_one(grad_first)
    input_grad = (grad_residual + grad_norm_one).astype(low)
    qkv_sums = jnp.sum(grad_qkv, axis=0, dtype=jnp.float32)
    hidden_sums = jnp.sum(grad_hidden, axis=0, dtype=jnp.float32)
    grad_vectors = jnp.concatenate(
        [
            jnp.stack(
                [
                    grad_gain_one,
                    grad_shift_one,
                    qkv_sums[:model_width],
                    qkv_sums[2 * model_width :],
                    jnp.sum(grad_branch, axis=0, dtype=jnp.float32),
                    grad_gain_two,
                    grad_shift_two,
                    jnp.sum(grad_out, axis=0),
                ]
            ),
            hidden_sums.reshape(-1, model_width),
        ],
        axis=0,
    )
    first_grad = jnp.concatenate(
        [
            blocked(grad_qkvw.astype(low), heights[0]),
            blocked(grad_vectors.T.astype(low), vec_rows),
        ],
        axis=2,
    )
    first_owned = sum_owned(first_grad)

    def gathered_moments(owned):
        columns = spread(owned.astype(low), "dp").reshape(model_width, -1)
        return spread_ns(columns)

    later_moment = later_owned + 0.5 * jnp.concatenate(moments[1:], axis=1)
    later_blocks = gathered_moments(later_moment)
    first_moment = first_owned[:, : heights[0]] + 0.5 * moments[0]
    first_blocks = gathered_moments(first_moment)
    cuts = (0, heights[1], heights[1] + heights[2], heights[1] + heights[2] + heights[3])
    blocks = [first_blocks] + [later_blocks[:, :, cuts[n] : cuts[n + 1]] for n in range(3)]
    moments_new = [first_moment] + [later_moment[:, cuts[n] : cuts[n + 1]] for n in range(3)]
    weights_new = []
    for number in range(4):
        ortho = orthogonal_rows(blocks[number], share)
        scale = MUON_RATE * 0.2 * math.sqrt(heights[number] * ns)
        weights_new.append(
            weights[number] * (1.0 - MUON_RATE * MUON_DECAY) - scale * ortho
        )
    vector_grad = first_owned[:, heights[0] :].T
    first_new = BETA_ONE * vector_moment + (1.0 - BETA_ONE) * vector_grad
    second_new = BETA_TWO * vector_square + (1.0 - BETA_TWO) * vector_grad * vector_grad
    first_hat = first_new / (1.0 - BETA_ONE**STEP)
    second_hat = second_new / (1.0 - BETA_TWO**STEP)
    vectors_new = vectors - ADAM_RATE * first_hat / (jnp.sqrt(second_hat) + ADAM_EPS)
    return (
        output,
        input_grad,
        *(w.T for w in weights_new),
        *(m.T for m in moments_new),
        first_new,
        second_new,
        vectors_new,
        *(w.T.astype(low) for w in weights_new),
    )


def solution(mesh):
    rows = P(("dp", "ns"), None)
    flat = P(("dp", "ns"))
    block = P("ns", "dp")
    return jax.shard_map(
        per_device,
        mesh=mesh,
        in_specs=(rows, rows, flat, flat) + (block,) * 11,
        out_specs=(rows, rows) + (block,) * 15,
        check_vma=False,
    )
```

```python
import math

import jax
import jax.numpy as jnp
from jax import lax
from jax.experimental import pallas as pl
from jax.experimental.pallas import tpu as pltpu
from jax.sharding import PartitionSpec as P

HEADS = 6
PAIRS = 3
MARGIN = 128
NS_STEPS = 5
STEP = 10
TILE = 256
SUB = 128
SPAN = 384
VEC_LANES = 16


EPS_NORM = 1e-06
NEWTON_A = 3.4445
NEWTON_B = -4.775
NEWTON_C = 2.0315
MUON_RATE = 0.2
MUON_DECAY = 0.1
ADAM_RATE = 0.4
BETA_ONE = 0.9
BETA_TWO = 0.999
ADAM_EPS = 1e-08
LOW = jnp.bfloat16
F32 = jnp.float32
TN = (((0,), (0,)), ((), ()))
NT = (((1,), (1,)), ((), ()))
NN = (((1,), (0,)), ((), ()))
VMEM_LIMIT = 56 * 1024 * 1024
ERF_P = 0.3275911
ERF_COEFS = (0.254829592, -0.284496736, 1.421413741, -1.453152027, 1.061405429)


def dot(left, right, dims=NN):
    return lax.dot_general(left, right, dims, preferred_element_type=F32)


def lane_numbers(shape):
    return lax.broadcasted_iota(jnp.int32, shape, len(shape) - 1)


def norm_parts(value):
    center = value - jnp.mean(value, axis=-1, keepdims=True)
    rate = lax.rsqrt(jnp.mean(center * center, axis=-1, keepdims=True) + EPS_NORM)
    return center * rate, rate


def norm_back(grad, normed, rate, gain):
    scaled = grad * gain
    first = jnp.mean(scaled, axis=-1, keepdims=True)
    second = jnp.mean(scaled * normed, axis=-1, keepdims=True)
    return rate * (scaled - first - normed * second)


def gelu_both(value):
    size = jnp.abs(value) * (0.5**0.5)
    ratio = 1.0 / (1.0 + ERF_P * size)
    decay = jnp.exp(-(size * size))
    poly = ERF_COEFS[4]
    for coef in ERF_COEFS[3::-1]:
        poly = poly * ratio + coef
    tail = 0.5 * poly * ratio * decay
    phi = jnp.where(value >= 0, 1.0 - tail, tail)
    return value * phi, phi + value * decay * (1.0 / math.sqrt(2.0 * math.pi))


def pair_masks():
    lane = lane_numbers((1, SUB))
    first = (lane < SUB // 2).astype(F32)
    return first.astype(LOW), (1.0 - first).astype(LOW)


def both_heads(pair, masks):
    return jnp.concatenate([pair * masks[0], pair * masks[1]], axis=0)


def either_head(stacked):
    lane = lane_numbers((SUB, SUB))
    return jnp.where(lane < SUB // 2, stacked[:SUB], stacked[SUB:])


def attend_kernel(
    places, gathered, tokens, ids, qkv, mixed, expos, inverse, weight, vectors
):
    step = pl.program_id(0)
    chunks = pl.num_programs(0) - 1
    width = tokens.shape[1]
    block = 3 * width // gathered.shape[0]
    rows_each = 12 // gathered.shape[0]

    @pl.when(step == 0)
    def assemble():
        total = jnp.zeros((width, 3 * width), F32)
        turned = jnp.zeros((width, SUB), F32)
        for number in range(gathered.shape[0]):
            piece = gathered[places[number]].astype(F32)
            kept = jnp.where(lane_numbers(piece.shape) < block, piece, 0.0)
            wide = jnp.concatenate([kept, jnp.zeros((width, 2 * width), F32)], axis=1)
            total = total + (pltpu.roll(wide, block * number, 1) if number else wide)
            last = piece[:, 2 * SUB :]
            at = block - 2 * SUB
            lane = lane_numbers(last.shape)
            vec = jnp.where((lane >= at) & (lane < at + rows_each), last, 0.0)
            turned = turned + pltpu.roll(vec, (rows_each * number - at) % SUB, 1)
        weight[...] = total.astype(LOW)
        vectors[...] = turned.T[:VEC_LANES]
        qkv[pl.ds(0, MARGIN), :] = jnp.zeros((MARGIN, 3 * width), LOW)
        qkv[pl.ds(MARGIN + chunks * TILE, MARGIN), :] = jnp.zeros((MARGIN, 3 * width), LOW)

    @pl.when(step < chunks)
    def project():
        normed, _ = norm_parts(tokens[...].astype(F32))
        first_in = (normed * vectors[0:1, :] + vectors[1:2, :]).astype(LOW)
        result = dot(first_in, weight[...])
        at = pl.multiple_of(MARGIN + step * TILE, SUB)
        scale = (width // HEADS) ** (-0.5)
        query = (result[:, :width] + vectors[2:3, :]).astype(LOW)
        qkv[pl.ds(at, TILE), 0:width] = query * jnp.asarray(scale, LOW)
        qkv[pl.ds(at, TILE), width : 2 * width] = result[:, width : 2 * width].astype(LOW)
        value = result[:, 2 * width :] + vectors[3:4, :]
        qkv[pl.ds(at, TILE), 2 * width :] = value.astype(LOW)

    @pl.when(step > 0)
    def attend():
        masks = pair_masks()
        ones = jnp.ones((SPAN, SUB), LOW)
        for sub in range(TILE // SUB):
            tile = (step - 1) * (TILE // SUB) + sub
            start = pl.multiple_of(tile * SUB, SUB)
            own = jnp.broadcast_to(ids[pl.ds(tile + 1, 1), :], (SUB, SUB)).T
            near = [
                jnp.broadcast_to(ids[pl.ds(tile + j, 1), :], (SUB, SUB)) == own
                for j in range(SPAN // SUB)
            ]
            same = jnp.concatenate(near, axis=1)
            same = jnp.concatenate([same, same], axis=0)
            for pair in range(PAIRS):
                at = pair * SUB
                query = both_heads(qkv[pl.ds(start + MARGIN, SUB), at : at + SUB], masks)
                key = qkv[pl.ds(start, SPAN), width + at : width + at + SUB]
                value = qkv[pl.ds(start, SPAN), 2 * width + at : 2 * width + at + SUB]
                scores = jnp.where(same, dot(query, key, NT), -1e30)
                largest = jnp.max(scores, axis=1, keepdims=True)
                expo = jnp.exp(scores - largest).astype(LOW)
                expos[sub, pair] = expo
                both = dot(expo, jnp.concatenate([value, ones], axis=1))
                share = 1.0 / both[:, SUB:]
                here = pl.ds(sub * SUB, SUB)
                mixed[here, at : at + SUB] = either_head(both[:, :SUB] * share).astype(LOW)
                inverse[here, at : at + SUB] = either_head(share)


def attend_forward(places, gathered, tokens, ids):
    rows, width = tokens.shape
    chunks = rows // TILE
    before = lambda s, *_: (jnp.maximum(s - 1, 0), 0)
    whole = lambda *dims: pl.BlockSpec(dims, lambda s, *_: (0,) * len(dims))
    padded = rows + 2 * MARGIN
    return pl.pallas_call(
        attend_kernel,
        grid_spec=pltpu.PrefetchScalarGridSpec(
            num_scalar_prefetch=1,
            grid=(chunks + 1,),
            in_specs=[
                whole(*gathered.shape),
                pl.BlockSpec((TILE, width), lambda s, *_: (jnp.minimum(s, chunks - 1), 0)),
                whole(*ids.shape),
            ],
            out_specs=[
                whole(padded, 3 * width),
                pl.BlockSpec((TILE, width), before),
                pl.BlockSpec(
                    (TILE // SUB, PAIRS, 2 * SUB, SPAN),
                    lambda s, *_: (jnp.maximum(s - 1, 0), 0, 0, 0),
                ),
                pl.BlockSpec((TILE, width), before),
                whole(width, 3 * width),
                whole(VEC_LANES, width),
            ],
        ),
        out_shape=[
            jax.ShapeDtypeStruct((padded, 3 * width), LOW),
            jax.ShapeDtypeStruct((rows, width), LOW),
            jax.ShapeDtypeStruct((rows // SUB, PAIRS, 2 * SUB, SPAN), LOW),
            jax.ShapeDtypeStruct((rows, width), F32),
            jax.ShapeDtypeStruct((width, 3 * width), LOW),
            jax.ShapeDtypeStruct((VEC_LANES, width), F32),
        ],
        compiler_params=pltpu.CompilerParams(vmem_limit_bytes=VMEM_LIMIT),
        cost_estimate=pl.CostEstimate(
            flops=12_000_000_000, bytes_accessed=22_000_000, transcendentals=5_000_000
        ),
        name="attend_forward",
    )(places, gathered, tokens, ids)


def mlp_kernel(
    places,
    owners,
    gathered,
    vectors,
    mixed,
    tokens,
    cotangent,
    output,
    grad_residual,
    grad_mixed,
    grads,
    sums,
    proj,
    acc_one,
    acc_two,
    acc_proj,
):
    step = pl.program_id(0)
    width = tokens.shape[1]
    parts = gathered.shape[0]
    block = width // parts
    last_at = 2 * width

    @pl.when(step == 0)
    def assemble():
        total = jnp.zeros((width, width), F32)
        for number in range(parts):
            piece = gathered[places[number], :, last_at:].astype(F32)
            kept = jnp.where(lane_numbers(piece.shape) < block, piece, 0.0)
            wide = jnp.concatenate([kept, jnp.zeros((width, width - SUB), F32)], axis=1)
            total = total + (pltpu.roll(wide, block * number, 1) if number else wide)
        proj[...] = total.astype(LOW)
        acc_one[...] = jnp.zeros(acc_one.shape, F32)
        acc_two[...] = jnp.zeros(acc_two.shape, F32)
        acc_proj[...] = jnp.zeros(acc_proj.shape, F32)
        sums[...] = jnp.zeros(sums.shape, F32)

    def add_row(row, values):
        sums[pl.ds(row, 1), :] += jnp.sum(values, axis=0, keepdims=True)

    own = mixed[...]
    residual = tokens[...].astype(F32) + dot(own, proj[...], NT) + vectors[4:5, :]
    normed, rate = norm_parts(residual)
    gain = vectors[5:6, :]
    second_in = (normed * gain + vectors[6:7, :]).astype(LOW)
    out_low = cotangent[...]
    grad_out = out_low.astype(F32)
    second_turned = second_in.T
    out_turned = out_low.T
    result = residual + vectors[7:8, :]
    grad_second = jnp.zeros((TILE, width), F32)
    for part in range(parts):
        one = gathered[part, :, :width]
        two = gathered[part, :, width:last_at]
        row = 8 + owners[part]
        hidden = dot(second_in, one) + vectors[pl.ds(row, 1), :]
        active, slope = gelu_both(hidden)
        active = active.astype(LOW)
        grad_hidden = (dot(out_low, two) * slope).astype(LOW)
        result = result + dot(active, two, NT)
        grad_second = grad_second + dot(grad_hidden, one, NT)
        acc_one[part] += dot(second_turned, grad_hidden)
        acc_two[part] += dot(out_turned, active)
        add_row(row, grad_hidden.astype(F32))
    output[...] = result.astype(LOW)
    add_row(5, grad_second * normed)
    add_row(6, grad_second)
    add_row(7, grad_out)
    grad_res = grad_out + norm_back(grad_second, normed, rate, gain)
    grad_residual[...] = grad_res
    branch = grad_res.astype(LOW)
    add_row(4, branch.astype(F32))
    acc_proj[...] += dot(branch, own, TN)
    grad_mixed[...] = dot(branch, proj[...]).astype(LOW)

    @pl.when(step == pl.num_programs(0) - 1)
    def finish():
        for part in range(parts):
            grads[part, :, :width] = acc_one[part].astype(LOW)
            grads[part, :, width:last_at] = acc_two[part].astype(LOW)
        total = acc_proj[...]
        for number in range(parts):
            turned = pltpu.roll(total, (width - block * number) % width, 1) if number else total
            grads[places[number], :, last_at:] = turned[:, :SUB].astype(LOW)


def mlp_both(places, owners, gathered, vectors, mixed, tokens, cotangent):
    rows, width = tokens.shape
    parts = gathered.shape[0]
    tile = pl.BlockSpec((TILE, width), lambda s, *_: (s, 0))
    whole = lambda *dims: pl.BlockSpec(dims, lambda s, *_: (0,) * len(dims))
    return pl.pallas_call(
        mlp_kernel,
        grid_spec=pltpu.PrefetchScalarGridSpec(
            num_scalar_prefetch=2,
            grid=(rows // TILE,),
            in_specs=[whole(*gathered.shape), whole(*vectors.shape), tile, tile, tile],
            out_specs=[tile, tile, tile, whole(*gathered.shape), whole(*vectors.shape)],
            scratch_shapes=[
                pltpu.VMEM((width, width), LOW),
                pltpu.VMEM((parts, width, width), F32),
                pltpu.VMEM((parts, width, width), F32),
                pltpu.VMEM((width, width), F32),
            ],
        ),
        out_shape=[
            jax.ShapeDtypeStruct((rows, width), LOW),
            jax.ShapeDtypeStruct((rows, width), F32),
            jax.ShapeDtypeStruct((rows, width), LOW),
            jax.ShapeDtypeStruct(gathered.shape, LOW),
            jax.ShapeDtypeStruct(vectors.shape, F32),
        ],
        compiler_params=pltpu.CompilerParams(vmem_limit_bytes=VMEM_LIMIT),
        cost_estimate=pl.CostEstimate(
            flops=34_000_000_000, bytes_accessed=20_000_000, transcendentals=6_000_000
        ),
        name="mlp_both",
    )(places, owners, gathered, vectors, mixed, tokens, cotangent)


def attend_back_kernel(
    places,
    weight,
    vectors,
    sums_in,
    qkv,
    expos,
    inverse,
    mixed,
    grad_mixed,
    tokens,
    grad_residual,
    input_grad,
    grads,
    grad_query,
    acc_key,
    acc_value,
    acc_weight,
    sums,
):
    step = pl.program_id(0)
    chunks = pl.num_programs(0) - 1
    width = tokens.shape[1]
    parts = grads.shape[0]
    block = 3 * width // parts
    rows_each = 12 // parts
    scale = (width // HEADS) ** (-0.5)

    @pl.when(step == 0)
    def clear():
        acc_key[...] = jnp.zeros(acc_key.shape, F32)
        acc_value[...] = jnp.zeros(acc_value.shape, F32)
        acc_weight[...] = jnp.zeros(acc_weight.shape, F32)
        sums[0:VEC_LANES, :] = sums_in[...]
        sums[VEC_LANES:, :] = jnp.zeros((SUB - VEC_LANES, width), F32)

    @pl.when(step < chunks)
    def attend():
        masks = pair_masks()
        for sub in range(TILE // SUB):
            tile = step * (TILE // SUB) + sub
            start = pl.multiple_of(tile * SUB, SUB)
            here = pl.ds(sub * SUB, SUB)
            for pair in range(PAIRS):
                at = pair * SUB
                query = both_heads(qkv[pl.ds(start + MARGIN, SUB), at : at + SUB], masks)
                key = qkv[pl.ds(start, SPAN), width + at : width + at + SUB]
                value = qkv[pl.ds(start, SPAN), 2 * width + at : 2 * width + at + SUB]
                grad = grad_mixed[here, at : at + SUB].astype(F32) * inverse[here, at : at + SUB]
                product = grad * mixed[here, at : at + SUB].astype(F32)
                lane = lane_numbers(product.shape)
                first = jnp.sum(jnp.where(lane < SUB // 2, product, 0.0), axis=1, keepdims=True)
                second = jnp.sum(jnp.where(lane < SUB // 2, 0.0, product), axis=1, keepdims=True)
                inner = jnp.concatenate([first, second], axis=0)
                grad = both_heads(grad.astype(LOW), masks)
                expo = expos[sub, pair]
                scores = (expo.astype(F32) * (dot(grad, value, NT) - inner)).astype(LOW)
                query_grad = either_head(dot(scores, key)) * scale
                grad_query[pl.ds(start, SUB), at : at + SUB] = query_grad.astype(LOW)
                acc_key[pl.ds(start, SPAN), at : at + SUB] += dot(scores, query, TN)
                acc_value[pl.ds(start, SPAN), at : at + SUB] += dot(expo, grad, TN)

    @pl.when(step > 0)
    def project():
        at = pl.multiple_of((step - 1) * TILE, SUB)
        grad_q = grad_query[pl.ds(at, TILE), :]
        grad_k = acc_key[pl.ds(at + MARGIN, TILE), :].astype(LOW)
        grad_v = acc_value[pl.ds(at + MARGIN, TILE), :].astype(LOW)
        grad_qkv = jnp.concatenate([grad_q, grad_k, grad_v], axis=1)
        normed, rate = norm_parts(tokens[...].astype(F32))
        gain = vectors[0:1, :]
        first_in = (normed * gain + vectors[1:2, :]).astype(LOW)
        acc_weight[...] += dot(first_in.T, grad_qkv)
        grad_first = dot(grad_qkv, weight[...], NT)

        def add_row(row, values):
            sums[row : row + 1, :] += jnp.sum(values, axis=0, keepdims=True)

        add_row(0, grad_first * normed)
        add_row(1, grad_first)
        add_row(2, grad_q.astype(F32))
        add_row(3, grad_v.astype(F32))
        back = norm_back(grad_first, normed, rate, gain)
        input_grad[...] = (grad_residual[...] + back).astype(LOW)

    @pl.when(step == chunks)
    def finish():
        total = acc_weight[...]
        turned = sums[...].T
        at = block - 2 * SUB
        for number in range(parts):
            shift = (3 * width - block * number) % (3 * width)
            piece = (pltpu.roll(total, shift, 1) if number else total)[:, :width]
            vec = pltpu.roll(turned, (at - rows_each * number) % SUB, 1)
            lane = lane_numbers(vec.shape)
            last = jnp.where(lane < at, piece[:, 2 * SUB :], 0.0)
            last = jnp.where((lane >= at) & (lane < at + rows_each), vec, last)
            grads[places[number], :, : 2 * SUB] = piece[:, : 2 * SUB].astype(LOW)
            grads[places[number], :, 2 * SUB :] = last.astype(LOW)


def attend_backward(
    places, weight, vectors, sums, qkv, expos, inverse, mixed, grad_mixed, tokens, grad_residual
):
    rows, width = tokens.shape
    parts = places.shape[0]
    chunks = rows // TILE
    now = pl.BlockSpec((TILE, width), lambda s, *_: (jnp.minimum(s, chunks - 1), 0))
    before = pl.BlockSpec((TILE, width), lambda s, *_: (jnp.maximum(s - 1, 0), 0))
    whole = lambda *dims: pl.BlockSpec(dims, lambda s, *_: (0,) * len(dims))
    return pl.pallas_call(
        attend_back_kernel,
        grid_spec=pltpu.PrefetchScalarGridSpec(
            num_scalar_prefetch=1,
            grid=(chunks + 1,),
            in_specs=[
                whole(*weight.shape),
                whole(*vectors.shape),
                whole(*sums.shape),
                whole(*qkv.shape),
                pl.BlockSpec(
                    (TILE // SUB, PAIRS, 2 * SUB, SPAN),
                    lambda s, *_: (jnp.minimum(s, chunks - 1), 0, 0, 0),
                ),
                now,
                now,
                now,
                before,
                before,
            ],
            out_specs=[before, whole(parts, width, width)],
            scratch_shapes=[
                pltpu.VMEM((rows, width), LOW),
                pltpu.VMEM((rows + 2 * MARGIN, width), F32),
                pltpu.VMEM((rows + 2 * MARGIN, width), F32),
                pltpu.VMEM((width, 3 * width), F32),
                pltpu.VMEM((SUB, width), F32),
            ],
        ),
        out_shape=[
            jax.ShapeDtypeStruct((rows, width), LOW),
            jax.ShapeDtypeStruct((parts, width, width), LOW),
        ],
        compiler_params=pltpu.CompilerParams(vmem_limit_bytes=VMEM_LIMIT),
        cost_estimate=pl.CostEstimate(
            flops=20_000_000_000, bytes_accessed=26_000_000, transcendentals=10_000
        ),
        name="attend_backward",
    )(
        places, weight, vectors, sums, qkv, expos, inverse, mixed, grad_mixed, tokens,
        grad_residual,
    )


def halves(value):
    high = value.astype(LOW)
    return high, (value - high.astype(F32)).astype(LOW)


def dot_three(left, right):
    return dot(left[0], right[0]) + (dot(left[0], right[1]) + dot(left[1], right[0]))


def muon_kernel(lanes, count, height, offset, near, far, old, new, copy):
    depth = near.shape[1]
    rows = old.shape[0]
    wide = -(-count // SUB) * SUB

    def piece(ref, number):
        value = ref[number, :, lanes : lanes + wide]
        if wide != count:
            value = jnp.where(lane_numbers(value.shape) < count, value.astype(F32), 0.0).astype(LOW)
        return value

    own = piece(near, 0)
    gram = dot(own, own, NT)
    for ref, number in [(near, n) for n in range(1, near.shape[0])] + [
        (far, n) for n in range(far.shape[0])
    ]:
        part = piece(ref, number)
        gram = gram + dot(part, part, NT)
    down = lax.broadcasted_iota(jnp.int32, (depth, depth), 0)
    eye = (down == lane_numbers((depth, depth))).astype(F32)
    norm = 1.0 / (jnp.sqrt(jnp.sum(gram * eye, keepdims=True)) + 1e-07)
    gram = gram * (norm * norm)
    tall = -(-rows // 8) * 8
    place = lax.broadcasted_iota(jnp.int32, (tall, depth), 0) + offset[0]
    left = jnp.where(place == lane_numbers((tall, depth)), norm, 0.0)
    for step in range(NS_STEPS):
        pair = halves(gram)
        once = dot_three(halves(left), pair)
        if step < NS_STEPS - 1:
            square = dot_three(pair, pair)
            twice = dot_three(halves(left), halves(square))
            poly = halves(NEWTON_A * eye + NEWTON_B * gram + NEWTON_C * square)
            gram = dot_three(halves(dot_three(pair, poly)), poly)
        else:
            twice = dot_three(halves(once), pair)
        left = NEWTON_A * left + NEWTON_B * once + NEWTON_C * twice
    high, rest = halves(left)
    ortho = (dot(high, own) + dot(rest, own))[:rows, :count]
    scale = MUON_RATE * 0.2 * math.sqrt(height)
    result = old[...] * (1.0 - MUON_RATE * MUON_DECAY) - scale * ortho
    new[...] = result
    copy[...] = result.astype(LOW)


def muon(lanes, height, offset, near, far, old):
    rows, count = old.shape

    def kernel(*refs):
        muon_kernel(lanes, count, height, *refs)

    return pl.pallas_call(
        kernel,
        in_specs=[pl.BlockSpec(memory_space=pltpu.SMEM)]
        + [pl.BlockSpec(memory_space=pltpu.VMEM)] * 3,
        out_specs=[pl.BlockSpec(memory_space=pltpu.VMEM)] * 2,
        out_shape=[
            jax.ShapeDtypeStruct((rows, count), F32),
            jax.ShapeDtypeStruct((rows, count), LOW),
        ],
        compiler_params=pltpu.CompilerParams(vmem_limit_bytes=VMEM_LIMIT),
        cost_estimate=pl.CostEstimate(
            flops=9_000_000_000, bytes_accessed=2_000_000, transcendentals=10
        ),
        name="muon",
    )(offset, near, far, old)


def exchange(x, axis, mask):
    size = lax.axis_size(axis)
    return lax.ppermute(x, axis, [(i, i ^ mask) for i in range(size)])


def place_masks(size):
    masks = [0]
    bit = size // 2
    while bit >= 1:
        masks = masks + [m ^ bit for m in masks]
        bit //= 2
    return masks


def over_columns(own):
    size = lax.axis_size("dp")
    sent = jnp.broadcast_to(own[None], (size, *own.shape))
    got = lax.all_to_all(sent, "dp", split_axis=0, concat_axis=0, tiled=True)
    return got.reshape(size * own.shape[0], own.shape[1])


def over_rows(own):
    size = lax.axis_size("ns")
    held = own[None]
    bit = size // 2
    while bit > 1:
        held = jnp.concatenate([held, exchange(held, "ns", bit)])
        bit //= 2
    return held, exchange(held, "ns", 1)


def sum_owned(grad):
    size = grad.shape[0]
    held = grad
    bit = 1
    while bit < size:
        half = held.shape[0] // 2
        got = exchange(held[half:], "ns", bit)
        held = (held[:half].astype(F32) + got.astype(F32)).astype(LOW)
        bit *= 2
    devices = lax.axis_size("dp")
    pieces = held.reshape(devices, -1, held.shape[-1])
    got = lax.all_to_all(pieces, "dp", split_axis=0, concat_axis=0, tiled=True)
    return jnp.sum(got.astype(F32), axis=0)


def widened(arrays, lanes):
    joined = jnp.concatenate(arrays, axis=1)
    return jnp.pad(joined, ((0, 0), (0, lanes - joined.shape[1])))


def per_device(
    tokens,
    cotangent,
    segment,
    valid_rows,
    qkv_weight,
    proj_weight,
    fc1_weight,
    fc2_weight,
    qkv_moment,
    proj_moment,
    fc1_moment,
    fc2_moment,
    vectors,
    vector_moment,
    vector_square,
):
    rows, width = tokens.shape
    ns = lax.axis_size("ns")
    qkv_w, proj_w, fc1_w, fc2_w = (w.T for w in (qkv_weight, proj_weight, fc1_weight, fc2_weight))
    qkv_m, proj_m, fc1_m, fc2_m = (w.T for w in (qkv_moment, proj_moment, fc1_moment, fc2_moment))
    share, count = qkv_w.shape
    vec_rows = vectors.shape[0]
    first_lanes = width
    later_lanes = 2 * width + SUB

    index = lax.axis_index("ns")
    masks = place_masks(ns)
    owners = jnp.stack([index ^ mask for mask in masks]).astype(jnp.int32)
    places = jnp.stack(
        [sum(jnp.where(owners[p] == b, p, 0) for p in range(ns)) for b in range(ns)]
    ).astype(jnp.int32)
    offset = (lax.axis_index("dp") * share).astype(jnp.int32)[None]

    numbers = jnp.where(
        valid_rows > 0, segment, rows + jnp.arange(rows, dtype=jnp.int32)
    ).astype(F32)
    ids = jnp.pad(numbers, (MARGIN, MARGIN), constant_values=-1.0).reshape(-1, SUB)
    ids = jnp.pad(ids, ((0, -ids.shape[0] % 8), (0, 0)), constant_values=-1.0)

    first_shard = widened([qkv_w, vectors.T], first_lanes).astype(LOW)
    later_shard = widened([fc1_w, fc2_w, proj_w], later_lanes).astype(LOW)
    first_all = jnp.concatenate(over_rows(over_columns(first_shard)))
    later_all = jnp.concatenate(over_rows(over_columns(later_shard)))

    qkv, mixed, expos, inverse, weight, vector_full = attend_forward(
        places, first_all, tokens, ids
    )
    output, grad_residual, grad_mixed, later_grad, sums = mlp_both(
        places, owners, later_all, vector_full, mixed, tokens, cotangent
    )
    later_owned = sum_owned(later_grad)
    input_grad, first_grad = attend_backward(
        places, weight, vector_full, sums, qkv, expos, inverse, mixed, grad_mixed, tokens,
        grad_residual,
    )
    first_owned = sum_owned(first_grad)

    later_moment = later_owned + 0.5 * widened([fc1_m, fc2_m, proj_m], later_lanes)
    first_moment = first_owned + 0.5 * widened([qkv_m], first_lanes)
    later_near, later_far = over_rows(over_columns(later_moment.astype(LOW)))
    first_near, first_far = over_rows(over_columns(first_moment.astype(LOW)))

    fc1_new = muon(0, fc1_w.shape[1] * ns, offset, later_near, later_far, fc1_w)
    fc2_new = muon(width, fc2_w.shape[1] * ns, offset, later_near, later_far, fc2_w)
    proj_new = muon(2 * width, proj_w.shape[1] * ns, offset, later_near, later_far, proj_w)
    qkv_new = muon(0, count * ns, offset, first_near, first_far, qkv_w)
    news = (qkv_new, proj_new, fc1_new, fc2_new)
    moments_new = (
        first_moment[:, :count],
        later_moment[:, 2 * width : 2 * width + proj_w.shape[1]],
        later_moment[:, :width],
        later_moment[:, width : 2 * width],
    )

    vector_grad = first_owned[:, count : count + vec_rows].T
    first_new = BETA_ONE * vector_moment + (1.0 - BETA_ONE) * vector_grad
    second_new = BETA_TWO * vector_square + (1.0 - BETA_TWO) * vector_grad * vector_grad
    first_hat = first_new / (1.0 - BETA_ONE**STEP)
    second_hat = second_new / (1.0 - BETA_TWO**STEP)
    vectors_new = vectors - ADAM_RATE * first_hat / (jnp.sqrt(second_hat) + ADAM_EPS)
    return (
        output,
        input_grad,
        *(new[0].T for new in news),
        *(m.T for m in moments_new),
        first_new,
        second_new,
        vectors_new,
        *(new[1].T for new in news),
    )


def solution(mesh):
    rows = P(("dp", "ns"), None)
    flat = P(("dp", "ns"))
    block = P("ns", "dp")
    return jax.shard_map(
        per_device,
        mesh=mesh,
        in_specs=(rows, rows, flat, flat) + (block,) * 11,
        out_specs=(rows, rows) + (block,) * 15,
        check_vma=False,
    )
```

```python
import math

import jax
import jax.numpy as jnp
from jax import lax
from jax.experimental import pallas as pl
from jax.experimental.pallas import tpu as pltpu
from jax.sharding import PartitionSpec as P

HEADS = 6
PAIRS = 3
MARGIN = 128
NS_STEPS = 5
STEP = 10
TILE = 256
MLP_TILE = 256
SUB = 128
SPAN = 384
VEC_LANES = 16
BACK_CALLS = ((0,), (1,), (2,))


EPS_NORM = 1e-06
NEWTON_A = 3.4445
NEWTON_B = -4.775
NEWTON_C = 2.0315
MUON_RATE = 0.2
MUON_DECAY = 0.1
ADAM_RATE = 0.4
BETA_ONE = 0.9
BETA_TWO = 0.999
ADAM_EPS = 1e-08
LOW = jnp.bfloat16
F32 = jnp.float32
TN = (((0,), (0,)), ((), ()))
NT = (((1,), (1,)), ((), ()))
NN = (((1,), (0,)), ((), ()))
VMEM_LIMIT = 56 * 1024 * 1024
ERF_P = 0.3275911
ERF_COEFS = (0.254829592, -0.284496736, 1.421413741, -1.453152027, 1.061405429)


def dot(left, right, dims=NN):
    return lax.dot_general(left, right, dims, preferred_element_type=F32)


def lane_numbers(shape):
    return lax.broadcasted_iota(jnp.int32, shape, len(shape) - 1)


def norm_parts(value):
    center = value - jnp.mean(value, axis=-1, keepdims=True)
    rate = lax.rsqrt(jnp.mean(center * center, axis=-1, keepdims=True) + EPS_NORM)
    return center * rate, rate


def norm_back(grad, normed, rate, gain):
    scaled = grad * gain
    first = jnp.mean(scaled, axis=-1, keepdims=True)
    second = jnp.mean(scaled * normed, axis=-1, keepdims=True)
    return rate * (scaled - first - normed * second)


def gelu_both(value):
    ratio = 1.0 / (1.0 + (ERF_P * 0.5**0.5) * jnp.abs(value))
    decay = jnp.exp2((value * value) * (-0.5 * math.log2(math.e)))
    poly = 0.5 * ERF_COEFS[4]
    for coef in ERF_COEFS[3::-1]:
        poly = poly * ratio + 0.5 * coef
    tail = poly * ratio * decay
    phi = jnp.where(value >= 0, 1.0 - tail, tail)
    return value * phi, phi + value * decay * (1.0 / math.sqrt(2.0 * math.pi))


def halves_of(lanes):
    half = lanes.shape[0] // 2
    return lanes[:half, :SUB], lanes[half:, SUB:]


def block_diagonal(pair):
    half = pair.shape[0] // 2
    empty = jnp.zeros((half, pair.shape[1]), pair.dtype)
    first = jnp.concatenate([pair[:half], empty], axis=1)
    second = jnp.concatenate([empty, pair[half:]], axis=1)
    return jnp.concatenate([first, second], axis=0)


def both_heads(pair):
    first = (lane_numbers((1, SUB)) < SUB // 2).astype(F32).astype(pair.dtype)
    second = (lane_numbers((1, SUB)) >= SUB // 2).astype(F32).astype(pair.dtype)
    return jnp.concatenate([pair * first, pair * second], axis=0)


def fetch(pairs, sems):
    copies = [
        pltpu.make_async_copy(source, target, sems.at[n])
        for n, (source, target) in enumerate(pairs)
    ]
    for copy in copies:
        copy.start()
    for copy in copies:
        copy.wait()


def attend_kernel(
    places,
    near,
    far,
    tokens,
    ids,
    query,
    key,
    value,
    key_turned,
    normed_turned,
    mixed,
    mixed_turned,
    expos,
    inverse,
    weight,
    vectors,
    gathered,
    query_turned,
    value_turned,
    columns,
    sems,
):
    step = pl.program_id(0)
    chunks = pl.num_programs(0) - 1
    width = tokens.shape[1]
    parts, mid = gathered.shape[0], near.shape[0]
    block = 3 * width // parts
    rows_each = 12 // parts

    @pl.when(step == 0)
    def assemble():
        fetch([(near, gathered.at[:mid]), (far, gathered.at[mid:])], sems)
        total = jnp.zeros((width, 3 * width), F32)
        turned = jnp.zeros((width, SUB), F32)
        for number in range(parts):
            piece = gathered[places[number]].astype(F32)
            kept = jnp.where(lane_numbers(piece.shape) < block, piece, 0.0)
            wide = jnp.concatenate([kept, jnp.zeros((width, 2 * width), F32)], axis=1)
            total = total + (pltpu.roll(wide, block * number, 1) if number else wide)
            last = piece[:, 2 * SUB :]
            at = block - 2 * SUB
            lane = lane_numbers(last.shape)
            vec = jnp.where((lane >= at) & (lane < at + rows_each), last, 0.0)
            turned = turned + pltpu.roll(vec, (rows_each * number - at) % SUB, 1)
        weight[...] = total.astype(LOW)
        vectors[...] = turned.T[:VEC_LANES]
        edges = (pl.ds(0, MARGIN), pl.ds(MARGIN + chunks * TILE, MARGIN))
        for edge in edges:
            for ref in (query, key, value):
                ref[edge, :] = jnp.zeros((MARGIN, width), LOW)
            for ref in (key_turned, value_turned):
                ref[:, edge] = jnp.zeros((width, MARGIN), LOW)
        for number in range(chunks * TILE // SUB + 2):
            row = jnp.broadcast_to(ids[number : number + 1, :], (SUB, SUB))
            columns[number * SUB : (number + 1) * SUB, :] = row.T

    @pl.when(step < chunks)
    def project():
        normed, _ = norm_parts(tokens[...].astype(F32))
        normed_turned[...] = normed.astype(LOW).T
        first_in = (normed * vectors[0:1, :] + vectors[1:2, :]).astype(LOW)
        result = dot(first_in, weight[...])
        here = pl.ds(pl.multiple_of(MARGIN + step * TILE, SUB), TILE)
        scale = (width // HEADS) ** (-0.5)
        made = (result[:, :width] + vectors[2:3, :]).astype(LOW) * jnp.asarray(scale, LOW)
        query[here, :] = made
        query_turned[:, here] = made.T
        made = result[:, width : 2 * width].astype(LOW)
        key[here, :] = made
        key_turned[:, here] = made.T
        made = (result[:, 2 * width :] + vectors[3:4, :]).astype(LOW)
        value[here, :] = made
        value_turned[:, here] = made.T

    @pl.when(step > 0)
    def attend():
        ones = jnp.ones((16, SPAN), LOW)
        for sub in range(TILE // SUB):
            tile = (step - 1) * (TILE // SUB) + sub
            start = pl.multiple_of(tile * SUB, SUB)
            near_rows = pl.ds(start, SPAN)
            cols = pl.ds(sub * SUB, SUB)
            same = columns[near_rows, :] == ids[pl.ds(tile + 1, 1), :]
            same = jnp.concatenate([same, same], axis=1)
            for pair in range(PAIRS):
                at = pair * SUB
                heads = pl.ds(at, SUB)
                wanted = block_diagonal(query_turned[heads, pl.ds(start + MARGIN, SUB)])
                scores = jnp.where(same, dot(key[near_rows, heads], wanted), -1e30)
                largest = jnp.max(scores, axis=0, keepdims=True)
                expo = jnp.exp(scores - largest).astype(LOW)
                expos[pair, sub] = expo
                both = dot(jnp.concatenate([value_turned[heads, near_rows], ones], axis=0), expo)
                share = 1.0 / both[SUB : SUB + 1, :]
                first, second = halves_of(both[:SUB])
                first, second = first * share[:, :SUB], second * share[:, SUB:]
                turned = jnp.concatenate([first, second], axis=0)
                mixed_turned[heads, cols] = turned.astype(LOW)
                mixed[cols, heads] = turned.T.astype(LOW)
                inverse[2 * pair : 2 * pair + 1, cols] = share[:, :SUB]
                inverse[2 * pair + 1 : 2 * pair + 2, cols] = share[:, SUB:]


def attend_forward(places, near, far, tokens, ids):
    rows, width = tokens.shape
    chunks = rows // TILE
    tiles = TILE // SUB
    parts = near.shape[0] + far.shape[0]
    now = lambda s: jnp.minimum(s, chunks - 1)
    before = lambda s: jnp.maximum(s - 1, 0)
    whole = lambda *dims: pl.BlockSpec(dims, lambda s, *_: (0,) * len(dims))
    padded = rows + 2 * MARGIN
    return pl.pallas_call(
        attend_kernel,
        grid_spec=pltpu.PrefetchScalarGridSpec(
            num_scalar_prefetch=1,
            grid=(chunks + 1,),
            in_specs=[
                pl.BlockSpec(memory_space=pl.ANY),
                pl.BlockSpec(memory_space=pl.ANY),
                pl.BlockSpec((TILE, width), lambda s, *_: (now(s), 0)),
                whole(*ids.shape),
            ],
            out_specs=[
                whole(padded, width),
                whole(padded, width),
                whole(padded, width),
                whole(width, padded),
                pl.BlockSpec((width, TILE), lambda s, *_: (0, now(s))),
                pl.BlockSpec((TILE, width), lambda s, *_: (before(s), 0)),
                pl.BlockSpec((width, TILE), lambda s, *_: (0, before(s))),
                pl.BlockSpec((PAIRS, tiles, SPAN, 2 * SUB), lambda s, *_: (0, before(s), 0, 0)),
                pl.BlockSpec((8, TILE), lambda s, *_: (0, before(s))),
                whole(width, 3 * width),
                whole(VEC_LANES, width),
            ],
            scratch_shapes=[
                pltpu.VMEM((parts, *near.shape[1:]), LOW),
                pltpu.VMEM((width, padded), LOW),
                pltpu.VMEM((width, padded), LOW),
                pltpu.VMEM((padded, SUB), F32),
                pltpu.SemaphoreType.DMA((2,)),
            ],
        ),
        out_shape=[
            jax.ShapeDtypeStruct((padded, width), LOW),
            jax.ShapeDtypeStruct((padded, width), LOW),
            jax.ShapeDtypeStruct((padded, width), LOW),
            jax.ShapeDtypeStruct((width, padded), LOW),
            jax.ShapeDtypeStruct((width, rows), LOW),
            jax.ShapeDtypeStruct((rows, width), LOW),
            jax.ShapeDtypeStruct((width, rows), LOW),
            jax.ShapeDtypeStruct((PAIRS, rows // SUB, SPAN, 2 * SUB), LOW),
            jax.ShapeDtypeStruct((8, rows), F32),
            jax.ShapeDtypeStruct((width, 3 * width), LOW),
            jax.ShapeDtypeStruct((VEC_LANES, width), F32),
        ],
        compiler_params=pltpu.CompilerParams(vmem_limit_bytes=VMEM_LIMIT),
        cost_estimate=pl.CostEstimate(
            flops=12_000_000_000, bytes_accessed=22_000_000, transcendentals=5_000_000
        ),
        name="attend_forward",
    )(places, near, far, tokens, ids)


def mlp_kernel(
    places,
    owners,
    near,
    far,
    vectors,
    mixed,
    tokens,
    cotangent,
    output,
    grad_residual,
    grad_turned,
    grads_near,
    grads_far,
    sums,
    gathered,
    one_turned,
    two_turned,
    proj,
    proj_turned,
    acc_one,
    acc_two,
    acc_proj,
    proj_parts,
    sems,
):
    step = pl.program_id(0)
    width = tokens.shape[1]
    parts, mid = gathered.shape[0], near.shape[0]
    block = width // parts
    last_at = 2 * width

    @pl.when(step == 0)
    def assemble():
        fetch([(near, gathered.at[:mid]), (far, gathered.at[mid:])], sems)
        total = jnp.zeros((width, width), F32)
        for number in range(parts):
            piece = gathered[places[number], :, last_at:].astype(F32)
            kept = jnp.where(lane_numbers(piece.shape) < block, piece, 0.0)
            wide = jnp.concatenate([kept, jnp.zeros((width, width - SUB), F32)], axis=1)
            total = total + (pltpu.roll(wide, block * number, 1) if number else wide)
        total = total.astype(LOW)
        proj[...] = total
        proj_turned[...] = total.T
        for part in range(parts):
            one_turned[part] = gathered[part, :, :width].T
            two_turned[part] = gathered[part, :, width:last_at].T
        acc_one[...] = jnp.zeros(acc_one.shape, F32)
        acc_two[...] = jnp.zeros(acc_two.shape, F32)
        acc_proj[...] = jnp.zeros(acc_proj.shape, F32)
        sums[...] = jnp.zeros(sums.shape, F32)

    def add_row(row, values):
        sums[pl.ds(row, 1), :] += jnp.sum(values, axis=0, keepdims=True)

    own = mixed[...]
    residual = tokens[...].astype(F32) + dot(own, proj_turned[...]) + vectors[4:5, :]
    normed, rate = norm_parts(residual)
    gain = vectors[5:6, :]
    second_in = (normed * gain + vectors[6:7, :]).astype(LOW)
    out_low = cotangent[...]
    grad_out = out_low.astype(F32)
    second_turned = second_in.T
    out_turned = out_low.T
    result = residual + vectors[7:8, :]
    grad_second = jnp.zeros(residual.shape, F32)
    for part in range(parts):
        one = gathered[part, :, :width]
        two = gathered[part, :, width:last_at]
        row = 8 + owners[part]
        hidden = dot(second_in, one) + vectors[pl.ds(row, 1), :]
        active, slope = gelu_both(hidden)
        active = active.astype(LOW)
        grad_hidden = (dot(out_low, two) * slope).astype(LOW)
        result = result + dot(active, two_turned[part])
        grad_second = grad_second + dot(grad_hidden, one_turned[part])
        acc_one[part] += dot(second_turned, grad_hidden)
        acc_two[part] += dot(out_turned, active)
        add_row(row, grad_hidden.astype(F32))
    output[...] = result.astype(LOW)
    add_row(5, grad_second * normed)
    add_row(6, grad_second)
    add_row(7, grad_out)
    grad_res = grad_out + norm_back(grad_second, normed, rate, gain)
    grad_residual[...] = grad_res
    branch = grad_res.astype(LOW)
    branch_turned = branch.T
    add_row(4, branch.astype(F32))
    acc_proj[...] += dot(branch_turned, own)
    grad_turned[...] = dot(proj_turned[...], branch_turned).astype(LOW)

    @pl.when(step == pl.num_programs(0) - 1)
    def finish():
        total = acc_proj[...]
        for number in range(parts):
            turned = pltpu.roll(total, (width - block * number) % width, 1) if number else total
            proj_parts[places[number]] = turned[:, :SUB].astype(LOW)
        for part in range(parts):
            ref, at = (grads_near, part) if part < mid else (grads_far, part - mid)
            ref[at, :, :width] = acc_one[part].astype(LOW)
            ref[at, :, width:last_at] = acc_two[part].astype(LOW)
            ref[at, :, last_at:] = proj_parts[part]


def mlp_both(places, owners, near, far, vectors, mixed, tokens, cotangent):
    rows, width = tokens.shape
    parts = near.shape[0] + far.shape[0]
    tile = pl.BlockSpec((MLP_TILE, width), lambda s, *_: (s, 0))
    whole = lambda *dims: pl.BlockSpec(dims, lambda s, *_: (0,) * len(dims))
    return pl.pallas_call(
        mlp_kernel,
        grid_spec=pltpu.PrefetchScalarGridSpec(
            num_scalar_prefetch=2,
            grid=(rows // MLP_TILE,),
            in_specs=[
                pl.BlockSpec(memory_space=pl.ANY),
                pl.BlockSpec(memory_space=pl.ANY),
                whole(*vectors.shape),
                tile,
                tile,
                tile,
            ],
            out_specs=[
                tile,
                tile,
                pl.BlockSpec((width, MLP_TILE), lambda s, *_: (0, s)),
                whole(*near.shape),
                whole(*far.shape),
                whole(*vectors.shape),
            ],
            scratch_shapes=[
                pltpu.VMEM((parts, *near.shape[1:]), LOW),
                pltpu.VMEM((parts, width, width), LOW),
                pltpu.VMEM((parts, width, width), LOW),
                pltpu.VMEM((width, width), LOW),
                pltpu.VMEM((width, width), LOW),
                pltpu.VMEM((parts, width, width), F32),
                pltpu.VMEM((parts, width, width), F32),
                pltpu.VMEM((width, width), F32),
                pltpu.VMEM((parts, width, SUB), LOW),
                pltpu.SemaphoreType.DMA((2,)),
            ],
        ),
        out_shape=[
            jax.ShapeDtypeStruct((rows, width), LOW),
            jax.ShapeDtypeStruct((rows, width), F32),
            jax.ShapeDtypeStruct((width, rows), LOW),
            jax.ShapeDtypeStruct(near.shape, LOW),
            jax.ShapeDtypeStruct(far.shape, LOW),
            jax.ShapeDtypeStruct(vectors.shape, F32),
        ],
        compiler_params=pltpu.CompilerParams(vmem_limit_bytes=VMEM_LIMIT),
        cost_estimate=pl.CostEstimate(
            flops=34_000_000_000, bytes_accessed=20_000_000, transcendentals=6_000_000
        ),
        name="mlp_both",
    )(places, owners, near, far, vectors, mixed, tokens, cotangent)


def attend_back_kernel(
    pairs,
    query,
    key_turned,
    value,
    expos,
    inverse,
    mixed_turned,
    grad_turned,
    normed_turned,
    grad_qkv,
    normed_sums,
    column_sums,
    grad_query,
    acc_key,
    acc_value,
    acc_sums,
):
    step = pl.program_id(0)
    chunks = pl.num_programs(0) - 1
    count = len(pairs)
    scale = (SUB // 2) ** (-0.5)

    @pl.when(step == 0)
    def clear():
        acc_key[...] = jnp.zeros(acc_key.shape, F32)
        acc_value[...] = jnp.zeros(acc_value.shape, F32)
        normed_sums[...] = jnp.zeros(normed_sums.shape, F32)
        acc_sums[...] = jnp.zeros(acc_sums.shape, F32)

    @pl.when(step < chunks)
    def attend():
        for sub in range(TILE // SUB):
            tile = step * (TILE // SUB) + sub
            start = pl.multiple_of(tile * SUB, SUB)
            near_rows = pl.ds(start, SPAN)
            cols = pl.ds(sub * SUB, SUB)
            for number, pair in enumerate(pairs):
                heads = pl.ds(number * SUB, SUB)
                half = SUB // 2
                grad = grad_turned[heads, cols].astype(F32)
                first = grad[:half] * inverse[2 * pair : 2 * pair + 1, cols]
                second = grad[half:] * inverse[2 * pair + 1 : 2 * pair + 2, cols]
                seen = mixed_turned[heads, cols].astype(F32)
                inner = jnp.concatenate(
                    [
                        jnp.sum(first * seen[:half], axis=0, keepdims=True),
                        jnp.sum(second * seen[half:], axis=0, keepdims=True),
                    ],
                    axis=1,
                )
                grad = jnp.concatenate([first, second], axis=0).astype(LOW)
                expo = expos[number, sub]
                slopes = dot(value[near_rows, heads], block_diagonal(grad)) - inner
                scores = (expo.astype(F32) * slopes).astype(LOW)
                first, second = halves_of(dot(key_turned[heads, near_rows], scores))
                turned = jnp.concatenate([first, second], axis=0) * scale
                grad_query[pl.ds(start, SUB), heads] = turned.astype(LOW).T
                wanted = both_heads(query[pl.ds(start + MARGIN, SUB), heads])
                acc_key[near_rows, heads] += dot(scores, wanted)
                acc_value[near_rows, heads] += dot(expo, both_heads(grad.T))

    @pl.when(step > 0)
    def collect():
        here = pl.ds(pl.multiple_of((step - 1) * TILE, SUB), TILE)
        there = pl.ds(pl.multiple_of((step - 1) * TILE + MARGIN, SUB), TILE)
        parts = (
            grad_query[here, :],
            acc_key[there, :].astype(LOW),
            acc_value[there, :].astype(LOW),
        )
        joined = jnp.concatenate(parts, axis=1)
        grad_qkv[...] = joined
        normed_sums[...] += dot(normed_turned[...], joined)
        acc_sums[0:1, :] += jnp.sum(joined.astype(F32), axis=0, keepdims=True)

    @pl.when(step == chunks)
    def finish():
        column_sums[...] = acc_sums[...]


def attend_backward(
    pairs, query, key_turned, value, expos, inverse, mixed_turned, grad_turned, normed_turned
):
    width, rows = normed_turned.shape
    padded = query.shape[0]
    chunks = rows // TILE
    tiles = TILE // SUB
    count = len(pairs)
    lanes = count * SUB
    which = pairs[0] // count
    now = lambda s: jnp.minimum(s, chunks - 1)
    before = lambda s: jnp.maximum(s - 1, 0)
    normal = pl.BlockSpec((padded, lanes), lambda s: (0, which))
    turned = pl.BlockSpec((lanes, TILE), lambda s: (which, now(s)))

    def kernel(*refs):
        attend_back_kernel(pairs, *refs)

    return pl.pallas_call(
        kernel,
        grid=(chunks + 1,),
        in_specs=[
            normal,
            pl.BlockSpec((lanes, padded), lambda s: (which, 0)),
            normal,
            pl.BlockSpec((count, tiles, SPAN, 2 * SUB), lambda s: (which, now(s), 0, 0)),
            pl.BlockSpec((8, TILE), lambda s: (0, now(s))),
            turned,
            turned,
            pl.BlockSpec((width, TILE), lambda s: (0, before(s))),
        ],
        out_specs=[
            pl.BlockSpec((TILE, 3 * lanes), lambda s: (before(s), 0)),
            pl.BlockSpec((width, 3 * lanes), lambda s: (0, 0)),
            pl.BlockSpec((8, 3 * lanes), lambda s: (0, 0)),
        ],
        out_shape=[
            jax.ShapeDtypeStruct((rows, 3 * lanes), LOW),
            jax.ShapeDtypeStruct((width, 3 * lanes), F32),
            jax.ShapeDtypeStruct((8, 3 * lanes), F32),
        ],
        scratch_shapes=[
            pltpu.VMEM((rows, lanes), LOW),
            pltpu.VMEM((padded, lanes), F32),
            pltpu.VMEM((padded, lanes), F32),
            pltpu.VMEM((8, 3 * lanes), F32),
        ],
        compiler_params=pltpu.CompilerParams(vmem_limit_bytes=VMEM_LIMIT),
        cost_estimate=pl.CostEstimate(
            flops=5_000_000_000 * count, bytes_accessed=7_000_000 * count, transcendentals=0
        ),
        name="attend_backward",
    )(query, key_turned, value, expos, inverse, mixed_turned, grad_turned, normed_turned)


def in_order(pieces):
    lanes = pieces[0].shape[1] // 3
    return jnp.concatenate(
        [piece[:, n * lanes : (n + 1) * lanes] for n in range(3) for piece in pieces], axis=1
    )


def weight_grad_kernel(places, weight, vectors, sums, *refs):
    count = (len(refs) - 4) // 2
    normed_sums, column_sums = refs[:count], refs[count : 2 * count]
    near, far, blocks, rows = refs[2 * count :]
    width = weight.shape[0]
    parts, mid = blocks.shape[0], near.shape[0]
    block = 3 * width // parts
    rows_each = 12 // parts
    total = in_order([ref[...] for ref in normed_sums])
    columns = in_order([ref[0:1, :] for ref in column_sums])
    wide = weight[...].astype(F32)
    grad_gain = jnp.sum(total * wide, axis=1, keepdims=True)
    grad_shift = jnp.sum(wide * columns, axis=1, keepdims=True)
    rows[...] = jnp.zeros(rows.shape, F32)
    rows[0:VEC_LANES, :] = sums[...]
    rows[2:3, :] = columns[:, :width]
    rows[3:4, :] = columns[:, 2 * width :]
    rows[VEC_LANES : 2 * VEC_LANES, :] = vectors[...]
    turned = rows[...].T
    gain = turned[:, VEC_LANES : VEC_LANES + 1]
    shift = turned[:, VEC_LANES + 1 : VEC_LANES + 2]
    lane = lane_numbers(turned.shape)
    turned = jnp.where(lane == 0, grad_gain, jnp.where(lane == 1, grad_shift, turned))
    total = total * gain + shift * columns
    at = block - 2 * SUB
    for number in range(parts):
        away = (3 * width - block * number) % (3 * width)
        piece = (pltpu.roll(total, away, 1) if number else total)[:, :width]
        vec = pltpu.roll(turned, (at - rows_each * number) % SUB, 1)
        last = jnp.where(lane < at, piece[:, 2 * SUB :], 0.0)
        last = jnp.where((lane >= at) & (lane < at + rows_each), vec, last)
        blocks[places[number], :, : 2 * SUB] = piece[:, : 2 * SUB].astype(LOW)
        blocks[places[number], :, 2 * SUB :] = last.astype(LOW)
    near[...] = blocks[:mid]
    far[...] = blocks[mid:]


def weight_grad(places, weight, vectors, sums, normed_sums, column_sums):
    width = weight.shape[0]
    parts = places.shape[0]
    half = jax.ShapeDtypeStruct((parts // 2, width, width), LOW)
    vmem = pl.BlockSpec(memory_space=pltpu.VMEM)
    return pl.pallas_call(
        weight_grad_kernel,
        in_specs=[pl.BlockSpec(memory_space=pltpu.SMEM)] + [vmem] * (3 + 2 * len(normed_sums)),
        out_specs=[vmem, vmem],
        out_shape=[half, half],
        scratch_shapes=[pltpu.VMEM((parts, width, width), LOW), pltpu.VMEM((SUB, width), F32)],
        compiler_params=pltpu.CompilerParams(vmem_limit_bytes=VMEM_LIMIT),
        cost_estimate=pl.CostEstimate(
            flops=3_000_000, bytes_accessed=5_000_000, transcendentals=0
        ),
        name="weight_grad",
    )(places, weight, vectors, sums, *normed_sums, *column_sums)


def input_grad_kernel(weight, vectors, tokens, grad_residual, *refs):
    grads, (input_grad, turned) = refs[:-2], refs[-2:]

    @pl.when(pl.program_id(0) == 0)
    def assemble():
        turned[...] = weight[...].T

    joined = in_order([ref[...] for ref in grads])
    normed, rate = norm_parts(tokens[...].astype(F32))
    back = norm_back(dot(joined, turned[...]), normed, rate, vectors[0:1, :])
    input_grad[...] = (grad_residual[...] + back).astype(LOW)


def input_gradient(weight, vectors, tokens, grad_residual, grads):
    rows, width = tokens.shape
    tile = pl.BlockSpec((TILE, width), lambda s: (s, 0))
    whole = lambda ref: pl.BlockSpec(ref.shape, lambda s: (0, 0))
    return pl.pallas_call(
        input_grad_kernel,
        grid=(rows // TILE,),
        in_specs=[whole(weight), whole(vectors), tile, tile]
        + [pl.BlockSpec((TILE, grad.shape[1]), lambda s: (s, 0)) for grad in grads],
        out_specs=tile,
        out_shape=jax.ShapeDtypeStruct((rows, width), LOW),
        scratch_shapes=[pltpu.VMEM((3 * width, width), LOW)],
        compiler_params=pltpu.CompilerParams(vmem_limit_bytes=VMEM_LIMIT),
        cost_estimate=pl.CostEstimate(
            flops=4_000_000_000, bytes_accessed=13_000_000, transcendentals=2048
        ),
        name="input_gradient",
    )(weight, vectors, tokens, grad_residual, *grads)


def halves(value):
    high = value.astype(LOW)
    return high, (value - high.astype(F32)).astype(LOW)


def dot_three(left, right):
    tall = jnp.concatenate([right[0], right[0], right[1]], axis=0)
    return dot(jnp.concatenate([left[0], left[1], left[0]], axis=1), tall)


def muon_kernel(count, height, offset, near, far, old, new, copy):
    depth, wide = near.shape[1:]
    rows = old.shape[0]

    def piece(ref, number):
        value = ref[number]
        if wide != count:
            value = jnp.where(lane_numbers(value.shape) < count, value.astype(F32), 0.0).astype(LOW)
        return value

    own = piece(near, 0)
    gram = dot(own, own, NT)
    for ref, number in [(near, n) for n in range(1, near.shape[0])] + [
        (far, n) for n in range(far.shape[0])
    ]:
        part = piece(ref, number)
        gram = gram + dot(part, part, NT)
    down = lax.broadcasted_iota(jnp.int32, (depth, depth), 0)
    eye = (down == lane_numbers((depth, depth))).astype(F32)
    norm = 1.0 / (jnp.sqrt(jnp.sum(gram * eye, keepdims=True)) + 1e-07)
    gram = gram * (norm * norm)
    tall = -(-rows // 8) * 8
    place = lax.broadcasted_iota(jnp.int32, (tall, depth), 0) + offset[0]
    left = jnp.where(place == lane_numbers((tall, depth)), norm, 0.0)
    for step in range(NS_STEPS):
        pair = halves(gram)
        once = dot_three(halves(left), pair)
        if step < NS_STEPS - 1:
            square = dot_three(pair, pair)
            twice = dot_three(halves(left), halves(square))
            poly = halves(NEWTON_A * eye + NEWTON_B * gram + NEWTON_C * square)
            gram = dot_three(halves(dot_three(pair, poly)), poly)
        else:
            twice = dot_three(halves(once), pair)
        left = NEWTON_A * left + NEWTON_B * once + NEWTON_C * twice
    high, rest = halves(left)
    ortho = (dot(high, own) + dot(rest, own))[:rows, :count]
    scale = MUON_RATE * 0.2 * math.sqrt(height)
    result = old[...] * (1.0 - MUON_RATE * MUON_DECAY) - scale * ortho
    new[...] = result
    copy[...] = result.astype(LOW)


def muon(lanes, height, offset, near, far, old):
    rows, count = old.shape
    wide = -(-count // SUB) * SUB

    def kernel(*refs):
        muon_kernel(count, height, *refs)

    part = lambda ref: pl.BlockSpec(
        (ref.shape[0], ref.shape[1], wide), lambda s: (0, 0, lanes // wide)
    )
    own = pl.BlockSpec((rows, count), lambda s: (0, 0))
    return pl.pallas_call(
        kernel,
        grid=(1,),
        in_specs=[pl.BlockSpec(memory_space=pltpu.SMEM), part(near), part(far), own],
        out_specs=[own, own],
        out_shape=[
            jax.ShapeDtypeStruct((rows, count), F32),
            jax.ShapeDtypeStruct((rows, count), LOW),
        ],
        compiler_params=pltpu.CompilerParams(vmem_limit_bytes=VMEM_LIMIT),
        cost_estimate=pl.CostEstimate(
            flops=9_000_000_000, bytes_accessed=2_000_000, transcendentals=10
        ),
        name="muon",
    )(offset, near, far, old)


def exchange(x, axis, mask):
    size = lax.axis_size(axis)
    return lax.ppermute(x, axis, [(i, i ^ mask) for i in range(size)])


def place_masks(size):
    masks = [0]
    bit = size // 2
    while bit >= 1:
        masks = masks + [m ^ bit for m in masks]
        bit //= 2
    return masks


def over_columns(own):
    size = lax.axis_size("dp")
    sent = jnp.broadcast_to(own[None], (size, *own.shape))
    got = lax.all_to_all(sent, "dp", split_axis=0, concat_axis=0, tiled=True)
    return got.reshape(size * own.shape[0], own.shape[1])


def over_far_rows(own):
    held = own[None]
    bit = lax.axis_size("ns") // 2
    while bit > 1:
        held = jnp.concatenate([held, exchange(held, "ns", bit)])
        bit //= 2
    return held


def sum_owned(near, far):
    low = lambda keep, got: (keep.astype(F32) + got.astype(F32)).astype(LOW)
    held = low(near, exchange(far, "ns", 1))
    bit = 2
    while held.shape[0] > 1:
        half = held.shape[0] // 2
        held = low(held[:half], exchange(held[half:], "ns", bit))
        bit *= 2
    devices = lax.axis_size("dp")
    pieces = held.reshape(devices, -1, held.shape[-1])
    got = lax.all_to_all(pieces, "dp", split_axis=0, concat_axis=0, tiled=True)
    return jnp.sum(got.astype(F32), axis=0)


def widened(arrays, lanes):
    joined = jnp.concatenate(arrays, axis=1)
    return jnp.pad(joined, ((0, 0), (0, lanes - joined.shape[1])))


def per_device(
    tokens,
    cotangent,
    segment,
    valid_rows,
    qkv_weight,
    proj_weight,
    fc1_weight,
    fc2_weight,
    qkv_moment,
    proj_moment,
    fc1_moment,
    fc2_moment,
    vectors,
    vector_moment,
    vector_square,
):
    rows, width = tokens.shape
    ns = lax.axis_size("ns")
    qkv_w, proj_w, fc1_w, fc2_w = (w.T for w in (qkv_weight, proj_weight, fc1_weight, fc2_weight))
    qkv_m, proj_m, fc1_m, fc2_m = (w.T for w in (qkv_moment, proj_moment, fc1_moment, fc2_moment))
    share, count = qkv_w.shape
    vec_rows = vectors.shape[0]
    first_lanes = width
    later_lanes = 2 * width + SUB

    index = lax.axis_index("ns")
    masks = place_masks(ns)
    owners = jnp.stack([index ^ mask for mask in masks]).astype(jnp.int32)
    places = jnp.stack(
        [sum(jnp.where(owners[p] == b, p, 0) for p in range(ns)) for b in range(ns)]
    ).astype(jnp.int32)
    offset = (lax.axis_index("dp") * share).astype(jnp.int32)[None]

    numbers = jnp.where(
        valid_rows > 0, segment, rows + jnp.arange(rows, dtype=jnp.int32)
    ).astype(F32)
    ids = jnp.pad(numbers, (MARGIN, MARGIN), constant_values=-1.0).reshape(-1, SUB)
    ids = jnp.pad(ids, ((0, -ids.shape[0] % 8), (0, 0)), constant_values=-1.0)

    first_shard = widened([qkv_w, vectors.T], first_lanes).astype(LOW)
    later_shard = widened([fc1_w, fc2_w, proj_w], later_lanes).astype(LOW)
    first_near = over_far_rows(over_columns(first_shard))
    first_far = exchange(first_near, "ns", 1)
    later_near = over_far_rows(over_columns(later_shard))

    (query, key, value, key_turned, normed_turned, mixed, mixed_turned, expos, inverse, weight,
     vector_full) = attend_forward(places, first_near, first_far, tokens, ids)
    later_near, mixed = lax.optimization_barrier((later_near, mixed))
    later_far = exchange(later_near, "ns", 1)
    output, grad_residual, grad_turned, grads_near, grads_far, sums = mlp_both(
        places, owners, later_near, later_far, vector_full, mixed, tokens, cotangent
    )
    later_owned = sum_owned(grads_near, grads_far)
    grads, normed_sums, column_sums = zip(
        *(
            attend_backward(
                pairs, query, key_turned, value, expos, inverse, mixed_turned, grad_turned,
                normed_turned,
            )
            for pairs in BACK_CALLS
        )
    )
    grads_near, grads_far = weight_grad(
        places, weight, vector_full, sums, normed_sums, column_sums
    )
    first_owned = sum_owned(grads_near, grads_far)
    input_grad = input_gradient(weight, vector_full, tokens, grad_residual, grads)

    later_moment = later_owned + 0.5 * widened([fc1_m, fc2_m, proj_m], later_lanes)
    later_near = over_far_rows(over_columns(later_moment.astype(LOW)))
    later_far = exchange(later_near, "ns", 1)
    first_moment = first_owned + 0.5 * widened([qkv_m], first_lanes)
    first_near = over_far_rows(over_columns(first_moment.astype(LOW)))
    first_far = exchange(first_near, "ns", 1)

    fc1_new = muon(0, fc1_w.shape[1] * ns, offset, later_near, later_far, fc1_w)
    fc2_new = muon(width, fc2_w.shape[1] * ns, offset, later_near, later_far, fc2_w)
    proj_new = muon(2 * width, proj_w.shape[1] * ns, offset, later_near, later_far, proj_w)
    qkv_new = muon(0, count * ns, offset, first_near, first_far, qkv_w)
    news = (qkv_new, proj_new, fc1_new, fc2_new)
    moments_new = (
        first_moment[:, :count],
        later_moment[:, 2 * width : 2 * width + proj_w.shape[1]],
        later_moment[:, :width],
        later_moment[:, width : 2 * width],
    )

    vector_grad = first_owned[:, count : count + vec_rows].T
    first_new = BETA_ONE * vector_moment + (1.0 - BETA_ONE) * vector_grad
    second_new = BETA_TWO * vector_square + (1.0 - BETA_TWO) * vector_grad * vector_grad
    first_hat = first_new / (1.0 - BETA_ONE**STEP)
    second_hat = second_new / (1.0 - BETA_TWO**STEP)
    vectors_new = vectors - ADAM_RATE * first_hat / (jnp.sqrt(second_hat) + ADAM_EPS)
    return (
        output,
        input_grad,
        *(new[0].T for new in news),
        *(m.T for m in moments_new),
        first_new,
        second_new,
        vectors_new,
        *(new[1].T for new in news),
    )


def solution(mesh):
    rows = P(("dp", "ns"), None)
    flat = P(("dp", "ns"))
    block = P("ns", "dp")
    return jax.shard_map(
        per_device,
        mesh=mesh,
        in_specs=(rows, rows, flat, flat) + (block,) * 11,
        out_specs=(rows, rows) + (block,) * 15,
        check_vma=False,
    )
```

```python
import math

import jax
import jax.numpy as jnp
from jax import lax
from jax.experimental import pallas as pl
from jax.experimental.pallas import tpu as pltpu
from jax.sharding import PartitionSpec as P

HEADS = 6
PAIRS = 3
MARGIN = 128
NS_STEPS = 5
STEP = 10
TILE = 256
MLP_TILE = 512
FF_CHUNK = 512
SUB = 128
SPAN = 384
VEC_LANES = 16
BACK_CALLS = ((0, 1, 2),)


EPS_NORM = 1e-06
NEWTON_A = 3.4445
NEWTON_B = -4.775
NEWTON_C = 2.0315
MUON_RATE = 0.2
MUON_DECAY = 0.1
ADAM_RATE = 0.4
BETA_ONE = 0.9
BETA_TWO = 0.999
ADAM_EPS = 1e-08
LOW = jnp.bfloat16
F32 = jnp.float32
TN = (((0,), (0,)), ((), ()))
NT = (((1,), (1,)), ((), ()))
NN = (((1,), (0,)), ((), ()))
VMEM_LIMIT = 56 * 1024 * 1024
ERF_P = 0.3275911
ERF_COEFS = (0.254829592, -0.284496736, 1.421413741, -1.453152027, 1.061405429)


def dot(left, right, dims=NN):
    return lax.dot_general(left, right, dims, preferred_element_type=F32)


def lane_numbers(shape):
    return lax.broadcasted_iota(jnp.int32, shape, len(shape) - 1)


def norm_parts(value):
    center = value - jnp.mean(value, axis=-1, keepdims=True)
    rate = lax.rsqrt(jnp.mean(center * center, axis=-1, keepdims=True) + EPS_NORM)
    return center * rate, rate


def norm_back(grad, normed, rate, gain):
    scaled = grad * gain
    first = jnp.mean(scaled, axis=-1, keepdims=True)
    second = jnp.mean(scaled * normed, axis=-1, keepdims=True)
    return rate * (scaled - first - normed * second)


def gelu_both(value):
    ratio = 1.0 / (1.0 + (ERF_P * 0.5**0.5) * jnp.abs(value))
    decay = jnp.exp2((value * value) * (-0.5 * math.log2(math.e)))
    poly = 0.5 * ERF_COEFS[4]
    for coef in ERF_COEFS[3::-1]:
        poly = poly * ratio + 0.5 * coef
    tail = poly * ratio * decay
    phi = jnp.where(value >= 0, 1.0 - tail, tail)
    return value * phi, phi + value * decay * (1.0 / math.sqrt(2.0 * math.pi))


def gelu_rows(hidden, grad):
    active, back = [], []
    for row in range(0, hidden.shape[0], 16):
        value, slope = gelu_both(hidden[row : row + 16])
        active.append(value.astype(LOW))
        back.append((grad[row : row + 16] * slope).astype(LOW))
    return jnp.concatenate(active, axis=0), jnp.concatenate(back, axis=0)


def halves_of(lanes):
    half = lanes.shape[0] // 2
    return lanes[:half, :SUB], lanes[half:, SUB:]


def staged(count, first, second, third):
    made = [first(0)]
    kept = None
    for n in range(count):
        if n + 1 < count:
            made.append(first(n + 1))
        if kept is not None:
            third(n - 1, kept)
        kept = second(n, made[n])
        made[n] = None
    third(count - 1, kept)


def both_heads(pair):
    first = (lane_numbers((1, SUB)) < SUB // 2).astype(F32).astype(pair.dtype)
    second = (lane_numbers((1, SUB)) >= SUB // 2).astype(F32).astype(pair.dtype)
    return jnp.concatenate([pair * first, pair * second], axis=0)


def fetch(pairs, sems):
    copies = [
        pltpu.make_async_copy(source, target, sems.at[n])
        for n, (source, target) in enumerate(pairs)
    ]
    for copy in copies:
        copy.start()
    for copy in copies:
        copy.wait()


def attend_kernel(
    places,
    near,
    far,
    tokens,
    ids,
    query,
    key,
    value,
    key_turned,
    normed_turned,
    mixed,
    probs,
    weight,
    vectors,
    gathered,
    pair_weight,
    value_turned,
    columns,
    shifts,
    sems,
):
    step = pl.program_id(0)
    chunks = pl.num_programs(0) - 1
    width = tokens.shape[1]
    parts, mid = gathered.shape[0], near.shape[0]
    block = 3 * width // parts
    rows_each = 12 // parts

    @pl.when(step == 0)
    def assemble():
        fetch([(near, gathered.at[:mid]), (far, gathered.at[mid:])], sems)
        total = jnp.zeros((width, 3 * width), F32)
        turned = jnp.zeros((width, SUB), F32)
        for number in range(parts):
            piece = gathered[places[number]].astype(F32)
            kept = jnp.where(lane_numbers(piece.shape) < block, piece, 0.0)
            wide = jnp.concatenate([kept, jnp.zeros((width, 2 * width), F32)], axis=1)
            total = total + (pltpu.roll(wide, block * number, 1) if number else wide)
            last = piece[:, 2 * SUB :]
            at = block - 2 * SUB
            lane = lane_numbers(last.shape)
            vec = jnp.where((lane >= at) & (lane < at + rows_each), last, 0.0)
            turned = turned + pltpu.roll(vec, (rows_each * number - at) % SUB, 1)
        total = total.astype(LOW)
        weight[...] = total
        pair_weight[...] = total[:, width:].T
        vectors[...] = turned.T[:VEC_LANES]
        shifts[...] = turned
        edges = (pl.ds(0, MARGIN), pl.ds(MARGIN + chunks * TILE, MARGIN))
        for edge in edges:
            for ref in (query, key, value):
                ref[edge, :] = jnp.zeros((MARGIN, width), LOW)
            for ref in (key_turned, value_turned):
                ref[:, edge] = jnp.zeros((width, MARGIN), LOW)
        for number in range(chunks * TILE // SUB + 2):
            row = jnp.broadcast_to(ids[number : number + 1, :], (SUB, SUB))
            columns[number * SUB : (number + 1) * SUB, :] = row.T

    @pl.when(step < chunks)
    def project():
        normed, _ = norm_parts(tokens[...].astype(F32))
        normed_turned[...] = normed.astype(LOW).T
        first_in = (normed * vectors[0:1, :] + vectors[1:2, :]).astype(LOW)
        result = dot(first_in, weight[...])
        turned = dot(pair_weight[...], first_in, NT)
        here = pl.ds(pl.multiple_of(MARGIN + step * TILE, SUB), TILE)
        scale = (width // HEADS) ** (-0.5)
        made = (result[:, :width] + vectors[2:3, :]).astype(LOW) * jnp.asarray(scale, LOW)
        query[here, :] = made
        key[here, :] = result[:, width : 2 * width].astype(LOW)
        value[here, :] = (result[:, 2 * width :] + vectors[3:4, :]).astype(LOW)
        key_turned[:, here] = turned[:width].astype(LOW)
        value_turned[:, here] = (turned[width:] + shifts[:, 3:4]).astype(LOW)

    @pl.when(step > 0)
    def attend():
        def place(number):
            sub, pair = number // PAIRS, number % PAIRS
            tile = (step - 1) * (TILE // SUB) + sub
            start = pl.multiple_of(tile * SUB, SUB)
            return sub, pair, tile, start, pl.ds(start, SPAN), pl.ds(pair * SUB, SUB)

        def score(number):
            _, _, _, start, near_rows, heads = place(number)
            wanted = both_heads(query[pl.ds(start + MARGIN, SUB), heads])
            return dot(key[near_rows, heads], wanted, NT)

        def soften(number, scores):
            sub, pair, tile, _, near_rows, _ = place(number)
            row = ids[pl.ds(tile + 1, 1), :]
            both = []
            for head in range(2):
                same = columns[near_rows, :] == row
                own = jnp.where(same, scores[:, head * SUB : (head + 1) * SUB], -1e30)
                expo = jnp.exp(own - jnp.max(own, axis=0, keepdims=True))
                share = 1.0 / jnp.sum(expo, axis=0, keepdims=True)
                both.append((expo * share).astype(LOW))
            prob = jnp.concatenate(both, axis=1)
            probs[pair, sub] = prob
            return prob

        def mix(number, prob):
            sub, _, _, _, near_rows, heads = place(number)
            first, second = halves_of(dot(value_turned[heads, near_rows], prob))
            turned = jnp.concatenate([first, second], axis=0).astype(LOW)
            mixed[pl.ds(sub * SUB, SUB), heads] = turned.T

        staged(TILE // SUB * PAIRS, score, soften, mix)


def attend_forward(places, near, far, tokens, ids):
    rows, width = tokens.shape
    chunks = rows // TILE
    tiles = TILE // SUB
    parts = near.shape[0] + far.shape[0]
    now = lambda s: jnp.minimum(s, chunks - 1)
    before = lambda s: jnp.maximum(s - 1, 0)
    whole = lambda *dims: pl.BlockSpec(dims, lambda s, *_: (0,) * len(dims))
    padded = rows + 2 * MARGIN
    return pl.pallas_call(
        attend_kernel,
        grid_spec=pltpu.PrefetchScalarGridSpec(
            num_scalar_prefetch=1,
            grid=(chunks + 1,),
            in_specs=[
                pl.BlockSpec(memory_space=pl.ANY),
                pl.BlockSpec(memory_space=pl.ANY),
                pl.BlockSpec((TILE, width), lambda s, *_: (now(s), 0)),
                whole(*ids.shape),
            ],
            out_specs=[
                whole(padded, width),
                whole(padded, width),
                whole(padded, width),
                whole(width, padded),
                pl.BlockSpec((width, TILE), lambda s, *_: (0, now(s))),
                pl.BlockSpec((TILE, width), lambda s, *_: (before(s), 0)),
                pl.BlockSpec((PAIRS, tiles, SPAN, 2 * SUB), lambda s, *_: (0, before(s), 0, 0)),
                whole(width, 3 * width),
                whole(VEC_LANES, width),
            ],
            scratch_shapes=[
                pltpu.VMEM((parts, *near.shape[1:]), LOW),
                pltpu.VMEM((2 * width, width), LOW),
                pltpu.VMEM((width, padded), LOW),
                pltpu.VMEM((padded, SUB), F32),
                pltpu.VMEM((width, SUB), F32),
                pltpu.SemaphoreType.DMA((2,)),
            ],
        ),
        out_shape=[
            jax.ShapeDtypeStruct((padded, width), LOW),
            jax.ShapeDtypeStruct((padded, width), LOW),
            jax.ShapeDtypeStruct((padded, width), LOW),
            jax.ShapeDtypeStruct((width, padded), LOW),
            jax.ShapeDtypeStruct((width, rows), LOW),
            jax.ShapeDtypeStruct((rows, width), LOW),
            jax.ShapeDtypeStruct((PAIRS, rows // SUB, SPAN, 2 * SUB), LOW),
            jax.ShapeDtypeStruct((width, 3 * width), LOW),
            jax.ShapeDtypeStruct((VEC_LANES, width), F32),
        ],
        compiler_params=pltpu.CompilerParams(vmem_limit_bytes=VMEM_LIMIT),
        cost_estimate=pl.CostEstimate(
            flops=12_000_000_000, bytes_accessed=22_000_000, transcendentals=5_000_000
        ),
        name="attend_forward",
    )(places, near, far, tokens, ids)


def mlp_kernel(
    places,
    owners,
    near,
    far,
    vectors,
    mixed,
    tokens,
    cotangent,
    output,
    grad_residual,
    grad_mixed,
    inner,
    grads_near,
    grads_far,
    sums,
    one,
    two,
    proj_parts,
    proj,
    acc_one,
    acc_two,
    acc_proj,
    bias,
    acc_bias,
    sems,
):
    step = pl.program_id(0)
    width = tokens.shape[1]
    parts, mid = proj_parts.shape[0], near.shape[0]
    block = width // parts
    last_at = 2 * width
    hidden_width = one.shape[1]

    @pl.when(step == 0)
    def assemble():
        pairs = []
        for part in range(parts):
            source = near.at[part] if part < mid else far.at[part - mid]
            lanes = pl.ds(part * width, width)
            pairs.append((source.at[:, pl.ds(0, width)], one.at[:, lanes]))
            pairs.append((source.at[:, pl.ds(width, width)], two.at[:, lanes]))
            pairs.append((source.at[:, pl.ds(last_at, SUB)], proj_parts.at[part]))
        fetch(pairs, sems)
        total = jnp.zeros((width, width), F32)
        for number in range(parts):
            piece = proj_parts[places[number]].astype(F32)
            kept = jnp.where(lane_numbers(piece.shape) < block, piece, 0.0)
            wide = jnp.concatenate([kept, jnp.zeros((width, width - SUB), F32)], axis=1)
            total = total + (pltpu.roll(wide, block * number, 1) if number else wide)
        proj[...] = total.astype(LOW)
        for part in range(parts):
            bias[0:1, part * width : (part + 1) * width] = vectors[pl.ds(8 + owners[part], 1), :]
        acc_one[...] = jnp.zeros(acc_one.shape, F32)
        acc_two[...] = jnp.zeros(acc_two.shape, F32)
        acc_proj[...] = jnp.zeros(acc_proj.shape, F32)
        acc_bias[...] = jnp.zeros(acc_bias.shape, F32)
        sums[...] = jnp.zeros(sums.shape, F32)

    def add_row(row, values):
        sums[pl.ds(row, 1), :] += jnp.sum(values, axis=0, keepdims=True)

    own = mixed[...]
    residual = tokens[...].astype(F32) + dot(own, proj[...], NT) + vectors[4:5, :]
    normed, rate = norm_parts(residual)
    gain = vectors[5:6, :]
    second_in = (normed * gain + vectors[6:7, :]).astype(LOW)
    out_low = cotangent[...]
    grad_out = out_low.astype(F32)
    second_turned = second_in.T
    out_turned = out_low.T
    totals = [residual + vectors[7:8, :], jnp.zeros(residual.shape, F32)]

    def first(number):
        lanes = pl.ds(number * FF_CHUNK, FF_CHUNK)
        return dot(second_in, one[:, lanes]), dot(out_low, two[:, lanes])

    def second(number, made):
        lanes = pl.ds(number * FF_CHUNK, FF_CHUNK)
        active, grad_hidden = gelu_rows(made[0] + bias[0:1, lanes], made[1])
        acc_bias[0:1, lanes] += jnp.sum(grad_hidden.astype(F32), axis=0, keepdims=True)
        return active, grad_hidden

    def third(number, kept):
        lanes = pl.ds(number * FF_CHUNK, FF_CHUNK)
        active, grad_hidden = kept
        acc_one[:, lanes] += dot(second_turned, grad_hidden)
        acc_two[:, lanes] += dot(out_turned, active)
        totals[0] = totals[0] + dot(active, two[:, lanes], NT)
        totals[1] = totals[1] + dot(grad_hidden, one[:, lanes], NT)

    staged(hidden_width // FF_CHUNK, first, second, third)
    result, grad_second = totals
    output[...] = result.astype(LOW)
    add_row(5, grad_second * normed)
    add_row(6, grad_second)
    add_row(7, grad_out)
    grad_res = grad_out + norm_back(grad_second, normed, rate, gain)
    grad_residual[...] = grad_res
    branch = grad_res.astype(LOW)
    add_row(4, branch.astype(F32))
    acc_proj[...] += dot(branch.T, own)
    grad_own = dot(branch, proj[...]).astype(LOW)
    grad_mixed[...] = grad_own
    high, rest = halves(grad_own.astype(F32) * own.astype(F32))
    head = lax.broadcasted_iota(jnp.int32, (16, width), 0)
    chosen = (lane_numbers((16, width)) // (width // HEADS) == head).astype(F32).astype(LOW)
    inner[...] = (dot(chosen, high, NT) + dot(chosen, rest, NT))[:8]

    @pl.when(step == pl.num_programs(0) - 1)
    def finish():
        total = acc_proj[...]
        for number in range(parts):
            turned = pltpu.roll(total, (width - block * number) % width, 1) if number else total
            proj_parts[places[number]] = turned[:, :SUB].astype(LOW)
        for part in range(parts):
            ref, at = (grads_near, part) if part < mid else (grads_far, part - mid)
            lanes = pl.ds(part * width, width)
            ref[at, :, :width] = acc_one[:, lanes].astype(LOW)
            ref[at, :, width:last_at] = acc_two[:, lanes].astype(LOW)
            ref[at, :, last_at:] = proj_parts[part]
            sums[pl.ds(8 + owners[part], 1), :] = acc_bias[0:1, lanes]


def mlp_both(places, owners, near, far, vectors, mixed, tokens, cotangent):
    rows, width = tokens.shape
    parts = near.shape[0] + far.shape[0]
    hidden_width = parts * width
    tile = pl.BlockSpec((MLP_TILE, width), lambda s, *_: (s, 0))
    whole = lambda *dims: pl.BlockSpec(dims, lambda s, *_: (0,) * len(dims))
    return pl.pallas_call(
        mlp_kernel,
        grid_spec=pltpu.PrefetchScalarGridSpec(
            num_scalar_prefetch=2,
            grid=(rows // MLP_TILE,),
            in_specs=[
                pl.BlockSpec(memory_space=pl.ANY),
                pl.BlockSpec(memory_space=pl.ANY),
                whole(*vectors.shape),
                tile,
                tile,
                tile,
            ],
            out_specs=[
                tile,
                tile,
                tile,
                pl.BlockSpec((8, MLP_TILE), lambda s, *_: (0, s)),
                whole(*near.shape),
                whole(*far.shape),
                whole(*vectors.shape),
            ],
            scratch_shapes=[
                pltpu.VMEM((width, hidden_width), LOW),
                pltpu.VMEM((width, hidden_width), LOW),
                pltpu.VMEM((parts, width, SUB), LOW),
                pltpu.VMEM((width, width), LOW),
                pltpu.VMEM((width, hidden_width), F32),
                pltpu.VMEM((width, hidden_width), F32),
                pltpu.VMEM((width, width), F32),
                pltpu.VMEM((8, hidden_width), F32),
                pltpu.VMEM((8, hidden_width), F32),
                pltpu.SemaphoreType.DMA((3 * parts,)),
            ],
        ),
        out_shape=[
            jax.ShapeDtypeStruct((rows, width), LOW),
            jax.ShapeDtypeStruct((rows, width), F32),
            jax.ShapeDtypeStruct((rows, width), LOW),
            jax.ShapeDtypeStruct((8, rows), F32),
            jax.ShapeDtypeStruct(near.shape, LOW),
            jax.ShapeDtypeStruct(far.shape, LOW),
            jax.ShapeDtypeStruct(vectors.shape, F32),
        ],
        compiler_params=pltpu.CompilerParams(vmem_limit_bytes=VMEM_LIMIT),
        cost_estimate=pl.CostEstimate(
            flops=34_000_000_000, bytes_accessed=20_000_000, transcendentals=6_000_000
        ),
        name="mlp_both",
    )(places, owners, near, far, vectors, mixed, tokens, cotangent)


def attend_back_kernel(
    pairs,
    query,
    key_turned,
    value,
    probs,
    inner,
    grad_mixed,
    normed_turned,
    grad_qkv,
    normed_sums,
    column_sums,
    grad_query,
    acc_key,
    acc_value,
    acc_sums,
):
    step = pl.program_id(0)
    chunks = pl.num_programs(0) - 1
    count = len(pairs)
    scale = (SUB // 2) ** (-0.5)

    @pl.when(step == 0)
    def clear():
        acc_key[...] = jnp.zeros(acc_key.shape, F32)
        acc_value[...] = jnp.zeros(acc_value.shape, F32)
        normed_sums[...] = jnp.zeros(normed_sums.shape, F32)
        acc_sums[...] = jnp.zeros(acc_sums.shape, F32)

    @pl.when(step < chunks)
    def attend():
        def place(number):
            sub, at = number // count, number % count
            start = pl.multiple_of((step * (TILE // SUB) + sub) * SUB, SUB)
            return sub, at, start, pl.ds(start, SPAN), pl.ds(at * SUB, SUB)

        def slope(number):
            sub, _, _, near_rows, heads = place(number)
            grad = both_heads(grad_mixed[pl.ds(sub * SUB, SUB), heads])
            return dot(value[near_rows, heads], grad, NT)

        def soften(number, slopes):
            sub, at, _, _, _ = place(number)
            pair = pairs[at]
            cols = pl.ds(sub * SUB, SUB)
            both = []
            for head in range(2):
                lanes = slice(head * SUB, (head + 1) * SUB)
                less = slopes[:, lanes] - inner[2 * pair + head : 2 * pair + head + 1, cols]
                both.append((probs[at, sub, :, lanes].astype(F32) * less).astype(LOW))
            return jnp.concatenate(both, axis=1)

        def collect(number, scores):
            sub, at, start, near_rows, heads = place(number)
            first, second = halves_of(dot(key_turned[heads, near_rows], scores))
            turned = (jnp.concatenate([first, second], axis=0) * scale).astype(LOW)
            grad_query[pl.ds(start, SUB), heads] = turned.T
            wanted = both_heads(query[pl.ds(start + MARGIN, SUB), heads])
            acc_key[near_rows, heads] += dot(scores, wanted)
            grad = both_heads(grad_mixed[pl.ds(sub * SUB, SUB), heads])
            acc_value[near_rows, heads] += dot(probs[at, sub], grad)

        staged(TILE // SUB * count, slope, soften, collect)

    @pl.when(step > 0)
    def collect():
        here = pl.ds(pl.multiple_of((step - 1) * TILE, SUB), TILE)
        there = pl.ds(pl.multiple_of((step - 1) * TILE + MARGIN, SUB), TILE)
        parts = (
            grad_query[here, :],
            acc_key[there, :].astype(LOW),
            acc_value[there, :].astype(LOW),
        )
        joined = jnp.concatenate(parts, axis=1)
        grad_qkv[...] = joined
        normed_sums[...] += dot(normed_turned[...], joined)
        acc_sums[0:1, :] += jnp.sum(joined.astype(F32), axis=0, keepdims=True)

    @pl.when(step == chunks)
    def finish():
        column_sums[...] = acc_sums[...]


def attend_backward(pairs, query, key_turned, value, probs, inner, grad_mixed, normed_turned):
    width, rows = normed_turned.shape
    padded = query.shape[0]
    chunks = rows // TILE
    tiles = TILE // SUB
    count = len(pairs)
    lanes = count * SUB
    which = pairs[0] // count
    now = lambda s: jnp.minimum(s, chunks - 1)
    before = lambda s: jnp.maximum(s - 1, 0)
    normal = pl.BlockSpec((padded, lanes), lambda s: (0, which))

    def kernel(*refs):
        attend_back_kernel(pairs, *refs)

    return pl.pallas_call(
        kernel,
        grid=(chunks + 1,),
        in_specs=[
            normal,
            pl.BlockSpec((lanes, padded), lambda s: (which, 0)),
            normal,
            pl.BlockSpec((count, tiles, SPAN, 2 * SUB), lambda s: (which, now(s), 0, 0)),
            pl.BlockSpec((8, TILE), lambda s: (0, now(s))),
            pl.BlockSpec((TILE, lanes), lambda s: (now(s), which)),
            pl.BlockSpec((width, TILE), lambda s: (0, before(s))),
        ],
        out_specs=[
            pl.BlockSpec((TILE, 3 * lanes), lambda s: (before(s), 0)),
            pl.BlockSpec((width, 3 * lanes), lambda s: (0, 0)),
            pl.BlockSpec((8, 3 * lanes), lambda s: (0, 0)),
        ],
        out_shape=[
            jax.ShapeDtypeStruct((rows, 3 * lanes), LOW),
            jax.ShapeDtypeStruct((width, 3 * lanes), F32),
            jax.ShapeDtypeStruct((8, 3 * lanes), F32),
        ],
        scratch_shapes=[
            pltpu.VMEM((rows, lanes), LOW),
            pltpu.VMEM((padded, lanes), F32),
            pltpu.VMEM((padded, lanes), F32),
            pltpu.VMEM((8, 3 * lanes), F32),
        ],
        compiler_params=pltpu.CompilerParams(vmem_limit_bytes=VMEM_LIMIT),
        cost_estimate=pl.CostEstimate(
            flops=5_000_000_000 * count, bytes_accessed=7_000_000 * count, transcendentals=0
        ),
        name="attend_backward",
    )(query, key_turned, value, probs, inner, grad_mixed, normed_turned)


def in_order(pieces):
    lanes = pieces[0].shape[1] // 3
    return jnp.concatenate(
        [piece[:, n * lanes : (n + 1) * lanes] for n in range(3) for piece in pieces], axis=1
    )


def weight_grad_kernel(places, weight, vectors, sums, *refs):
    count = (len(refs) - 4) // 2
    normed_sums, column_sums = refs[:count], refs[count : 2 * count]
    near, far, blocks, rows = refs[2 * count :]
    width = weight.shape[0]
    parts, mid = blocks.shape[0], near.shape[0]
    block = 3 * width // parts
    rows_each = 12 // parts
    total = in_order([ref[...] for ref in normed_sums])
    columns = in_order([ref[0:1, :] for ref in column_sums])
    wide = weight[...].astype(F32)
    grad_gain = jnp.sum(total * wide, axis=1, keepdims=True)
    grad_shift = jnp.sum(wide * columns, axis=1, keepdims=True)
    rows[...] = jnp.zeros(rows.shape, F32)
    rows[0:VEC_LANES, :] = sums[...]
    rows[2:3, :] = columns[:, :width]
    rows[3:4, :] = columns[:, 2 * width :]
    rows[VEC_LANES : 2 * VEC_LANES, :] = vectors[...]
    turned = rows[...].T
    gain = turned[:, VEC_LANES : VEC_LANES + 1]
    shift = turned[:, VEC_LANES + 1 : VEC_LANES + 2]
    lane = lane_numbers(turned.shape)
    turned = jnp.where(lane == 0, grad_gain, jnp.where(lane == 1, grad_shift, turned))
    total = total * gain + shift * columns
    at = block - 2 * SUB
    for number in range(parts):
        away = (3 * width - block * number) % (3 * width)
        piece = (pltpu.roll(total, away, 1) if number else total)[:, :width]
        vec = pltpu.roll(turned, (at - rows_each * number) % SUB, 1)
        last = jnp.where(lane < at, piece[:, 2 * SUB :], 0.0)
        last = jnp.where((lane >= at) & (lane < at + rows_each), vec, last)
        blocks[places[number], :, : 2 * SUB] = piece[:, : 2 * SUB].astype(LOW)
        blocks[places[number], :, 2 * SUB :] = last.astype(LOW)
    near[...] = blocks[:mid]
    far[...] = blocks[mid:]


def weight_grad(places, weight, vectors, sums, normed_sums, column_sums):
    width = weight.shape[0]
    parts = places.shape[0]
    half = jax.ShapeDtypeStruct((parts // 2, width, width), LOW)
    vmem = pl.BlockSpec(memory_space=pltpu.VMEM)
    return pl.pallas_call(
        weight_grad_kernel,
        in_specs=[pl.BlockSpec(memory_space=pltpu.SMEM)] + [vmem] * (3 + 2 * len(normed_sums)),
        out_specs=[vmem, vmem],
        out_shape=[half, half],
        scratch_shapes=[pltpu.VMEM((parts, width, width), LOW), pltpu.VMEM((SUB, width), F32)],
        compiler_params=pltpu.CompilerParams(vmem_limit_bytes=VMEM_LIMIT),
        cost_estimate=pl.CostEstimate(
            flops=3_000_000, bytes_accessed=5_000_000, transcendentals=0
        ),
        name="weight_grad",
    )(places, weight, vectors, sums, *normed_sums, *column_sums)


def input_grad_kernel(weight, vectors, tokens, grad_residual, *refs):
    grads, (input_grad, turned) = refs[:-2], refs[-2:]

    @pl.when(pl.program_id(0) == 0)
    def assemble():
        turned[...] = weight[...].T

    joined = in_order([ref[...] for ref in grads])
    normed, rate = norm_parts(tokens[...].astype(F32))
    back = norm_back(dot(joined, turned[...]), normed, rate, vectors[0:1, :])
    input_grad[...] = (grad_residual[...] + back).astype(LOW)


def input_gradient(weight, vectors, tokens, grad_residual, grads):
    rows, width = tokens.shape
    tile = pl.BlockSpec((TILE, width), lambda s: (s, 0))
    whole = lambda ref: pl.BlockSpec(ref.shape, lambda s: (0, 0))
    return pl.pallas_call(
        input_grad_kernel,
        grid=(rows // TILE,),
        in_specs=[whole(weight), whole(vectors), tile, tile]
        + [pl.BlockSpec((TILE, grad.shape[1]), lambda s: (s, 0)) for grad in grads],
        out_specs=tile,
        out_shape=jax.ShapeDtypeStruct((rows, width), LOW),
        scratch_shapes=[pltpu.VMEM((3 * width, width), LOW)],
        compiler_params=pltpu.CompilerParams(vmem_limit_bytes=VMEM_LIMIT),
        cost_estimate=pl.CostEstimate(
            flops=4_000_000_000, bytes_accessed=13_000_000, transcendentals=2048
        ),
        name="input_gradient",
    )(weight, vectors, tokens, grad_residual, *grads)


def halves(value):
    high = value.astype(LOW)
    return high, (value - high.astype(F32)).astype(LOW)


def dot_three(left, right):
    tall = jnp.concatenate([right[0], right[0], right[1]], axis=0)
    return dot(jnp.concatenate([left[0], left[1], left[0]], axis=1), tall)


def muon_kernel(count, height, offset, near, far, old, new, copy):
    depth, wide = near.shape[1:]
    rows = old.shape[0]

    def piece(ref, number):
        value = ref[number]
        if wide != count:
            value = jnp.where(lane_numbers(value.shape) < count, value.astype(F32), 0.0).astype(LOW)
        return value

    own = piece(near, 0)
    gram = dot(own, own, NT)
    for ref, number in [(near, n) for n in range(1, near.shape[0])] + [
        (far, n) for n in range(far.shape[0])
    ]:
        part = piece(ref, number)
        gram = gram + dot(part, part, NT)
    down = lax.broadcasted_iota(jnp.int32, (depth, depth), 0)
    eye = (down == lane_numbers((depth, depth))).astype(F32)
    norm = 1.0 / (jnp.sqrt(jnp.sum(gram * eye, keepdims=True)) + 1e-07)
    gram = gram * (norm * norm)
    tall = -(-rows // 8) * 8
    place = lax.broadcasted_iota(jnp.int32, (tall, depth), 0) + offset[0]
    left = jnp.where(place == lane_numbers((tall, depth)), norm, 0.0)
    for step in range(NS_STEPS):
        pair = halves(gram)
        once = dot_three(halves(left), pair)
        if step < NS_STEPS - 1:
            square = dot_three(pair, pair)
            twice = dot_three(halves(left), halves(square))
            poly = halves(NEWTON_A * eye + NEWTON_B * gram + NEWTON_C * square)
            gram = dot_three(halves(dot_three(pair, poly)), poly)
        else:
            twice = dot_three(halves(once), pair)
        left = NEWTON_A * left + NEWTON_B * once + NEWTON_C * twice
    high, rest = halves(left)
    ortho = (dot(high, own) + dot(rest, own))[:rows, :count]
    scale = MUON_RATE * 0.2 * math.sqrt(height)
    result = old[...] * (1.0 - MUON_RATE * MUON_DECAY) - scale * ortho
    new[...] = result
    copy[...] = result.astype(LOW)


def muon(lanes, height, offset, near, far, old):
    rows, count = old.shape
    wide = -(-count // SUB) * SUB

    def kernel(*refs):
        muon_kernel(count, height, *refs)

    part = lambda ref: pl.BlockSpec(
        (ref.shape[0], ref.shape[1], wide), lambda s: (0, 0, lanes // wide)
    )
    own = pl.BlockSpec((rows, count), lambda s: (0, 0))
    return pl.pallas_call(
        kernel,
        grid=(1,),
        in_specs=[pl.BlockSpec(memory_space=pltpu.SMEM), part(near), part(far), own],
        out_specs=[own, own],
        out_shape=[
            jax.ShapeDtypeStruct((rows, count), F32),
            jax.ShapeDtypeStruct((rows, count), LOW),
        ],
        compiler_params=pltpu.CompilerParams(vmem_limit_bytes=VMEM_LIMIT),
        cost_estimate=pl.CostEstimate(
            flops=9_000_000_000, bytes_accessed=2_000_000, transcendentals=10
        ),
        name="muon",
    )(offset, near, far, old)


def exchange(x, axis, mask):
    size = lax.axis_size(axis)
    return lax.ppermute(x, axis, [(i, i ^ mask) for i in range(size)])


def place_masks(size):
    masks = [0]
    bit = size // 2
    while bit >= 1:
        masks = masks + [m ^ bit for m in masks]
        bit //= 2
    return masks


def over_columns(own):
    size = lax.axis_size("dp")
    sent = jnp.broadcast_to(own[None], (size, *own.shape))
    got = lax.all_to_all(sent, "dp", split_axis=0, concat_axis=0, tiled=True)
    return got.reshape(size * own.shape[0], own.shape[1])


def over_far_rows(own):
    held = own[None]
    bit = lax.axis_size("ns") // 2
    while bit > 1:
        held = jnp.concatenate([held, exchange(held, "ns", bit)])
        bit //= 2
    return held


def sum_owned(near, far):
    low = lambda keep, got: (keep.astype(F32) + got.astype(F32)).astype(LOW)
    held = low(near, exchange(far, "ns", 1))
    bit = 2
    while held.shape[0] > 1:
        half = held.shape[0] // 2
        held = low(held[:half], exchange(held[half:], "ns", bit))
        bit *= 2
    devices = lax.axis_size("dp")
    pieces = held.reshape(devices, -1, held.shape[-1])
    got = lax.all_to_all(pieces, "dp", split_axis=0, concat_axis=0, tiled=True)
    return jnp.sum(got.astype(F32), axis=0)


def widened(arrays, lanes):
    joined = jnp.concatenate(arrays, axis=1)
    return jnp.pad(joined, ((0, 0), (0, lanes - joined.shape[1])))


def per_device(
    tokens,
    cotangent,
    segment,
    valid_rows,
    qkv_weight,
    proj_weight,
    fc1_weight,
    fc2_weight,
    qkv_moment,
    proj_moment,
    fc1_moment,
    fc2_moment,
    vectors,
    vector_moment,
    vector_square,
):
    rows, width = tokens.shape
    ns = lax.axis_size("ns")
    qkv_w, proj_w, fc1_w, fc2_w = (w.T for w in (qkv_weight, proj_weight, fc1_weight, fc2_weight))
    qkv_m, proj_m, fc1_m, fc2_m = (w.T for w in (qkv_moment, proj_moment, fc1_moment, fc2_moment))
    share, count = qkv_w.shape
    vec_rows = vectors.shape[0]
    first_lanes = width
    later_lanes = 2 * width + SUB

    index = lax.axis_index("ns")
    masks = place_masks(ns)
    owners = jnp.stack([index ^ mask for mask in masks]).astype(jnp.int32)
    places = jnp.stack(
        [sum(jnp.where(owners[p] == b, p, 0) for p in range(ns)) for b in range(ns)]
    ).astype(jnp.int32)
    offset = (lax.axis_index("dp") * share).astype(jnp.int32)[None]

    numbers = jnp.where(
        valid_rows > 0, segment, rows + jnp.arange(rows, dtype=jnp.int32)
    ).astype(F32)
    ids = jnp.pad(numbers, (MARGIN, MARGIN), constant_values=-1.0).reshape(-1, SUB)
    ids = jnp.pad(ids, ((0, -ids.shape[0] % 8), (0, 0)), constant_values=-1.0)

    first_shard = widened([qkv_w, vectors.T], first_lanes).astype(LOW)
    later_shard = widened([fc1_w, fc2_w, proj_w], later_lanes).astype(LOW)
    first_near = over_far_rows(over_columns(first_shard))
    first_far = exchange(first_near, "ns", 1)
    later_near = over_far_rows(over_columns(later_shard))

    (query, _, value, key_turned, normed_turned, mixed, probs, weight, vector_full) = (
        attend_forward(places, first_near, first_far, tokens, ids)
    )
    later_near, mixed = lax.optimization_barrier((later_near, mixed))
    later_far = exchange(later_near, "ns", 1)
    output, grad_residual, grad_mixed, inner, grads_near, grads_far, sums = mlp_both(
        places, owners, later_near, later_far, vector_full, mixed, tokens, cotangent
    )
    later_owned = sum_owned(grads_near, grads_far)
    grads, normed_sums, column_sums = zip(
        *(
            attend_backward(
                pairs, query, key_turned, value, probs, inner, grad_mixed, normed_turned
            )
            for pairs in BACK_CALLS
        )
    )
    grads_near, grads_far = weight_grad(
        places, weight, vector_full, sums, normed_sums, column_sums
    )
    first_owned = sum_owned(grads_near, grads_far)
    input_grad = input_gradient(weight, vector_full, tokens, grad_residual, grads)

    later_moment = later_owned + 0.5 * widened([fc1_m, fc2_m, proj_m], later_lanes)
    later_near = over_far_rows(over_columns(later_moment.astype(LOW)))
    later_far = exchange(later_near, "ns", 1)
    first_moment = first_owned + 0.5 * widened([qkv_m], first_lanes)
    first_near = over_far_rows(over_columns(first_moment.astype(LOW)))
    first_far = exchange(first_near, "ns", 1)

    fc1_new = muon(0, fc1_w.shape[1] * ns, offset, later_near, later_far, fc1_w)
    fc2_new = muon(width, fc2_w.shape[1] * ns, offset, later_near, later_far, fc2_w)
    proj_new = muon(2 * width, proj_w.shape[1] * ns, offset, later_near, later_far, proj_w)
    qkv_new = muon(0, count * ns, offset, first_near, first_far, qkv_w)
    news = (qkv_new, proj_new, fc1_new, fc2_new)
    moments_new = (
        first_moment[:, :count],
        later_moment[:, 2 * width : 2 * width + proj_w.shape[1]],
        later_moment[:, :width],
        later_moment[:, width : 2 * width],
    )

    vector_grad = first_owned[:, count : count + vec_rows].T
    first_new = BETA_ONE * vector_moment + (1.0 - BETA_ONE) * vector_grad
    second_new = BETA_TWO * vector_square + (1.0 - BETA_TWO) * vector_grad * vector_grad
    first_hat = first_new / (1.0 - BETA_ONE**STEP)
    second_hat = second_new / (1.0 - BETA_TWO**STEP)
    vectors_new = vectors - ADAM_RATE * first_hat / (jnp.sqrt(second_hat) + ADAM_EPS)
    return (
        output,
        input_grad,
        *(new[0].T for new in news),
        *(m.T for m in moments_new),
        first_new,
        second_new,
        vectors_new,
        *(new[1].T for new in news),
    )


def solution(mesh):
    rows = P(("dp", "ns"), None)
    flat = P(("dp", "ns"))
    block = P("ns", "dp")
    return jax.shard_map(
        per_device,
        mesh=mesh,
        in_specs=(rows, rows, flat, flat) + (block,) * 11,
        out_specs=(rows, rows) + (block,) * 15,
        check_vma=False,
    )
```

```python
import math

import jax
import jax.numpy as jnp
from jax import lax
from jax.experimental import pallas as pl
from jax.experimental.pallas import tpu as pltpu
from jax.sharding import PartitionSpec as P

HEADS = 6
PAIRS = 3
MARGIN = 128
NS_STEPS = 5
STEP = 10
TILE = 256
MLP_TILE = 512
FF_CHUNK = 512
SUB = 128
SPAN = 384
VEC_LANES = 16
BACK_CALLS = ((0, 1), (2,))


EPS_NORM = 1e-06
NEWTON_A = 3.4445
NEWTON_B = -4.775
NEWTON_C = 2.0315
MUON_RATE = 0.2
MUON_DECAY = 0.1
ADAM_RATE = 0.4
BETA_ONE = 0.9
BETA_TWO = 0.999
ADAM_EPS = 1e-08
LOW = jnp.bfloat16
F32 = jnp.float32
TN = (((0,), (0,)), ((), ()))
NT = (((1,), (1,)), ((), ()))
NN = (((1,), (0,)), ((), ()))
VMEM_LIMIT = 56 * 1024 * 1024
ERF_P = 0.3275911
ERF_COEFS = (0.254829592, -0.284496736, 1.421413741, -1.453152027, 1.061405429)


def dot(left, right, dims=NN):
    return lax.dot_general(left, right, dims, preferred_element_type=F32)


def lane_numbers(shape):
    return lax.broadcasted_iota(jnp.int32, shape, len(shape) - 1)


def norm_parts(value):
    center = value - jnp.mean(value, axis=-1, keepdims=True)
    rate = lax.rsqrt(jnp.mean(center * center, axis=-1, keepdims=True) + EPS_NORM)
    return center * rate, rate


def norm_back(grad, normed, rate, gain):
    scaled = grad * gain
    first = jnp.mean(scaled, axis=-1, keepdims=True)
    second = jnp.mean(scaled * normed, axis=-1, keepdims=True)
    return rate * (scaled - first - normed * second)


def gelu_both(value):
    ratio = 1.0 / (1.0 + (ERF_P * 0.5**0.5) * jnp.abs(value))
    decay = jnp.exp2((value * value) * (-0.5 * math.log2(math.e)))
    poly = 0.5 * ERF_COEFS[4]
    for coef in ERF_COEFS[3::-1]:
        poly = poly * ratio + 0.5 * coef
    tail = poly * ratio * decay
    phi = jnp.where(value >= 0, 1.0 - tail, tail)
    return value * phi, phi + value * decay * (1.0 / math.sqrt(2.0 * math.pi))


def gelu_rows(hidden, grad):
    active, back = [], []
    for row in range(0, hidden.shape[0], 16):
        value, slope = gelu_both(hidden[row : row + 16])
        active.append(value.astype(LOW))
        back.append((grad[row : row + 16] * slope).astype(LOW))
    return jnp.concatenate(active, axis=0), jnp.concatenate(back, axis=0)


def halves_of(lanes):
    half = lanes.shape[0] // 2
    return lanes[:half, :SUB], lanes[half:, SUB:]


def staged(count, first, second, third):
    made = [first(0)]
    kept = None
    for n in range(count):
        if n + 1 < count:
            made.append(first(n + 1))
        if kept is not None:
            third(n - 1, kept)
        kept = second(n, made[n])
        made[n] = None
    third(count - 1, kept)


def both_heads(pair):
    first = (lane_numbers((1, SUB)) < SUB // 2).astype(F32).astype(pair.dtype)
    second = (lane_numbers((1, SUB)) >= SUB // 2).astype(F32).astype(pair.dtype)
    return jnp.concatenate([pair * first, pair * second], axis=0)


def fetch(pairs, sems):
    copies = [
        pltpu.make_async_copy(source, target, sems.at[n])
        for n, (source, target) in enumerate(pairs)
    ]
    for copy in copies:
        copy.start()
    for copy in copies:
        copy.wait()


def attend_kernel(
    places,
    *refs,
):
    (tokens, ids, query, key, value, key_turned, normed_turned, mixed, probs, weight, vectors,
     gathered, pair_weight, value_turned, columns, shifts, sems) = refs[-17:]
    pieces = refs[:-17]
    step = pl.program_id(0)
    chunks = pl.num_programs(0) - 1
    width = tokens.shape[1]
    parts = len(pieces)
    block = 3 * width // parts
    rows_each = 12 // parts

    @pl.when(step == 0)
    def assemble():
        fetch([(piece, gathered.at[n]) for n, piece in enumerate(pieces)], sems)
        total = jnp.zeros((width, 3 * width), F32)
        turned = jnp.zeros((width, SUB), F32)
        for number in range(parts):
            piece = gathered[places[number]].astype(F32)
            kept = jnp.where(lane_numbers(piece.shape) < block, piece, 0.0)
            wide = jnp.concatenate([kept, jnp.zeros((width, 2 * width), F32)], axis=1)
            total = total + (pltpu.roll(wide, block * number, 1) if number else wide)
            last = piece[:, 2 * SUB :]
            at = block - 2 * SUB
            lane = lane_numbers(last.shape)
            vec = jnp.where((lane >= at) & (lane < at + rows_each), last, 0.0)
            turned = turned + pltpu.roll(vec, (rows_each * number - at) % SUB, 1)
        total = total.astype(LOW)
        weight[...] = total
        pair_weight[...] = total[:, width:].T
        vectors[...] = turned.T[:VEC_LANES]
        shifts[...] = turned
        edges = (pl.ds(0, MARGIN), pl.ds(MARGIN + chunks * TILE, MARGIN))
        for edge in edges:
            for ref in (query, key, value):
                ref[edge, :] = jnp.zeros((MARGIN, width), LOW)
            for ref in (key_turned, value_turned):
                ref[:, edge] = jnp.zeros((width, MARGIN), LOW)
        for number in range(chunks * TILE // SUB + 2):
            row = jnp.broadcast_to(ids[number : number + 1, :], (SUB, SUB))
            columns[number * SUB : (number + 1) * SUB, :] = row.T

    @pl.when(step < chunks)
    def project():
        normed, _ = norm_parts(tokens[...].astype(F32))
        normed_turned[...] = normed.astype(LOW).T
        first_in = (normed * vectors[0:1, :] + vectors[1:2, :]).astype(LOW)
        result = dot(first_in, weight[...])
        turned = dot(pair_weight[...], first_in, NT)
        here = pl.ds(pl.multiple_of(MARGIN + step * TILE, SUB), TILE)
        scale = (width // HEADS) ** (-0.5)
        made = (result[:, :width] + vectors[2:3, :]).astype(LOW) * jnp.asarray(scale, LOW)
        query[here, :] = made
        key[here, :] = result[:, width : 2 * width].astype(LOW)
        value[here, :] = (result[:, 2 * width :] + vectors[3:4, :]).astype(LOW)
        key_turned[:, here] = turned[:width].astype(LOW)
        value_turned[:, here] = (turned[width:] + shifts[:, 3:4]).astype(LOW)

    @pl.when(step > 0)
    def attend():
        def place(number):
            sub, pair = number // PAIRS, number % PAIRS
            tile = (step - 1) * (TILE // SUB) + sub
            start = pl.multiple_of(tile * SUB, SUB)
            return sub, pair, tile, start, pl.ds(start, SPAN), pl.ds(pair * SUB, SUB)

        def score(number):
            _, _, _, start, near_rows, heads = place(number)
            wanted = both_heads(query[pl.ds(start + MARGIN, SUB), heads])
            return dot(key[near_rows, heads], wanted, NT)

        def soften(number, scores):
            sub, pair, tile, _, near_rows, _ = place(number)
            row = ids[pl.ds(tile + 1, 1), :]
            both = []
            for head in range(2):
                same = columns[near_rows, :] == row
                own = jnp.where(same, scores[:, head * SUB : (head + 1) * SUB], -1e30)
                expo = jnp.exp(own - jnp.max(own, axis=0, keepdims=True))
                share = 1.0 / jnp.sum(expo, axis=0, keepdims=True)
                both.append((expo * share).astype(LOW))
            prob = jnp.concatenate(both, axis=1)
            probs[pair, sub] = prob
            return prob

        def mix(number, prob):
            sub, _, _, _, near_rows, heads = place(number)
            first, second = halves_of(dot(value_turned[heads, near_rows], prob))
            turned = jnp.concatenate([first, second], axis=0).astype(LOW)
            mixed[pl.ds(sub * SUB, SUB), heads] = turned.T

        staged(TILE // SUB * PAIRS, score, soften, mix)


def attend_forward(places, pieces, tokens, ids):
    rows, width = tokens.shape
    chunks = rows // TILE
    tiles = TILE // SUB
    parts = len(pieces)
    now = lambda s: jnp.minimum(s, chunks - 1)
    before = lambda s: jnp.maximum(s - 1, 0)
    whole = lambda *dims: pl.BlockSpec(dims, lambda s, *_: (0,) * len(dims))
    padded = rows + 2 * MARGIN
    return pl.pallas_call(
        attend_kernel,
        grid_spec=pltpu.PrefetchScalarGridSpec(
            num_scalar_prefetch=1,
            grid=(chunks + 1,),
            in_specs=[pl.BlockSpec(memory_space=pl.ANY)] * parts
            + [
                pl.BlockSpec((TILE, width), lambda s, *_: (now(s), 0)),
                whole(*ids.shape),
            ],
            out_specs=[
                whole(padded, width),
                whole(padded, width),
                whole(padded, width),
                whole(width, padded),
                pl.BlockSpec((width, TILE), lambda s, *_: (0, now(s))),
                pl.BlockSpec((TILE, width), lambda s, *_: (before(s), 0)),
                pl.BlockSpec((PAIRS, tiles, SPAN, 2 * SUB), lambda s, *_: (0, before(s), 0, 0)),
                whole(width, 3 * width),
                whole(VEC_LANES, width),
            ],
            scratch_shapes=[
                pltpu.VMEM((parts, *pieces[0].shape), LOW),
                pltpu.VMEM((2 * width, width), LOW),
                pltpu.VMEM((width, padded), LOW),
                pltpu.VMEM((padded, SUB), F32),
                pltpu.VMEM((width, SUB), F32),
                pltpu.SemaphoreType.DMA((parts,)),
            ],
        ),
        out_shape=[
            jax.ShapeDtypeStruct((padded, width), LOW),
            jax.ShapeDtypeStruct((padded, width), LOW),
            jax.ShapeDtypeStruct((padded, width), LOW),
            jax.ShapeDtypeStruct((width, padded), LOW),
            jax.ShapeDtypeStruct((width, rows), LOW),
            jax.ShapeDtypeStruct((rows, width), LOW),
            jax.ShapeDtypeStruct((PAIRS, rows // SUB, SPAN, 2 * SUB), LOW),
            jax.ShapeDtypeStruct((width, 3 * width), LOW),
            jax.ShapeDtypeStruct((VEC_LANES, width), F32),
        ],
        compiler_params=pltpu.CompilerParams(vmem_limit_bytes=VMEM_LIMIT),
        cost_estimate=pl.CostEstimate(
            flops=12_000_000_000, bytes_accessed=22_000_000, transcendentals=5_000_000
        ),
        name="attend_forward",
    )(places, *pieces, tokens, ids)


def mlp_kernel(places, owners, *refs):
    (vectors, mixed, tokens, cotangent, output, grad_residual, grad_mixed, inner, grads_near,
     grads_far, sums, one, two, proj_parts, proj, acc_one, acc_two, acc_proj, bias, acc_bias,
     sems) = refs[-21:]
    pieces = refs[:-21]
    step = pl.program_id(0)
    width = tokens.shape[1]
    parts, mid = len(pieces), len(pieces) // 2
    block = width // parts
    last_at = 2 * width
    hidden_width = one.shape[1]

    @pl.when(step == 0)
    def assemble():
        pairs = []
        for part in range(parts):
            source = pieces[part]
            lanes = pl.ds(part * width, width)
            pairs.append((source.at[:, pl.ds(0, width)], one.at[:, lanes]))
            pairs.append((source.at[:, pl.ds(width, width)], two.at[:, lanes]))
            pairs.append((source.at[:, pl.ds(last_at, SUB)], proj_parts.at[part]))
        fetch(pairs, sems)
        total = jnp.zeros((width, width), F32)
        for number in range(parts):
            piece = proj_parts[places[number]].astype(F32)
            kept = jnp.where(lane_numbers(piece.shape) < block, piece, 0.0)
            wide = jnp.concatenate([kept, jnp.zeros((width, width - SUB), F32)], axis=1)
            total = total + (pltpu.roll(wide, block * number, 1) if number else wide)
        proj[...] = total.astype(LOW)
        for part in range(parts):
            bias[0:1, part * width : (part + 1) * width] = vectors[pl.ds(8 + owners[part], 1), :]
        acc_one[...] = jnp.zeros(acc_one.shape, F32)
        acc_two[...] = jnp.zeros(acc_two.shape, F32)
        acc_proj[...] = jnp.zeros(acc_proj.shape, F32)
        acc_bias[...] = jnp.zeros(acc_bias.shape, F32)
        sums[...] = jnp.zeros(sums.shape, F32)

    def add_row(row, values):
        sums[pl.ds(row, 1), :] += jnp.sum(values, axis=0, keepdims=True)

    own = mixed[...]
    residual = tokens[...].astype(F32) + dot(own, proj[...], NT) + vectors[4:5, :]
    normed, rate = norm_parts(residual)
    gain = vectors[5:6, :]
    second_in = (normed * gain + vectors[6:7, :]).astype(LOW)
    out_low = cotangent[...]
    grad_out = out_low.astype(F32)
    second_turned = second_in.T
    out_turned = out_low.T
    totals = [residual + vectors[7:8, :], jnp.zeros(residual.shape, F32)]

    def first(number):
        lanes = pl.ds(number * FF_CHUNK, FF_CHUNK)
        return dot(second_in, one[:, lanes]), dot(out_low, two[:, lanes])

    def second(number, made):
        lanes = pl.ds(number * FF_CHUNK, FF_CHUNK)
        active, grad_hidden = gelu_rows(made[0] + bias[0:1, lanes], made[1])
        acc_bias[0:1, lanes] += jnp.sum(grad_hidden.astype(F32), axis=0, keepdims=True)
        return active, grad_hidden

    def third(number, kept):
        lanes = pl.ds(number * FF_CHUNK, FF_CHUNK)
        active, grad_hidden = kept
        acc_one[:, lanes] += dot(second_turned, grad_hidden)
        acc_two[:, lanes] += dot(out_turned, active)
        totals[0] = totals[0] + dot(active, two[:, lanes], NT)
        totals[1] = totals[1] + dot(grad_hidden, one[:, lanes], NT)

    staged(hidden_width // FF_CHUNK, first, second, third)
    result, grad_second = totals
    output[...] = result.astype(LOW)
    add_row(5, grad_second * normed)
    add_row(6, grad_second)
    add_row(7, grad_out)
    grad_res = grad_out + norm_back(grad_second, normed, rate, gain)
    grad_residual[...] = grad_res
    branch = grad_res.astype(LOW)
    add_row(4, branch.astype(F32))
    acc_proj[...] += dot(branch.T, own)
    grad_own = dot(branch, proj[...]).astype(LOW)
    grad_mixed[...] = grad_own
    high, rest = halves(grad_own.astype(F32) * own.astype(F32))
    head = lax.broadcasted_iota(jnp.int32, (16, width), 0)
    chosen = (lane_numbers((16, width)) // (width // HEADS) == head).astype(F32).astype(LOW)
    inner[...] = (dot(chosen, high, NT) + dot(chosen, rest, NT))[:8]

    @pl.when(step == pl.num_programs(0) - 1)
    def finish():
        total = acc_proj[...]
        for number in range(parts):
            turned = pltpu.roll(total, (width - block * number) % width, 1) if number else total
            proj_parts[places[number]] = turned[:, :SUB].astype(LOW)
        for part in range(parts):
            ref, at = (grads_near, part) if part < mid else (grads_far, part - mid)
            lanes = pl.ds(part * width, width)
            ref[at, :, :width] = acc_one[:, lanes].astype(LOW)
            ref[at, :, width:last_at] = acc_two[:, lanes].astype(LOW)
            ref[at, :, last_at:] = proj_parts[part]
            sums[pl.ds(8 + owners[part], 1), :] = acc_bias[0:1, lanes]


def mlp_both(places, owners, pieces, vectors, mixed, tokens, cotangent):
    rows, width = tokens.shape
    parts = len(pieces)
    half = (parts // 2, *pieces[0].shape)
    hidden_width = parts * width
    tile = pl.BlockSpec((MLP_TILE, width), lambda s, *_: (s, 0))
    whole = lambda *dims: pl.BlockSpec(dims, lambda s, *_: (0,) * len(dims))
    return pl.pallas_call(
        mlp_kernel,
        grid_spec=pltpu.PrefetchScalarGridSpec(
            num_scalar_prefetch=2,
            grid=(rows // MLP_TILE,),
            in_specs=[pl.BlockSpec(memory_space=pl.ANY)] * parts
            + [whole(*vectors.shape), tile, tile, tile],
            out_specs=[
                tile,
                tile,
                tile,
                pl.BlockSpec((8, MLP_TILE), lambda s, *_: (0, s)),
                whole(*half),
                whole(*half),
                whole(*vectors.shape),
            ],
            scratch_shapes=[
                pltpu.VMEM((width, hidden_width), LOW),
                pltpu.VMEM((width, hidden_width), LOW),
                pltpu.VMEM((parts, width, SUB), LOW),
                pltpu.VMEM((width, width), LOW),
                pltpu.VMEM((width, hidden_width), F32),
                pltpu.VMEM((width, hidden_width), F32),
                pltpu.VMEM((width, width), F32),
                pltpu.VMEM((8, hidden_width), F32),
                pltpu.VMEM((8, hidden_width), F32),
                pltpu.SemaphoreType.DMA((3 * parts,)),
            ],
        ),
        out_shape=[
            jax.ShapeDtypeStruct((rows, width), LOW),
            jax.ShapeDtypeStruct((rows, width), F32),
            jax.ShapeDtypeStruct((rows, width), LOW),
            jax.ShapeDtypeStruct((8, rows), F32),
            jax.ShapeDtypeStruct(half, LOW),
            jax.ShapeDtypeStruct(half, LOW),
            jax.ShapeDtypeStruct(vectors.shape, F32),
        ],
        compiler_params=pltpu.CompilerParams(vmem_limit_bytes=VMEM_LIMIT),
        cost_estimate=pl.CostEstimate(
            flops=34_000_000_000, bytes_accessed=20_000_000, transcendentals=6_000_000
        ),
        name="mlp_both",
    )(places, owners, *pieces, vectors, mixed, tokens, cotangent)


def attend_back_kernel(
    pairs,
    query,
    key_turned,
    value,
    probs,
    inner,
    grad_mixed,
    normed_turned,
    grad_qkv,
    normed_sums,
    column_sums,
    grad_query,
    acc_key,
    acc_value,
    acc_sums,
):
    step = pl.program_id(0)
    chunks = pl.num_programs(0) - 1
    count = len(pairs)
    scale = (SUB // 2) ** (-0.5)

    @pl.when(step == 0)
    def clear():
        acc_key[...] = jnp.zeros(acc_key.shape, F32)
        acc_value[...] = jnp.zeros(acc_value.shape, F32)
        normed_sums[...] = jnp.zeros(normed_sums.shape, F32)
        acc_sums[...] = jnp.zeros(acc_sums.shape, F32)

    @pl.when(step < chunks)
    def attend():
        def place(number):
            sub, at = number // count, number % count
            start = pl.multiple_of((step * (TILE // SUB) + sub) * SUB, SUB)
            return sub, at, start, pl.ds(start, SPAN), pl.ds(at * SUB, SUB)

        def slope(number):
            sub, _, _, near_rows, heads = place(number)
            grad = both_heads(grad_mixed[pl.ds(sub * SUB, SUB), heads])
            return dot(value[near_rows, heads], grad, NT)

        def soften(number, slopes):
            sub, at, _, _, _ = place(number)
            pair = pairs[at]
            cols = pl.ds(sub * SUB, SUB)
            both = []
            for head in range(2):
                lanes = slice(head * SUB, (head + 1) * SUB)
                less = slopes[:, lanes] - inner[2 * pair + head : 2 * pair + head + 1, cols]
                both.append((probs[at, sub, :, lanes].astype(F32) * less).astype(LOW))
            return jnp.concatenate(both, axis=1)

        def collect(number, scores):
            sub, at, start, near_rows, heads = place(number)
            first, second = halves_of(dot(key_turned[heads, near_rows], scores))
            turned = (jnp.concatenate([first, second], axis=0) * scale).astype(LOW)
            grad_query[pl.ds(start, SUB), heads] = turned.T
            wanted = both_heads(query[pl.ds(start + MARGIN, SUB), heads])
            acc_key[near_rows, heads] += dot(scores, wanted)
            grad = both_heads(grad_mixed[pl.ds(sub * SUB, SUB), heads])
            acc_value[near_rows, heads] += dot(probs[at, sub], grad)

        staged(TILE // SUB * count, slope, soften, collect)

    @pl.when(step > 0)
    def collect():
        here = pl.ds(pl.multiple_of((step - 1) * TILE, SUB), TILE)
        there = pl.ds(pl.multiple_of((step - 1) * TILE + MARGIN, SUB), TILE)
        parts = (
            grad_query[here, :],
            acc_key[there, :].astype(LOW),
            acc_value[there, :].astype(LOW),
        )
        joined = jnp.concatenate(parts, axis=1)
        grad_qkv[...] = joined
        normed_sums[...] += dot(normed_turned[...], joined)
        acc_sums[0:1, :] += jnp.sum(joined.astype(F32), axis=0, keepdims=True)

    @pl.when(step == chunks)
    def finish():
        column_sums[...] = acc_sums[...]


def attend_backward(pairs, query, key_turned, value, probs, inner, grad_mixed, normed_turned):
    width, rows = normed_turned.shape
    padded = query.shape[0]
    chunks = rows // TILE
    tiles = TILE // SUB
    count = len(pairs)
    lanes = count * SUB
    which = pairs[0] // count
    assert pairs[0] % count == 0
    now = lambda s: jnp.minimum(s, chunks - 1)
    before = lambda s: jnp.maximum(s - 1, 0)
    normal = pl.BlockSpec((padded, lanes), lambda s: (0, which))

    def kernel(*refs):
        attend_back_kernel(pairs, *refs)

    return pl.pallas_call(
        kernel,
        grid=(chunks + 1,),
        in_specs=[
            normal,
            pl.BlockSpec((lanes, padded), lambda s: (which, 0)),
            normal,
            pl.BlockSpec((count, tiles, SPAN, 2 * SUB), lambda s: (which, now(s), 0, 0)),
            pl.BlockSpec((8, TILE), lambda s: (0, now(s))),
            pl.BlockSpec((TILE, lanes), lambda s: (now(s), which)),
            pl.BlockSpec((width, TILE), lambda s: (0, before(s))),
        ],
        out_specs=[
            pl.BlockSpec((TILE, 3 * lanes), lambda s: (before(s), 0)),
            pl.BlockSpec((width, 3 * lanes), lambda s: (0, 0)),
            pl.BlockSpec((8, 3 * lanes), lambda s: (0, 0)),
        ],
        out_shape=[
            jax.ShapeDtypeStruct((rows, 3 * lanes), LOW),
            jax.ShapeDtypeStruct((width, 3 * lanes), F32),
            jax.ShapeDtypeStruct((8, 3 * lanes), F32),
        ],
        scratch_shapes=[
            pltpu.VMEM((rows, lanes), LOW),
            pltpu.VMEM((padded, lanes), F32),
            pltpu.VMEM((padded, lanes), F32),
            pltpu.VMEM((8, 3 * lanes), F32),
        ],
        compiler_params=pltpu.CompilerParams(vmem_limit_bytes=VMEM_LIMIT),
        cost_estimate=pl.CostEstimate(
            flops=5_000_000_000 * count, bytes_accessed=7_000_000 * count, transcendentals=0
        ),
        name="attend_backward",
    )(query, key_turned, value, probs, inner, grad_mixed, normed_turned)


def in_order(pieces):
    return jnp.concatenate(
        [
            piece[:, n * piece.shape[1] // 3 : (n + 1) * piece.shape[1] // 3]
            for n in range(3)
            for piece in pieces
        ],
        axis=1,
    )


def weight_grad_kernel(places, weight, vectors, sums, *refs):
    count = (len(refs) - 4) // 2
    normed_sums, column_sums = refs[:count], refs[count : 2 * count]
    near, far, blocks, rows = refs[2 * count :]
    width = weight.shape[0]
    parts, mid = blocks.shape[0], near.shape[0]
    block = 3 * width // parts
    rows_each = 12 // parts
    total = in_order([ref[...] for ref in normed_sums])
    columns = in_order([ref[0:1, :] for ref in column_sums])
    wide = weight[...].astype(F32)
    grad_gain = jnp.sum(total * wide, axis=1, keepdims=True)
    grad_shift = jnp.sum(wide * columns, axis=1, keepdims=True)
    rows[...] = jnp.zeros(rows.shape, F32)
    rows[0:VEC_LANES, :] = sums[...]
    rows[2:3, :] = columns[:, :width]
    rows[3:4, :] = columns[:, 2 * width :]
    rows[VEC_LANES : 2 * VEC_LANES, :] = vectors[...]
    turned = rows[...].T
    gain = turned[:, VEC_LANES : VEC_LANES + 1]
    shift = turned[:, VEC_LANES + 1 : VEC_LANES + 2]
    lane = lane_numbers(turned.shape)
    turned = jnp.where(lane == 0, grad_gain, jnp.where(lane == 1, grad_shift, turned))
    total = total * gain + shift * columns
    at = block - 2 * SUB
    for number in range(parts):
        away = (3 * width - block * number) % (3 * width)
        piece = (pltpu.roll(total, away, 1) if number else total)[:, :width]
        vec = pltpu.roll(turned, (at - rows_each * number) % SUB, 1)
        last = jnp.where(lane < at, piece[:, 2 * SUB :], 0.0)
        last = jnp.where((lane >= at) & (lane < at + rows_each), vec, last)
        blocks[places[number], :, : 2 * SUB] = piece[:, : 2 * SUB].astype(LOW)
        blocks[places[number], :, 2 * SUB :] = last.astype(LOW)
    near[...] = blocks[:mid]
    far[...] = blocks[mid:]


def weight_grad(places, weight, vectors, sums, normed_sums, column_sums):
    width = weight.shape[0]
    parts = places.shape[0]
    half = jax.ShapeDtypeStruct((parts // 2, width, width), LOW)
    vmem = pl.BlockSpec(memory_space=pltpu.VMEM)
    return pl.pallas_call(
        weight_grad_kernel,
        in_specs=[pl.BlockSpec(memory_space=pltpu.SMEM)] + [vmem] * (3 + 2 * len(normed_sums)),
        out_specs=[vmem, vmem],
        out_shape=[half, half],
        scratch_shapes=[pltpu.VMEM((parts, width, width), LOW), pltpu.VMEM((SUB, width), F32)],
        compiler_params=pltpu.CompilerParams(vmem_limit_bytes=VMEM_LIMIT),
        cost_estimate=pl.CostEstimate(
            flops=3_000_000, bytes_accessed=5_000_000, transcendentals=0
        ),
        name="weight_grad",
    )(places, weight, vectors, sums, *normed_sums, *column_sums)


def input_grad_kernel(weight, vectors, tokens, grad_residual, *refs):
    grads, (input_grad, turned) = refs[:-2], refs[-2:]

    @pl.when(pl.program_id(0) == 0)
    def assemble():
        turned[...] = weight[...].T

    joined = in_order([ref[...] for ref in grads])
    normed, rate = norm_parts(tokens[...].astype(F32))
    back = norm_back(dot(joined, turned[...]), normed, rate, vectors[0:1, :])
    input_grad[...] = (grad_residual[...] + back).astype(LOW)


def input_gradient(weight, vectors, tokens, grad_residual, grads):
    rows, width = tokens.shape
    tile = pl.BlockSpec((TILE, width), lambda s: (s, 0))
    whole = lambda ref: pl.BlockSpec(ref.shape, lambda s: (0, 0))
    return pl.pallas_call(
        input_grad_kernel,
        grid=(rows // TILE,),
        in_specs=[whole(weight), whole(vectors), tile, tile]
        + [pl.BlockSpec((TILE, grad.shape[1]), lambda s: (s, 0)) for grad in grads],
        out_specs=tile,
        out_shape=jax.ShapeDtypeStruct((rows, width), LOW),
        scratch_shapes=[pltpu.VMEM((3 * width, width), LOW)],
        compiler_params=pltpu.CompilerParams(vmem_limit_bytes=VMEM_LIMIT),
        cost_estimate=pl.CostEstimate(
            flops=4_000_000_000, bytes_accessed=13_000_000, transcendentals=2048
        ),
        name="input_gradient",
    )(weight, vectors, tokens, grad_residual, *grads)


def halves(value):
    high = value.astype(LOW)
    return high, (value - high.astype(F32)).astype(LOW)


def dot_three(left, right):
    tall = jnp.concatenate([right[0], right[0], right[1]], axis=0)
    return dot(jnp.concatenate([left[0], left[1], left[0]], axis=1), tall)


def newton_rows(blocks, offset, rows):
    gram = dot(blocks[0], blocks[0], NT)
    for part in blocks[1:]:
        gram = gram + dot(part, part, NT)
    depth = gram.shape[0]
    down = lax.broadcasted_iota(jnp.int32, (depth, depth), 0)
    eye = (down == lane_numbers((depth, depth))).astype(F32)
    norm = 1.0 / (jnp.sqrt(jnp.sum(gram * eye, keepdims=True)) + 1e-07)
    gram = gram * (norm * norm)
    place = lax.broadcasted_iota(jnp.int32, (rows, depth), 0) + offset
    left = jnp.where(place == lane_numbers((rows, depth)), norm, 0.0)
    for step in range(NS_STEPS - 1):
        pair = halves(gram)
        poly = halves(NEWTON_A * eye + NEWTON_B * gram + NEWTON_C * dot_three(pair, pair))
        lefts = halves(left)
        both = dot_three([jnp.concatenate([pair[n], lefts[n]], axis=0) for n in range(2)], poly)
        left = both[depth:]
        gram = dot_three(halves(both[:depth]), poly)
    pair = halves(gram)
    once = dot_three(halves(left), pair)
    return NEWTON_A * left + NEWTON_B * once + NEWTON_C * dot_three(halves(once), pair)


def stepped(left, own, height, old):
    high, rest = halves(left)
    ortho = (dot(high, own) + dot(rest, own))[: old.shape[0], : old.shape[1]]
    return old * (1.0 - MUON_RATE * MUON_DECAY) - (MUON_RATE * 0.2 * math.sqrt(height)) * ortho


def kept_lanes(value, low, high):
    lane = lane_numbers(value.shape)
    return jnp.where((lane >= low) & (lane < high), value.astype(F32), 0.0).astype(LOW)


def tall_of(rows):
    return -(-rows // 16) * 16


def muon_kernel(height, offset, *refs):
    old, new, copy = refs[-3:]
    count = old.shape[1]
    blocks = [kept_lanes(ref[...], 0, count) for ref in refs[:-3]]
    left = newton_rows(blocks, offset[0], tall_of(old.shape[0]))
    result = stepped(left, blocks[0], height, old[...])
    new[...] = result
    copy[...] = result.astype(LOW)


def muon(height, offset, blocks, old):
    vmem = pl.BlockSpec(memory_space=pltpu.VMEM)

    def kernel(*refs):
        muon_kernel(height, *refs)

    return pl.pallas_call(
        kernel,
        in_specs=[pl.BlockSpec(memory_space=pltpu.SMEM)] + [vmem] * (len(blocks) + 1),
        out_specs=[vmem, vmem],
        out_shape=[
            jax.ShapeDtypeStruct(old.shape, F32),
            jax.ShapeDtypeStruct(old.shape, LOW),
        ],
        compiler_params=pltpu.CompilerParams(vmem_limit_bytes=VMEM_LIMIT),
        cost_estimate=pl.CostEstimate(
            flops=9_000_000_000, bytes_accessed=2_000_000, transcendentals=10
        ),
        name="muon",
    )(offset, *blocks, old)


def pick_kernel(starts, columns, *refs):
    outs, sems = refs[:-1], refs[-1]
    fetch(
        [
            (columns.at[:, pl.ds(pl.multiple_of(starts[n] * SUB, SUB), out.shape[1])], out)
            for n, out in enumerate(outs)
        ],
        sems,
    )


def pick(starts, columns):
    depth = columns.shape[0]
    count = starts.shape[0]
    anywhere = pl.BlockSpec(memory_space=pl.ANY)
    return pl.pallas_call(
        pick_kernel,
        in_specs=[pl.BlockSpec(memory_space=pltpu.SMEM), anywhere],
        out_specs=[anywhere] * count,
        out_shape=[jax.ShapeDtypeStruct((depth, depth), LOW)] * count,
        scratch_shapes=[pltpu.SemaphoreType.DMA((count,))],
        name="pick",
    )(starts, columns)


def newton_kernel(numbers, *refs):
    left = refs[-1]
    blocks = [kept_lanes(ref[...], numbers[1], numbers[2]) for ref in refs[:-1]]
    left[...] = newton_rows(blocks, numbers[0], left.shape[0])


def newton(numbers, blocks, rows):
    vmem = pl.BlockSpec(memory_space=pltpu.VMEM)
    return pl.pallas_call(
        newton_kernel,
        in_specs=[pl.BlockSpec(memory_space=pltpu.SMEM)] + [vmem] * len(blocks),
        out_specs=vmem,
        out_shape=jax.ShapeDtypeStruct((tall_of(rows), blocks[0].shape[0]), F32),
        compiler_params=pltpu.CompilerParams(vmem_limit_bytes=VMEM_LIMIT),
        cost_estimate=pl.CostEstimate(
            flops=9_000_000_000, bytes_accessed=2_000_000, transcendentals=10
        ),
        name="newton",
    )(numbers, *blocks)


def finish_kernel(heights, lanes, which, columns, *refs):
    count = len(heights)
    store = refs[-1]
    news = refs[-1 - 2 * count : -1]
    olds = refs[-1 - 3 * count : -1 - 2 * count]
    lefts = refs[: -1 - 3 * count]
    for n, left in enumerate(lefts):
        store[n] = left[...]
    for n in range(count):
        wide = -(-olds[n].shape[1] // SUB) * SUB
        own = columns[:, lanes[n] : lanes[n] + wide]
        result = stepped(store[which[n]], own, heights[n], olds[n][...])
        news[2 * n][...] = result
        news[2 * n + 1][...] = result.astype(LOW)


def finish(heights, lanes, which, columns, lefts, olds):
    vmem = pl.BlockSpec(memory_space=pltpu.VMEM)
    count = len(olds)

    def kernel(*refs):
        finish_kernel(heights, lanes, *refs)

    outs = pl.pallas_call(
        kernel,
        in_specs=[pl.BlockSpec(memory_space=pltpu.SMEM)] + [vmem] * (1 + len(lefts) + count),
        out_specs=[vmem] * (2 * count),
        out_shape=[
            jax.ShapeDtypeStruct(old.shape, kind) for old in olds for kind in (F32, LOW)
        ],
        scratch_shapes=[pltpu.VMEM((len(lefts), *lefts[0].shape), F32)],
        compiler_params=pltpu.CompilerParams(vmem_limit_bytes=VMEM_LIMIT),
        cost_estimate=pl.CostEstimate(
            flops=200_000_000, bytes_accessed=2_000_000, transcendentals=0
        ),
        name="finish",
    )(which, columns, *lefts, *olds)
    return [(outs[2 * n], outs[2 * n + 1]) for n in range(count)]


def exchange(x, axis, mask):
    size = lax.axis_size(axis)
    return lax.ppermute(x, axis, [(i, i ^ mask) for i in range(size)])


def place_masks(size):
    masks = [0]
    bit = size // 2
    while bit >= 1:
        masks = masks + [m ^ bit for m in masks]
        bit //= 2
    return masks


def over_columns(own):
    size = lax.axis_size("dp")
    sent = jnp.broadcast_to(own[None], (size, *own.shape))
    got = lax.all_to_all(sent, "dp", split_axis=0, concat_axis=0, tiled=True)
    return got.reshape(size * own.shape[0], own.shape[1])


def over_rows(own):
    held = [own]
    bit = lax.axis_size("ns") // 2
    while bit >= 1:
        held = held + [exchange(block, "ns", bit) for block in held]
        bit //= 2
    return held


def added(keep, got):
    return (keep.astype(F32) + got.astype(F32)).astype(LOW)


def sum_rows(held):
    bit = 2
    while held.shape[0] > 1:
        half = held.shape[0] // 2
        held = added(held[:half], exchange(held[half:], "ns", bit))
        bit *= 2
    return held[0]


def sum_columns(held):
    devices = lax.axis_size("dp")
    pieces = held.reshape(devices, -1, held.shape[-1])
    got = lax.all_to_all(pieces, "dp", split_axis=0, concat_axis=0, tiled=True)
    return jnp.sum(got.astype(F32), axis=0)


def widened(arrays, lanes):
    joined = jnp.concatenate(arrays, axis=1)
    return jnp.pad(joined, ((0, 0), (0, lanes - joined.shape[1])))


def per_device(
    tokens,
    cotangent,
    segment,
    valid_rows,
    qkv_weight,
    proj_weight,
    fc1_weight,
    fc2_weight,
    qkv_moment,
    proj_moment,
    fc1_moment,
    fc2_moment,
    vectors,
    vector_moment,
    vector_square,
):
    rows, width = tokens.shape
    ns = lax.axis_size("ns")
    qkv_w, proj_w, fc1_w, fc2_w = (w.T for w in (qkv_weight, proj_weight, fc1_weight, fc2_weight))
    qkv_m, proj_m, fc1_m, fc2_m = (w.T for w in (qkv_moment, proj_moment, fc1_moment, fc2_moment))
    share, count = qkv_w.shape
    vec_rows = vectors.shape[0]
    first_lanes = width
    later_lanes = 2 * width + SUB

    index = lax.axis_index("ns")
    masks = place_masks(ns)
    owners = jnp.stack([index ^ mask for mask in masks]).astype(jnp.int32)
    places = jnp.stack(
        [sum(jnp.where(owners[p] == b, p, 0) for p in range(ns)) for b in range(ns)]
    ).astype(jnp.int32)
    offset = (lax.axis_index("dp") * share).astype(jnp.int32)[None]

    numbers = jnp.where(
        valid_rows > 0, segment, rows + jnp.arange(rows, dtype=jnp.int32)
    ).astype(F32)
    ids = jnp.pad(numbers, (MARGIN, MARGIN), constant_values=-1.0).reshape(-1, SUB)
    ids = jnp.pad(ids, ((0, -ids.shape[0] % 8), (0, 0)), constant_values=-1.0)

    shard = widened([fc1_w, fc2_w, proj_w], later_lanes)
    shard = widened([shard, qkv_w, vectors.T], later_lanes + first_lanes).astype(LOW)
    columns = over_columns(shard)
    first_own, later_own = columns[:, later_lanes:], columns[:, :later_lanes]
    first_pieces = over_rows(first_own)
    later_pieces = over_rows(later_own)[: ns // 2]

    (query, _, value, key_turned, normed_turned, mixed, probs, weight, vector_full) = (
        attend_forward(places, first_pieces, tokens, ids)
    )
    later_pieces[1:], mixed = lax.optimization_barrier((later_pieces[1:], mixed))
    later_pieces = later_pieces + [exchange(piece, "ns", 1) for piece in later_pieces]
    output, grad_residual, grad_mixed, inner, grads_near, grads_far, sums = mlp_both(
        places, owners, later_pieces, vector_full, mixed, tokens, cotangent
    )
    held = added(grads_near, exchange(grads_far, "ns", 1))
    held, grad_mixed = lax.optimization_barrier((held, grad_mixed))
    held = sum_rows(held)
    backs = []
    for pairs in BACK_CALLS:
        if backs:
            held, grad_mixed, backs = lax.optimization_barrier((held, grad_mixed, backs))
        backs.append(
            attend_backward(
                pairs, query, key_turned, value, probs, inner, grad_mixed, normed_turned
            )
        )
    later_owned = sum_columns(held)
    grads, normed_sums, column_sums = zip(*backs)
    grads_near, grads_far = weight_grad(
        places, weight, vector_full, sums, normed_sums, column_sums
    )
    first_owned = sum_columns(sum_rows(added(grads_near, exchange(grads_far, "ns", 1))))
    input_grad = input_gradient(weight, vector_full, tokens, grad_residual, grads)

    later_moment = later_owned + 0.5 * widened([fc1_m, fc2_m, proj_m], later_lanes)
    columns = over_columns(later_moment.astype(LOW))
    tasks = jnp.array(((0, 0, width), (3, 0, width)) + ((4, 2 * SUB, 2 * SUB + proj_w.shape[1]),) * 2)
    tasks = tasks.astype(jnp.int32)
    starts = jnp.stack([tasks[index ^ mask, 0] for mask in range(ns)])
    chosen = pick(starts, columns)
    blocks = [chosen[0]] + [exchange(chosen[mask], "ns", mask) for mask in range(1, ns)]
    numbers = jnp.concatenate([offset, tasks[index, 1:]])
    left = newton(numbers, blocks, share)
    lefts = [left] + [exchange(left, "ns", mask) for mask in range(1, ns)]
    which = jnp.stack([index ^ owner for owner in range(3)]).astype(jnp.int32)
    fc1_new, fc2_new, proj_new = finish(
        [w.shape[1] * ns for w in (fc1_w, fc2_w, proj_w)],
        (0, width, 2 * width),
        which,
        columns,
        lefts,
        (fc1_w, fc2_w, proj_w),
    )

    first_moment = first_owned + 0.5 * widened([qkv_m], first_lanes)
    first_pieces = over_rows(over_columns(first_moment.astype(LOW)))
    qkv_new = muon(count * ns, offset, first_pieces, qkv_w)
    news = (qkv_new, proj_new, fc1_new, fc2_new)
    moments_new = (
        first_moment[:, :count],
        later_moment[:, 2 * width : 2 * width + proj_w.shape[1]],
        later_moment[:, :width],
        later_moment[:, width : 2 * width],
    )

    vector_grad = first_owned[:, count : count + vec_rows].T
    first_new = BETA_ONE * vector_moment + (1.0 - BETA_ONE) * vector_grad
    second_new = BETA_TWO * vector_square + (1.0 - BETA_TWO) * vector_grad * vector_grad
    first_hat = first_new / (1.0 - BETA_ONE**STEP)
    second_hat = second_new / (1.0 - BETA_TWO**STEP)
    vectors_new = vectors - ADAM_RATE * first_hat / (jnp.sqrt(second_hat) + ADAM_EPS)
    return (
        output,
        input_grad,
        *(new[0].T for new in news),
        *(m.T for m in moments_new),
        first_new,
        second_new,
        vectors_new,
        *(new[1].T for new in news),
    )


def solution(mesh):
    rows = P(("dp", "ns"), None)
    flat = P(("dp", "ns"))
    block = P("ns", "dp")
    return jax.shard_map(
        per_device,
        mesh=mesh,
        in_specs=(rows, rows, flat, flat) + (block,) * 11,
        out_specs=(rows, rows) + (block,) * 15,
        check_vma=False,
    )
```

```python
import math

import jax
import jax.numpy as jnp
import numpy as np
from jax import lax
from jax.experimental import pallas as pl
from jax.experimental.pallas import tpu as pltpu
from jax.sharding import PartitionSpec as P

HEADS = 6
PAIRS = 3
MARGIN = 128
NS_STEPS = 5
STEP = 10
TILE = 256
MLP_TILE = 512
FF_CHUNK = 512
SUB = 128
SPAN = 384
VEC_LANES = 16
BACK_CALLS = ((0, 1, 2),)


EPS_NORM = 1e-06
NEWTON_A = 3.4445
NEWTON_B = -4.775
NEWTON_C = 2.0315
MUON_RATE = 0.2
MUON_DECAY = 0.1
ADAM_RATE = 0.4
BETA_ONE = 0.9
BETA_TWO = 0.999
ADAM_EPS = 1e-08
LOW = jnp.bfloat16
F32 = jnp.float32
TN = (((0,), (0,)), ((), ()))
NT = (((1,), (1,)), ((), ()))
NN = (((1,), (0,)), ((), ()))
VMEM_LIMIT = 56 * 1024 * 1024
ERF_P = 0.3275911
ERF_COEFS = (0.254829592, -0.284496736, 1.421413741, -1.453152027, 1.061405429)


def dot(left, right, dims=NN):
    return lax.dot_general(left, right, dims, preferred_element_type=F32)


PLACES, OWNERS, STARTS, WHICH, OFFSET, LOW_LANE, HIGH_LANE = 0, 4, 8, 12, 16, 17, 18


def lane_numbers(shape):
    return lax.broadcasted_iota(jnp.int32, shape, len(shape) - 1)


def norm_parts(value):
    center = value - jnp.mean(value, axis=-1, keepdims=True)
    rate = lax.rsqrt(jnp.mean(center * center, axis=-1, keepdims=True) + EPS_NORM)
    return center * rate, rate


def norm_back(grad, normed, rate, gain):
    scaled = grad * gain
    first = jnp.mean(scaled, axis=-1, keepdims=True)
    second = jnp.mean(scaled * normed, axis=-1, keepdims=True)
    return rate * (scaled - first - normed * second)


def gelu_both(value):
    ratio = 1.0 / (1.0 + (ERF_P * 0.5**0.5) * jnp.abs(value))
    decay = jnp.exp2((value * value) * (-0.5 * math.log2(math.e)))
    poly = 0.5 * ERF_COEFS[4]
    for coef in ERF_COEFS[3::-1]:
        poly = poly * ratio + 0.5 * coef
    tail = poly * ratio * decay
    phi = jnp.where(value >= 0, 1.0 - tail, tail)
    return value * phi, phi + value * decay * (1.0 / math.sqrt(2.0 * math.pi))


def gelu_rows(hidden, grad):
    active, back = [], []
    for row in range(0, hidden.shape[0], 16):
        value, slope = gelu_both(hidden[row : row + 16])
        active.append(value.astype(LOW))
        back.append((grad[row : row + 16] * slope).astype(LOW))
    return jnp.concatenate(active, axis=0), jnp.concatenate(back, axis=0)


def halves_of(lanes):
    half = lanes.shape[0] // 2
    return lanes[:half, :SUB], lanes[half:, SUB:]


def staged(count, first, second, third):
    made = [first(0)]
    kept = None
    for n in range(count):
        if n + 1 < count:
            made.append(first(n + 1))
        if kept is not None:
            third(n - 1, kept)
        kept = second(n, made[n])
        made[n] = None
    third(count - 1, kept)


def both_heads(pair):
    first = (lane_numbers((1, SUB)) < SUB // 2).astype(F32).astype(pair.dtype)
    second = (lane_numbers((1, SUB)) >= SUB // 2).astype(F32).astype(pair.dtype)
    return jnp.concatenate([pair * first, pair * second], axis=0)


def fetch(pairs, sems):
    copies = [
        pltpu.make_async_copy(source, target, sems.at[n])
        for n, (source, target) in enumerate(pairs)
    ]
    for copy in copies:
        copy.start()
    for copy in copies:
        copy.wait()


def attend_kernel(numbers, *refs):
    (tokens, ids, query, key, value, key_turned, normed_turned, mixed, probs, weight, vectors,
     gathered, pair_weight, value_turned, columns, shifts, sems) = refs[-17:]
    pieces = refs[:-17]
    step = pl.program_id(0)
    chunks = pl.num_programs(0) - 1
    width = tokens.shape[1]
    parts = len(pieces)
    block = 3 * width // parts
    rows_each = 12 // parts

    @pl.when(step == 0)
    def assemble():
        fetch([(piece, gathered.at[n]) for n, piece in enumerate(pieces)], sems)
        total = jnp.zeros((width, 3 * width), F32)
        turned = jnp.zeros((width, SUB), F32)
        for number in range(parts):
            piece = gathered[numbers[PLACES + number]].astype(F32)
            kept = jnp.where(lane_numbers(piece.shape) < block, piece, 0.0)
            wide = jnp.concatenate([kept, jnp.zeros((width, 2 * width), F32)], axis=1)
            total = total + (pltpu.roll(wide, block * number, 1) if number else wide)
            last = piece[:, 2 * SUB :]
            at = block - 2 * SUB
            lane = lane_numbers(last.shape)
            vec = jnp.where((lane >= at) & (lane < at + rows_each), last, 0.0)
            turned = turned + pltpu.roll(vec, (rows_each * number - at) % SUB, 1)
        total = total.astype(LOW)
        weight[...] = total
        pair_weight[...] = total[:, width:].T
        vectors[...] = turned.T[:VEC_LANES]
        shifts[...] = turned
        edges = (pl.ds(0, MARGIN), pl.ds(MARGIN + chunks * TILE, MARGIN))
        for edge in edges:
            for ref in (query, key, value):
                ref[edge, :] = jnp.zeros((MARGIN, width), LOW)
            for ref in (key_turned, value_turned):
                ref[:, edge] = jnp.zeros((width, MARGIN), LOW)
        for number in range(chunks * TILE // SUB + 2):
            row = jnp.broadcast_to(ids[number : number + 1, :], (SUB, SUB))
            columns[number * SUB : (number + 1) * SUB, :] = row.T

    @pl.when(step < chunks)
    def project():
        normed, _ = norm_parts(tokens[...].astype(F32))
        normed_turned[...] = normed.astype(LOW).T
        first_in = (normed * vectors[0:1, :] + vectors[1:2, :]).astype(LOW)
        result = dot(first_in, weight[...])
        turned = dot(pair_weight[...], first_in, NT)
        here = pl.ds(pl.multiple_of(MARGIN + step * TILE, SUB), TILE)
        scale = (width // HEADS) ** (-0.5)
        made = (result[:, :width] + vectors[2:3, :]).astype(LOW) * jnp.asarray(scale, LOW)
        query[here, :] = made
        key[here, :] = result[:, width : 2 * width].astype(LOW)
        value[here, :] = (result[:, 2 * width :] + vectors[3:4, :]).astype(LOW)
        key_turned[:, here] = turned[:width].astype(LOW)
        value_turned[:, here] = (turned[width:] + shifts[:, 3:4]).astype(LOW)

    @pl.when(step > 0)
    def attend():
        def place(number):
            sub, pair = number // PAIRS, number % PAIRS
            tile = (step - 1) * (TILE // SUB) + sub
            start = pl.multiple_of(tile * SUB, SUB)
            return sub, pair, tile, start, pl.ds(start, SPAN), pl.ds(pair * SUB, SUB)

        def score(number):
            _, _, _, start, near_rows, heads = place(number)
            wanted = both_heads(query[pl.ds(start + MARGIN, SUB), heads])
            return dot(key[near_rows, heads], wanted, NT)

        def soften(number, scores):
            sub, pair, tile, _, near_rows, _ = place(number)
            row = ids[pl.ds(tile + 1, 1), :]
            both = []
            for head in range(2):
                same = columns[near_rows, :] == row
                own = jnp.where(same, scores[:, head * SUB : (head + 1) * SUB], -1e30)
                expo = jnp.exp(own - jnp.max(own, axis=0, keepdims=True))
                share = 1.0 / jnp.sum(expo, axis=0, keepdims=True)
                both.append((expo * share).astype(LOW))
            prob = jnp.concatenate(both, axis=1)
            probs[pair, sub] = prob
            return prob

        def mix(number, prob):
            sub, _, _, _, near_rows, heads = place(number)
            first, second = halves_of(dot(value_turned[heads, near_rows], prob))
            turned = jnp.concatenate([first, second], axis=0).astype(LOW)
            mixed[pl.ds(sub * SUB, SUB), heads] = turned.T

        staged(TILE // SUB * PAIRS, score, soften, mix)


def attend_forward(numbers, pieces, tokens, ids):
    rows, width = tokens.shape
    chunks = rows // TILE
    tiles = TILE // SUB
    parts = len(pieces)
    now = lambda s: jnp.minimum(s, chunks - 1)
    before = lambda s: jnp.maximum(s - 1, 0)
    whole = lambda *dims: pl.BlockSpec(dims, lambda s, *_: (0,) * len(dims))
    padded = rows + 2 * MARGIN
    return pl.pallas_call(
        attend_kernel,
        grid_spec=pltpu.PrefetchScalarGridSpec(
            num_scalar_prefetch=1,
            grid=(chunks + 1,),
            in_specs=[pl.BlockSpec(memory_space=pl.ANY)] * parts
            + [
                pl.BlockSpec((TILE, width), lambda s, *_: (now(s), 0)),
                whole(*ids.shape),
            ],
            out_specs=[
                whole(padded, width),
                whole(padded, width),
                whole(padded, width),
                whole(width, padded),
                pl.BlockSpec((width, TILE), lambda s, *_: (0, now(s))),
                pl.BlockSpec((TILE, width), lambda s, *_: (before(s), 0)),
                pl.BlockSpec((PAIRS, tiles, SPAN, 2 * SUB), lambda s, *_: (0, before(s), 0, 0)),
                whole(width, 3 * width),
                whole(VEC_LANES, width),
            ],
            scratch_shapes=[
                pltpu.VMEM((parts, *pieces[0].shape), LOW),
                pltpu.VMEM((2 * width, width), LOW),
                pltpu.VMEM((width, padded), LOW),
                pltpu.VMEM((padded, SUB), F32),
                pltpu.VMEM((width, SUB), F32),
                pltpu.SemaphoreType.DMA((parts,)),
            ],
        ),
        out_shape=[
            jax.ShapeDtypeStruct((padded, width), LOW),
            jax.ShapeDtypeStruct((padded, width), LOW),
            jax.ShapeDtypeStruct((padded, width), LOW),
            jax.ShapeDtypeStruct((width, padded), LOW),
            jax.ShapeDtypeStruct((width, rows), LOW),
            jax.ShapeDtypeStruct((rows, width), LOW),
            jax.ShapeDtypeStruct((PAIRS, rows // SUB, SPAN, 2 * SUB), LOW),
            jax.ShapeDtypeStruct((width, 3 * width), LOW),
            jax.ShapeDtypeStruct((VEC_LANES, width), F32),
        ],
        compiler_params=pltpu.CompilerParams(vmem_limit_bytes=VMEM_LIMIT),
        cost_estimate=pl.CostEstimate(
            flops=12_000_000_000, bytes_accessed=22_000_000, transcendentals=5_000_000
        ),
        name="attend_forward",
    )(numbers, *pieces, tokens, ids)


def mlp_kernel(numbers, near, far, *refs):
    (vectors, mixed, tokens, cotangent, output, grad_residual, grad_mixed, inner, grads_near,
     grads_far, sums, one, two, proj_parts, proj, acc_one, acc_two, acc_proj, bias, acc_bias
    ) = refs
    step = pl.program_id(0)
    width = tokens.shape[1]
    mid = near.shape[1]
    parts = mid + far.shape[1]
    block = width // parts
    last_at = 2 * width
    hidden_width = one.shape[1]

    @pl.when(step == 0)
    def assemble():
        for part in range(parts):
            ref, at = (near, part) if part < mid else (far, part - mid)
            lanes = pl.ds(part * width, width)
            for group in range(near.shape[0]):
                here = pl.ds(group * near.shape[2], near.shape[2])
                one[here, lanes] = ref[group, at, :, :width]
                two[here, lanes] = ref[group, at, :, width:last_at]
                proj_parts[part, here, :] = ref[group, at, :, last_at:]
        total = jnp.zeros((width, width), F32)
        for number in range(parts):
            piece = proj_parts[numbers[PLACES + number]].astype(F32)
            kept = jnp.where(lane_numbers(piece.shape) < block, piece, 0.0)
            wide = jnp.concatenate([kept, jnp.zeros((width, width - SUB), F32)], axis=1)
            total = total + (pltpu.roll(wide, block * number, 1) if number else wide)
        proj[...] = total.astype(LOW)
        for part in range(parts):
            row = vectors[pl.ds(8 + numbers[OWNERS + part], 1), :]
            bias[0:1, part * width : (part + 1) * width] = row
        acc_one[...] = jnp.zeros(acc_one.shape, F32)
        acc_two[...] = jnp.zeros(acc_two.shape, F32)
        acc_proj[...] = jnp.zeros(acc_proj.shape, F32)
        acc_bias[...] = jnp.zeros(acc_bias.shape, F32)
        sums[...] = jnp.zeros(sums.shape, F32)

    def add_row(row, values):
        sums[pl.ds(row, 1), :] += jnp.sum(values, axis=0, keepdims=True)

    own = mixed[...]
    residual = tokens[...].astype(F32) + dot(own, proj[...], NT) + vectors[4:5, :]
    normed, rate = norm_parts(residual)
    gain = vectors[5:6, :]
    second_in = (normed * gain + vectors[6:7, :]).astype(LOW)
    out_low = cotangent[...]
    grad_out = out_low.astype(F32)
    second_turned = second_in.T
    out_turned = out_low.T
    totals = [residual + vectors[7:8, :], jnp.zeros(residual.shape, F32)]

    def first(number):
        lanes = pl.ds(number * FF_CHUNK, FF_CHUNK)
        return dot(second_in, one[:, lanes]), dot(out_low, two[:, lanes])

    def second(number, made):
        lanes = pl.ds(number * FF_CHUNK, FF_CHUNK)
        active, grad_hidden = gelu_rows(made[0] + bias[0:1, lanes], made[1])
        acc_bias[0:1, lanes] += jnp.sum(grad_hidden.astype(F32), axis=0, keepdims=True)
        return active, grad_hidden

    def third(number, kept):
        lanes = pl.ds(number * FF_CHUNK, FF_CHUNK)
        active, grad_hidden = kept
        acc_one[:, lanes] += dot(second_turned, grad_hidden)
        acc_two[:, lanes] += dot(out_turned, active)
        totals[0] = totals[0] + dot(active, two[:, lanes], NT)
        totals[1] = totals[1] + dot(grad_hidden, one[:, lanes], NT)

    staged(hidden_width // FF_CHUNK, first, second, third)
    result, grad_second = totals
    output[...] = result.astype(LOW)
    add_row(5, grad_second * normed)
    add_row(6, grad_second)
    add_row(7, grad_out)
    grad_res = grad_out + norm_back(grad_second, normed, rate, gain)
    grad_residual[...] = grad_res
    branch = grad_res.astype(LOW)
    add_row(4, branch.astype(F32))
    acc_proj[...] += dot(branch.T, own)
    grad_own = dot(branch, proj[...]).astype(LOW)
    grad_mixed[...] = grad_own
    high, rest = halves(grad_own.astype(F32) * own.astype(F32))
    head = lax.broadcasted_iota(jnp.int32, (16, width), 0)
    chosen = (lane_numbers((16, width)) // (width // HEADS) == head).astype(F32).astype(LOW)
    inner[...] = (dot(chosen, high, NT) + dot(chosen, rest, NT))[:8]

    @pl.when(step == pl.num_programs(0) - 1)
    def finish():
        total = acc_proj[...]
        for number in range(parts):
            turned = pltpu.roll(total, (width - block * number) % width, 1) if number else total
            proj_parts[numbers[PLACES + number]] = turned[:, :SUB].astype(LOW)
        for part in range(parts):
            ref, at = (grads_near, part) if part < mid else (grads_far, part - mid)
            lanes = pl.ds(part * width, width)
            ref[at, :, :width] = acc_one[:, lanes].astype(LOW)
            ref[at, :, width:last_at] = acc_two[:, lanes].astype(LOW)
            ref[at, :, last_at:] = proj_parts[part]
            sums[pl.ds(8 + numbers[OWNERS + part], 1), :] = acc_bias[0:1, lanes]


def mlp_both(numbers, near, far, vectors, mixed, tokens, cotangent):
    rows, width = tokens.shape
    parts = near.shape[1] + far.shape[1]
    half = (parts // 2, width, near.shape[3])
    hidden_width = parts * width
    tile = pl.BlockSpec((MLP_TILE, width), lambda s, *_: (s, 0))
    whole = lambda *dims: pl.BlockSpec(dims, lambda s, *_: (0,) * len(dims))
    return pl.pallas_call(
        mlp_kernel,
        grid_spec=pltpu.PrefetchScalarGridSpec(
            num_scalar_prefetch=1,
            grid=(rows // MLP_TILE,),
            in_specs=[
                whole(*near.shape), whole(*far.shape), whole(*vectors.shape), tile, tile, tile
            ],
            out_specs=[
                tile,
                tile,
                tile,
                pl.BlockSpec((8, MLP_TILE), lambda s, *_: (0, s)),
                whole(*half),
                whole(*half),
                whole(*vectors.shape),
            ],
            scratch_shapes=[
                pltpu.VMEM((width, hidden_width), LOW),
                pltpu.VMEM((width, hidden_width), LOW),
                pltpu.VMEM((parts, width, SUB), LOW),
                pltpu.VMEM((width, width), LOW),
                pltpu.VMEM((width, hidden_width), F32),
                pltpu.VMEM((width, hidden_width), F32),
                pltpu.VMEM((width, width), F32),
                pltpu.VMEM((8, hidden_width), F32),
                pltpu.VMEM((8, hidden_width), F32),
            ],
        ),
        out_shape=[
            jax.ShapeDtypeStruct((rows, width), LOW),
            jax.ShapeDtypeStruct((rows, width), F32),
            jax.ShapeDtypeStruct((rows, width), LOW),
            jax.ShapeDtypeStruct((8, rows), F32),
            jax.ShapeDtypeStruct(half, LOW),
            jax.ShapeDtypeStruct(half, LOW),
            jax.ShapeDtypeStruct(vectors.shape, F32),
        ],
        compiler_params=pltpu.CompilerParams(vmem_limit_bytes=VMEM_LIMIT),
        cost_estimate=pl.CostEstimate(
            flops=34_000_000_000, bytes_accessed=20_000_000, transcendentals=6_000_000
        ),
        name="mlp_both",
    )(numbers, near, far, vectors, mixed, tokens, cotangent)


def attend_back_kernel(
    pairs,
    query,
    key_turned,
    value,
    probs,
    inner,
    grad_mixed,
    normed_turned,
    grad_qkv,
    normed_sums,
    column_sums,
    grad_query,
    acc_key,
    acc_value,
    acc_sums,
):
    step = pl.program_id(0)
    chunks = pl.num_programs(0) - 1
    count = len(pairs)
    scale = (SUB // 2) ** (-0.5)

    @pl.when(step == 0)
    def clear():
        acc_key[...] = jnp.zeros(acc_key.shape, F32)
        acc_value[...] = jnp.zeros(acc_value.shape, F32)
        normed_sums[...] = jnp.zeros(normed_sums.shape, F32)
        acc_sums[...] = jnp.zeros(acc_sums.shape, F32)

    @pl.when(step < chunks)
    def attend():
        def place(number):
            sub, at = number // count, number % count
            start = pl.multiple_of((step * (TILE // SUB) + sub) * SUB, SUB)
            return sub, at, start, pl.ds(start, SPAN), pl.ds(at * SUB, SUB)

        def slope(number):
            sub, _, _, near_rows, heads = place(number)
            grad = both_heads(grad_mixed[pl.ds(sub * SUB, SUB), heads])
            return dot(value[near_rows, heads], grad, NT)

        def soften(number, slopes):
            sub, at, _, _, _ = place(number)
            pair = pairs[at]
            cols = pl.ds(sub * SUB, SUB)
            both = []
            for head in range(2):
                lanes = slice(head * SUB, (head + 1) * SUB)
                less = slopes[:, lanes] - inner[2 * pair + head : 2 * pair + head + 1, cols]
                both.append((probs[at, sub, :, lanes].astype(F32) * less).astype(LOW))
            return jnp.concatenate(both, axis=1)

        def collect(number, scores):
            sub, at, start, near_rows, heads = place(number)
            first, second = halves_of(dot(key_turned[heads, near_rows], scores))
            turned = (jnp.concatenate([first, second], axis=0) * scale).astype(LOW)
            grad_query[pl.ds(start, SUB), heads] = turned.T
            wanted = both_heads(query[pl.ds(start + MARGIN, SUB), heads])
            acc_key[near_rows, heads] += dot(scores, wanted)
            grad = both_heads(grad_mixed[pl.ds(sub * SUB, SUB), heads])
            acc_value[near_rows, heads] += dot(probs[at, sub], grad)

        staged(TILE // SUB * count, slope, soften, collect)

    @pl.when(step > 0)
    def collect():
        here = pl.ds(pl.multiple_of((step - 1) * TILE, SUB), TILE)
        there = pl.ds(pl.multiple_of((step - 1) * TILE + MARGIN, SUB), TILE)
        parts = (
            grad_query[here, :],
            acc_key[there, :].astype(LOW),
            acc_value[there, :].astype(LOW),
        )
        joined = jnp.concatenate(parts, axis=1)
        grad_qkv[...] = joined
        normed_sums[...] += dot(normed_turned[...], joined)
        acc_sums[0:1, :] += jnp.sum(joined.astype(F32), axis=0, keepdims=True)

    @pl.when(step == chunks)
    def finish():
        column_sums[...] = acc_sums[...]


def attend_backward(pairs, query, key_turned, value, probs, inner, grad_mixed, normed_turned):
    width, rows = normed_turned.shape
    padded = query.shape[0]
    chunks = rows // TILE
    tiles = TILE // SUB
    count = len(pairs)
    lanes = count * SUB
    which = pairs[0] // count
    assert pairs[0] % count == 0
    now = lambda s: jnp.minimum(s, chunks - 1)
    before = lambda s: jnp.maximum(s - 1, 0)
    normal = pl.BlockSpec((padded, lanes), lambda s: (0, which))

    def kernel(*refs):
        attend_back_kernel(pairs, *refs)

    return pl.pallas_call(
        kernel,
        grid=(chunks + 1,),
        in_specs=[
            normal,
            pl.BlockSpec((lanes, padded), lambda s: (which, 0)),
            normal,
            pl.BlockSpec((count, tiles, SPAN, 2 * SUB), lambda s: (which, now(s), 0, 0)),
            pl.BlockSpec((8, TILE), lambda s: (0, now(s))),
            pl.BlockSpec((TILE, lanes), lambda s: (now(s), which)),
            pl.BlockSpec((width, TILE), lambda s: (0, before(s))),
        ],
        out_specs=[
            pl.BlockSpec((TILE, 3 * lanes), lambda s: (before(s), 0)),
            pl.BlockSpec((width, 3 * lanes), lambda s: (0, 0)),
            pl.BlockSpec((8, 3 * lanes), lambda s: (0, 0)),
        ],
        out_shape=[
            jax.ShapeDtypeStruct((rows, 3 * lanes), LOW),
            jax.ShapeDtypeStruct((width, 3 * lanes), F32),
            jax.ShapeDtypeStruct((8, 3 * lanes), F32),
        ],
        scratch_shapes=[
            pltpu.VMEM((rows, lanes), LOW),
            pltpu.VMEM((padded, lanes), F32),
            pltpu.VMEM((padded, lanes), F32),
            pltpu.VMEM((8, 3 * lanes), F32),
        ],
        compiler_params=pltpu.CompilerParams(vmem_limit_bytes=VMEM_LIMIT),
        cost_estimate=pl.CostEstimate(
            flops=5_000_000_000 * count, bytes_accessed=7_000_000 * count, transcendentals=0
        ),
        name="attend_backward",
    )(query, key_turned, value, probs, inner, grad_mixed, normed_turned)


def in_order(pieces):
    return jnp.concatenate(
        [
            piece[:, n * piece.shape[1] // 3 : (n + 1) * piece.shape[1] // 3]
            for n in range(3)
            for piece in pieces
        ],
        axis=1,
    )


def weight_grad_kernel(numbers, weight, vectors, sums, *refs):
    count = (len(refs) - 4) // 2
    normed_sums, column_sums = refs[:count], refs[count : 2 * count]
    near, far, blocks, rows = refs[2 * count :]
    width = weight.shape[0]
    parts, mid = blocks.shape[0], near.shape[0]
    block = 3 * width // parts
    rows_each = 12 // parts
    total = in_order([ref[...] for ref in normed_sums])
    columns = in_order([ref[0:1, :] for ref in column_sums])
    wide = weight[...].astype(F32)
    grad_gain = jnp.sum(total * wide, axis=1, keepdims=True)
    grad_shift = jnp.sum(wide * columns, axis=1, keepdims=True)
    rows[...] = jnp.zeros(rows.shape, F32)
    rows[0:VEC_LANES, :] = sums[...]
    rows[2:3, :] = columns[:, :width]
    rows[3:4, :] = columns[:, 2 * width :]
    rows[VEC_LANES : 2 * VEC_LANES, :] = vectors[...]
    turned = rows[...].T
    gain = turned[:, VEC_LANES : VEC_LANES + 1]
    shift = turned[:, VEC_LANES + 1 : VEC_LANES + 2]
    lane = lane_numbers(turned.shape)
    turned = jnp.where(lane == 0, grad_gain, jnp.where(lane == 1, grad_shift, turned))
    total = total * gain + shift * columns
    at = block - 2 * SUB
    for number in range(parts):
        away = (3 * width - block * number) % (3 * width)
        piece = (pltpu.roll(total, away, 1) if number else total)[:, :width]
        vec = pltpu.roll(turned, (at - rows_each * number) % SUB, 1)
        last = jnp.where(lane < at, piece[:, 2 * SUB :], 0.0)
        last = jnp.where((lane >= at) & (lane < at + rows_each), vec, last)
        at_place = numbers[PLACES + number]
        blocks[at_place, :, : 2 * SUB] = piece[:, : 2 * SUB].astype(LOW)
        blocks[at_place, :, 2 * SUB :] = last.astype(LOW)
    near[...] = blocks[:mid]
    far[...] = blocks[mid:]


def weight_grad(numbers, parts, weight, vectors, sums, normed_sums, column_sums):
    width = weight.shape[0]
    half = jax.ShapeDtypeStruct((parts // 2, width, width), LOW)
    vmem = pl.BlockSpec(memory_space=pltpu.VMEM)
    return pl.pallas_call(
        weight_grad_kernel,
        in_specs=[pl.BlockSpec(memory_space=pltpu.SMEM)] + [vmem] * (3 + 2 * len(normed_sums)),
        out_specs=[vmem, vmem],
        out_shape=[half, half],
        scratch_shapes=[pltpu.VMEM((parts, width, width), LOW), pltpu.VMEM((SUB, width), F32)],
        compiler_params=pltpu.CompilerParams(vmem_limit_bytes=VMEM_LIMIT),
        cost_estimate=pl.CostEstimate(
            flops=3_000_000, bytes_accessed=5_000_000, transcendentals=0
        ),
        name="weight_grad",
    )(numbers, weight, vectors, sums, *normed_sums, *column_sums)


def input_grad_kernel(weight, vectors, tokens, grad_residual, *refs):
    grads, (input_grad, turned) = refs[:-2], refs[-2:]

    @pl.when(pl.program_id(0) == 0)
    def assemble():
        turned[...] = weight[...].T

    joined = in_order([ref[...] for ref in grads])
    normed, rate = norm_parts(tokens[...].astype(F32))
    back = norm_back(dot(joined, turned[...]), normed, rate, vectors[0:1, :])
    input_grad[...] = (grad_residual[...] + back).astype(LOW)


def input_gradient(weight, vectors, tokens, grad_residual, grads):
    rows, width = tokens.shape
    tile = pl.BlockSpec((TILE, width), lambda s: (s, 0))
    whole = lambda ref: pl.BlockSpec(ref.shape, lambda s: (0, 0))
    return pl.pallas_call(
        input_grad_kernel,
        grid=(rows // TILE,),
        in_specs=[whole(weight), whole(vectors), tile, tile]
        + [pl.BlockSpec((TILE, grad.shape[1]), lambda s: (s, 0)) for grad in grads],
        out_specs=tile,
        out_shape=jax.ShapeDtypeStruct((rows, width), LOW),
        scratch_shapes=[pltpu.VMEM((3 * width, width), LOW)],
        compiler_params=pltpu.CompilerParams(vmem_limit_bytes=VMEM_LIMIT),
        cost_estimate=pl.CostEstimate(
            flops=4_000_000_000, bytes_accessed=13_000_000, transcendentals=2048
        ),
        name="input_gradient",
    )(weight, vectors, tokens, grad_residual, *grads)


def halves(value):
    high = value.astype(LOW)
    return high, (value - high.astype(F32)).astype(LOW)


def dot_three(left, right):
    tall = jnp.concatenate([right[0], right[0], right[1]], axis=0)
    return dot(jnp.concatenate([left[0], left[1], left[0]], axis=1), tall)


def newton_rows(blocks, offset, rows):
    gram = dot(blocks[0], blocks[0], NT)
    for part in blocks[1:]:
        gram = gram + dot(part, part, NT)
    depth = gram.shape[0]
    down = lax.broadcasted_iota(jnp.int32, (depth, depth), 0)
    eye = (down == lane_numbers((depth, depth))).astype(F32)
    norm = 1.0 / (jnp.sqrt(jnp.sum(gram * eye, keepdims=True)) + 1e-07)
    gram = gram * (norm * norm)
    place = lax.broadcasted_iota(jnp.int32, (rows, depth), 0) + offset
    left = jnp.where(place == lane_numbers((rows, depth)), norm, 0.0)
    for step in range(NS_STEPS - 1):
        pair = halves(gram)
        poly = halves(NEWTON_A * eye + NEWTON_B * gram + NEWTON_C * dot_three(pair, pair))
        lefts = halves(left)
        both = dot_three([jnp.concatenate([pair[n], lefts[n]], axis=0) for n in range(2)], poly)
        left = both[depth:]
        gram = dot_three(halves(both[:depth]), poly)
    pair = halves(gram)
    once = dot_three(halves(left), pair)
    return NEWTON_A * left + NEWTON_B * once + NEWTON_C * dot_three(halves(once), pair)


def stepped(left, own, height, old):
    high, rest = halves(left)
    ortho = (dot(high, own) + dot(rest, own))[: old.shape[0], : old.shape[1]]
    return old * (1.0 - MUON_RATE * MUON_DECAY) - (MUON_RATE * 0.2 * math.sqrt(height)) * ortho


def kept_lanes(value, low, high):
    lane = lane_numbers(value.shape)
    return jnp.where((lane >= low) & (lane < high), value.astype(F32), 0.0).astype(LOW)


def tall_of(rows):
    return -(-rows // 16) * 16


def muon_kernel(height, numbers, *refs):
    old, new, copy = refs[-3:]
    count = old.shape[1]
    blocks = [kept_lanes(ref[...], 0, count) for ref in refs[:-3]]
    left = newton_rows(blocks, numbers[OFFSET], tall_of(old.shape[0]))
    result = stepped(left, blocks[0], height, old[...])
    new[...] = result
    copy[...] = result.astype(LOW)


def muon(height, numbers, blocks, old):
    vmem = pl.BlockSpec(memory_space=pltpu.VMEM)

    def kernel(*refs):
        muon_kernel(height, *refs)

    return pl.pallas_call(
        kernel,
        in_specs=[pl.BlockSpec(memory_space=pltpu.SMEM)] + [vmem] * (len(blocks) + 1),
        out_specs=[vmem, vmem],
        out_shape=[
            jax.ShapeDtypeStruct(old.shape, F32),
            jax.ShapeDtypeStruct(old.shape, LOW),
        ],
        compiler_params=pltpu.CompilerParams(vmem_limit_bytes=VMEM_LIMIT),
        cost_estimate=pl.CostEstimate(
            flops=9_000_000_000, bytes_accessed=2_000_000, transcendentals=10
        ),
        name="muon",
    )(numbers, *blocks, old)


def pick_kernel(numbers, columns, *outs):
    for n, out in enumerate(outs):
        at = pl.multiple_of(numbers[STARTS + n] * SUB, SUB)
        out[...] = columns[:, pl.ds(at, out.shape[1])]


def pick(numbers, columns, count):
    depth = columns.shape[0]
    vmem = pl.BlockSpec(memory_space=pltpu.VMEM)
    return pl.pallas_call(
        pick_kernel,
        in_specs=[pl.BlockSpec(memory_space=pltpu.SMEM), vmem],
        out_specs=[vmem] * count,
        out_shape=[jax.ShapeDtypeStruct((depth, depth), LOW)] * count,
        name="pick",
    )(numbers, columns)


def newton_kernel(numbers, *refs):
    left = refs[-1]
    bounds = numbers[LOW_LANE], numbers[HIGH_LANE]
    blocks = [kept_lanes(ref[...], *bounds) for ref in refs[:-1]]
    left[...] = newton_rows(blocks, numbers[OFFSET], left.shape[0])


def newton(numbers, blocks, rows):
    vmem = pl.BlockSpec(memory_space=pltpu.VMEM)
    return pl.pallas_call(
        newton_kernel,
        in_specs=[pl.BlockSpec(memory_space=pltpu.SMEM)] + [vmem] * len(blocks),
        out_specs=vmem,
        out_shape=jax.ShapeDtypeStruct((tall_of(rows), blocks[0].shape[0]), F32),
        compiler_params=pltpu.CompilerParams(vmem_limit_bytes=VMEM_LIMIT),
        cost_estimate=pl.CostEstimate(
            flops=9_000_000_000, bytes_accessed=2_000_000, transcendentals=10
        ),
        name="newton",
    )(numbers, *blocks)


def finish_kernel(heights, lanes, numbers, columns, *refs):
    count = len(heights)
    store = refs[-1]
    news = refs[-1 - 2 * count : -1]
    olds = refs[-1 - 3 * count : -1 - 2 * count]
    lefts = refs[: -1 - 3 * count]
    for n, left in enumerate(lefts):
        store[n] = left[...]
    for n in range(count):
        wide = -(-olds[n].shape[1] // SUB) * SUB
        own = columns[:, lanes[n] : lanes[n] + wide]
        result = stepped(store[numbers[WHICH + n]], own, heights[n], olds[n][...])
        news[2 * n][...] = result
        news[2 * n + 1][...] = result.astype(LOW)


def finish(heights, lanes, numbers, columns, lefts, olds):
    vmem = pl.BlockSpec(memory_space=pltpu.VMEM)
    count = len(olds)

    def kernel(*refs):
        finish_kernel(heights, lanes, *refs)

    outs = pl.pallas_call(
        kernel,
        in_specs=[pl.BlockSpec(memory_space=pltpu.SMEM)] + [vmem] * (1 + len(lefts) + count),
        out_specs=[vmem] * (2 * count),
        out_shape=[
            jax.ShapeDtypeStruct(old.shape, kind) for old in olds for kind in (F32, LOW)
        ],
        scratch_shapes=[pltpu.VMEM((len(lefts), *lefts[0].shape), F32)],
        compiler_params=pltpu.CompilerParams(vmem_limit_bytes=VMEM_LIMIT),
        cost_estimate=pl.CostEstimate(
            flops=200_000_000, bytes_accessed=2_000_000, transcendentals=0
        ),
        name="finish",
    )(numbers, columns, *lefts, *olds)
    return [(outs[2 * n], outs[2 * n + 1]) for n in range(count)]


def exchange(x, axis, mask):
    size = lax.axis_size(axis)
    return lax.ppermute(x, axis, [(i, i ^ mask) for i in range(size)])


def place_masks(size):
    masks = [0]
    bit = size // 2
    while bit >= 1:
        masks = masks + [m ^ bit for m in masks]
        bit //= 2
    return masks


def from_columns(own):
    size = lax.axis_size("dp")
    sent = jnp.broadcast_to(own[None], (size, *own.shape))
    return lax.all_to_all(sent, "dp", split_axis=0, concat_axis=0, tiled=True)


def over_columns(own):
    return from_columns(own).reshape(-1, own.shape[1])


def device_numbers(dp, ns, share, width, proj_rows):
    masks = place_masks(ns)
    tasks = [(0, 0, width), (width // SUB, 0, width)]
    tasks += [(width // SUB + 1, 2 * SUB, 2 * SUB + proj_rows)] * (ns - 2)
    table = np.zeros((dp * ns, 24), np.int32)
    for device in range(dp * ns):
        column, index = device // ns, device % ns
        row = table[device]
        for n in range(ns):
            row[OWNERS + n] = index ^ masks[n]
            row[PLACES + (index ^ masks[n])] = n
            row[STARTS + n] = tasks[index ^ n][0]
        for n in range(3):
            row[WHICH + n] = index ^ n
        row[OFFSET] = column * share
        row[LOW_LANE], row[HIGH_LANE] = tasks[index][1:]
    return table


def over_rows(own):
    held = [own]
    bit = lax.axis_size("ns") // 2
    while bit >= 1:
        held = held + [exchange(block, "ns", bit) for block in held]
        bit //= 2
    return held


def added(keep, got):
    return (keep.astype(F32) + got.astype(F32)).astype(LOW)


def sum_rows(held):
    bit = 2
    while held.shape[0] > 1:
        half = held.shape[0] // 2
        held = added(held[:half], exchange(held[half:], "ns", bit))
        bit *= 2
    return held[0]


def sum_columns(held):
    devices = lax.axis_size("dp")
    pieces = held.reshape(devices, -1, held.shape[-1])
    got = lax.all_to_all(pieces, "dp", split_axis=0, concat_axis=0, tiled=True)
    return jnp.sum(got.astype(F32), axis=0)


def widened(arrays, lanes):
    joined = jnp.concatenate(arrays, axis=1)
    return jnp.pad(joined, ((0, 0), (0, lanes - joined.shape[1])))


def per_device(
    tokens,
    cotangent,
    segment,
    valid_rows,
    qkv_weight,
    proj_weight,
    fc1_weight,
    fc2_weight,
    qkv_moment,
    proj_moment,
    fc1_moment,
    fc2_moment,
    vectors,
    vector_moment,
    vector_square,
):
    rows, width = tokens.shape
    ns = lax.axis_size("ns")
    qkv_w, proj_w, fc1_w, fc2_w = (w.T for w in (qkv_weight, proj_weight, fc1_weight, fc2_weight))
    qkv_m, proj_m, fc1_m, fc2_m = (w.T for w in (qkv_moment, proj_moment, fc1_moment, fc2_moment))
    share, count = qkv_w.shape
    vec_rows = vectors.shape[0]
    first_lanes = width
    later_lanes = 2 * width + SUB

    table = device_numbers(lax.axis_size("dp"), ns, share, width, proj_w.shape[1])
    device = lax.axis_index("dp") * ns + lax.axis_index("ns")
    numbers = lax.dynamic_slice(jnp.asarray(table), (device, 0), (1, table.shape[1]))[0]

    row_ids = jnp.where(
        valid_rows > 0, segment, rows + jnp.arange(rows, dtype=jnp.int32)
    ).astype(F32)
    ids = jnp.pad(row_ids, (MARGIN, MARGIN), constant_values=-1.0).reshape(-1, SUB)
    ids = jnp.pad(ids, ((0, -ids.shape[0] % 8), (0, 0)), constant_values=-1.0)

    later_own = widened([fc1_w, fc2_w, proj_w], later_lanes).astype(LOW)
    later_pair = jnp.stack([later_own, exchange(later_own, "ns", ns // 2)])
    first_own = widened([qkv_w, vectors.T], first_lanes).astype(LOW)
    first_pieces = over_rows(over_columns(first_own))
    later_near = from_columns(later_pair)
    if share % 16:
        later_near = jnp.moveaxis(later_near, 0, 1).reshape(1, ns // 2, width, later_lanes)

    (query, _, value, key_turned, normed_turned, mixed, probs, weight, vector_full) = (
        attend_forward(numbers, first_pieces, tokens, ids)
    )
    later_near, mixed = lax.optimization_barrier((later_near, mixed))
    later_far = exchange(later_near, "ns", 1)
    output, grad_residual, grad_mixed, inner, grads_near, grads_far, sums = mlp_both(
        numbers, later_near, later_far, vector_full, mixed, tokens, cotangent
    )
    held = added(grads_near, exchange(grads_far, "ns", 1))
    held, grad_mixed = lax.optimization_barrier((held, grad_mixed))
    held = sum_rows(held)
    backs = []
    for pairs in BACK_CALLS:
        if backs:
            held, grad_mixed, backs = lax.optimization_barrier((held, grad_mixed, backs))
        backs.append(
            attend_backward(
                pairs, query, key_turned, value, probs, inner, grad_mixed, normed_turned
            )
        )
    later_owned = sum_columns(held)
    grads, normed_sums, column_sums = zip(*backs)
    grads_near, grads_far = weight_grad(
        numbers, ns, weight, vector_full, sums, normed_sums, column_sums
    )
    first_held = sum_rows(added(grads_near, exchange(grads_far, "ns", 1)))
    input_grad = input_gradient(weight, vector_full, tokens, grad_residual, grads)

    later_moment = later_owned + 0.5 * widened([fc1_m, fc2_m, proj_m], later_lanes)
    columns = over_columns(later_moment.astype(LOW))
    columns, first_held = lax.optimization_barrier((columns, first_held))
    first_owned = sum_columns(first_held)
    chosen = pick(numbers, columns, ns)
    blocks = [chosen[0]] + [exchange(chosen[mask], "ns", mask) for mask in range(1, ns)]
    left = newton(numbers, blocks, share)
    lefts = [left] + [exchange(left, "ns", mask) for mask in range(1, ns)]
    fc1_new, fc2_new, proj_new = finish(
        [w.shape[1] * ns for w in (fc1_w, fc2_w, proj_w)],
        (0, width, 2 * width),
        numbers,
        columns,
        lefts,
        (fc1_w, fc2_w, proj_w),
    )

    first_moment = first_owned + 0.5 * widened([qkv_m], first_lanes)
    first_pieces = over_rows(over_columns(first_moment.astype(LOW)))
    qkv_new = muon(count * ns, numbers, first_pieces, qkv_w)
    news = (qkv_new, proj_new, fc1_new, fc2_new)
    moments_new = (
        first_moment[:, :count],
        later_moment[:, 2 * width : 2 * width + proj_w.shape[1]],
        later_moment[:, :width],
        later_moment[:, width : 2 * width],
    )

    vector_grad = first_owned[:, count : count + vec_rows].T
    first_new = BETA_ONE * vector_moment + (1.0 - BETA_ONE) * vector_grad
    second_new = BETA_TWO * vector_square + (1.0 - BETA_TWO) * vector_grad * vector_grad
    first_hat = first_new / (1.0 - BETA_ONE**STEP)
    second_hat = second_new / (1.0 - BETA_TWO**STEP)
    vectors_new = vectors - ADAM_RATE * first_hat / (jnp.sqrt(second_hat) + ADAM_EPS)
    return (
        output,
        input_grad,
        *(new[0].T for new in news),
        *(m.T for m in moments_new),
        first_new,
        second_new,
        vectors_new,
        *(new[1].T for new in news),
    )


def solution(mesh):
    rows = P(("dp", "ns"), None)
    flat = P(("dp", "ns"))
    block = P("ns", "dp")
    return jax.shard_map(
        per_device,
        mesh=mesh,
        in_specs=(rows, rows, flat, flat) + (block,) * 11,
        out_specs=(rows, rows) + (block,) * 15,
        check_vma=False,
    )
```

```python
import functools
import math

import jax
import jax.numpy as jnp
import numpy as np
from jax import lax
from jax.experimental import pallas as pl
from jax.experimental.pallas import tpu as pltpu
from jax.sharding import PartitionSpec as P

HEADS = 6
PAIRS = 3
MARGIN = 128
NS_STEPS = 5
STEP = 10
TILE = 256
MLP_TILE = 512
FF_CHUNK = 256
SUB = 128
SPAN = 384
VEC_LANES = 16


EPS_NORM = 1e-06
NEWTON_A = 3.4445
NEWTON_B = -4.775
NEWTON_C = 2.0315
MUON_RATE = 0.2
MUON_DECAY = 0.1
ADAM_RATE = 0.4
BETA_ONE = 0.9
BETA_TWO = 0.999
ADAM_EPS = 1e-08
LOW = jnp.bfloat16
F32 = jnp.float32
TN = (((0,), (0,)), ((), ()))
NT = (((1,), (1,)), ((), ()))
NN = (((1,), (0,)), ((), ()))
VMEM_LIMIT = 56 * 1024 * 1024
ERF_P = 0.3275911
ERF_COEFS = (0.254829592, -0.284496736, 1.421413741, -1.453152027, 1.061405429)


def dot(left, right, dims=NN):
    return lax.dot_general(left, right, dims, preferred_element_type=F32)


PLACES, OWNERS, STARTS, WHICH, OFFSET, LOW_LANE, HIGH_LANE, COLUMN = 0, 4, 8, 12, 16, 17, 18, 19


def lane_numbers(shape):
    return lax.broadcasted_iota(jnp.int32, shape, len(shape) - 1)


def norm_parts(value):
    center = value - jnp.mean(value, axis=-1, keepdims=True)
    rate = lax.rsqrt(jnp.mean(center * center, axis=-1, keepdims=True) + EPS_NORM)
    return center * rate, rate


def norm_back(grad, normed, rate, gain):
    scaled = grad * gain
    first = jnp.mean(scaled, axis=-1, keepdims=True)
    second = jnp.mean(scaled * normed, axis=-1, keepdims=True)
    return rate * (scaled - first - normed * second)


def gelu_both(value):
    below = 1.0 + (ERF_P * 0.5**0.5) * jnp.abs(value)
    ratio = pl.reciprocal(below, approx=True)
    ratio = ratio * (2.0 - below * ratio)
    decay = jnp.exp2((value * value) * (-0.5 * math.log2(math.e)))
    poly = 0.5 * ERF_COEFS[4]
    for coef in ERF_COEFS[3::-1]:
        poly = poly * ratio + 0.5 * coef
    tail = poly * ratio * decay
    phi = jnp.where(value >= 0, 1.0 - tail, tail)
    return value * phi, phi + (value * (1.0 / math.sqrt(2.0 * math.pi))) * decay


def gelu_rows(hidden, bias, grad, between):
    active, back = [], []
    rows = hidden.shape[0]
    pieces = rows // 16
    for n in range(pieces):
        if n * len(between) // pieces != (n - 1) * len(between) // pieces:
            between[n * len(between) // pieces]()
        here = slice(n * 16, (n + 1) * 16)
        value, slope = gelu_both(hidden[here] + bias)
        active.append(value.astype(LOW))
        back.append((grad[here] * slope).astype(LOW))
    return jnp.concatenate(active, axis=0), jnp.concatenate(back, axis=0)


def halves_of(lanes):
    half = lanes.shape[0] // 2
    return lanes[:half, :SUB], lanes[half:, SUB:]


def staged(count, first, second, third):
    made = [first(0)]
    kept = None
    for n in range(count):
        if n + 1 < count:
            made.append(first(n + 1))
        if kept is not None:
            third(n - 1, kept)
        kept = second(n, made[n])
        made[n] = None
    third(count - 1, kept)


def both_heads(pair):
    first = (lane_numbers((1, SUB)) < SUB // 2).astype(F32).astype(pair.dtype)
    second = (lane_numbers((1, SUB)) >= SUB // 2).astype(F32).astype(pair.dtype)
    return jnp.concatenate([pair * first, pair * second], axis=0)


def fetch(pairs, sems):
    copies = [
        pltpu.make_async_copy(source, target, sems.at[n])
        for n, (source, target) in enumerate(pairs)
    ]
    for copy in copies:
        copy.start()
    for copy in copies:
        copy.wait()


def attend_kernel(numbers, *refs):
    (tokens, ids, query, key, value, key_turned, normed_turned, mixed, probs, weight, vectors,
     gathered, pair_weight, value_turned, columns, shifts, sems) = refs[-17:]
    pieces = refs[:-17]
    step = pl.program_id(0)
    chunks = pl.num_programs(0) - 1
    width = tokens.shape[1]
    parts = len(pieces)
    block = 3 * width // parts
    rows_each = 12 // parts

    @pl.when(step == 0)
    def assemble():
        fetch([(piece, gathered.at[n]) for n, piece in enumerate(pieces)], sems)
        total = jnp.zeros((width, 3 * width), F32)
        turned = jnp.zeros((width, SUB), F32)
        for number in range(parts):
            piece = gathered[numbers[PLACES + number]].astype(F32)
            kept = jnp.where(lane_numbers(piece.shape) < block, piece, 0.0)
            wide = jnp.concatenate([kept, jnp.zeros((width, 2 * width), F32)], axis=1)
            total = total + (pltpu.roll(wide, block * number, 1) if number else wide)
            last = piece[:, 2 * SUB :]
            at = block - 2 * SUB
            lane = lane_numbers(last.shape)
            vec = jnp.where((lane >= at) & (lane < at + rows_each), last, 0.0)
            turned = turned + pltpu.roll(vec, (rows_each * number - at) % SUB, 1)
        total = total.astype(LOW)
        weight[...] = total
        pair_weight[...] = total[:, width:].T
        vectors[...] = turned.T[:VEC_LANES]
        shifts[...] = turned
        edges = (pl.ds(0, MARGIN), pl.ds(MARGIN + chunks * TILE, MARGIN))
        for edge in edges:
            for ref in (query, key, value):
                ref[edge, :] = jnp.zeros((MARGIN, width), LOW)
            for ref in (key_turned, value_turned):
                ref[:, edge] = jnp.zeros((width, MARGIN), LOW)
        for number in range(chunks * TILE // SUB + 2):
            row = jnp.broadcast_to(ids[number : number + 1, :], (SUB, SUB))
            columns[number * SUB : (number + 1) * SUB, :] = row.T

    @pl.when(step < chunks)
    def project():
        normed, _ = norm_parts(tokens[...].astype(F32))
        normed_turned[...] = normed.astype(LOW).T
        first_in = (normed * vectors[0:1, :] + vectors[1:2, :]).astype(LOW)
        result = dot(first_in, weight[...])
        turned = dot(pair_weight[...], first_in, NT)
        here = pl.ds(pl.multiple_of(MARGIN + step * TILE, SUB), TILE)
        scale = (width // HEADS) ** (-0.5)
        made = (result[:, :width] + vectors[2:3, :]).astype(LOW) * jnp.asarray(scale, LOW)
        query[here, :] = made
        key[here, :] = result[:, width : 2 * width].astype(LOW)
        value[here, :] = (result[:, 2 * width :] + vectors[3:4, :]).astype(LOW)
        key_turned[:, here] = turned[:width].astype(LOW)
        value_turned[:, here] = (turned[width:] + shifts[:, 3:4]).astype(LOW)

    @pl.when(step > 0)
    def attend():
        def place(number):
            sub, pair = number // PAIRS, number % PAIRS
            tile = (step - 1) * (TILE // SUB) + sub
            start = pl.multiple_of(tile * SUB, SUB)
            return sub, pair, tile, start, pl.ds(start, SPAN), pl.ds(pair * SUB, SUB)

        def score(number):
            _, _, _, start, near_rows, heads = place(number)
            wanted = both_heads(query[pl.ds(start + MARGIN, SUB), heads])
            return dot(key[near_rows, heads], wanted, NT)

        def soften(number, scores):
            sub, pair, tile, _, near_rows, _ = place(number)
            row = ids[pl.ds(tile + 1, 1), :]
            both = []
            for head in range(2):
                same = columns[near_rows, :] == row
                own = jnp.where(same, scores[:, head * SUB : (head + 1) * SUB], -1e30)
                expo = jnp.exp(own - jnp.max(own, axis=0, keepdims=True))
                share = 1.0 / jnp.sum(expo, axis=0, keepdims=True)
                both.append((expo * share).astype(LOW))
            prob = jnp.concatenate(both, axis=1)
            probs[pair, sub] = prob
            return prob

        def mix(number, prob):
            sub, _, _, _, near_rows, heads = place(number)
            first, second = halves_of(dot(value_turned[heads, near_rows], prob))
            turned = jnp.concatenate([first, second], axis=0).astype(LOW)
            mixed[pl.ds(sub * SUB, SUB), heads] = turned.T

        staged(TILE // SUB * PAIRS, score, soften, mix)


def attend_forward(numbers, pieces, tokens, ids):
    rows, width = tokens.shape
    chunks = rows // TILE
    tiles = TILE // SUB
    parts = len(pieces)
    now = lambda s: jnp.minimum(s, chunks - 1)
    before = lambda s: jnp.maximum(s - 1, 0)
    whole = lambda *dims: pl.BlockSpec(dims, lambda s, *_: (0,) * len(dims))
    padded = rows + 2 * MARGIN
    return pl.pallas_call(
        attend_kernel,
        grid_spec=pltpu.PrefetchScalarGridSpec(
            num_scalar_prefetch=1,
            grid=(chunks + 1,),
            in_specs=[pl.BlockSpec(memory_space=pl.ANY)] * parts
            + [
                pl.BlockSpec((TILE, width), lambda s, *_: (now(s), 0)),
                whole(*ids.shape),
            ],
            out_specs=[
                whole(padded, width),
                whole(padded, width),
                whole(padded, width),
                whole(width, padded),
                pl.BlockSpec((width, TILE), lambda s, *_: (0, now(s))),
                pl.BlockSpec((TILE, width), lambda s, *_: (before(s), 0)),
                pl.BlockSpec((PAIRS, tiles, SPAN, 2 * SUB), lambda s, *_: (0, before(s), 0, 0)),
                whole(width, 3 * width),
                whole(VEC_LANES, width),
            ],
            scratch_shapes=[
                pltpu.VMEM((parts, *pieces[0].shape), LOW),
                pltpu.VMEM((2 * width, width), LOW),
                pltpu.VMEM((width, padded), LOW),
                pltpu.VMEM((padded, SUB), F32),
                pltpu.VMEM((width, SUB), F32),
                pltpu.SemaphoreType.DMA((parts,)),
            ],
        ),
        out_shape=[
            jax.ShapeDtypeStruct((padded, width), LOW),
            jax.ShapeDtypeStruct((padded, width), LOW),
            jax.ShapeDtypeStruct((padded, width), LOW),
            jax.ShapeDtypeStruct((width, padded), LOW),
            jax.ShapeDtypeStruct((width, rows), LOW),
            jax.ShapeDtypeStruct((rows, width), LOW),
            jax.ShapeDtypeStruct((PAIRS, rows // SUB, SPAN, 2 * SUB), LOW),
            jax.ShapeDtypeStruct((width, 3 * width), LOW),
            jax.ShapeDtypeStruct((VEC_LANES, width), F32),
        ],
        compiler_params=pltpu.CompilerParams(vmem_limit_bytes=VMEM_LIMIT),
        cost_estimate=pl.CostEstimate(
            flops=12_000_000_000, bytes_accessed=22_000_000, transcendentals=5_000_000
        ),
        name="attend_forward",
    )(numbers, *pieces, tokens, ids)


def mlp_kernel(numbers, near, far, *refs):
    (vectors, mixed, tokens, cotangent, output, grad_residual, grad_mixed, inner, grads_near,
     grads_far, sums, one, two, proj_parts, proj, acc_one, acc_two, acc_proj, bias
    ) = refs
    step = pl.program_id(0)
    width = tokens.shape[1]
    mid = near.shape[1]
    parts = mid + far.shape[1]
    block = width // parts
    last_at = 2 * width
    hidden_width = one.shape[1]

    @pl.when(step == 0)
    def assemble():
        for part in range(parts):
            ref, at = (near, part) if part < mid else (far, part - mid)
            lanes = pl.ds(part * width, width)
            for group in range(near.shape[0]):
                here = pl.ds(group * near.shape[2], near.shape[2])
                one[here, lanes] = ref[group, at, :, :width]
                two[here, lanes] = ref[group, at, :, width:last_at]
                proj_parts[part, here, :] = ref[group, at, :, last_at:]
        total = jnp.zeros((width, width), F32)
        for number in range(parts):
            piece = proj_parts[numbers[PLACES + number]].astype(F32)
            kept = jnp.where(lane_numbers(piece.shape) < block, piece, 0.0)
            wide = jnp.concatenate([kept, jnp.zeros((width, width - SUB), F32)], axis=1)
            total = total + (pltpu.roll(wide, block * number, 1) if number else wide)
        proj[...] = total.astype(LOW)
        for part in range(parts):
            row = vectors[pl.ds(8 + numbers[OWNERS + part], 1), :]
            bias[0:1, part * width : (part + 1) * width] = row
        acc_one[...] = jnp.zeros(acc_one.shape, F32)
        acc_two[...] = jnp.zeros(acc_two.shape, F32)
        acc_proj[...] = jnp.zeros(acc_proj.shape, F32)
        sums[...] = jnp.zeros(sums.shape, F32)

    def add_row(row, values):
        sums[pl.ds(row, 1), :] += jnp.sum(values, axis=0, keepdims=True)

    own = mixed[...]
    residual = tokens[...].astype(F32) + dot(own, proj[...], NT) + vectors[4:5, :]
    normed, rate = norm_parts(residual)
    gain = vectors[5:6, :]
    second_in = (normed * gain + vectors[6:7, :]).astype(LOW)
    out_low = cotangent[...]
    grad_out = out_low.astype(F32)
    second_turned = second_in.T
    out_turned = out_low.T
    totals = [residual + vectors[7:8, :], jnp.zeros(residual.shape, F32)]

    count = hidden_width // FF_CHUNK
    ones = jnp.ones((16, MLP_TILE), LOW)
    second_and_ones = jnp.concatenate([second_turned, ones], axis=0)
    hiddens, slopes, kept = {}, {}, {}

    def lanes_of(number):
        return pl.ds(number * FF_CHUNK, FF_CHUNK)

    def make_hidden(number):
        hiddens[number] = dot(second_in, one[:, lanes_of(number)])

    def make_slope(number):
        slopes[number] = dot(out_low, two[:, lanes_of(number)])

    def add_one(number):
        acc_one[:, lanes_of(number)] += dot(second_and_ones, kept[number][1])

    def add_two(number):
        acc_two[:, lanes_of(number)] += dot(out_turned, kept[number][0])

    def add_result(number):
        totals[0] = totals[0] + dot(kept[number][0], two[:, lanes_of(number)], NT)

    def add_second(number):
        totals[1] = totals[1] + dot(kept[number][1], one[:, lanes_of(number)], NT)

    make_hidden(0)
    make_slope(0)
    for number in range(count):
        between = []
        if number + 1 < count:
            between += [functools.partial(f, number + 1) for f in (make_hidden, make_slope)]
        if number > 0:
            between += [
                functools.partial(f, number - 1)
                for f in (add_result, add_second, add_one, add_two)
            ]
        kept[number] = gelu_rows(
            hiddens.pop(number), bias[0:1, lanes_of(number)], slopes.pop(number), between
        )
    for f in (add_result, add_second, add_one, add_two):
        f(count - 1)
    result, grad_second = totals
    output[...] = result.astype(LOW)
    add_row(5, grad_second * normed)
    add_row(6, grad_second)
    add_row(7, grad_out)
    grad_res = grad_out + norm_back(grad_second, normed, rate, gain)
    grad_residual[...] = grad_res
    branch = grad_res.astype(LOW)
    add_row(4, branch.astype(F32))
    acc_proj[...] += dot(branch.T, own)
    grad_own = dot(branch, proj[...]).astype(LOW)
    grad_mixed[...] = grad_own
    high, rest = halves(grad_own.astype(F32) * own.astype(F32))
    head = lax.broadcasted_iota(jnp.int32, (16, width), 0)
    chosen = (lane_numbers((16, width)) // (width // HEADS) == head).astype(F32).astype(LOW)
    inner[...] = (dot(chosen, high, NT) + dot(chosen, rest, NT))[:8]

    @pl.when(step == pl.num_programs(0) - 1)
    def finish():
        total = acc_proj[...]
        for number in range(parts):
            turned = pltpu.roll(total, (width - block * number) % width, 1) if number else total
            proj_parts[numbers[PLACES + number]] = turned[:, :SUB].astype(LOW)
        for part in range(parts):
            ref, at = (grads_near, part) if part < mid else (grads_far, part - mid)
            lanes = pl.ds(part * width, width)
            for group in range(ref.shape[0]):
                here = pl.ds(group * ref.shape[2], ref.shape[2])
                ref[group, at, :, :width] = acc_one[here, lanes].astype(LOW)
                ref[group, at, :, width:last_at] = acc_two[here, lanes].astype(LOW)
                ref[group, at, :, last_at:] = proj_parts[part, here, :]
            sums[pl.ds(8 + numbers[OWNERS + part], 1), :] = acc_one[width : width + 1, lanes]


def mlp_both(numbers, near, far, vectors, mixed, tokens, cotangent):
    rows, width = tokens.shape
    parts = near.shape[1] + far.shape[1]
    hidden_width = parts * width
    tile = pl.BlockSpec((MLP_TILE, width), lambda s, *_: (s, 0))
    whole = lambda *dims: pl.BlockSpec(dims, lambda s, *_: (0,) * len(dims))
    return pl.pallas_call(
        mlp_kernel,
        grid_spec=pltpu.PrefetchScalarGridSpec(
            num_scalar_prefetch=1,
            grid=(rows // MLP_TILE,),
            in_specs=[
                whole(*near.shape), whole(*far.shape), whole(*vectors.shape), tile, tile, tile
            ],
            out_specs=[
                tile,
                tile,
                tile,
                pl.BlockSpec((8, MLP_TILE), lambda s, *_: (0, s)),
                whole(*near.shape),
                whole(*far.shape),
                whole(*vectors.shape),
            ],
            scratch_shapes=[
                pltpu.VMEM((width, hidden_width), LOW),
                pltpu.VMEM((width, hidden_width), LOW),
                pltpu.VMEM((parts, width, SUB), LOW),
                pltpu.VMEM((width, width), LOW),
                pltpu.VMEM((width + 16, hidden_width), F32),
                pltpu.VMEM((width, hidden_width), F32),
                pltpu.VMEM((width, width), F32),
                pltpu.VMEM((8, hidden_width), F32),
            ],
        ),
        out_shape=[
            jax.ShapeDtypeStruct((rows, width), LOW),
            jax.ShapeDtypeStruct((rows, width), F32),
            jax.ShapeDtypeStruct((rows, width), LOW),
            jax.ShapeDtypeStruct((8, rows), F32),
            jax.ShapeDtypeStruct(near.shape, LOW),
            jax.ShapeDtypeStruct(far.shape, LOW),
            jax.ShapeDtypeStruct(vectors.shape, F32),
        ],
        compiler_params=pltpu.CompilerParams(vmem_limit_bytes=VMEM_LIMIT),
        cost_estimate=pl.CostEstimate(
            flops=34_000_000_000, bytes_accessed=20_000_000, transcendentals=6_000_000
        ),
        name="mlp_both",
    )(numbers, near, far, vectors, mixed, tokens, cotangent)


def attend_back_kernel(
    numbers,
    query,
    key_turned,
    value,
    probs,
    inner,
    grad_mixed,
    normed_turned,
    weight,
    vectors,
    sums,
    grad_qkv,
    near,
    far,
    grad_query,
    acc_key,
    acc_value,
    acc_sums,
    normed_sums,
    blocks,
    rows,
):
    step = pl.program_id(0)
    chunks = pl.num_programs(0) - 1
    pairs = range(PAIRS)
    count = len(pairs)
    scale = (SUB // 2) ** (-0.5)

    @pl.when(step == 0)
    def clear():
        acc_key[...] = jnp.zeros(acc_key.shape, F32)
        acc_value[...] = jnp.zeros(acc_value.shape, F32)
        normed_sums[...] = jnp.zeros(normed_sums.shape, F32)
        acc_sums[...] = jnp.zeros(acc_sums.shape, F32)

    @pl.when(step < chunks)
    def attend():
        def place(number):
            sub, at = number // count, number % count
            start = pl.multiple_of((step * (TILE // SUB) + sub) * SUB, SUB)
            return sub, at, start, pl.ds(start, SPAN), pl.ds(at * SUB, SUB)

        def slope(number):
            sub, _, _, near_rows, heads = place(number)
            grad = both_heads(grad_mixed[pl.ds(sub * SUB, SUB), heads])
            return dot(value[near_rows, heads], grad, NT)

        def soften(number, slopes):
            sub, at, _, _, _ = place(number)
            pair = pairs[at]
            cols = pl.ds(sub * SUB, SUB)
            both = []
            for head in range(2):
                lanes = slice(head * SUB, (head + 1) * SUB)
                less = slopes[:, lanes] - inner[2 * pair + head : 2 * pair + head + 1, cols]
                both.append((probs[at, sub, :, lanes].astype(F32) * less).astype(LOW))
            return jnp.concatenate(both, axis=1)

        def collect(number, scores):
            sub, at, start, near_rows, heads = place(number)
            first, second = halves_of(dot(key_turned[heads, near_rows], scores))
            turned = (jnp.concatenate([first, second], axis=0) * scale).astype(LOW)
            grad_query[pl.ds(start, SUB), heads] = turned.T
            wanted = both_heads(query[pl.ds(start + MARGIN, SUB), heads])
            acc_key[near_rows, heads] += dot(scores, wanted)
            grad = both_heads(grad_mixed[pl.ds(sub * SUB, SUB), heads])
            acc_value[near_rows, heads] += dot(probs[at, sub], grad)

        staged(TILE // SUB * count, slope, soften, collect)

    @pl.when(step > 0)
    def collect():
        here = pl.ds(pl.multiple_of((step - 1) * TILE, SUB), TILE)
        there = pl.ds(pl.multiple_of((step - 1) * TILE + MARGIN, SUB), TILE)
        parts = (
            grad_query[here, :],
            acc_key[there, :].astype(LOW),
            acc_value[there, :].astype(LOW),
        )
        joined = jnp.concatenate(parts, axis=1)
        grad_qkv[...] = joined
        normed_sums[...] += dot(normed_turned[...], joined)
        acc_sums[0:1, :] += jnp.sum(joined.astype(F32), axis=0, keepdims=True)

    @pl.when(step == chunks)
    def finish():
        weight_grad(
            numbers, normed_sums[...], acc_sums[0:1, :], weight, vectors, sums, near, far, blocks, rows
        )


def weight_grad(numbers, total, columns, weight, vectors, sums, near, far, blocks, rows):
    width = weight.shape[0]
    parts, mid = blocks.shape[0], near.shape[0]
    block = 3 * width // parts
    rows_each = 12 // parts
    wide = weight[...].astype(F32)
    grad_gain = jnp.sum(total * wide, axis=1, keepdims=True)
    grad_shift = jnp.sum(wide * columns, axis=1, keepdims=True)
    rows[...] = jnp.zeros(rows.shape, F32)
    rows[0:VEC_LANES, :] = sums[...]
    rows[2:3, :] = columns[:, :width]
    rows[3:4, :] = columns[:, 2 * width :]
    rows[VEC_LANES : 2 * VEC_LANES, :] = vectors[...]
    turned = rows[...].T
    gain = turned[:, VEC_LANES : VEC_LANES + 1]
    shift = turned[:, VEC_LANES + 1 : VEC_LANES + 2]
    lane = lane_numbers(turned.shape)
    turned = jnp.where(lane == 0, grad_gain, jnp.where(lane == 1, grad_shift, turned))
    total = total * gain + shift * columns
    at = block - 2 * SUB
    for number in range(parts):
        away = (3 * width - block * number) % (3 * width)
        piece = (pltpu.roll(total, away, 1) if number else total)[:, :width]
        vec = pltpu.roll(turned, (at - rows_each * number) % SUB, 1)
        last = jnp.where(lane < at, piece[:, 2 * SUB :], 0.0)
        last = jnp.where((lane >= at) & (lane < at + rows_each), vec, last)
        at_place = numbers[PLACES + number]
        blocks[at_place, :, : 2 * SUB] = piece[:, : 2 * SUB].astype(LOW)
        blocks[at_place, :, 2 * SUB :] = last.astype(LOW)
    near[...] = blocks[:mid]
    far[...] = blocks[mid:]


def attend_backward(
    numbers, parts, query, key_turned, value, probs, inner, grad_mixed, normed_turned, weight,
    vectors, sums,
):
    width, rows = normed_turned.shape
    padded = query.shape[0]
    chunks = rows // TILE
    tiles = TILE // SUB
    now = lambda s: jnp.minimum(s, chunks - 1)
    before = lambda s: jnp.maximum(s - 1, 0)
    whole = lambda *dims: pl.BlockSpec(dims, lambda s, *_: (0,) * len(dims))
    half = (parts // 2, width, width)
    return pl.pallas_call(
        attend_back_kernel,
        grid_spec=pltpu.PrefetchScalarGridSpec(
            num_scalar_prefetch=1,
            grid=(chunks + 1,),
            in_specs=[
                whole(padded, width),
                whole(width, padded),
                whole(padded, width),
                pl.BlockSpec((PAIRS, tiles, SPAN, 2 * SUB), lambda s, *_: (0, now(s), 0, 0)),
                pl.BlockSpec((8, TILE), lambda s, *_: (0, now(s))),
                pl.BlockSpec((TILE, width), lambda s, *_: (now(s), 0)),
                pl.BlockSpec((width, TILE), lambda s, *_: (0, before(s))),
                whole(*weight.shape),
                whole(*vectors.shape),
                whole(*sums.shape),
            ],
            out_specs=[
                pl.BlockSpec((TILE, 3 * width), lambda s, *_: (before(s), 0)),
                whole(*half),
                whole(*half),
            ],
            scratch_shapes=[
                pltpu.VMEM((rows, width), LOW),
                pltpu.VMEM((padded, width), F32),
                pltpu.VMEM((padded, width), F32),
                pltpu.VMEM((8, 3 * width), F32),
                pltpu.VMEM((width, 3 * width), F32),
                pltpu.VMEM((parts, width, width), LOW),
                pltpu.VMEM((SUB, width), F32),
            ],
        ),
        out_shape=[
            jax.ShapeDtypeStruct((rows, 3 * width), LOW),
            jax.ShapeDtypeStruct(half, LOW),
            jax.ShapeDtypeStruct(half, LOW),
        ],
        compiler_params=pltpu.CompilerParams(vmem_limit_bytes=VMEM_LIMIT),
        cost_estimate=pl.CostEstimate(
            flops=16_000_000_000, bytes_accessed=24_000_000, transcendentals=0
        ),
        name="attend_backward",
    )(
        numbers, query, key_turned, value, probs, inner, grad_mixed, normed_turned, weight, vectors,
        sums,
    )


def input_grad_kernel(weight, vectors, tokens, grad_residual, grad_qkv, input_grad):
    normed, rate = norm_parts(tokens[...].astype(F32))
    grad_first = dot(grad_qkv[...], weight[...], NT)
    back = norm_back(grad_first, normed, rate, vectors[0:1, :])
    input_grad[...] = (grad_residual[...] + back).astype(LOW)


def input_gradient(weight, vectors, tokens, grad_residual, grad_qkv):
    rows, width = tokens.shape
    size = 2 * TILE
    tile = pl.BlockSpec((size, width), lambda s: (s, 0))
    whole = lambda ref: pl.BlockSpec(ref.shape, lambda s: (0, 0))
    return pl.pallas_call(
        input_grad_kernel,
        grid=(rows // size,),
        in_specs=[
            whole(weight), whole(vectors), tile, tile,
            pl.BlockSpec((size, 3 * width), lambda s: (s, 0)),
        ],
        out_specs=tile,
        out_shape=jax.ShapeDtypeStruct((rows, width), LOW),
        compiler_params=pltpu.CompilerParams(vmem_limit_bytes=VMEM_LIMIT),
        cost_estimate=pl.CostEstimate(
            flops=4_000_000_000, bytes_accessed=13_000_000, transcendentals=2048
        ),
        name="input_gradient",
    )(weight, vectors, tokens, grad_residual, grad_qkv)


def halves(value):
    high = value.astype(LOW)
    return high, (value - high.astype(F32)).astype(LOW)


def dot_three(left, right):
    tall = jnp.concatenate([right[0], right[0], right[1]], axis=0)
    return dot(jnp.concatenate([left[0], left[1], left[0]], axis=1), tall)


def newton_rows(blocks, offset, rows):
    gram = dot(blocks[0], blocks[0], NT)
    for part in blocks[1:]:
        gram = gram + dot(part, part, NT)
    depth = gram.shape[0]
    down = lax.broadcasted_iota(jnp.int32, (depth, depth), 0)
    eye = (down == lane_numbers((depth, depth))).astype(F32)
    norm = 1.0 / (jnp.sqrt(jnp.sum(gram * eye, keepdims=True)) + 1e-07)
    gram = gram * (norm * norm)
    place = lax.broadcasted_iota(jnp.int32, (rows, depth), 0) + offset
    left = jnp.where(place == lane_numbers((rows, depth)), norm, 0.0)
    for step in range(NS_STEPS - 1):
        pair = halves(gram)
        poly = halves(NEWTON_A * eye + NEWTON_B * gram + NEWTON_C * dot_three(pair, pair))
        lefts = halves(left)
        both = dot_three([jnp.concatenate([pair[n], lefts[n]], axis=0) for n in range(2)], poly)
        left = both[depth:]
        gram = dot_three(halves(both[:depth]), poly)
    pair = halves(gram)
    once = dot_three(halves(left), pair)
    return NEWTON_A * left + NEWTON_B * once + NEWTON_C * dot_three(halves(once), pair)


def stepped(left, own, height, old):
    high, rest = halves(left)
    ortho = (dot(high, own) + dot(rest, own))[: old.shape[0], : old.shape[1]]
    return old * (1.0 - MUON_RATE * MUON_DECAY) - (MUON_RATE * 0.2 * math.sqrt(height)) * ortho


def kept_lanes(value, low, high):
    lane = lane_numbers(value.shape)
    return jnp.where((lane >= low) & (lane < high), value.astype(F32), 0.0).astype(LOW)


def tall_of(rows):
    return -(-rows // 16) * 16


def muon_kernel(height, numbers, *refs):
    old, new, copy = refs[-3:]
    count = old.shape[1]
    blocks = [kept_lanes(ref[...], 0, count) for ref in refs[:-3]]
    left = newton_rows(blocks, numbers[OFFSET], tall_of(old.shape[0]))
    result = stepped(left, blocks[0], height, old[...])
    new[...] = result
    copy[...] = result.astype(LOW)


def muon(height, numbers, blocks, old):
    vmem = pl.BlockSpec(memory_space=pltpu.VMEM)

    def kernel(*refs):
        muon_kernel(height, *refs)

    return pl.pallas_call(
        kernel,
        in_specs=[pl.BlockSpec(memory_space=pltpu.SMEM)] + [vmem] * (len(blocks) + 1),
        out_specs=[vmem, vmem],
        out_shape=[
            jax.ShapeDtypeStruct(old.shape, F32),
            jax.ShapeDtypeStruct(old.shape, LOW),
        ],
        compiler_params=pltpu.CompilerParams(vmem_limit_bytes=VMEM_LIMIT),
        cost_estimate=pl.CostEstimate(
            flops=9_000_000_000, bytes_accessed=2_000_000, transcendentals=10
        ),
        name="muon",
    )(numbers, *blocks, old)


def pick_kernel(numbers, columns, *outs):
    for n, out in enumerate(outs):
        at = pl.multiple_of(numbers[STARTS + n] * SUB, SUB)
        out[...] = columns[:, pl.ds(at, out.shape[1])]


def pick(numbers, columns, count):
    depth = columns.shape[0]
    vmem = pl.BlockSpec(memory_space=pltpu.VMEM)
    return pl.pallas_call(
        pick_kernel,
        in_specs=[pl.BlockSpec(memory_space=pltpu.SMEM), vmem],
        out_specs=[vmem] * count,
        out_shape=[jax.ShapeDtypeStruct((depth, depth), LOW)] * count,
        name="pick",
    )(numbers, columns)


def newton_kernel(numbers, *refs):
    left = refs[-1]
    bounds = numbers[LOW_LANE], numbers[HIGH_LANE]
    blocks = [kept_lanes(ref[...], *bounds) for ref in refs[:-1]]
    left[...] = newton_rows(blocks, numbers[OFFSET], left.shape[0])


def newton(numbers, blocks, rows):
    vmem = pl.BlockSpec(memory_space=pltpu.VMEM)
    return pl.pallas_call(
        newton_kernel,
        in_specs=[pl.BlockSpec(memory_space=pltpu.SMEM)] + [vmem] * len(blocks),
        out_specs=vmem,
        out_shape=jax.ShapeDtypeStruct((tall_of(rows), blocks[0].shape[0]), F32),
        compiler_params=pltpu.CompilerParams(vmem_limit_bytes=VMEM_LIMIT),
        cost_estimate=pl.CostEstimate(
            flops=9_000_000_000, bytes_accessed=2_000_000, transcendentals=10
        ),
        name="newton",
    )(numbers, *blocks)


def finish_kernel(heights, lanes, numbers, columns, *refs):
    count = len(heights)
    store = refs[-1]
    news = refs[-1 - 2 * count : -1]
    olds = refs[-1 - 3 * count : -1 - 2 * count]
    lefts = refs[: -1 - 3 * count]
    for n, left in enumerate(lefts):
        store[n] = left[...]
    for n in range(count):
        wide = -(-olds[n].shape[1] // SUB) * SUB
        own = columns[:, lanes[n] : lanes[n] + wide]
        result = stepped(store[numbers[WHICH + n]], own, heights[n], olds[n][...])
        news[2 * n][...] = result
        news[2 * n + 1][...] = result.astype(LOW)


def finish(heights, lanes, numbers, columns, lefts, olds):
    vmem = pl.BlockSpec(memory_space=pltpu.VMEM)
    count = len(olds)

    def kernel(*refs):
        finish_kernel(heights, lanes, *refs)

    outs = pl.pallas_call(
        kernel,
        in_specs=[pl.BlockSpec(memory_space=pltpu.SMEM)] + [vmem] * (1 + len(lefts) + count),
        out_specs=[vmem] * (2 * count),
        out_shape=[
            jax.ShapeDtypeStruct(old.shape, kind) for old in olds for kind in (F32, LOW)
        ],
        scratch_shapes=[pltpu.VMEM((len(lefts), *lefts[0].shape), F32)],
        compiler_params=pltpu.CompilerParams(vmem_limit_bytes=VMEM_LIMIT),
        cost_estimate=pl.CostEstimate(
            flops=200_000_000, bytes_accessed=2_000_000, transcendentals=0
        ),
        name="finish",
    )(numbers, columns, *lefts, *olds)
    return [(outs[2 * n], outs[2 * n + 1]) for n in range(count)]


def exchange(x, axis, mask):
    size = lax.axis_size(axis)
    return lax.ppermute(x, axis, [(i, i ^ mask) for i in range(size)])


def place_masks(size):
    masks = [0]
    bit = size // 2
    while bit >= 1:
        masks = masks + [m ^ bit for m in masks]
        bit //= 2
    return masks


def from_columns(own):
    size = lax.axis_size("dp")
    sent = jnp.broadcast_to(own[None], (size, *own.shape))
    return lax.all_to_all(sent, "dp", split_axis=0, concat_axis=0, tiled=True)


def over_columns(own):
    return from_columns(own).reshape(-1, own.shape[1])


def device_numbers(dp, ns, share, width, proj_rows):
    masks = place_masks(ns)
    tasks = [(0, 0, width), (width // SUB, 0, width)]
    tasks += [(width // SUB + 1, 2 * SUB, 2 * SUB + proj_rows)] * (ns - 2)
    table = np.zeros((dp * ns, 24), np.int32)
    for device in range(dp * ns):
        column, index = device // ns, device % ns
        row = table[device]
        for n in range(ns):
            row[OWNERS + n] = index ^ masks[n]
            row[PLACES + (index ^ masks[n])] = n
            row[STARTS + n] = tasks[index ^ n][0]
        for n in range(3):
            row[WHICH + n] = index ^ n
        row[OFFSET] = column * share
        row[COLUMN] = column
        row[LOW_LANE], row[HIGH_LANE] = tasks[index][1:]
    return table


def over_rows(own):
    held = [own]
    bit = lax.axis_size("ns") // 2
    while bit >= 1:
        held = held + [exchange(block, "ns", bit) for block in held]
        bit //= 2
    return held


def added(keep, got):
    return (keep.astype(F32) + got.astype(F32)).astype(LOW)


def sum_columns(pieces):
    got = lax.all_to_all(pieces, "dp", split_axis=0, concat_axis=0, tiled=True)
    return jnp.sum(got.astype(F32), axis=0)


def split_kernel(numbers, keep, got, *outs):
    share = outs[0].shape[0]
    for mask, out in enumerate(outs):
        at = pl.ds(pl.multiple_of((numbers[COLUMN] ^ mask) * share, 16), share)
        out[...] = added(keep[at, :], got[at, :])


def split_sum(numbers, keep, got, devices):
    vmem = pl.BlockSpec(memory_space=pltpu.VMEM)
    shape = jax.ShapeDtypeStruct((keep.shape[0] // devices, keep.shape[1]), LOW)
    return pl.pallas_call(
        split_kernel,
        in_specs=[pl.BlockSpec(memory_space=pltpu.SMEM), vmem, vmem],
        out_specs=[vmem] * devices,
        out_shape=[shape] * devices,
        cost_estimate=pl.CostEstimate(
            flops=200_000, bytes_accessed=1_000_000, transcendentals=0
        ),
        name="split_sum",
    )(numbers, keep, got)


def sum_columns_direct(numbers, keep, got):
    devices = lax.axis_size("dp")
    if devices > 8 or keep.shape[0] // devices % 16:
        return sum_columns(added(keep, got).reshape(devices, -1, keep.shape[1]))
    pieces = split_sum(numbers, keep, got, devices)
    total = pieces[0].astype(F32)
    for mask in range(1, devices):
        total = total + exchange(pieces[mask], "dp", mask).astype(F32)
    return total


def widened(arrays, lanes):
    joined = jnp.concatenate(arrays, axis=1)
    return jnp.pad(joined, ((0, 0), (0, lanes - joined.shape[1])))


def per_device(
    tokens,
    cotangent,
    segment,
    valid_rows,
    qkv_weight,
    proj_weight,
    fc1_weight,
    fc2_weight,
    qkv_moment,
    proj_moment,
    fc1_moment,
    fc2_moment,
    vectors,
    vector_moment,
    vector_square,
):
    rows, width = tokens.shape
    ns = lax.axis_size("ns")
    qkv_w, proj_w, fc1_w, fc2_w = (w.T for w in (qkv_weight, proj_weight, fc1_weight, fc2_weight))
    qkv_m, proj_m, fc1_m, fc2_m = (w.T for w in (qkv_moment, proj_moment, fc1_moment, fc2_moment))
    share, count = qkv_w.shape
    vec_rows = vectors.shape[0]
    first_lanes = width
    later_lanes = 2 * width + SUB

    table = device_numbers(lax.axis_size("dp"), ns, share, width, proj_w.shape[1])
    device = lax.axis_index("dp") * ns + lax.axis_index("ns")
    numbers = lax.dynamic_slice(jnp.asarray(table), (device, 0), (1, table.shape[1]))[0]

    row_ids = jnp.where(
        valid_rows > 0, segment, rows + jnp.arange(rows, dtype=jnp.int32)
    ).astype(F32)
    ids = jnp.pad(row_ids, (MARGIN, MARGIN), constant_values=-1.0).reshape(-1, SUB)
    ids = jnp.pad(ids, ((0, -ids.shape[0] % 8), (0, 0)), constant_values=-1.0)

    later_own = widened([fc1_w, fc2_w, proj_w], later_lanes).astype(LOW)
    later_pair = jnp.stack([later_own, exchange(later_own, "ns", ns // 2)])
    first_own = widened([qkv_w, vectors.T], first_lanes).astype(LOW)
    first_pieces = over_rows(over_columns(first_own))
    later_near = from_columns(later_pair)
    if share % 16:
        later_near = jnp.moveaxis(later_near, 0, 1).reshape(1, ns // 2, width, later_lanes)

    (query, _, value, key_turned, normed_turned, mixed, probs, weight, vector_full) = (
        attend_forward(numbers, first_pieces, tokens, ids)
    )
    later_near, mixed = lax.optimization_barrier((later_near, mixed))
    later_far = exchange(later_near, "ns", 1)
    output, grad_residual, grad_mixed, inner, grads_near, grads_far, sums = mlp_both(
        numbers, later_near, later_far, vector_full, mixed, tokens, cotangent
    )
    held = added(grads_near, exchange(grads_far, "ns", 1))
    held, grad_mixed = lax.optimization_barrier((held, grad_mixed))
    if share % 16:
        held = jnp.moveaxis(held.reshape(ns // 2, -1, share, later_lanes), 1, 0)
    later_sums = sum_columns(held)
    later_owned = later_sums[0] + exchange(later_sums[1].astype(LOW), "ns", ns // 2).astype(F32)

    grad_qkv, grads_near, grads_far = attend_backward(
        numbers, ns, query, key_turned, value, probs, inner, grad_mixed, normed_turned, weight,
        vector_full, sums,
    )
    held = added(grads_near, exchange(grads_far, "ns", 1))
    got = exchange(held[1], "ns", ns // 2)
    input_grad = input_gradient(weight, vector_full, tokens, grad_residual, grad_qkv)
    got, input_grad = lax.optimization_barrier((got, input_grad))
    first_owned = sum_columns_direct(numbers, held[0], got)

    later_moment = later_owned + 0.5 * widened([fc1_m, fc2_m, proj_m], later_lanes)
    columns = over_columns(later_moment.astype(LOW))
    chosen = pick(numbers, columns, ns)
    blocks = [chosen[0]] + [exchange(chosen[mask], "ns", mask) for mask in range(1, ns)]
    left = newton(numbers, blocks, share)

    first_moment = first_owned + 0.5 * widened([qkv_m], first_lanes)
    first_own = over_columns(first_moment.astype(LOW))
    first_far = exchange(first_own, "ns", ns // 2)
    left, first_far = lax.optimization_barrier((left, first_far))
    first_pieces = [first_own, first_far]
    first_pieces += [exchange(piece, "ns", 1) for piece in first_pieces]
    qkv_new = muon(count * ns, numbers, first_pieces, qkv_w)

    lefts = [left] + [exchange(left, "ns", mask) for mask in range(1, ns)]
    fc1_new, fc2_new, proj_new = finish(
        [w.shape[1] * ns for w in (fc1_w, fc2_w, proj_w)],
        (0, width, 2 * width),
        numbers,
        columns,
        lefts,
        (fc1_w, fc2_w, proj_w),
    )

    news = (qkv_new, proj_new, fc1_new, fc2_new)
    moments_new = (
        first_moment[:, :count],
        later_moment[:, 2 * width : 2 * width + proj_w.shape[1]],
        later_moment[:, :width],
        later_moment[:, width : 2 * width],
    )

    vector_grad = first_owned[:, count : count + vec_rows].T
    first_new = BETA_ONE * vector_moment + (1.0 - BETA_ONE) * vector_grad
    second_new = BETA_TWO * vector_square + (1.0 - BETA_TWO) * vector_grad * vector_grad
    first_hat = first_new / (1.0 - BETA_ONE**STEP)
    second_hat = second_new / (1.0 - BETA_TWO**STEP)
    vectors_new = vectors - ADAM_RATE * first_hat / (jnp.sqrt(second_hat) + ADAM_EPS)
    return (
        output,
        input_grad,
        *(new[0].T for new in news),
        *(m.T for m in moments_new),
        first_new,
        second_new,
        vectors_new,
        *(new[1].T for new in news),
    )


def solution(mesh):
    rows = P(("dp", "ns"), None)
    flat = P(("dp", "ns"))
    block = P("ns", "dp")
    return jax.shard_map(
        per_device,
        mesh=mesh,
        in_specs=(rows, rows, flat, flat) + (block,) * 11,
        out_specs=(rows, rows) + (block,) * 15,
        check_vma=False,
    )
```

```python
import functools
import math

import jax
import jax.numpy as jnp
import numpy as np
from jax import lax
from jax.experimental import pallas as pl
from jax.experimental.pallas import tpu as pltpu
from jax.sharding import PartitionSpec as P

HEADS = 6
PAIRS = 3
MARGIN = 128
NS_STEPS = 5
STEP = 10
TILE = 256
MLP_TILE = 512
FF_CHUNK = 256
SUB = 128
SPAN = 384
VEC_LANES = 16


EPS_NORM = 1e-06
NEWTON_A = 3.4445
NEWTON_B = -4.775
NEWTON_C = 2.0315
MUON_RATE = 0.2
MUON_DECAY = 0.1
ADAM_RATE = 0.4
BETA_ONE = 0.9
BETA_TWO = 0.999
ADAM_EPS = 1e-08
LOW = jnp.bfloat16
F32 = jnp.float32
TN = (((0,), (0,)), ((), ()))
NT = (((1,), (1,)), ((), ()))
NN = (((1,), (0,)), ((), ()))
VMEM_LIMIT = 56 * 1024 * 1024
ERF_P = 0.3275911
ERF_COEFS = (0.254829592, -0.284496736, 1.421413741, -1.453152027, 1.061405429)


def dot(left, right, dims=NN):
    return lax.dot_general(left, right, dims, preferred_element_type=F32)


PLACES, OWNERS, STARTS, WHICH, OFFSET, LOW_LANE, HIGH_LANE, COLUMN = 0, 4, 8, 12, 16, 17, 18, 19


def lane_numbers(shape):
    return lax.broadcasted_iota(jnp.int32, shape, len(shape) - 1)


def norm_parts(value):
    center = value - jnp.mean(value, axis=-1, keepdims=True)
    rate = lax.rsqrt(jnp.mean(center * center, axis=-1, keepdims=True) + EPS_NORM)
    return center * rate, rate


def norm_back(grad, normed, rate, gain):
    scaled = grad * gain
    first = jnp.mean(scaled, axis=-1, keepdims=True)
    second = jnp.mean(scaled * normed, axis=-1, keepdims=True)
    return rate * (scaled - first - normed * second)


def gelu_both(value):
    below = 1.0 + (ERF_P * 0.5**0.5) * jnp.abs(value)
    ratio = pl.reciprocal(below, approx=True)
    ratio = ratio * (2.0 - below * ratio)
    decay = jnp.exp2((value * value) * (-0.5 * math.log2(math.e)))
    poly = 0.5 * ERF_COEFS[4]
    for coef in ERF_COEFS[3::-1]:
        poly = poly * ratio + 0.5 * coef
    tail = poly * ratio * decay
    phi = jnp.where(value >= 0, 1.0 - tail, tail)
    return value * phi, phi + (value * (1.0 / math.sqrt(2.0 * math.pi))) * decay


def gelu_rows(hidden, bias, grad, between):
    active, back = [], []
    rows = hidden.shape[0]
    pieces = rows // 16
    for n in range(pieces):
        if n * len(between) // pieces != (n - 1) * len(between) // pieces:
            between[n * len(between) // pieces]()
        here = slice(n * 16, (n + 1) * 16)
        value, slope = gelu_both(hidden[here] + bias)
        active.append(value.astype(LOW))
        back.append((grad[here] * slope).astype(LOW))
    return jnp.concatenate(active, axis=0), jnp.concatenate(back, axis=0)


def halves_of(lanes):
    half = lanes.shape[0] // 2
    return lanes[:half, :SUB], lanes[half:, SUB:]


def staged(count, first, second, third):
    made = [first(0)]
    kept = None
    for n in range(count):
        if n + 1 < count:
            made.append(first(n + 1))
        if kept is not None:
            third(n - 1, kept)
        kept = second(n, made[n])
        made[n] = None
    third(count - 1, kept)


def both_heads(pair):
    first = (lane_numbers((1, SUB)) < SUB // 2).astype(F32).astype(pair.dtype)
    second = (lane_numbers((1, SUB)) >= SUB // 2).astype(F32).astype(pair.dtype)
    return jnp.concatenate([pair * first, pair * second], axis=0)


def fetch(pairs, sems):
    copies = [
        pltpu.make_async_copy(source, target, sems.at[n])
        for n, (source, target) in enumerate(pairs)
    ]
    for copy in copies:
        copy.start()
    for copy in copies:
        copy.wait()


def attend_kernel(numbers, *refs):
    (tokens, ids, query, key, value, key_turned, normed_turned, mixed, probs, weight, vectors,
     gathered, pair_weight, value_turned, columns, shifts, sems) = refs[-17:]
    pieces = refs[:-17]
    step = pl.program_id(0)
    chunks = pl.num_programs(0) - 1
    width = tokens.shape[1]
    parts = len(pieces)
    block = 3 * width // parts
    rows_each = 12 // parts

    @pl.when(step == 0)
    def assemble():
        fetch([(piece, gathered.at[n]) for n, piece in enumerate(pieces)], sems)
        total = jnp.zeros((width, 3 * width), F32)
        turned = jnp.zeros((width, SUB), F32)
        for number in range(parts):
            piece = gathered[numbers[PLACES + number]].astype(F32)
            kept = jnp.where(lane_numbers(piece.shape) < block, piece, 0.0)
            wide = jnp.concatenate([kept, jnp.zeros((width, 2 * width), F32)], axis=1)
            total = total + (pltpu.roll(wide, block * number, 1) if number else wide)
            last = piece[:, 2 * SUB :]
            at = block - 2 * SUB
            lane = lane_numbers(last.shape)
            vec = jnp.where((lane >= at) & (lane < at + rows_each), last, 0.0)
            turned = turned + pltpu.roll(vec, (rows_each * number - at) % SUB, 1)
        total = total.astype(LOW)
        weight[...] = total
        pair_weight[...] = total[:, width:].T
        vectors[...] = turned.T[:VEC_LANES]
        shifts[...] = turned
        edges = (pl.ds(0, MARGIN), pl.ds(MARGIN + chunks * TILE, MARGIN))
        for edge in edges:
            for ref in (query, key, value):
                ref[edge, :] = jnp.zeros((MARGIN, width), LOW)
            for ref in (key_turned, value_turned):
                ref[:, edge] = jnp.zeros((width, MARGIN), LOW)
        for number in range(chunks * TILE // SUB + 2):
            row = jnp.broadcast_to(ids[number : number + 1, :], (SUB, SUB))
            columns[number * SUB : (number + 1) * SUB, :] = row.T

    @pl.when(step < chunks)
    def project():
        normed, _ = norm_parts(tokens[...].astype(F32))
        normed_turned[...] = normed.astype(LOW).T
        first_in = (normed * vectors[0:1, :] + vectors[1:2, :]).astype(LOW)
        result = dot(first_in, weight[...])
        turned = dot(pair_weight[...], first_in, NT)
        here = pl.ds(pl.multiple_of(MARGIN + step * TILE, SUB), TILE)
        scale = (width // HEADS) ** (-0.5)
        made = (result[:, :width] + vectors[2:3, :]).astype(LOW) * jnp.asarray(scale, LOW)
        query[here, :] = made
        key[here, :] = result[:, width : 2 * width].astype(LOW)
        value[here, :] = (result[:, 2 * width :] + vectors[3:4, :]).astype(LOW)
        key_turned[:, here] = turned[:width].astype(LOW)
        value_turned[:, here] = (turned[width:] + shifts[:, 3:4]).astype(LOW)

    @pl.when(step > 0)
    def attend():
        def place(number):
            sub, pair = number // PAIRS, number % PAIRS
            tile = (step - 1) * (TILE // SUB) + sub
            start = pl.multiple_of(tile * SUB, SUB)
            return sub, pair, tile, start, pl.ds(start, SPAN), pl.ds(pair * SUB, SUB)

        def score(number):
            _, _, _, start, near_rows, heads = place(number)
            wanted = both_heads(query[pl.ds(start + MARGIN, SUB), heads])
            return dot(key[near_rows, heads], wanted, NT)

        def soften(number, scores):
            sub, pair, tile, _, near_rows, _ = place(number)
            row = ids[pl.ds(tile + 1, 1), :]
            both = []
            for head in range(2):
                same = columns[near_rows, :] == row
                own = jnp.where(same, scores[:, head * SUB : (head + 1) * SUB], -1e30)
                expo = jnp.exp(own - jnp.max(own, axis=0, keepdims=True))
                share = 1.0 / jnp.sum(expo, axis=0, keepdims=True)
                both.append((expo * share).astype(LOW))
            prob = jnp.concatenate(both, axis=1)
            probs[pair, sub] = prob
            return prob

        def mix(number, prob):
            sub, _, _, _, near_rows, heads = place(number)
            first, second = halves_of(dot(value_turned[heads, near_rows], prob))
            turned = jnp.concatenate([first, second], axis=0).astype(LOW)
            mixed[pl.ds(sub * SUB, SUB), heads] = turned.T

        staged(TILE // SUB * PAIRS, score, soften, mix)


def attend_forward(numbers, pieces, tokens, ids):
    rows, width = tokens.shape
    chunks = rows // TILE
    tiles = TILE // SUB
    parts = len(pieces)
    now = lambda s: jnp.minimum(s, chunks - 1)
    before = lambda s: jnp.maximum(s - 1, 0)
    whole = lambda *dims: pl.BlockSpec(dims, lambda s, *_: (0,) * len(dims))
    padded = rows + 2 * MARGIN
    return pl.pallas_call(
        attend_kernel,
        grid_spec=pltpu.PrefetchScalarGridSpec(
            num_scalar_prefetch=1,
            grid=(chunks + 1,),
            in_specs=[pl.BlockSpec(memory_space=pl.ANY)] * parts
            + [
                pl.BlockSpec((TILE, width), lambda s, *_: (now(s), 0)),
                whole(*ids.shape),
            ],
            out_specs=[
                whole(padded, width),
                whole(padded, width),
                whole(padded, width),
                whole(width, padded),
                pl.BlockSpec((width, TILE), lambda s, *_: (0, now(s))),
                pl.BlockSpec((TILE, width), lambda s, *_: (before(s), 0)),
                pl.BlockSpec((PAIRS, tiles, SPAN, 2 * SUB), lambda s, *_: (0, before(s), 0, 0)),
                whole(width, 3 * width),
                whole(VEC_LANES, width),
            ],
            scratch_shapes=[
                pltpu.VMEM((parts, *pieces[0].shape), LOW),
                pltpu.VMEM((2 * width, width), LOW),
                pltpu.VMEM((width, padded), LOW),
                pltpu.VMEM((padded, SUB), F32),
                pltpu.VMEM((width, SUB), F32),
                pltpu.SemaphoreType.DMA((parts,)),
            ],
        ),
        out_shape=[
            jax.ShapeDtypeStruct((padded, width), LOW),
            jax.ShapeDtypeStruct((padded, width), LOW),
            jax.ShapeDtypeStruct((padded, width), LOW),
            jax.ShapeDtypeStruct((width, padded), LOW),
            jax.ShapeDtypeStruct((width, rows), LOW),
            jax.ShapeDtypeStruct((rows, width), LOW),
            jax.ShapeDtypeStruct((PAIRS, rows // SUB, SPAN, 2 * SUB), LOW),
            jax.ShapeDtypeStruct((width, 3 * width), LOW),
            jax.ShapeDtypeStruct((VEC_LANES, width), F32),
        ],
        compiler_params=pltpu.CompilerParams(vmem_limit_bytes=VMEM_LIMIT),
        cost_estimate=pl.CostEstimate(
            flops=12_000_000_000, bytes_accessed=22_000_000, transcendentals=5_000_000
        ),
        name="attend_forward",
    )(numbers, *pieces, tokens, ids)


def joined_rows(ref, at, lanes):
    return jnp.concatenate([ref[group, at, :, lanes] for group in range(ref.shape[0])], axis=0)


def fill_weights(pieces, bias_rows, vectors, one, two, bias):
    width = one.shape[0]
    for n, (ref, at) in enumerate(pieces):
        lanes = pl.ds(n * width, width)
        one[:, lanes] = joined_rows(ref, at, slice(0, width))
        two[:, lanes] = joined_rows(ref, at, slice(width, 2 * width))
        bias[0:1, lanes] = vectors[pl.ds(8 + bias_rows[n], 1), :]


def mlp_bodies(second_in, out_low, one, two, bias, acc_one, acc_two, active, grad_second):
    second_turned = jnp.concatenate(
        [second_in.T, jnp.ones((16, second_in.shape[0]), LOW)], axis=0
    )
    out_turned = out_low.T
    count = one.shape[1] // FF_CHUNK
    total = [grad_second]
    hiddens, slopes, kept = {}, {}, {}

    def lanes_of(number):
        return pl.ds(number * FF_CHUNK, FF_CHUNK)

    def make_hidden(number):
        hiddens[number] = dot(second_in, one[:, lanes_of(number)])

    def make_slope(number):
        slopes[number] = dot(out_low, two[:, lanes_of(number)])

    def add_one(number):
        acc_one[:, lanes_of(number)] += dot(second_turned, kept[number][1])

    def add_two(number):
        acc_two[:, lanes_of(number)] += dot(out_turned, kept[number][0])

    def add_second(number):
        total[0] = total[0] + dot(kept[number][1], one[:, lanes_of(number)], NT)

    make_hidden(0)
    make_slope(0)
    for number in range(count):
        between = []
        if number + 1 < count:
            between += [functools.partial(f, number + 1) for f in (make_hidden, make_slope)]
        if number > 0:
            between += [
                functools.partial(f, number - 1) for f in (add_second, add_one, add_two)
            ]
        kept[number] = gelu_rows(
            hiddens.pop(number), bias[0:1, lanes_of(number)], slopes.pop(number), between
        )
        active[:, lanes_of(number)] = kept[number][0]
    for f in (add_second, add_one, add_two):
        f(count - 1)
    return total[0]


def write_grads(acc_one, acc_two, refs):
    width = acc_two.shape[0]
    for n, ref in enumerate(refs):
        lanes = pl.ds(n * width, width)
        for group in range(ref.shape[0]):
            here = pl.ds(group * ref.shape[1], ref.shape[1])
            ref[group, :, :width] = acc_one[here, lanes].astype(LOW)
            ref[group, :, width:] = acc_two[here, lanes].astype(LOW)


def mlp_first_kernel(
    numbers, near, far, vectors, mixed, tokens, cotangent, residual, grad_second, active, keep,
    send, bias_sums, proj, one, two, acc_one, acc_two, bias, proj_parts,
):
    step = pl.program_id(0)
    width = tokens.shape[1]
    mid = near.shape[1]
    parts = mid + far.shape[1]
    block = width // parts

    @pl.when(step == 0)
    def assemble():
        owners = [numbers[OWNERS + n] for n in range(parts)]
        fill_weights(
            [(near, mid - 1), (far, mid - 1)], (owners[mid - 1], owners[-1]), vectors, one, two, bias
        )
        for part in range(parts):
            ref, at = (near, part) if part < mid else (far, part - mid)
            proj_parts[part] = joined_rows(ref, at, slice(2 * width, None))
        total = jnp.zeros((width, width), F32)
        for number in range(parts):
            piece = proj_parts[numbers[PLACES + number]].astype(F32)
            kept = jnp.where(lane_numbers(piece.shape) < block, piece, 0.0)
            wide = jnp.concatenate([kept, jnp.zeros((width, width - SUB), F32)], axis=1)
            total = total + (pltpu.roll(wide, block * number, 1) if number else wide)
        proj[...] = total.astype(LOW)
        acc_one[...] = jnp.zeros(acc_one.shape, F32)
        acc_two[...] = jnp.zeros(acc_two.shape, F32)

    value = tokens[...].astype(F32) + dot(mixed[...], proj[...], NT) + vectors[4:5, :]
    residual[...] = value
    normed, _ = norm_parts(value)
    second_in = (normed * vectors[5:6, :] + vectors[6:7, :]).astype(LOW)
    grad_second[...] = mlp_bodies(
        second_in, cotangent[...], one, two, bias, acc_one, acc_two, active,
        jnp.zeros(value.shape, F32),
    )

    @pl.when(step == pl.num_programs(0) - 1)
    def finish():
        write_grads(acc_one, acc_two, (keep, send))
        bias_sums[...] = acc_one[width : width + 8, :]


def mlp_second_kernel(
    numbers, near, far, vectors, mixed, residual, partial_second, cotangent, bias_sums, proj,
    grad_residual, grad_mixed, inner, active, keep, send, proj_keep, proj_send, sums, one, two,
    acc_one, acc_two, bias, acc_proj, proj_parts,
):
    step = pl.program_id(0)
    width = mixed.shape[1]
    mid = proj_keep.shape[1]
    parts = 2 * mid
    block = width // parts

    @pl.when(step == 0)
    def assemble():
        fill_weights(
            [(near, 0), (far, 0)], (numbers[OWNERS], numbers[OWNERS + mid]), vectors, one, two, bias
        )
        acc_one[...] = jnp.zeros(acc_one.shape, F32)
        acc_two[...] = jnp.zeros(acc_two.shape, F32)
        acc_proj[...] = jnp.zeros(acc_proj.shape, F32)
        sums[...] = jnp.zeros(sums.shape, F32)

    def add_row(row, values):
        sums[row : row + 1, :] += jnp.sum(values, axis=0, keepdims=True)

    own = mixed[...]
    normed, rate = norm_parts(residual[...])
    gain = vectors[5:6, :]
    second_in = (normed * gain + vectors[6:7, :]).astype(LOW)
    out_low = cotangent[...]
    grad_out = out_low.astype(F32)
    grad_second = mlp_bodies(
        second_in, out_low, one, two, bias, acc_one, acc_two, active, partial_second[...]
    )
    add_row(5, grad_second * normed)
    add_row(6, grad_second)
    add_row(7, grad_out)
    grad_res = grad_out + norm_back(grad_second, normed, rate, gain)
    grad_residual[...] = grad_res
    branch = grad_res.astype(LOW)
    add_row(4, branch.astype(F32))
    acc_proj[...] += dot(branch.T, own)
    grad_own = dot(branch, proj[...]).astype(LOW)
    grad_mixed[...] = grad_own
    high, rest = halves(grad_own.astype(F32) * own.astype(F32))
    head = lax.broadcasted_iota(jnp.int32, (16, width), 0)
    chosen = (lane_numbers((16, width)) // (width // HEADS) == head).astype(F32).astype(LOW)
    inner[...] = (dot(chosen, high, NT) + dot(chosen, rest, NT))[:8]

    @pl.when(step == pl.num_programs(0) - 1)
    def finish():
        write_grads(acc_one, acc_two, (keep, send))
        total = acc_proj[...]
        for number in range(parts):
            turned = pltpu.roll(total, (width - block * number) % width, 1) if number else total
            proj_parts[numbers[PLACES + number]] = turned[:, :SUB].astype(LOW)
        for part in range(parts):
            ref, at = (proj_keep, part) if part < mid else (proj_send, part - mid)
            for group in range(ref.shape[0]):
                ref[group, at] = proj_parts[part, pl.ds(group * ref.shape[2], ref.shape[2]), :]
        for n, part in enumerate((0, mid)):
            lanes = slice(n * width, (n + 1) * width)
            row = acc_one[width : width + 1, lanes]
            sums[pl.ds(8 + numbers[OWNERS + part], 1), :] = row
            last = numbers[OWNERS + part + mid - 1]
            sums[pl.ds(8 + last, 1), :] = bias_sums[0:1, lanes]


MLP_COST = pl.CostEstimate(
    flops=16_000_000_000, bytes_accessed=16_000_000, transcendentals=3_000_000
)


def mlp_first(numbers, near, far, vectors, mixed, tokens, cotangent):
    rows, width = tokens.shape
    groups, _, share, _ = near.shape
    hidden = 2 * width
    tile = pl.BlockSpec((MLP_TILE, width), lambda s, *_: (s, 0))
    whole = lambda *dims: pl.BlockSpec(dims, lambda s, *_: (0,) * len(dims))
    return pl.pallas_call(
        mlp_first_kernel,
        grid_spec=pltpu.PrefetchScalarGridSpec(
            num_scalar_prefetch=1,
            grid=(rows // MLP_TILE,),
            in_specs=[
                whole(*near.shape), whole(*far.shape), whole(*vectors.shape), tile, tile, tile
            ],
            out_specs=[
                tile,
                tile,
                pl.BlockSpec((MLP_TILE, hidden), lambda s, *_: (s, 0)),
                whole(groups, share, hidden),
                whole(groups, share, hidden),
                whole(8, hidden),
                whole(width, width),
            ],
            scratch_shapes=[
                pltpu.VMEM((width, hidden), LOW),
                pltpu.VMEM((width, hidden), LOW),
                pltpu.VMEM((width + 16, hidden), F32),
                pltpu.VMEM((width, hidden), F32),
                pltpu.VMEM((8, hidden), F32),
                pltpu.VMEM((near.shape[1] + far.shape[1], width, SUB), LOW),
            ],
        ),
        out_shape=[
            jax.ShapeDtypeStruct((rows, width), F32),
            jax.ShapeDtypeStruct((rows, width), F32),
            jax.ShapeDtypeStruct((rows, hidden), LOW),
            jax.ShapeDtypeStruct((groups, share, hidden), LOW),
            jax.ShapeDtypeStruct((groups, share, hidden), LOW),
            jax.ShapeDtypeStruct((8, hidden), F32),
            jax.ShapeDtypeStruct((width, width), LOW),
        ],
        compiler_params=pltpu.CompilerParams(vmem_limit_bytes=VMEM_LIMIT),
        cost_estimate=MLP_COST,
        name="mlp_first",
    )(numbers, near, far, vectors, mixed, tokens, cotangent)


def mlp_second(
    numbers, near, far, vectors, mixed, residual, partial_second, cotangent, bias_sums, proj
):
    rows, width = mixed.shape
    groups, mid, share, wide = near.shape
    hidden = 2 * width
    tile = pl.BlockSpec((MLP_TILE, width), lambda s, *_: (s, 0))
    whole = lambda *dims: pl.BlockSpec(dims, lambda s, *_: (0,) * len(dims))
    return pl.pallas_call(
        mlp_second_kernel,
        grid_spec=pltpu.PrefetchScalarGridSpec(
            num_scalar_prefetch=1,
            grid=(rows // MLP_TILE,),
            in_specs=[
                whole(groups, 1, share, wide), whole(groups, 1, share, wide),
                whole(*vectors.shape), tile, tile, tile, tile, whole(8, hidden),
                whole(width, width),
            ],
            out_specs=[
                tile,
                tile,
                pl.BlockSpec((8, MLP_TILE), lambda s, *_: (0, s)),
                pl.BlockSpec((MLP_TILE, hidden), lambda s, *_: (s, 0)),
                whole(groups, share, hidden),
                whole(groups, share, hidden),
                whole(groups, mid, share, SUB),
                whole(groups, mid, share, SUB),
                whole(*vectors.shape),
            ],
            scratch_shapes=[
                pltpu.VMEM((width, hidden), LOW),
                pltpu.VMEM((width, hidden), LOW),
                pltpu.VMEM((width + 16, hidden), F32),
                pltpu.VMEM((width, hidden), F32),
                pltpu.VMEM((8, hidden), F32),
                pltpu.VMEM((width, width), F32),
                pltpu.VMEM((2 * mid, width, SUB), LOW),
            ],
        ),
        out_shape=[
            jax.ShapeDtypeStruct((rows, width), F32),
            jax.ShapeDtypeStruct((rows, width), LOW),
            jax.ShapeDtypeStruct((8, rows), F32),
            jax.ShapeDtypeStruct((rows, hidden), LOW),
            jax.ShapeDtypeStruct((groups, share, hidden), LOW),
            jax.ShapeDtypeStruct((groups, share, hidden), LOW),
            jax.ShapeDtypeStruct((groups, mid, share, SUB), LOW),
            jax.ShapeDtypeStruct((groups, mid, share, SUB), LOW),
            jax.ShapeDtypeStruct(vectors.shape, F32),
        ],
        compiler_params=pltpu.CompilerParams(vmem_limit_bytes=VMEM_LIMIT),
        cost_estimate=MLP_COST,
        name="mlp_second",
    )(
        numbers, near, far, vectors, mixed, residual, partial_second, cotangent, bias_sums, proj
    )


def output_part(part, last, near, far, vectors, base, active):
    rows, width = base.shape
    groups, _, share, wide = near.shape
    piece = pl.BlockSpec((groups, 1, share, wide), lambda s: (0, part, 0, 0))
    tile = pl.BlockSpec((MLP_TILE, width), lambda s: (s, 0))

    def kernel(near, far, vectors, base, active, output, two):
        @pl.when(pl.program_id(0) == 0)
        def assemble():
            for n, ref in enumerate((near, far)):
                lanes = pl.ds(n * width, width)
                two[:, lanes] = joined_rows(ref, 0, slice(width, 2 * width))

        result = base[...] + dot(active[...], two[...], NT)
        if last:
            result = result + vectors[7:8, :]
        output[...] = result.astype(output.dtype)

    return pl.pallas_call(
        kernel,
        grid=(rows // MLP_TILE,),
        in_specs=[
            piece,
            piece,
            pl.BlockSpec(vectors.shape, lambda s: (0, 0)),
            tile,
            pl.BlockSpec((MLP_TILE, 2 * width), lambda s: (s, 0)),
        ],
        out_specs=tile,
        out_shape=jax.ShapeDtypeStruct((rows, width), LOW if last else F32),
        scratch_shapes=[pltpu.VMEM((width, 2 * width), LOW)],
        compiler_params=pltpu.CompilerParams(vmem_limit_bytes=VMEM_LIMIT),
        cost_estimate=pl.CostEstimate(
            flops=2_400_000_000, bytes_accessed=10_000_000, transcendentals=0
        ),
        name="output_part",
    )(near, far, vectors, base, active)


def attend_back_kernel(
    numbers,
    query,
    key_turned,
    value,
    probs,
    inner,
    grad_mixed,
    normed_turned,
    weight,
    vectors,
    sums,
    grad_qkv,
    near,
    far,
    grad_query,
    acc_key,
    acc_value,
    acc_sums,
    normed_sums,
    blocks,
    rows,
):
    step = pl.program_id(0)
    chunks = pl.num_programs(0) - 1
    pairs = range(PAIRS)
    count = len(pairs)
    scale = (SUB // 2) ** (-0.5)

    @pl.when(step == 0)
    def clear():
        acc_key[...] = jnp.zeros(acc_key.shape, F32)
        acc_value[...] = jnp.zeros(acc_value.shape, F32)
        normed_sums[...] = jnp.zeros(normed_sums.shape, F32)
        acc_sums[...] = jnp.zeros(acc_sums.shape, F32)

    @pl.when(step < chunks)
    def attend():
        def place(number):
            sub, at = number // count, number % count
            start = pl.multiple_of((step * (TILE // SUB) + sub) * SUB, SUB)
            return sub, at, start, pl.ds(start, SPAN), pl.ds(at * SUB, SUB)

        def slope(number):
            sub, _, _, near_rows, heads = place(number)
            grad = both_heads(grad_mixed[pl.ds(sub * SUB, SUB), heads])
            return dot(value[near_rows, heads], grad, NT)

        def soften(number, slopes):
            sub, at, _, _, _ = place(number)
            pair = pairs[at]
            cols = pl.ds(sub * SUB, SUB)
            both = []
            for head in range(2):
                lanes = slice(head * SUB, (head + 1) * SUB)
                less = slopes[:, lanes] - inner[2 * pair + head : 2 * pair + head + 1, cols]
                both.append((probs[at, sub, :, lanes].astype(F32) * less).astype(LOW))
            return jnp.concatenate(both, axis=1)

        def collect(number, scores):
            sub, at, start, near_rows, heads = place(number)
            first, second = halves_of(dot(key_turned[heads, near_rows], scores))
            turned = (jnp.concatenate([first, second], axis=0) * scale).astype(LOW)
            grad_query[pl.ds(start, SUB), heads] = turned.T
            wanted = both_heads(query[pl.ds(start + MARGIN, SUB), heads])
            acc_key[near_rows, heads] += dot(scores, wanted)
            grad = both_heads(grad_mixed[pl.ds(sub * SUB, SUB), heads])
            acc_value[near_rows, heads] += dot(probs[at, sub], grad)

        staged(TILE // SUB * count, slope, soften, collect)

    @pl.when(step > 0)
    def collect():
        here = pl.ds(pl.multiple_of((step - 1) * TILE, SUB), TILE)
        there = pl.ds(pl.multiple_of((step - 1) * TILE + MARGIN, SUB), TILE)
        parts = (
            grad_query[here, :],
            acc_key[there, :].astype(LOW),
            acc_value[there, :].astype(LOW),
        )
        joined = jnp.concatenate(parts, axis=1)
        grad_qkv[...] = joined
        normed_sums[...] += dot(normed_turned[...], joined)
        acc_sums[0:1, :] += jnp.sum(joined.astype(F32), axis=0, keepdims=True)

    @pl.when(step == chunks)
    def finish():
        weight_grad(
            numbers, normed_sums[...], acc_sums[0:1, :], weight, vectors, sums, near, far, blocks, rows
        )


def weight_grad(numbers, total, columns, weight, vectors, sums, near, far, blocks, rows):
    width = weight.shape[0]
    parts, mid = blocks.shape[0], near.shape[0]
    block = 3 * width // parts
    rows_each = 12 // parts
    wide = weight[...].astype(F32)
    grad_gain = jnp.sum(total * wide, axis=1, keepdims=True)
    grad_shift = jnp.sum(wide * columns, axis=1, keepdims=True)
    rows[...] = jnp.zeros(rows.shape, F32)
    rows[0:VEC_LANES, :] = sums[...]
    rows[2:3, :] = columns[:, :width]
    rows[3:4, :] = columns[:, 2 * width :]
    rows[VEC_LANES : 2 * VEC_LANES, :] = vectors[...]
    turned = rows[...].T
    gain = turned[:, VEC_LANES : VEC_LANES + 1]
    shift = turned[:, VEC_LANES + 1 : VEC_LANES + 2]
    lane = lane_numbers(turned.shape)
    turned = jnp.where(lane == 0, grad_gain, jnp.where(lane == 1, grad_shift, turned))
    total = total * gain + shift * columns
    at = block - 2 * SUB
    for number in range(parts):
        away = (3 * width - block * number) % (3 * width)
        piece = (pltpu.roll(total, away, 1) if number else total)[:, :width]
        vec = pltpu.roll(turned, (at - rows_each * number) % SUB, 1)
        last = jnp.where(lane < at, piece[:, 2 * SUB :], 0.0)
        last = jnp.where((lane >= at) & (lane < at + rows_each), vec, last)
        at_place = numbers[PLACES + number]
        blocks[at_place, :, : 2 * SUB] = piece[:, : 2 * SUB].astype(LOW)
        blocks[at_place, :, 2 * SUB :] = last.astype(LOW)
    near[...] = blocks[:mid]
    far[...] = blocks[mid:]


def attend_backward(
    numbers, parts, query, key_turned, value, probs, inner, grad_mixed, normed_turned, weight,
    vectors, sums,
):
    width, rows = normed_turned.shape
    padded = query.shape[0]
    chunks = rows // TILE
    tiles = TILE // SUB
    now = lambda s: jnp.minimum(s, chunks - 1)
    before = lambda s: jnp.maximum(s - 1, 0)
    whole = lambda *dims: pl.BlockSpec(dims, lambda s, *_: (0,) * len(dims))
    half = (parts // 2, width, width)
    return pl.pallas_call(
        attend_back_kernel,
        grid_spec=pltpu.PrefetchScalarGridSpec(
            num_scalar_prefetch=1,
            grid=(chunks + 1,),
            in_specs=[
                whole(padded, width),
                whole(width, padded),
                whole(padded, width),
                pl.BlockSpec((PAIRS, tiles, SPAN, 2 * SUB), lambda s, *_: (0, now(s), 0, 0)),
                pl.BlockSpec((8, TILE), lambda s, *_: (0, now(s))),
                pl.BlockSpec((TILE, width), lambda s, *_: (now(s), 0)),
                pl.BlockSpec((width, TILE), lambda s, *_: (0, before(s))),
                whole(*weight.shape),
                whole(*vectors.shape),
                whole(*sums.shape),
            ],
            out_specs=[
                pl.BlockSpec((TILE, 3 * width), lambda s, *_: (before(s), 0)),
                whole(*half),
                whole(*half),
            ],
            scratch_shapes=[
                pltpu.VMEM((rows, width), LOW),
                pltpu.VMEM((padded, width), F32),
                pltpu.VMEM((padded, width), F32),
                pltpu.VMEM((8, 3 * width), F32),
                pltpu.VMEM((width, 3 * width), F32),
                pltpu.VMEM((parts, width, width), LOW),
                pltpu.VMEM((SUB, width), F32),
            ],
        ),
        out_shape=[
            jax.ShapeDtypeStruct((rows, 3 * width), LOW),
            jax.ShapeDtypeStruct(half, LOW),
            jax.ShapeDtypeStruct(half, LOW),
        ],
        compiler_params=pltpu.CompilerParams(vmem_limit_bytes=VMEM_LIMIT),
        cost_estimate=pl.CostEstimate(
            flops=16_000_000_000, bytes_accessed=24_000_000, transcendentals=0
        ),
        name="attend_backward",
    )(
        numbers, query, key_turned, value, probs, inner, grad_mixed, normed_turned, weight, vectors,
        sums,
    )


def input_grad_kernel(weight, vectors, tokens, grad_residual, grad_qkv, input_grad):
    normed, rate = norm_parts(tokens[...].astype(F32))
    grad_first = dot(grad_qkv[...], weight[...], NT)
    back = norm_back(grad_first, normed, rate, vectors[0:1, :])
    input_grad[...] = (grad_residual[...] + back).astype(LOW)


def input_gradient(weight, vectors, tokens, grad_residual, grad_qkv):
    rows, width = tokens.shape
    size = 2 * TILE
    tile = pl.BlockSpec((size, width), lambda s: (s, 0))
    whole = lambda ref: pl.BlockSpec(ref.shape, lambda s: (0, 0))
    return pl.pallas_call(
        input_grad_kernel,
        grid=(rows // size,),
        in_specs=[
            whole(weight), whole(vectors), tile, tile,
            pl.BlockSpec((size, 3 * width), lambda s: (s, 0)),
        ],
        out_specs=tile,
        out_shape=jax.ShapeDtypeStruct((rows, width), LOW),
        compiler_params=pltpu.CompilerParams(vmem_limit_bytes=VMEM_LIMIT),
        cost_estimate=pl.CostEstimate(
            flops=4_000_000_000, bytes_accessed=13_000_000, transcendentals=2048
        ),
        name="input_gradient",
    )(weight, vectors, tokens, grad_residual, grad_qkv)


def halves(value):
    high = value.astype(LOW)
    return high, (value - high.astype(F32)).astype(LOW)


def dot_three(left, right):
    tall = jnp.concatenate([right[0], right[0], right[1]], axis=0)
    return dot(jnp.concatenate([left[0], left[1], left[0]], axis=1), tall)


def newton_rows(blocks, offset, rows):
    gram = dot(blocks[0], blocks[0], NT)
    for part in blocks[1:]:
        gram = gram + dot(part, part, NT)
    depth = gram.shape[0]
    down = lax.broadcasted_iota(jnp.int32, (depth, depth), 0)
    eye = (down == lane_numbers((depth, depth))).astype(F32)
    norm = 1.0 / (jnp.sqrt(jnp.sum(gram * eye, keepdims=True)) + 1e-07)
    gram = gram * (norm * norm)
    place = lax.broadcasted_iota(jnp.int32, (rows, depth), 0) + offset
    left = jnp.where(place == lane_numbers((rows, depth)), norm, 0.0)
    for step in range(NS_STEPS - 1):
        pair = halves(gram)
        poly = halves(NEWTON_A * eye + NEWTON_B * gram + NEWTON_C * dot_three(pair, pair))
        lefts = halves(left)
        both = dot_three([jnp.concatenate([pair[n], lefts[n]], axis=0) for n in range(2)], poly)
        left = both[depth:]
        gram = dot_three(halves(both[:depth]), poly)
    pair = halves(gram)
    once = dot_three(halves(left), pair)
    return NEWTON_A * left + NEWTON_B * once + NEWTON_C * dot_three(halves(once), pair)


def stepped(left, own, height, old):
    high, rest = halves(left)
    ortho = (dot(high, own) + dot(rest, own))[: old.shape[0], : old.shape[1]]
    return old * (1.0 - MUON_RATE * MUON_DECAY) - (MUON_RATE * 0.2 * math.sqrt(height)) * ortho


def kept_lanes(value, low, high):
    lane = lane_numbers(value.shape)
    return jnp.where((lane >= low) & (lane < high), value.astype(F32), 0.0).astype(LOW)


def tall_of(rows):
    return -(-rows // 16) * 16


def muon_kernel(height, numbers, *refs):
    old, new, copy = refs[-3:]
    count = old.shape[1]
    blocks = [kept_lanes(ref[...], 0, count) for ref in refs[:-3]]
    left = newton_rows(blocks, numbers[OFFSET], tall_of(old.shape[0]))
    result = stepped(left, blocks[0], height, old[...])
    new[...] = result
    copy[...] = result.astype(LOW)


def muon(height, numbers, blocks, old):
    vmem = pl.BlockSpec(memory_space=pltpu.VMEM)

    def kernel(*refs):
        muon_kernel(height, *refs)

    return pl.pallas_call(
        kernel,
        in_specs=[pl.BlockSpec(memory_space=pltpu.SMEM)] + [vmem] * (len(blocks) + 1),
        out_specs=[vmem, vmem],
        out_shape=[
            jax.ShapeDtypeStruct(old.shape, F32),
            jax.ShapeDtypeStruct(old.shape, LOW),
        ],
        compiler_params=pltpu.CompilerParams(vmem_limit_bytes=VMEM_LIMIT),
        cost_estimate=pl.CostEstimate(
            flops=9_000_000_000, bytes_accessed=2_000_000, transcendentals=10
        ),
        name="muon",
    )(numbers, *blocks, old)


def pick_kernel(numbers, columns, *outs):
    for n, out in enumerate(outs):
        at = pl.multiple_of(numbers[STARTS + n] * SUB, SUB)
        out[...] = columns[:, pl.ds(at, out.shape[1])]


def pick(numbers, columns, count):
    depth = columns.shape[0]
    vmem = pl.BlockSpec(memory_space=pltpu.VMEM)
    return pl.pallas_call(
        pick_kernel,
        in_specs=[pl.BlockSpec(memory_space=pltpu.SMEM), vmem],
        out_specs=[vmem] * count,
        out_shape=[jax.ShapeDtypeStruct((depth, depth), LOW)] * count,
        name="pick",
    )(numbers, columns)


def newton_kernel(numbers, *refs):
    left = refs[-1]
    bounds = numbers[LOW_LANE], numbers[HIGH_LANE]
    blocks = [kept_lanes(ref[...], *bounds) for ref in refs[:-1]]
    left[...] = newton_rows(blocks, numbers[OFFSET], left.shape[0])


def newton(numbers, blocks, rows):
    vmem = pl.BlockSpec(memory_space=pltpu.VMEM)
    return pl.pallas_call(
        newton_kernel,
        in_specs=[pl.BlockSpec(memory_space=pltpu.SMEM)] + [vmem] * len(blocks),
        out_specs=vmem,
        out_shape=jax.ShapeDtypeStruct((tall_of(rows), blocks[0].shape[0]), F32),
        compiler_params=pltpu.CompilerParams(vmem_limit_bytes=VMEM_LIMIT),
        cost_estimate=pl.CostEstimate(
            flops=9_000_000_000, bytes_accessed=2_000_000, transcendentals=10
        ),
        name="newton",
    )(numbers, *blocks)


def finish_kernel(heights, lanes, numbers, columns, *refs):
    count = len(heights)
    store = refs[-1]
    news = refs[-1 - 2 * count : -1]
    olds = refs[-1 - 3 * count : -1 - 2 * count]
    lefts = refs[: -1 - 3 * count]
    for n, left in enumerate(lefts):
        store[n] = left[...]
    for n in range(count):
        wide = -(-olds[n].shape[1] // SUB) * SUB
        own = columns[:, lanes[n] : lanes[n] + wide]
        result = stepped(store[numbers[WHICH + n]], own, heights[n], olds[n][...])
        news[2 * n][...] = result
        news[2 * n + 1][...] = result.astype(LOW)


def finish(heights, lanes, numbers, columns, lefts, olds):
    vmem = pl.BlockSpec(memory_space=pltpu.VMEM)
    count = len(olds)

    def kernel(*refs):
        finish_kernel(heights, lanes, *refs)

    outs = pl.pallas_call(
        kernel,
        in_specs=[pl.BlockSpec(memory_space=pltpu.SMEM)] + [vmem] * (1 + len(lefts) + count),
        out_specs=[vmem] * (2 * count),
        out_shape=[
            jax.ShapeDtypeStruct(old.shape, kind) for old in olds for kind in (F32, LOW)
        ],
        scratch_shapes=[pltpu.VMEM((len(lefts), *lefts[0].shape), F32)],
        compiler_params=pltpu.CompilerParams(vmem_limit_bytes=VMEM_LIMIT),
        cost_estimate=pl.CostEstimate(
            flops=200_000_000, bytes_accessed=2_000_000, transcendentals=0
        ),
        name="finish",
    )(numbers, columns, *lefts, *olds)
    return [(outs[2 * n], outs[2 * n + 1]) for n in range(count)]


def exchange(x, axis, mask):
    size = lax.axis_size(axis)
    return lax.ppermute(x, axis, [(i, i ^ mask) for i in range(size)])


def place_masks(size):
    masks = [0]
    bit = size // 2
    while bit >= 1:
        masks = masks + [m ^ bit for m in masks]
        bit //= 2
    return masks


def from_columns(own):
    size = lax.axis_size("dp")
    sent = jnp.broadcast_to(own[None], (size, *own.shape))
    return lax.all_to_all(sent, "dp", split_axis=0, concat_axis=0, tiled=True)


def over_columns(own):
    return from_columns(own).reshape(-1, own.shape[1])


def device_numbers(dp, ns, share, width, proj_rows):
    masks = place_masks(ns)
    tasks = [(0, 0, width), (width // SUB, 0, width)]
    tasks += [(width // SUB + 1, 2 * SUB, 2 * SUB + proj_rows)] * (ns - 2)
    table = np.zeros((dp * ns, 24), np.int32)
    for device in range(dp * ns):
        column, index = device // ns, device % ns
        row = table[device]
        for n in range(ns):
            row[OWNERS + n] = index ^ masks[n]
            row[PLACES + (index ^ masks[n])] = n
            row[STARTS + n] = tasks[index ^ n][0]
        for n in range(3):
            row[WHICH + n] = index ^ n
        row[OFFSET] = column * share
        row[COLUMN] = column
        row[LOW_LANE], row[HIGH_LANE] = tasks[index][1:]
    return table


def over_rows(own):
    held = [own]
    bit = lax.axis_size("ns") // 2
    while bit >= 1:
        held = held + [exchange(block, "ns", bit) for block in held]
        bit //= 2
    return held


def added(keep, got):
    return (keep.astype(F32) + got.astype(F32)).astype(LOW)


def sum_columns(pieces):
    got = lax.all_to_all(pieces, "dp", split_axis=0, concat_axis=0, tiled=True)
    return jnp.sum(got.astype(F32), axis=0)


def split_kernel(numbers, keep, got, *outs):
    share = outs[0].shape[0]
    for mask, out in enumerate(outs):
        at = pl.ds(pl.multiple_of((numbers[COLUMN] ^ mask) * share, 16), share)
        out[...] = added(keep[at, :], got[at, :])


def split_sum(numbers, keep, got, devices):
    vmem = pl.BlockSpec(memory_space=pltpu.VMEM)
    shape = jax.ShapeDtypeStruct((keep.shape[0] // devices, keep.shape[1]), LOW)
    return pl.pallas_call(
        split_kernel,
        in_specs=[pl.BlockSpec(memory_space=pltpu.SMEM), vmem, vmem],
        out_specs=[vmem] * devices,
        out_shape=[shape] * devices,
        cost_estimate=pl.CostEstimate(
            flops=200_000, bytes_accessed=1_000_000, transcendentals=0
        ),
        name="split_sum",
    )(numbers, keep, got)


def sum_columns_direct(numbers, keep, got):
    devices = lax.axis_size("dp")
    if devices > 8 or keep.shape[0] // devices % 16:
        return sum_columns(added(keep, got).reshape(devices, -1, keep.shape[1]))
    pieces = split_sum(numbers, keep, got, devices)
    total = pieces[0].astype(F32)
    for mask in range(1, devices):
        total = total + exchange(pieces[mask], "dp", mask).astype(F32)
    return total


def widened(arrays, lanes):
    joined = jnp.concatenate(arrays, axis=1)
    return jnp.pad(joined, ((0, 0), (0, lanes - joined.shape[1])))


def per_device(
    tokens,
    cotangent,
    segment,
    valid_rows,
    qkv_weight,
    proj_weight,
    fc1_weight,
    fc2_weight,
    qkv_moment,
    proj_moment,
    fc1_moment,
    fc2_moment,
    vectors,
    vector_moment,
    vector_square,
):
    rows, width = tokens.shape
    ns = lax.axis_size("ns")
    qkv_w, proj_w, fc1_w, fc2_w = (w.T for w in (qkv_weight, proj_weight, fc1_weight, fc2_weight))
    qkv_m, proj_m, fc1_m, fc2_m = (w.T for w in (qkv_moment, proj_moment, fc1_moment, fc2_moment))
    share, count = qkv_w.shape
    vec_rows = vectors.shape[0]
    first_lanes = width
    later_lanes = 2 * width + SUB

    table = device_numbers(lax.axis_size("dp"), ns, share, width, proj_w.shape[1])
    device = lax.axis_index("dp") * ns + lax.axis_index("ns")
    numbers = lax.dynamic_slice(jnp.asarray(table), (device, 0), (1, table.shape[1]))[0]

    row_ids = jnp.where(
        valid_rows > 0, segment, rows + jnp.arange(rows, dtype=jnp.int32)
    ).astype(F32)
    ids = jnp.pad(row_ids, (MARGIN, MARGIN), constant_values=-1.0).reshape(-1, SUB)
    ids = jnp.pad(ids, ((0, -ids.shape[0] % 8), (0, 0)), constant_values=-1.0)

    later_own = widened([fc1_w, fc2_w, proj_w], later_lanes).astype(LOW)
    later_pair = jnp.stack([later_own, exchange(later_own, "ns", ns // 2)])
    first_own = widened([qkv_w, vectors.T], first_lanes).astype(LOW)
    first_pieces = over_rows(over_columns(first_own))
    later_near = from_columns(later_pair)
    if share % 16:
        later_near = jnp.moveaxis(later_near, 0, 1).reshape(1, ns // 2, width, later_lanes)

    (query, _, value, key_turned, normed_turned, mixed, probs, weight, vector_full) = (
        attend_forward(numbers, first_pieces, tokens, ids)
    )
    later_near, mixed = lax.optimization_barrier((later_near, mixed))
    later_far = exchange(later_near, "ns", 1)
    residual, second_part, active, keep, send, bias_sums, proj = mlp_first(
        numbers, later_near, later_far, vector_full, mixed, tokens, cotangent
    )
    output = output_part(ns // 2 - 1, False, later_near, later_far, vector_full, residual, active)
    got, output = lax.optimization_barrier((exchange(send, "ns", 1), output))
    held, residual = lax.optimization_barrier((added(keep, got), residual))
    crossed = exchange(held, "ns", ns // 2)
    (grad_residual, grad_mixed, inner, active, keep, send, proj_keep, proj_send, sums) = mlp_second(
        numbers, later_near, later_far, vector_full, mixed, residual, second_part, cotangent,
        bias_sums, proj,
    )
    output = output_part(0, True, later_near, later_far, vector_full, output, active)
    got = exchange(send, "ns", 1)
    proj_held = added(proj_keep, exchange(proj_send, "ns", 1))
    proj_far = exchange(proj_held[:, 1], "ns", ns // 2)
    got, proj_far, output = lax.optimization_barrier((got, proj_far, output))
    held = keep.astype(F32) + got.astype(F32) + crossed.astype(F32)
    held = jnp.concatenate([held.astype(LOW), added(proj_held[:, 0], proj_far)], axis=2)
    held, grad_mixed = lax.optimization_barrier((held, grad_mixed))
    later_owned = sum_columns(held.reshape(lax.axis_size("dp"), share, later_lanes))

    grad_qkv, grads_near, grads_far = attend_backward(
        numbers, ns, query, key_turned, value, probs, inner, grad_mixed, normed_turned, weight,
        vector_full, sums,
    )
    held = added(grads_near, exchange(grads_far, "ns", 1))
    got = exchange(held[1], "ns", ns // 2)
    later_moment = later_owned + 0.5 * widened([fc1_m, fc2_m, proj_m], later_lanes)
    columns = over_columns(later_moment.astype(LOW))
    input_grad = input_gradient(weight, vector_full, tokens, grad_residual, grad_qkv)
    got, input_grad = lax.optimization_barrier((got, input_grad))
    first_owned = sum_columns_direct(numbers, held[0], got)

    chosen = pick(numbers, columns, ns)
    blocks = [chosen[0]] + [exchange(chosen[mask], "ns", mask) for mask in range(1, ns)]
    left = newton(numbers, blocks, share)

    first_moment = first_owned + 0.5 * widened([qkv_m], first_lanes)
    first_own = over_columns(first_moment.astype(LOW))
    first_far = exchange(first_own, "ns", ns // 2)
    left, first_far = lax.optimization_barrier((left, first_far))
    first_pieces = [first_own, first_far]
    first_pieces += [exchange(piece, "ns", 1) for piece in first_pieces]
    qkv_new = muon(count * ns, numbers, first_pieces, qkv_w)

    lefts = [left] + [exchange(left, "ns", mask) for mask in range(1, ns)]
    fc1_new, fc2_new, proj_new = finish(
        [w.shape[1] * ns for w in (fc1_w, fc2_w, proj_w)],
        (0, width, 2 * width),
        numbers,
        columns,
        lefts,
        (fc1_w, fc2_w, proj_w),
    )

    news = (qkv_new, proj_new, fc1_new, fc2_new)
    moments_new = (
        first_moment[:, :count],
        later_moment[:, 2 * width : 2 * width + proj_w.shape[1]],
        later_moment[:, :width],
        later_moment[:, width : 2 * width],
    )

    vector_grad = first_owned[:, count : count + vec_rows].T
    first_new = BETA_ONE * vector_moment + (1.0 - BETA_ONE) * vector_grad
    second_new = BETA_TWO * vector_square + (1.0 - BETA_TWO) * vector_grad * vector_grad
    first_hat = first_new / (1.0 - BETA_ONE**STEP)
    second_hat = second_new / (1.0 - BETA_TWO**STEP)
    vectors_new = vectors - ADAM_RATE * first_hat / (jnp.sqrt(second_hat) + ADAM_EPS)
    return (
        output,
        input_grad,
        *(new[0].T for new in news),
        *(m.T for m in moments_new),
        first_new,
        second_new,
        vectors_new,
        *(new[1].T for new in news),
    )


def solution(mesh):
    rows = P(("dp", "ns"), None)
    flat = P(("dp", "ns"))
    block = P("ns", "dp")
    return jax.shard_map(
        per_device,
        mesh=mesh,
        in_specs=(rows, rows, flat, flat) + (block,) * 11,
        out_specs=(rows, rows) + (block,) * 15,
        check_vma=False,
    )
```

```python
import functools
import math

import jax
import jax.numpy as jnp
import numpy as np
from jax import lax
from jax.experimental import pallas as pl
from jax.experimental.pallas import tpu as pltpu
from jax.sharding import PartitionSpec as P

HEADS = 6
PAIRS = 3
MARGIN = 128
NS_STEPS = 5
STEP = 10
TILE = 512
MLP_TILE = 1024
FF_CHUNK = 256
SUB = 128
SPAN = 384
VEC_LANES = 16


EPS_NORM = 1e-06
NEWTON_A = 3.4445
NEWTON_B = -4.775
NEWTON_C = 2.0315
MUON_RATE = 0.2
MUON_DECAY = 0.1
ADAM_RATE = 0.4
BETA_ONE = 0.9
BETA_TWO = 0.999
ADAM_EPS = 1e-08
LOW = jnp.bfloat16
F32 = jnp.float32
TN = (((0,), (0,)), ((), ()))
NT = (((1,), (1,)), ((), ()))
NN = (((1,), (0,)), ((), ()))
VMEM_LIMIT = 56 * 1024 * 1024
ERF_P = 0.3275911
ERF_COEFS = (0.254829592, -0.284496736, 1.421413741, -1.453152027, 1.061405429)


def dot(left, right, dims=NN):
    return lax.dot_general(left, right, dims, preferred_element_type=F32)


PLACES, OWNERS, STARTS, WHICH, OFFSET, LOW_LANE, HIGH_LANE, COLUMN = 0, 4, 8, 12, 16, 17, 18, 19


def lane_numbers(shape):
    return lax.broadcasted_iota(jnp.int32, shape, len(shape) - 1)


def norm_parts(value):
    center = value - jnp.mean(value, axis=-1, keepdims=True)
    rate = lax.rsqrt(jnp.mean(center * center, axis=-1, keepdims=True) + EPS_NORM)
    return center * rate, rate


def norm_back(grad, normed, rate, gain):
    scaled = grad * gain
    first = jnp.mean(scaled, axis=-1, keepdims=True)
    second = jnp.mean(scaled * normed, axis=-1, keepdims=True)
    return rate * (scaled - first - normed * second)


def gelu_both(value):
    below = 1.0 + (ERF_P * 0.5**0.5) * jnp.abs(value)
    ratio = pl.reciprocal(below, approx=True)
    ratio = ratio * (2.0 - below * ratio)
    decay = jnp.exp2((value * value) * (-0.5 * math.log2(math.e)))
    poly = 0.5 * ERF_COEFS[4]
    for coef in ERF_COEFS[3::-1]:
        poly = poly * ratio + 0.5 * coef
    tail = poly * ratio * decay
    phi = jnp.where(value >= 0, 1.0 - tail, tail)
    return value * phi, phi + (value * (1.0 / math.sqrt(2.0 * math.pi))) * decay


def gelu_rows(hidden, bias, grad, between):
    active, back = [], []
    rows = hidden.shape[0]
    pieces = rows // 16
    for n in range(pieces):
        if n * len(between) // pieces != (n - 1) * len(between) // pieces:
            between[n * len(between) // pieces]()
        here = slice(n * 16, (n + 1) * 16)
        value, slope = gelu_both(hidden[here] + bias)
        active.append(value.astype(LOW))
        back.append((grad[here] * slope).astype(LOW))
    return jnp.concatenate(active, axis=0), jnp.concatenate(back, axis=0)


def halves_of(lanes):
    half = lanes.shape[0] // 2
    return lanes[:half, :SUB], lanes[half:, SUB:]


def staged(count, first, second, third):
    made = [first(0)]
    kept = None
    for n in range(count):
        if n + 1 < count:
            made.append(first(n + 1))
        if kept is not None:
            third(n - 1, kept)
        kept = second(n, made[n])
        made[n] = None
    third(count - 1, kept)


def both_heads(pair):
    first = (lane_numbers((1, SUB)) < SUB // 2).astype(F32).astype(pair.dtype)
    second = (lane_numbers((1, SUB)) >= SUB // 2).astype(F32).astype(pair.dtype)
    return jnp.concatenate([pair * first, pair * second], axis=0)


def fetch(pairs, sems):
    copies = [
        pltpu.make_async_copy(source, target, sems.at[n])
        for n, (source, target) in enumerate(pairs)
    ]
    for copy in copies:
        copy.start()
    for copy in copies:
        copy.wait()


def attend_kernel(numbers, *refs):
    (tokens, ids, query, key, value, key_turned, normed_turned, mixed, probs, weight, vectors,
     gathered, pair_weight, value_turned, columns, shifts, sems) = refs[-17:]
    pieces = refs[:-17]
    step = pl.program_id(0)
    chunks = pl.num_programs(0) - 1
    width = tokens.shape[1]
    parts = len(pieces)
    block = 3 * width // parts
    rows_each = 12 // parts

    @pl.when(step == 0)
    def assemble():
        fetch([(piece, gathered.at[n]) for n, piece in enumerate(pieces)], sems)
        total = jnp.zeros((width, 3 * width), F32)
        turned = jnp.zeros((width, SUB), F32)
        for number in range(parts):
            piece = gathered[numbers[PLACES + number]].astype(F32)
            kept = jnp.where(lane_numbers(piece.shape) < block, piece, 0.0)
            wide = jnp.concatenate([kept, jnp.zeros((width, 2 * width), F32)], axis=1)
            total = total + (pltpu.roll(wide, block * number, 1) if number else wide)
            last = piece[:, 2 * SUB :]
            at = block - 2 * SUB
            lane = lane_numbers(last.shape)
            vec = jnp.where((lane >= at) & (lane < at + rows_each), last, 0.0)
            turned = turned + pltpu.roll(vec, (rows_each * number - at) % SUB, 1)
        total = total.astype(LOW)
        weight[...] = total
        pair_weight[...] = total[:, width:].T
        vectors[...] = turned.T[:VEC_LANES]
        shifts[...] = turned
        edges = (pl.ds(0, MARGIN), pl.ds(MARGIN + chunks * TILE, MARGIN))
        for edge in edges:
            for ref in (query, key, value):
                ref[edge, :] = jnp.zeros((MARGIN, width), LOW)
            for ref in (key_turned, value_turned):
                ref[:, edge] = jnp.zeros((width, MARGIN), LOW)
        for number in range(chunks * TILE // SUB + 2):
            row = jnp.broadcast_to(ids[number : number + 1, :], (SUB, SUB))
            columns[number * SUB : (number + 1) * SUB, :] = row.T

    @pl.when(step < chunks)
    def project():
        normed, _ = norm_parts(tokens[...].astype(F32))
        normed_turned[...] = normed.astype(LOW).T
        first_in = (normed * vectors[0:1, :] + vectors[1:2, :]).astype(LOW)
        result = dot(first_in, weight[...])
        turned = dot(pair_weight[...], first_in, NT)
        here = pl.ds(pl.multiple_of(MARGIN + step * TILE, SUB), TILE)
        scale = (width // HEADS) ** (-0.5)
        made = (result[:, :width] + vectors[2:3, :]).astype(LOW) * jnp.asarray(scale, LOW)
        query[here, :] = made
        key[here, :] = result[:, width : 2 * width].astype(LOW)
        value[here, :] = (result[:, 2 * width :] + vectors[3:4, :]).astype(LOW)
        key_turned[:, here] = turned[:width].astype(LOW)
        value_turned[:, here] = (turned[width:] + shifts[:, 3:4]).astype(LOW)

    @pl.when(step > 0)
    def attend():
        def place(number):
            sub, pair = number // PAIRS, number % PAIRS
            tile = (step - 1) * (TILE // SUB) + sub
            start = pl.multiple_of(tile * SUB, SUB)
            return sub, pair, tile, start, pl.ds(start, SPAN), pl.ds(pair * SUB, SUB)

        def score(number):
            _, _, _, start, near_rows, heads = place(number)
            wanted = both_heads(query[pl.ds(start + MARGIN, SUB), heads])
            return dot(key[near_rows, heads], wanted, NT)

        def soften(number, scores):
            sub, pair, tile, _, near_rows, _ = place(number)
            row = ids[pl.ds(tile + 1, 1), :]
            both = []
            for head in range(2):
                same = columns[near_rows, :] == row
                own = jnp.where(same, scores[:, head * SUB : (head + 1) * SUB], -1e30)
                expo = jnp.exp(own - jnp.max(own, axis=0, keepdims=True))
                share = 1.0 / jnp.sum(expo, axis=0, keepdims=True)
                both.append((expo * share).astype(LOW))
            prob = jnp.concatenate(both, axis=1)
            probs[pair, sub] = prob
            return prob

        def mix(number, prob):
            sub, _, _, _, near_rows, heads = place(number)
            first, second = halves_of(dot(value_turned[heads, near_rows], prob))
            turned = jnp.concatenate([first, second], axis=0).astype(LOW)
            mixed[pl.ds(sub * SUB, SUB), heads] = turned.T

        staged(TILE // SUB * PAIRS, score, soften, mix)


def attend_forward(numbers, pieces, tokens, ids):
    rows, width = tokens.shape
    chunks = rows // TILE
    tiles = TILE // SUB
    parts = len(pieces)
    now = lambda s: jnp.minimum(s, chunks - 1)
    before = lambda s: jnp.maximum(s - 1, 0)
    whole = lambda *dims: pl.BlockSpec(dims, lambda s, *_: (0,) * len(dims))
    padded = rows + 2 * MARGIN
    return pl.pallas_call(
        attend_kernel,
        grid_spec=pltpu.PrefetchScalarGridSpec(
            num_scalar_prefetch=1,
            grid=(chunks + 1,),
            in_specs=[pl.BlockSpec(memory_space=pl.ANY)] * parts
            + [
                pl.BlockSpec((TILE, width), lambda s, *_: (now(s), 0)),
                whole(*ids.shape),
            ],
            out_specs=[
                whole(padded, width),
                whole(padded, width),
                whole(padded, width),
                whole(width, padded),
                pl.BlockSpec((width, TILE), lambda s, *_: (0, now(s))),
                pl.BlockSpec((TILE, width), lambda s, *_: (before(s), 0)),
                pl.BlockSpec((PAIRS, tiles, SPAN, 2 * SUB), lambda s, *_: (0, before(s), 0, 0)),
                whole(width, 3 * width),
                whole(VEC_LANES, width),
            ],
            scratch_shapes=[
                pltpu.VMEM((parts, *pieces[0].shape), LOW),
                pltpu.VMEM((2 * width, width), LOW),
                pltpu.VMEM((width, padded), LOW),
                pltpu.VMEM((padded, SUB), F32),
                pltpu.VMEM((width, SUB), F32),
                pltpu.SemaphoreType.DMA((parts,)),
            ],
        ),
        out_shape=[
            jax.ShapeDtypeStruct((padded, width), LOW),
            jax.ShapeDtypeStruct((padded, width), LOW),
            jax.ShapeDtypeStruct((padded, width), LOW),
            jax.ShapeDtypeStruct((width, padded), LOW),
            jax.ShapeDtypeStruct((width, rows), LOW),
            jax.ShapeDtypeStruct((rows, width), LOW),
            jax.ShapeDtypeStruct((PAIRS, rows // SUB, SPAN, 2 * SUB), LOW),
            jax.ShapeDtypeStruct((width, 3 * width), LOW),
            jax.ShapeDtypeStruct((VEC_LANES, width), F32),
        ],
        compiler_params=pltpu.CompilerParams(vmem_limit_bytes=VMEM_LIMIT),
        cost_estimate=pl.CostEstimate(
            flops=12_000_000_000, bytes_accessed=22_000_000, transcendentals=5_000_000
        ),
        name="attend_forward",
    )(numbers, *pieces, tokens, ids)


def mlp_kernel(numbers, near, far, *refs):
    (vectors, mixed, tokens, cotangent, output, grad_residual, grad_mixed, inner, grads_near,
     grads_far, sums, one, two, proj_parts, proj, acc_one, acc_two, acc_proj, bias
    ) = refs
    step = pl.program_id(0)
    width = tokens.shape[1]
    mid = near.shape[1]
    parts = mid + far.shape[1]
    block = width // parts
    last_at = 2 * width
    hidden_width = one.shape[1]

    @pl.when(step == 0)
    def assemble():
        for part in range(parts):
            ref, at = (near, part) if part < mid else (far, part - mid)
            lanes = pl.ds(part * width, width)
            for group in range(near.shape[0]):
                here = pl.ds(group * near.shape[2], near.shape[2])
                one[here, lanes] = ref[group, at, :, :width]
                two[here, lanes] = ref[group, at, :, width:last_at]
                proj_parts[part, here, :] = ref[group, at, :, last_at:]
        total = jnp.zeros((width, width), F32)
        for number in range(parts):
            piece = proj_parts[numbers[PLACES + number]].astype(F32)
            kept = jnp.where(lane_numbers(piece.shape) < block, piece, 0.0)
            wide = jnp.concatenate([kept, jnp.zeros((width, width - SUB), F32)], axis=1)
            total = total + (pltpu.roll(wide, block * number, 1) if number else wide)
        proj[...] = total.astype(LOW)
        for part in range(parts):
            row = vectors[pl.ds(8 + numbers[OWNERS + part], 1), :]
            bias[0:1, part * width : (part + 1) * width] = row
        acc_one[...] = jnp.zeros(acc_one.shape, F32)
        acc_two[...] = jnp.zeros(acc_two.shape, F32)
        acc_proj[...] = jnp.zeros(acc_proj.shape, F32)
        sums[...] = jnp.zeros(sums.shape, F32)

    def add_row(row, values):
        sums[pl.ds(row, 1), :] += jnp.sum(values, axis=0, keepdims=True)

    own = mixed[...]
    residual = tokens[...].astype(F32) + dot(own, proj[...], NT) + vectors[4:5, :]
    normed, rate = norm_parts(residual)
    gain = vectors[5:6, :]
    second_in = (normed * gain + vectors[6:7, :]).astype(LOW)
    out_low = cotangent[...]
    grad_out = out_low.astype(F32)
    second_turned = second_in.T
    out_turned = out_low.T
    totals = [residual + vectors[7:8, :], jnp.zeros(residual.shape, F32)]

    count = hidden_width // FF_CHUNK
    ones = jnp.ones((16, MLP_TILE), LOW)
    second_and_ones = jnp.concatenate([second_turned, ones], axis=0)
    hiddens, slopes, kept = {}, {}, {}

    def lanes_of(number):
        return pl.ds(number * FF_CHUNK, FF_CHUNK)

    def make_hidden(number):
        hiddens[number] = dot(second_in, one[:, lanes_of(number)])

    def make_slope(number):
        slopes[number] = dot(out_low, two[:, lanes_of(number)])

    def add_one(number):
        acc_one[:, lanes_of(number)] += dot(second_and_ones, kept[number][1])

    def add_two(number):
        acc_two[:, lanes_of(number)] += dot(out_turned, kept[number][0])

    def add_result(number):
        totals[0] = totals[0] + dot(kept[number][0], two[:, lanes_of(number)], NT)

    def add_second(number):
        totals[1] = totals[1] + dot(kept[number][1], one[:, lanes_of(number)], NT)

    make_hidden(0)
    make_slope(0)
    for number in range(count):
        between = []
        if number + 1 < count:
            between += [functools.partial(f, number + 1) for f in (make_hidden, make_slope)]
        if number > 0:
            between += [
                functools.partial(f, number - 1)
                for f in (add_result, add_second, add_one, add_two)
            ]
        kept[number] = gelu_rows(
            hiddens.pop(number), bias[0:1, lanes_of(number)], slopes.pop(number), between
        )
    for f in (add_result, add_second, add_one, add_two):
        f(count - 1)
    result, grad_second = totals
    output[...] = result.astype(LOW)
    add_row(5, grad_second * normed)
    add_row(6, grad_second)
    add_row(7, grad_out)
    grad_res = grad_out + norm_back(grad_second, normed, rate, gain)
    grad_residual[...] = grad_res
    branch = grad_res.astype(LOW)
    add_row(4, branch.astype(F32))
    acc_proj[...] += dot(branch.T, own)
    grad_own = dot(branch, proj[...]).astype(LOW)
    grad_mixed[...] = grad_own
    high, rest = halves(grad_own.astype(F32) * own.astype(F32))
    head = lax.broadcasted_iota(jnp.int32, (16, width), 0)
    chosen = (lane_numbers((16, width)) // (width // HEADS) == head).astype(F32).astype(LOW)
    inner[...] = (dot(chosen, high, NT) + dot(chosen, rest, NT))[:8]

    @pl.when(step == pl.num_programs(0) - 1)
    def finish():
        total = acc_proj[...]
        for number in range(parts):
            turned = pltpu.roll(total, (width - block * number) % width, 1) if number else total
            proj_parts[numbers[PLACES + number]] = turned[:, :SUB].astype(LOW)
        for part in range(parts):
            ref, at = (grads_near, part) if part < mid else (grads_far, part - mid)
            lanes = pl.ds(part * width, width)
            for group in range(ref.shape[0]):
                here = pl.ds(group * ref.shape[2], ref.shape[2])
                ref[group, at, :, :width] = acc_one[here, lanes].astype(LOW)
                ref[group, at, :, width:last_at] = acc_two[here, lanes].astype(LOW)
                ref[group, at, :, last_at:] = proj_parts[part, here, :]
            sums[pl.ds(8 + numbers[OWNERS + part], 1), :] = acc_one[width : width + 1, lanes]


def mlp_both(numbers, near, far, vectors, mixed, tokens, cotangent):
    rows, width = tokens.shape
    parts = near.shape[1] + far.shape[1]
    hidden_width = parts * width
    tile = pl.BlockSpec((MLP_TILE, width), lambda s, *_: (s, 0))
    whole = lambda *dims: pl.BlockSpec(dims, lambda s, *_: (0,) * len(dims))
    return pl.pallas_call(
        mlp_kernel,
        grid_spec=pltpu.PrefetchScalarGridSpec(
            num_scalar_prefetch=1,
            grid=(rows // MLP_TILE,),
            in_specs=[
                whole(*near.shape), whole(*far.shape), whole(*vectors.shape), tile, tile, tile
            ],
            out_specs=[
                tile,
                tile,
                tile,
                pl.BlockSpec((8, MLP_TILE), lambda s, *_: (0, s)),
                whole(*near.shape),
                whole(*far.shape),
                whole(*vectors.shape),
            ],
            scratch_shapes=[
                pltpu.VMEM((width, hidden_width), LOW),
                pltpu.VMEM((width, hidden_width), LOW),
                pltpu.VMEM((parts, width, SUB), LOW),
                pltpu.VMEM((width, width), LOW),
                pltpu.VMEM((width + 16, hidden_width), F32),
                pltpu.VMEM((width, hidden_width), F32),
                pltpu.VMEM((width, width), F32),
                pltpu.VMEM((8, hidden_width), F32),
            ],
        ),
        out_shape=[
            jax.ShapeDtypeStruct((rows, width), LOW),
            jax.ShapeDtypeStruct((rows, width), F32),
            jax.ShapeDtypeStruct((rows, width), LOW),
            jax.ShapeDtypeStruct((8, rows), F32),
            jax.ShapeDtypeStruct(near.shape, LOW),
            jax.ShapeDtypeStruct(far.shape, LOW),
            jax.ShapeDtypeStruct(vectors.shape, F32),
        ],
        compiler_params=pltpu.CompilerParams(vmem_limit_bytes=VMEM_LIMIT),
        cost_estimate=pl.CostEstimate(
            flops=34_000_000_000, bytes_accessed=20_000_000, transcendentals=6_000_000
        ),
        name="mlp_both",
    )(numbers, near, far, vectors, mixed, tokens, cotangent)


def attend_back_kernel(
    numbers,
    query,
    key_turned,
    value,
    probs,
    inner,
    grad_mixed,
    normed_turned,
    weight,
    vectors,
    sums,
    grad_qkv,
    near,
    far,
    grad_query,
    acc_key,
    acc_value,
    acc_sums,
    normed_sums,
    blocks,
    rows,
):
    step = pl.program_id(0)
    chunks = pl.num_programs(0) - 1
    pairs = range(PAIRS)
    count = len(pairs)
    scale = (SUB // 2) ** (-0.5)

    @pl.when(step == 0)
    def clear():
        acc_key[...] = jnp.zeros(acc_key.shape, F32)
        acc_value[...] = jnp.zeros(acc_value.shape, F32)
        normed_sums[...] = jnp.zeros(normed_sums.shape, F32)
        acc_sums[...] = jnp.zeros(acc_sums.shape, F32)

    @pl.when(step < chunks)
    def attend():
        def place(number):
            sub, at = number // count, number % count
            start = pl.multiple_of((step * (TILE // SUB) + sub) * SUB, SUB)
            return sub, at, start, pl.ds(start, SPAN), pl.ds(at * SUB, SUB)

        def slope(number):
            sub, _, _, near_rows, heads = place(number)
            grad = both_heads(grad_mixed[pl.ds(sub * SUB, SUB), heads])
            return dot(value[near_rows, heads], grad, NT)

        def soften(number, slopes):
            sub, at, _, _, _ = place(number)
            pair = pairs[at]
            cols = pl.ds(sub * SUB, SUB)
            both = []
            for head in range(2):
                lanes = slice(head * SUB, (head + 1) * SUB)
                less = slopes[:, lanes] - inner[2 * pair + head : 2 * pair + head + 1, cols]
                both.append((probs[at, sub, :, lanes].astype(F32) * less).astype(LOW))
            return jnp.concatenate(both, axis=1)

        def collect(number, scores):
            sub, at, start, near_rows, heads = place(number)
            first, second = halves_of(dot(key_turned[heads, near_rows], scores))
            turned = (jnp.concatenate([first, second], axis=0) * scale).astype(LOW)
            grad_query[pl.ds(start, SUB), heads] = turned.T
            wanted = both_heads(query[pl.ds(start + MARGIN, SUB), heads])
            acc_key[near_rows, heads] += dot(scores, wanted)
            grad = both_heads(grad_mixed[pl.ds(sub * SUB, SUB), heads])
            acc_value[near_rows, heads] += dot(probs[at, sub], grad)

        staged(TILE // SUB * count, slope, soften, collect)

    @pl.when(step > 0)
    def collect():
        here = pl.ds(pl.multiple_of((step - 1) * TILE, SUB), TILE)
        there = pl.ds(pl.multiple_of((step - 1) * TILE + MARGIN, SUB), TILE)
        parts = (
            grad_query[here, :],
            acc_key[there, :].astype(LOW),
            acc_value[there, :].astype(LOW),
        )
        joined = jnp.concatenate(parts, axis=1)
        grad_qkv[...] = joined
        normed_sums[...] += dot(normed_turned[...], joined)
        acc_sums[0:1, :] += jnp.sum(joined.astype(F32), axis=0, keepdims=True)

    @pl.when(step == chunks)
    def finish():
        weight_grad(
            numbers, normed_sums[...], acc_sums[0:1, :], weight, vectors, sums, near, far, blocks, rows
        )


def weight_grad(numbers, total, columns, weight, vectors, sums, near, far, blocks, rows):
    width = weight.shape[0]
    parts, mid = blocks.shape[0], near.shape[0]
    block = 3 * width // parts
    rows_each = 12 // parts
    wide = weight[...].astype(F32)
    grad_gain = jnp.sum(total * wide, axis=1, keepdims=True)
    grad_shift = jnp.sum(wide * columns, axis=1, keepdims=True)
    rows[...] = jnp.zeros(rows.shape, F32)
    rows[0:VEC_LANES, :] = sums[...]
    rows[2:3, :] = columns[:, :width]
    rows[3:4, :] = columns[:, 2 * width :]
    rows[VEC_LANES : 2 * VEC_LANES, :] = vectors[...]
    turned = rows[...].T
    gain = turned[:, VEC_LANES : VEC_LANES + 1]
    shift = turned[:, VEC_LANES + 1 : VEC_LANES + 2]
    lane = lane_numbers(turned.shape)
    turned = jnp.where(lane == 0, grad_gain, jnp.where(lane == 1, grad_shift, turned))
    total = total * gain + shift * columns
    at = block - 2 * SUB
    for number in range(parts):
        away = (3 * width - block * number) % (3 * width)
        piece = (pltpu.roll(total, away, 1) if number else total)[:, :width]
        vec = pltpu.roll(turned, (at - rows_each * number) % SUB, 1)
        last = jnp.where(lane < at, piece[:, 2 * SUB :], 0.0)
        last = jnp.where((lane >= at) & (lane < at + rows_each), vec, last)
        at_place = numbers[PLACES + number]
        blocks[at_place, :, : 2 * SUB] = piece[:, : 2 * SUB].astype(LOW)
        blocks[at_place, :, 2 * SUB :] = last.astype(LOW)
    near[...] = blocks[:mid]
    far[...] = blocks[mid:]


def attend_backward(
    numbers, parts, query, key_turned, value, probs, inner, grad_mixed, normed_turned, weight,
    vectors, sums,
):
    width, rows = normed_turned.shape
    padded = query.shape[0]
    chunks = rows // TILE
    tiles = TILE // SUB
    now = lambda s: jnp.minimum(s, chunks - 1)
    before = lambda s: jnp.maximum(s - 1, 0)
    whole = lambda *dims: pl.BlockSpec(dims, lambda s, *_: (0,) * len(dims))
    half = (parts // 2, width, width)
    return pl.pallas_call(
        attend_back_kernel,
        grid_spec=pltpu.PrefetchScalarGridSpec(
            num_scalar_prefetch=1,
            grid=(chunks + 1,),
            in_specs=[
                whole(padded, width),
                whole(width, padded),
                whole(padded, width),
                pl.BlockSpec((PAIRS, tiles, SPAN, 2 * SUB), lambda s, *_: (0, now(s), 0, 0)),
                pl.BlockSpec((8, TILE), lambda s, *_: (0, now(s))),
                pl.BlockSpec((TILE, width), lambda s, *_: (now(s), 0)),
                pl.BlockSpec((width, TILE), lambda s, *_: (0, before(s))),
                whole(*weight.shape),
                whole(*vectors.shape),
                whole(*sums.shape),
            ],
            out_specs=[
                pl.BlockSpec((TILE, 3 * width), lambda s, *_: (before(s), 0)),
                whole(*half),
                whole(*half),
            ],
            scratch_shapes=[
                pltpu.VMEM((rows, width), LOW),
                pltpu.VMEM((padded, width), F32),
                pltpu.VMEM((padded, width), F32),
                pltpu.VMEM((8, 3 * width), F32),
                pltpu.VMEM((width, 3 * width), F32),
                pltpu.VMEM((parts, width, width), LOW),
                pltpu.VMEM((SUB, width), F32),
            ],
        ),
        out_shape=[
            jax.ShapeDtypeStruct((rows, 3 * width), LOW),
            jax.ShapeDtypeStruct(half, LOW),
            jax.ShapeDtypeStruct(half, LOW),
        ],
        compiler_params=pltpu.CompilerParams(vmem_limit_bytes=VMEM_LIMIT),
        cost_estimate=pl.CostEstimate(
            flops=16_000_000_000, bytes_accessed=24_000_000, transcendentals=0
        ),
        name="attend_backward",
    )(
        numbers, query, key_turned, value, probs, inner, grad_mixed, normed_turned, weight, vectors,
        sums,
    )


def input_grad_kernel(weight, vectors, tokens, grad_residual, grad_qkv, input_grad):
    normed, rate = norm_parts(tokens[...].astype(F32))
    grad_first = dot(grad_qkv[...], weight[...], NT)
    back = norm_back(grad_first, normed, rate, vectors[0:1, :])
    input_grad[...] = (grad_residual[...] + back).astype(LOW)


def input_gradient(weight, vectors, tokens, grad_residual, grad_qkv):
    rows, width = tokens.shape
    size = TILE
    tile = pl.BlockSpec((size, width), lambda s: (s, 0))
    whole = lambda ref: pl.BlockSpec(ref.shape, lambda s: (0, 0))
    return pl.pallas_call(
        input_grad_kernel,
        grid=(rows // size,),
        in_specs=[
            whole(weight), whole(vectors), tile, tile,
            pl.BlockSpec((size, 3 * width), lambda s: (s, 0)),
        ],
        out_specs=tile,
        out_shape=jax.ShapeDtypeStruct((rows, width), LOW),
        compiler_params=pltpu.CompilerParams(vmem_limit_bytes=VMEM_LIMIT),
        cost_estimate=pl.CostEstimate(
            flops=4_000_000_000, bytes_accessed=13_000_000, transcendentals=2048
        ),
        name="input_gradient",
    )(weight, vectors, tokens, grad_residual, grad_qkv)


def halves(value):
    high = value.astype(LOW)
    return high, (value - high.astype(F32)).astype(LOW)


def dot_three(left, right):
    tall = jnp.concatenate([right[0], right[0], right[1]], axis=0)
    return dot(jnp.concatenate([left[0], left[1], left[0]], axis=1), tall)


def newton_rows(blocks, offset, rows):
    gram = dot(blocks[0], blocks[0], NT)
    for part in blocks[1:]:
        gram = gram + dot(part, part, NT)
    depth = gram.shape[0]
    down = lax.broadcasted_iota(jnp.int32, (depth, depth), 0)
    eye = (down == lane_numbers((depth, depth))).astype(F32)
    norm = 1.0 / (jnp.sqrt(jnp.sum(gram * eye, keepdims=True)) + 1e-07)
    gram = gram * (norm * norm)
    place = lax.broadcasted_iota(jnp.int32, (rows, depth), 0) + offset
    left = jnp.where(place == lane_numbers((rows, depth)), norm, 0.0)
    for step in range(NS_STEPS - 1):
        pair = halves(gram)
        poly = halves(NEWTON_A * eye + NEWTON_B * gram + NEWTON_C * dot_three(pair, pair))
        lefts = halves(left)
        both = dot_three([jnp.concatenate([pair[n], lefts[n]], axis=0) for n in range(2)], poly)
        left = both[depth:]
        gram = dot_three(halves(both[:depth]), poly)
    pair = halves(gram)
    once = dot_three(halves(left), pair)
    return NEWTON_A * left + NEWTON_B * once + NEWTON_C * dot_three(halves(once), pair)


def stepped(left, own, height, old):
    high, rest = halves(left)
    ortho = (dot(high, own) + dot(rest, own))[: old.shape[0], : old.shape[1]]
    return old * (1.0 - MUON_RATE * MUON_DECAY) - (MUON_RATE * 0.2 * math.sqrt(height)) * ortho


def kept_lanes(value, low, high):
    lane = lane_numbers(value.shape)
    return jnp.where((lane >= low) & (lane < high), value.astype(F32), 0.0).astype(LOW)


def tall_of(rows):
    return -(-rows // 16) * 16


def muon_kernel(height, numbers, *refs):
    old, new, copy = refs[-3:]
    count = old.shape[1]
    blocks = [kept_lanes(ref[...], 0, count) for ref in refs[:-3]]
    left = newton_rows(blocks, numbers[OFFSET], tall_of(old.shape[0]))
    result = stepped(left, blocks[0], height, old[...])
    new[...] = result
    copy[...] = result.astype(LOW)


def muon(height, numbers, blocks, old):
    vmem = pl.BlockSpec(memory_space=pltpu.VMEM)

    def kernel(*refs):
        muon_kernel(height, *refs)

    return pl.pallas_call(
        kernel,
        in_specs=[pl.BlockSpec(memory_space=pltpu.SMEM)] + [vmem] * (len(blocks) + 1),
        out_specs=[vmem, vmem],
        out_shape=[
            jax.ShapeDtypeStruct(old.shape, F32),
            jax.ShapeDtypeStruct(old.shape, LOW),
        ],
        compiler_params=pltpu.CompilerParams(vmem_limit_bytes=VMEM_LIMIT),
        cost_estimate=pl.CostEstimate(
            flops=9_000_000_000, bytes_accessed=2_000_000, transcendentals=10
        ),
        name="muon",
    )(numbers, *blocks, old)


def pick_kernel(numbers, columns, *outs):
    for n, out in enumerate(outs):
        at = pl.multiple_of(numbers[STARTS + n] * SUB, SUB)
        out[...] = columns[:, pl.ds(at, out.shape[1])]


def pick(numbers, columns, count):
    depth = columns.shape[0]
    vmem = pl.BlockSpec(memory_space=pltpu.VMEM)
    return pl.pallas_call(
        pick_kernel,
        in_specs=[pl.BlockSpec(memory_space=pltpu.SMEM), vmem],
        out_specs=[vmem] * count,
        out_shape=[jax.ShapeDtypeStruct((depth, depth), LOW)] * count,
        name="pick",
    )(numbers, columns)


def newton_kernel(numbers, *refs):
    left = refs[-1]
    bounds = numbers[LOW_LANE], numbers[HIGH_LANE]
    blocks = [kept_lanes(ref[...], *bounds) for ref in refs[:-1]]
    left[...] = newton_rows(blocks, numbers[OFFSET], left.shape[0])


def newton(numbers, blocks, rows):
    vmem = pl.BlockSpec(memory_space=pltpu.VMEM)
    return pl.pallas_call(
        newton_kernel,
        in_specs=[pl.BlockSpec(memory_space=pltpu.SMEM)] + [vmem] * len(blocks),
        out_specs=vmem,
        out_shape=jax.ShapeDtypeStruct((tall_of(rows), blocks[0].shape[0]), F32),
        compiler_params=pltpu.CompilerParams(vmem_limit_bytes=VMEM_LIMIT),
        cost_estimate=pl.CostEstimate(
            flops=9_000_000_000, bytes_accessed=2_000_000, transcendentals=10
        ),
        name="newton",
    )(numbers, *blocks)


def finish_kernel(heights, lanes, numbers, columns, *refs):
    count = len(heights)
    store = refs[-1]
    news = refs[-1 - 2 * count : -1]
    olds = refs[-1 - 3 * count : -1 - 2 * count]
    lefts = refs[: -1 - 3 * count]
    for n, left in enumerate(lefts):
        store[n] = left[...]
    for n in range(count):
        wide = -(-olds[n].shape[1] // SUB) * SUB
        own = columns[:, lanes[n] : lanes[n] + wide]
        result = stepped(store[numbers[WHICH + n]], own, heights[n], olds[n][...])
        news[2 * n][...] = result
        news[2 * n + 1][...] = result.astype(LOW)


def finish(heights, lanes, numbers, columns, lefts, olds):
    vmem = pl.BlockSpec(memory_space=pltpu.VMEM)
    count = len(olds)

    def kernel(*refs):
        finish_kernel(heights, lanes, *refs)

    outs = pl.pallas_call(
        kernel,
        in_specs=[pl.BlockSpec(memory_space=pltpu.SMEM)] + [vmem] * (1 + len(lefts) + count),
        out_specs=[vmem] * (2 * count),
        out_shape=[
            jax.ShapeDtypeStruct(old.shape, kind) for old in olds for kind in (F32, LOW)
        ],
        scratch_shapes=[pltpu.VMEM((len(lefts), *lefts[0].shape), F32)],
        compiler_params=pltpu.CompilerParams(vmem_limit_bytes=VMEM_LIMIT),
        cost_estimate=pl.CostEstimate(
            flops=200_000_000, bytes_accessed=2_000_000, transcendentals=0
        ),
        name="finish",
    )(numbers, columns, *lefts, *olds)
    return [(outs[2 * n], outs[2 * n + 1]) for n in range(count)]


def exchange(x, axis, mask):
    size = lax.axis_size(axis)
    return lax.ppermute(x, axis, [(i, i ^ mask) for i in range(size)])


def place_masks(size):
    masks = [0]
    bit = size // 2
    while bit >= 1:
        masks = masks + [m ^ bit for m in masks]
        bit //= 2
    return masks


def from_columns(own):
    size = lax.axis_size("dp")
    sent = jnp.broadcast_to(own[None], (size, *own.shape))
    return lax.all_to_all(sent, "dp", split_axis=0, concat_axis=0, tiled=True)


def over_columns(own):
    return from_columns(own).reshape(-1, own.shape[1])


def device_numbers(dp, ns, share, width, proj_rows):
    masks = place_masks(ns)
    tasks = [(0, 0, width), (width // SUB, 0, width)]
    tasks += [(width // SUB + 1, 2 * SUB, 2 * SUB + proj_rows)] * (ns - 2)
    table = np.zeros((dp * ns, 24), np.int32)
    for device in range(dp * ns):
        column, index = device // ns, device % ns
        row = table[device]
        for n in range(ns):
            row[OWNERS + n] = index ^ masks[n]
            row[PLACES + (index ^ masks[n])] = n
            row[STARTS + n] = tasks[index ^ n][0]
        for n in range(3):
            row[WHICH + n] = index ^ n
        row[OFFSET] = column * share
        row[COLUMN] = column
        row[LOW_LANE], row[HIGH_LANE] = tasks[index][1:]
    return table


def over_rows(own):
    held = [own]
    bit = lax.axis_size("ns") // 2
    while bit >= 1:
        held = held + [exchange(block, "ns", bit) for block in held]
        bit //= 2
    return held


def added(keep, got):
    return (keep.astype(F32) + got.astype(F32)).astype(LOW)


def sum_columns(pieces):
    return summed(lax.all_to_all(pieces, "dp", split_axis=0, concat_axis=0, tiled=True))


def summed(pieces):
    return jnp.sum(pieces.astype(F32), axis=0)


def split_kernel(numbers, keep, got, *outs):
    share = outs[0].shape[0]
    for mask, out in enumerate(outs):
        at = pl.ds(pl.multiple_of((numbers[COLUMN] ^ mask) * share, 16), share)
        out[...] = added(keep[at, :], got[at, :])


def split_sum(numbers, keep, got, devices):
    vmem = pl.BlockSpec(memory_space=pltpu.VMEM)
    shape = jax.ShapeDtypeStruct((keep.shape[0] // devices, keep.shape[1]), LOW)
    return pl.pallas_call(
        split_kernel,
        in_specs=[pl.BlockSpec(memory_space=pltpu.SMEM), vmem, vmem],
        out_specs=[vmem] * devices,
        out_shape=[shape] * devices,
        cost_estimate=pl.CostEstimate(
            flops=200_000, bytes_accessed=1_000_000, transcendentals=0
        ),
        name="split_sum",
    )(numbers, keep, got)


def sum_columns_direct(numbers, keep, got):
    devices = lax.axis_size("dp")
    if devices > 8 or keep.shape[0] // devices % 16:
        return sum_columns(added(keep, got).reshape(devices, -1, keep.shape[1]))
    pieces = split_sum(numbers, keep, got, devices)
    total = pieces[0].astype(F32)
    for mask in range(1, devices):
        total = total + exchange(pieces[mask], "dp", mask).astype(F32)
    return total


def widened(arrays, lanes):
    joined = jnp.concatenate(arrays, axis=1)
    return jnp.pad(joined, ((0, 0), (0, lanes - joined.shape[1])))


def per_device(
    tokens,
    cotangent,
    segment,
    valid_rows,
    qkv_weight,
    proj_weight,
    fc1_weight,
    fc2_weight,
    qkv_moment,
    proj_moment,
    fc1_moment,
    fc2_moment,
    vectors,
    vector_moment,
    vector_square,
):
    rows, width = tokens.shape
    ns = lax.axis_size("ns")
    qkv_w, proj_w, fc1_w, fc2_w = (w.T for w in (qkv_weight, proj_weight, fc1_weight, fc2_weight))
    qkv_m, proj_m, fc1_m, fc2_m = (w.T for w in (qkv_moment, proj_moment, fc1_moment, fc2_moment))
    share, count = qkv_w.shape
    vec_rows = vectors.shape[0]
    first_lanes = width
    later_lanes = 2 * width + SUB

    table = device_numbers(lax.axis_size("dp"), ns, share, width, proj_w.shape[1])
    device = lax.axis_index("dp") * ns + lax.axis_index("ns")
    numbers = lax.dynamic_slice(jnp.asarray(table), (device, 0), (1, table.shape[1]))[0]

    row_ids = jnp.where(
        valid_rows > 0, segment, rows + jnp.arange(rows, dtype=jnp.int32)
    ).astype(F32)
    ids = jnp.pad(row_ids, (MARGIN, MARGIN), constant_values=-1.0).reshape(-1, SUB)
    ids = jnp.pad(ids, ((0, -ids.shape[0] % 8), (0, 0)), constant_values=-1.0)

    later_own = widened([fc1_w, fc2_w, proj_w], later_lanes).astype(LOW)
    later_pair = jnp.stack([later_own, exchange(later_own, "ns", ns // 2)])
    first_own = widened([qkv_w, vectors.T], first_lanes).astype(LOW)
    first_pieces = over_rows(over_columns(first_own))
    later_near = from_columns(later_pair)
    if share % 16:
        later_near = jnp.moveaxis(later_near, 0, 1).reshape(1, ns // 2, width, later_lanes)

    (query, _, value, key_turned, normed_turned, mixed, probs, weight, vector_full) = (
        attend_forward(numbers, first_pieces, tokens, ids)
    )
    later_near, mixed = lax.optimization_barrier((later_near, mixed))
    later_far = exchange(later_near, "ns", 1)
    output, grad_residual, grad_mixed, inner, grads_near, grads_far, sums = mlp_both(
        numbers, later_near, later_far, vector_full, mixed, tokens, cotangent
    )
    held = added(grads_near, exchange(grads_far, "ns", 1))
    held, grad_mixed = lax.optimization_barrier((held, grad_mixed))
    if share % 16:
        held = jnp.moveaxis(held.reshape(ns // 2, -1, share, later_lanes), 1, 0)
    later_got = lax.all_to_all(held, "dp", split_axis=0, concat_axis=0, tiled=True)

    grad_qkv, grads_near, grads_far = attend_backward(
        numbers, ns, query, key_turned, value, probs, inner, grad_mixed, normed_turned, weight,
        vector_full, sums,
    )
    held = added(grads_near, exchange(grads_far, "ns", 1))
    got = exchange(held[1], "ns", ns // 2)
    input_grad = input_gradient(weight, vector_full, tokens, grad_residual, grad_qkv)
    got, input_grad, later_got = lax.optimization_barrier((got, input_grad, later_got))
    first_owned = sum_columns_direct(numbers, held[0], got)

    later_sums = summed(later_got)
    later_owned = later_sums[0] + exchange(later_sums[1].astype(LOW), "ns", ns // 2).astype(F32)
    later_moment = later_owned + 0.5 * widened([fc1_m, fc2_m, proj_m], later_lanes)
    columns = lax.all_gather(later_moment.astype(LOW), "dp", axis=0, tiled=True)
    chosen = pick(numbers, columns, ns)
    blocks = [chosen[0]] + [exchange(chosen[mask], "ns", mask) for mask in range(1, ns)]
    left = newton(numbers, blocks, share)

    first_moment = first_owned + 0.5 * widened([qkv_m], first_lanes)
    first_own = over_columns(first_moment.astype(LOW))
    first_far = exchange(first_own, "ns", ns // 2)
    left, first_far = lax.optimization_barrier((left, first_far))
    first_pieces = [first_own, first_far]
    first_pieces += [exchange(piece, "ns", 1) for piece in first_pieces]
    qkv_new = muon(count * ns, numbers, first_pieces, qkv_w)

    lefts = [left] + [exchange(left, "ns", mask) for mask in range(1, ns)]
    fc1_new, fc2_new, proj_new = finish(
        [w.shape[1] * ns for w in (fc1_w, fc2_w, proj_w)],
        (0, width, 2 * width),
        numbers,
        columns,
        lefts,
        (fc1_w, fc2_w, proj_w),
    )

    news = (qkv_new, proj_new, fc1_new, fc2_new)
    moments_new = (
        first_moment[:, :count],
        later_moment[:, 2 * width : 2 * width + proj_w.shape[1]],
        later_moment[:, :width],
        later_moment[:, width : 2 * width],
    )

    vector_grad = first_owned[:, count : count + vec_rows].T
    first_new = BETA_ONE * vector_moment + (1.0 - BETA_ONE) * vector_grad
    second_new = BETA_TWO * vector_square + (1.0 - BETA_TWO) * vector_grad * vector_grad
    first_hat = first_new / (1.0 - BETA_ONE**STEP)
    second_hat = second_new / (1.0 - BETA_TWO**STEP)
    vectors_new = vectors - ADAM_RATE * first_hat / (jnp.sqrt(second_hat) + ADAM_EPS)
    return (
        output,
        input_grad,
        *(new[0].T for new in news),
        *(m.T for m in moments_new),
        first_new,
        second_new,
        vectors_new,
        *(new[1].T for new in news),
    )


def solution(mesh):
    rows = P(("dp", "ns"), None)
    flat = P(("dp", "ns"))
    block = P("ns", "dp")
    return jax.shard_map(
        per_device,
        mesh=mesh,
        in_specs=(rows, rows, flat, flat) + (block,) * 11,
        out_specs=(rows, rows) + (block,) * 15,
        check_vma=False,
    )
```

```python
import functools
import math

import jax
import jax.numpy as jnp
import numpy as np
from jax import lax
from jax.experimental import pallas as pl
from jax.experimental.pallas import tpu as pltpu
from jax.sharding import PartitionSpec as P

HEADS = 6
PAIRS = 3
MARGIN = 128
NS_STEPS = 5
STEP = 10
TILE = 512
MLP_TILE = 256
FF_CHUNK = 256
SUB = 128
SPAN = 384
VEC_LANES = 16


EPS_NORM = 1e-06
NEWTON_A = 3.4445
NEWTON_B = -4.775
NEWTON_C = 2.0315
MUON_RATE = 0.2
MUON_DECAY = 0.1
ADAM_RATE = 0.4
BETA_ONE = 0.9
BETA_TWO = 0.999
ADAM_EPS = 1e-08
LOW = jnp.bfloat16
F32 = jnp.float32
TN = (((0,), (0,)), ((), ()))
NT = (((1,), (1,)), ((), ()))
NN = (((1,), (0,)), ((), ()))
VMEM_LIMIT = 56 * 1024 * 1024
ERF_P = 0.3275911
ERF_COEFS = (0.254829592, -0.284496736, 1.421413741, -1.453152027, 1.061405429)


def dot(left, right, dims=NN):
    return lax.dot_general(left, right, dims, preferred_element_type=F32)


PLACES, OWNERS, STARTS, WHICH, OFFSET, LOW_LANE, HIGH_LANE, COLUMN = 0, 4, 8, 12, 16, 17, 18, 19


def lane_numbers(shape):
    return lax.broadcasted_iota(jnp.int32, shape, len(shape) - 1)


def norm_parts(value):
    center = value - jnp.mean(value, axis=-1, keepdims=True)
    rate = lax.rsqrt(jnp.mean(center * center, axis=-1, keepdims=True) + EPS_NORM)
    return center * rate, rate


def norm_back(grad, normed, rate, gain):
    scaled = grad * gain
    first = jnp.mean(scaled, axis=-1, keepdims=True)
    second = jnp.mean(scaled * normed, axis=-1, keepdims=True)
    return rate * (scaled - first - normed * second)


def gelu_both(value):
    below = 1.0 + (ERF_P * 0.5**0.5) * jnp.abs(value)
    ratio = pl.reciprocal(below, approx=True)
    ratio = ratio * (2.0 - below * ratio)
    decay = jnp.exp2((value * value) * (-0.5 * math.log2(math.e)))
    poly = 0.5 * ERF_COEFS[4]
    for coef in ERF_COEFS[3::-1]:
        poly = poly * ratio + 0.5 * coef
    tail = poly * ratio * decay
    phi = jnp.where(value >= 0, 1.0 - tail, tail)
    return value * phi, phi + (value * (1.0 / math.sqrt(2.0 * math.pi))) * decay


def gelu_rows(hidden, bias, grad, between):
    active, back = [], []
    rows = hidden.shape[0]
    pieces = rows // 16
    for n in range(pieces):
        if n * len(between) // pieces != (n - 1) * len(between) // pieces:
            between[n * len(between) // pieces]()
        here = slice(n * 16, (n + 1) * 16)
        value, slope = gelu_both(hidden[here] + bias)
        active.append(value.astype(LOW))
        back.append((grad[here] * slope).astype(LOW))
    return jnp.concatenate(active, axis=0), jnp.concatenate(back, axis=0)


def halves_of(lanes):
    half = lanes.shape[0] // 2
    return lanes[:half, :SUB], lanes[half:, SUB:]


def staged(count, first, second, third):
    made = [first(0)]
    kept = None
    for n in range(count):
        if n + 1 < count:
            made.append(first(n + 1))
        if kept is not None:
            third(n - 1, kept)
        kept = second(n, made[n])
        made[n] = None
    third(count - 1, kept)


def both_heads(pair):
    first = (lane_numbers((1, SUB)) < SUB // 2).astype(F32).astype(pair.dtype)
    second = (lane_numbers((1, SUB)) >= SUB // 2).astype(F32).astype(pair.dtype)
    return jnp.concatenate([pair * first, pair * second], axis=0)


def fetch(pairs, sems):
    copies = [
        pltpu.make_async_copy(source, target, sems.at[n])
        for n, (source, target) in enumerate(pairs)
    ]
    for copy in copies:
        copy.start()
    for copy in copies:
        copy.wait()


def attend_kernel(numbers, *refs):
    (tokens, ids, query, key, value, key_turned, normed_turned, mixed, probs, weight, vectors,
     gathered, pair_weight, value_turned, columns, shifts, sems) = refs[-17:]
    pieces = refs[:-17]
    step = pl.program_id(0)
    chunks = pl.num_programs(0) - 1
    width = tokens.shape[1]
    parts = len(pieces)
    block = 3 * width // parts
    rows_each = 12 // parts

    @pl.when(step == 0)
    def assemble():
        fetch([(piece, gathered.at[n]) for n, piece in enumerate(pieces)], sems)
        total = jnp.zeros((width, 3 * width), F32)
        turned = jnp.zeros((width, SUB), F32)
        for number in range(parts):
            piece = gathered[numbers[PLACES + number]].astype(F32)
            kept = jnp.where(lane_numbers(piece.shape) < block, piece, 0.0)
            wide = jnp.concatenate([kept, jnp.zeros((width, 2 * width), F32)], axis=1)
            total = total + (pltpu.roll(wide, block * number, 1) if number else wide)
            last = piece[:, 2 * SUB :]
            at = block - 2 * SUB
            lane = lane_numbers(last.shape)
            vec = jnp.where((lane >= at) & (lane < at + rows_each), last, 0.0)
            turned = turned + pltpu.roll(vec, (rows_each * number - at) % SUB, 1)
        total = total.astype(LOW)
        weight[...] = total
        pair_weight[...] = total[:, width:].T
        vectors[...] = turned.T[:VEC_LANES]
        shifts[...] = turned
        edges = (pl.ds(0, MARGIN), pl.ds(MARGIN + chunks * TILE, MARGIN))
        for edge in edges:
            for ref in (query, key, value):
                ref[edge, :] = jnp.zeros((MARGIN, width), LOW)
            for ref in (key_turned, value_turned):
                ref[:, edge] = jnp.zeros((width, MARGIN), LOW)
        for number in range(chunks * TILE // SUB + 2):
            row = jnp.broadcast_to(ids[number : number + 1, :], (SUB, SUB))
            columns[number * SUB : (number + 1) * SUB, :] = row.T

    @pl.when(step < chunks)
    def project():
        normed, _ = norm_parts(tokens[...].astype(F32))
        normed_turned[...] = normed.astype(LOW).T
        first_in = (normed * vectors[0:1, :] + vectors[1:2, :]).astype(LOW)
        result = dot(first_in, weight[...])
        turned = dot(pair_weight[...], first_in, NT)
        here = pl.ds(pl.multiple_of(MARGIN + step * TILE, SUB), TILE)
        scale = (width // HEADS) ** (-0.5)
        made = (result[:, :width] + vectors[2:3, :]).astype(LOW) * jnp.asarray(scale, LOW)
        query[here, :] = made
        key[here, :] = result[:, width : 2 * width].astype(LOW)
        value[here, :] = (result[:, 2 * width :] + vectors[3:4, :]).astype(LOW)
        key_turned[:, here] = turned[:width].astype(LOW)
        value_turned[:, here] = (turned[width:] + shifts[:, 3:4]).astype(LOW)

    @pl.when(step > 0)
    def attend():
        def place(number):
            sub, pair = number // PAIRS, number % PAIRS
            tile = (step - 1) * (TILE // SUB) + sub
            start = pl.multiple_of(tile * SUB, SUB)
            return sub, pair, tile, start, pl.ds(start, SPAN), pl.ds(pair * SUB, SUB)

        def score(number):
            _, _, _, start, near_rows, heads = place(number)
            wanted = both_heads(query[pl.ds(start + MARGIN, SUB), heads])
            return dot(key[near_rows, heads], wanted, NT)

        def soften(number, scores):
            sub, pair, tile, _, near_rows, _ = place(number)
            row = ids[pl.ds(tile + 1, 1), :]
            both = []
            for head in range(2):
                same = columns[near_rows, :] == row
                own = jnp.where(same, scores[:, head * SUB : (head + 1) * SUB], -1e30)
                expo = jnp.exp(own - jnp.max(own, axis=0, keepdims=True))
                share = 1.0 / jnp.sum(expo, axis=0, keepdims=True)
                both.append((expo * share).astype(LOW))
            prob = jnp.concatenate(both, axis=1)
            probs[pair, sub] = prob
            return prob

        def mix(number, prob):
            sub, _, _, _, near_rows, heads = place(number)
            first, second = halves_of(dot(value_turned[heads, near_rows], prob))
            turned = jnp.concatenate([first, second], axis=0).astype(LOW)
            mixed[pl.ds(sub * SUB, SUB), heads] = turned.T

        staged(TILE // SUB * PAIRS, score, soften, mix)


def attend_forward(numbers, pieces, tokens, ids):
    rows, width = tokens.shape
    chunks = rows // TILE
    tiles = TILE // SUB
    parts = len(pieces)
    now = lambda s: jnp.minimum(s, chunks - 1)
    before = lambda s: jnp.maximum(s - 1, 0)
    whole = lambda *dims: pl.BlockSpec(dims, lambda s, *_: (0,) * len(dims))
    padded = rows + 2 * MARGIN
    return pl.pallas_call(
        attend_kernel,
        grid_spec=pltpu.PrefetchScalarGridSpec(
            num_scalar_prefetch=1,
            grid=(chunks + 1,),
            in_specs=[pl.BlockSpec(memory_space=pl.ANY)] * parts
            + [
                pl.BlockSpec((TILE, width), lambda s, *_: (now(s), 0)),
                whole(*ids.shape),
            ],
            out_specs=[
                whole(padded, width),
                whole(padded, width),
                whole(padded, width),
                whole(width, padded),
                pl.BlockSpec((width, TILE), lambda s, *_: (0, now(s))),
                pl.BlockSpec((TILE, width), lambda s, *_: (before(s), 0)),
                pl.BlockSpec((PAIRS, tiles, SPAN, 2 * SUB), lambda s, *_: (0, before(s), 0, 0)),
                whole(width, 3 * width),
                whole(VEC_LANES, width),
            ],
            scratch_shapes=[
                pltpu.VMEM((parts, *pieces[0].shape), LOW),
                pltpu.VMEM((2 * width, width), LOW),
                pltpu.VMEM((width, padded), LOW),
                pltpu.VMEM((padded, SUB), F32),
                pltpu.VMEM((width, SUB), F32),
                pltpu.SemaphoreType.DMA((parts,)),
            ],
        ),
        out_shape=[
            jax.ShapeDtypeStruct((padded, width), LOW),
            jax.ShapeDtypeStruct((padded, width), LOW),
            jax.ShapeDtypeStruct((padded, width), LOW),
            jax.ShapeDtypeStruct((width, padded), LOW),
            jax.ShapeDtypeStruct((width, rows), LOW),
            jax.ShapeDtypeStruct((rows, width), LOW),
            jax.ShapeDtypeStruct((PAIRS, rows // SUB, SPAN, 2 * SUB), LOW),
            jax.ShapeDtypeStruct((width, 3 * width), LOW),
            jax.ShapeDtypeStruct((VEC_LANES, width), F32),
        ],
        compiler_params=pltpu.CompilerParams(vmem_limit_bytes=VMEM_LIMIT),
        cost_estimate=pl.CostEstimate(
            flops=12_000_000_000, bytes_accessed=22_000_000, transcendentals=5_000_000
        ),
        name="attend_forward",
    )(numbers, *pieces, tokens, ids)


def mlp_kernel(numbers, near, far, *refs):
    (vectors, mixed, tokens, cotangent, output, grad_residual, grad_mixed, inner, grads_near,
     grads_far, sums, one, two, proj_parts, proj, acc_one, acc_two, acc_proj, bias
    ) = refs
    step = pl.program_id(0)
    width = tokens.shape[1]
    mid = near.shape[1]
    parts = mid + far.shape[1]
    block = width // parts
    last_at = 2 * width
    hidden_width = one.shape[1]

    @pl.when(step == 0)
    def assemble():
        for part in range(parts):
            ref, at = (near, part) if part < mid else (far, part - mid)
            lanes = pl.ds(part * width, width)
            for group in range(near.shape[0]):
                here = pl.ds(group * near.shape[2], near.shape[2])
                one[here, lanes] = ref[group, at, :, :width]
                two[here, lanes] = ref[group, at, :, width:last_at]
                proj_parts[part, here, :] = ref[group, at, :, last_at:]
        total = jnp.zeros((width, width), F32)
        for number in range(parts):
            piece = proj_parts[numbers[PLACES + number]].astype(F32)
            kept = jnp.where(lane_numbers(piece.shape) < block, piece, 0.0)
            wide = jnp.concatenate([kept, jnp.zeros((width, width - SUB), F32)], axis=1)
            total = total + (pltpu.roll(wide, block * number, 1) if number else wide)
        proj[...] = total.astype(LOW)
        for part in range(parts):
            row = vectors[pl.ds(8 + numbers[OWNERS + part], 1), :]
            bias[0:1, part * width : (part + 1) * width] = row
        acc_one[...] = jnp.zeros(acc_one.shape, F32)
        acc_two[...] = jnp.zeros(acc_two.shape, F32)
        acc_proj[...] = jnp.zeros(acc_proj.shape, F32)
        sums[...] = jnp.zeros(sums.shape, F32)

    def add_row(row, values):
        sums[pl.ds(row, 1), :] += jnp.sum(values, axis=0, keepdims=True)

    own = mixed[...]
    residual = tokens[...].astype(F32) + dot(own, proj[...], NT) + vectors[4:5, :]
    normed, rate = norm_parts(residual)
    gain = vectors[5:6, :]
    second_in = (normed * gain + vectors[6:7, :]).astype(LOW)
    out_low = cotangent[...]
    grad_out = out_low.astype(F32)
    second_turned = second_in.T
    out_turned = out_low.T
    totals = [residual + vectors[7:8, :], jnp.zeros(residual.shape, F32)]

    count = hidden_width // FF_CHUNK
    ones = jnp.ones((16, MLP_TILE), LOW)
    second_and_ones = jnp.concatenate([second_turned, ones], axis=0)
    hiddens, slopes, kept = {}, {}, {}

    def lanes_of(number):
        return pl.ds(number * FF_CHUNK, FF_CHUNK)

    def make_hidden(number):
        hiddens[number] = dot(second_in, one[:, lanes_of(number)])

    def make_slope(number):
        slopes[number] = dot(out_low, two[:, lanes_of(number)])

    def add_one(number):
        acc_one[:, lanes_of(number)] += dot(second_and_ones, kept[number][1])

    def add_two(number):
        acc_two[:, lanes_of(number)] += dot(out_turned, kept[number][0])

    def add_result(number):
        totals[0] = totals[0] + dot(kept[number][0], two[:, lanes_of(number)], NT)

    def add_second(number):
        totals[1] = totals[1] + dot(kept[number][1], one[:, lanes_of(number)], NT)

    make_hidden(0)
    make_slope(0)
    for number in range(count):
        between = []
        if number + 1 < count:
            between += [functools.partial(f, number + 1) for f in (make_hidden, make_slope)]
        if number > 0:
            between += [
                functools.partial(f, number - 1)
                for f in (add_result, add_second, add_one, add_two)
            ]
        kept[number] = gelu_rows(
            hiddens.pop(number), bias[0:1, lanes_of(number)], slopes.pop(number), between
        )
    for f in (add_result, add_second, add_one, add_two):
        f(count - 1)
    result, grad_second = totals
    output[...] = result.astype(LOW)
    add_row(5, grad_second * normed)
    add_row(6, grad_second)
    add_row(7, grad_out)
    grad_res = grad_out + norm_back(grad_second, normed, rate, gain)
    grad_residual[...] = grad_res
    branch = grad_res.astype(LOW)
    add_row(4, branch.astype(F32))
    acc_proj[...] += dot(branch.T, own)
    grad_own = dot(branch, proj[...]).astype(LOW)
    grad_mixed[...] = grad_own
    high, rest = halves(grad_own.astype(F32) * own.astype(F32))
    head = lax.broadcasted_iota(jnp.int32, (16, width), 0)
    chosen = (lane_numbers((16, width)) // (width // HEADS) == head).astype(F32).astype(LOW)
    inner[...] = (dot(chosen, high, NT) + dot(chosen, rest, NT))[:8]

    @pl.when(step == pl.num_programs(0) - 1)
    def finish():
        total = acc_proj[...]
        for number in range(parts):
            turned = pltpu.roll(total, (width - block * number) % width, 1) if number else total
            proj_parts[numbers[PLACES + number]] = turned[:, :SUB].astype(LOW)
        for part in range(parts):
            ref, at = (grads_near, part) if part < mid else (grads_far, part - mid)
            lanes = pl.ds(part * width, width)
            for group in range(ref.shape[0]):
                here = pl.ds(group * ref.shape[2], ref.shape[2])
                ref[group, at, :, :width] = acc_one[here, lanes].astype(LOW)
                ref[group, at, :, width:last_at] = acc_two[here, lanes].astype(LOW)
                ref[group, at, :, last_at:] = proj_parts[part, here, :]
            sums[pl.ds(8 + numbers[OWNERS + part], 1), :] = acc_one[width : width + 1, lanes]


def mlp_both(numbers, near, far, vectors, mixed, tokens, cotangent):
    rows, width = tokens.shape
    parts = near.shape[1] + far.shape[1]
    hidden_width = parts * width
    tile = pl.BlockSpec((MLP_TILE, width), lambda s, *_: (s, 0))
    whole = lambda *dims: pl.BlockSpec(dims, lambda s, *_: (0,) * len(dims))
    return pl.pallas_call(
        mlp_kernel,
        grid_spec=pltpu.PrefetchScalarGridSpec(
            num_scalar_prefetch=1,
            grid=(rows // MLP_TILE,),
            in_specs=[
                whole(*near.shape), whole(*far.shape), whole(*vectors.shape), tile, tile, tile
            ],
            out_specs=[
                tile,
                tile,
                tile,
                pl.BlockSpec((8, MLP_TILE), lambda s, *_: (0, s)),
                whole(*near.shape),
                whole(*far.shape),
                whole(*vectors.shape),
            ],
            scratch_shapes=[
                pltpu.VMEM((width, hidden_width), LOW),
                pltpu.VMEM((width, hidden_width), LOW),
                pltpu.VMEM((parts, width, SUB), LOW),
                pltpu.VMEM((width, width), LOW),
                pltpu.VMEM((width + 16, hidden_width), F32),
                pltpu.VMEM((width, hidden_width), F32),
                pltpu.VMEM((width, width), F32),
                pltpu.VMEM((8, hidden_width), F32),
            ],
        ),
        out_shape=[
            jax.ShapeDtypeStruct((rows, width), LOW),
            jax.ShapeDtypeStruct((rows, width), F32),
            jax.ShapeDtypeStruct((rows, width), LOW),
            jax.ShapeDtypeStruct((8, rows), F32),
            jax.ShapeDtypeStruct(near.shape, LOW),
            jax.ShapeDtypeStruct(far.shape, LOW),
            jax.ShapeDtypeStruct(vectors.shape, F32),
        ],
        compiler_params=pltpu.CompilerParams(vmem_limit_bytes=VMEM_LIMIT),
        cost_estimate=pl.CostEstimate(
            flops=34_000_000_000, bytes_accessed=20_000_000, transcendentals=6_000_000
        ),
        name="mlp_both",
    )(numbers, near, far, vectors, mixed, tokens, cotangent)


def attend_back_kernel(
    numbers,
    query,
    key_turned,
    value,
    probs,
    inner,
    grad_mixed,
    normed_turned,
    weight,
    vectors,
    sums,
    grad_qkv,
    near,
    far,
    grad_query,
    acc_key,
    acc_value,
    acc_sums,
    normed_sums,
    blocks,
    rows,
):
    step = pl.program_id(0)
    chunks = pl.num_programs(0) - 1
    pairs = range(PAIRS)
    count = len(pairs)
    scale = (SUB // 2) ** (-0.5)

    @pl.when(step == 0)
    def clear():
        acc_key[...] = jnp.zeros(acc_key.shape, F32)
        acc_value[...] = jnp.zeros(acc_value.shape, F32)
        normed_sums[...] = jnp.zeros(normed_sums.shape, F32)
        acc_sums[...] = jnp.zeros(acc_sums.shape, F32)

    @pl.when(step < chunks)
    def attend():
        def place(number):
            sub, at = number // count, number % count
            start = pl.multiple_of((step * (TILE // SUB) + sub) * SUB, SUB)
            return sub, at, start, pl.ds(start, SPAN), pl.ds(at * SUB, SUB)

        def slope(number):
            sub, _, _, near_rows, heads = place(number)
            grad = both_heads(grad_mixed[pl.ds(sub * SUB, SUB), heads])
            return dot(value[near_rows, heads], grad, NT)

        def soften(number, slopes):
            sub, at, _, _, _ = place(number)
            pair = pairs[at]
            cols = pl.ds(sub * SUB, SUB)
            both = []
            for head in range(2):
                lanes = slice(head * SUB, (head + 1) * SUB)
                less = slopes[:, lanes] - inner[2 * pair + head : 2 * pair + head + 1, cols]
                both.append((probs[at, sub, :, lanes].astype(F32) * less).astype(LOW))
            return jnp.concatenate(both, axis=1)

        def collect(number, scores):
            sub, at, start, near_rows, heads = place(number)
            first, second = halves_of(dot(key_turned[heads, near_rows], scores))
            turned = (jnp.concatenate([first, second], axis=0) * scale).astype(LOW)
            grad_query[pl.ds(start, SUB), heads] = turned.T
            wanted = both_heads(query[pl.ds(start + MARGIN, SUB), heads])
            acc_key[near_rows, heads] += dot(scores, wanted)
            grad = both_heads(grad_mixed[pl.ds(sub * SUB, SUB), heads])
            acc_value[near_rows, heads] += dot(probs[at, sub], grad)

        staged(TILE // SUB * count, slope, soften, collect)

    @pl.when(step > 0)
    def collect():
        here = pl.ds(pl.multiple_of((step - 1) * TILE, SUB), TILE)
        there = pl.ds(pl.multiple_of((step - 1) * TILE + MARGIN, SUB), TILE)
        parts = (
            grad_query[here, :],
            acc_key[there, :].astype(LOW),
            acc_value[there, :].astype(LOW),
        )
        joined = jnp.concatenate(parts, axis=1)
        grad_qkv[...] = joined
        normed_sums[...] += dot(normed_turned[...], joined)
        acc_sums[0:1, :] += jnp.sum(joined.astype(F32), axis=0, keepdims=True)

    @pl.when(step == chunks)
    def finish():
        weight_grad(
            numbers, normed_sums[...], acc_sums[0:1, :], weight, vectors, sums, near, far, blocks, rows
        )


def weight_grad(numbers, total, columns, weight, vectors, sums, near, far, blocks, rows):
    width = weight.shape[0]
    parts, mid = blocks.shape[0], near.shape[0]
    block = 3 * width // parts
    rows_each = 12 // parts
    wide = weight[...].astype(F32)
    grad_gain = jnp.sum(total * wide, axis=1, keepdims=True)
    grad_shift = jnp.sum(wide * columns, axis=1, keepdims=True)
    rows[...] = jnp.zeros(rows.shape, F32)
    rows[0:VEC_LANES, :] = sums[...]
    rows[2:3, :] = columns[:, :width]
    rows[3:4, :] = columns[:, 2 * width :]
    rows[VEC_LANES : 2 * VEC_LANES, :] = vectors[...]
    turned = rows[...].T
    gain = turned[:, VEC_LANES : VEC_LANES + 1]
    shift = turned[:, VEC_LANES + 1 : VEC_LANES + 2]
    lane = lane_numbers(turned.shape)
    turned = jnp.where(lane == 0, grad_gain, jnp.where(lane == 1, grad_shift, turned))
    total = total * gain + shift * columns
    at = block - 2 * SUB
    for number in range(parts):
        away = (3 * width - block * number) % (3 * width)
        piece = (pltpu.roll(total, away, 1) if number else total)[:, :width]
        vec = pltpu.roll(turned, (at - rows_each * number) % SUB, 1)
        last = jnp.where(lane < at, piece[:, 2 * SUB :], 0.0)
        last = jnp.where((lane >= at) & (lane < at + rows_each), vec, last)
        at_place = numbers[PLACES + number]
        blocks[at_place, :, : 2 * SUB] = piece[:, : 2 * SUB].astype(LOW)
        blocks[at_place, :, 2 * SUB :] = last.astype(LOW)
    near[...] = blocks[:mid]
    far[...] = blocks[mid:]


def attend_backward(
    numbers, parts, query, key_turned, value, probs, inner, grad_mixed, normed_turned, weight,
    vectors, sums,
):
    width, rows = normed_turned.shape
    padded = query.shape[0]
    chunks = rows // TILE
    tiles = TILE // SUB
    now = lambda s: jnp.minimum(s, chunks - 1)
    before = lambda s: jnp.maximum(s - 1, 0)
    whole = lambda *dims: pl.BlockSpec(dims, lambda s, *_: (0,) * len(dims))
    half = (parts // 2, width, width)
    return pl.pallas_call(
        attend_back_kernel,
        grid_spec=pltpu.PrefetchScalarGridSpec(
            num_scalar_prefetch=1,
            grid=(chunks + 1,),
            in_specs=[
                whole(padded, width),
                whole(width, padded),
                whole(padded, width),
                pl.BlockSpec((PAIRS, tiles, SPAN, 2 * SUB), lambda s, *_: (0, now(s), 0, 0)),
                pl.BlockSpec((8, TILE), lambda s, *_: (0, now(s))),
                pl.BlockSpec((TILE, width), lambda s, *_: (now(s), 0)),
                pl.BlockSpec((width, TILE), lambda s, *_: (0, before(s))),
                whole(*weight.shape),
                whole(*vectors.shape),
                whole(*sums.shape),
            ],
            out_specs=[
                pl.BlockSpec((TILE, 3 * width), lambda s, *_: (before(s), 0)),
                whole(*half),
                whole(*half),
            ],
            scratch_shapes=[
                pltpu.VMEM((rows, width), LOW),
                pltpu.VMEM((padded, width), F32),
                pltpu.VMEM((padded, width), F32),
                pltpu.VMEM((8, 3 * width), F32),
                pltpu.VMEM((width, 3 * width), F32),
                pltpu.VMEM((parts, width, width), LOW),
                pltpu.VMEM((SUB, width), F32),
            ],
        ),
        out_shape=[
            jax.ShapeDtypeStruct((rows, 3 * width), LOW),
            jax.ShapeDtypeStruct(half, LOW),
            jax.ShapeDtypeStruct(half, LOW),
        ],
        compiler_params=pltpu.CompilerParams(vmem_limit_bytes=VMEM_LIMIT),
        cost_estimate=pl.CostEstimate(
            flops=16_000_000_000, bytes_accessed=24_000_000, transcendentals=0
        ),
        name="attend_backward",
    )(
        numbers, query, key_turned, value, probs, inner, grad_mixed, normed_turned, weight, vectors,
        sums,
    )


def input_grad_kernel(weight, vectors, tokens, grad_residual, grad_qkv, input_grad):
    normed, rate = norm_parts(tokens[...].astype(F32))
    grad_first = dot(grad_qkv[...], weight[...], NT)
    back = norm_back(grad_first, normed, rate, vectors[0:1, :])
    input_grad[...] = (grad_residual[...] + back).astype(LOW)


def input_gradient(weight, vectors, tokens, grad_residual, grad_qkv):
    rows, width = tokens.shape
    size = TILE
    tile = pl.BlockSpec((size, width), lambda s: (s, 0))
    whole = lambda ref: pl.BlockSpec(ref.shape, lambda s: (0, 0))
    return pl.pallas_call(
        input_grad_kernel,
        grid=(rows // size,),
        in_specs=[
            whole(weight), whole(vectors), tile, tile,
            pl.BlockSpec((size, 3 * width), lambda s: (s, 0)),
        ],
        out_specs=tile,
        out_shape=jax.ShapeDtypeStruct((rows, width), LOW),
        compiler_params=pltpu.CompilerParams(vmem_limit_bytes=VMEM_LIMIT),
        cost_estimate=pl.CostEstimate(
            flops=4_000_000_000, bytes_accessed=13_000_000, transcendentals=2048
        ),
        name="input_gradient",
    )(weight, vectors, tokens, grad_residual, grad_qkv)


def halves(value):
    high = value.astype(LOW)
    return high, (value - high.astype(F32)).astype(LOW)


def dot_three(left, right):
    tall = jnp.concatenate([right[0], right[0], right[1]], axis=0)
    return dot(jnp.concatenate([left[0], left[1], left[0]], axis=1), tall)


def dot_symmetric(left, right):
    depth = right[0].shape[1]
    cut = depth - depth % (2 * SUB)
    if cut == depth:
        return dot_three(left, right)
    first = dot_three(left, [part[:, :cut] for part in right])
    last = dot_three([part[cut:] for part in left], [part[:, cut:] for part in right])
    return jnp.concatenate(
        [first, jnp.concatenate([first[cut:].T, last], axis=0)], axis=1
    )


def newton_rows(blocks, offset, rows):
    gram = dot(blocks[0], blocks[0], NT)
    for part in blocks[1:]:
        gram = gram + dot(part, part, NT)
    depth = gram.shape[0]
    down = lax.broadcasted_iota(jnp.int32, (depth, depth), 0)
    eye = (down == lane_numbers((depth, depth))).astype(F32)
    norm = 1.0 / (jnp.sqrt(jnp.sum(gram * eye, keepdims=True)) + 1e-07)
    gram = gram * (norm * norm)
    place = lax.broadcasted_iota(jnp.int32, (rows, depth), 0) + offset
    left = jnp.where(place == lane_numbers((rows, depth)), norm, 0.0)
    for step in range(NS_STEPS - 1):
        pair = halves(gram)
        poly = halves(NEWTON_A * eye + NEWTON_B * gram + NEWTON_C * dot_symmetric(pair, pair))
        lefts = halves(left)
        both = dot_three([jnp.concatenate([pair[n], lefts[n]], axis=0) for n in range(2)], poly)
        left = both[depth:]
        gram = dot_symmetric(halves(both[:depth]), poly)
    pair = halves(gram)
    once = dot_three(halves(left), pair)
    return NEWTON_A * left + NEWTON_B * once + NEWTON_C * dot_three(halves(once), pair)


def stepped(left, own, height, old):
    high, rest = halves(left)
    ortho = (dot(high, own) + dot(rest, own))[: old.shape[0], : old.shape[1]]
    return old * (1.0 - MUON_RATE * MUON_DECAY) - (MUON_RATE * 0.2 * math.sqrt(height)) * ortho


def kept_lanes(value, low, high):
    lane = lane_numbers(value.shape)
    return jnp.where((lane >= low) & (lane < high), value.astype(F32), 0.0).astype(LOW)


def tall_of(rows):
    return -(-rows // 16) * 16


def muon_kernel(height, numbers, *refs):
    old, new, copy = refs[-3:]
    count = old.shape[1]
    blocks = [kept_lanes(ref[...], 0, count) for ref in refs[:-3]]
    left = newton_rows(blocks, numbers[OFFSET], tall_of(old.shape[0]))
    result = stepped(left, blocks[0], height, old[...])
    new[...] = result
    copy[...] = result.astype(LOW)


def muon(height, numbers, blocks, old):
    vmem = pl.BlockSpec(memory_space=pltpu.VMEM)

    def kernel(*refs):
        muon_kernel(height, *refs)

    return pl.pallas_call(
        kernel,
        in_specs=[pl.BlockSpec(memory_space=pltpu.SMEM)] + [vmem] * (len(blocks) + 1),
        out_specs=[vmem, vmem],
        out_shape=[
            jax.ShapeDtypeStruct(old.shape, F32),
            jax.ShapeDtypeStruct(old.shape, LOW),
        ],
        compiler_params=pltpu.CompilerParams(vmem_limit_bytes=VMEM_LIMIT),
        cost_estimate=pl.CostEstimate(
            flops=9_000_000_000, bytes_accessed=2_000_000, transcendentals=10
        ),
        name="muon",
    )(numbers, *blocks, old)


def pick_kernel(count, numbers, *refs):
    pieces, columns, outs = refs[:count], refs[count], refs[count + 1 :]
    share = pieces[0].shape[0]
    for k, piece in enumerate(pieces):
        columns[k * share : (k + 1) * share, :] = piece[...]
        for n, out in enumerate(outs):
            at = pl.multiple_of(numbers[STARTS + n] * SUB, SUB)
            out[k * share : (k + 1) * share, :] = piece[:, pl.ds(at, out.shape[1])]


def pick(numbers, pieces, count):
    depth = len(pieces) * pieces[0].shape[0]
    vmem = pl.BlockSpec(memory_space=pltpu.VMEM)

    def kernel(*refs):
        pick_kernel(len(pieces), *refs)

    return pl.pallas_call(
        kernel,
        in_specs=[pl.BlockSpec(memory_space=pltpu.SMEM)] + [vmem] * len(pieces),
        out_specs=[vmem] * (count + 1),
        out_shape=[jax.ShapeDtypeStruct((depth, pieces[0].shape[1]), LOW)]
        + [jax.ShapeDtypeStruct((depth, depth), LOW)] * count,
        name="pick",
    )(numbers, *pieces)


def newton_kernel(at, numbers, *refs):
    left = refs[-1]
    bounds = numbers[LOW_LANE], numbers[HIGH_LANE]
    blocks = [kept_lanes(ref[...], *bounds) for ref in refs[:-1]]
    left[...] = newton_rows(blocks, numbers[OFFSET] if at is None else at, left.shape[0])


def newton(at, numbers, blocks, rows):
    vmem = pl.BlockSpec(memory_space=pltpu.VMEM)

    def kernel(*refs):
        newton_kernel(at, *refs)

    return pl.pallas_call(
        kernel,
        in_specs=[pl.BlockSpec(memory_space=pltpu.SMEM)] + [vmem] * len(blocks),
        out_specs=vmem,
        out_shape=jax.ShapeDtypeStruct((tall_of(rows), blocks[0].shape[0]), F32),
        compiler_params=pltpu.CompilerParams(vmem_limit_bytes=VMEM_LIMIT),
        cost_estimate=pl.CostEstimate(
            flops=9_000_000_000, bytes_accessed=2_000_000, transcendentals=10
        ),
        name="newton",
    )(numbers, *blocks)


def finish_kernel(heights, lanes, numbers, columns, *refs):
    count = len(heights)
    store = refs[-1]
    news = refs[-1 - 2 * count : -1]
    olds = refs[-1 - 3 * count : -1 - 2 * count]
    lefts = refs[: -1 - 3 * count]
    for n, left in enumerate(lefts):
        store[n] = left[...]
    for n in range(count):
        wide = -(-olds[n].shape[1] // SUB) * SUB
        own = columns[:, lanes[n] : lanes[n] + wide]
        result = stepped(store[numbers[WHICH + n]], own, heights[n], olds[n][...])
        news[2 * n][...] = result
        news[2 * n + 1][...] = result.astype(LOW)


def finish(heights, lanes, numbers, columns, lefts, olds):
    vmem = pl.BlockSpec(memory_space=pltpu.VMEM)
    count = len(olds)

    def kernel(*refs):
        finish_kernel(heights, lanes, *refs)

    outs = pl.pallas_call(
        kernel,
        in_specs=[pl.BlockSpec(memory_space=pltpu.SMEM)] + [vmem] * (1 + len(lefts) + count),
        out_specs=[vmem] * (2 * count),
        out_shape=[
            jax.ShapeDtypeStruct(old.shape, kind) for old in olds for kind in (F32, LOW)
        ],
        scratch_shapes=[pltpu.VMEM((len(lefts), *lefts[0].shape), F32)],
        compiler_params=pltpu.CompilerParams(vmem_limit_bytes=VMEM_LIMIT),
        cost_estimate=pl.CostEstimate(
            flops=200_000_000, bytes_accessed=2_000_000, transcendentals=0
        ),
        name="finish",
    )(numbers, columns, *lefts, *olds)
    return [(outs[2 * n], outs[2 * n + 1]) for n in range(count)]


def exchange(x, axis, mask):
    size = lax.axis_size(axis)
    return lax.ppermute(x, axis, [(i, i ^ mask) for i in range(size)])


def place_masks(size):
    masks = [0]
    bit = size // 2
    while bit >= 1:
        masks = masks + [m ^ bit for m in masks]
        bit //= 2
    return masks


def from_columns(own):
    size = lax.axis_size("dp")
    sent = jnp.broadcast_to(own[None], (size, *own.shape))
    return lax.all_to_all(sent, "dp", split_axis=0, concat_axis=0, tiled=True)


def over_columns(own):
    return from_columns(own).reshape(-1, own.shape[1])


def device_numbers(dp, ns, share, width, proj_rows):
    masks = place_masks(ns)
    tasks = [(0, 0, width), (width // SUB, 0, width)]
    tasks += [(width // SUB + 1, 2 * SUB, 2 * SUB + proj_rows)] * (ns - 2)
    table = np.zeros((dp * ns, 24), np.int32)
    for device in range(dp * ns):
        column, index = device // ns, device % ns
        row = table[device]
        for n in range(ns):
            row[OWNERS + n] = index ^ masks[n]
            row[PLACES + (index ^ masks[n])] = n
            row[STARTS + n] = tasks[index ^ n][0]
        for n in range(3):
            row[WHICH + n] = index ^ n
        row[OFFSET] = column * share
        row[COLUMN] = column
        row[LOW_LANE], row[HIGH_LANE] = tasks[index][1:]
    return table


def over_rows(own):
    held = [own]
    bit = lax.axis_size("ns") // 2
    while bit >= 1:
        held = held + [exchange(block, "ns", bit) for block in held]
        bit //= 2
    return held


def added(keep, got):
    return (keep.astype(F32) + got.astype(F32)).astype(LOW)


def sum_columns(pieces):
    return summed(lax.all_to_all(pieces, "dp", split_axis=0, concat_axis=0, tiled=True))


def summed(pieces):
    return jnp.sum(pieces.astype(F32), axis=0)


def columns_direct(own):
    devices = lax.axis_size("dp")
    if devices > 8 or own.shape[0] % 16:
        return [over_columns(own)], None
    return [own] + [exchange(own, "dp", mask) for mask in range(1, devices)], 0


def widened(arrays, lanes):
    joined = jnp.concatenate(arrays, axis=1)
    return jnp.pad(joined, ((0, 0), (0, lanes - joined.shape[1])))


def per_device(
    tokens,
    cotangent,
    segment,
    valid_rows,
    qkv_weight,
    proj_weight,
    fc1_weight,
    fc2_weight,
    qkv_moment,
    proj_moment,
    fc1_moment,
    fc2_moment,
    vectors,
    vector_moment,
    vector_square,
):
    rows, width = tokens.shape
    ns = lax.axis_size("ns")
    qkv_w, proj_w, fc1_w, fc2_w = (w.T for w in (qkv_weight, proj_weight, fc1_weight, fc2_weight))
    qkv_m, proj_m, fc1_m, fc2_m = (w.T for w in (qkv_moment, proj_moment, fc1_moment, fc2_moment))
    share, count = qkv_w.shape
    vec_rows = vectors.shape[0]
    first_lanes = width
    later_lanes = 2 * width + SUB

    table = device_numbers(lax.axis_size("dp"), ns, share, width, proj_w.shape[1])
    device = lax.axis_index("dp") * ns + lax.axis_index("ns")
    numbers = lax.dynamic_slice(jnp.asarray(table), (device, 0), (1, table.shape[1]))[0]

    row_ids = jnp.where(
        valid_rows > 0, segment, rows + jnp.arange(rows, dtype=jnp.int32)
    ).astype(F32)
    ids = jnp.pad(row_ids, (MARGIN, MARGIN), constant_values=-1.0).reshape(-1, SUB)
    ids = jnp.pad(ids, ((0, -ids.shape[0] % 8), (0, 0)), constant_values=-1.0)

    later_own = widened([fc1_w, fc2_w, proj_w], later_lanes).astype(LOW)
    later_pair = jnp.stack([later_own, exchange(later_own, "ns", ns // 2)])
    first_own = widened([qkv_w, vectors.T], first_lanes).astype(LOW)
    first_pieces = over_rows(over_columns(first_own))
    later_near = from_columns(later_pair)
    if share % 16:
        later_near = jnp.moveaxis(later_near, 0, 1).reshape(1, ns // 2, width, later_lanes)

    (query, _, value, key_turned, normed_turned, mixed, probs, weight, vector_full) = (
        attend_forward(numbers, first_pieces, tokens, ids)
    )
    later_near, mixed = lax.optimization_barrier((later_near, mixed))
    later_far = exchange(later_near, "ns", 1)
    output, grad_residual, grad_mixed, inner, grads_near, grads_far, sums = mlp_both(
        numbers, later_near, later_far, vector_full, mixed, tokens, cotangent
    )
    held = added(grads_near, exchange(grads_far, "ns", 1))
    held, grad_mixed = lax.optimization_barrier((held, grad_mixed))
    if share % 16:
        held = jnp.moveaxis(held.reshape(ns // 2, -1, share, later_lanes), 1, 0)
    later_got = lax.all_to_all(held, "dp", split_axis=0, concat_axis=0, tiled=True)

    grad_qkv, grads_near, grads_far = attend_backward(
        numbers, ns, query, key_turned, value, probs, inner, grad_mixed, normed_turned, weight,
        vector_full, sums,
    )
    held = added(grads_near, exchange(grads_far, "ns", 1))
    got = exchange(held[1], "ns", ns // 2)
    input_grad = input_gradient(weight, vector_full, tokens, grad_residual, grad_qkv)
    got, input_grad, later_got = lax.optimization_barrier((got, input_grad, later_got))
    first_held = added(held[0], got)
    first_owned = sum_columns(first_held.reshape(lax.axis_size("dp"), share, first_lanes))

    later_sums = summed(later_got)
    later_owned = later_sums[0] + exchange(later_sums[1].astype(LOW), "ns", ns // 2).astype(F32)
    later_moment = later_owned + 0.5 * widened([fc1_m, fc2_m, proj_m], later_lanes)
    pieces, at = columns_direct(later_moment.astype(LOW))
    columns, *chosen = pick(numbers, pieces, ns)
    blocks = [chosen[0]] + [exchange(chosen[mask], "ns", mask) for mask in range(1, ns)]
    left = newton(at, numbers, blocks, share)

    first_moment = first_owned + 0.5 * widened([qkv_m], first_lanes)
    first_own = over_columns(first_moment.astype(LOW))
    first_far = exchange(first_own, "ns", ns // 2)
    left, first_far = lax.optimization_barrier((left, first_far))
    first_pieces = [first_own, first_far]
    first_pieces += [exchange(piece, "ns", 1) for piece in first_pieces]
    qkv_new = muon(count * ns, numbers, first_pieces, qkv_w)

    lefts = [left] + [exchange(left, "ns", mask) for mask in range(1, ns)]
    fc1_new, fc2_new, proj_new = finish(
        [w.shape[1] * ns for w in (fc1_w, fc2_w, proj_w)],
        (0, width, 2 * width),
        numbers,
        columns,
        lefts,
        (fc1_w, fc2_w, proj_w),
    )

    news = (qkv_new, proj_new, fc1_new, fc2_new)
    moments_new = (
        first_moment[:, :count],
        later_moment[:, 2 * width : 2 * width + proj_w.shape[1]],
        later_moment[:, :width],
        later_moment[:, width : 2 * width],
    )

    vector_grad = first_owned[:, count : count + vec_rows].T
    first_new = BETA_ONE * vector_moment + (1.0 - BETA_ONE) * vector_grad
    second_new = BETA_TWO * vector_square + (1.0 - BETA_TWO) * vector_grad * vector_grad
    first_hat = first_new / (1.0 - BETA_ONE**STEP)
    second_hat = second_new / (1.0 - BETA_TWO**STEP)
    vectors_new = vectors - ADAM_RATE * first_hat / (jnp.sqrt(second_hat) + ADAM_EPS)
    return (
        output,
        input_grad,
        *(new[0].T for new in news),
        *(m.T for m in moments_new),
        first_new,
        second_new,
        vectors_new,
        *(new[1].T for new in news),
    )


def solution(mesh):
    rows = P(("dp", "ns"), None)
    flat = P(("dp", "ns"))
    block = P("ns", "dp")
    return jax.shard_map(
        per_device,
        mesh=mesh,
        in_specs=(rows, rows, flat, flat) + (block,) * 11,
        out_specs=(rows, rows) + (block,) * 15,
        check_vma=False,
    )
```

```python
import functools
import math

import jax
import jax.numpy as jnp
import numpy as np
from jax import lax
from jax.experimental import pallas as pl
from jax.experimental.pallas import tpu as pltpu
from jax.sharding import PartitionSpec as P

HEADS = 6
PAIRS = 3
MARGIN = 128
NS_STEPS = 5
STEP = 10
TILE = 512
MLP_TILE = 512
FF_CHUNK = 256
SUB = 128
SPAN = 384
VEC_LANES = 16
GROUP = 2


EPS_NORM = 1e-06
NEWTON_A = 3.4445
NEWTON_B = -4.775
NEWTON_C = 2.0315
MUON_RATE = 0.2
MUON_DECAY = 0.1
ADAM_RATE = 0.4
BETA_ONE = 0.9
BETA_TWO = 0.999
ADAM_EPS = 1e-08
LOW = jnp.bfloat16
F32 = jnp.float32
TN = (((0,), (0,)), ((), ()))
NT = (((1,), (1,)), ((), ()))
NN = (((1,), (0,)), ((), ()))
VMEM_LIMIT = 56 * 1024 * 1024
ERF_P = 0.3275911
ERF_COEFS = (0.254829592, -0.284496736, 1.421413741, -1.453152027, 1.061405429)


def dot(left, right, dims=NN):
    return lax.dot_general(left, right, dims, preferred_element_type=F32)


PLACES, OWNERS, STARTS, WHICH, OFFSET, LOW_LANE, HIGH_LANE, COLUMN = 0, 4, 8, 12, 16, 17, 18, 19


def lane_numbers(shape):
    return lax.broadcasted_iota(jnp.int32, shape, len(shape) - 1)


def norm_parts(value):
    center = value - jnp.mean(value, axis=-1, keepdims=True)
    rate = lax.rsqrt(jnp.mean(center * center, axis=-1, keepdims=True) + EPS_NORM)
    return center * rate, rate


def norm_back(grad, normed, rate, gain):
    scaled = grad * gain
    first = jnp.mean(scaled, axis=-1, keepdims=True)
    second = jnp.mean(scaled * normed, axis=-1, keepdims=True)
    return rate * (scaled - first - normed * second)


def gelu_both(value):
    below = 1.0 + (ERF_P * 0.5**0.5) * jnp.abs(value)
    ratio = pl.reciprocal(below, approx=True)
    ratio = ratio * (2.0 - below * ratio)
    decay = jnp.exp2((value * value) * (-0.5 * math.log2(math.e)))
    poly = 0.5 * ERF_COEFS[4]
    for coef in ERF_COEFS[3::-1]:
        poly = poly * ratio + 0.5 * coef
    tail = poly * ratio * decay
    phi = jnp.where(value >= 0, 1.0 - tail, tail)
    return value * phi, phi + (value * (1.0 / math.sqrt(2.0 * math.pi))) * decay


def gelu_rows(hidden, bias, grad, between):
    active, back = [], []
    rows = hidden.shape[0]
    pieces = rows // 16
    for n in range(pieces):
        if n * len(between) // pieces != (n - 1) * len(between) // pieces:
            between[n * len(between) // pieces]()
        here = slice(n * 16, (n + 1) * 16)
        value, slope = gelu_both(hidden[here] + bias)
        active.append(value.astype(LOW))
        back.append((grad[here] * slope).astype(LOW))
    return jnp.concatenate(active, axis=0), jnp.concatenate(back, axis=0)


def halves_of(lanes):
    half = lanes.shape[0] // 2
    return lanes[:half, :SUB], lanes[half:, SUB:]


def staged(count, first, second, third):
    made = first(0)
    kept = None
    for n in range(count):
        coming = first(n + 1) if n + 1 < count else None
        if kept is not None:
            third(n - 1, kept)
        kept = second(n, made)
        made = coming
    third(count - 1, kept)


def both_heads(pair):
    first = (lane_numbers((1, SUB)) < SUB // 2).astype(F32).astype(pair.dtype)
    second = (lane_numbers((1, SUB)) >= SUB // 2).astype(F32).astype(pair.dtype)
    return jnp.concatenate([pair * first, pair * second], axis=0)


def fetch(pairs, sems):
    copies = [
        pltpu.make_async_copy(source, target, sems.at[n])
        for n, (source, target) in enumerate(pairs)
    ]
    for copy in copies:
        copy.start()
    for copy in copies:
        copy.wait()


def prepare_kernel(tokens, cotangent, ids, normed, normed_turned, out_turned, columns, sums):
    step = pl.program_id(0)
    parts = columns.shape[0] // SUB

    @pl.when(step == 0)
    def clear():
        sums[...] = jnp.zeros(sums.shape, F32)
        for number in range(parts):
            row = jnp.broadcast_to(ids[number : number + 1, :], (SUB, SUB))
            columns[number * SUB : (number + 1) * SUB, :] = row.T

    value, _ = norm_parts(tokens[...].astype(F32))
    normed[...] = value
    normed_turned[...] = value.astype(LOW).T
    out_low = cotangent[...]
    out_turned[...] = out_low.T
    sums[0:1, :] += jnp.sum(out_low.astype(F32), axis=0, keepdims=True)


def prepare(tokens, cotangent, ids):
    rows, width = tokens.shape
    padded = rows + 2 * MARGIN
    tile = pl.BlockSpec((TILE, width), lambda s: (s, 0))
    turned = pl.BlockSpec((width, TILE), lambda s: (0, s))
    whole = lambda *dims: pl.BlockSpec(dims, lambda s: (0,) * len(dims))
    return pl.pallas_call(
        prepare_kernel,
        grid=(rows // TILE,),
        in_specs=[tile, tile, whole(*ids.shape)],
        out_specs=[tile, turned, turned, whole(padded, SUB), whole(8, width)],
        out_shape=[
            jax.ShapeDtypeStruct((rows, width), F32),
            jax.ShapeDtypeStruct((width, rows), LOW),
            jax.ShapeDtypeStruct((width, rows), LOW),
            jax.ShapeDtypeStruct((padded, SUB), F32),
            jax.ShapeDtypeStruct((8, width), F32),
        ],
        compiler_params=pltpu.CompilerParams(vmem_limit_bytes=VMEM_LIMIT),
        cost_estimate=pl.CostEstimate(
            flops=20_000_000, bytes_accessed=12_000_000, transcendentals=2048
        ),
        name="prepare",
    )(tokens, cotangent, ids)


def attend_kernel(numbers, *refs):
    (normed, ids, columns, query, key, value, key_turned, mixed, probs, weight, vectors,
     gathered, pair_weight, value_turned, shifts, sems) = refs[-16:]
    pieces = refs[:-16]
    step = pl.program_id(0)
    chunks = pl.num_programs(0) - 1
    width = normed.shape[1]
    parts = len(pieces)
    block = 3 * width // parts
    rows_each = 12 // parts

    @pl.when(step == 0)
    def assemble():
        fetch([(piece, gathered.at[n]) for n, piece in enumerate(pieces)], sems)
        total = jnp.zeros((width, 3 * width), F32)
        turned = jnp.zeros((width, SUB), F32)
        for number in range(parts):
            piece = gathered[numbers[PLACES + number]].astype(F32)
            kept = jnp.where(lane_numbers(piece.shape) < block, piece, 0.0)
            wide = jnp.concatenate([kept, jnp.zeros((width, 2 * width), F32)], axis=1)
            total = total + (pltpu.roll(wide, block * number, 1) if number else wide)
            last = piece[:, 2 * SUB :]
            at = block - 2 * SUB
            lane = lane_numbers(last.shape)
            vec = jnp.where((lane >= at) & (lane < at + rows_each), last, 0.0)
            turned = turned + pltpu.roll(vec, (rows_each * number - at) % SUB, 1)
        total = total.astype(LOW)
        weight[...] = total
        pair_weight[...] = total[:, width:].T
        vectors[...] = turned.T[:VEC_LANES]
        shifts[...] = turned
        edges = (pl.ds(0, MARGIN), pl.ds(MARGIN + chunks * TILE, MARGIN))
        for edge in edges:
            for ref in (query, key, value):
                ref[edge, :] = jnp.zeros((MARGIN, width), LOW)
            for ref in (key_turned, value_turned):
                ref[:, edge] = jnp.zeros((width, MARGIN), LOW)

    @pl.when(step < chunks)
    def project():
        first_in = (normed[...] * vectors[0:1, :] + vectors[1:2, :]).astype(LOW)
        result = dot(first_in, weight[...])
        turned = dot(pair_weight[...], first_in, NT)
        here = pl.ds(pl.multiple_of(MARGIN + step * TILE, SUB), TILE)
        scale = (width // HEADS) ** (-0.5)
        made = (result[:, :width] + vectors[2:3, :]).astype(LOW) * jnp.asarray(scale, LOW)
        query[here, :] = made
        key[here, :] = result[:, width : 2 * width].astype(LOW)
        value[here, :] = (result[:, 2 * width :] + vectors[3:4, :]).astype(LOW)
        key_turned[:, here] = turned[:width].astype(LOW)
        value_turned[:, here] = (turned[width:] + shifts[:, 3:4]).astype(LOW)

    @pl.when(step > 0)
    def attend():
        def place(number):
            sub, pair = number // PAIRS, number % PAIRS
            tile = (step - 1) * (TILE // SUB) + sub
            start = pl.multiple_of(tile * SUB, SUB)
            return sub, pair, tile, start, pl.ds(start, SPAN), pl.ds(pair * SUB, SUB)

        def of_group(group):
            return range(group * GROUP, (group + 1) * GROUP)

        def score(group):
            made = []
            for number in of_group(group):
                _, _, _, start, near_rows, heads = place(number)
                wanted = both_heads(query[pl.ds(start + MARGIN, SUB), heads])
                made.append(dot(key[near_rows, heads], wanted, NT))
            return made

        def soften(group, made):
            own = []
            for number, scores in zip(of_group(group), made):
                _, _, tile, _, near_rows, _ = place(number)
                same = columns[near_rows, :] == ids[pl.ds(tile + 1, 1), :]
                own += [
                    jnp.where(same, scores[:, head * SUB : (head + 1) * SUB], -1e30)
                    for head in range(2)
                ]
            largest = [jnp.max(part, axis=0, keepdims=True) for part in own]
            expo = [jnp.exp(part - most) for part, most in zip(own, largest)]
            share = [1.0 / jnp.sum(part, axis=0, keepdims=True) for part in expo]
            scaled = [(part * by).astype(LOW) for part, by in zip(expo, share)]
            result = []
            for n, number in enumerate(of_group(group)):
                sub, pair, _, _, _, _ = place(number)
                result.append(jnp.concatenate(scaled[2 * n : 2 * n + 2], axis=1))
                probs[pair, sub] = result[-1]
            return result

        def mix(group, kept):
            for number, prob in zip(of_group(group), kept):
                sub, _, _, _, near_rows, heads = place(number)
                first, second = halves_of(dot(value_turned[heads, near_rows], prob))
                turned = jnp.concatenate([first, second], axis=0).astype(LOW)
                mixed[pl.ds(sub * SUB, SUB), heads] = turned.T

        staged(TILE // SUB * PAIRS // GROUP, score, soften, mix)


def attend_forward(numbers, pieces, normed, ids, columns):
    rows, width = normed.shape
    chunks = rows // TILE
    tiles = TILE // SUB
    parts = len(pieces)
    now = lambda s: jnp.minimum(s, chunks - 1)
    before = lambda s: jnp.maximum(s - 1, 0)
    whole = lambda *dims: pl.BlockSpec(dims, lambda s, *_: (0,) * len(dims))
    padded = rows + 2 * MARGIN
    return pl.pallas_call(
        attend_kernel,
        grid_spec=pltpu.PrefetchScalarGridSpec(
            num_scalar_prefetch=1,
            grid=(chunks + 1,),
            in_specs=[pl.BlockSpec(memory_space=pl.ANY)] * parts
            + [
                pl.BlockSpec((TILE, width), lambda s, *_: (now(s), 0)),
                whole(*ids.shape),
                whole(*columns.shape),
            ],
            out_specs=[
                whole(padded, width),
                whole(padded, width),
                whole(padded, width),
                whole(width, padded),
                pl.BlockSpec((TILE, width), lambda s, *_: (before(s), 0)),
                pl.BlockSpec((PAIRS, tiles, SPAN, 2 * SUB), lambda s, *_: (0, before(s), 0, 0)),
                whole(width, 3 * width),
                whole(VEC_LANES, width),
            ],
            scratch_shapes=[
                pltpu.VMEM((parts, *pieces[0].shape), LOW),
                pltpu.VMEM((2 * width, width), LOW),
                pltpu.VMEM((width, padded), LOW),
                pltpu.VMEM((width, SUB), F32),
                pltpu.SemaphoreType.DMA((parts,)),
            ],
        ),
        out_shape=[
            jax.ShapeDtypeStruct((padded, width), LOW),
            jax.ShapeDtypeStruct((padded, width), LOW),
            jax.ShapeDtypeStruct((padded, width), LOW),
            jax.ShapeDtypeStruct((width, padded), LOW),
            jax.ShapeDtypeStruct((rows, width), LOW),
            jax.ShapeDtypeStruct((PAIRS, rows // SUB, SPAN, 2 * SUB), LOW),
            jax.ShapeDtypeStruct((width, 3 * width), LOW),
            jax.ShapeDtypeStruct((VEC_LANES, width), F32),
        ],
        compiler_params=pltpu.CompilerParams(vmem_limit_bytes=VMEM_LIMIT),
        cost_estimate=pl.CostEstimate(
            flops=12_000_000_000, bytes_accessed=22_000_000, transcendentals=5_000_000
        ),
        name="attend_forward",
    )(numbers, *pieces, normed, ids, columns)


def mlp_kernel(numbers, near, far, *refs):
    (vectors, mixed, tokens, cotangent, out_turned, out_sums, output, grad_residual, grad_mixed, inner, grads_near,
     grads_far, sums, one, two, proj_parts, proj, acc_one, acc_two, acc_proj, bias
    ) = refs
    step = pl.program_id(0)
    width = tokens.shape[1]
    mid = near.shape[1]
    parts = mid + far.shape[1]
    block = width // parts
    last_at = 2 * width
    hidden_width = one.shape[1]

    @pl.when(step == 0)
    def assemble():
        for part in range(parts):
            ref, at = (near, part) if part < mid else (far, part - mid)
            lanes = pl.ds(part * width, width)
            for group in range(near.shape[0]):
                here = pl.ds(group * near.shape[2], near.shape[2])
                one[here, lanes] = ref[group, at, :, :width]
                two[here, lanes] = ref[group, at, :, width:last_at]
                proj_parts[part, here, :] = ref[group, at, :, last_at:]
        total = jnp.zeros((width, width), F32)
        for number in range(parts):
            piece = proj_parts[numbers[PLACES + number]].astype(F32)
            kept = jnp.where(lane_numbers(piece.shape) < block, piece, 0.0)
            wide = jnp.concatenate([kept, jnp.zeros((width, width - SUB), F32)], axis=1)
            total = total + (pltpu.roll(wide, block * number, 1) if number else wide)
        proj[...] = total.astype(LOW)
        for part in range(parts):
            row = vectors[pl.ds(8 + numbers[OWNERS + part], 1), :]
            bias[0:1, part * width : (part + 1) * width] = row
        acc_one[...] = jnp.zeros(acc_one.shape, F32)
        acc_two[...] = jnp.zeros(acc_two.shape, F32)
        acc_proj[...] = jnp.zeros(acc_proj.shape, F32)
        sums[...] = jnp.zeros(sums.shape, F32)
        sums[7:8, :] = out_sums[0:1, :]

    def add_row(row, values):
        sums[pl.ds(row, 1), :] += jnp.sum(values, axis=0, keepdims=True)

    own = mixed[...]
    residual = tokens[...].astype(F32) + dot(own, proj[...], NT) + vectors[4:5, :]
    normed, rate = norm_parts(residual)
    gain = vectors[5:6, :]
    second_in = (normed * gain + vectors[6:7, :]).astype(LOW)
    out_low = cotangent[...]
    grad_out = out_low.astype(F32)
    second_turned = second_in.T
    out_turned = out_turned[...]
    totals = [residual + vectors[7:8, :], jnp.zeros(residual.shape, F32)]

    count = hidden_width // FF_CHUNK
    ones = jnp.ones((16, MLP_TILE), LOW)
    second_and_ones = jnp.concatenate([second_turned, ones], axis=0)
    hiddens, slopes, kept = {}, {}, {}

    def lanes_of(number):
        return pl.ds(number * FF_CHUNK, FF_CHUNK)

    def make_hidden(number):
        hiddens[number] = dot(second_in, one[:, lanes_of(number)])

    def make_slope(number):
        slopes[number] = dot(out_low, two[:, lanes_of(number)])

    def add_one(number):
        acc_one[:, lanes_of(number)] += dot(second_and_ones, kept[number][1])

    def add_two(number):
        acc_two[:, lanes_of(number)] += dot(out_turned, kept[number][0])

    def add_result(number):
        totals[0] = totals[0] + dot(kept[number][0], two[:, lanes_of(number)], NT)

    def add_second(number):
        totals[1] = totals[1] + dot(kept[number][1], one[:, lanes_of(number)], NT)

    make_hidden(0)
    make_slope(0)
    for number in range(count):
        between = []
        if number + 1 < count:
            between += [functools.partial(f, number + 1) for f in (make_hidden, make_slope)]
        if number > 0:
            between += [
                functools.partial(f, number - 1)
                for f in (add_result, add_second, add_one, add_two)
            ]
        kept[number] = gelu_rows(
            hiddens.pop(number), bias[0:1, lanes_of(number)], slopes.pop(number), between
        )
    for f in (add_result, add_second, add_one, add_two):
        f(count - 1)
    result, grad_second = totals
    output[...] = result.astype(LOW)
    add_row(5, grad_second * normed)
    add_row(6, grad_second)
    grad_res = grad_out + norm_back(grad_second, normed, rate, gain)
    grad_residual[...] = grad_res
    branch = grad_res.astype(LOW)
    add_row(4, branch.astype(F32))
    acc_proj[...] += dot(branch.T, own)
    grad_own = dot(branch, proj[...]).astype(LOW)
    grad_mixed[...] = grad_own
    high, rest = halves(grad_own.astype(F32) * own.astype(F32))
    head = lax.broadcasted_iota(jnp.int32, (16, width), 0)
    chosen = (lane_numbers((16, width)) // (width // HEADS) == head).astype(F32).astype(LOW)
    inner[...] = (dot(chosen, high, NT) + dot(chosen, rest, NT))[:8]

    @pl.when(step == pl.num_programs(0) - 1)
    def finish():
        total = acc_proj[...]
        for number in range(parts):
            turned = pltpu.roll(total, (width - block * number) % width, 1) if number else total
            proj_parts[numbers[PLACES + number]] = turned[:, :SUB].astype(LOW)
        for part in range(parts):
            ref, at = (grads_near, part) if part < mid else (grads_far, part - mid)
            lanes = pl.ds(part * width, width)
            for group in range(ref.shape[0]):
                here = pl.ds(group * ref.shape[2], ref.shape[2])
                ref[group, at, :, :width] = acc_one[here, lanes].astype(LOW)
                ref[group, at, :, width:last_at] = acc_two[here, lanes].astype(LOW)
                ref[group, at, :, last_at:] = proj_parts[part, here, :]
            sums[pl.ds(8 + numbers[OWNERS + part], 1), :] = acc_one[width : width + 1, lanes]


def mlp_both(numbers, near, far, vectors, mixed, tokens, cotangent, out_turned, out_sums):
    rows, width = tokens.shape
    parts = near.shape[1] + far.shape[1]
    hidden_width = parts * width
    tile = pl.BlockSpec((MLP_TILE, width), lambda s, *_: (s, 0))
    whole = lambda *dims: pl.BlockSpec(dims, lambda s, *_: (0,) * len(dims))
    return pl.pallas_call(
        mlp_kernel,
        grid_spec=pltpu.PrefetchScalarGridSpec(
            num_scalar_prefetch=1,
            grid=(rows // MLP_TILE,),
            in_specs=[
                whole(*near.shape), whole(*far.shape), whole(*vectors.shape), tile, tile, tile,
                pl.BlockSpec((width, MLP_TILE), lambda s, *_: (0, s)), whole(*out_sums.shape),
            ],
            out_specs=[
                tile,
                tile,
                tile,
                pl.BlockSpec((8, MLP_TILE), lambda s, *_: (0, s)),
                whole(*near.shape),
                whole(*far.shape),
                whole(*vectors.shape),
            ],
            scratch_shapes=[
                pltpu.VMEM((width, hidden_width), LOW),
                pltpu.VMEM((width, hidden_width), LOW),
                pltpu.VMEM((parts, width, SUB), LOW),
                pltpu.VMEM((width, width), LOW),
                pltpu.VMEM((width + 16, hidden_width), F32),
                pltpu.VMEM((width, hidden_width), F32),
                pltpu.VMEM((width, width), F32),
                pltpu.VMEM((8, hidden_width), F32),
            ],
        ),
        out_shape=[
            jax.ShapeDtypeStruct((rows, width), LOW),
            jax.ShapeDtypeStruct((rows, width), F32),
            jax.ShapeDtypeStruct((rows, width), LOW),
            jax.ShapeDtypeStruct((8, rows), F32),
            jax.ShapeDtypeStruct(near.shape, LOW),
            jax.ShapeDtypeStruct(far.shape, LOW),
            jax.ShapeDtypeStruct(vectors.shape, F32),
        ],
        compiler_params=pltpu.CompilerParams(vmem_limit_bytes=VMEM_LIMIT),
        cost_estimate=pl.CostEstimate(
            flops=34_000_000_000, bytes_accessed=20_000_000, transcendentals=6_000_000
        ),
        name="mlp_both",
    )(numbers, near, far, vectors, mixed, tokens, cotangent, out_turned, out_sums)


def attend_back_kernel(
    numbers,
    query,
    key_turned,
    value,
    probs,
    inner,
    grad_mixed,
    normed_turned,
    weight,
    vectors,
    sums,
    grad_qkv,
    near,
    far,
    grad_query,
    acc_key,
    acc_value,
    acc_sums,
    normed_sums,
    blocks,
    rows,
):
    step = pl.program_id(0)
    chunks = pl.num_programs(0) - 1
    pairs = range(PAIRS)
    count = len(pairs)
    scale = (SUB // 2) ** (-0.5)

    @pl.when(step == 0)
    def clear():
        acc_key[...] = jnp.zeros(acc_key.shape, F32)
        acc_value[...] = jnp.zeros(acc_value.shape, F32)
        normed_sums[...] = jnp.zeros(normed_sums.shape, F32)
        acc_sums[...] = jnp.zeros(acc_sums.shape, F32)

    @pl.when(step < chunks)
    def attend():
        def place(number):
            sub, at = number // count, number % count
            start = pl.multiple_of((step * (TILE // SUB) + sub) * SUB, SUB)
            return sub, at, start, pl.ds(start, SPAN), pl.ds(at * SUB, SUB)

        def slope(number):
            sub, _, _, near_rows, heads = place(number)
            grad = both_heads(grad_mixed[pl.ds(sub * SUB, SUB), heads])
            return dot(value[near_rows, heads], grad, NT)

        def soften(number, slopes):
            sub, at, _, _, _ = place(number)
            pair = pairs[at]
            cols = pl.ds(sub * SUB, SUB)
            both = []
            for head in range(2):
                lanes = slice(head * SUB, (head + 1) * SUB)
                less = slopes[:, lanes] - inner[2 * pair + head : 2 * pair + head + 1, cols]
                both.append((probs[at, sub, :, lanes].astype(F32) * less).astype(LOW))
            return jnp.concatenate(both, axis=1)

        def collect(number, scores):
            sub, at, start, near_rows, heads = place(number)
            first, second = halves_of(dot(key_turned[heads, near_rows], scores))
            turned = (jnp.concatenate([first, second], axis=0) * scale).astype(LOW)
            grad_query[pl.ds(start, SUB), heads] = turned.T
            wanted = both_heads(query[pl.ds(start + MARGIN, SUB), heads])
            acc_key[near_rows, heads] += dot(scores, wanted)
            grad = both_heads(grad_mixed[pl.ds(sub * SUB, SUB), heads])
            acc_value[near_rows, heads] += dot(probs[at, sub], grad)

        staged(TILE // SUB * count, slope, soften, collect)

    @pl.when(step > 0)
    def collect():
        here = pl.ds(pl.multiple_of((step - 1) * TILE, SUB), TILE)
        there = pl.ds(pl.multiple_of((step - 1) * TILE + MARGIN, SUB), TILE)
        parts = (
            grad_query[here, :],
            acc_key[there, :].astype(LOW),
            acc_value[there, :].astype(LOW),
        )
        joined = jnp.concatenate(parts, axis=1)
        grad_qkv[...] = joined
        normed_sums[...] += dot(normed_turned[...], joined)
        acc_sums[0:1, :] += jnp.sum(joined.astype(F32), axis=0, keepdims=True)

    @pl.when(step == chunks)
    def finish():
        weight_grad(
            numbers, normed_sums[...], acc_sums[0:1, :], weight, vectors, sums, near, far, blocks, rows
        )


def weight_grad(numbers, total, columns, weight, vectors, sums, near, far, blocks, rows):
    width = weight.shape[0]
    parts, mid = blocks.shape[0], near.shape[0]
    block = 3 * width // parts
    rows_each = 12 // parts
    wide = weight[...].astype(F32)
    grad_gain = jnp.sum(total * wide, axis=1, keepdims=True)
    grad_shift = jnp.sum(wide * columns, axis=1, keepdims=True)
    rows[...] = jnp.zeros(rows.shape, F32)
    rows[0:VEC_LANES, :] = sums[...]
    rows[2:3, :] = columns[:, :width]
    rows[3:4, :] = columns[:, 2 * width :]
    rows[VEC_LANES : 2 * VEC_LANES, :] = vectors[...]
    turned = rows[...].T
    gain = turned[:, VEC_LANES : VEC_LANES + 1]
    shift = turned[:, VEC_LANES + 1 : VEC_LANES + 2]
    lane = lane_numbers(turned.shape)
    turned = jnp.where(lane == 0, grad_gain, jnp.where(lane == 1, grad_shift, turned))
    total = total * gain + shift * columns
    at = block - 2 * SUB
    for number in range(parts):
        away = (3 * width - block * number) % (3 * width)
        piece = (pltpu.roll(total, away, 1) if number else total)[:, :width]
        vec = pltpu.roll(turned, (at - rows_each * number) % SUB, 1)
        last = jnp.where(lane < at, piece[:, 2 * SUB :], 0.0)
        last = jnp.where((lane >= at) & (lane < at + rows_each), vec, last)
        at_place = numbers[PLACES + number]
        blocks[at_place, :, : 2 * SUB] = piece[:, : 2 * SUB].astype(LOW)
        blocks[at_place, :, 2 * SUB :] = last.astype(LOW)
    near[...] = blocks[:mid]
    far[...] = blocks[mid:]


def attend_backward(
    numbers, parts, query, key_turned, value, probs, inner, grad_mixed, normed_turned, weight,
    vectors, sums,
):
    width, rows = normed_turned.shape
    padded = query.shape[0]
    chunks = rows // TILE
    tiles = TILE // SUB
    now = lambda s: jnp.minimum(s, chunks - 1)
    before = lambda s: jnp.maximum(s - 1, 0)
    whole = lambda *dims: pl.BlockSpec(dims, lambda s, *_: (0,) * len(dims))
    half = (parts // 2, width, width)
    return pl.pallas_call(
        attend_back_kernel,
        grid_spec=pltpu.PrefetchScalarGridSpec(
            num_scalar_prefetch=1,
            grid=(chunks + 1,),
            in_specs=[
                whole(padded, width),
                whole(width, padded),
                whole(padded, width),
                pl.BlockSpec((PAIRS, tiles, SPAN, 2 * SUB), lambda s, *_: (0, now(s), 0, 0)),
                pl.BlockSpec((8, TILE), lambda s, *_: (0, now(s))),
                pl.BlockSpec((TILE, width), lambda s, *_: (now(s), 0)),
                pl.BlockSpec((width, TILE), lambda s, *_: (0, before(s))),
                whole(*weight.shape),
                whole(*vectors.shape),
                whole(*sums.shape),
            ],
            out_specs=[
                pl.BlockSpec((TILE, 3 * width), lambda s, *_: (before(s), 0)),
                whole(*half),
                whole(*half),
            ],
            scratch_shapes=[
                pltpu.VMEM((rows, width), LOW),
                pltpu.VMEM((padded, width), F32),
                pltpu.VMEM((padded, width), F32),
                pltpu.VMEM((8, 3 * width), F32),
                pltpu.VMEM((width, 3 * width), F32),
                pltpu.VMEM((parts, width, width), LOW),
                pltpu.VMEM((SUB, width), F32),
            ],
        ),
        out_shape=[
            jax.ShapeDtypeStruct((rows, 3 * width), LOW),
            jax.ShapeDtypeStruct(half, LOW),
            jax.ShapeDtypeStruct(half, LOW),
        ],
        compiler_params=pltpu.CompilerParams(vmem_limit_bytes=VMEM_LIMIT),
        cost_estimate=pl.CostEstimate(
            flops=16_000_000_000, bytes_accessed=24_000_000, transcendentals=0
        ),
        name="attend_backward",
    )(
        numbers, query, key_turned, value, probs, inner, grad_mixed, normed_turned, weight, vectors,
        sums,
    )


def input_grad_kernel(weight, vectors, tokens, grad_residual, grad_qkv, input_grad):
    normed, rate = norm_parts(tokens[...].astype(F32))
    grad_first = dot(grad_qkv[...], weight[...], NT)
    back = norm_back(grad_first, normed, rate, vectors[0:1, :])
    input_grad[...] = (grad_residual[...] + back).astype(LOW)


def input_gradient(weight, vectors, tokens, grad_residual, grad_qkv):
    rows, width = tokens.shape
    size = TILE
    tile = pl.BlockSpec((size, width), lambda s: (s, 0))
    whole = lambda ref: pl.BlockSpec(ref.shape, lambda s: (0, 0))
    return pl.pallas_call(
        input_grad_kernel,
        grid=(rows // size,),
        in_specs=[
            whole(weight), whole(vectors), tile, tile,
            pl.BlockSpec((size, 3 * width), lambda s: (s, 0)),
        ],
        out_specs=tile,
        out_shape=jax.ShapeDtypeStruct((rows, width), LOW),
        compiler_params=pltpu.CompilerParams(vmem_limit_bytes=VMEM_LIMIT),
        cost_estimate=pl.CostEstimate(
            flops=4_000_000_000, bytes_accessed=13_000_000, transcendentals=2048
        ),
        name="input_gradient",
    )(weight, vectors, tokens, grad_residual, grad_qkv)


def halves(value):
    high = value.astype(LOW)
    return high, (value - high.astype(F32)).astype(LOW)


def dot_three(left, right):
    tall = jnp.concatenate([right[0], right[0], right[1]], axis=0)
    return dot(jnp.concatenate([left[0], left[1], left[0]], axis=1), tall)


def newton_rows(blocks, offset, rows):
    gram = dot(blocks[0], blocks[0], NT)
    for part in blocks[1:]:
        gram = gram + dot(part, part, NT)
    depth = gram.shape[0]
    down = lax.broadcasted_iota(jnp.int32, (depth, depth), 0)
    eye = (down == lane_numbers((depth, depth))).astype(F32)
    norm = 1.0 / (jnp.sqrt(jnp.sum(gram * eye, keepdims=True)) + 1e-07)
    gram = gram * (norm * norm)
    place = lax.broadcasted_iota(jnp.int32, (rows, depth), 0) + offset
    left = jnp.where(place == lane_numbers((rows, depth)), norm, 0.0)
    for step in range(NS_STEPS - 1):
        pair = halves(gram)
        poly = halves(NEWTON_A * eye + NEWTON_B * gram + NEWTON_C * dot_three(pair, pair))
        lefts = halves(left)
        both = dot_three([jnp.concatenate([pair[n], lefts[n]], axis=0) for n in range(2)], poly)
        left = both[depth:]
        gram = dot_three(halves(both[:depth]), poly)
    pair = halves(gram)
    once = dot_three(halves(left), pair)
    return NEWTON_A * left + NEWTON_B * once + NEWTON_C * dot_three(halves(once), pair)


def stepped(left, own, height, old):
    high, rest = halves(left)
    ortho = (dot(high, own) + dot(rest, own))[: old.shape[0], : old.shape[1]]
    return old * (1.0 - MUON_RATE * MUON_DECAY) - (MUON_RATE * 0.2 * math.sqrt(height)) * ortho


def kept_lanes(value, low, high):
    lane = lane_numbers(value.shape)
    return jnp.where((lane >= low) & (lane < high), value.astype(F32), 0.0).astype(LOW)


def tall_of(rows):
    return -(-rows // 16) * 16


def muon_kernel(height, numbers, *refs):
    old, new, copy = refs[-3:]
    count = old.shape[1]
    blocks = [kept_lanes(ref[...], 0, count) for ref in refs[:-3]]
    left = newton_rows(blocks, numbers[OFFSET], tall_of(old.shape[0]))
    result = stepped(left, blocks[0], height, old[...])
    new[...] = result
    copy[...] = result.astype(LOW)


def muon(height, numbers, blocks, old):
    vmem = pl.BlockSpec(memory_space=pltpu.VMEM)

    def kernel(*refs):
        muon_kernel(height, *refs)

    return pl.pallas_call(
        kernel,
        in_specs=[pl.BlockSpec(memory_space=pltpu.SMEM)] + [vmem] * (len(blocks) + 1),
        out_specs=[vmem, vmem],
        out_shape=[
            jax.ShapeDtypeStruct(old.shape, F32),
            jax.ShapeDtypeStruct(old.shape, LOW),
        ],
        compiler_params=pltpu.CompilerParams(vmem_limit_bytes=VMEM_LIMIT),
        cost_estimate=pl.CostEstimate(
            flops=9_000_000_000, bytes_accessed=2_000_000, transcendentals=10
        ),
        name="muon",
    )(numbers, *blocks, old)


def pick_kernel(count, numbers, *refs):
    pieces, columns, outs = refs[:count], refs[count], refs[count + 1 :]
    share = pieces[0].shape[0]
    for k, piece in enumerate(pieces):
        columns[k * share : (k + 1) * share, :] = piece[...]
        for n, out in enumerate(outs):
            at = pl.multiple_of(numbers[STARTS + n] * SUB, SUB)
            out[k * share : (k + 1) * share, :] = piece[:, pl.ds(at, out.shape[1])]


def pick(numbers, pieces, count):
    depth = len(pieces) * pieces[0].shape[0]
    vmem = pl.BlockSpec(memory_space=pltpu.VMEM)

    def kernel(*refs):
        pick_kernel(len(pieces), *refs)

    return pl.pallas_call(
        kernel,
        in_specs=[pl.BlockSpec(memory_space=pltpu.SMEM)] + [vmem] * len(pieces),
        out_specs=[vmem] * (count + 1),
        out_shape=[jax.ShapeDtypeStruct((depth, pieces[0].shape[1]), LOW)]
        + [jax.ShapeDtypeStruct((depth, depth), LOW)] * count,
        name="pick",
    )(numbers, *pieces)


def newton_kernel(at, numbers, *refs):
    left = refs[-1]
    bounds = numbers[LOW_LANE], numbers[HIGH_LANE]
    blocks = [kept_lanes(ref[...], *bounds) for ref in refs[:-1]]
    left[...] = newton_rows(blocks, numbers[OFFSET] if at is None else at, left.shape[0])


def newton(at, numbers, blocks, rows):
    vmem = pl.BlockSpec(memory_space=pltpu.VMEM)

    def kernel(*refs):
        newton_kernel(at, *refs)

    return pl.pallas_call(
        kernel,
        in_specs=[pl.BlockSpec(memory_space=pltpu.SMEM)] + [vmem] * len(blocks),
        out_specs=vmem,
        out_shape=jax.ShapeDtypeStruct((tall_of(rows), blocks[0].shape[0]), F32),
        compiler_params=pltpu.CompilerParams(vmem_limit_bytes=VMEM_LIMIT),
        cost_estimate=pl.CostEstimate(
            flops=9_000_000_000, bytes_accessed=2_000_000, transcendentals=10
        ),
        name="newton",
    )(numbers, *blocks)


def finish_kernel(heights, lanes, numbers, columns, *refs):
    count = len(heights)
    store = refs[-1]
    news = refs[-1 - 2 * count : -1]
    olds = refs[-1 - 3 * count : -1 - 2 * count]
    lefts = refs[: -1 - 3 * count]
    for n, left in enumerate(lefts):
        store[n] = left[...]
    for n in range(count):
        wide = -(-olds[n].shape[1] // SUB) * SUB
        own = columns[:, lanes[n] : lanes[n] + wide]
        result = stepped(store[numbers[WHICH + n]], own, heights[n], olds[n][...])
        news[2 * n][...] = result
        news[2 * n + 1][...] = result.astype(LOW)


def finish(heights, lanes, numbers, columns, lefts, olds):
    vmem = pl.BlockSpec(memory_space=pltpu.VMEM)
    count = len(olds)

    def kernel(*refs):
        finish_kernel(heights, lanes, *refs)

    outs = pl.pallas_call(
        kernel,
        in_specs=[pl.BlockSpec(memory_space=pltpu.SMEM)] + [vmem] * (1 + len(lefts) + count),
        out_specs=[vmem] * (2 * count),
        out_shape=[
            jax.ShapeDtypeStruct(old.shape, kind) for old in olds for kind in (F32, LOW)
        ],
        scratch_shapes=[pltpu.VMEM((len(lefts), *lefts[0].shape), F32)],
        compiler_params=pltpu.CompilerParams(vmem_limit_bytes=VMEM_LIMIT),
        cost_estimate=pl.CostEstimate(
            flops=200_000_000, bytes_accessed=2_000_000, transcendentals=0
        ),
        name="finish",
    )(numbers, columns, *lefts, *olds)
    return [(outs[2 * n], outs[2 * n + 1]) for n in range(count)]


def exchange(x, axis, mask):
    size = lax.axis_size(axis)
    return lax.ppermute(x, axis, [(i, i ^ mask) for i in range(size)])


def place_masks(size):
    masks = [0]
    bit = size // 2
    while bit >= 1:
        masks = masks + [m ^ bit for m in masks]
        bit //= 2
    return masks


def from_columns(own):
    size = lax.axis_size("dp")
    sent = jnp.broadcast_to(own[None], (size, *own.shape))
    return lax.all_to_all(sent, "dp", split_axis=0, concat_axis=0, tiled=True)


def over_columns(own):
    return from_columns(own).reshape(-1, own.shape[1])


def device_numbers(dp, ns, share, width, proj_rows):
    masks = place_masks(ns)
    tasks = [(0, 0, width), (width // SUB, 0, width)]
    tasks += [(width // SUB + 1, 2 * SUB, 2 * SUB + proj_rows)] * (ns - 2)
    table = np.zeros((dp * ns, 24), np.int32)
    for device in range(dp * ns):
        column, index = device // ns, device % ns
        row = table[device]
        for n in range(ns):
            row[OWNERS + n] = index ^ masks[n]
            row[PLACES + (index ^ masks[n])] = n
            row[STARTS + n] = tasks[index ^ n][0]
        for n in range(3):
            row[WHICH + n] = index ^ n
        row[OFFSET] = column * share
        row[COLUMN] = column
        row[LOW_LANE], row[HIGH_LANE] = tasks[index][1:]
    return table


def over_rows(own):
    held = [own]
    bit = lax.axis_size("ns") // 2
    while bit >= 1:
        held = held + [exchange(block, "ns", bit) for block in held]
        bit //= 2
    return held


def added(keep, got):
    return (keep.astype(F32) + got.astype(F32)).astype(LOW)


def sum_columns(pieces):
    return summed(lax.all_to_all(pieces, "dp", split_axis=0, concat_axis=0, tiled=True))


def summed(pieces):
    return jnp.sum(pieces.astype(F32), axis=0)


def columns_direct(own):
    devices = lax.axis_size("dp")
    if devices > 8 or own.shape[0] % 16:
        return [over_columns(own)], None
    return [own] + [exchange(own, "dp", mask) for mask in range(1, devices)], 0


def widened(arrays, lanes):
    joined = jnp.concatenate(arrays, axis=1)
    return jnp.pad(joined, ((0, 0), (0, lanes - joined.shape[1])))


def per_device(
    tokens,
    cotangent,
    segment,
    valid_rows,
    qkv_weight,
    proj_weight,
    fc1_weight,
    fc2_weight,
    qkv_moment,
    proj_moment,
    fc1_moment,
    fc2_moment,
    vectors,
    vector_moment,
    vector_square,
):
    rows, width = tokens.shape
    ns = lax.axis_size("ns")
    qkv_w, proj_w, fc1_w, fc2_w = (w.T for w in (qkv_weight, proj_weight, fc1_weight, fc2_weight))
    qkv_m, proj_m, fc1_m, fc2_m = (w.T for w in (qkv_moment, proj_moment, fc1_moment, fc2_moment))
    share, count = qkv_w.shape
    vec_rows = vectors.shape[0]
    first_lanes = width
    later_lanes = 2 * width + SUB

    table = device_numbers(lax.axis_size("dp"), ns, share, width, proj_w.shape[1])
    device = lax.axis_index("dp") * ns + lax.axis_index("ns")
    numbers = lax.dynamic_slice(jnp.asarray(table), (device, 0), (1, table.shape[1]))[0]

    row_ids = jnp.where(
        valid_rows > 0, segment, rows + jnp.arange(rows, dtype=jnp.int32)
    ).astype(F32)
    ids = jnp.pad(row_ids, (MARGIN, MARGIN), constant_values=-1.0).reshape(-1, SUB)
    ids = jnp.pad(ids, ((0, -ids.shape[0] % 8), (0, 0)), constant_values=-1.0)

    later_own = widened([fc1_w, fc2_w, proj_w], later_lanes).astype(LOW)
    later_pair = jnp.stack([later_own, exchange(later_own, "ns", ns // 2)])
    first_own = widened([qkv_w, vectors.T], first_lanes).astype(LOW)
    first_pieces = over_rows(over_columns(first_own))
    later_near = from_columns(later_pair)
    if share % 16:
        later_near = jnp.moveaxis(later_near, 0, 1).reshape(1, ns // 2, width, later_lanes)

    normed, normed_turned, out_turned, columns, out_sums = prepare(tokens, cotangent, ids)
    query, _, value, key_turned, mixed, probs, weight, vector_full = attend_forward(
        numbers, first_pieces, normed, ids, columns
    )
    later_near, mixed = lax.optimization_barrier((later_near, mixed))
    later_far = exchange(later_near, "ns", 1)
    output, grad_residual, grad_mixed, inner, grads_near, grads_far, sums = mlp_both(
        numbers, later_near, later_far, vector_full, mixed, tokens, cotangent, out_turned, out_sums
    )
    held = added(grads_near, exchange(grads_far, "ns", 1))
    held, grad_mixed = lax.optimization_barrier((held, grad_mixed))
    if share % 16:
        held = jnp.moveaxis(held.reshape(ns // 2, -1, share, later_lanes), 1, 0)
    later_got = lax.all_to_all(held, "dp", split_axis=0, concat_axis=0, tiled=True)

    grad_qkv, grads_near, grads_far = attend_backward(
        numbers, ns, query, key_turned, value, probs, inner, grad_mixed, normed_turned, weight,
        vector_full, sums,
    )
    held = added(grads_near, exchange(grads_far, "ns", 1))
    got = exchange(held[1], "ns", ns // 2)
    input_grad = input_gradient(weight, vector_full, tokens, grad_residual, grad_qkv)
    got, input_grad, later_got = lax.optimization_barrier((got, input_grad, later_got))
    first_held = added(held[0], got)
    first_owned = sum_columns(first_held.reshape(lax.axis_size("dp"), share, first_lanes))

    later_sums = summed(later_got)
    later_owned = later_sums[0] + exchange(later_sums[1].astype(LOW), "ns", ns // 2).astype(F32)
    later_moment = later_owned + 0.5 * widened([fc1_m, fc2_m, proj_m], later_lanes)
    pieces, at = columns_direct(later_moment.astype(LOW))
    columns, *chosen = pick(numbers, pieces, ns)
    blocks = [chosen[0]] + [exchange(chosen[mask], "ns", mask) for mask in range(1, ns)]
    left = newton(at, numbers, blocks, share)

    first_moment = first_owned + 0.5 * widened([qkv_m], first_lanes)
    first_own = over_columns(first_moment.astype(LOW))
    first_pieces = [first_own] + [exchange(first_own, "ns", mask) for mask in range(1, ns)]
    qkv_new = muon(count * ns, numbers, first_pieces, qkv_w)

    lefts = [left] + [exchange(left, "ns", mask) for mask in range(1, ns)]
    fc1_new, fc2_new, proj_new = finish(
        [w.shape[1] * ns for w in (fc1_w, fc2_w, proj_w)],
        (0, width, 2 * width),
        numbers,
        columns,
        lefts,
        (fc1_w, fc2_w, proj_w),
    )

    news = (qkv_new, proj_new, fc1_new, fc2_new)
    moments_new = (
        first_moment[:, :count],
        later_moment[:, 2 * width : 2 * width + proj_w.shape[1]],
        later_moment[:, :width],
        later_moment[:, width : 2 * width],
    )

    vector_grad = first_owned[:, count : count + vec_rows].T
    first_new = BETA_ONE * vector_moment + (1.0 - BETA_ONE) * vector_grad
    second_new = BETA_TWO * vector_square + (1.0 - BETA_TWO) * vector_grad * vector_grad
    first_hat = first_new / (1.0 - BETA_ONE**STEP)
    second_hat = second_new / (1.0 - BETA_TWO**STEP)
    vectors_new = vectors - ADAM_RATE * first_hat / (jnp.sqrt(second_hat) + ADAM_EPS)
    return (
        output,
        input_grad,
        *(new[0].T for new in news),
        *(m.T for m in moments_new),
        first_new,
        second_new,
        vectors_new,
        *(new[1].T for new in news),
    )


def solution(mesh):
    rows = P(("dp", "ns"), None)
    flat = P(("dp", "ns"))
    block = P("ns", "dp")
    return jax.shard_map(
        per_device,
        mesh=mesh,
        in_specs=(rows, rows, flat, flat) + (block,) * 11,
        out_specs=(rows, rows) + (block,) * 15,
        check_vma=False,
    )
```

```python
import functools
import math

import jax
import jax.numpy as jnp
import numpy as np
from jax import lax
from jax.experimental import pallas as pl
from jax.experimental.pallas import tpu as pltpu
from jax.sharding import PartitionSpec as P

HEADS = 6
PAIRS = 3
MARGIN = 128
NS_STEPS = 5
STEP = 10
TILE = 512
MLP_TILE = 512
FF_CHUNK = 256
SUB = 128
SPAN = 384
VEC_LANES = 16
GROUP = 2


EPS_NORM = 1e-06
NEWTON_A = 3.4445
NEWTON_B = -4.775
NEWTON_C = 2.0315
MUON_RATE = 0.2
MUON_DECAY = 0.1
ADAM_RATE = 0.4
BETA_ONE = 0.9
BETA_TWO = 0.999
ADAM_EPS = 1e-08
LOW = jnp.bfloat16
F32 = jnp.float32
TN = (((0,), (0,)), ((), ()))
NT = (((1,), (1,)), ((), ()))
NN = (((1,), (0,)), ((), ()))
VMEM_LIMIT = 56 * 1024 * 1024
ERF_P = 0.3275911
ERF_COEFS = (0.254829592, -0.284496736, 1.421413741, -1.453152027, 1.061405429)


def dot(left, right, dims=NN):
    return lax.dot_general(left, right, dims, preferred_element_type=F32)


PLACES, OWNERS, STARTS, WHICH, OFFSET, LOW_LANE, HIGH_LANE, COLUMN = 0, 4, 8, 12, 16, 17, 18, 19


def lane_numbers(shape):
    return lax.broadcasted_iota(jnp.int32, shape, len(shape) - 1)


def norm_parts(value):
    center = value - jnp.mean(value, axis=-1, keepdims=True)
    rate = lax.rsqrt(jnp.mean(center * center, axis=-1, keepdims=True) + EPS_NORM)
    return center * rate, rate


def norm_back(grad, normed, rate, gain):
    scaled = grad * gain
    first = jnp.mean(scaled, axis=-1, keepdims=True)
    second = jnp.mean(scaled * normed, axis=-1, keepdims=True)
    return rate * (scaled - first - normed * second)


def gelu_both(value):
    below = 1.0 + (ERF_P * 0.5**0.5) * jnp.abs(value)
    ratio = pl.reciprocal(below, approx=True)
    ratio = ratio * (2.0 - below * ratio)
    decay = jnp.exp2((value * value) * (-0.5 * math.log2(math.e)))
    poly = 0.5 * ERF_COEFS[4]
    for coef in ERF_COEFS[3::-1]:
        poly = poly * ratio + 0.5 * coef
    tail = poly * ratio * decay
    phi = jnp.where(value >= 0, 1.0 - tail, tail)
    return value * phi, phi + (value * (1.0 / math.sqrt(2.0 * math.pi))) * decay


def gelu_rows(hidden, bias, grad, between):
    active, back = [], []
    rows = hidden.shape[0]
    pieces = rows // 16
    for n in range(pieces):
        if n * len(between) // pieces != (n - 1) * len(between) // pieces:
            between[n * len(between) // pieces]()
        here = slice(n * 16, (n + 1) * 16)
        value, slope = gelu_both(hidden[here] + bias)
        active.append(value.astype(LOW))
        back.append((grad[here] * slope).astype(LOW))
    return jnp.concatenate(active, axis=0), jnp.concatenate(back, axis=0)


def halves_of(lanes):
    half = lanes.shape[0] // 2
    return lanes[:half, :SUB], lanes[half:, SUB:]


def staged(count, first, second, third):
    made = first(0)
    kept = None
    for n in range(count):
        coming = first(n + 1) if n + 1 < count else None
        if kept is not None:
            third(n - 1, kept)
        kept = second(n, made)
        made = coming
    third(count - 1, kept)


def both_heads(pair):
    first = (lane_numbers((1, SUB)) < SUB // 2).astype(F32).astype(pair.dtype)
    second = (lane_numbers((1, SUB)) >= SUB // 2).astype(F32).astype(pair.dtype)
    return jnp.concatenate([pair * first, pair * second], axis=0)


def fetch(pairs, sems):
    copies = [
        pltpu.make_async_copy(source, target, sems.at[n])
        for n, (source, target) in enumerate(pairs)
    ]
    for copy in copies:
        copy.start()
    for copy in copies:
        copy.wait()


def prepare_kernel(tokens, cotangent, ids, normed, normed_turned, out_turned, columns, sums):
    step = pl.program_id(0)
    parts = columns.shape[0] // SUB

    @pl.when(step == 0)
    def clear():
        sums[...] = jnp.zeros(sums.shape, F32)
        for number in range(parts):
            row = jnp.broadcast_to(ids[number : number + 1, :], (SUB, SUB))
            columns[number * SUB : (number + 1) * SUB, :] = row.T

    value, _ = norm_parts(tokens[...].astype(F32))
    normed[...] = value
    normed_turned[...] = value.astype(LOW).T
    out_low = cotangent[...]
    out_turned[...] = out_low.T
    sums[0:1, :] += jnp.sum(out_low.astype(F32), axis=0, keepdims=True)


def prepare(tokens, cotangent, ids):
    rows, width = tokens.shape
    padded = rows + 2 * MARGIN
    tile = pl.BlockSpec((TILE, width), lambda s: (s, 0))
    turned = pl.BlockSpec((width, TILE), lambda s: (0, s))
    whole = lambda *dims: pl.BlockSpec(dims, lambda s: (0,) * len(dims))
    return pl.pallas_call(
        prepare_kernel,
        grid=(rows // TILE,),
        in_specs=[tile, tile, whole(*ids.shape)],
        out_specs=[tile, turned, turned, whole(padded, SUB), whole(8, width)],
        out_shape=[
            jax.ShapeDtypeStruct((rows, width), F32),
            jax.ShapeDtypeStruct((width, rows), LOW),
            jax.ShapeDtypeStruct((width, rows), LOW),
            jax.ShapeDtypeStruct((padded, SUB), F32),
            jax.ShapeDtypeStruct((8, width), F32),
        ],
        compiler_params=pltpu.CompilerParams(vmem_limit_bytes=VMEM_LIMIT),
        cost_estimate=pl.CostEstimate(
            flops=20_000_000, bytes_accessed=12_000_000, transcendentals=2048
        ),
        name="prepare",
    )(tokens, cotangent, ids)


def attend_kernel(numbers, *refs):
    (normed, ids, columns, query, key, value, key_turned, mixed, probs, weight, vectors,
     gathered, pair_weight, value_turned, shifts, sems) = refs[-16:]
    pieces = refs[:-16]
    step = pl.program_id(0)
    chunks = pl.num_programs(0) - 1
    width = normed.shape[1]
    parts = len(pieces)
    block = 3 * width // parts
    rows_each = 12 // parts

    @pl.when(step == 0)
    def assemble():
        fetch([(piece, gathered.at[n]) for n, piece in enumerate(pieces)], sems)
        total = jnp.zeros((width, 3 * width), F32)
        turned = jnp.zeros((width, SUB), F32)
        for number in range(parts):
            piece = gathered[numbers[PLACES + number]].astype(F32)
            kept = jnp.where(lane_numbers(piece.shape) < block, piece, 0.0)
            wide = jnp.concatenate([kept, jnp.zeros((width, 2 * width), F32)], axis=1)
            total = total + (pltpu.roll(wide, block * number, 1) if number else wide)
            last = piece[:, 2 * SUB :]
            at = block - 2 * SUB
            lane = lane_numbers(last.shape)
            vec = jnp.where((lane >= at) & (lane < at + rows_each), last, 0.0)
            turned = turned + pltpu.roll(vec, (rows_each * number - at) % SUB, 1)
        total = total.astype(LOW)
        weight[...] = total
        pair_weight[...] = total[:, width:].T
        vectors[...] = turned.T[:VEC_LANES]
        shifts[...] = turned
        edges = (pl.ds(0, MARGIN), pl.ds(MARGIN + chunks * TILE, MARGIN))
        for edge in edges:
            for ref in (query, key, value):
                ref[edge, :] = jnp.zeros((MARGIN, width), LOW)
            for ref in (key_turned, value_turned):
                ref[:, edge] = jnp.zeros((width, MARGIN), LOW)

    @pl.when(step < chunks)
    def project():
        first_in = (normed[...] * vectors[0:1, :] + vectors[1:2, :]).astype(LOW)
        result = dot(first_in, weight[...])
        turned = dot(pair_weight[...], first_in, NT)
        here = pl.ds(pl.multiple_of(MARGIN + step * TILE, SUB), TILE)
        scale = (width // HEADS) ** (-0.5)
        made = (result[:, :width] + vectors[2:3, :]).astype(LOW) * jnp.asarray(scale, LOW)
        query[here, :] = made
        key[here, :] = result[:, width : 2 * width].astype(LOW)
        value[here, :] = (result[:, 2 * width :] + vectors[3:4, :]).astype(LOW)
        key_turned[:, here] = turned[:width].astype(LOW)
        value_turned[:, here] = (turned[width:] + shifts[:, 3:4]).astype(LOW)

    @pl.when(step > 0)
    def attend():
        def place(number):
            sub, pair = number // PAIRS, number % PAIRS
            tile = (step - 1) * (TILE // SUB) + sub
            start = pl.multiple_of(tile * SUB, SUB)
            return sub, pair, tile, start, pl.ds(start, SPAN), pl.ds(pair * SUB, SUB)

        def of_group(group):
            return range(group * GROUP, (group + 1) * GROUP)

        def score(group):
            made = []
            for number in of_group(group):
                _, _, _, start, near_rows, heads = place(number)
                wanted = both_heads(query[pl.ds(start + MARGIN, SUB), heads])
                made.append(dot(key[near_rows, heads], wanted, NT))
            return made

        def soften(group, made):
            own = []
            for number, scores in zip(of_group(group), made):
                _, _, tile, _, near_rows, _ = place(number)
                same = columns[near_rows, :] == ids[pl.ds(tile + 1, 1), :]
                own += [
                    jnp.where(same, scores[:, head * SUB : (head + 1) * SUB], -1e30)
                    for head in range(2)
                ]
            largest = [jnp.max(part, axis=0, keepdims=True) for part in own]
            expo = [jnp.exp(part - most) for part, most in zip(own, largest)]
            share = [1.0 / jnp.sum(part, axis=0, keepdims=True) for part in expo]
            scaled = [(part * by).astype(LOW) for part, by in zip(expo, share)]
            result = []
            for n, number in enumerate(of_group(group)):
                sub, pair, _, _, _, _ = place(number)
                result.append(jnp.concatenate(scaled[2 * n : 2 * n + 2], axis=1))
                probs[pair, sub] = result[-1]
            return result

        def mix(group, kept):
            for number, prob in zip(of_group(group), kept):
                sub, _, _, _, near_rows, heads = place(number)
                first, second = halves_of(dot(value_turned[heads, near_rows], prob))
                turned = jnp.concatenate([first, second], axis=0).astype(LOW)
                mixed[pl.ds(sub * SUB, SUB), heads] = turned.T

        staged(TILE // SUB * PAIRS // GROUP, score, soften, mix)


def attend_forward(numbers, pieces, normed, ids, columns):
    rows, width = normed.shape
    chunks = rows // TILE
    tiles = TILE // SUB
    parts = len(pieces)
    now = lambda s: jnp.minimum(s, chunks - 1)
    before = lambda s: jnp.maximum(s - 1, 0)
    whole = lambda *dims: pl.BlockSpec(dims, lambda s, *_: (0,) * len(dims))
    padded = rows + 2 * MARGIN
    return pl.pallas_call(
        attend_kernel,
        grid_spec=pltpu.PrefetchScalarGridSpec(
            num_scalar_prefetch=1,
            grid=(chunks + 1,),
            in_specs=[pl.BlockSpec(memory_space=pl.ANY)] * parts
            + [
                pl.BlockSpec((TILE, width), lambda s, *_: (now(s), 0)),
                whole(*ids.shape),
                whole(*columns.shape),
            ],
            out_specs=[
                whole(padded, width),
                whole(padded, width),
                whole(padded, width),
                whole(width, padded),
                pl.BlockSpec((TILE, width), lambda s, *_: (before(s), 0)),
                pl.BlockSpec((PAIRS, tiles, SPAN, 2 * SUB), lambda s, *_: (0, before(s), 0, 0)),
                whole(width, 3 * width),
                whole(VEC_LANES, width),
            ],
            scratch_shapes=[
                pltpu.VMEM((parts, *pieces[0].shape), LOW),
                pltpu.VMEM((2 * width, width), LOW),
                pltpu.VMEM((width, padded), LOW),
                pltpu.VMEM((width, SUB), F32),
                pltpu.SemaphoreType.DMA((parts,)),
            ],
        ),
        out_shape=[
            jax.ShapeDtypeStruct((padded, width), LOW),
            jax.ShapeDtypeStruct((padded, width), LOW),
            jax.ShapeDtypeStruct((padded, width), LOW),
            jax.ShapeDtypeStruct((width, padded), LOW),
            jax.ShapeDtypeStruct((rows, width), LOW),
            jax.ShapeDtypeStruct((PAIRS, rows // SUB, SPAN, 2 * SUB), LOW),
            jax.ShapeDtypeStruct((width, 3 * width), LOW),
            jax.ShapeDtypeStruct((VEC_LANES, width), F32),
        ],
        compiler_params=pltpu.CompilerParams(vmem_limit_bytes=VMEM_LIMIT),
        cost_estimate=pl.CostEstimate(
            flops=12_000_000_000, bytes_accessed=22_000_000, transcendentals=5_000_000
        ),
        name="attend_forward",
    )(numbers, *pieces, normed, ids, columns)


def mlp_kernel(numbers, near, far, *refs):
    (vectors, mixed, tokens, cotangent, out_turned, out_sums, output, grad_residual, grad_mixed, inner, grads_near,
     grads_far, sums, one, two, proj_parts, proj, acc_one, acc_two, acc_proj, bias
    ) = refs
    step = pl.program_id(0)
    width = tokens.shape[1]
    mid = near.shape[1]
    parts = mid + far.shape[1]
    block = width // parts
    last_at = 2 * width
    hidden_width = one.shape[1]

    @pl.when(step == 0)
    def assemble():
        for part in range(parts):
            ref, at = (near, part) if part < mid else (far, part - mid)
            lanes = pl.ds(part * width, width)
            for group in range(near.shape[0]):
                here = pl.ds(group * near.shape[2], near.shape[2])
                one[here, lanes] = ref[group, at, :, :width]
                two[here, lanes] = ref[group, at, :, width:last_at]
                proj_parts[part, here, :] = ref[group, at, :, last_at:]
        total = jnp.zeros((width, width), F32)
        for number in range(parts):
            piece = proj_parts[numbers[PLACES + number]].astype(F32)
            kept = jnp.where(lane_numbers(piece.shape) < block, piece, 0.0)
            wide = jnp.concatenate([kept, jnp.zeros((width, width - SUB), F32)], axis=1)
            total = total + (pltpu.roll(wide, block * number, 1) if number else wide)
        proj[...] = total.astype(LOW)
        for part in range(parts):
            row = vectors[pl.ds(8 + numbers[OWNERS + part], 1), :]
            bias[0:1, part * width : (part + 1) * width] = row
        acc_one[...] = jnp.zeros(acc_one.shape, F32)
        acc_two[...] = jnp.zeros(acc_two.shape, F32)
        acc_proj[...] = jnp.zeros(acc_proj.shape, F32)
        sums[...] = jnp.zeros(sums.shape, F32)
        sums[7:8, :] = out_sums[0:1, :]

    def add_row(row, values):
        sums[pl.ds(row, 1), :] += jnp.sum(values, axis=0, keepdims=True)

    own = mixed[...]
    residual = tokens[...].astype(F32) + dot(own, proj[...], NT) + vectors[4:5, :]
    normed, rate = norm_parts(residual)
    gain = vectors[5:6, :]
    second_in = (normed * gain + vectors[6:7, :]).astype(LOW)
    out_low = cotangent[...]
    grad_out = out_low.astype(F32)
    second_turned = second_in.T
    out_turned = out_turned[...]
    totals = [residual + vectors[7:8, :], jnp.zeros(residual.shape, F32)]

    count = hidden_width // FF_CHUNK
    ones = jnp.ones((16, MLP_TILE), LOW)
    second_and_ones = jnp.concatenate([second_turned, ones], axis=0)
    hiddens, slopes, kept = {}, {}, {}

    def lanes_of(number):
        return pl.ds(number * FF_CHUNK, FF_CHUNK)

    def make_hidden(number):
        hiddens[number] = dot(second_in, one[:, lanes_of(number)])

    def make_slope(number):
        slopes[number] = dot(out_low, two[:, lanes_of(number)])

    def add_one(number):
        acc_one[:, lanes_of(number)] += dot(second_and_ones, kept[number][1])

    def add_two(number):
        acc_two[:, lanes_of(number)] += dot(out_turned, kept[number][0])

    def add_result(number):
        totals[0] = totals[0] + dot(kept[number][0], two[:, lanes_of(number)], NT)

    def add_second(number):
        totals[1] = totals[1] + dot(kept[number][1], one[:, lanes_of(number)], NT)

    make_hidden(0)
    make_slope(0)
    for number in range(count):
        between = []
        if number + 1 < count:
            between += [functools.partial(f, number + 1) for f in (make_hidden, make_slope)]
        if number > 0:
            between += [
                functools.partial(f, number - 1)
                for f in (add_result, add_second, add_one, add_two)
            ]
        kept[number] = gelu_rows(
            hiddens.pop(number), bias[0:1, lanes_of(number)], slopes.pop(number), between
        )
    for f in (add_result, add_second, add_one, add_two):
        f(count - 1)
    result, grad_second = totals
    output[...] = result.astype(LOW)
    add_row(5, grad_second * normed)
    add_row(6, grad_second)
    grad_res = grad_out + norm_back(grad_second, normed, rate, gain)
    grad_residual[...] = grad_res
    branch = grad_res.astype(LOW)
    add_row(4, branch.astype(F32))
    acc_proj[...] += dot(branch.T, own)
    grad_own = dot(branch, proj[...]).astype(LOW)
    grad_mixed[...] = grad_own
    high, rest = halves(grad_own.astype(F32) * own.astype(F32))
    head = lax.broadcasted_iota(jnp.int32, (16, width), 0)
    chosen = (lane_numbers((16, width)) // (width // HEADS) == head).astype(F32).astype(LOW)
    inner[...] = (dot(chosen, high, NT) + dot(chosen, rest, NT))[:8]

    @pl.when(step == pl.num_programs(0) - 1)
    def finish():
        total = acc_proj[...]
        for number in range(parts):
            turned = pltpu.roll(total, (width - block * number) % width, 1) if number else total
            proj_parts[numbers[PLACES + number]] = turned[:, :SUB].astype(LOW)
        for part in range(parts):
            ref, at = (grads_near, part) if part < mid else (grads_far, part - mid)
            lanes = pl.ds(part * width, width)
            for group in range(ref.shape[0]):
                here = pl.ds(group * ref.shape[2], ref.shape[2])
                ref[group, at, :, :width] = acc_one[here, lanes].astype(LOW)
                ref[group, at, :, width:last_at] = acc_two[here, lanes].astype(LOW)
                ref[group, at, :, last_at:] = proj_parts[part, here, :]
            sums[pl.ds(8 + numbers[OWNERS + part], 1), :] = acc_one[width : width + 1, lanes]


def mlp_both(numbers, near, far, vectors, mixed, tokens, cotangent, out_turned, out_sums):
    rows, width = tokens.shape
    parts = near.shape[1] + far.shape[1]
    hidden_width = parts * width
    tile = pl.BlockSpec((MLP_TILE, width), lambda s, *_: (s, 0))
    whole = lambda *dims: pl.BlockSpec(dims, lambda s, *_: (0,) * len(dims))
    return pl.pallas_call(
        mlp_kernel,
        grid_spec=pltpu.PrefetchScalarGridSpec(
            num_scalar_prefetch=1,
            grid=(rows // MLP_TILE,),
            in_specs=[
                whole(*near.shape), whole(*far.shape), whole(*vectors.shape), tile, tile, tile,
                pl.BlockSpec((width, MLP_TILE), lambda s, *_: (0, s)), whole(*out_sums.shape),
            ],
            out_specs=[
                tile,
                tile,
                tile,
                pl.BlockSpec((8, MLP_TILE), lambda s, *_: (0, s)),
                whole(*near.shape),
                whole(*far.shape),
                whole(*vectors.shape),
            ],
            scratch_shapes=[
                pltpu.VMEM((width, hidden_width), LOW),
                pltpu.VMEM((width, hidden_width), LOW),
                pltpu.VMEM((parts, width, SUB), LOW),
                pltpu.VMEM((width, width), LOW),
                pltpu.VMEM((width + 16, hidden_width), F32),
                pltpu.VMEM((width, hidden_width), F32),
                pltpu.VMEM((width, width), F32),
                pltpu.VMEM((8, hidden_width), F32),
            ],
        ),
        out_shape=[
            jax.ShapeDtypeStruct((rows, width), LOW),
            jax.ShapeDtypeStruct((rows, width), F32),
            jax.ShapeDtypeStruct((rows, width), LOW),
            jax.ShapeDtypeStruct((8, rows), F32),
            jax.ShapeDtypeStruct(near.shape, LOW),
            jax.ShapeDtypeStruct(far.shape, LOW),
            jax.ShapeDtypeStruct(vectors.shape, F32),
        ],
        compiler_params=pltpu.CompilerParams(vmem_limit_bytes=VMEM_LIMIT),
        cost_estimate=pl.CostEstimate(
            flops=34_000_000_000, bytes_accessed=20_000_000, transcendentals=6_000_000
        ),
        name="mlp_both",
    )(numbers, near, far, vectors, mixed, tokens, cotangent, out_turned, out_sums)


def attend_back_kernel(
    numbers,
    query,
    key_turned,
    value,
    probs,
    inner,
    grad_mixed,
    normed_turned,
    weight,
    vectors,
    sums,
    grad_qkv,
    near,
    far,
    grad_query,
    acc_key,
    acc_value,
    acc_sums,
    normed_sums,
    blocks,
    rows,
):
    step = pl.program_id(0)
    chunks = pl.num_programs(0) - 1
    pairs = range(PAIRS)
    count = len(pairs)
    scale = (SUB // 2) ** (-0.5)

    @pl.when(step == 0)
    def clear():
        acc_key[...] = jnp.zeros(acc_key.shape, F32)
        acc_value[...] = jnp.zeros(acc_value.shape, F32)
        normed_sums[...] = jnp.zeros(normed_sums.shape, F32)
        acc_sums[...] = jnp.zeros(acc_sums.shape, F32)

    @pl.when(step < chunks)
    def attend():
        def place(number):
            sub, at = number // count, number % count
            start = pl.multiple_of((step * (TILE // SUB) + sub) * SUB, SUB)
            return sub, at, start, pl.ds(start, SPAN), pl.ds(at * SUB, SUB)

        def slope(number):
            sub, _, _, near_rows, heads = place(number)
            grad = both_heads(grad_mixed[pl.ds(sub * SUB, SUB), heads])
            return dot(value[near_rows, heads], grad, NT)

        def soften(number, slopes):
            sub, at, _, _, _ = place(number)
            pair = pairs[at]
            cols = pl.ds(sub * SUB, SUB)
            both = []
            for head in range(2):
                lanes = slice(head * SUB, (head + 1) * SUB)
                less = slopes[:, lanes] - inner[2 * pair + head : 2 * pair + head + 1, cols]
                both.append((probs[at, sub, :, lanes].astype(F32) * less).astype(LOW))
            return jnp.concatenate(both, axis=1)

        def collect(number, scores):
            sub, at, start, near_rows, heads = place(number)
            first, second = halves_of(dot(key_turned[heads, near_rows], scores))
            turned = (jnp.concatenate([first, second], axis=0) * scale).astype(LOW)
            grad_query[pl.ds(start, SUB), heads] = turned.T
            wanted = both_heads(query[pl.ds(start + MARGIN, SUB), heads])
            acc_key[near_rows, heads] += dot(scores, wanted)
            grad = both_heads(grad_mixed[pl.ds(sub * SUB, SUB), heads])
            acc_value[near_rows, heads] += dot(probs[at, sub], grad)

        staged(TILE // SUB * count, slope, soften, collect)

    @pl.when(step > 0)
    def collect():
        here = pl.ds(pl.multiple_of((step - 1) * TILE, SUB), TILE)
        there = pl.ds(pl.multiple_of((step - 1) * TILE + MARGIN, SUB), TILE)
        parts = (
            grad_query[here, :],
            acc_key[there, :].astype(LOW),
            acc_value[there, :].astype(LOW),
        )
        joined = jnp.concatenate(parts, axis=1)
        grad_qkv[...] = joined
        normed_sums[...] += dot(normed_turned[...], joined)
        acc_sums[0:1, :] += jnp.sum(joined.astype(F32), axis=0, keepdims=True)

    @pl.when(step == chunks)
    def finish():
        weight_grad(
            numbers, normed_sums[...], acc_sums[0:1, :], weight, vectors, sums, near, far, blocks, rows
        )


def weight_grad(numbers, total, columns, weight, vectors, sums, near, far, blocks, rows):
    width = weight.shape[0]
    parts, mid = blocks.shape[0], near.shape[0]
    block = 3 * width // parts
    rows_each = 12 // parts
    wide = weight[...].astype(F32)
    grad_gain = jnp.sum(total * wide, axis=1, keepdims=True)
    grad_shift = jnp.sum(wide * columns, axis=1, keepdims=True)
    rows[...] = jnp.zeros(rows.shape, F32)
    rows[0:VEC_LANES, :] = sums[...]
    rows[2:3, :] = columns[:, :width]
    rows[3:4, :] = columns[:, 2 * width :]
    rows[VEC_LANES : 2 * VEC_LANES, :] = vectors[...]
    turned = rows[...].T
    gain = turned[:, VEC_LANES : VEC_LANES + 1]
    shift = turned[:, VEC_LANES + 1 : VEC_LANES + 2]
    lane = lane_numbers(turned.shape)
    turned = jnp.where(lane == 0, grad_gain, jnp.where(lane == 1, grad_shift, turned))
    total = total * gain + shift * columns
    at = block - 2 * SUB
    for number in range(parts):
        away = (3 * width - block * number) % (3 * width)
        piece = (pltpu.roll(total, away, 1) if number else total)[:, :width]
        vec = pltpu.roll(turned, (at - rows_each * number) % SUB, 1)
        last = jnp.where(lane < at, piece[:, 2 * SUB :], 0.0)
        last = jnp.where((lane >= at) & (lane < at + rows_each), vec, last)
        at_place = numbers[PLACES + number]
        blocks[at_place, :, : 2 * SUB] = piece[:, : 2 * SUB].astype(LOW)
        blocks[at_place, :, 2 * SUB :] = last.astype(LOW)
    near[...] = blocks[:mid]
    far[...] = blocks[mid:]


def attend_backward(
    numbers, parts, query, key_turned, value, probs, inner, grad_mixed, normed_turned, weight,
    vectors, sums,
):
    width, rows = normed_turned.shape
    padded = query.shape[0]
    chunks = rows // TILE
    tiles = TILE // SUB
    now = lambda s: jnp.minimum(s, chunks - 1)
    before = lambda s: jnp.maximum(s - 1, 0)
    whole = lambda *dims: pl.BlockSpec(dims, lambda s, *_: (0,) * len(dims))
    half = (parts // 2, width, width)
    return pl.pallas_call(
        attend_back_kernel,
        grid_spec=pltpu.PrefetchScalarGridSpec(
            num_scalar_prefetch=1,
            grid=(chunks + 1,),
            in_specs=[
                whole(padded, width),
                whole(width, padded),
                whole(padded, width),
                pl.BlockSpec((PAIRS, tiles, SPAN, 2 * SUB), lambda s, *_: (0, now(s), 0, 0)),
                pl.BlockSpec((8, TILE), lambda s, *_: (0, now(s))),
                pl.BlockSpec((TILE, width), lambda s, *_: (now(s), 0)),
                pl.BlockSpec((width, TILE), lambda s, *_: (0, before(s))),
                whole(*weight.shape),
                whole(*vectors.shape),
                whole(*sums.shape),
            ],
            out_specs=[
                pl.BlockSpec((TILE, 3 * width), lambda s, *_: (before(s), 0)),
                whole(*half),
                whole(*half),
            ],
            scratch_shapes=[
                pltpu.VMEM((rows, width), LOW),
                pltpu.VMEM((padded, width), F32),
                pltpu.VMEM((padded, width), F32),
                pltpu.VMEM((8, 3 * width), F32),
                pltpu.VMEM((width, 3 * width), F32),
                pltpu.VMEM((parts, width, width), LOW),
                pltpu.VMEM((SUB, width), F32),
            ],
        ),
        out_shape=[
            jax.ShapeDtypeStruct((rows, 3 * width), LOW),
            jax.ShapeDtypeStruct(half, LOW),
            jax.ShapeDtypeStruct(half, LOW),
        ],
        compiler_params=pltpu.CompilerParams(vmem_limit_bytes=VMEM_LIMIT),
        cost_estimate=pl.CostEstimate(
            flops=16_000_000_000, bytes_accessed=24_000_000, transcendentals=0
        ),
        name="attend_backward",
    )(
        numbers, query, key_turned, value, probs, inner, grad_mixed, normed_turned, weight, vectors,
        sums,
    )


def input_grad_kernel(weight, vectors, tokens, grad_residual, grad_qkv, input_grad):
    normed, rate = norm_parts(tokens[...].astype(F32))
    grad_first = dot(grad_qkv[...], weight[...], NT)
    back = norm_back(grad_first, normed, rate, vectors[0:1, :])
    input_grad[...] = (grad_residual[...] + back).astype(LOW)


def input_gradient(weight, vectors, tokens, grad_residual, grad_qkv):
    rows, width = tokens.shape
    size = TILE
    tile = pl.BlockSpec((size, width), lambda s: (s, 0))
    whole = lambda ref: pl.BlockSpec(ref.shape, lambda s: (0, 0))
    return pl.pallas_call(
        input_grad_kernel,
        grid=(rows // size,),
        in_specs=[
            whole(weight), whole(vectors), tile, tile,
            pl.BlockSpec((size, 3 * width), lambda s: (s, 0)),
        ],
        out_specs=tile,
        out_shape=jax.ShapeDtypeStruct((rows, width), LOW),
        compiler_params=pltpu.CompilerParams(vmem_limit_bytes=VMEM_LIMIT),
        cost_estimate=pl.CostEstimate(
            flops=4_000_000_000, bytes_accessed=13_000_000, transcendentals=2048
        ),
        name="input_gradient",
    )(weight, vectors, tokens, grad_residual, grad_qkv)


def halves(value):
    high = value.astype(LOW)
    return high, (value - high.astype(F32)).astype(LOW)


def dot_three(left, right):
    tall = jnp.concatenate([right[0], right[0], right[1]], axis=0)
    return dot(jnp.concatenate([left[0], left[1], left[0]], axis=1), tall)


def newton_rows(blocks, offset, rows):
    gram = dot(blocks[0], blocks[0], NT)
    for part in blocks[1:]:
        gram = gram + dot(part, part, NT)
    depth = gram.shape[0]
    down = lax.broadcasted_iota(jnp.int32, (depth, depth), 0)
    eye = (down == lane_numbers((depth, depth))).astype(F32)
    norm = 1.0 / (jnp.sqrt(jnp.sum(gram * eye, keepdims=True)) + 1e-07)
    gram = gram * (norm * norm)
    place = lax.broadcasted_iota(jnp.int32, (rows, depth), 0) + offset
    left = jnp.where(place == lane_numbers((rows, depth)), norm, 0.0)
    for step in range(NS_STEPS - 1):
        pair = halves(gram)
        poly = halves(NEWTON_A * eye + NEWTON_B * gram + NEWTON_C * dot_three(pair, pair))
        lefts = halves(left)
        both = dot_three([jnp.concatenate([pair[n], lefts[n]], axis=0) for n in range(2)], poly)
        left = both[depth:]
        gram = dot_three(halves(both[:depth]), poly)
    pair = halves(gram)
    once = dot_three(halves(left), pair)
    return NEWTON_A * left + NEWTON_B * once + NEWTON_C * dot_three(halves(once), pair)


def stepped(left, own, height, old):
    high, rest = halves(left)
    ortho = (dot(high, own) + dot(rest, own))[: old.shape[0], : old.shape[1]]
    return old * (1.0 - MUON_RATE * MUON_DECAY) - (MUON_RATE * 0.2 * math.sqrt(height)) * ortho


def kept_lanes(value, low, high):
    lane = lane_numbers(value.shape)
    return jnp.where((lane >= low) & (lane < high), value.astype(F32), 0.0).astype(LOW)


def tall_of(rows):
    return -(-rows // 16) * 16


def muon_kernel(height, numbers, *refs):
    old, new, copy = refs[-3:]
    count = old.shape[1]
    blocks = [kept_lanes(ref[...], 0, count) for ref in refs[:-3]]
    left = newton_rows(blocks, numbers[OFFSET], tall_of(old.shape[0]))
    result = stepped(left, blocks[0], height, old[...])
    new[...] = result
    copy[...] = result.astype(LOW)


def muon(height, numbers, blocks, old):
    vmem = pl.BlockSpec(memory_space=pltpu.VMEM)

    def kernel(*refs):
        muon_kernel(height, *refs)

    return pl.pallas_call(
        kernel,
        in_specs=[pl.BlockSpec(memory_space=pltpu.SMEM)] + [vmem] * (len(blocks) + 1),
        out_specs=[vmem, vmem],
        out_shape=[
            jax.ShapeDtypeStruct(old.shape, F32),
            jax.ShapeDtypeStruct(old.shape, LOW),
        ],
        compiler_params=pltpu.CompilerParams(vmem_limit_bytes=VMEM_LIMIT),
        cost_estimate=pl.CostEstimate(
            flops=9_000_000_000, bytes_accessed=2_000_000, transcendentals=10
        ),
        name="muon",
    )(numbers, *blocks, old)


def pick_kernel(count, numbers, *refs):
    pieces, columns, outs = refs[:count], refs[count], refs[count + 1 :]
    share = pieces[0].shape[0]
    for k, piece in enumerate(pieces):
        columns[k * share : (k + 1) * share, :] = piece[...]
        for n, out in enumerate(outs):
            at = pl.multiple_of(numbers[STARTS + n] * SUB, SUB)
            out[k * share : (k + 1) * share, :] = piece[:, pl.ds(at, out.shape[1])]


def pick(numbers, pieces, count):
    depth = len(pieces) * pieces[0].shape[0]
    vmem = pl.BlockSpec(memory_space=pltpu.VMEM)

    def kernel(*refs):
        pick_kernel(len(pieces), *refs)

    return pl.pallas_call(
        kernel,
        in_specs=[pl.BlockSpec(memory_space=pltpu.SMEM)] + [vmem] * len(pieces),
        out_specs=[vmem] * (count + 1),
        out_shape=[jax.ShapeDtypeStruct((depth, pieces[0].shape[1]), LOW)]
        + [jax.ShapeDtypeStruct((depth, depth), LOW)] * count,
        name="pick",
    )(numbers, *pieces)


def newton_kernel(at, numbers, *refs):
    left = refs[-1]
    bounds = numbers[LOW_LANE], numbers[HIGH_LANE]
    blocks = [kept_lanes(ref[...], *bounds) for ref in refs[:-1]]
    left[...] = newton_rows(blocks, numbers[OFFSET] if at is None else at, left.shape[0])


def newton(at, numbers, blocks, rows):
    vmem = pl.BlockSpec(memory_space=pltpu.VMEM)

    def kernel(*refs):
        newton_kernel(at, *refs)

    return pl.pallas_call(
        kernel,
        in_specs=[pl.BlockSpec(memory_space=pltpu.SMEM)] + [vmem] * len(blocks),
        out_specs=vmem,
        out_shape=jax.ShapeDtypeStruct((tall_of(rows), blocks[0].shape[0]), F32),
        compiler_params=pltpu.CompilerParams(vmem_limit_bytes=VMEM_LIMIT),
        cost_estimate=pl.CostEstimate(
            flops=9_000_000_000, bytes_accessed=2_000_000, transcendentals=10
        ),
        name="newton",
    )(numbers, *blocks)


def finish_kernel(heights, lanes, numbers, columns, *refs):
    count = len(heights)
    store = refs[-1]
    news = refs[-1 - 2 * count : -1]
    olds = refs[-1 - 3 * count : -1 - 2 * count]
    lefts = refs[: -1 - 3 * count]
    for n, left in enumerate(lefts):
        store[n] = left[...]
    for n in range(count):
        wide = -(-olds[n].shape[1] // SUB) * SUB
        own = columns[:, lanes[n] : lanes[n] + wide]
        result = stepped(store[numbers[WHICH + n]], own, heights[n], olds[n][...])
        news[2 * n][...] = result
        news[2 * n + 1][...] = result.astype(LOW)


def finish(heights, lanes, numbers, columns, lefts, olds):
    vmem = pl.BlockSpec(memory_space=pltpu.VMEM)
    count = len(olds)

    def kernel(*refs):
        finish_kernel(heights, lanes, *refs)

    outs = pl.pallas_call(
        kernel,
        in_specs=[pl.BlockSpec(memory_space=pltpu.SMEM)] + [vmem] * (1 + len(lefts) + count),
        out_specs=[vmem] * (2 * count),
        out_shape=[
            jax.ShapeDtypeStruct(old.shape, kind) for old in olds for kind in (F32, LOW)
        ],
        scratch_shapes=[pltpu.VMEM((len(lefts), *lefts[0].shape), F32)],
        compiler_params=pltpu.CompilerParams(vmem_limit_bytes=VMEM_LIMIT),
        cost_estimate=pl.CostEstimate(
            flops=200_000_000, bytes_accessed=2_000_000, transcendentals=0
        ),
        name="finish",
    )(numbers, columns, *lefts, *olds)
    return [(outs[2 * n], outs[2 * n + 1]) for n in range(count)]


def exchange(x, axis, mask):
    size = lax.axis_size(axis)
    return lax.ppermute(x, axis, [(i, i ^ mask) for i in range(size)])


def place_masks(size):
    masks = [0]
    bit = size // 2
    while bit >= 1:
        masks = masks + [m ^ bit for m in masks]
        bit //= 2
    return masks


def from_columns(own):
    size = lax.axis_size("dp")
    sent = jnp.broadcast_to(own[None], (size, *own.shape))
    return lax.all_to_all(sent, "dp", split_axis=0, concat_axis=0, tiled=True)


def over_columns(own):
    return from_columns(own).reshape(-1, own.shape[1])


def device_numbers(dp, ns, share, width, proj_rows):
    masks = place_masks(ns)
    tasks = [(0, 0, width), (width // SUB, 0, width)]
    tasks += [(width // SUB + 1, 2 * SUB, 2 * SUB + proj_rows)] * (ns - 2)
    table = np.zeros((dp * ns, 24), np.int32)
    for device in range(dp * ns):
        column, index = device // ns, device % ns
        row = table[device]
        for n in range(ns):
            row[OWNERS + n] = index ^ masks[n]
            row[PLACES + (index ^ masks[n])] = n
            row[STARTS + n] = tasks[index ^ n][0]
        for n in range(3):
            row[WHICH + n] = index ^ n
        row[OFFSET] = column * share
        row[COLUMN] = column
        row[LOW_LANE], row[HIGH_LANE] = tasks[index][1:]
    return table


def over_rows(own):
    held = [own]
    bit = lax.axis_size("ns") // 2
    while bit >= 1:
        held = held + [exchange(block, "ns", bit) for block in held]
        bit //= 2
    return held


def added(keep, got):
    return (keep.astype(F32) + got.astype(F32)).astype(LOW)


def sum_columns(pieces):
    return summed(lax.all_to_all(pieces, "dp", split_axis=0, concat_axis=0, tiled=True))


def summed(pieces):
    return jnp.sum(pieces.astype(F32), axis=0)


def columns_direct(own, other):
    devices = lax.axis_size("dp")
    if devices > 8 or own.shape[0] % 16:
        return [over_columns(own)], None
    pieces = [own] + [exchange(own, "dp", mask) for mask in range(1, devices // 2)]
    again, _ = lax.optimization_barrier((own, other))
    return pieces + [exchange(again, "dp", mask) for mask in range(devices // 2, devices)], 0


def widened(arrays, lanes):
    joined = jnp.concatenate(arrays, axis=1)
    return jnp.pad(joined, ((0, 0), (0, lanes - joined.shape[1])))


def per_device(
    tokens,
    cotangent,
    segment,
    valid_rows,
    qkv_weight,
    proj_weight,
    fc1_weight,
    fc2_weight,
    qkv_moment,
    proj_moment,
    fc1_moment,
    fc2_moment,
    vectors,
    vector_moment,
    vector_square,
):
    rows, width = tokens.shape
    ns = lax.axis_size("ns")
    qkv_w, proj_w, fc1_w, fc2_w = (w.T for w in (qkv_weight, proj_weight, fc1_weight, fc2_weight))
    qkv_m, proj_m, fc1_m, fc2_m = (w.T for w in (qkv_moment, proj_moment, fc1_moment, fc2_moment))
    share, count = qkv_w.shape
    vec_rows = vectors.shape[0]
    first_lanes = width
    later_lanes = 2 * width + SUB

    table = device_numbers(lax.axis_size("dp"), ns, share, width, proj_w.shape[1])
    device = lax.axis_index("dp") * ns + lax.axis_index("ns")
    numbers = lax.dynamic_slice(jnp.asarray(table), (device, 0), (1, table.shape[1]))[0]

    row_ids = jnp.where(
        valid_rows > 0, segment, rows + jnp.arange(rows, dtype=jnp.int32)
    ).astype(F32)
    ids = jnp.pad(row_ids, (MARGIN, MARGIN), constant_values=-1.0).reshape(-1, SUB)
    ids = jnp.pad(ids, ((0, -ids.shape[0] % 8), (0, 0)), constant_values=-1.0)

    later_own = widened([fc1_w, fc2_w, proj_w], later_lanes).astype(LOW)
    later_pair = jnp.stack([later_own, exchange(later_own, "ns", ns // 2)])
    first_own = widened([qkv_w, vectors.T], first_lanes).astype(LOW)
    prepared = prepare(tokens, cotangent, ids)
    first_columns, prepared = lax.optimization_barrier((over_columns(first_own), prepared))
    normed, normed_turned, out_turned, columns, out_sums = prepared
    first_pieces = over_rows(first_columns)
    later_near = from_columns(later_pair)
    if share % 16:
        later_near = jnp.moveaxis(later_near, 0, 1).reshape(1, ns // 2, width, later_lanes)

    query, _, value, key_turned, mixed, probs, weight, vector_full = attend_forward(
        numbers, first_pieces, normed, ids, columns
    )
    later_near, mixed = lax.optimization_barrier((later_near, mixed))
    later_far = exchange(later_near, "ns", 1)
    output, grad_residual, grad_mixed, inner, grads_near, grads_far, sums = mlp_both(
        numbers, later_near, later_far, vector_full, mixed, tokens, cotangent, out_turned, out_sums
    )
    held = added(grads_near, exchange(grads_far, "ns", 1))
    held, grad_mixed = lax.optimization_barrier((held, grad_mixed))
    if share % 16:
        held = jnp.moveaxis(held.reshape(ns // 2, -1, share, later_lanes), 1, 0)
    later_got = lax.all_to_all(held, "dp", split_axis=0, concat_axis=0, tiled=True)

    grad_qkv, grads_near, grads_far = attend_backward(
        numbers, ns, query, key_turned, value, probs, inner, grad_mixed, normed_turned, weight,
        vector_full, sums,
    )
    held = added(grads_near, exchange(grads_far, "ns", 1))
    got = exchange(held[1], "ns", ns // 2)
    input_grad = input_gradient(weight, vector_full, tokens, grad_residual, grad_qkv)
    got, input_grad, later_got = lax.optimization_barrier((got, input_grad, later_got))
    first_held = added(held[0], got)
    first_owned = sum_columns(first_held.reshape(lax.axis_size("dp"), share, first_lanes))

    later_sums = summed(later_got)
    later_owned = later_sums[0] + exchange(later_sums[1].astype(LOW), "ns", ns // 2).astype(F32)
    later_moment = later_owned + 0.5 * widened([fc1_m, fc2_m, proj_m], later_lanes)
    first_moment = first_owned + 0.5 * widened([qkv_m], first_lanes)
    later_low, first_low = later_moment.astype(LOW), first_moment.astype(LOW)
    pieces, at = columns_direct(later_low, first_low)
    columns, *chosen = pick(numbers, pieces, ns)
    blocks = [chosen[0]] + [exchange(chosen[mask], "ns", mask) for mask in range(1, ns)]
    left = newton(at, numbers, blocks, share)

    first_own = over_columns(first_low)
    first_pieces = [first_own] + [exchange(first_own, "ns", mask) for mask in range(1, ns)]
    qkv_new = muon(count * ns, numbers, first_pieces, qkv_w)

    lefts = [left] + [exchange(left, "ns", mask) for mask in range(1, ns)]
    fc1_new, fc2_new, proj_new = finish(
        [w.shape[1] * ns for w in (fc1_w, fc2_w, proj_w)],
        (0, width, 2 * width),
        numbers,
        columns,
        lefts,
        (fc1_w, fc2_w, proj_w),
    )

    news = (qkv_new, proj_new, fc1_new, fc2_new)
    moments_new = (
        first_moment[:, :count],
        later_moment[:, 2 * width : 2 * width + proj_w.shape[1]],
        later_moment[:, :width],
        later_moment[:, width : 2 * width],
    )

    vector_grad = first_owned[:, count : count + vec_rows].T
    first_new = BETA_ONE * vector_moment + (1.0 - BETA_ONE) * vector_grad
    second_new = BETA_TWO * vector_square + (1.0 - BETA_TWO) * vector_grad * vector_grad
    first_hat = first_new / (1.0 - BETA_ONE**STEP)
    second_hat = second_new / (1.0 - BETA_TWO**STEP)
    vectors_new = vectors - ADAM_RATE * first_hat / (jnp.sqrt(second_hat) + ADAM_EPS)
    return (
        output,
        input_grad,
        *(new[0].T for new in news),
        *(m.T for m in moments_new),
        first_new,
        second_new,
        vectors_new,
        *(new[1].T for new in news),
    )


def solution(mesh):
    rows = P(("dp", "ns"), None)
    flat = P(("dp", "ns"))
    block = P("ns", "dp")
    return jax.shard_map(
        per_device,
        mesh=mesh,
        in_specs=(rows, rows, flat, flat) + (block,) * 11,
        out_specs=(rows, rows) + (block,) * 15,
        check_vma=False,
    )
```

```python
import functools
import math

import jax
import jax.numpy as jnp
import numpy as np
from jax import lax
from jax.experimental import pallas as pl
from jax.experimental.pallas import tpu as pltpu
from jax.sharding import PartitionSpec as P

HEADS = 6
PAIRS = 3
MARGIN = 128
NS_STEPS = 5
STEP = 10
TILE = 512
MLP_TILE = 512
FF_CHUNK = 256
SUB = 128
SPAN = 384
VEC_LANES = 16
GROUP = 2


EPS_NORM = 1e-06
NEWTON_A = 3.4445
NEWTON_B = -4.775
NEWTON_C = 2.0315
MUON_RATE = 0.2
MUON_DECAY = 0.1
ADAM_RATE = 0.4
BETA_ONE = 0.9
BETA_TWO = 0.999
ADAM_EPS = 1e-08
LOW = jnp.bfloat16
F32 = jnp.float32
TN = (((0,), (0,)), ((), ()))
NT = (((1,), (1,)), ((), ()))
NN = (((1,), (0,)), ((), ()))
VMEM_LIMIT = 56 * 1024 * 1024
ERF_P = 0.3275911
ERF_COEFS = (0.254829592, -0.284496736, 1.421413741, -1.453152027, 1.061405429)


def dot(left, right, dims=NN):
    return lax.dot_general(left, right, dims, preferred_element_type=F32)


PLACES, OWNERS, STARTS, WHICH, OFFSET, LOW_LANE, HIGH_LANE, COLUMN = 0, 4, 8, 12, 16, 17, 18, 19


def lane_numbers(shape):
    return lax.broadcasted_iota(jnp.int32, shape, len(shape) - 1)


def norm_parts(value):
    center = value - jnp.mean(value, axis=-1, keepdims=True)
    rate = lax.rsqrt(jnp.mean(center * center, axis=-1, keepdims=True) + EPS_NORM)
    return center * rate, rate


def norm_back(grad, normed, rate, gain):
    scaled = grad * gain
    first = jnp.mean(scaled, axis=-1, keepdims=True)
    second = jnp.mean(scaled * normed, axis=-1, keepdims=True)
    return rate * (scaled - first - normed * second)


def gelu_both(value):
    below = 1.0 + (ERF_P * 0.5**0.5) * jnp.abs(value)
    ratio = pl.reciprocal(below, approx=True)
    ratio = ratio * (2.0 - below * ratio)
    decay = jnp.exp2((value * value) * (-0.5 * math.log2(math.e)))
    poly = 0.5 * ERF_COEFS[4]
    for coef in ERF_COEFS[3::-1]:
        poly = poly * ratio + 0.5 * coef
    tail = poly * ratio * decay
    phi = jnp.where(value >= 0, 1.0 - tail, tail)
    return value * phi, phi + (value * (1.0 / math.sqrt(2.0 * math.pi))) * decay


def gelu_rows(hidden, bias, grad, between):
    active, back = [], []
    rows = hidden.shape[0]
    pieces = rows // 16
    for n in range(pieces):
        if n * len(between) // pieces != (n - 1) * len(between) // pieces:
            between[n * len(between) // pieces]()
        here = slice(n * 16, (n + 1) * 16)
        value, slope = gelu_both(hidden[here] + bias)
        active.append(value.astype(LOW))
        back.append((grad[here] * slope).astype(LOW))
    return jnp.concatenate(active, axis=0), jnp.concatenate(back, axis=0)


def halves_of(lanes):
    half = lanes.shape[0] // 2
    return lanes[:half, :SUB], lanes[half:, SUB:]


def staged(count, first, second, third):
    made = first(0)
    kept = None
    for n in range(count):
        coming = first(n + 1) if n + 1 < count else None
        if kept is not None:
            third(n - 1, kept)
        kept = second(n, made)
        made = coming
    third(count - 1, kept)


def both_heads(pair):
    first = (lane_numbers((1, SUB)) < SUB // 2).astype(F32).astype(pair.dtype)
    second = (lane_numbers((1, SUB)) >= SUB // 2).astype(F32).astype(pair.dtype)
    return jnp.concatenate([pair * first, pair * second], axis=0)


def fetch(pairs, sems):
    copies = [
        pltpu.make_async_copy(source, target, sems.at[n])
        for n, (source, target) in enumerate(pairs)
    ]
    for copy in copies:
        copy.start()
    for copy in copies:
        copy.wait()


def prepare_kernel(tokens, cotangent, ids, normed, normed_turned, out_turned, columns, sums):
    step = pl.program_id(0)
    parts = columns.shape[0] // SUB

    @pl.when(step == 0)
    def clear():
        sums[...] = jnp.zeros(sums.shape, F32)
        for number in range(parts):
            row = jnp.broadcast_to(ids[number : number + 1, :], (SUB, SUB))
            columns[number * SUB : (number + 1) * SUB, :] = row.T

    value, _ = norm_parts(tokens[...].astype(F32))
    normed[...] = value
    normed_turned[...] = value.astype(LOW).T
    out_low = cotangent[...]
    out_turned[...] = out_low.T
    sums[0:1, :] += jnp.sum(out_low.astype(F32), axis=0, keepdims=True)


def prepare(tokens, cotangent, ids):
    rows, width = tokens.shape
    padded = rows + 2 * MARGIN
    tile = pl.BlockSpec((TILE, width), lambda s: (s, 0))
    turned = pl.BlockSpec((width, TILE), lambda s: (0, s))
    whole = lambda *dims: pl.BlockSpec(dims, lambda s: (0,) * len(dims))
    return pl.pallas_call(
        prepare_kernel,
        grid=(rows // TILE,),
        in_specs=[tile, tile, whole(*ids.shape)],
        out_specs=[tile, turned, turned, whole(padded, SUB), whole(8, width)],
        out_shape=[
            jax.ShapeDtypeStruct((rows, width), F32),
            jax.ShapeDtypeStruct((width, rows), LOW),
            jax.ShapeDtypeStruct((width, rows), LOW),
            jax.ShapeDtypeStruct((padded, SUB), F32),
            jax.ShapeDtypeStruct((8, width), F32),
        ],
        compiler_params=pltpu.CompilerParams(vmem_limit_bytes=VMEM_LIMIT),
        cost_estimate=pl.CostEstimate(
            flops=20_000_000, bytes_accessed=12_000_000, transcendentals=2048
        ),
        name="prepare",
    )(tokens, cotangent, ids)


def attend_kernel(numbers, *refs):
    (normed, ids, columns, query, key, value, key_turned, mixed, probs, weight, vectors,
     gathered, pair_weight, value_turned, shifts, sems) = refs[-16:]
    pieces = refs[:-16]
    step = pl.program_id(0)
    chunks = pl.num_programs(0) - 1
    width = normed.shape[1]
    parts = len(pieces)
    block = 3 * width // parts
    rows_each = 12 // parts

    @pl.when(step == 0)
    def assemble():
        fetch([(piece, gathered.at[n]) for n, piece in enumerate(pieces)], sems)
        total = jnp.zeros((width, 3 * width), F32)
        turned = jnp.zeros((width, SUB), F32)
        for number in range(parts):
            piece = gathered[numbers[PLACES + number]].astype(F32)
            kept = jnp.where(lane_numbers(piece.shape) < block, piece, 0.0)
            wide = jnp.concatenate([kept, jnp.zeros((width, 2 * width), F32)], axis=1)
            total = total + (pltpu.roll(wide, block * number, 1) if number else wide)
            last = piece[:, 2 * SUB :]
            at = block - 2 * SUB
            lane = lane_numbers(last.shape)
            vec = jnp.where((lane >= at) & (lane < at + rows_each), last, 0.0)
            turned = turned + pltpu.roll(vec, (rows_each * number - at) % SUB, 1)
        total = total.astype(LOW)
        weight[...] = total
        pair_weight[...] = total[:, width:].T
        vectors[...] = turned.T[:VEC_LANES]
        shifts[...] = turned
        edges = (pl.ds(0, MARGIN), pl.ds(MARGIN + chunks * TILE, MARGIN))
        for edge in edges:
            for ref in (query, key, value):
                ref[edge, :] = jnp.zeros((MARGIN, width), LOW)
            for ref in (key_turned, value_turned):
                ref[:, edge] = jnp.zeros((width, MARGIN), LOW)

    @pl.when(step < chunks)
    def project():
        first_in = (normed[...] * vectors[0:1, :] + vectors[1:2, :]).astype(LOW)
        result = dot(first_in, weight[...])
        turned = dot(pair_weight[...], first_in, NT)
        here = pl.ds(pl.multiple_of(MARGIN + step * TILE, SUB), TILE)
        scale = (width // HEADS) ** (-0.5)
        made = (result[:, :width] + vectors[2:3, :]).astype(LOW) * jnp.asarray(scale, LOW)
        query[here, :] = made
        key[here, :] = result[:, width : 2 * width].astype(LOW)
        value[here, :] = (result[:, 2 * width :] + vectors[3:4, :]).astype(LOW)
        key_turned[:, here] = turned[:width].astype(LOW)
        value_turned[:, here] = (turned[width:] + shifts[:, 3:4]).astype(LOW)

    @pl.when(step > 0)
    def attend():
        def place(number):
            sub, pair = number // PAIRS, number % PAIRS
            tile = (step - 1) * (TILE // SUB) + sub
            start = pl.multiple_of(tile * SUB, SUB)
            return sub, pair, tile, start, pl.ds(start, SPAN), pl.ds(pair * SUB, SUB)

        def of_group(group):
            return range(group * GROUP, (group + 1) * GROUP)

        def score(group):
            made = []
            for number in of_group(group):
                _, _, _, start, near_rows, heads = place(number)
                wanted = both_heads(query[pl.ds(start + MARGIN, SUB), heads])
                made.append(dot(key[near_rows, heads], wanted, NT))
            return made

        def soften(group, made):
            own = []
            for number, scores in zip(of_group(group), made):
                _, _, tile, _, near_rows, _ = place(number)
                same = columns[near_rows, :] == ids[pl.ds(tile + 1, 1), :]
                own += [
                    jnp.where(same, scores[:, head * SUB : (head + 1) * SUB], -1e30)
                    for head in range(2)
                ]
            largest = [jnp.max(part, axis=0, keepdims=True) for part in own]
            expo = [jnp.exp(part - most) for part, most in zip(own, largest)]
            share = [1.0 / jnp.sum(part, axis=0, keepdims=True) for part in expo]
            scaled = [(part * by).astype(LOW) for part, by in zip(expo, share)]
            result = []
            for n, number in enumerate(of_group(group)):
                sub, pair, _, _, _, _ = place(number)
                result.append(jnp.concatenate(scaled[2 * n : 2 * n + 2], axis=1))
                probs[pair, sub] = result[-1]
            return result

        def mix(group, kept):
            for number, prob in zip(of_group(group), kept):
                sub, _, _, _, near_rows, heads = place(number)
                first, second = halves_of(dot(value_turned[heads, near_rows], prob))
                turned = jnp.concatenate([first, second], axis=0).astype(LOW)
                mixed[pl.ds(sub * SUB, SUB), heads] = turned.T

        staged(TILE // SUB * PAIRS // GROUP, score, soften, mix)


def attend_forward(numbers, pieces, normed, ids, columns):
    rows, width = normed.shape
    chunks = rows // TILE
    tiles = TILE // SUB
    parts = len(pieces)
    now = lambda s: jnp.minimum(s, chunks - 1)
    before = lambda s: jnp.maximum(s - 1, 0)
    whole = lambda *dims: pl.BlockSpec(dims, lambda s, *_: (0,) * len(dims))
    padded = rows + 2 * MARGIN
    return pl.pallas_call(
        attend_kernel,
        grid_spec=pltpu.PrefetchScalarGridSpec(
            num_scalar_prefetch=1,
            grid=(chunks + 1,),
            in_specs=[pl.BlockSpec(memory_space=pl.ANY)] * parts
            + [
                pl.BlockSpec((TILE, width), lambda s, *_: (now(s), 0)),
                whole(*ids.shape),
                whole(*columns.shape),
            ],
            out_specs=[
                whole(padded, width),
                whole(padded, width),
                whole(padded, width),
                whole(width, padded),
                pl.BlockSpec((TILE, width), lambda s, *_: (before(s), 0)),
                pl.BlockSpec((PAIRS, tiles, SPAN, 2 * SUB), lambda s, *_: (0, before(s), 0, 0)),
                whole(width, 3 * width),
                whole(VEC_LANES, width),
            ],
            scratch_shapes=[
                pltpu.VMEM((parts, *pieces[0].shape), LOW),
                pltpu.VMEM((2 * width, width), LOW),
                pltpu.VMEM((width, padded), LOW),
                pltpu.VMEM((width, SUB), F32),
                pltpu.SemaphoreType.DMA((parts,)),
            ],
        ),
        out_shape=[
            jax.ShapeDtypeStruct((padded, width), LOW),
            jax.ShapeDtypeStruct((padded, width), LOW),
            jax.ShapeDtypeStruct((padded, width), LOW),
            jax.ShapeDtypeStruct((width, padded), LOW),
            jax.ShapeDtypeStruct((rows, width), LOW),
            jax.ShapeDtypeStruct((PAIRS, rows // SUB, SPAN, 2 * SUB), LOW),
            jax.ShapeDtypeStruct((width, 3 * width), LOW),
            jax.ShapeDtypeStruct((VEC_LANES, width), F32),
        ],
        compiler_params=pltpu.CompilerParams(vmem_limit_bytes=VMEM_LIMIT),
        cost_estimate=pl.CostEstimate(
            flops=12_000_000_000, bytes_accessed=22_000_000, transcendentals=5_000_000
        ),
        name="attend_forward",
    )(numbers, *pieces, normed, ids, columns)


def mlp_kernel(numbers, near, far, *refs):
    (vectors, mixed, tokens, cotangent, out_turned, out_sums, output, grad_residual, grad_mixed, inner, grads_near,
     grads_far, sums, one, two, proj_parts, proj, acc_one, acc_two, acc_proj, bias
    ) = refs
    step = pl.program_id(0)
    width = tokens.shape[1]
    mid = near.shape[1]
    parts = mid + far.shape[1]
    block = width // parts
    last_at = 2 * width
    hidden_width = one.shape[1]

    @pl.when(step == 0)
    def assemble():
        for part in range(parts):
            ref, at = (near, part) if part < mid else (far, part - mid)
            lanes = pl.ds(part * width, width)
            for group in range(near.shape[0]):
                here = pl.ds(group * near.shape[2], near.shape[2])
                one[here, lanes] = ref[group, at, :, :width]
                two[here, lanes] = ref[group, at, :, width:last_at]
                proj_parts[part, here, :] = ref[group, at, :, last_at:]
        total = jnp.zeros((width, width), F32)
        for number in range(parts):
            piece = proj_parts[numbers[PLACES + number]].astype(F32)
            kept = jnp.where(lane_numbers(piece.shape) < block, piece, 0.0)
            wide = jnp.concatenate([kept, jnp.zeros((width, width - SUB), F32)], axis=1)
            total = total + (pltpu.roll(wide, block * number, 1) if number else wide)
        proj[...] = total.astype(LOW)
        for part in range(parts):
            row = vectors[pl.ds(8 + numbers[OWNERS + part], 1), :]
            bias[0:1, part * width : (part + 1) * width] = row
        acc_one[...] = jnp.zeros(acc_one.shape, F32)
        acc_two[...] = jnp.zeros(acc_two.shape, F32)
        acc_proj[...] = jnp.zeros(acc_proj.shape, F32)
        sums[...] = jnp.zeros(sums.shape, F32)
        sums[7:8, :] = out_sums[0:1, :]

    def add_row(row, values):
        sums[pl.ds(row, 1), :] += jnp.sum(values, axis=0, keepdims=True)

    own = mixed[...]
    residual = tokens[...].astype(F32) + dot(own, proj[...], NT) + vectors[4:5, :]
    normed, rate = norm_parts(residual)
    gain = vectors[5:6, :]
    second_in = (normed * gain + vectors[6:7, :]).astype(LOW)
    out_low = cotangent[...]
    grad_out = out_low.astype(F32)
    second_turned = second_in.T
    out_turned = out_turned[...]
    totals = [residual + vectors[7:8, :], jnp.zeros(residual.shape, F32)]

    count = hidden_width // FF_CHUNK
    ones = jnp.ones((16, MLP_TILE), LOW)
    second_and_ones = jnp.concatenate([second_turned, ones], axis=0)
    hiddens, slopes, kept = {}, {}, {}

    def lanes_of(number):
        return pl.ds(number * FF_CHUNK, FF_CHUNK)

    def make_hidden(number):
        hiddens[number] = dot(second_in, one[:, lanes_of(number)])

    def make_slope(number):
        slopes[number] = dot(out_low, two[:, lanes_of(number)])

    def add_one(number):
        acc_one[:, lanes_of(number)] += dot(second_and_ones, kept[number][1])

    def add_two(number):
        acc_two[:, lanes_of(number)] += dot(out_turned, kept[number][0])

    def add_result(number):
        totals[0] = totals[0] + dot(kept[number][0], two[:, lanes_of(number)], NT)

    def add_second(number):
        totals[1] = totals[1] + dot(kept[number][1], one[:, lanes_of(number)], NT)

    make_hidden(0)
    make_slope(0)
    for number in range(count):
        between = []
        if number + 1 < count:
            between += [functools.partial(f, number + 1) for f in (make_hidden, make_slope)]
        if number > 0:
            between += [
                functools.partial(f, number - 1)
                for f in (add_result, add_second, add_one, add_two)
            ]
        kept[number] = gelu_rows(
            hiddens.pop(number), bias[0:1, lanes_of(number)], slopes.pop(number), between
        )
    for f in (add_result, add_second, add_one, add_two):
        f(count - 1)
    result, grad_second = totals
    output[...] = result.astype(LOW)
    add_row(5, grad_second * normed)
    add_row(6, grad_second)
    grad_res = grad_out + norm_back(grad_second, normed, rate, gain)
    grad_residual[...] = grad_res
    branch = grad_res.astype(LOW)
    add_row(4, branch.astype(F32))
    acc_proj[...] += dot(branch.T, own)
    grad_own = dot(branch, proj[...]).astype(LOW)
    grad_mixed[...] = grad_own
    high, rest = halves(grad_own.astype(F32) * own.astype(F32))
    head = lax.broadcasted_iota(jnp.int32, (16, width), 0)
    chosen = (lane_numbers((16, width)) // (width // HEADS) == head).astype(F32).astype(LOW)
    inner[...] = (dot(chosen, high, NT) + dot(chosen, rest, NT))[:8]

    @pl.when(step == pl.num_programs(0) - 1)
    def finish():
        total = acc_proj[...]
        for number in range(parts):
            turned = pltpu.roll(total, (width - block * number) % width, 1) if number else total
            proj_parts[numbers[PLACES + number]] = turned[:, :SUB].astype(LOW)
        for part in range(parts):
            ref, at = (grads_near, part) if part < mid else (grads_far, part - mid)
            lanes = pl.ds(part * width, width)
            for group in range(ref.shape[0]):
                here = pl.ds(group * ref.shape[2], ref.shape[2])
                ref[group, at, :, :width] = acc_one[here, lanes].astype(LOW)
                ref[group, at, :, width:last_at] = acc_two[here, lanes].astype(LOW)
                ref[group, at, :, last_at:] = proj_parts[part, here, :]
            sums[pl.ds(8 + numbers[OWNERS + part], 1), :] = acc_one[width : width + 1, lanes]


def mlp_both(numbers, near, far, vectors, mixed, tokens, cotangent, out_turned, out_sums):
    rows, width = tokens.shape
    parts = near.shape[1] + far.shape[1]
    hidden_width = parts * width
    tile = pl.BlockSpec((MLP_TILE, width), lambda s, *_: (s, 0))
    whole = lambda *dims: pl.BlockSpec(dims, lambda s, *_: (0,) * len(dims))
    return pl.pallas_call(
        mlp_kernel,
        grid_spec=pltpu.PrefetchScalarGridSpec(
            num_scalar_prefetch=1,
            grid=(rows // MLP_TILE,),
            in_specs=[
                whole(*near.shape), whole(*far.shape), whole(*vectors.shape), tile, tile, tile,
                pl.BlockSpec((width, MLP_TILE), lambda s, *_: (0, s)), whole(*out_sums.shape),
            ],
            out_specs=[
                tile,
                tile,
                tile,
                pl.BlockSpec((8, MLP_TILE), lambda s, *_: (0, s)),
                whole(*near.shape),
                whole(*far.shape),
                whole(*vectors.shape),
            ],
            scratch_shapes=[
                pltpu.VMEM((width, hidden_width), LOW),
                pltpu.VMEM((width, hidden_width), LOW),
                pltpu.VMEM((parts, width, SUB), LOW),
                pltpu.VMEM((width, width), LOW),
                pltpu.VMEM((width + 16, hidden_width), F32),
                pltpu.VMEM((width, hidden_width), F32),
                pltpu.VMEM((width, width), F32),
                pltpu.VMEM((8, hidden_width), F32),
            ],
        ),
        out_shape=[
            jax.ShapeDtypeStruct((rows, width), LOW),
            jax.ShapeDtypeStruct((rows, width), F32),
            jax.ShapeDtypeStruct((rows, width), LOW),
            jax.ShapeDtypeStruct((8, rows), F32),
            jax.ShapeDtypeStruct(near.shape, LOW),
            jax.ShapeDtypeStruct(far.shape, LOW),
            jax.ShapeDtypeStruct(vectors.shape, F32),
        ],
        compiler_params=pltpu.CompilerParams(vmem_limit_bytes=VMEM_LIMIT),
        cost_estimate=pl.CostEstimate(
            flops=34_000_000_000, bytes_accessed=20_000_000, transcendentals=6_000_000
        ),
        name="mlp_both",
    )(numbers, near, far, vectors, mixed, tokens, cotangent, out_turned, out_sums)


def attend_back_kernel(
    numbers,
    query,
    key_turned,
    value,
    probs,
    inner,
    grad_mixed,
    normed_turned,
    weight,
    vectors,
    sums,
    grad_qkv,
    near,
    far,
    grad_query,
    acc_key,
    acc_value,
    acc_sums,
    normed_sums,
    blocks,
    rows,
):
    step = pl.program_id(0)
    chunks = pl.num_programs(0) - 1
    pairs = range(PAIRS)
    count = len(pairs)
    scale = (SUB // 2) ** (-0.5)

    @pl.when(step == 0)
    def clear():
        acc_key[...] = jnp.zeros(acc_key.shape, F32)
        acc_value[...] = jnp.zeros(acc_value.shape, F32)
        normed_sums[...] = jnp.zeros(normed_sums.shape, F32)
        acc_sums[...] = jnp.zeros(acc_sums.shape, F32)

    @pl.when(step < chunks)
    def attend():
        def place(number):
            sub, at = number // count, number % count
            start = pl.multiple_of((step * (TILE // SUB) + sub) * SUB, SUB)
            return sub, at, start, pl.ds(start, SPAN), pl.ds(at * SUB, SUB)

        def slope(number):
            sub, _, _, near_rows, heads = place(number)
            grad = both_heads(grad_mixed[pl.ds(sub * SUB, SUB), heads])
            return dot(value[near_rows, heads], grad, NT)

        def soften(number, slopes):
            sub, at, _, _, _ = place(number)
            pair = pairs[at]
            cols = pl.ds(sub * SUB, SUB)
            both = []
            for head in range(2):
                lanes = slice(head * SUB, (head + 1) * SUB)
                less = slopes[:, lanes] - inner[2 * pair + head : 2 * pair + head + 1, cols]
                both.append((probs[at, sub, :, lanes].astype(F32) * less).astype(LOW))
            return jnp.concatenate(both, axis=1)

        def collect(number, scores):
            sub, at, start, near_rows, heads = place(number)
            first, second = halves_of(dot(key_turned[heads, near_rows], scores))
            turned = (jnp.concatenate([first, second], axis=0) * scale).astype(LOW)
            grad_query[pl.ds(start, SUB), heads] = turned.T
            wanted = both_heads(query[pl.ds(start + MARGIN, SUB), heads])
            acc_key[near_rows, heads] += dot(scores, wanted)
            grad = both_heads(grad_mixed[pl.ds(sub * SUB, SUB), heads])
            acc_value[near_rows, heads] += dot(probs[at, sub], grad)

        staged(TILE // SUB * count, slope, soften, collect)

    @pl.when(step > 0)
    def collect():
        here = pl.ds(pl.multiple_of((step - 1) * TILE, SUB), TILE)
        there = pl.ds(pl.multiple_of((step - 1) * TILE + MARGIN, SUB), TILE)
        parts = (
            grad_query[here, :],
            acc_key[there, :].astype(LOW),
            acc_value[there, :].astype(LOW),
        )
        joined = jnp.concatenate(parts, axis=1)
        grad_qkv[...] = joined
        normed_sums[...] += dot(normed_turned[...], joined)
        acc_sums[0:1, :] += jnp.sum(joined.astype(F32), axis=0, keepdims=True)

    @pl.when(step == chunks)
    def finish():
        weight_grad(
            numbers, normed_sums[...], acc_sums[0:1, :], weight, vectors, sums, near, far, blocks, rows
        )


def weight_grad(numbers, total, columns, weight, vectors, sums, near, far, blocks, rows):
    width = weight.shape[0]
    parts, mid = blocks.shape[0], near.shape[0]
    block = 3 * width // parts
    rows_each = 12 // parts
    wide = weight[...].astype(F32)
    grad_gain = jnp.sum(total * wide, axis=1, keepdims=True)
    grad_shift = jnp.sum(wide * columns, axis=1, keepdims=True)
    rows[...] = jnp.zeros(rows.shape, F32)
    rows[0:VEC_LANES, :] = sums[...]
    rows[2:3, :] = columns[:, :width]
    rows[3:4, :] = columns[:, 2 * width :]
    rows[VEC_LANES : 2 * VEC_LANES, :] = vectors[...]
    turned = rows[...].T
    gain = turned[:, VEC_LANES : VEC_LANES + 1]
    shift = turned[:, VEC_LANES + 1 : VEC_LANES + 2]
    lane = lane_numbers(turned.shape)
    turned = jnp.where(lane == 0, grad_gain, jnp.where(lane == 1, grad_shift, turned))
    total = total * gain + shift * columns
    at = block - 2 * SUB
    for number in range(parts):
        away = (3 * width - block * number) % (3 * width)
        piece = (pltpu.roll(total, away, 1) if number else total)[:, :width]
        vec = pltpu.roll(turned, (at - rows_each * number) % SUB, 1)
        last = jnp.where(lane < at, piece[:, 2 * SUB :], 0.0)
        last = jnp.where((lane >= at) & (lane < at + rows_each), vec, last)
        at_place = numbers[PLACES + number]
        blocks[at_place, :, : 2 * SUB] = piece[:, : 2 * SUB].astype(LOW)
        blocks[at_place, :, 2 * SUB :] = last.astype(LOW)
    near[...] = blocks[:mid]
    far[...] = blocks[mid:]


def attend_backward(
    numbers, parts, query, key_turned, value, probs, inner, grad_mixed, normed_turned, weight,
    vectors, sums,
):
    width, rows = normed_turned.shape
    padded = query.shape[0]
    chunks = rows // TILE
    tiles = TILE // SUB
    now = lambda s: jnp.minimum(s, chunks - 1)
    before = lambda s: jnp.maximum(s - 1, 0)
    whole = lambda *dims: pl.BlockSpec(dims, lambda s, *_: (0,) * len(dims))
    half = (parts // 2, width, width)
    return pl.pallas_call(
        attend_back_kernel,
        grid_spec=pltpu.PrefetchScalarGridSpec(
            num_scalar_prefetch=1,
            grid=(chunks + 1,),
            in_specs=[
                whole(padded, width),
                whole(width, padded),
                whole(padded, width),
                pl.BlockSpec((PAIRS, tiles, SPAN, 2 * SUB), lambda s, *_: (0, now(s), 0, 0)),
                pl.BlockSpec((8, TILE), lambda s, *_: (0, now(s))),
                pl.BlockSpec((TILE, width), lambda s, *_: (now(s), 0)),
                pl.BlockSpec((width, TILE), lambda s, *_: (0, before(s))),
                whole(*weight.shape),
                whole(*vectors.shape),
                whole(*sums.shape),
            ],
            out_specs=[
                pl.BlockSpec((TILE, 3 * width), lambda s, *_: (before(s), 0)),
                whole(*half),
                whole(*half),
            ],
            scratch_shapes=[
                pltpu.VMEM((rows, width), LOW),
                pltpu.VMEM((padded, width), F32),
                pltpu.VMEM((padded, width), F32),
                pltpu.VMEM((8, 3 * width), F32),
                pltpu.VMEM((width, 3 * width), F32),
                pltpu.VMEM((parts, width, width), LOW),
                pltpu.VMEM((SUB, width), F32),
            ],
        ),
        out_shape=[
            jax.ShapeDtypeStruct((rows, 3 * width), LOW),
            jax.ShapeDtypeStruct(half, LOW),
            jax.ShapeDtypeStruct(half, LOW),
        ],
        compiler_params=pltpu.CompilerParams(vmem_limit_bytes=VMEM_LIMIT),
        cost_estimate=pl.CostEstimate(
            flops=16_000_000_000, bytes_accessed=24_000_000, transcendentals=0
        ),
        name="attend_backward",
    )(
        numbers, query, key_turned, value, probs, inner, grad_mixed, normed_turned, weight, vectors,
        sums,
    )


def input_grad_kernel(weight, vectors, tokens, grad_residual, grad_qkv, input_grad):
    normed, rate = norm_parts(tokens[...].astype(F32))
    grad_first = dot(grad_qkv[...], weight[...], NT)
    back = norm_back(grad_first, normed, rate, vectors[0:1, :])
    input_grad[...] = (grad_residual[...] + back).astype(LOW)


def input_gradient(weight, vectors, tokens, grad_residual, grad_qkv):
    rows, width = tokens.shape
    size = TILE
    tile = pl.BlockSpec((size, width), lambda s: (s, 0))
    whole = lambda ref: pl.BlockSpec(ref.shape, lambda s: (0, 0))
    return pl.pallas_call(
        input_grad_kernel,
        grid=(rows // size,),
        in_specs=[
            whole(weight), whole(vectors), tile, tile,
            pl.BlockSpec((size, 3 * width), lambda s: (s, 0)),
        ],
        out_specs=tile,
        out_shape=jax.ShapeDtypeStruct((rows, width), LOW),
        compiler_params=pltpu.CompilerParams(vmem_limit_bytes=VMEM_LIMIT),
        cost_estimate=pl.CostEstimate(
            flops=4_000_000_000, bytes_accessed=13_000_000, transcendentals=2048
        ),
        name="input_gradient",
    )(weight, vectors, tokens, grad_residual, grad_qkv)


def halves(value):
    high = value.astype(LOW)
    return high, (value - high.astype(F32)).astype(LOW)


def dot_three(left, right):
    tall = jnp.concatenate([right[0], right[0], right[1]], axis=0)
    return dot(jnp.concatenate([left[0], left[1], left[0]], axis=1), tall)


def newton_rows(blocks, offset, rows):
    gram = dot(blocks[0], blocks[0], NT)
    for part in blocks[1:]:
        gram = gram + dot(part, part, NT)
    depth = gram.shape[0]
    down = lax.broadcasted_iota(jnp.int32, (depth, depth), 0)
    eye = (down == lane_numbers((depth, depth))).astype(F32)
    norm = 1.0 / (jnp.sqrt(jnp.sum(gram * eye, keepdims=True)) + 1e-07)
    gram = gram * (norm * norm)
    place = lax.broadcasted_iota(jnp.int32, (rows, depth), 0) + offset
    left = jnp.where(place == lane_numbers((rows, depth)), norm, 0.0)
    for step in range(NS_STEPS - 1):
        pair = halves(gram)
        poly = halves(NEWTON_A * eye + NEWTON_B * gram + NEWTON_C * dot_three(pair, pair))
        lefts = halves(left)
        both = dot_three([jnp.concatenate([pair[n], lefts[n]], axis=0) for n in range(2)], poly)
        left = both[depth:]
        gram = dot_three(halves(both[:depth]), poly)
    pair = halves(gram)
    once = dot_three(halves(left), pair)
    return NEWTON_A * left + NEWTON_B * once + NEWTON_C * dot_three(halves(once), pair)


def stepped(left, own, height, old):
    high, rest = halves(left)
    ortho = (dot(high, own) + dot(rest, own))[: old.shape[0], : old.shape[1]]
    return old * (1.0 - MUON_RATE * MUON_DECAY) - (MUON_RATE * 0.2 * math.sqrt(height)) * ortho


def kept_lanes(value, low, high):
    lane = lane_numbers(value.shape)
    return jnp.where((lane >= low) & (lane < high), value.astype(F32), 0.0).astype(LOW)


def tall_of(rows):
    return -(-rows // 16) * 16


def muon_kernel(height, numbers, *refs):
    old, new, copy = refs[-3:]
    count = old.shape[1]
    blocks = [kept_lanes(ref[...], 0, count) for ref in refs[:-3]]
    left = newton_rows(blocks, numbers[OFFSET], tall_of(old.shape[0]))
    result = stepped(left, blocks[0], height, old[...])
    new[...] = result
    copy[...] = result.astype(LOW)


def muon(height, numbers, blocks, old):
    vmem = pl.BlockSpec(memory_space=pltpu.VMEM)

    def kernel(*refs):
        muon_kernel(height, *refs)

    return pl.pallas_call(
        kernel,
        in_specs=[pl.BlockSpec(memory_space=pltpu.SMEM)] + [vmem] * (len(blocks) + 1),
        out_specs=[vmem, vmem],
        out_shape=[
            jax.ShapeDtypeStruct(old.shape, F32),
            jax.ShapeDtypeStruct(old.shape, LOW),
        ],
        compiler_params=pltpu.CompilerParams(vmem_limit_bytes=VMEM_LIMIT),
        cost_estimate=pl.CostEstimate(
            flops=9_000_000_000, bytes_accessed=2_000_000, transcendentals=10
        ),
        name="muon",
    )(numbers, *blocks, old)


def pick_kernel(count, numbers, *refs):
    pieces, columns, outs = refs[:count], refs[count], refs[count + 1 :]
    share = pieces[0].shape[0]
    for k, piece in enumerate(pieces):
        columns[k * share : (k + 1) * share, :] = piece[...]
        for n, out in enumerate(outs):
            at = pl.multiple_of(numbers[STARTS + n] * SUB, SUB)
            out[k * share : (k + 1) * share, :] = piece[:, pl.ds(at, out.shape[1])]


def pick(numbers, pieces, count):
    depth = len(pieces) * pieces[0].shape[0]
    vmem = pl.BlockSpec(memory_space=pltpu.VMEM)

    def kernel(*refs):
        pick_kernel(len(pieces), *refs)

    return pl.pallas_call(
        kernel,
        in_specs=[pl.BlockSpec(memory_space=pltpu.SMEM)] + [vmem] * len(pieces),
        out_specs=[vmem] * (count + 1),
        out_shape=[jax.ShapeDtypeStruct((depth, pieces[0].shape[1]), LOW)]
        + [jax.ShapeDtypeStruct((depth, depth), LOW)] * count,
        name="pick",
    )(numbers, *pieces)


def newton_kernel(at, numbers, *refs):
    left = refs[-1]
    bounds = numbers[LOW_LANE], numbers[HIGH_LANE]
    blocks = [kept_lanes(ref[...], *bounds) for ref in refs[:-1]]
    left[...] = newton_rows(blocks, numbers[OFFSET] if at is None else at, left.shape[0])


def newton(at, numbers, blocks, rows):
    vmem = pl.BlockSpec(memory_space=pltpu.VMEM)

    def kernel(*refs):
        newton_kernel(at, *refs)

    return pl.pallas_call(
        kernel,
        in_specs=[pl.BlockSpec(memory_space=pltpu.SMEM)] + [vmem] * len(blocks),
        out_specs=vmem,
        out_shape=jax.ShapeDtypeStruct((tall_of(rows), blocks[0].shape[0]), F32),
        compiler_params=pltpu.CompilerParams(vmem_limit_bytes=VMEM_LIMIT),
        cost_estimate=pl.CostEstimate(
            flops=9_000_000_000, bytes_accessed=2_000_000, transcendentals=10
        ),
        name="newton",
    )(numbers, *blocks)


def finish_kernel(heights, lanes, numbers, columns, *refs):
    count = len(heights)
    store = refs[-1]
    news = refs[-1 - 2 * count : -1]
    olds = refs[-1 - 3 * count : -1 - 2 * count]
    lefts = refs[: -1 - 3 * count]
    for n, left in enumerate(lefts):
        store[n] = left[...]
    for n in range(count):
        wide = -(-olds[n].shape[1] // SUB) * SUB
        own = columns[:, lanes[n] : lanes[n] + wide]
        result = stepped(store[numbers[WHICH + n]], own, heights[n], olds[n][...])
        news[2 * n][...] = result
        news[2 * n + 1][...] = result.astype(LOW)


def finish(heights, lanes, numbers, columns, lefts, olds):
    vmem = pl.BlockSpec(memory_space=pltpu.VMEM)
    count = len(olds)

    def kernel(*refs):
        finish_kernel(heights, lanes, *refs)

    outs = pl.pallas_call(
        kernel,
        in_specs=[pl.BlockSpec(memory_space=pltpu.SMEM)] + [vmem] * (1 + len(lefts) + count),
        out_specs=[vmem] * (2 * count),
        out_shape=[
            jax.ShapeDtypeStruct(old.shape, kind) for old in olds for kind in (F32, LOW)
        ],
        scratch_shapes=[pltpu.VMEM((len(lefts), *lefts[0].shape), F32)],
        compiler_params=pltpu.CompilerParams(vmem_limit_bytes=VMEM_LIMIT),
        cost_estimate=pl.CostEstimate(
            flops=200_000_000, bytes_accessed=2_000_000, transcendentals=0
        ),
        name="finish",
    )(numbers, columns, *lefts, *olds)
    return [(outs[2 * n], outs[2 * n + 1]) for n in range(count)]


def exchange(x, axis, mask):
    size = lax.axis_size(axis)
    return lax.ppermute(x, axis, [(i, i ^ mask) for i in range(size)])


def place_masks(size):
    masks = [0]
    bit = size // 2
    while bit >= 1:
        masks = masks + [m ^ bit for m in masks]
        bit //= 2
    return masks


def from_columns(own):
    size = lax.axis_size("dp")
    sent = jnp.broadcast_to(own[None], (size, *own.shape))
    return lax.all_to_all(sent, "dp", split_axis=0, concat_axis=0, tiled=True)


def over_columns(own):
    return from_columns(own).reshape(-1, own.shape[1])


def device_numbers(dp, ns, share, width, proj_rows):
    masks = place_masks(ns)
    tasks = [(0, 0, width), (width // SUB, 0, width)]
    tasks += [(width // SUB + 1, 2 * SUB, 2 * SUB + proj_rows)] * (ns - 2)
    table = np.zeros((dp * ns, 24), np.int32)
    for device in range(dp * ns):
        column, index = device // ns, device % ns
        row = table[device]
        for n in range(ns):
            row[OWNERS + n] = index ^ masks[n]
            row[PLACES + (index ^ masks[n])] = n
            row[STARTS + n] = tasks[index ^ n][0]
        for n in range(3):
            row[WHICH + n] = index ^ n
        row[OFFSET] = column * share
        row[COLUMN] = column
        row[LOW_LANE], row[HIGH_LANE] = tasks[index][1:]
    return table


def half_rows(own):
    held = [own]
    bit = lax.axis_size("ns") // 2
    while bit > 1:
        held = held + [exchange(block, "ns", bit) for block in held]
        bit //= 2
    return held


def added(keep, got):
    return (keep.astype(F32) + got.astype(F32)).astype(LOW)


def sum_columns(pieces):
    return summed(lax.all_to_all(pieces, "dp", split_axis=0, concat_axis=0, tiled=True))


def summed(pieces):
    return jnp.sum(pieces.astype(F32), axis=0)


def columns_direct(own, other):
    devices = lax.axis_size("dp")
    if devices > 8 or own.shape[0] % 16:
        return [over_columns(own)], None
    pieces = [own] + [exchange(own, "dp", mask) for mask in range(1, devices // 2)]
    again, _ = lax.optimization_barrier((own, other))
    return pieces + [exchange(again, "dp", mask) for mask in range(devices // 2, devices)], 0


def widened(arrays, lanes):
    joined = jnp.concatenate(arrays, axis=1)
    return jnp.pad(joined, ((0, 0), (0, lanes - joined.shape[1])))


def per_device(
    tokens,
    cotangent,
    segment,
    valid_rows,
    qkv_weight,
    proj_weight,
    fc1_weight,
    fc2_weight,
    qkv_moment,
    proj_moment,
    fc1_moment,
    fc2_moment,
    vectors,
    vector_moment,
    vector_square,
):
    rows, width = tokens.shape
    ns = lax.axis_size("ns")
    qkv_w, proj_w, fc1_w, fc2_w = (w.T for w in (qkv_weight, proj_weight, fc1_weight, fc2_weight))
    qkv_m, proj_m, fc1_m, fc2_m = (w.T for w in (qkv_moment, proj_moment, fc1_moment, fc2_moment))
    share, count = qkv_w.shape
    vec_rows = vectors.shape[0]
    first_lanes = width
    later_lanes = 2 * width + SUB

    table = device_numbers(lax.axis_size("dp"), ns, share, width, proj_w.shape[1])
    device = lax.axis_index("dp") * ns + lax.axis_index("ns")
    numbers = lax.dynamic_slice(jnp.asarray(table), (device, 0), (1, table.shape[1]))[0]

    row_ids = jnp.where(
        valid_rows > 0, segment, rows + jnp.arange(rows, dtype=jnp.int32)
    ).astype(F32)
    ids = jnp.pad(row_ids, (MARGIN, MARGIN), constant_values=-1.0).reshape(-1, SUB)
    ids = jnp.pad(ids, ((0, -ids.shape[0] % 8), (0, 0)), constant_values=-1.0)

    later_own = widened([fc1_w, fc2_w, proj_w], later_lanes).astype(LOW)
    later_pair = jnp.stack([later_own, exchange(later_own, "ns", ns // 2)])
    first_own = widened([qkv_w, vectors.T], first_lanes).astype(LOW)
    prepared = prepare(tokens, cotangent, ids)
    first_pieces = half_rows(over_columns(first_own))
    first_pieces, prepared = lax.optimization_barrier((first_pieces, prepared))
    normed, normed_turned, out_turned, columns, out_sums = prepared
    first_pieces = first_pieces + [exchange(piece, "ns", 1) for piece in first_pieces]
    later_near = from_columns(later_pair)
    if share % 16:
        later_near = jnp.moveaxis(later_near, 0, 1).reshape(1, ns // 2, width, later_lanes)

    query, _, value, key_turned, mixed, probs, weight, vector_full = attend_forward(
        numbers, first_pieces, normed, ids, columns
    )
    later_near, mixed = lax.optimization_barrier((later_near, mixed))
    later_far = exchange(later_near, "ns", 1)
    output, grad_residual, grad_mixed, inner, grads_near, grads_far, sums = mlp_both(
        numbers, later_near, later_far, vector_full, mixed, tokens, cotangent, out_turned, out_sums
    )
    held = added(grads_near, exchange(grads_far, "ns", 1))
    held, grad_mixed = lax.optimization_barrier((held, grad_mixed))
    if share % 16:
        held = jnp.moveaxis(held.reshape(ns // 2, -1, share, later_lanes), 1, 0)
    later_got = lax.all_to_all(held, "dp", split_axis=0, concat_axis=0, tiled=True)

    grad_qkv, grads_near, grads_far = attend_backward(
        numbers, ns, query, key_turned, value, probs, inner, grad_mixed, normed_turned, weight,
        vector_full, sums,
    )
    held = added(grads_near, exchange(grads_far, "ns", 1))
    got = exchange(held[1], "ns", ns // 2)
    input_grad = input_gradient(weight, vector_full, tokens, grad_residual, grad_qkv)
    got, input_grad, later_got = lax.optimization_barrier((got, input_grad, later_got))
    first_held = added(held[0], got)
    first_owned = sum_columns(first_held.reshape(lax.axis_size("dp"), share, first_lanes))

    later_sums = summed(later_got)
    later_owned = later_sums[0] + exchange(later_sums[1].astype(LOW), "ns", ns // 2).astype(F32)
    later_moment = later_owned + 0.5 * widened([fc1_m, fc2_m, proj_m], later_lanes)
    first_moment = first_owned + 0.5 * widened([qkv_m], first_lanes)
    later_low, first_low = later_moment.astype(LOW), first_moment.astype(LOW)
    pieces, at = columns_direct(later_low, first_low)
    first_own = over_columns(first_low)
    pieces, first_own = lax.optimization_barrier((pieces, first_own))
    columns, *chosen = pick(numbers, pieces, ns)
    blocks = [chosen[0]] + [exchange(chosen[mask], "ns", mask) for mask in range(1, ns)]
    first_pieces = half_rows(first_own)
    left = newton(at, numbers, blocks, share)
    left, first_pieces = lax.optimization_barrier((left, first_pieces))
    first_pieces = first_pieces + [exchange(piece, "ns", 1) for piece in first_pieces]
    qkv_new = muon(count * ns, numbers, first_pieces, qkv_w)

    lefts = [left] + [exchange(left, "ns", mask) for mask in range(1, ns)]
    fc1_new, fc2_new, proj_new = finish(
        [w.shape[1] * ns for w in (fc1_w, fc2_w, proj_w)],
        (0, width, 2 * width),
        numbers,
        columns,
        lefts,
        (fc1_w, fc2_w, proj_w),
    )

    news = (qkv_new, proj_new, fc1_new, fc2_new)
    moments_new = (
        first_moment[:, :count],
        later_moment[:, 2 * width : 2 * width + proj_w.shape[1]],
        later_moment[:, :width],
        later_moment[:, width : 2 * width],
    )

    vector_grad = first_owned[:, count : count + vec_rows].T
    first_new = BETA_ONE * vector_moment + (1.0 - BETA_ONE) * vector_grad
    second_new = BETA_TWO * vector_square + (1.0 - BETA_TWO) * vector_grad * vector_grad
    first_hat = first_new / (1.0 - BETA_ONE**STEP)
    second_hat = second_new / (1.0 - BETA_TWO**STEP)
    vectors_new = vectors - ADAM_RATE * first_hat / (jnp.sqrt(second_hat) + ADAM_EPS)
    return (
        output,
        input_grad,
        *(new[0].T for new in news),
        *(m.T for m in moments_new),
        first_new,
        second_new,
        vectors_new,
        *(new[1].T for new in news),
    )


def solution(mesh):
    rows = P(("dp", "ns"), None)
    flat = P(("dp", "ns"))
    block = P("ns", "dp")
    return jax.shard_map(
        per_device,
        mesh=mesh,
        in_specs=(rows, rows, flat, flat) + (block,) * 11,
        out_specs=(rows, rows) + (block,) * 15,
        check_vma=False,
    )
```

```python
import functools
import math

import jax
import jax.numpy as jnp
import numpy as np
from jax import lax
from jax.experimental import pallas as pl
from jax.experimental.pallas import tpu as pltpu
from jax.sharding import PartitionSpec as P

HEADS = 6
PAIRS = 3
MARGIN = 128
NS_STEPS = 5
STEP = 10
TILE = 512
MLP_TILE = 512
FF_CHUNK = 256
SUB = 128
SPAN = 384
VEC_LANES = 16
GROUP = 2


EPS_NORM = 1e-06
NEWTON_A = 3.4445
NEWTON_B = -4.775
NEWTON_C = 2.0315
MUON_RATE = 0.2
MUON_DECAY = 0.1
ADAM_RATE = 0.4
BETA_ONE = 0.9
BETA_TWO = 0.999
ADAM_EPS = 1e-08
LOW = jnp.bfloat16
F32 = jnp.float32
TN = (((0,), (0,)), ((), ()))
NT = (((1,), (1,)), ((), ()))
NN = (((1,), (0,)), ((), ()))
VMEM_LIMIT = 56 * 1024 * 1024
ERF_P = 0.3275911
ERF_COEFS = (0.254829592, -0.284496736, 1.421413741, -1.453152027, 1.061405429)


def dot(left, right, dims=NN):
    return lax.dot_general(left, right, dims, preferred_element_type=F32)


PLACES, OWNERS, STARTS, WHICH, OFFSET, LOW_LANE, HIGH_LANE, COLUMN = 0, 4, 8, 12, 16, 17, 18, 19


def lane_numbers(shape):
    return lax.broadcasted_iota(jnp.int32, shape, len(shape) - 1)


def norm_parts(value):
    center = value - jnp.mean(value, axis=-1, keepdims=True)
    rate = lax.rsqrt(jnp.mean(center * center, axis=-1, keepdims=True) + EPS_NORM)
    return center * rate, rate


def norm_back(grad, normed, rate, gain):
    scaled = grad * gain
    first = jnp.mean(scaled, axis=-1, keepdims=True)
    second = jnp.mean(scaled * normed, axis=-1, keepdims=True)
    return rate * (scaled - first - normed * second)


def gelu_both(value):
    below = 1.0 + (ERF_P * 0.5**0.5) * jnp.abs(value)
    ratio = pl.reciprocal(below, approx=True)
    ratio = ratio * (2.0 - below * ratio)
    decay = jnp.exp2((value * value) * (-0.5 * math.log2(math.e)))
    poly = 0.5 * ERF_COEFS[4]
    for coef in ERF_COEFS[3::-1]:
        poly = poly * ratio + 0.5 * coef
    tail = poly * ratio * decay
    phi = jnp.where(value >= 0, 1.0 - tail, tail)
    return value * phi, phi + (value * (1.0 / math.sqrt(2.0 * math.pi))) * decay


def gelu_rows(hidden, bias, grad, between):
    active, back = [], []
    rows = hidden.shape[0]
    pieces = rows // 16
    for n in range(pieces):
        if n * len(between) // pieces != (n - 1) * len(between) // pieces:
            between[n * len(between) // pieces]()
        here = slice(n * 16, (n + 1) * 16)
        value, slope = gelu_both(hidden[here] + bias)
        active.append(value.astype(LOW))
        back.append((grad[here] * slope).astype(LOW))
    return jnp.concatenate(active, axis=0), jnp.concatenate(back, axis=0)


def halves_of(lanes):
    half = lanes.shape[0] // 2
    return lanes[:half, :SUB], lanes[half:, SUB:]


def staged(count, first, second, third):
    made = first(0)
    kept = None
    for n in range(count):
        coming = first(n + 1) if n + 1 < count else None
        if kept is not None:
            third(n - 1, kept)
        kept = second(n, made)
        made = coming
    third(count - 1, kept)


def both_heads(pair):
    first = (lane_numbers((1, SUB)) < SUB // 2).astype(F32).astype(pair.dtype)
    second = (lane_numbers((1, SUB)) >= SUB // 2).astype(F32).astype(pair.dtype)
    return jnp.concatenate([pair * first, pair * second], axis=0)


def fetch(pairs, sems):
    copies = [
        pltpu.make_async_copy(source, target, sems.at[n])
        for n, (source, target) in enumerate(pairs)
    ]
    for copy in copies:
        copy.start()
    for copy in copies:
        copy.wait()


def prepare_kernel(tokens, cotangent, ids, normed, normed_turned, out_turned, columns, sums):
    step = pl.program_id(0)
    parts = columns.shape[0] // SUB

    @pl.when(step == 0)
    def clear():
        sums[...] = jnp.zeros(sums.shape, F32)
        for number in range(parts):
            row = jnp.broadcast_to(ids[number : number + 1, :], (SUB, SUB))
            columns[number * SUB : (number + 1) * SUB, :] = row.T

    value, _ = norm_parts(tokens[...].astype(F32))
    normed[...] = value
    normed_turned[...] = value.astype(LOW).T
    out_low = cotangent[...]
    out_turned[...] = out_low.T
    sums[0:1, :] += jnp.sum(out_low.astype(F32), axis=0, keepdims=True)


def prepare(tokens, cotangent, ids):
    rows, width = tokens.shape
    padded = rows + 2 * MARGIN
    tile = pl.BlockSpec((TILE, width), lambda s: (s, 0))
    turned = pl.BlockSpec((width, TILE), lambda s: (0, s))
    whole = lambda *dims: pl.BlockSpec(dims, lambda s: (0,) * len(dims))
    return pl.pallas_call(
        prepare_kernel,
        grid=(rows // TILE,),
        in_specs=[tile, tile, whole(*ids.shape)],
        out_specs=[tile, turned, turned, whole(padded, SUB), whole(8, width)],
        out_shape=[
            jax.ShapeDtypeStruct((rows, width), F32),
            jax.ShapeDtypeStruct((width, rows), LOW),
            jax.ShapeDtypeStruct((width, rows), LOW),
            jax.ShapeDtypeStruct((padded, SUB), F32),
            jax.ShapeDtypeStruct((8, width), F32),
        ],
        compiler_params=pltpu.CompilerParams(vmem_limit_bytes=VMEM_LIMIT),
        cost_estimate=pl.CostEstimate(
            flops=20_000_000, bytes_accessed=12_000_000, transcendentals=2048
        ),
        name="prepare",
    )(tokens, cotangent, ids)


def attend_kernel(numbers, *refs):
    (normed, ids, columns, query, key, value, key_turned, mixed, probs, weight, vectors,
     gathered, pair_weight, value_turned, shifts, sems) = refs[-16:]
    pieces = refs[:-16]
    step = pl.program_id(0)
    chunks = pl.num_programs(0) - 1
    width = normed.shape[1]
    parts = len(pieces)
    block = 3 * width // parts
    rows_each = 12 // parts

    @pl.when(step == 0)
    def assemble():
        fetch([(piece, gathered.at[n]) for n, piece in enumerate(pieces)], sems)
        total = jnp.zeros((width, 3 * width), F32)
        turned = jnp.zeros((width, SUB), F32)
        for number in range(parts):
            piece = gathered[numbers[PLACES + number]].astype(F32)
            kept = jnp.where(lane_numbers(piece.shape) < block, piece, 0.0)
            wide = jnp.concatenate([kept, jnp.zeros((width, 2 * width), F32)], axis=1)
            total = total + (pltpu.roll(wide, block * number, 1) if number else wide)
            last = piece[:, 2 * SUB :]
            at = block - 2 * SUB
            lane = lane_numbers(last.shape)
            vec = jnp.where((lane >= at) & (lane < at + rows_each), last, 0.0)
            turned = turned + pltpu.roll(vec, (rows_each * number - at) % SUB, 1)
        total = total.astype(LOW)
        weight[...] = total
        pair_weight[...] = total[:, width:].T
        vectors[...] = turned.T[:VEC_LANES]
        shifts[...] = turned
        edges = (pl.ds(0, MARGIN), pl.ds(MARGIN + chunks * TILE, MARGIN))
        for edge in edges:
            for ref in (query, key, value):
                ref[edge, :] = jnp.zeros((MARGIN, width), LOW)
            for ref in (key_turned, value_turned):
                ref[:, edge] = jnp.zeros((width, MARGIN), LOW)

    @pl.when(step < chunks)
    def project():
        first_in = (normed[...] * vectors[0:1, :] + vectors[1:2, :]).astype(LOW)
        result = dot(first_in, weight[...])
        turned = dot(pair_weight[...], first_in, NT)
        here = pl.ds(pl.multiple_of(MARGIN + step * TILE, SUB), TILE)
        scale = (width // HEADS) ** (-0.5)
        made = (result[:, :width] + vectors[2:3, :]).astype(LOW) * jnp.asarray(scale, LOW)
        query[here, :] = made
        key[here, :] = result[:, width : 2 * width].astype(LOW)
        value[here, :] = (result[:, 2 * width :] + vectors[3:4, :]).astype(LOW)
        key_turned[:, here] = turned[:width].astype(LOW)
        value_turned[:, here] = (turned[width:] + shifts[:, 3:4]).astype(LOW)

    @pl.when(step > 0)
    def attend():
        def place(number):
            sub, pair = number // PAIRS, number % PAIRS
            tile = (step - 1) * (TILE // SUB) + sub
            start = pl.multiple_of(tile * SUB, SUB)
            return sub, pair, tile, start, pl.ds(start, SPAN), pl.ds(pair * SUB, SUB)

        def of_group(group):
            return range(group * GROUP, (group + 1) * GROUP)

        def score(group):
            made = []
            for number in of_group(group):
                _, _, _, start, near_rows, heads = place(number)
                wanted = both_heads(query[pl.ds(start + MARGIN, SUB), heads])
                made.append(dot(key[near_rows, heads], wanted, NT))
            return made

        def soften(group, made):
            own = []
            for number, scores in zip(of_group(group), made):
                _, _, tile, _, near_rows, _ = place(number)
                same = columns[near_rows, :] == ids[pl.ds(tile + 1, 1), :]
                own += [
                    jnp.where(same, scores[:, head * SUB : (head + 1) * SUB], -1e30)
                    for head in range(2)
                ]
            largest = [jnp.max(part, axis=0, keepdims=True) for part in own]
            expo = [jnp.exp(part - most) for part, most in zip(own, largest)]
            share = [1.0 / jnp.sum(part, axis=0, keepdims=True) for part in expo]
            scaled = [(part * by).astype(LOW) for part, by in zip(expo, share)]
            result = []
            for n, number in enumerate(of_group(group)):
                sub, pair, _, _, _, _ = place(number)
                result.append(jnp.concatenate(scaled[2 * n : 2 * n + 2], axis=1))
                probs[pair, sub] = result[-1]
            return result

        def mix(group, kept):
            for number, prob in zip(of_group(group), kept):
                sub, _, _, _, near_rows, heads = place(number)
                first, second = halves_of(dot(value_turned[heads, near_rows], prob))
                turned = jnp.concatenate([first, second], axis=0).astype(LOW)
                mixed[pl.ds(sub * SUB, SUB), heads] = turned.T

        staged(TILE // SUB * PAIRS // GROUP, score, soften, mix)


def attend_forward(numbers, pieces, normed, ids, columns):
    rows, width = normed.shape
    chunks = rows // TILE
    tiles = TILE // SUB
    parts = len(pieces)
    now = lambda s: jnp.minimum(s, chunks - 1)
    before = lambda s: jnp.maximum(s - 1, 0)
    whole = lambda *dims: pl.BlockSpec(dims, lambda s, *_: (0,) * len(dims))
    padded = rows + 2 * MARGIN
    return pl.pallas_call(
        attend_kernel,
        grid_spec=pltpu.PrefetchScalarGridSpec(
            num_scalar_prefetch=1,
            grid=(chunks + 1,),
            in_specs=[pl.BlockSpec(memory_space=pl.ANY)] * parts
            + [
                pl.BlockSpec((TILE, width), lambda s, *_: (now(s), 0)),
                whole(*ids.shape),
                whole(*columns.shape),
            ],
            out_specs=[
                whole(padded, width),
                whole(padded, width),
                whole(padded, width),
                whole(width, padded),
                pl.BlockSpec((TILE, width), lambda s, *_: (before(s), 0)),
                pl.BlockSpec((PAIRS, tiles, SPAN, 2 * SUB), lambda s, *_: (0, before(s), 0, 0)),
                whole(width, 3 * width),
                whole(VEC_LANES, width),
            ],
            scratch_shapes=[
                pltpu.VMEM((parts, *pieces[0].shape), LOW),
                pltpu.VMEM((2 * width, width), LOW),
                pltpu.VMEM((width, padded), LOW),
                pltpu.VMEM((width, SUB), F32),
                pltpu.SemaphoreType.DMA((parts,)),
            ],
        ),
        out_shape=[
            jax.ShapeDtypeStruct((padded, width), LOW),
            jax.ShapeDtypeStruct((padded, width), LOW),
            jax.ShapeDtypeStruct((padded, width), LOW),
            jax.ShapeDtypeStruct((width, padded), LOW),
            jax.ShapeDtypeStruct((rows, width), LOW),
            jax.ShapeDtypeStruct((PAIRS, rows // SUB, SPAN, 2 * SUB), LOW),
            jax.ShapeDtypeStruct((width, 3 * width), LOW),
            jax.ShapeDtypeStruct((VEC_LANES, width), F32),
        ],
        compiler_params=pltpu.CompilerParams(vmem_limit_bytes=VMEM_LIMIT),
        cost_estimate=pl.CostEstimate(
            flops=12_000_000_000, bytes_accessed=22_000_000, transcendentals=5_000_000
        ),
        name="attend_forward",
    )(numbers, *pieces, normed, ids, columns)


def mlp_kernel(numbers, near, far, *refs):
    (vectors, mixed, tokens, cotangent, out_turned, out_sums, output, grad_residual, grad_mixed, inner, grads_near,
     grads_far, sums, one, two, proj_parts, proj, acc_one, acc_two, acc_proj, bias
    ) = refs
    step = pl.program_id(0)
    width = tokens.shape[1]
    mid = near.shape[1]
    parts = mid + far.shape[1]
    block = width // parts
    last_at = 2 * width
    hidden_width = one.shape[1]

    @pl.when(step == 0)
    def assemble():
        for part in range(parts):
            ref, at = (near, part) if part < mid else (far, part - mid)
            lanes = pl.ds(part * width, width)
            for group in range(near.shape[0]):
                here = pl.ds(group * near.shape[2], near.shape[2])
                one[here, lanes] = ref[group, at, :, :width]
                two[here, lanes] = ref[group, at, :, width:last_at]
                proj_parts[part, here, :] = ref[group, at, :, last_at:]
        total = jnp.zeros((width, width), F32)
        for number in range(parts):
            piece = proj_parts[numbers[PLACES + number]].astype(F32)
            kept = jnp.where(lane_numbers(piece.shape) < block, piece, 0.0)
            wide = jnp.concatenate([kept, jnp.zeros((width, width - SUB), F32)], axis=1)
            total = total + (pltpu.roll(wide, block * number, 1) if number else wide)
        proj[...] = total.astype(LOW)
        for part in range(parts):
            row = vectors[pl.ds(8 + numbers[OWNERS + part], 1), :]
            bias[0:1, part * width : (part + 1) * width] = row
        acc_one[...] = jnp.zeros(acc_one.shape, F32)
        acc_two[...] = jnp.zeros(acc_two.shape, F32)
        acc_proj[...] = jnp.zeros(acc_proj.shape, F32)
        sums[...] = jnp.zeros(sums.shape, F32)
        sums[7:8, :] = out_sums[0:1, :]

    def add_row(row, values):
        sums[pl.ds(row, 1), :] += jnp.sum(values, axis=0, keepdims=True)

    own = mixed[...]
    residual = tokens[...].astype(F32) + dot(own, proj[...], NT) + vectors[4:5, :]
    normed, rate = norm_parts(residual)
    gain = vectors[5:6, :]
    second_in = (normed * gain + vectors[6:7, :]).astype(LOW)
    out_low = cotangent[...]
    grad_out = out_low.astype(F32)
    second_turned = second_in.T
    out_turned = out_turned[...]
    totals = [residual + vectors[7:8, :], jnp.zeros(residual.shape, F32)]

    count = hidden_width // FF_CHUNK
    ones = jnp.ones((16, MLP_TILE), LOW)
    second_and_ones = jnp.concatenate([second_turned, ones], axis=0)
    hiddens, slopes, kept = {}, {}, {}

    def lanes_of(number):
        return pl.ds(number * FF_CHUNK, FF_CHUNK)

    def make_hidden(number):
        hiddens[number] = dot(second_in, one[:, lanes_of(number)])

    def make_slope(number):
        slopes[number] = dot(out_low, two[:, lanes_of(number)])

    def add_one(number):
        acc_one[:, lanes_of(number)] += dot(second_and_ones, kept[number][1])

    def add_two(number):
        acc_two[:, lanes_of(number)] += dot(out_turned, kept[number][0])

    def add_result(number):
        totals[0] = totals[0] + dot(kept[number][0], two[:, lanes_of(number)], NT)

    def add_second(number):
        totals[1] = totals[1] + dot(kept[number][1], one[:, lanes_of(number)], NT)

    make_hidden(0)
    make_slope(0)
    for number in range(count):
        between = []
        if number + 1 < count:
            between += [functools.partial(f, number + 1) for f in (make_hidden, make_slope)]
        if number > 0:
            between += [
                functools.partial(f, number - 1)
                for f in (add_result, add_second, add_one, add_two)
            ]
        kept[number] = gelu_rows(
            hiddens.pop(number), bias[0:1, lanes_of(number)], slopes.pop(number), between
        )
    for f in (add_result, add_second, add_one, add_two):
        f(count - 1)
    result, grad_second = totals
    output[...] = result.astype(LOW)
    add_row(5, grad_second * normed)
    add_row(6, grad_second)
    grad_res = grad_out + norm_back(grad_second, normed, rate, gain)
    grad_residual[...] = grad_res
    branch = grad_res.astype(LOW)
    add_row(4, branch.astype(F32))
    acc_proj[...] += dot(branch.T, own)
    grad_own = dot(branch, proj[...]).astype(LOW)
    grad_mixed[...] = grad_own
    high, rest = halves(grad_own.astype(F32) * own.astype(F32))
    head = lax.broadcasted_iota(jnp.int32, (16, width), 0)
    chosen = (lane_numbers((16, width)) // (width // HEADS) == head).astype(F32).astype(LOW)
    inner[...] = (dot(chosen, high, NT) + dot(chosen, rest, NT))[:8]

    @pl.when(step == pl.num_programs(0) - 1)
    def finish():
        total = acc_proj[...]
        for number in range(parts):
            turned = pltpu.roll(total, (width - block * number) % width, 1) if number else total
            proj_parts[numbers[PLACES + number]] = turned[:, :SUB].astype(LOW)
        for part in range(parts):
            ref, at = (grads_near, part) if part < mid else (grads_far, part - mid)
            lanes = pl.ds(part * width, width)
            for group in range(ref.shape[0]):
                here = pl.ds(group * ref.shape[2], ref.shape[2])
                ref[group, at, :, :width] = acc_one[here, lanes].astype(LOW)
                ref[group, at, :, width:last_at] = acc_two[here, lanes].astype(LOW)
                ref[group, at, :, last_at:] = proj_parts[part, here, :]
            sums[pl.ds(8 + numbers[OWNERS + part], 1), :] = acc_one[width : width + 1, lanes]


def mlp_both(numbers, near, far, vectors, mixed, tokens, cotangent, out_turned, out_sums):
    rows, width = tokens.shape
    parts = near.shape[1] + far.shape[1]
    hidden_width = parts * width
    tile = pl.BlockSpec((MLP_TILE, width), lambda s, *_: (s, 0))
    whole = lambda *dims: pl.BlockSpec(dims, lambda s, *_: (0,) * len(dims))
    return pl.pallas_call(
        mlp_kernel,
        grid_spec=pltpu.PrefetchScalarGridSpec(
            num_scalar_prefetch=1,
            grid=(rows // MLP_TILE,),
            in_specs=[
                whole(*near.shape), whole(*far.shape), whole(*vectors.shape), tile, tile, tile,
                pl.BlockSpec((width, MLP_TILE), lambda s, *_: (0, s)), whole(*out_sums.shape),
            ],
            out_specs=[
                tile,
                tile,
                tile,
                pl.BlockSpec((8, MLP_TILE), lambda s, *_: (0, s)),
                whole(*near.shape),
                whole(*far.shape),
                whole(*vectors.shape),
            ],
            scratch_shapes=[
                pltpu.VMEM((width, hidden_width), LOW),
                pltpu.VMEM((width, hidden_width), LOW),
                pltpu.VMEM((parts, width, SUB), LOW),
                pltpu.VMEM((width, width), LOW),
                pltpu.VMEM((width + 16, hidden_width), F32),
                pltpu.VMEM((width, hidden_width), F32),
                pltpu.VMEM((width, width), F32),
                pltpu.VMEM((8, hidden_width), F32),
            ],
        ),
        out_shape=[
            jax.ShapeDtypeStruct((rows, width), LOW),
            jax.ShapeDtypeStruct((rows, width), F32),
            jax.ShapeDtypeStruct((rows, width), LOW),
            jax.ShapeDtypeStruct((8, rows), F32),
            jax.ShapeDtypeStruct(near.shape, LOW),
            jax.ShapeDtypeStruct(far.shape, LOW),
            jax.ShapeDtypeStruct(vectors.shape, F32),
        ],
        compiler_params=pltpu.CompilerParams(vmem_limit_bytes=VMEM_LIMIT),
        cost_estimate=pl.CostEstimate(
            flops=34_000_000_000, bytes_accessed=20_000_000, transcendentals=6_000_000
        ),
        name="mlp_both",
    )(numbers, near, far, vectors, mixed, tokens, cotangent, out_turned, out_sums)


def attend_back_kernel(
    numbers,
    query,
    key_turned,
    value,
    probs,
    inner,
    grad_mixed,
    normed_turned,
    weight,
    vectors,
    sums,
    grad_qkv,
    near,
    far,
    grad_query,
    acc_key,
    acc_value,
    acc_sums,
    normed_sums,
    blocks,
    rows,
):
    step = pl.program_id(0)
    chunks = pl.num_programs(0) - 1
    pairs = range(PAIRS)
    count = len(pairs)
    scale = (SUB // 2) ** (-0.5)

    @pl.when(step == 0)
    def clear():
        acc_key[...] = jnp.zeros(acc_key.shape, F32)
        acc_value[...] = jnp.zeros(acc_value.shape, F32)
        normed_sums[...] = jnp.zeros(normed_sums.shape, F32)
        acc_sums[...] = jnp.zeros(acc_sums.shape, F32)

    @pl.when(step < chunks)
    def attend():
        def place(number):
            sub, at = number // count, number % count
            start = pl.multiple_of((step * (TILE // SUB) + sub) * SUB, SUB)
            return sub, at, start, pl.ds(start, SPAN), pl.ds(at * SUB, SUB)

        def slope(number):
            sub, _, _, near_rows, heads = place(number)
            grad = both_heads(grad_mixed[pl.ds(sub * SUB, SUB), heads])
            return dot(value[near_rows, heads], grad, NT)

        def soften(number, slopes):
            sub, at, _, _, _ = place(number)
            pair = pairs[at]
            cols = pl.ds(sub * SUB, SUB)
            both = []
            for head in range(2):
                lanes = slice(head * SUB, (head + 1) * SUB)
                less = slopes[:, lanes] - inner[2 * pair + head : 2 * pair + head + 1, cols]
                both.append((probs[at, sub, :, lanes].astype(F32) * less).astype(LOW))
            return jnp.concatenate(both, axis=1)

        def collect(number, scores):
            sub, at, start, near_rows, heads = place(number)
            first, second = halves_of(dot(key_turned[heads, near_rows], scores))
            turned = (jnp.concatenate([first, second], axis=0) * scale).astype(LOW)
            grad_query[pl.ds(start, SUB), heads] = turned.T
            wanted = both_heads(query[pl.ds(start + MARGIN, SUB), heads])
            acc_key[near_rows, heads] += dot(scores, wanted)
            grad = both_heads(grad_mixed[pl.ds(sub * SUB, SUB), heads])
            acc_value[near_rows, heads] += dot(probs[at, sub], grad)

        staged(TILE // SUB * count, slope, soften, collect)

    @pl.when(step > 0)
    def collect():
        here = pl.ds(pl.multiple_of((step - 1) * TILE, SUB), TILE)
        there = pl.ds(pl.multiple_of((step - 1) * TILE + MARGIN, SUB), TILE)
        parts = (
            grad_query[here, :],
            acc_key[there, :].astype(LOW),
            acc_value[there, :].astype(LOW),
        )
        joined = jnp.concatenate(parts, axis=1)
        grad_qkv[...] = joined
        normed_sums[...] += dot(normed_turned[...], joined)
        acc_sums[0:1, :] += jnp.sum(joined.astype(F32), axis=0, keepdims=True)

    @pl.when(step == chunks)
    def finish():
        weight_grad(
            numbers, normed_sums[...], acc_sums[0:1, :], weight, vectors, sums, near, far, blocks, rows
        )


def weight_grad(numbers, total, columns, weight, vectors, sums, near, far, blocks, rows):
    width = weight.shape[0]
    parts, mid = blocks.shape[0], near.shape[0]
    block = 3 * width // parts
    rows_each = 12 // parts
    wide = weight[...].astype(F32)
    grad_gain = jnp.sum(total * wide, axis=1, keepdims=True)
    grad_shift = jnp.sum(wide * columns, axis=1, keepdims=True)
    rows[...] = jnp.zeros(rows.shape, F32)
    rows[0:VEC_LANES, :] = sums[...]
    rows[2:3, :] = columns[:, :width]
    rows[3:4, :] = columns[:, 2 * width :]
    rows[VEC_LANES : 2 * VEC_LANES, :] = vectors[...]
    turned = rows[...].T
    gain = turned[:, VEC_LANES : VEC_LANES + 1]
    shift = turned[:, VEC_LANES + 1 : VEC_LANES + 2]
    lane = lane_numbers(turned.shape)
    turned = jnp.where(lane == 0, grad_gain, jnp.where(lane == 1, grad_shift, turned))
    total = total * gain + shift * columns
    at = block - 2 * SUB
    for number in range(parts):
        away = (3 * width - block * number) % (3 * width)
        piece = (pltpu.roll(total, away, 1) if number else total)[:, :width]
        vec = pltpu.roll(turned, (at - rows_each * number) % SUB, 1)
        last = jnp.where(lane < at, piece[:, 2 * SUB :], 0.0)
        last = jnp.where((lane >= at) & (lane < at + rows_each), vec, last)
        at_place = numbers[PLACES + number]
        blocks[at_place, :, : 2 * SUB] = piece[:, : 2 * SUB].astype(LOW)
        blocks[at_place, :, 2 * SUB :] = last.astype(LOW)
    near[...] = blocks[:mid]
    far[...] = blocks[mid:]


def attend_backward(
    numbers, parts, query, key_turned, value, probs, inner, grad_mixed, normed_turned, weight,
    vectors, sums,
):
    width, rows = normed_turned.shape
    padded = query.shape[0]
    chunks = rows // TILE
    tiles = TILE // SUB
    now = lambda s: jnp.minimum(s, chunks - 1)
    before = lambda s: jnp.maximum(s - 1, 0)
    whole = lambda *dims: pl.BlockSpec(dims, lambda s, *_: (0,) * len(dims))
    half = (parts // 2, width, width)
    return pl.pallas_call(
        attend_back_kernel,
        grid_spec=pltpu.PrefetchScalarGridSpec(
            num_scalar_prefetch=1,
            grid=(chunks + 1,),
            in_specs=[
                whole(padded, width),
                whole(width, padded),
                whole(padded, width),
                pl.BlockSpec((PAIRS, tiles, SPAN, 2 * SUB), lambda s, *_: (0, now(s), 0, 0)),
                pl.BlockSpec((8, TILE), lambda s, *_: (0, now(s))),
                pl.BlockSpec((TILE, width), lambda s, *_: (now(s), 0)),
                pl.BlockSpec((width, TILE), lambda s, *_: (0, before(s))),
                whole(*weight.shape),
                whole(*vectors.shape),
                whole(*sums.shape),
            ],
            out_specs=[
                pl.BlockSpec((TILE, 3 * width), lambda s, *_: (before(s), 0)),
                whole(*half),
                whole(*half),
            ],
            scratch_shapes=[
                pltpu.VMEM((rows, width), LOW),
                pltpu.VMEM((padded, width), F32),
                pltpu.VMEM((padded, width), F32),
                pltpu.VMEM((8, 3 * width), F32),
                pltpu.VMEM((width, 3 * width), F32),
                pltpu.VMEM((parts, width, width), LOW),
                pltpu.VMEM((SUB, width), F32),
            ],
        ),
        out_shape=[
            jax.ShapeDtypeStruct((rows, 3 * width), LOW),
            jax.ShapeDtypeStruct(half, LOW),
            jax.ShapeDtypeStruct(half, LOW),
        ],
        compiler_params=pltpu.CompilerParams(vmem_limit_bytes=VMEM_LIMIT),
        cost_estimate=pl.CostEstimate(
            flops=16_000_000_000, bytes_accessed=24_000_000, transcendentals=0
        ),
        name="attend_backward",
    )(
        numbers, query, key_turned, value, probs, inner, grad_mixed, normed_turned, weight, vectors,
        sums,
    )


def input_grad_kernel(weight, vectors, tokens, grad_residual, grad_qkv, input_grad):
    normed, rate = norm_parts(tokens[...].astype(F32))
    grad_first = dot(grad_qkv[...], weight[...], NT)
    back = norm_back(grad_first, normed, rate, vectors[0:1, :])
    input_grad[...] = (grad_residual[...] + back).astype(LOW)


def input_gradient(weight, vectors, tokens, grad_residual, grad_qkv):
    rows, width = tokens.shape
    size = TILE
    tile = pl.BlockSpec((size, width), lambda s: (s, 0))
    whole = lambda ref: pl.BlockSpec(ref.shape, lambda s: (0, 0))
    return pl.pallas_call(
        input_grad_kernel,
        grid=(rows // size,),
        in_specs=[
            whole(weight), whole(vectors), tile, tile,
            pl.BlockSpec((size, 3 * width), lambda s: (s, 0)),
        ],
        out_specs=tile,
        out_shape=jax.ShapeDtypeStruct((rows, width), LOW),
        compiler_params=pltpu.CompilerParams(vmem_limit_bytes=VMEM_LIMIT),
        cost_estimate=pl.CostEstimate(
            flops=4_000_000_000, bytes_accessed=13_000_000, transcendentals=2048
        ),
        name="input_gradient",
    )(weight, vectors, tokens, grad_residual, grad_qkv)


def halves(value):
    high = value.astype(LOW)
    return high, (value - high.astype(F32)).astype(LOW)


def dot_three(left, right):
    tall = jnp.concatenate([right[0], right[0], right[1]], axis=0)
    return dot(jnp.concatenate([left[0], left[1], left[0]], axis=1), tall)


def newton_rows(blocks, offset, rows):
    gram = dot(blocks[0], blocks[0], NT)
    for part in blocks[1:]:
        gram = gram + dot(part, part, NT)
    depth = gram.shape[0]
    down = lax.broadcasted_iota(jnp.int32, (depth, depth), 0)
    eye = (down == lane_numbers((depth, depth))).astype(F32)
    norm = 1.0 / (jnp.sqrt(jnp.sum(gram * eye, keepdims=True)) + 1e-07)
    gram = gram * (norm * norm)
    place = lax.broadcasted_iota(jnp.int32, (rows, depth), 0) + offset
    left = jnp.where(place == lane_numbers((rows, depth)), norm, 0.0)
    for step in range(NS_STEPS - 1):
        pair = halves(gram)
        poly = halves(NEWTON_A * eye + NEWTON_B * gram + NEWTON_C * dot_three(pair, pair))
        lefts = halves(left)
        both = dot_three([jnp.concatenate([pair[n], lefts[n]], axis=0) for n in range(2)], poly)
        left = both[depth:]
        gram = dot_three(halves(both[:depth]), poly)
    pair = halves(gram)
    once = dot_three(halves(left), pair)
    return NEWTON_A * left + NEWTON_B * once + NEWTON_C * dot_three(halves(once), pair)


def stepped(left, own, height, old):
    high, rest = halves(left)
    ortho = (dot(high, own) + dot(rest, own))[: old.shape[0], : old.shape[1]]
    return old * (1.0 - MUON_RATE * MUON_DECAY) - (MUON_RATE * 0.2 * math.sqrt(height)) * ortho


def kept_lanes(value, low, high):
    lane = lane_numbers(value.shape)
    return jnp.where((lane >= low) & (lane < high), value.astype(F32), 0.0).astype(LOW)


def tall_of(rows):
    return -(-rows // 16) * 16


def muon_kernel(height, numbers, *refs):
    old, new, copy = refs[-3:]
    count = old.shape[1]
    blocks = [kept_lanes(ref[...], 0, count) for ref in refs[:-3]]
    left = newton_rows(blocks, numbers[OFFSET], tall_of(old.shape[0]))
    result = stepped(left, blocks[0], height, old[...])
    new[...] = result
    copy[...] = result.astype(LOW)


def muon(height, numbers, blocks, old):
    vmem = pl.BlockSpec(memory_space=pltpu.VMEM)

    def kernel(*refs):
        muon_kernel(height, *refs)

    return pl.pallas_call(
        kernel,
        in_specs=[pl.BlockSpec(memory_space=pltpu.SMEM)] + [vmem] * (len(blocks) + 1),
        out_specs=[vmem, vmem],
        out_shape=[
            jax.ShapeDtypeStruct(old.shape, F32),
            jax.ShapeDtypeStruct(old.shape, LOW),
        ],
        compiler_params=pltpu.CompilerParams(vmem_limit_bytes=VMEM_LIMIT),
        cost_estimate=pl.CostEstimate(
            flops=9_000_000_000, bytes_accessed=2_000_000, transcendentals=10
        ),
        name="muon",
    )(numbers, *blocks, old)


def pick_kernel(count, numbers, *refs):
    pieces, columns, outs = refs[:count], refs[count], refs[count + 1 :]
    share = pieces[0].shape[0]
    for k, piece in enumerate(pieces):
        columns[k * share : (k + 1) * share, :] = piece[...]
        for n, out in enumerate(outs):
            at = pl.multiple_of(numbers[STARTS + n] * SUB, SUB)
            out[k * share : (k + 1) * share, :] = piece[:, pl.ds(at, out.shape[1])]


def pick(numbers, pieces, count):
    depth = len(pieces) * pieces[0].shape[0]
    vmem = pl.BlockSpec(memory_space=pltpu.VMEM)

    def kernel(*refs):
        pick_kernel(len(pieces), *refs)

    return pl.pallas_call(
        kernel,
        in_specs=[pl.BlockSpec(memory_space=pltpu.SMEM)] + [vmem] * len(pieces),
        out_specs=[vmem] * (count + 1),
        out_shape=[jax.ShapeDtypeStruct((depth, pieces[0].shape[1]), LOW)]
        + [jax.ShapeDtypeStruct((depth, depth), LOW)] * count,
        name="pick",
    )(numbers, *pieces)


def newton_kernel(at, numbers, *refs):
    left = refs[-1]
    bounds = numbers[LOW_LANE], numbers[HIGH_LANE]
    blocks = [kept_lanes(ref[...], *bounds) for ref in refs[:-1]]
    left[...] = newton_rows(blocks, numbers[OFFSET] if at is None else at, left.shape[0])


def newton(at, numbers, blocks, rows):
    vmem = pl.BlockSpec(memory_space=pltpu.VMEM)

    def kernel(*refs):
        newton_kernel(at, *refs)

    return pl.pallas_call(
        kernel,
        in_specs=[pl.BlockSpec(memory_space=pltpu.SMEM)] + [vmem] * len(blocks),
        out_specs=vmem,
        out_shape=jax.ShapeDtypeStruct((tall_of(rows), blocks[0].shape[0]), F32),
        compiler_params=pltpu.CompilerParams(vmem_limit_bytes=VMEM_LIMIT),
        cost_estimate=pl.CostEstimate(
            flops=9_000_000_000, bytes_accessed=2_000_000, transcendentals=10
        ),
        name="newton",
    )(numbers, *blocks)


def finish_kernel(heights, lanes, numbers, columns, *refs):
    count = len(heights)
    store = refs[-1]
    news = refs[-1 - 2 * count : -1]
    olds = refs[-1 - 3 * count : -1 - 2 * count]
    lefts = refs[: -1 - 3 * count]
    for n, left in enumerate(lefts):
        store[n] = left[...]
    for n in range(count):
        wide = -(-olds[n].shape[1] // SUB) * SUB
        own = columns[:, lanes[n] : lanes[n] + wide]
        result = stepped(store[numbers[WHICH + n]], own, heights[n], olds[n][...])
        news[2 * n][...] = result
        news[2 * n + 1][...] = result.astype(LOW)


def finish(heights, lanes, numbers, columns, lefts, olds):
    vmem = pl.BlockSpec(memory_space=pltpu.VMEM)
    count = len(olds)

    def kernel(*refs):
        finish_kernel(heights, lanes, *refs)

    outs = pl.pallas_call(
        kernel,
        in_specs=[pl.BlockSpec(memory_space=pltpu.SMEM)] + [vmem] * (1 + len(lefts) + count),
        out_specs=[vmem] * (2 * count),
        out_shape=[
            jax.ShapeDtypeStruct(old.shape, kind) for old in olds for kind in (F32, LOW)
        ],
        scratch_shapes=[pltpu.VMEM((len(lefts), *lefts[0].shape), F32)],
        compiler_params=pltpu.CompilerParams(vmem_limit_bytes=VMEM_LIMIT),
        cost_estimate=pl.CostEstimate(
            flops=200_000_000, bytes_accessed=2_000_000, transcendentals=0
        ),
        name="finish",
    )(numbers, columns, *lefts, *olds)
    return [(outs[2 * n], outs[2 * n + 1]) for n in range(count)]


def exchange(x, axis, mask):
    size = lax.axis_size(axis)
    return lax.ppermute(x, axis, [(i, i ^ mask) for i in range(size)])


def place_masks(size):
    masks = [0]
    bit = size // 2
    while bit >= 1:
        masks = masks + [m ^ bit for m in masks]
        bit //= 2
    return masks


def from_columns(own):
    size = lax.axis_size("dp")
    sent = jnp.broadcast_to(own[None], (size, *own.shape))
    return lax.all_to_all(sent, "dp", split_axis=0, concat_axis=0, tiled=True)


def over_columns(own):
    return from_columns(own).reshape(-1, own.shape[1])


def device_numbers(dp, ns, share, width, proj_rows):
    masks = place_masks(ns)
    tasks = [(0, 0, width), (width // SUB, 0, width)]
    tasks += [(width // SUB + 1, 2 * SUB, 2 * SUB + proj_rows)] * (ns - 2)
    table = np.zeros((dp * ns, 24), np.int32)
    for device in range(dp * ns):
        column, index = device // ns, device % ns
        row = table[device]
        for n in range(ns):
            row[OWNERS + n] = index ^ masks[n]
            row[PLACES + (index ^ masks[n])] = n
            row[STARTS + n] = tasks[index ^ n][0]
        for n in range(3):
            row[WHICH + n] = index ^ n
        row[OFFSET] = column * share
        row[COLUMN] = column
        row[LOW_LANE], row[HIGH_LANE] = tasks[index][1:]
    return table


def half_rows(own):
    held = [own]
    bit = lax.axis_size("ns") // 2
    while bit > 1:
        held = held + [exchange(block, "ns", bit) for block in held]
        bit //= 2
    return held


def added(keep, got):
    return (keep.astype(F32) + got.astype(F32)).astype(LOW)


def sum_columns(pieces):
    return summed(lax.all_to_all(pieces, "dp", split_axis=0, concat_axis=0, tiled=True))


def summed(pieces):
    return jnp.sum(pieces.astype(F32), axis=0)


def columns_direct(own):
    devices = lax.axis_size("dp")
    if devices > 8 or own.shape[0] % 16:
        return [over_columns(own)], None
    return [own] + [exchange(own, "dp", mask) for mask in range(1, devices)], 0


def widened(arrays, lanes):
    joined = jnp.concatenate(arrays, axis=1)
    return jnp.pad(joined, ((0, 0), (0, lanes - joined.shape[1])))


def per_device(
    tokens,
    cotangent,
    segment,
    valid_rows,
    qkv_weight,
    proj_weight,
    fc1_weight,
    fc2_weight,
    qkv_moment,
    proj_moment,
    fc1_moment,
    fc2_moment,
    vectors,
    vector_moment,
    vector_square,
):
    rows, width = tokens.shape
    ns = lax.axis_size("ns")
    qkv_w, proj_w, fc1_w, fc2_w = (w.T for w in (qkv_weight, proj_weight, fc1_weight, fc2_weight))
    qkv_m, proj_m, fc1_m, fc2_m = (w.T for w in (qkv_moment, proj_moment, fc1_moment, fc2_moment))
    share, count = qkv_w.shape
    vec_rows = vectors.shape[0]
    first_lanes = width
    later_lanes = 2 * width + SUB

    table = device_numbers(lax.axis_size("dp"), ns, share, width, proj_w.shape[1])
    device = lax.axis_index("dp") * ns + lax.axis_index("ns")
    numbers = lax.dynamic_slice(jnp.asarray(table), (device, 0), (1, table.shape[1]))[0]

    row_ids = jnp.where(
        valid_rows > 0, segment, rows + jnp.arange(rows, dtype=jnp.int32)
    ).astype(F32)
    ids = jnp.pad(row_ids, (MARGIN, MARGIN), constant_values=-1.0).reshape(-1, SUB)
    ids = jnp.pad(ids, ((0, -ids.shape[0] % 8), (0, 0)), constant_values=-1.0)

    later_own = widened([fc1_w, fc2_w, proj_w], later_lanes).astype(LOW)
    later_pair = jnp.stack([later_own, exchange(later_own, "ns", ns // 2)])
    first_own = widened([qkv_w, vectors.T], first_lanes).astype(LOW)
    prepared = prepare(tokens, cotangent, ids)
    first_pieces = half_rows(over_columns(first_own))
    first_pieces, prepared = lax.optimization_barrier((first_pieces, prepared))
    normed, normed_turned, out_turned, columns, out_sums = prepared
    first_pieces = first_pieces + [exchange(piece, "ns", 1) for piece in first_pieces]
    later_near = from_columns(later_pair)
    if share % 16:
        later_near = jnp.moveaxis(later_near, 0, 1).reshape(1, ns // 2, width, later_lanes)

    query, _, value, key_turned, mixed, probs, weight, vector_full = attend_forward(
        numbers, first_pieces, normed, ids, columns
    )
    later_near, mixed = lax.optimization_barrier((later_near, mixed))
    later_far = exchange(later_near, "ns", 1)
    output, grad_residual, grad_mixed, inner, grads_near, grads_far, sums = mlp_both(
        numbers, later_near, later_far, vector_full, mixed, tokens, cotangent, out_turned, out_sums
    )
    held = added(grads_near, exchange(grads_far, "ns", 1))
    held, grad_mixed = lax.optimization_barrier((held, grad_mixed))
    if share % 16:
        held = jnp.moveaxis(held.reshape(ns // 2, -1, share, later_lanes), 1, 0)
    later_got = lax.all_to_all(held, "dp", split_axis=0, concat_axis=0, tiled=True)

    grad_qkv, grads_near, grads_far = attend_backward(
        numbers, ns, query, key_turned, value, probs, inner, grad_mixed, normed_turned, weight,
        vector_full, sums,
    )
    held = added(grads_near, exchange(grads_far, "ns", 1))
    got = exchange(held[1], "ns", ns // 2)
    input_grad = input_gradient(weight, vector_full, tokens, grad_residual, grad_qkv)
    got, input_grad, later_got = lax.optimization_barrier((got, input_grad, later_got))
    first_held = added(held[0], got).reshape(lax.axis_size("dp"), share, first_lanes)
    first_got = lax.all_to_all(first_held, "dp", split_axis=0, concat_axis=0, tiled=True)
    later_sums = summed(later_got)
    later_far = exchange(later_sums[1].astype(LOW), "ns", ns // 2)
    first_got, later_far = lax.optimization_barrier((first_got, later_far))
    first_owned = summed(first_got)
    later_owned = later_sums[0] + later_far.astype(F32)
    first_moment = first_owned + 0.5 * widened([qkv_m], first_lanes)
    later_moment = later_owned + 0.5 * widened([fc1_m, fc2_m, proj_m], later_lanes)
    later_low, first_low = lax.optimization_barrier(
        (later_moment.astype(LOW), first_moment.astype(LOW))
    )
    first_own = over_columns(first_low)
    pieces, at = columns_direct(later_low)
    pieces, first_own = lax.optimization_barrier((pieces, first_own))
    first_pieces = half_rows(first_own)
    columns, *chosen = pick(numbers, pieces, ns)
    chosen, first_pieces = lax.optimization_barrier((chosen, first_pieces))
    first_pieces = first_pieces + [exchange(piece, "ns", 1) for piece in first_pieces]
    blocks = [chosen[0]] + [exchange(chosen[mask], "ns", mask) for mask in range(1, ns)]
    qkv_new = muon(count * ns, numbers, first_pieces, qkv_w)
    blocks, qkv_new = lax.optimization_barrier((blocks, qkv_new))
    left = newton(at, numbers, blocks, share)
    lefts = [left] + [exchange(left, "ns", mask) for mask in range(1, ns)]
    fc1_new, fc2_new, proj_new = finish(
        [w.shape[1] * ns for w in (fc1_w, fc2_w, proj_w)],
        (0, width, 2 * width),
        numbers,
        columns,
        lefts,
        (fc1_w, fc2_w, proj_w),
    )

    news = (qkv_new, proj_new, fc1_new, fc2_new)
    moments_new = (
        first_moment[:, :count],
        later_moment[:, 2 * width : 2 * width + proj_w.shape[1]],
        later_moment[:, :width],
        later_moment[:, width : 2 * width],
    )

    vector_grad = first_owned[:, count : count + vec_rows].T
    first_new = BETA_ONE * vector_moment + (1.0 - BETA_ONE) * vector_grad
    second_new = BETA_TWO * vector_square + (1.0 - BETA_TWO) * vector_grad * vector_grad
    first_hat = first_new / (1.0 - BETA_ONE**STEP)
    second_hat = second_new / (1.0 - BETA_TWO**STEP)
    vectors_new = vectors - ADAM_RATE * first_hat / (jnp.sqrt(second_hat) + ADAM_EPS)
    return (
        output,
        input_grad,
        *(new[0].T for new in news),
        *(m.T for m in moments_new),
        first_new,
        second_new,
        vectors_new,
        *(new[1].T for new in news),
    )


def solution(mesh):
    rows = P(("dp", "ns"), None)
    flat = P(("dp", "ns"))
    block = P("ns", "dp")
    return jax.shard_map(
        per_device,
        mesh=mesh,
        in_specs=(rows, rows, flat, flat) + (block,) * 11,
        out_specs=(rows, rows) + (block,) * 15,
        check_vma=False,
    )
```

```python
import functools
import math

import jax
import jax.numpy as jnp
import numpy as np
from jax import lax
from jax.experimental import pallas as pl
from jax.experimental.pallas import tpu as pltpu
from jax.sharding import PartitionSpec as P

HEADS = 6
PAIRS = 3
MARGIN = 128
NS_STEPS = 5
STEP = 10
TILE = 512
MLP_TILE = 512
FF_CHUNK = 256
SUB = 128
SPAN = 384
VEC_LANES = 16
GROUP = 2


EPS_NORM = 1e-06
NEWTON_A = 3.4445
NEWTON_B = -4.775
NEWTON_C = 2.0315
MUON_RATE = 0.2
MUON_DECAY = 0.1
ADAM_RATE = 0.4
BETA_ONE = 0.9
BETA_TWO = 0.999
ADAM_EPS = 1e-08
LOW = jnp.bfloat16
F32 = jnp.float32
TN = (((0,), (0,)), ((), ()))
NT = (((1,), (1,)), ((), ()))
NN = (((1,), (0,)), ((), ()))
VMEM_LIMIT = 56 * 1024 * 1024
ERF_P = 0.3275911
ERF_COEFS = (0.254829592, -0.284496736, 1.421413741, -1.453152027, 1.061405429)


def dot(left, right, dims=NN):
    return lax.dot_general(left, right, dims, preferred_element_type=F32)


PLACES, OWNERS, STARTS, WHICH, OFFSET, LOW_LANE, HIGH_LANE, COLUMN = 0, 4, 8, 12, 16, 17, 18, 19


def lane_numbers(shape):
    return lax.broadcasted_iota(jnp.int32, shape, len(shape) - 1)


def norm_parts(value):
    center = value - jnp.mean(value, axis=-1, keepdims=True)
    rate = lax.rsqrt(jnp.mean(center * center, axis=-1, keepdims=True) + EPS_NORM)
    return center * rate, rate


def norm_back(grad, normed, rate, gain):
    scaled = grad * gain
    first = jnp.mean(scaled, axis=-1, keepdims=True)
    second = jnp.mean(scaled * normed, axis=-1, keepdims=True)
    return rate * (scaled - first - normed * second)


def gelu_both(value):
    below = 1.0 + (ERF_P * 0.5**0.5) * jnp.abs(value)
    ratio = pl.reciprocal(below, approx=True)
    ratio = ratio * (2.0 - below * ratio)
    decay = jnp.exp2((value * value) * (-0.5 * math.log2(math.e)))
    poly = 0.5 * ERF_COEFS[4]
    for coef in ERF_COEFS[3::-1]:
        poly = poly * ratio + 0.5 * coef
    tail = poly * ratio * decay
    phi = jnp.where(value >= 0, 1.0 - tail, tail)
    return value * phi, phi + (value * (1.0 / math.sqrt(2.0 * math.pi))) * decay


def gelu_rows(hidden, bias, grad, between):
    active, back = [], []
    rows = hidden.shape[0]
    pieces = rows // 16
    for n in range(pieces):
        if n * len(between) // pieces != (n - 1) * len(between) // pieces:
            between[n * len(between) // pieces]()
        here = slice(n * 16, (n + 1) * 16)
        value, slope = gelu_both(hidden[here] + bias)
        active.append(value.astype(LOW))
        back.append((grad[here] * slope).astype(LOW))
    return jnp.concatenate(active, axis=0), jnp.concatenate(back, axis=0)


def halves_of(lanes):
    half = lanes.shape[0] // 2
    return lanes[:half, :SUB], lanes[half:, SUB:]


def staged(count, first, second, third):
    made = first(0)
    kept = None
    for n in range(count):
        coming = first(n + 1) if n + 1 < count else None
        if kept is not None:
            third(n - 1, kept)
        kept = second(n, made)
        made = coming
    third(count - 1, kept)


def both_heads(pair):
    first = (lane_numbers((1, SUB)) < SUB // 2).astype(F32).astype(pair.dtype)
    second = (lane_numbers((1, SUB)) >= SUB // 2).astype(F32).astype(pair.dtype)
    return jnp.concatenate([pair * first, pair * second], axis=0)


def fetch(pairs, sems):
    copies = [
        pltpu.make_async_copy(source, target, sems.at[n])
        for n, (source, target) in enumerate(pairs)
    ]
    for copy in copies:
        copy.start()
    for copy in copies:
        copy.wait()


def prepare_kernel(tokens, cotangent, ids, normed, normed_turned, out_turned, columns, sums):
    step = pl.program_id(0)
    parts = columns.shape[0] // SUB

    @pl.when(step == 0)
    def clear():
        sums[...] = jnp.zeros(sums.shape, F32)
        for number in range(parts):
            row = jnp.broadcast_to(ids[number : number + 1, :], (SUB, SUB))
            columns[number * SUB : (number + 1) * SUB, :] = row.T

    value, _ = norm_parts(tokens[...].astype(F32))
    normed[...] = value
    normed_turned[...] = value.astype(LOW).T
    out_low = cotangent[...]
    out_turned[...] = out_low.T
    sums[0:1, :] += jnp.sum(out_low.astype(F32), axis=0, keepdims=True)


def prepare(tokens, cotangent, ids):
    rows, width = tokens.shape
    padded = rows + 2 * MARGIN
    tile = pl.BlockSpec((TILE, width), lambda s: (s, 0))
    turned = pl.BlockSpec((width, TILE), lambda s: (0, s))
    whole = lambda *dims: pl.BlockSpec(dims, lambda s: (0,) * len(dims))
    return pl.pallas_call(
        prepare_kernel,
        grid=(rows // TILE,),
        in_specs=[tile, tile, whole(*ids.shape)],
        out_specs=[tile, turned, turned, whole(padded, SUB), whole(8, width)],
        out_shape=[
            jax.ShapeDtypeStruct((rows, width), F32),
            jax.ShapeDtypeStruct((width, rows), LOW),
            jax.ShapeDtypeStruct((width, rows), LOW),
            jax.ShapeDtypeStruct((padded, SUB), F32),
            jax.ShapeDtypeStruct((8, width), F32),
        ],
        compiler_params=pltpu.CompilerParams(vmem_limit_bytes=VMEM_LIMIT),
        cost_estimate=pl.CostEstimate(
            flops=20_000_000, bytes_accessed=12_000_000, transcendentals=2048
        ),
        name="prepare",
    )(tokens, cotangent, ids)


def attend_kernel(numbers, *refs):
    (normed, ids, columns, query, key, value, key_turned, mixed, probs, weight, vectors,
     gathered, pair_weight, value_turned, shifts, sems) = refs[-16:]
    pieces = refs[:-16]
    step = pl.program_id(0)
    chunks = pl.num_programs(0) - 1
    width = normed.shape[1]
    parts = len(pieces)
    block = 3 * width // parts
    rows_each = 12 // parts

    @pl.when(step == 0)
    def assemble():
        fetch([(piece, gathered.at[n]) for n, piece in enumerate(pieces)], sems)
        total = jnp.zeros((width, 3 * width), F32)
        turned = jnp.zeros((width, SUB), F32)
        for number in range(parts):
            piece = gathered[numbers[PLACES + number]].astype(F32)
            kept = jnp.where(lane_numbers(piece.shape) < block, piece, 0.0)
            wide = jnp.concatenate([kept, jnp.zeros((width, 2 * width), F32)], axis=1)
            total = total + (pltpu.roll(wide, block * number, 1) if number else wide)
            last = piece[:, 2 * SUB :]
            at = block - 2 * SUB
            lane = lane_numbers(last.shape)
            vec = jnp.where((lane >= at) & (lane < at + rows_each), last, 0.0)
            turned = turned + pltpu.roll(vec, (rows_each * number - at) % SUB, 1)
        total = total.astype(LOW)
        weight[...] = total
        pair_weight[...] = total[:, width:].T
        vectors[...] = turned.T[:VEC_LANES]
        shifts[...] = turned
        edges = (pl.ds(0, MARGIN), pl.ds(MARGIN + chunks * TILE, MARGIN))
        for edge in edges:
            for ref in (query, key, value):
                ref[edge, :] = jnp.zeros((MARGIN, width), LOW)
            for ref in (key_turned, value_turned):
                ref[:, edge] = jnp.zeros((width, MARGIN), LOW)

    @pl.when(step < chunks)
    def project():
        first_in = (normed[...] * vectors[0:1, :] + vectors[1:2, :]).astype(LOW)
        result = dot(first_in, weight[...])
        turned = dot(pair_weight[...], first_in, NT)
        here = pl.ds(pl.multiple_of(MARGIN + step * TILE, SUB), TILE)
        scale = (width // HEADS) ** (-0.5)
        made = (result[:, :width] + vectors[2:3, :]).astype(LOW) * jnp.asarray(scale, LOW)
        query[here, :] = made
        key[here, :] = result[:, width : 2 * width].astype(LOW)
        value[here, :] = (result[:, 2 * width :] + vectors[3:4, :]).astype(LOW)
        key_turned[:, here] = turned[:width].astype(LOW)
        value_turned[:, here] = (turned[width:] + shifts[:, 3:4]).astype(LOW)

    @pl.when(step > 0)
    def attend():
        def place(number):
            sub, pair = number // PAIRS, number % PAIRS
            tile = (step - 1) * (TILE // SUB) + sub
            start = pl.multiple_of(tile * SUB, SUB)
            return sub, pair, tile, start, pl.ds(start, SPAN), pl.ds(pair * SUB, SUB)

        def of_group(group):
            return range(group * GROUP, (group + 1) * GROUP)

        def score(group):
            made = []
            for number in of_group(group):
                _, _, _, start, near_rows, heads = place(number)
                wanted = both_heads(query[pl.ds(start + MARGIN, SUB), heads])
                made.append(dot(key[near_rows, heads], wanted, NT))
            return made

        def soften(group, made):
            own = []
            for number, scores in zip(of_group(group), made):
                _, _, tile, _, near_rows, _ = place(number)
                same = columns[near_rows, :] == ids[pl.ds(tile + 1, 1), :]
                own += [
                    jnp.where(same, scores[:, head * SUB : (head + 1) * SUB], -1e30)
                    for head in range(2)
                ]
            largest = [jnp.max(part, axis=0, keepdims=True) for part in own]
            expo = [jnp.exp(part - most) for part, most in zip(own, largest)]
            share = [1.0 / jnp.sum(part, axis=0, keepdims=True) for part in expo]
            scaled = [(part * by).astype(LOW) for part, by in zip(expo, share)]
            result = []
            for n, number in enumerate(of_group(group)):
                sub, pair, _, _, _, _ = place(number)
                result.append(jnp.concatenate(scaled[2 * n : 2 * n + 2], axis=1))
                probs[pair, sub] = result[-1]
            return result

        def mix(group, kept):
            for number, prob in zip(of_group(group), kept):
                sub, _, _, _, near_rows, heads = place(number)
                first, second = halves_of(dot(value_turned[heads, near_rows], prob))
                turned = jnp.concatenate([first, second], axis=0).astype(LOW)
                mixed[pl.ds(sub * SUB, SUB), heads] = turned.T

        staged(TILE // SUB * PAIRS // GROUP, score, soften, mix)


def attend_forward(numbers, pieces, normed, ids, columns):
    rows, width = normed.shape
    chunks = rows // TILE
    tiles = TILE // SUB
    parts = len(pieces)
    now = lambda s: jnp.minimum(s, chunks - 1)
    before = lambda s: jnp.maximum(s - 1, 0)
    whole = lambda *dims: pl.BlockSpec(dims, lambda s, *_: (0,) * len(dims))
    padded = rows + 2 * MARGIN
    return pl.pallas_call(
        attend_kernel,
        grid_spec=pltpu.PrefetchScalarGridSpec(
            num_scalar_prefetch=1,
            grid=(chunks + 1,),
            in_specs=[pl.BlockSpec(memory_space=pl.ANY)] * parts
            + [
                pl.BlockSpec((TILE, width), lambda s, *_: (now(s), 0)),
                whole(*ids.shape),
                whole(*columns.shape),
            ],
            out_specs=[
                whole(padded, width),
                whole(padded, width),
                whole(padded, width),
                whole(width, padded),
                pl.BlockSpec((TILE, width), lambda s, *_: (before(s), 0)),
                pl.BlockSpec((PAIRS, tiles, SPAN, 2 * SUB), lambda s, *_: (0, before(s), 0, 0)),
                whole(width, 3 * width),
                whole(VEC_LANES, width),
            ],
            scratch_shapes=[
                pltpu.VMEM((parts, *pieces[0].shape), LOW),
                pltpu.VMEM((2 * width, width), LOW),
                pltpu.VMEM((width, padded), LOW),
                pltpu.VMEM((width, SUB), F32),
                pltpu.SemaphoreType.DMA((parts,)),
            ],
        ),
        out_shape=[
            jax.ShapeDtypeStruct((padded, width), LOW),
            jax.ShapeDtypeStruct((padded, width), LOW),
            jax.ShapeDtypeStruct((padded, width), LOW),
            jax.ShapeDtypeStruct((width, padded), LOW),
            jax.ShapeDtypeStruct((rows, width), LOW),
            jax.ShapeDtypeStruct((PAIRS, rows // SUB, SPAN, 2 * SUB), LOW),
            jax.ShapeDtypeStruct((width, 3 * width), LOW),
            jax.ShapeDtypeStruct((VEC_LANES, width), F32),
        ],
        compiler_params=pltpu.CompilerParams(vmem_limit_bytes=VMEM_LIMIT),
        cost_estimate=pl.CostEstimate(
            flops=12_000_000_000, bytes_accessed=22_000_000, transcendentals=5_000_000
        ),
        name="attend_forward",
    )(numbers, *pieces, normed, ids, columns)


def mlp_kernel(numbers, near, far, *refs):
    (vectors, mixed, tokens, cotangent, out_turned, out_sums, output, grad_residual, grad_mixed, inner, grads_near,
     grads_far, sums, one, two, proj_parts, proj, acc_one, acc_two, acc_proj, bias
    ) = refs
    step = pl.program_id(0)
    width = tokens.shape[1]
    mid = near.shape[1]
    parts = mid + far.shape[1]
    block = width // parts
    last_at = 2 * width
    hidden_width = one.shape[1]

    @pl.when(step == 0)
    def assemble():
        for part in range(parts):
            ref, at = (near, part) if part < mid else (far, part - mid)
            lanes = pl.ds(part * width, width)
            for group in range(near.shape[0]):
                here = pl.ds(group * near.shape[2], near.shape[2])
                one[here, lanes] = ref[group, at, :, :width]
                two[here, lanes] = ref[group, at, :, width:last_at]
                proj_parts[part, here, :] = ref[group, at, :, last_at:]
        total = jnp.zeros((width, width), F32)
        for number in range(parts):
            piece = proj_parts[numbers[PLACES + number]].astype(F32)
            kept = jnp.where(lane_numbers(piece.shape) < block, piece, 0.0)
            wide = jnp.concatenate([kept, jnp.zeros((width, width - SUB), F32)], axis=1)
            total = total + (pltpu.roll(wide, block * number, 1) if number else wide)
        proj[...] = total.astype(LOW)
        for part in range(parts):
            row = vectors[pl.ds(8 + numbers[OWNERS + part], 1), :]
            bias[0:1, part * width : (part + 1) * width] = row
        acc_one[...] = jnp.zeros(acc_one.shape, F32)
        acc_two[...] = jnp.zeros(acc_two.shape, F32)
        acc_proj[...] = jnp.zeros(acc_proj.shape, F32)
        sums[...] = jnp.zeros(sums.shape, F32)
        sums[7:8, :] = out_sums[0:1, :]

    def add_row(row, values):
        sums[pl.ds(row, 1), :] += jnp.sum(values, axis=0, keepdims=True)

    own = mixed[...]
    residual = tokens[...].astype(F32) + dot(own, proj[...], NT) + vectors[4:5, :]
    normed, rate = norm_parts(residual)
    gain = vectors[5:6, :]
    second_in = (normed * gain + vectors[6:7, :]).astype(LOW)
    out_low = cotangent[...]
    grad_out = out_low.astype(F32)
    second_turned = second_in.T
    out_turned = out_turned[...]
    totals = [residual + vectors[7:8, :], jnp.zeros(residual.shape, F32)]

    count = hidden_width // FF_CHUNK
    ones = jnp.ones((16, MLP_TILE), LOW)
    second_and_ones = jnp.concatenate([second_turned, ones], axis=0)
    hiddens, slopes, kept = {}, {}, {}

    def lanes_of(number):
        return pl.ds(number * FF_CHUNK, FF_CHUNK)

    def make_hidden(number):
        hiddens[number] = dot(second_in, one[:, lanes_of(number)])

    def make_slope(number):
        slopes[number] = dot(out_low, two[:, lanes_of(number)])

    def add_one(number):
        acc_one[:, lanes_of(number)] += dot(second_and_ones, kept[number][1])

    def add_two(number):
        acc_two[:, lanes_of(number)] += dot(out_turned, kept[number][0])

    def add_result(number):
        totals[0] = totals[0] + dot(kept[number][0], two[:, lanes_of(number)], NT)

    def add_second(number):
        totals[1] = totals[1] + dot(kept[number][1], one[:, lanes_of(number)], NT)

    make_hidden(0)
    make_slope(0)
    for number in range(count):
        between = []
        if number + 1 < count:
            between += [functools.partial(f, number + 1) for f in (make_hidden, make_slope)]
        if number > 0:
            between += [
                functools.partial(f, number - 1)
                for f in (add_result, add_second, add_one, add_two)
            ]
        kept[number] = gelu_rows(
            hiddens.pop(number), bias[0:1, lanes_of(number)], slopes.pop(number), between
        )
    for f in (add_result, add_second, add_one, add_two):
        f(count - 1)
    result, grad_second = totals
    output[...] = result.astype(LOW)
    add_row(5, grad_second * normed)
    add_row(6, grad_second)
    grad_res = grad_out + norm_back(grad_second, normed, rate, gain)
    grad_residual[...] = grad_res
    branch = grad_res.astype(LOW)
    add_row(4, branch.astype(F32))
    acc_proj[...] += dot(branch.T, own)
    grad_own = dot(branch, proj[...]).astype(LOW)
    grad_mixed[...] = grad_own
    high, rest = halves(grad_own.astype(F32) * own.astype(F32))
    head = lax.broadcasted_iota(jnp.int32, (16, width), 0)
    chosen = (lane_numbers((16, width)) // (width // HEADS) == head).astype(F32).astype(LOW)
    inner[...] = (dot(chosen, high, NT) + dot(chosen, rest, NT))[:8]

    @pl.when(step == pl.num_programs(0) - 1)
    def finish():
        total = acc_proj[...]
        for number in range(parts):
            turned = pltpu.roll(total, (width - block * number) % width, 1) if number else total
            proj_parts[numbers[PLACES + number]] = turned[:, :SUB].astype(LOW)
        for part in range(parts):
            ref, at = (grads_near, part) if part < mid else (grads_far, part - mid)
            lanes = pl.ds(part * width, width)
            for group in range(ref.shape[0]):
                here = pl.ds(group * ref.shape[2], ref.shape[2])
                ref[group, at, :, :width] = acc_one[here, lanes].astype(LOW)
                ref[group, at, :, width:last_at] = acc_two[here, lanes].astype(LOW)
                ref[group, at, :, last_at:] = proj_parts[part, here, :]
            sums[pl.ds(8 + numbers[OWNERS + part], 1), :] = acc_one[width : width + 1, lanes]


def mlp_both(numbers, near, far, vectors, mixed, tokens, cotangent, out_turned, out_sums):
    rows, width = tokens.shape
    parts = near.shape[1] + far.shape[1]
    hidden_width = parts * width
    tile = pl.BlockSpec((MLP_TILE, width), lambda s, *_: (s, 0))
    whole = lambda *dims: pl.BlockSpec(dims, lambda s, *_: (0,) * len(dims))
    return pl.pallas_call(
        mlp_kernel,
        grid_spec=pltpu.PrefetchScalarGridSpec(
            num_scalar_prefetch=1,
            grid=(rows // MLP_TILE,),
            in_specs=[
                whole(*near.shape), whole(*far.shape), whole(*vectors.shape), tile, tile, tile,
                pl.BlockSpec((width, MLP_TILE), lambda s, *_: (0, s)), whole(*out_sums.shape),
            ],
            out_specs=[
                tile,
                tile,
                tile,
                pl.BlockSpec((8, MLP_TILE), lambda s, *_: (0, s)),
                whole(*near.shape),
                whole(*far.shape),
                whole(*vectors.shape),
            ],
            scratch_shapes=[
                pltpu.VMEM((width, hidden_width), LOW),
                pltpu.VMEM((width, hidden_width), LOW),
                pltpu.VMEM((parts, width, SUB), LOW),
                pltpu.VMEM((width, width), LOW),
                pltpu.VMEM((width + 16, hidden_width), F32),
                pltpu.VMEM((width, hidden_width), F32),
                pltpu.VMEM((width, width), F32),
                pltpu.VMEM((8, hidden_width), F32),
            ],
        ),
        out_shape=[
            jax.ShapeDtypeStruct((rows, width), LOW),
            jax.ShapeDtypeStruct((rows, width), F32),
            jax.ShapeDtypeStruct((rows, width), LOW),
            jax.ShapeDtypeStruct((8, rows), F32),
            jax.ShapeDtypeStruct(near.shape, LOW),
            jax.ShapeDtypeStruct(far.shape, LOW),
            jax.ShapeDtypeStruct(vectors.shape, F32),
        ],
        compiler_params=pltpu.CompilerParams(vmem_limit_bytes=VMEM_LIMIT),
        cost_estimate=pl.CostEstimate(
            flops=34_000_000_000, bytes_accessed=20_000_000, transcendentals=6_000_000
        ),
        name="mlp_both",
    )(numbers, near, far, vectors, mixed, tokens, cotangent, out_turned, out_sums)


def attend_back_kernel(
    numbers,
    query,
    key_turned,
    value,
    probs,
    inner,
    grad_mixed,
    normed_turned,
    weight,
    vectors,
    sums,
    grad_qkv,
    near,
    far,
    grad_query,
    acc_key,
    acc_value,
    acc_sums,
    normed_sums,
    blocks,
    rows,
):
    step = pl.program_id(0)
    chunks = pl.num_programs(0) - 1
    pairs = range(PAIRS)
    count = len(pairs)
    scale = (SUB // 2) ** (-0.5)

    @pl.when(step == 0)
    def clear():
        acc_key[...] = jnp.zeros(acc_key.shape, F32)
        acc_value[...] = jnp.zeros(acc_value.shape, F32)
        normed_sums[...] = jnp.zeros(normed_sums.shape, F32)
        acc_sums[...] = jnp.zeros(acc_sums.shape, F32)

    @pl.when(step < chunks)
    def attend():
        def place(number):
            sub, at = number // count, number % count
            start = pl.multiple_of((step * (TILE // SUB) + sub) * SUB, SUB)
            return sub, at, start, pl.ds(start, SPAN), pl.ds(at * SUB, SUB)

        def slope(number):
            sub, _, _, near_rows, heads = place(number)
            grad = both_heads(grad_mixed[pl.ds(sub * SUB, SUB), heads])
            return dot(value[near_rows, heads], grad, NT)

        def soften(number, slopes):
            sub, at, _, _, _ = place(number)
            pair = pairs[at]
            cols = pl.ds(sub * SUB, SUB)
            both = []
            for head in range(2):
                lanes = slice(head * SUB, (head + 1) * SUB)
                less = slopes[:, lanes] - inner[2 * pair + head : 2 * pair + head + 1, cols]
                both.append((probs[at, sub, :, lanes].astype(F32) * less).astype(LOW))
            return jnp.concatenate(both, axis=1)

        def collect(number, scores):
            sub, at, start, near_rows, heads = place(number)
            first, second = halves_of(dot(key_turned[heads, near_rows], scores))
            turned = (jnp.concatenate([first, second], axis=0) * scale).astype(LOW)
            grad_query[pl.ds(start, SUB), heads] = turned.T
            wanted = both_heads(query[pl.ds(start + MARGIN, SUB), heads])
            acc_key[near_rows, heads] += dot(scores, wanted)
            grad = both_heads(grad_mixed[pl.ds(sub * SUB, SUB), heads])
            acc_value[near_rows, heads] += dot(probs[at, sub], grad)

        staged(TILE // SUB * count, slope, soften, collect)

    @pl.when(step > 0)
    def collect():
        here = pl.ds(pl.multiple_of((step - 1) * TILE, SUB), TILE)
        there = pl.ds(pl.multiple_of((step - 1) * TILE + MARGIN, SUB), TILE)
        parts = (
            grad_query[here, :],
            acc_key[there, :].astype(LOW),
            acc_value[there, :].astype(LOW),
        )
        joined = jnp.concatenate(parts, axis=1)
        grad_qkv[...] = joined
        normed_sums[...] += dot(normed_turned[...], joined)
        acc_sums[0:1, :] += jnp.sum(joined.astype(F32), axis=0, keepdims=True)

    @pl.when(step == chunks)
    def finish():
        weight_grad(
            numbers, normed_sums[...], acc_sums[0:1, :], weight, vectors, sums, near, far, blocks, rows
        )


def weight_grad(numbers, total, columns, weight, vectors, sums, near, far, blocks, rows):
    width = weight.shape[0]
    parts, mid = blocks.shape[0], near.shape[0]
    block = 3 * width // parts
    rows_each = 12 // parts
    wide = weight[...].astype(F32)
    grad_gain = jnp.sum(total * wide, axis=1, keepdims=True)
    grad_shift = jnp.sum(wide * columns, axis=1, keepdims=True)
    rows[...] = jnp.zeros(rows.shape, F32)
    rows[0:VEC_LANES, :] = sums[...]
    rows[2:3, :] = columns[:, :width]
    rows[3:4, :] = columns[:, 2 * width :]
    rows[VEC_LANES : 2 * VEC_LANES, :] = vectors[...]
    turned = rows[...].T
    gain = turned[:, VEC_LANES : VEC_LANES + 1]
    shift = turned[:, VEC_LANES + 1 : VEC_LANES + 2]
    lane = lane_numbers(turned.shape)
    turned = jnp.where(lane == 0, grad_gain, jnp.where(lane == 1, grad_shift, turned))
    total = total * gain + shift * columns
    at = block - 2 * SUB
    for number in range(parts):
        away = (3 * width - block * number) % (3 * width)
        piece = (pltpu.roll(total, away, 1) if number else total)[:, :width]
        vec = pltpu.roll(turned, (at - rows_each * number) % SUB, 1)
        last = jnp.where(lane < at, piece[:, 2 * SUB :], 0.0)
        last = jnp.where((lane >= at) & (lane < at + rows_each), vec, last)
        at_place = numbers[PLACES + number]
        blocks[at_place, :, : 2 * SUB] = piece[:, : 2 * SUB].astype(LOW)
        blocks[at_place, :, 2 * SUB :] = last.astype(LOW)
    near[...] = blocks[:mid]
    far[...] = blocks[mid:]


def attend_backward(
    numbers, parts, query, key_turned, value, probs, inner, grad_mixed, normed_turned, weight,
    vectors, sums,
):
    width, rows = normed_turned.shape
    padded = query.shape[0]
    chunks = rows // TILE
    tiles = TILE // SUB
    now = lambda s: jnp.minimum(s, chunks - 1)
    before = lambda s: jnp.maximum(s - 1, 0)
    whole = lambda *dims: pl.BlockSpec(dims, lambda s, *_: (0,) * len(dims))
    half = (parts // 2, width, width)
    return pl.pallas_call(
        attend_back_kernel,
        grid_spec=pltpu.PrefetchScalarGridSpec(
            num_scalar_prefetch=1,
            grid=(chunks + 1,),
            in_specs=[
                whole(padded, width),
                whole(width, padded),
                whole(padded, width),
                pl.BlockSpec((PAIRS, tiles, SPAN, 2 * SUB), lambda s, *_: (0, now(s), 0, 0)),
                pl.BlockSpec((8, TILE), lambda s, *_: (0, now(s))),
                pl.BlockSpec((TILE, width), lambda s, *_: (now(s), 0)),
                pl.BlockSpec((width, TILE), lambda s, *_: (0, before(s))),
                whole(*weight.shape),
                whole(*vectors.shape),
                whole(*sums.shape),
            ],
            out_specs=[
                pl.BlockSpec((TILE, 3 * width), lambda s, *_: (before(s), 0)),
                whole(*half),
                whole(*half),
            ],
            scratch_shapes=[
                pltpu.VMEM((rows, width), LOW),
                pltpu.VMEM((padded, width), F32),
                pltpu.VMEM((padded, width), F32),
                pltpu.VMEM((8, 3 * width), F32),
                pltpu.VMEM((width, 3 * width), F32),
                pltpu.VMEM((parts, width, width), LOW),
                pltpu.VMEM((SUB, width), F32),
            ],
        ),
        out_shape=[
            jax.ShapeDtypeStruct((rows, 3 * width), LOW),
            jax.ShapeDtypeStruct(half, LOW),
            jax.ShapeDtypeStruct(half, LOW),
        ],
        compiler_params=pltpu.CompilerParams(vmem_limit_bytes=VMEM_LIMIT),
        cost_estimate=pl.CostEstimate(
            flops=16_000_000_000, bytes_accessed=24_000_000, transcendentals=0
        ),
        name="attend_backward",
    )(
        numbers, query, key_turned, value, probs, inner, grad_mixed, normed_turned, weight, vectors,
        sums,
    )


def input_grad_kernel(weight, vectors, tokens, grad_residual, grad_qkv, input_grad):
    normed, rate = norm_parts(tokens[...].astype(F32))
    grad_first = dot(grad_qkv[...], weight[...], NT)
    back = norm_back(grad_first, normed, rate, vectors[0:1, :])
    input_grad[...] = (grad_residual[...] + back).astype(LOW)


def input_gradient(weight, vectors, tokens, grad_residual, grad_qkv):
    rows, width = tokens.shape
    size = TILE
    tile = pl.BlockSpec((size, width), lambda s: (s, 0))
    whole = lambda ref: pl.BlockSpec(ref.shape, lambda s: (0, 0))
    return pl.pallas_call(
        input_grad_kernel,
        grid=(rows // size,),
        in_specs=[
            whole(weight), whole(vectors), tile, tile,
            pl.BlockSpec((size, 3 * width), lambda s: (s, 0)),
        ],
        out_specs=tile,
        out_shape=jax.ShapeDtypeStruct((rows, width), LOW),
        compiler_params=pltpu.CompilerParams(vmem_limit_bytes=VMEM_LIMIT),
        cost_estimate=pl.CostEstimate(
            flops=4_000_000_000, bytes_accessed=13_000_000, transcendentals=2048
        ),
        name="input_gradient",
    )(weight, vectors, tokens, grad_residual, grad_qkv)


def halves(value):
    high = value.astype(LOW)
    return high, (value - high.astype(F32)).astype(LOW)


def dot_three(left, right):
    tall = jnp.concatenate([right[0], right[0], right[1]], axis=0)
    return dot(jnp.concatenate([left[0], left[1], left[0]], axis=1), tall)


def newton_rows(blocks, offset, rows, store):
    gram = dot(blocks[0], blocks[0], NT)
    for part in blocks[1:]:
        gram = gram + dot(part, part, NT)
    depth = gram.shape[0]
    down = lax.broadcasted_iota(jnp.int32, (depth, depth), 0)
    eye = (down == lane_numbers((depth, depth))).astype(F32)
    norm = 1.0 / (jnp.sqrt(jnp.sum(gram * eye, keepdims=True)) + 1e-07)
    gram = gram * (norm * norm)
    place = lax.broadcasted_iota(jnp.int32, (rows, depth), 0) + offset
    left = jnp.where(place == lane_numbers((rows, depth)), norm, 0.0)
    store[0:depth, :] = gram
    store[depth:, :] = left

    @pl.loop(0, NS_STEPS - 1)
    def advance(_):
        both = halves(store[...])
        pair = [part[:depth] for part in both]
        down = lax.broadcasted_iota(jnp.int32, (depth, depth), 0)
        eye = (down == lane_numbers((depth, depth))).astype(F32)
        square = dot_three(pair, pair)
        poly = halves(NEWTON_A * eye + NEWTON_B * store[0:depth, :] + NEWTON_C * square)
        made = dot_three(both, poly)
        store[depth:, :] = made[depth:]
        store[0:depth, :] = dot_three(halves(made[:depth]), poly)

    left = store[depth:, :]
    pair = halves(store[0:depth, :])
    once = dot_three(halves(left), pair)
    return NEWTON_A * left + NEWTON_B * once + NEWTON_C * dot_three(halves(once), pair)


def newton_store(depth, rows):
    return pltpu.VMEM((depth + tall_of(rows), depth), F32)


def stepped(left, own, height, old):
    high, rest = halves(left)
    ortho = (dot(high, own) + dot(rest, own))[: old.shape[0], : old.shape[1]]
    return old * (1.0 - MUON_RATE * MUON_DECAY) - (MUON_RATE * 0.2 * math.sqrt(height)) * ortho


def kept_lanes(value, low, high):
    lane = lane_numbers(value.shape)
    return jnp.where((lane >= low) & (lane < high), value.astype(F32), 0.0).astype(LOW)


def tall_of(rows):
    return -(-rows // 16) * 16


def muon_kernel(height, numbers, *refs):
    old, new, copy, store = refs[-4:]
    count = old.shape[1]
    blocks = [kept_lanes(ref[...], 0, count) for ref in refs[:-4]]
    left = newton_rows(blocks, numbers[OFFSET], tall_of(old.shape[0]), store)
    result = stepped(left, blocks[0], height, old[...])
    new[...] = result
    copy[...] = result.astype(LOW)


def muon(height, numbers, blocks, old):
    vmem = pl.BlockSpec(memory_space=pltpu.VMEM)

    def kernel(*refs):
        muon_kernel(height, *refs)

    return pl.pallas_call(
        kernel,
        in_specs=[pl.BlockSpec(memory_space=pltpu.SMEM)] + [vmem] * (len(blocks) + 1),
        out_specs=[vmem, vmem],
        out_shape=[
            jax.ShapeDtypeStruct(old.shape, F32),
            jax.ShapeDtypeStruct(old.shape, LOW),
        ],
        scratch_shapes=[newton_store(blocks[0].shape[0], old.shape[0])],
        compiler_params=pltpu.CompilerParams(vmem_limit_bytes=VMEM_LIMIT),
        cost_estimate=pl.CostEstimate(
            flops=9_000_000_000, bytes_accessed=2_000_000, transcendentals=10
        ),
        name="muon",
    )(numbers, *blocks, old)


def pick_kernel(count, numbers, *refs):
    pieces, columns, outs = refs[:count], refs[count], refs[count + 1 :]
    share = pieces[0].shape[0]
    for k, piece in enumerate(pieces):
        columns[k * share : (k + 1) * share, :] = piece[...]
        for n, out in enumerate(outs):
            at = pl.multiple_of(numbers[STARTS + n] * SUB, SUB)
            out[k * share : (k + 1) * share, :] = piece[:, pl.ds(at, out.shape[1])]


def pick(numbers, pieces, count):
    depth = len(pieces) * pieces[0].shape[0]
    vmem = pl.BlockSpec(memory_space=pltpu.VMEM)

    def kernel(*refs):
        pick_kernel(len(pieces), *refs)

    return pl.pallas_call(
        kernel,
        in_specs=[pl.BlockSpec(memory_space=pltpu.SMEM)] + [vmem] * len(pieces),
        out_specs=[vmem] * (count + 1),
        out_shape=[jax.ShapeDtypeStruct((depth, pieces[0].shape[1]), LOW)]
        + [jax.ShapeDtypeStruct((depth, depth), LOW)] * count,
        name="pick",
    )(numbers, *pieces)


def newton_kernel(at, numbers, *refs):
    left, store = refs[-2:]
    bounds = numbers[LOW_LANE], numbers[HIGH_LANE]
    blocks = [kept_lanes(ref[...], *bounds) for ref in refs[:-2]]
    start = numbers[OFFSET] if at is None else at
    left[...] = newton_rows(blocks, start, left.shape[0], store)


def newton(at, numbers, blocks, rows):
    vmem = pl.BlockSpec(memory_space=pltpu.VMEM)

    def kernel(*refs):
        newton_kernel(at, *refs)

    return pl.pallas_call(
        kernel,
        in_specs=[pl.BlockSpec(memory_space=pltpu.SMEM)] + [vmem] * len(blocks),
        out_specs=vmem,
        out_shape=jax.ShapeDtypeStruct((tall_of(rows), blocks[0].shape[0]), F32),
        scratch_shapes=[newton_store(blocks[0].shape[0], rows)],
        compiler_params=pltpu.CompilerParams(vmem_limit_bytes=VMEM_LIMIT),
        cost_estimate=pl.CostEstimate(
            flops=9_000_000_000, bytes_accessed=2_000_000, transcendentals=10
        ),
        name="newton",
    )(numbers, *blocks)


def finish_kernel(heights, lanes, numbers, columns, *refs):
    count = len(heights)
    store = refs[-1]
    news = refs[-1 - 2 * count : -1]
    olds = refs[-1 - 3 * count : -1 - 2 * count]
    lefts = refs[: -1 - 3 * count]
    for n, left in enumerate(lefts):
        store[n] = left[...]
    for n in range(count):
        wide = -(-olds[n].shape[1] // SUB) * SUB
        own = columns[:, lanes[n] : lanes[n] + wide]
        result = stepped(store[numbers[WHICH + n]], own, heights[n], olds[n][...])
        news[2 * n][...] = result
        news[2 * n + 1][...] = result.astype(LOW)


def finish(heights, lanes, numbers, columns, lefts, olds):
    vmem = pl.BlockSpec(memory_space=pltpu.VMEM)
    count = len(olds)

    def kernel(*refs):
        finish_kernel(heights, lanes, *refs)

    outs = pl.pallas_call(
        kernel,
        in_specs=[pl.BlockSpec(memory_space=pltpu.SMEM)] + [vmem] * (1 + len(lefts) + count),
        out_specs=[vmem] * (2 * count),
        out_shape=[
            jax.ShapeDtypeStruct(old.shape, kind) for old in olds for kind in (F32, LOW)
        ],
        scratch_shapes=[pltpu.VMEM((len(lefts), *lefts[0].shape), F32)],
        compiler_params=pltpu.CompilerParams(vmem_limit_bytes=VMEM_LIMIT),
        cost_estimate=pl.CostEstimate(
            flops=200_000_000, bytes_accessed=2_000_000, transcendentals=0
        ),
        name="finish",
    )(numbers, columns, *lefts, *olds)
    return [(outs[2 * n], outs[2 * n + 1]) for n in range(count)]


def exchange(x, axis, mask):
    size = lax.axis_size(axis)
    return lax.ppermute(x, axis, [(i, i ^ mask) for i in range(size)])


def place_masks(size):
    masks = [0]
    bit = size // 2
    while bit >= 1:
        masks = masks + [m ^ bit for m in masks]
        bit //= 2
    return masks


def from_columns(own):
    size = lax.axis_size("dp")
    sent = jnp.broadcast_to(own[None], (size, *own.shape))
    return lax.all_to_all(sent, "dp", split_axis=0, concat_axis=0, tiled=True)


def over_columns(own):
    return from_columns(own).reshape(-1, own.shape[1])


def device_numbers(dp, ns, share, width, proj_rows):
    masks = place_masks(ns)
    tasks = [(0, 0, width), (width // SUB, 0, width)]
    tasks += [(width // SUB + 1, 2 * SUB, 2 * SUB + proj_rows)] * (ns - 2)
    table = np.zeros((dp * ns, 24), np.int32)
    for device in range(dp * ns):
        column, index = device // ns, device % ns
        row = table[device]
        for n in range(ns):
            row[OWNERS + n] = index ^ masks[n]
            row[PLACES + (index ^ masks[n])] = n
            row[STARTS + n] = tasks[index ^ n][0]
        for n in range(3):
            row[WHICH + n] = index ^ n
        row[OFFSET] = column * share
        row[COLUMN] = column
        row[LOW_LANE], row[HIGH_LANE] = tasks[index][1:]
    return table


def half_rows(own):
    held = [own]
    bit = lax.axis_size("ns") // 2
    while bit > 1:
        held = held + [exchange(block, "ns", bit) for block in held]
        bit //= 2
    return held


def added(keep, got):
    return (keep.astype(F32) + got.astype(F32)).astype(LOW)


def sum_columns(pieces):
    return summed(lax.all_to_all(pieces, "dp", split_axis=0, concat_axis=0, tiled=True))


def summed(pieces):
    return jnp.sum(pieces.astype(F32), axis=0)


def columns_direct(own):
    devices = lax.axis_size("dp")
    if devices > 8 or own.shape[0] % 16:
        return [over_columns(own)], None
    return [own] + [exchange(own, "dp", mask) for mask in range(1, devices)], 0


def widened(arrays, lanes):
    joined = jnp.concatenate(arrays, axis=1)
    return jnp.pad(joined, ((0, 0), (0, lanes - joined.shape[1])))


def per_device(
    tokens,
    cotangent,
    segment,
    valid_rows,
    qkv_weight,
    proj_weight,
    fc1_weight,
    fc2_weight,
    qkv_moment,
    proj_moment,
    fc1_moment,
    fc2_moment,
    vectors,
    vector_moment,
    vector_square,
):
    rows, width = tokens.shape
    ns = lax.axis_size("ns")
    qkv_w, proj_w, fc1_w, fc2_w = (w.T for w in (qkv_weight, proj_weight, fc1_weight, fc2_weight))
    qkv_m, proj_m, fc1_m, fc2_m = (w.T for w in (qkv_moment, proj_moment, fc1_moment, fc2_moment))
    share, count = qkv_w.shape
    vec_rows = vectors.shape[0]
    first_lanes = width
    later_lanes = 2 * width + SUB

    table = device_numbers(lax.axis_size("dp"), ns, share, width, proj_w.shape[1])
    device = lax.axis_index("dp") * ns + lax.axis_index("ns")
    numbers = lax.dynamic_slice(jnp.asarray(table), (device, 0), (1, table.shape[1]))[0]

    row_ids = jnp.where(
        valid_rows > 0, segment, rows + jnp.arange(rows, dtype=jnp.int32)
    ).astype(F32)
    ids = jnp.pad(row_ids, (MARGIN, MARGIN), constant_values=-1.0).reshape(-1, SUB)
    ids = jnp.pad(ids, ((0, -ids.shape[0] % 8), (0, 0)), constant_values=-1.0)

    later_own = widened([fc1_w, fc2_w, proj_w], later_lanes).astype(LOW)
    later_pair = jnp.stack([later_own, exchange(later_own, "ns", ns // 2)])
    first_own = widened([qkv_w, vectors.T], first_lanes).astype(LOW)
    prepared = prepare(tokens, cotangent, ids)
    first_pieces = half_rows(over_columns(first_own))
    first_pieces, prepared = lax.optimization_barrier((first_pieces, prepared))
    normed, normed_turned, out_turned, columns, out_sums = prepared
    first_pieces = first_pieces + [exchange(piece, "ns", 1) for piece in first_pieces]
    later_near = from_columns(later_pair)
    if share % 16:
        later_near = jnp.moveaxis(later_near, 0, 1).reshape(1, ns // 2, width, later_lanes)

    query, _, value, key_turned, mixed, probs, weight, vector_full = attend_forward(
        numbers, first_pieces, normed, ids, columns
    )
    later_near, mixed = lax.optimization_barrier((later_near, mixed))
    later_far = exchange(later_near, "ns", 1)
    output, grad_residual, grad_mixed, inner, grads_near, grads_far, sums = mlp_both(
        numbers, later_near, later_far, vector_full, mixed, tokens, cotangent, out_turned, out_sums
    )
    held = added(grads_near, exchange(grads_far, "ns", 1))
    held, grad_mixed = lax.optimization_barrier((held, grad_mixed))
    if share % 16:
        held = jnp.moveaxis(held.reshape(ns // 2, -1, share, later_lanes), 1, 0)
    later_got = lax.all_to_all(held, "dp", split_axis=0, concat_axis=0, tiled=True)

    grad_qkv, grads_near, grads_far = attend_backward(
        numbers, ns, query, key_turned, value, probs, inner, grad_mixed, normed_turned, weight,
        vector_full, sums,
    )
    held = added(grads_near, exchange(grads_far, "ns", 1))
    got = exchange(held[1], "ns", ns // 2)
    input_grad = input_gradient(weight, vector_full, tokens, grad_residual, grad_qkv)
    got, input_grad, later_got = lax.optimization_barrier((got, input_grad, later_got))
    first_held = added(held[0], got).reshape(lax.axis_size("dp"), share, first_lanes)
    first_owned = sum_columns(first_held)
    later_sums = summed(later_got)
    later_owned = later_sums[0] + exchange(later_sums[1].astype(LOW), "ns", ns // 2).astype(F32)
    later_moment = later_owned + 0.5 * widened([fc1_m, fc2_m, proj_m], later_lanes)
    pieces, at = columns_direct(later_moment.astype(LOW))
    columns, *chosen = pick(numbers, pieces, ns)
    blocks = [chosen[0]] + [exchange(chosen[mask], "ns", mask) for mask in range(1, ns)]

    first_moment = first_owned + 0.5 * widened([qkv_m], first_lanes)
    first_pieces = half_rows(over_columns(first_moment.astype(LOW)))
    blocks, first_pieces = lax.optimization_barrier((blocks, first_pieces))
    first_pieces = first_pieces + [exchange(piece, "ns", 1) for piece in first_pieces]
    left = newton(at, numbers, blocks, share)
    left, first_pieces[0] = lax.optimization_barrier((left, first_pieces[0]))
    qkv_new = muon(count * ns, numbers, first_pieces, qkv_w)
    lefts = [left] + [exchange(left, "ns", mask) for mask in range(1, ns)]
    lefts, qkv_new = lax.optimization_barrier((lefts, qkv_new))
    fc1_new, fc2_new, proj_new = finish(
        [w.shape[1] * ns for w in (fc1_w, fc2_w, proj_w)],
        (0, width, 2 * width),
        numbers,
        columns,
        lefts,
        (fc1_w, fc2_w, proj_w),
    )

    news = (qkv_new, proj_new, fc1_new, fc2_new)
    moments_new = (
        first_moment[:, :count],
        later_moment[:, 2 * width : 2 * width + proj_w.shape[1]],
        later_moment[:, :width],
        later_moment[:, width : 2 * width],
    )

    vector_grad = first_owned[:, count : count + vec_rows].T
    first_new = BETA_ONE * vector_moment + (1.0 - BETA_ONE) * vector_grad
    second_new = BETA_TWO * vector_square + (1.0 - BETA_TWO) * vector_grad * vector_grad
    first_hat = first_new / (1.0 - BETA_ONE**STEP)
    second_hat = second_new / (1.0 - BETA_TWO**STEP)
    vectors_new = vectors - ADAM_RATE * first_hat / (jnp.sqrt(second_hat) + ADAM_EPS)
    return (
        output,
        input_grad,
        *(new[0].T for new in news),
        *(m.T for m in moments_new),
        first_new,
        second_new,
        vectors_new,
        *(new[1].T for new in news),
    )


def solution(mesh):
    rows = P(("dp", "ns"), None)
    flat = P(("dp", "ns"))
    block = P("ns", "dp")
    return jax.shard_map(
        per_device,
        mesh=mesh,
        in_specs=(rows, rows, flat, flat) + (block,) * 11,
        out_specs=(rows, rows) + (block,) * 15,
        check_vma=False,
    )
```

```python
import functools
import math

import jax
import jax.numpy as jnp
import numpy as np
from jax import lax
from jax.experimental import pallas as pl
from jax.experimental.pallas import tpu as pltpu
from jax.sharding import PartitionSpec as P

HEADS = 6
PAIRS = 3
MARGIN = 128
NS_STEPS = 5
STEP = 10
TILE = 512
MLP_TILE = 512
FF_CHUNK = 256
SUB = 128
SPAN = 384
VEC_LANES = 16
GROUP = 2


EPS_NORM = 1e-06
NEWTON_A = 3.4445
NEWTON_B = -4.775
NEWTON_C = 2.0315
MUON_RATE = 0.2
MUON_DECAY = 0.1
ADAM_RATE = 0.4
BETA_ONE = 0.9
BETA_TWO = 0.999
ADAM_EPS = 1e-08
LOW = jnp.bfloat16
F32 = jnp.float32
TN = (((0,), (0,)), ((), ()))
NT = (((1,), (1,)), ((), ()))
NN = (((1,), (0,)), ((), ()))
VMEM_LIMIT = 56 * 1024 * 1024
ERF_P = 0.3275911
ERF_COEFS = (0.254829592, -0.284496736, 1.421413741, -1.453152027, 1.061405429)


def dot(left, right, dims=NN):
    return lax.dot_general(left, right, dims, preferred_element_type=F32)


PLACES, OWNERS, STARTS, WHICH, OFFSET, LOW_LANE, HIGH_LANE, COLUMN = 0, 4, 8, 12, 16, 17, 18, 19


def lane_numbers(shape):
    return lax.broadcasted_iota(jnp.int32, shape, len(shape) - 1)


def norm_parts(value):
    center = value - jnp.mean(value, axis=-1, keepdims=True)
    rate = lax.rsqrt(jnp.mean(center * center, axis=-1, keepdims=True) + EPS_NORM)
    return center * rate, rate


def norm_back(grad, normed, rate, gain):
    scaled = grad * gain
    first = jnp.mean(scaled, axis=-1, keepdims=True)
    second = jnp.mean(scaled * normed, axis=-1, keepdims=True)
    return rate * (scaled - first - normed * second)


def gelu_both(value):
    below = 1.0 + (ERF_P * 0.5**0.5) * jnp.abs(value)
    ratio = pl.reciprocal(below, approx=True)
    ratio = ratio * (2.0 - below * ratio)
    decay = jnp.exp2((value * value) * (-0.5 * math.log2(math.e)))
    poly = 0.5 * ERF_COEFS[4]
    for coef in ERF_COEFS[3::-1]:
        poly = poly * ratio + 0.5 * coef
    tail = poly * ratio * decay
    phi = jnp.where(value >= 0, 1.0 - tail, tail)
    return value * phi, phi + (value * (1.0 / math.sqrt(2.0 * math.pi))) * decay


def gelu_rows(hidden, bias, grad, between):
    active, back = [], []
    rows = hidden.shape[0]
    pieces = rows // 16
    for n in range(pieces):
        if n * len(between) // pieces != (n - 1) * len(between) // pieces:
            between[n * len(between) // pieces]()
        here = slice(n * 16, (n + 1) * 16)
        value, slope = gelu_both(hidden[here] + bias)
        active.append(value.astype(LOW))
        back.append((grad[here] * slope).astype(LOW))
    return jnp.concatenate(active, axis=0), jnp.concatenate(back, axis=0)


def halves_of(lanes):
    half = lanes.shape[0] // 2
    return lanes[:half, :SUB], lanes[half:, SUB:]


def staged(count, first, second, third):
    made = first(0)
    kept = None
    for n in range(count):
        coming = first(n + 1) if n + 1 < count else None
        if kept is not None:
            third(n - 1, kept)
        kept = second(n, made)
        made = coming
    third(count - 1, kept)


def both_heads(pair):
    first = (lane_numbers((1, SUB)) < SUB // 2).astype(F32).astype(pair.dtype)
    second = (lane_numbers((1, SUB)) >= SUB // 2).astype(F32).astype(pair.dtype)
    return jnp.concatenate([pair * first, pair * second], axis=0)


def fetch(pairs, sems):
    copies = [
        pltpu.make_async_copy(source, target, sems.at[n])
        for n, (source, target) in enumerate(pairs)
    ]
    for copy in copies:
        copy.start()
    for copy in copies:
        copy.wait()


def prepare_kernel(tokens, cotangent, ids, normed, normed_turned, out_turned, columns, sums):
    step = pl.program_id(0)
    parts = columns.shape[0] // SUB

    @pl.when(step == 0)
    def clear():
        sums[...] = jnp.zeros(sums.shape, F32)
        for number in range(parts):
            row = jnp.broadcast_to(ids[number : number + 1, :], (SUB, SUB))
            columns[number * SUB : (number + 1) * SUB, :] = row.T

    value, _ = norm_parts(tokens[...].astype(F32))
    normed[...] = value
    normed_turned[...] = value.astype(LOW).T
    out_low = cotangent[...]
    out_turned[...] = out_low.T
    sums[0:1, :] += jnp.sum(out_low.astype(F32), axis=0, keepdims=True)


def prepare(tokens, cotangent, ids):
    rows, width = tokens.shape
    padded = rows + 2 * MARGIN
    tile = pl.BlockSpec((TILE, width), lambda s: (s, 0))
    turned = pl.BlockSpec((width, TILE), lambda s: (0, s))
    whole = lambda *dims: pl.BlockSpec(dims, lambda s: (0,) * len(dims))
    return pl.pallas_call(
        prepare_kernel,
        grid=(rows // TILE,),
        in_specs=[tile, tile, whole(*ids.shape)],
        out_specs=[tile, turned, turned, whole(padded, SUB), whole(8, width)],
        out_shape=[
            jax.ShapeDtypeStruct((rows, width), F32),
            jax.ShapeDtypeStruct((width, rows), LOW),
            jax.ShapeDtypeStruct((width, rows), LOW),
            jax.ShapeDtypeStruct((padded, SUB), F32),
            jax.ShapeDtypeStruct((8, width), F32),
        ],
        compiler_params=pltpu.CompilerParams(vmem_limit_bytes=VMEM_LIMIT),
        cost_estimate=pl.CostEstimate(
            flops=20_000_000, bytes_accessed=12_000_000, transcendentals=2048
        ),
        name="prepare",
    )(tokens, cotangent, ids)


def attend_kernel(numbers, *refs):
    (normed, ids, columns, query, key, value, key_turned, mixed, probs, weight, vectors,
     gathered, pair_weight, value_turned, shifts, sems) = refs[-16:]
    pieces = refs[:-16]
    step = pl.program_id(0)
    chunks = pl.num_programs(0) - 1
    width = normed.shape[1]
    parts = len(pieces)
    block = 3 * width // parts
    rows_each = 12 // parts

    @pl.when(step == 0)
    def assemble():
        fetch([(piece, gathered.at[n]) for n, piece in enumerate(pieces)], sems)
        total = jnp.zeros((width, 3 * width), F32)
        turned = jnp.zeros((width, SUB), F32)
        for number in range(parts):
            piece = gathered[numbers[PLACES + number]].astype(F32)
            kept = jnp.where(lane_numbers(piece.shape) < block, piece, 0.0)
            wide = jnp.concatenate([kept, jnp.zeros((width, 2 * width), F32)], axis=1)
            total = total + (pltpu.roll(wide, block * number, 1) if number else wide)
            last = piece[:, 2 * SUB :]
            at = block - 2 * SUB
            lane = lane_numbers(last.shape)
            vec = jnp.where((lane >= at) & (lane < at + rows_each), last, 0.0)
            turned = turned + pltpu.roll(vec, (rows_each * number - at) % SUB, 1)
        total = total.astype(LOW)
        weight[...] = total
        pair_weight[...] = total[:, width:].T
        vectors[...] = turned.T[:VEC_LANES]
        shifts[...] = turned
        edges = (pl.ds(0, MARGIN), pl.ds(MARGIN + chunks * TILE, MARGIN))
        for edge in edges:
            for ref in (query, key, value):
                ref[edge, :] = jnp.zeros((MARGIN, width), LOW)
            for ref in (key_turned, value_turned):
                ref[:, edge] = jnp.zeros((width, MARGIN), LOW)

    @pl.when(step < chunks)
    def project():
        first_in = (normed[...] * vectors[0:1, :] + vectors[1:2, :]).astype(LOW)
        result = dot(first_in, weight[...])
        turned = dot(pair_weight[...], first_in, NT)
        here = pl.ds(pl.multiple_of(MARGIN + step * TILE, SUB), TILE)
        scale = (width // HEADS) ** (-0.5)
        made = (result[:, :width] + vectors[2:3, :]).astype(LOW) * jnp.asarray(scale, LOW)
        query[here, :] = made
        key[here, :] = result[:, width : 2 * width].astype(LOW)
        value[here, :] = (result[:, 2 * width :] + vectors[3:4, :]).astype(LOW)
        key_turned[:, here] = turned[:width].astype(LOW)
        value_turned[:, here] = (turned[width:] + shifts[:, 3:4]).astype(LOW)

    @pl.when(step > 0)
    def attend():
        def place(number):
            sub, pair = number // PAIRS, number % PAIRS
            tile = (step - 1) * (TILE // SUB) + sub
            start = pl.multiple_of(tile * SUB, SUB)
            return sub, pair, tile, start, pl.ds(start, SPAN), pl.ds(pair * SUB, SUB)

        def of_group(group):
            return range(group * GROUP, (group + 1) * GROUP)

        def score(group):
            made = []
            for number in of_group(group):
                _, _, _, start, near_rows, heads = place(number)
                wanted = both_heads(query[pl.ds(start + MARGIN, SUB), heads])
                made.append(dot(key[near_rows, heads], wanted, NT))
            return made

        def soften(group, made):
            own = []
            for number, scores in zip(of_group(group), made):
                _, _, tile, _, near_rows, _ = place(number)
                same = columns[near_rows, :] == ids[pl.ds(tile + 1, 1), :]
                own += [
                    jnp.where(same, scores[:, head * SUB : (head + 1) * SUB], -1e30)
                    for head in range(2)
                ]
            largest = [jnp.max(part, axis=0, keepdims=True) for part in own]
            expo = [jnp.exp(part - most) for part, most in zip(own, largest)]
            share = [1.0 / jnp.sum(part, axis=0, keepdims=True) for part in expo]
            scaled = [(part * by).astype(LOW) for part, by in zip(expo, share)]
            result = []
            for n, number in enumerate(of_group(group)):
                sub, pair, _, _, _, _ = place(number)
                result.append(jnp.concatenate(scaled[2 * n : 2 * n + 2], axis=1))
                probs[pair, sub] = result[-1]
            return result

        def mix(group, kept):
            for number, prob in zip(of_group(group), kept):
                sub, _, _, _, near_rows, heads = place(number)
                first, second = halves_of(dot(value_turned[heads, near_rows], prob))
                turned = jnp.concatenate([first, second], axis=0).astype(LOW)
                mixed[pl.ds(sub * SUB, SUB), heads] = turned.T

        staged(TILE // SUB * PAIRS // GROUP, score, soften, mix)


def attend_forward(numbers, pieces, normed, ids, columns):
    rows, width = normed.shape
    chunks = rows // TILE
    tiles = TILE // SUB
    parts = len(pieces)
    now = lambda s: jnp.minimum(s, chunks - 1)
    before = lambda s: jnp.maximum(s - 1, 0)
    whole = lambda *dims: pl.BlockSpec(dims, lambda s, *_: (0,) * len(dims))
    padded = rows + 2 * MARGIN
    return pl.pallas_call(
        attend_kernel,
        grid_spec=pltpu.PrefetchScalarGridSpec(
            num_scalar_prefetch=1,
            grid=(chunks + 1,),
            in_specs=[pl.BlockSpec(memory_space=pl.ANY)] * parts
            + [
                pl.BlockSpec((TILE, width), lambda s, *_: (now(s), 0)),
                whole(*ids.shape),
                whole(*columns.shape),
            ],
            out_specs=[
                whole(padded, width),
                whole(padded, width),
                whole(padded, width),
                whole(width, padded),
                pl.BlockSpec((TILE, width), lambda s, *_: (before(s), 0)),
                pl.BlockSpec((PAIRS, tiles, SPAN, 2 * SUB), lambda s, *_: (0, before(s), 0, 0)),
                whole(width, 3 * width),
                whole(VEC_LANES, width),
            ],
            scratch_shapes=[
                pltpu.VMEM((parts, *pieces[0].shape), LOW),
                pltpu.VMEM((2 * width, width), LOW),
                pltpu.VMEM((width, padded), LOW),
                pltpu.VMEM((width, SUB), F32),
                pltpu.SemaphoreType.DMA((parts,)),
            ],
        ),
        out_shape=[
            jax.ShapeDtypeStruct((padded, width), LOW),
            jax.ShapeDtypeStruct((padded, width), LOW),
            jax.ShapeDtypeStruct((padded, width), LOW),
            jax.ShapeDtypeStruct((width, padded), LOW),
            jax.ShapeDtypeStruct((rows, width), LOW),
            jax.ShapeDtypeStruct((PAIRS, rows // SUB, SPAN, 2 * SUB), LOW),
            jax.ShapeDtypeStruct((width, 3 * width), LOW),
            jax.ShapeDtypeStruct((VEC_LANES, width), F32),
        ],
        compiler_params=pltpu.CompilerParams(vmem_limit_bytes=VMEM_LIMIT),
        cost_estimate=pl.CostEstimate(
            flops=12_000_000_000, bytes_accessed=22_000_000, transcendentals=5_000_000
        ),
        name="attend_forward",
    )(numbers, *pieces, normed, ids, columns)


def mlp_kernel(numbers, near, far, *refs):
    (vectors, mixed, tokens, cotangent, out_turned, out_sums, output, grad_residual, grad_mixed, inner, grads_near,
     grads_far, sums, one, two, proj_parts, proj, acc_one, acc_two, acc_proj, bias
    ) = refs
    step = pl.program_id(0)
    width = tokens.shape[1]
    mid = near.shape[1]
    parts = mid + far.shape[1]
    block = width // parts
    last_at = 2 * width
    hidden_width = one.shape[1]

    @pl.when(step == 0)
    def assemble():
        for part in range(parts):
            ref, at = (near, part) if part < mid else (far, part - mid)
            lanes = pl.ds(part * width, width)
            for group in range(near.shape[0]):
                here = pl.ds(group * near.shape[2], near.shape[2])
                one[here, lanes] = ref[group, at, :, :width]
                two[here, lanes] = ref[group, at, :, width:last_at]
                proj_parts[part, here, :] = ref[group, at, :, last_at:]
        total = jnp.zeros((width, width), F32)
        for number in range(parts):
            piece = proj_parts[numbers[PLACES + number]].astype(F32)
            kept = jnp.where(lane_numbers(piece.shape) < block, piece, 0.0)
            wide = jnp.concatenate([kept, jnp.zeros((width, width - SUB), F32)], axis=1)
            total = total + (pltpu.roll(wide, block * number, 1) if number else wide)
        proj[...] = total.astype(LOW)
        for part in range(parts):
            row = vectors[pl.ds(8 + numbers[OWNERS + part], 1), :]
            bias[0:1, part * width : (part + 1) * width] = row
        acc_one[...] = jnp.zeros(acc_one.shape, F32)
        acc_two[...] = jnp.zeros(acc_two.shape, F32)
        acc_proj[...] = jnp.zeros(acc_proj.shape, F32)
        sums[...] = jnp.zeros(sums.shape, F32)
        sums[7:8, :] = out_sums[0:1, :]

    def add_row(row, values):
        sums[pl.ds(row, 1), :] += jnp.sum(values, axis=0, keepdims=True)

    own = mixed[...]
    residual = tokens[...].astype(F32) + dot(own, proj[...], NT) + vectors[4:5, :]
    normed, rate = norm_parts(residual)
    gain = vectors[5:6, :]
    second_in = (normed * gain + vectors[6:7, :]).astype(LOW)
    out_low = cotangent[...]
    grad_out = out_low.astype(F32)
    second_turned = second_in.T
    out_turned = out_turned[...]
    totals = [residual + vectors[7:8, :], jnp.zeros(residual.shape, F32)]

    count = hidden_width // FF_CHUNK
    ones = jnp.ones((16, MLP_TILE), LOW)
    second_and_ones = jnp.concatenate([second_turned, ones], axis=0)
    hiddens, slopes, kept = {}, {}, {}

    def lanes_of(number):
        return pl.ds(number * FF_CHUNK, FF_CHUNK)

    def make_hidden(number):
        hiddens[number] = dot(second_in, one[:, lanes_of(number)])

    def make_slope(number):
        slopes[number] = dot(out_low, two[:, lanes_of(number)])

    def add_one(number):
        acc_one[:, lanes_of(number)] += dot(second_and_ones, kept[number][1])

    def add_two(number):
        acc_two[:, lanes_of(number)] += dot(out_turned, kept[number][0])

    def add_result(number):
        totals[0] = totals[0] + dot(kept[number][0], two[:, lanes_of(number)], NT)

    def add_second(number):
        totals[1] = totals[1] + dot(kept[number][1], one[:, lanes_of(number)], NT)

    make_hidden(0)
    make_slope(0)
    for number in range(count):
        between = []
        if number + 1 < count:
            between += [functools.partial(f, number + 1) for f in (make_hidden, make_slope)]
        if number > 0:
            between += [
                functools.partial(f, number - 1)
                for f in (add_result, add_second, add_one, add_two)
            ]
        kept[number] = gelu_rows(
            hiddens.pop(number), bias[0:1, lanes_of(number)], slopes.pop(number), between
        )
    for f in (add_result, add_second, add_one, add_two):
        f(count - 1)
    result, grad_second = totals
    output[...] = result.astype(LOW)
    add_row(5, grad_second * normed)
    add_row(6, grad_second)
    grad_res = grad_out + norm_back(grad_second, normed, rate, gain)
    grad_residual[...] = grad_res
    branch = grad_res.astype(LOW)
    add_row(4, branch.astype(F32))
    acc_proj[...] += dot(branch.T, own)
    grad_own = dot(branch, proj[...]).astype(LOW)
    grad_mixed[...] = grad_own
    high, rest = halves(grad_own.astype(F32) * own.astype(F32))
    head = lax.broadcasted_iota(jnp.int32, (16, width), 0)
    chosen = (lane_numbers((16, width)) // (width // HEADS) == head).astype(F32).astype(LOW)
    inner[...] = (dot(chosen, high, NT) + dot(chosen, rest, NT))[:8]

    @pl.when(step == pl.num_programs(0) - 1)
    def finish():
        total = acc_proj[...]
        for number in range(parts):
            turned = pltpu.roll(total, (width - block * number) % width, 1) if number else total
            proj_parts[numbers[PLACES + number]] = turned[:, :SUB].astype(LOW)
        for part in range(parts):
            ref, at = (grads_near, part) if part < mid else (grads_far, part - mid)
            lanes = pl.ds(part * width, width)
            for group in range(ref.shape[0]):
                here = pl.ds(group * ref.shape[2], ref.shape[2])
                ref[group, at, :, :width] = acc_one[here, lanes].astype(LOW)
                ref[group, at, :, width:last_at] = acc_two[here, lanes].astype(LOW)
                ref[group, at, :, last_at:] = proj_parts[part, here, :]
            sums[pl.ds(8 + numbers[OWNERS + part], 1), :] = acc_one[width : width + 1, lanes]


def mlp_both(numbers, near, far, vectors, mixed, tokens, cotangent, out_turned, out_sums):
    rows, width = tokens.shape
    parts = near.shape[1] + far.shape[1]
    hidden_width = parts * width
    tile = pl.BlockSpec((MLP_TILE, width), lambda s, *_: (s, 0))
    whole = lambda *dims: pl.BlockSpec(dims, lambda s, *_: (0,) * len(dims))
    return pl.pallas_call(
        mlp_kernel,
        grid_spec=pltpu.PrefetchScalarGridSpec(
            num_scalar_prefetch=1,
            grid=(rows // MLP_TILE,),
            in_specs=[
                whole(*near.shape), whole(*far.shape), whole(*vectors.shape), tile, tile, tile,
                pl.BlockSpec((width, MLP_TILE), lambda s, *_: (0, s)), whole(*out_sums.shape),
            ],
            out_specs=[
                tile,
                tile,
                tile,
                pl.BlockSpec((8, MLP_TILE), lambda s, *_: (0, s)),
                whole(*near.shape),
                whole(*far.shape),
                whole(*vectors.shape),
            ],
            scratch_shapes=[
                pltpu.VMEM((width, hidden_width), LOW),
                pltpu.VMEM((width, hidden_width), LOW),
                pltpu.VMEM((parts, width, SUB), LOW),
                pltpu.VMEM((width, width), LOW),
                pltpu.VMEM((width + 16, hidden_width), F32),
                pltpu.VMEM((width, hidden_width), F32),
                pltpu.VMEM((width, width), F32),
                pltpu.VMEM((8, hidden_width), F32),
            ],
        ),
        out_shape=[
            jax.ShapeDtypeStruct((rows, width), LOW),
            jax.ShapeDtypeStruct((rows, width), F32),
            jax.ShapeDtypeStruct((rows, width), LOW),
            jax.ShapeDtypeStruct((8, rows), F32),
            jax.ShapeDtypeStruct(near.shape, LOW),
            jax.ShapeDtypeStruct(far.shape, LOW),
            jax.ShapeDtypeStruct(vectors.shape, F32),
        ],
        compiler_params=pltpu.CompilerParams(vmem_limit_bytes=VMEM_LIMIT),
        cost_estimate=pl.CostEstimate(
            flops=34_000_000_000, bytes_accessed=20_000_000, transcendentals=6_000_000
        ),
        name="mlp_both",
    )(numbers, near, far, vectors, mixed, tokens, cotangent, out_turned, out_sums)


def attend_back_kernel(
    numbers,
    query,
    key_turned,
    value,
    probs,
    inner,
    grad_mixed,
    normed_turned,
    weight,
    vectors,
    sums,
    grad_qkv,
    near,
    far,
    grad_query,
    acc_key,
    acc_value,
    acc_sums,
    normed_sums,
    blocks,
    rows,
):
    step = pl.program_id(0)
    chunks = pl.num_programs(0) - 1
    pairs = range(PAIRS)
    count = len(pairs)
    scale = (SUB // 2) ** (-0.5)

    @pl.when(step == 0)
    def clear():
        acc_key[...] = jnp.zeros(acc_key.shape, F32)
        acc_value[...] = jnp.zeros(acc_value.shape, F32)
        normed_sums[...] = jnp.zeros(normed_sums.shape, F32)
        acc_sums[...] = jnp.zeros(acc_sums.shape, F32)

    @pl.when(step < chunks)
    def attend():
        def place(number):
            sub, at = number // count, number % count
            start = pl.multiple_of((step * (TILE // SUB) + sub) * SUB, SUB)
            return sub, at, start, pl.ds(start, SPAN), pl.ds(at * SUB, SUB)

        def slope(number):
            sub, _, _, near_rows, heads = place(number)
            grad = both_heads(grad_mixed[pl.ds(sub * SUB, SUB), heads])
            return dot(value[near_rows, heads], grad, NT)

        def soften(number, slopes):
            sub, at, _, _, _ = place(number)
            pair = pairs[at]
            cols = pl.ds(sub * SUB, SUB)
            both = []
            for head in range(2):
                lanes = slice(head * SUB, (head + 1) * SUB)
                less = slopes[:, lanes] - inner[2 * pair + head : 2 * pair + head + 1, cols]
                both.append((probs[at, sub, :, lanes].astype(F32) * less).astype(LOW))
            return jnp.concatenate(both, axis=1)

        def collect(number, scores):
            sub, at, start, near_rows, heads = place(number)
            first, second = halves_of(dot(key_turned[heads, near_rows], scores))
            turned = (jnp.concatenate([first, second], axis=0) * scale).astype(LOW)
            grad_query[pl.ds(start, SUB), heads] = turned.T
            wanted = both_heads(query[pl.ds(start + MARGIN, SUB), heads])
            acc_key[near_rows, heads] += dot(scores, wanted)
            grad = both_heads(grad_mixed[pl.ds(sub * SUB, SUB), heads])
            acc_value[near_rows, heads] += dot(probs[at, sub], grad)

        staged(TILE // SUB * count, slope, soften, collect)

    @pl.when(step > 0)
    def collect():
        here = pl.ds(pl.multiple_of((step - 1) * TILE, SUB), TILE)
        there = pl.ds(pl.multiple_of((step - 1) * TILE + MARGIN, SUB), TILE)
        parts = (
            grad_query[here, :],
            acc_key[there, :].astype(LOW),
            acc_value[there, :].astype(LOW),
        )
        joined = jnp.concatenate(parts, axis=1)
        grad_qkv[...] = joined
        normed_sums[...] += dot(normed_turned[...], joined)
        acc_sums[0:1, :] += jnp.sum(joined.astype(F32), axis=0, keepdims=True)

    @pl.when(step == chunks)
    def finish():
        weight_grad(
            numbers, normed_sums[...], acc_sums[0:1, :], weight, vectors, sums, near, far, blocks, rows
        )


def weight_grad(numbers, total, columns, weight, vectors, sums, near, far, blocks, rows):
    width = weight.shape[0]
    parts, mid = blocks.shape[0], near.shape[0]
    block = 3 * width // parts
    rows_each = 12 // parts
    wide = weight[...].astype(F32)
    grad_gain = jnp.sum(total * wide, axis=1, keepdims=True)
    grad_shift = jnp.sum(wide * columns, axis=1, keepdims=True)
    rows[...] = jnp.zeros(rows.shape, F32)
    rows[0:VEC_LANES, :] = sums[...]
    rows[2:3, :] = columns[:, :width]
    rows[3:4, :] = columns[:, 2 * width :]
    rows[VEC_LANES : 2 * VEC_LANES, :] = vectors[...]
    turned = rows[...].T
    gain = turned[:, VEC_LANES : VEC_LANES + 1]
    shift = turned[:, VEC_LANES + 1 : VEC_LANES + 2]
    lane = lane_numbers(turned.shape)
    turned = jnp.where(lane == 0, grad_gain, jnp.where(lane == 1, grad_shift, turned))
    total = total * gain + shift * columns
    at = block - 2 * SUB
    for number in range(parts):
        away = (3 * width - block * number) % (3 * width)
        piece = (pltpu.roll(total, away, 1) if number else total)[:, :width]
        vec = pltpu.roll(turned, (at - rows_each * number) % SUB, 1)
        last = jnp.where(lane < at, piece[:, 2 * SUB :], 0.0)
        last = jnp.where((lane >= at) & (lane < at + rows_each), vec, last)
        at_place = numbers[PLACES + number]
        blocks[at_place, :, : 2 * SUB] = piece[:, : 2 * SUB].astype(LOW)
        blocks[at_place, :, 2 * SUB :] = last.astype(LOW)
    near[...] = blocks[:mid]
    far[...] = blocks[mid:]


def attend_backward(
    numbers, parts, query, key_turned, value, probs, inner, grad_mixed, normed_turned, weight,
    vectors, sums,
):
    width, rows = normed_turned.shape
    padded = query.shape[0]
    chunks = rows // TILE
    tiles = TILE // SUB
    now = lambda s: jnp.minimum(s, chunks - 1)
    before = lambda s: jnp.maximum(s - 1, 0)
    whole = lambda *dims: pl.BlockSpec(dims, lambda s, *_: (0,) * len(dims))
    half = (parts // 2, width, width)
    return pl.pallas_call(
        attend_back_kernel,
        grid_spec=pltpu.PrefetchScalarGridSpec(
            num_scalar_prefetch=1,
            grid=(chunks + 1,),
            in_specs=[
                whole(padded, width),
                whole(width, padded),
                whole(padded, width),
                pl.BlockSpec((PAIRS, tiles, SPAN, 2 * SUB), lambda s, *_: (0, now(s), 0, 0)),
                pl.BlockSpec((8, TILE), lambda s, *_: (0, now(s))),
                pl.BlockSpec((TILE, width), lambda s, *_: (now(s), 0)),
                pl.BlockSpec((width, TILE), lambda s, *_: (0, before(s))),
                whole(*weight.shape),
                whole(*vectors.shape),
                whole(*sums.shape),
            ],
            out_specs=[
                pl.BlockSpec((TILE, 3 * width), lambda s, *_: (before(s), 0)),
                whole(*half),
                whole(*half),
            ],
            scratch_shapes=[
                pltpu.VMEM((rows, width), LOW),
                pltpu.VMEM((padded, width), F32),
                pltpu.VMEM((padded, width), F32),
                pltpu.VMEM((8, 3 * width), F32),
                pltpu.VMEM((width, 3 * width), F32),
                pltpu.VMEM((parts, width, width), LOW),
                pltpu.VMEM((SUB, width), F32),
            ],
        ),
        out_shape=[
            jax.ShapeDtypeStruct((rows, 3 * width), LOW),
            jax.ShapeDtypeStruct(half, LOW),
            jax.ShapeDtypeStruct(half, LOW),
        ],
        compiler_params=pltpu.CompilerParams(vmem_limit_bytes=VMEM_LIMIT),
        cost_estimate=pl.CostEstimate(
            flops=16_000_000_000, bytes_accessed=24_000_000, transcendentals=0
        ),
        name="attend_backward",
    )(
        numbers, query, key_turned, value, probs, inner, grad_mixed, normed_turned, weight, vectors,
        sums,
    )


def input_grad_kernel(weight, vectors, tokens, grad_residual, grad_qkv, input_grad):
    normed, rate = norm_parts(tokens[...].astype(F32))
    grad_first = dot(grad_qkv[...], weight[...], NT)
    back = norm_back(grad_first, normed, rate, vectors[0:1, :])
    input_grad[...] = (grad_residual[...] + back).astype(LOW)


def input_gradient(weight, vectors, tokens, grad_residual, grad_qkv):
    rows, width = tokens.shape
    size = TILE
    tile = pl.BlockSpec((size, width), lambda s: (s, 0))
    whole = lambda ref: pl.BlockSpec(ref.shape, lambda s: (0, 0))
    return pl.pallas_call(
        input_grad_kernel,
        grid=(rows // size,),
        in_specs=[
            whole(weight), whole(vectors), tile, tile,
            pl.BlockSpec((size, 3 * width), lambda s: (s, 0)),
        ],
        out_specs=tile,
        out_shape=jax.ShapeDtypeStruct((rows, width), LOW),
        compiler_params=pltpu.CompilerParams(vmem_limit_bytes=VMEM_LIMIT),
        cost_estimate=pl.CostEstimate(
            flops=4_000_000_000, bytes_accessed=13_000_000, transcendentals=2048
        ),
        name="input_gradient",
    )(weight, vectors, tokens, grad_residual, grad_qkv)


def halves(value):
    high = value.astype(LOW)
    return high, (value - high.astype(F32)).astype(LOW)


def dot_three(left, right):
    tall = jnp.concatenate([right[0], right[0], right[1]], axis=0)
    return dot(jnp.concatenate([left[0], left[1], left[0]], axis=1), tall)


def newton_rows(blocks, offset, rows, store):
    gram = dot(blocks[0], blocks[0], NT)
    for part in blocks[1:]:
        gram = gram + dot(part, part, NT)
    depth = gram.shape[0]
    down = lax.broadcasted_iota(jnp.int32, (depth, depth), 0)
    eye = (down == lane_numbers((depth, depth))).astype(F32)
    norm = 1.0 / (jnp.sqrt(jnp.sum(gram * eye, keepdims=True)) + 1e-07)
    gram = gram * (norm * norm)
    place = lax.broadcasted_iota(jnp.int32, (rows, depth), 0) + offset
    left = jnp.where(place == lane_numbers((rows, depth)), norm, 0.0)
    store[0:depth, :] = gram
    store[depth:, :] = left

    @pl.loop(0, NS_STEPS - 1)
    def advance(_):
        both = halves(store[...])
        pair = [part[:depth] for part in both]
        down = lax.broadcasted_iota(jnp.int32, (depth, depth), 0)
        eye = (down == lane_numbers((depth, depth))).astype(F32)
        square = dot_three(pair, pair)
        poly = halves(NEWTON_A * eye + NEWTON_B * store[0:depth, :] + NEWTON_C * square)
        made = dot_three(both, poly)
        store[depth:, :] = made[depth:]
        store[0:depth, :] = dot_three(halves(made[:depth]), poly)

    left = store[depth:, :]
    pair = halves(store[0:depth, :])
    once = dot_three(halves(left), pair)
    return NEWTON_A * left + NEWTON_B * once + NEWTON_C * dot_three(halves(once), pair)


def newton_store(depth, rows):
    return pltpu.VMEM((depth + tall_of(rows), depth), F32)


def stepped(left, own, height, old):
    high, rest = halves(left)
    ortho = (dot(high, own) + dot(rest, own))[: old.shape[0], : old.shape[1]]
    return old * (1.0 - MUON_RATE * MUON_DECAY) - (MUON_RATE * 0.2 * math.sqrt(height)) * ortho


def kept_lanes(value, low, high):
    lane = lane_numbers(value.shape)
    return jnp.where((lane >= low) & (lane < high), value.astype(F32), 0.0).astype(LOW)


def tall_of(rows):
    return -(-rows // 16) * 16


def muon_kernel(height, numbers, *refs):
    old, new, copy, store = refs[-4:]
    count = old.shape[1]
    blocks = [kept_lanes(ref[...], 0, count) for ref in refs[:-4]]
    left = newton_rows(blocks, numbers[OFFSET], tall_of(old.shape[0]), store)
    result = stepped(left, blocks[0], height, old[...])
    new[...] = result
    copy[...] = result.astype(LOW)


def muon(height, numbers, blocks, old):
    vmem = pl.BlockSpec(memory_space=pltpu.VMEM)

    def kernel(*refs):
        muon_kernel(height, *refs)

    return pl.pallas_call(
        kernel,
        in_specs=[pl.BlockSpec(memory_space=pltpu.SMEM)] + [vmem] * (len(blocks) + 1),
        out_specs=[vmem, vmem],
        out_shape=[
            jax.ShapeDtypeStruct(old.shape, F32),
            jax.ShapeDtypeStruct(old.shape, LOW),
        ],
        scratch_shapes=[newton_store(blocks[0].shape[0], old.shape[0])],
        compiler_params=pltpu.CompilerParams(vmem_limit_bytes=VMEM_LIMIT),
        cost_estimate=pl.CostEstimate(
            flops=9_000_000_000, bytes_accessed=2_000_000, transcendentals=10
        ),
        name="muon",
    )(numbers, *blocks, old)


def pick_kernel(count, numbers, *refs):
    pieces, columns, outs = refs[:count], refs[count], refs[count + 1 :]
    share = pieces[0].shape[0]
    for k, piece in enumerate(pieces):
        columns[k * share : (k + 1) * share, :] = piece[...]
        for n, out in enumerate(outs):
            at = pl.multiple_of(numbers[STARTS + n] * SUB, SUB)
            out[k * share : (k + 1) * share, :] = piece[:, pl.ds(at, out.shape[1])]


def pick(numbers, pieces, count):
    depth = len(pieces) * pieces[0].shape[0]
    vmem = pl.BlockSpec(memory_space=pltpu.VMEM)

    def kernel(*refs):
        pick_kernel(len(pieces), *refs)

    return pl.pallas_call(
        kernel,
        in_specs=[pl.BlockSpec(memory_space=pltpu.SMEM)] + [vmem] * len(pieces),
        out_specs=[vmem] * (count + 1),
        out_shape=[jax.ShapeDtypeStruct((depth, pieces[0].shape[1]), LOW)]
        + [jax.ShapeDtypeStruct((depth, depth), LOW)] * count,
        name="pick",
    )(numbers, *pieces)


def newton_kernel(at, numbers, *refs):
    left, store = refs[-2:]
    bounds = numbers[LOW_LANE], numbers[HIGH_LANE]
    blocks = [kept_lanes(ref[...], *bounds) for ref in refs[:-2]]
    start = numbers[OFFSET] if at is None else at
    left[...] = newton_rows(blocks, start, left.shape[0], store)


def newton(at, numbers, blocks, rows):
    vmem = pl.BlockSpec(memory_space=pltpu.VMEM)

    def kernel(*refs):
        newton_kernel(at, *refs)

    return pl.pallas_call(
        kernel,
        in_specs=[pl.BlockSpec(memory_space=pltpu.SMEM)] + [vmem] * len(blocks),
        out_specs=vmem,
        out_shape=jax.ShapeDtypeStruct((tall_of(rows), blocks[0].shape[0]), F32),
        scratch_shapes=[newton_store(blocks[0].shape[0], rows)],
        compiler_params=pltpu.CompilerParams(vmem_limit_bytes=VMEM_LIMIT),
        cost_estimate=pl.CostEstimate(
            flops=9_000_000_000, bytes_accessed=2_000_000, transcendentals=10
        ),
        name="newton",
    )(numbers, *blocks)


def finish_kernel(heights, lanes, numbers, columns, *refs):
    count = len(heights)
    store = refs[-1]
    news = refs[-1 - 2 * count : -1]
    olds = refs[-1 - 3 * count : -1 - 2 * count]
    lefts = refs[: -1 - 3 * count]
    for n, left in enumerate(lefts):
        store[n] = left[...]
    for n in range(count):
        wide = -(-olds[n].shape[1] // SUB) * SUB
        own = columns[:, lanes[n] : lanes[n] + wide]
        result = stepped(store[numbers[WHICH + n]], own, heights[n], olds[n][...])
        news[2 * n][...] = result
        news[2 * n + 1][...] = result.astype(LOW)


def finish(heights, lanes, numbers, columns, lefts, olds):
    vmem = pl.BlockSpec(memory_space=pltpu.VMEM)
    count = len(olds)

    def kernel(*refs):
        finish_kernel(heights, lanes, *refs)

    outs = pl.pallas_call(
        kernel,
        in_specs=[pl.BlockSpec(memory_space=pltpu.SMEM)] + [vmem] * (1 + len(lefts) + count),
        out_specs=[vmem] * (2 * count),
        out_shape=[
            jax.ShapeDtypeStruct(old.shape, kind) for old in olds for kind in (F32, LOW)
        ],
        scratch_shapes=[pltpu.VMEM((len(lefts), *lefts[0].shape), F32)],
        compiler_params=pltpu.CompilerParams(vmem_limit_bytes=VMEM_LIMIT),
        cost_estimate=pl.CostEstimate(
            flops=200_000_000, bytes_accessed=2_000_000, transcendentals=0
        ),
        name="finish",
    )(numbers, columns, *lefts, *olds)
    return [(outs[2 * n], outs[2 * n + 1]) for n in range(count)]


def exchange(x, axis, mask):
    size = lax.axis_size(axis)
    return lax.ppermute(x, axis, [(i, i ^ mask) for i in range(size)])


def place_masks(size):
    masks = [0]
    bit = size // 2
    while bit >= 1:
        masks = masks + [m ^ bit for m in masks]
        bit //= 2
    return masks


def from_columns(own):
    size = lax.axis_size("dp")
    sent = jnp.broadcast_to(own[None], (size, *own.shape))
    return lax.all_to_all(sent, "dp", split_axis=0, concat_axis=0, tiled=True)


def over_columns(own):
    return from_columns(own).reshape(-1, own.shape[1])


def device_numbers(dp, ns, share, width, proj_rows):
    masks = place_masks(ns)
    tasks = [(0, 0, width), (width // SUB, 0, width)]
    tasks += [(width // SUB + 1, 2 * SUB, 2 * SUB + proj_rows)] * (ns - 2)
    table = np.zeros((dp * ns, 24), np.int32)
    for device in range(dp * ns):
        column, index = device // ns, device % ns
        row = table[device]
        for n in range(ns):
            row[OWNERS + n] = index ^ masks[n]
            row[PLACES + (index ^ masks[n])] = n
            row[STARTS + n] = tasks[index ^ n][0]
        for n in range(3):
            row[WHICH + n] = index ^ n
        row[OFFSET] = column * share
        row[COLUMN] = column
        row[LOW_LANE], row[HIGH_LANE] = tasks[index][1:]
    return table


def half_rows(own):
    held = [own]
    bit = lax.axis_size("ns") // 2
    while bit > 1:
        held = held + [exchange(block, "ns", bit) for block in held]
        bit //= 2
    return held


def added(keep, got):
    return (keep.astype(F32) + got.astype(F32)).astype(LOW)


def sum_columns(pieces):
    return summed(lax.all_to_all(pieces, "dp", split_axis=0, concat_axis=0, tiled=True))


def summed(pieces):
    return jnp.sum(pieces.astype(F32), axis=0)


def columns_direct(own):
    devices = lax.axis_size("dp")
    if devices > 8 or own.shape[0] % 16:
        return [over_columns(own)], None
    return [own] + [exchange(own, "dp", mask) for mask in range(1, devices)], 0


def widened(arrays, lanes):
    joined = jnp.concatenate(arrays, axis=1)
    return jnp.pad(joined, ((0, 0), (0, lanes - joined.shape[1])))


def per_device(
    tokens,
    cotangent,
    segment,
    valid_rows,
    qkv_weight,
    proj_weight,
    fc1_weight,
    fc2_weight,
    qkv_moment,
    proj_moment,
    fc1_moment,
    fc2_moment,
    vectors,
    vector_moment,
    vector_square,
):
    rows, width = tokens.shape
    ns = lax.axis_size("ns")
    qkv_w, proj_w, fc1_w, fc2_w = (w.T for w in (qkv_weight, proj_weight, fc1_weight, fc2_weight))
    qkv_m, proj_m, fc1_m, fc2_m = (w.T for w in (qkv_moment, proj_moment, fc1_moment, fc2_moment))
    share, count = qkv_w.shape
    vec_rows = vectors.shape[0]
    first_lanes = width
    later_lanes = 2 * width + SUB

    table = device_numbers(lax.axis_size("dp"), ns, share, width, proj_w.shape[1])
    device = lax.axis_index("dp") * ns + lax.axis_index("ns")
    numbers = lax.dynamic_slice(jnp.asarray(table), (device, 0), (1, table.shape[1]))[0]

    row_ids = jnp.where(
        valid_rows > 0, segment, rows + jnp.arange(rows, dtype=jnp.int32)
    ).astype(F32)
    ids = jnp.pad(row_ids, (MARGIN, MARGIN), constant_values=-1.0).reshape(-1, SUB)
    ids = jnp.pad(ids, ((0, -ids.shape[0] % 8), (0, 0)), constant_values=-1.0)

    later_own = widened([fc1_w, fc2_w, proj_w], later_lanes).astype(LOW)
    later_pair = jnp.stack([later_own, exchange(later_own, "ns", ns // 2)])
    first_own = widened([qkv_w, vectors.T], first_lanes).astype(LOW)
    prepared = prepare(tokens, cotangent, ids)
    first_pieces = half_rows(over_columns(first_own))
    first_pieces, prepared = lax.optimization_barrier((first_pieces, prepared))
    normed, normed_turned, out_turned, columns, out_sums = prepared
    first_pieces = first_pieces + [exchange(piece, "ns", 1) for piece in first_pieces]
    later_near = from_columns(later_pair)
    if share % 16:
        later_near = jnp.moveaxis(later_near, 0, 1).reshape(1, ns // 2, width, later_lanes)

    query, _, value, key_turned, mixed, probs, weight, vector_full = attend_forward(
        numbers, first_pieces, normed, ids, columns
    )
    later_near, mixed = lax.optimization_barrier((later_near, mixed))
    later_far = exchange(later_near, "ns", 1)
    output, grad_residual, grad_mixed, inner, grads_near, grads_far, sums = mlp_both(
        numbers, later_near, later_far, vector_full, mixed, tokens, cotangent, out_turned, out_sums
    )
    held = added(grads_near, exchange(grads_far, "ns", 1))
    held, grad_mixed = lax.optimization_barrier((held, grad_mixed))
    if share % 16:
        held = jnp.moveaxis(held.reshape(ns // 2, -1, share, later_lanes), 1, 0)
    later_got = lax.all_to_all(held, "dp", split_axis=0, concat_axis=0, tiled=True)

    grad_qkv, grads_near, grads_far = attend_backward(
        numbers, ns, query, key_turned, value, probs, inner, grad_mixed, normed_turned, weight,
        vector_full, sums,
    )
    held = added(grads_near, exchange(grads_far, "ns", 1))
    got = exchange(held[1], "ns", ns // 2)
    input_grad = input_gradient(weight, vector_full, tokens, grad_residual, grad_qkv)
    got, input_grad, later_got = lax.optimization_barrier((got, input_grad, later_got))
    first_held = added(held[0], got).reshape(lax.axis_size("dp"), share, first_lanes)
    first_got = lax.all_to_all(first_held, "dp", split_axis=0, concat_axis=0, tiled=True)
    later_sums = summed(later_got)
    later_owned = later_sums[0] + exchange(later_sums[1].astype(LOW), "ns", ns // 2).astype(F32)
    later_moment = later_owned + 0.5 * widened([fc1_m, fc2_m, proj_m], later_lanes)
    pieces, at = columns_direct(later_moment.astype(LOW))
    first_got, pieces = lax.optimization_barrier((first_got, pieces))
    columns, *chosen = pick(numbers, pieces, ns)
    blocks = [chosen[0]] + [exchange(chosen[mask], "ns", mask) for mask in range(1, ns)]

    first_owned = summed(first_got)
    first_moment = first_owned + 0.5 * widened([qkv_m], first_lanes)
    first_pieces = half_rows(over_columns(first_moment.astype(LOW)))
    left = newton(at, numbers, blocks, share)
    left, first_pieces = lax.optimization_barrier((left, first_pieces))
    first_pieces = first_pieces + [exchange(piece, "ns", 1) for piece in first_pieces]
    qkv_new = muon(count * ns, numbers, first_pieces, qkv_w)
    lefts = [left] + [exchange(left, "ns", mask) for mask in range(1, ns)]
    lefts, qkv_new = lax.optimization_barrier((lefts, qkv_new))
    fc1_new, fc2_new, proj_new = finish(
        [w.shape[1] * ns for w in (fc1_w, fc2_w, proj_w)],
        (0, width, 2 * width),
        numbers,
        columns,
        lefts,
        (fc1_w, fc2_w, proj_w),
    )

    news = (qkv_new, proj_new, fc1_new, fc2_new)
    moments_new = (
        first_moment[:, :count],
        later_moment[:, 2 * width : 2 * width + proj_w.shape[1]],
        later_moment[:, :width],
        later_moment[:, width : 2 * width],
    )

    vector_grad = first_owned[:, count : count + vec_rows].T
    first_new = BETA_ONE * vector_moment + (1.0 - BETA_ONE) * vector_grad
    second_new = BETA_TWO * vector_square + (1.0 - BETA_TWO) * vector_grad * vector_grad
    first_hat = first_new / (1.0 - BETA_ONE**STEP)
    second_hat = second_new / (1.0 - BETA_TWO**STEP)
    vectors_new = vectors - ADAM_RATE * first_hat / (jnp.sqrt(second_hat) + ADAM_EPS)
    return (
        output,
        input_grad,
        *(new[0].T for new in news),
        *(m.T for m in moments_new),
        first_new,
        second_new,
        vectors_new,
        *(new[1].T for new in news),
    )


def solution(mesh):
    rows = P(("dp", "ns"), None)
    flat = P(("dp", "ns"))
    block = P("ns", "dp")
    return jax.shard_map(
        per_device,
        mesh=mesh,
        in_specs=(rows, rows, flat, flat) + (block,) * 11,
        out_specs=(rows, rows) + (block,) * 15,
        check_vma=False,
    )
```

```python
import functools
import math

import jax
import jax.numpy as jnp
import numpy as np
from jax import lax
from jax.experimental import pallas as pl
from jax.experimental.pallas import tpu as pltpu
from jax.sharding import PartitionSpec as P

HEADS = 6
PAIRS = 3
MARGIN = 128
NS_STEPS = 5
STEP = 10
TILE = 512
MLP_TILE = 512
FF_CHUNK = 256
SUB = 128
SPAN = 384
VEC_LANES = 16
GROUP = 2


EPS_NORM = 1e-06
NEWTON_A = 3.4445
NEWTON_B = -4.775
NEWTON_C = 2.0315
MUON_RATE = 0.2
MUON_DECAY = 0.1
ADAM_RATE = 0.4
BETA_ONE = 0.9
BETA_TWO = 0.999
ADAM_EPS = 1e-08
LOW = jnp.bfloat16
F32 = jnp.float32
TN = (((0,), (0,)), ((), ()))
NT = (((1,), (1,)), ((), ()))
NN = (((1,), (0,)), ((), ()))
VMEM_LIMIT = 56 * 1024 * 1024
ERF_P = 0.3275911
ERF_COEFS = (0.254829592, -0.284496736, 1.421413741, -1.453152027, 1.061405429)


def dot(left, right, dims=NN):
    return lax.dot_general(left, right, dims, preferred_element_type=F32)


PLACES, OWNERS, STARTS, WHICH, OFFSET, LOW_LANE, HIGH_LANE, COLUMN = 0, 4, 8, 12, 16, 17, 18, 19


def lane_numbers(shape):
    return lax.broadcasted_iota(jnp.int32, shape, len(shape) - 1)


def norm_parts(value):
    center = value - jnp.mean(value, axis=-1, keepdims=True)
    rate = lax.rsqrt(jnp.mean(center * center, axis=-1, keepdims=True) + EPS_NORM)
    return center * rate, rate


def norm_back(grad, normed, rate, gain):
    scaled = grad * gain
    first = jnp.mean(scaled, axis=-1, keepdims=True)
    second = jnp.mean(scaled * normed, axis=-1, keepdims=True)
    return rate * (scaled - first - normed * second)


def gelu_both(value):
    below = 1.0 + (ERF_P * 0.5**0.5) * jnp.abs(value)
    ratio = pl.reciprocal(below, approx=True)
    ratio = ratio * (2.0 - below * ratio)
    decay = jnp.exp2((value * value) * (-0.5 * math.log2(math.e)))
    poly = 0.5 * ERF_COEFS[4]
    for coef in ERF_COEFS[3::-1]:
        poly = poly * ratio + 0.5 * coef
    tail = poly * ratio * decay
    phi = jnp.where(value >= 0, 1.0 - tail, tail)
    return value * phi, phi + (value * (1.0 / math.sqrt(2.0 * math.pi))) * decay


def gelu_rows(hidden, bias, grad, between):
    active, back = [], []
    rows = hidden.shape[0]
    pieces = rows // 16
    for n in range(pieces):
        if n * len(between) // pieces != (n - 1) * len(between) // pieces:
            between[n * len(between) // pieces]()
        here = slice(n * 16, (n + 1) * 16)
        value, slope = gelu_both(hidden[here] + bias)
        active.append(value.astype(LOW))
        back.append((grad[here] * slope).astype(LOW))
    return jnp.concatenate(active, axis=0), jnp.concatenate(back, axis=0)


def halves_of(lanes):
    half = lanes.shape[0] // 2
    return lanes[:half, :SUB], lanes[half:, SUB:]


def staged(count, first, second, third):
    made = first(0)
    kept = None
    for n in range(count):
        coming = first(n + 1) if n + 1 < count else None
        if kept is not None:
            third(n - 1, kept)
        kept = second(n, made)
        made = coming
    third(count - 1, kept)


def both_heads(pair):
    first = (lane_numbers((1, SUB)) < SUB // 2).astype(F32).astype(pair.dtype)
    second = (lane_numbers((1, SUB)) >= SUB // 2).astype(F32).astype(pair.dtype)
    return jnp.concatenate([pair * first, pair * second], axis=0)


def fetch(pairs, sems):
    copies = [
        pltpu.make_async_copy(source, target, sems.at[n])
        for n, (source, target) in enumerate(pairs)
    ]
    for copy in copies:
        copy.start()
    for copy in copies:
        copy.wait()


def prepare_kernel(tokens, cotangent, ids, normed, normed_turned, out_turned, columns, sums):
    step = pl.program_id(0)
    parts = columns.shape[0] // SUB

    @pl.when(step == 0)
    def clear():
        sums[...] = jnp.zeros(sums.shape, F32)
        for number in range(parts):
            row = jnp.broadcast_to(ids[number : number + 1, :], (SUB, SUB))
            columns[number * SUB : (number + 1) * SUB, :] = row.T

    value, _ = norm_parts(tokens[...].astype(F32))
    normed[...] = value
    normed_turned[...] = value.astype(LOW).T
    out_low = cotangent[...]
    out_turned[...] = out_low.T
    sums[0:1, :] += jnp.sum(out_low.astype(F32), axis=0, keepdims=True)


def prepare(tokens, cotangent, ids):
    rows, width = tokens.shape
    padded = rows + 2 * MARGIN
    tile = pl.BlockSpec((TILE, width), lambda s: (s, 0))
    turned = pl.BlockSpec((width, TILE), lambda s: (0, s))
    whole = lambda *dims: pl.BlockSpec(dims, lambda s: (0,) * len(dims))
    return pl.pallas_call(
        prepare_kernel,
        grid=(rows // TILE,),
        in_specs=[tile, tile, whole(*ids.shape)],
        out_specs=[tile, turned, turned, whole(padded, SUB), whole(8, width)],
        out_shape=[
            jax.ShapeDtypeStruct((rows, width), F32),
            jax.ShapeDtypeStruct((width, rows), LOW),
            jax.ShapeDtypeStruct((width, rows), LOW),
            jax.ShapeDtypeStruct((padded, SUB), F32),
            jax.ShapeDtypeStruct((8, width), F32),
        ],
        compiler_params=pltpu.CompilerParams(vmem_limit_bytes=VMEM_LIMIT),
        cost_estimate=pl.CostEstimate(
            flops=20_000_000, bytes_accessed=12_000_000, transcendentals=2048
        ),
        name="prepare",
    )(tokens, cotangent, ids)


def attend_kernel(numbers, *refs):
    (normed, ids, columns, query, key, value, key_turned, mixed, probs, weight, vectors,
     gathered, pair_weight, value_turned, shifts, sems) = refs[-16:]
    pieces = refs[:-16]
    step = pl.program_id(0)
    chunks = pl.num_programs(0) - 1
    width = normed.shape[1]
    parts = len(pieces)
    block = 3 * width // parts
    rows_each = 12 // parts

    @pl.when(step == 0)
    def assemble():
        fetch([(piece, gathered.at[n]) for n, piece in enumerate(pieces)], sems)
        tiles = [jnp.zeros((width, SUB), F32)] * (3 * width // SUB + 1)
        turned = jnp.zeros((width, SUB), F32)
        for number in range(parts):
            piece = gathered[numbers[PLACES + number]].astype(F32)
            kept = jnp.where(lane_numbers(piece.shape) < block, piece, 0.0)
            wide = jnp.concatenate([kept, jnp.zeros((width, SUB), F32)], axis=1)
            over = block * number % SUB
            wide = pltpu.roll(wide, over, 1) if over else wide
            for n in range(wide.shape[1] // SUB):
                at = block * number // SUB + n
                if at < len(tiles):
                    tiles[at] = tiles[at] + wide[:, n * SUB : (n + 1) * SUB]
            last = piece[:, 2 * SUB :]
            at = block - 2 * SUB
            lane = lane_numbers(last.shape)
            vec = jnp.where((lane >= at) & (lane < at + rows_each), last, 0.0)
            turned = turned + pltpu.roll(vec, (rows_each * number - at) % SUB, 1)
        total = jnp.concatenate(tiles[:-1], axis=1).astype(LOW)
        weight[...] = total
        pair_weight[...] = total[:, width:].T
        vectors[...] = turned.T[:VEC_LANES]
        shifts[...] = turned
        edges = (pl.ds(0, MARGIN), pl.ds(MARGIN + chunks * TILE, MARGIN))
        for edge in edges:
            for ref in (query, key, value):
                ref[edge, :] = jnp.zeros((MARGIN, width), LOW)
            for ref in (key_turned, value_turned):
                ref[:, edge] = jnp.zeros((width, MARGIN), LOW)

    @pl.when(step < chunks)
    def project():
        first_in = (normed[...] * vectors[0:1, :] + vectors[1:2, :]).astype(LOW)
        result = dot(first_in, weight[...])
        turned = dot(pair_weight[...], first_in, NT)
        here = pl.ds(pl.multiple_of(MARGIN + step * TILE, SUB), TILE)
        scale = (width // HEADS) ** (-0.5)
        made = (result[:, :width] + vectors[2:3, :]).astype(LOW) * jnp.asarray(scale, LOW)
        query[here, :] = made
        key[here, :] = result[:, width : 2 * width].astype(LOW)
        value[here, :] = (result[:, 2 * width :] + vectors[3:4, :]).astype(LOW)
        key_turned[:, here] = turned[:width].astype(LOW)
        value_turned[:, here] = (turned[width:] + shifts[:, 3:4]).astype(LOW)

    @pl.when(step > 0)
    def attend():
        def place(number):
            sub, pair = number // PAIRS, number % PAIRS
            tile = (step - 1) * (TILE // SUB) + sub
            start = pl.multiple_of(tile * SUB, SUB)
            return sub, pair, tile, start, pl.ds(start, SPAN), pl.ds(pair * SUB, SUB)

        def of_group(group):
            return range(group * GROUP, (group + 1) * GROUP)

        def score(group):
            made = []
            for number in of_group(group):
                _, _, _, start, near_rows, heads = place(number)
                wanted = both_heads(query[pl.ds(start + MARGIN, SUB), heads])
                made.append(dot(key[near_rows, heads], wanted, NT))
            return made

        def soften(group, made):
            own = []
            for number, scores in zip(of_group(group), made):
                _, _, tile, _, near_rows, _ = place(number)
                same = columns[near_rows, :] == ids[pl.ds(tile + 1, 1), :]
                own += [
                    jnp.where(same, scores[:, head * SUB : (head + 1) * SUB], -1e30)
                    for head in range(2)
                ]
            largest = [jnp.max(part, axis=0, keepdims=True) for part in own]
            expo = [jnp.exp(part - most) for part, most in zip(own, largest)]
            share = [1.0 / jnp.sum(part, axis=0, keepdims=True) for part in expo]
            scaled = [(part * by).astype(LOW) for part, by in zip(expo, share)]
            result = []
            for n, number in enumerate(of_group(group)):
                sub, pair, _, _, _, _ = place(number)
                result.append(jnp.concatenate(scaled[2 * n : 2 * n + 2], axis=1))
                probs[pair, sub] = result[-1]
            return result

        def mix(group, kept):
            for number, prob in zip(of_group(group), kept):
                sub, _, _, _, near_rows, heads = place(number)
                first, second = halves_of(dot(value_turned[heads, near_rows], prob))
                turned = jnp.concatenate([first, second], axis=0).astype(LOW)
                mixed[pl.ds(sub * SUB, SUB), heads] = turned.T

        staged(TILE // SUB * PAIRS // GROUP, score, soften, mix)


def attend_forward(numbers, pieces, normed, ids, columns):
    rows, width = normed.shape
    chunks = rows // TILE
    tiles = TILE // SUB
    parts = len(pieces)
    now = lambda s: jnp.minimum(s, chunks - 1)
    before = lambda s: jnp.maximum(s - 1, 0)
    whole = lambda *dims: pl.BlockSpec(dims, lambda s, *_: (0,) * len(dims))
    padded = rows + 2 * MARGIN
    return pl.pallas_call(
        attend_kernel,
        grid_spec=pltpu.PrefetchScalarGridSpec(
            num_scalar_prefetch=1,
            grid=(chunks + 1,),
            in_specs=[pl.BlockSpec(memory_space=pl.ANY)] * parts
            + [
                pl.BlockSpec((TILE, width), lambda s, *_: (now(s), 0)),
                whole(*ids.shape),
                whole(*columns.shape),
            ],
            out_specs=[
                whole(padded, width),
                whole(padded, width),
                whole(padded, width),
                whole(width, padded),
                pl.BlockSpec((TILE, width), lambda s, *_: (before(s), 0)),
                pl.BlockSpec((PAIRS, tiles, SPAN, 2 * SUB), lambda s, *_: (0, before(s), 0, 0)),
                whole(width, 3 * width),
                whole(VEC_LANES, width),
            ],
            scratch_shapes=[
                pltpu.VMEM((parts, *pieces[0].shape), LOW),
                pltpu.VMEM((2 * width, width), LOW),
                pltpu.VMEM((width, padded), LOW),
                pltpu.VMEM((width, SUB), F32),
                pltpu.SemaphoreType.DMA((parts,)),
            ],
        ),
        out_shape=[
            jax.ShapeDtypeStruct((padded, width), LOW),
            jax.ShapeDtypeStruct((padded, width), LOW),
            jax.ShapeDtypeStruct((padded, width), LOW),
            jax.ShapeDtypeStruct((width, padded), LOW),
            jax.ShapeDtypeStruct((rows, width), LOW),
            jax.ShapeDtypeStruct((PAIRS, rows // SUB, SPAN, 2 * SUB), LOW),
            jax.ShapeDtypeStruct((width, 3 * width), LOW),
            jax.ShapeDtypeStruct((VEC_LANES, width), F32),
        ],
        compiler_params=pltpu.CompilerParams(vmem_limit_bytes=VMEM_LIMIT),
        cost_estimate=pl.CostEstimate(
            flops=12_000_000_000, bytes_accessed=22_000_000, transcendentals=5_000_000
        ),
        name="attend_forward",
    )(numbers, *pieces, normed, ids, columns)


def mlp_kernel(numbers, near, far, *refs):
    (vectors, mixed, tokens, cotangent, out_turned, out_sums, output, grad_residual, grad_mixed, inner, grads_near,
     grads_far, sums, one, two, proj_parts, proj, acc_one, acc_two, acc_proj, bias
    ) = refs
    step = pl.program_id(0)
    width = tokens.shape[1]
    mid = near.shape[1]
    parts = mid + far.shape[1]
    block = width // parts
    last_at = 2 * width
    hidden_width = one.shape[1]

    @pl.when(step == 0)
    def assemble():
        for part in range(parts):
            ref, at = (near, part) if part < mid else (far, part - mid)
            lanes = pl.ds(part * width, width)
            for group in range(near.shape[0]):
                here = pl.ds(group * near.shape[2], near.shape[2])
                one[here, lanes] = ref[group, at, :, :width]
                two[here, lanes] = ref[group, at, :, width:last_at]
                proj_parts[part, here, :] = ref[group, at, :, last_at:]
        total = jnp.zeros((width, width), F32)
        for number in range(parts):
            piece = proj_parts[numbers[PLACES + number]].astype(F32)
            kept = jnp.where(lane_numbers(piece.shape) < block, piece, 0.0)
            wide = jnp.concatenate([kept, jnp.zeros((width, width - SUB), F32)], axis=1)
            total = total + (pltpu.roll(wide, block * number, 1) if number else wide)
        proj[...] = total.astype(LOW)
        for part in range(parts):
            row = vectors[pl.ds(8 + numbers[OWNERS + part], 1), :]
            bias[0:1, part * width : (part + 1) * width] = row
        acc_one[...] = jnp.zeros(acc_one.shape, F32)
        acc_two[...] = jnp.zeros(acc_two.shape, F32)
        acc_proj[...] = jnp.zeros(acc_proj.shape, F32)
        sums[...] = jnp.zeros(sums.shape, F32)
        sums[7:8, :] = out_sums[0:1, :]

    def add_row(row, values):
        sums[pl.ds(row, 1), :] += jnp.sum(values, axis=0, keepdims=True)

    own = mixed[...]
    residual = tokens[...].astype(F32) + dot(own, proj[...], NT) + vectors[4:5, :]
    normed, rate = norm_parts(residual)
    gain = vectors[5:6, :]
    second_in = (normed * gain + vectors[6:7, :]).astype(LOW)
    out_low = cotangent[...]
    grad_out = out_low.astype(F32)
    second_turned = second_in.T
    out_turned = out_turned[...]
    totals = [residual + vectors[7:8, :], jnp.zeros(residual.shape, F32)]

    count = hidden_width // FF_CHUNK
    ones = jnp.ones((16, MLP_TILE), LOW)
    second_and_ones = jnp.concatenate([second_turned, ones], axis=0)
    hiddens, slopes, kept = {}, {}, {}

    def lanes_of(number):
        return pl.ds(number * FF_CHUNK, FF_CHUNK)

    def make_hidden(number):
        hiddens[number] = dot(second_in, one[:, lanes_of(number)])

    def make_slope(number):
        slopes[number] = dot(out_low, two[:, lanes_of(number)])

    def add_one(number):
        acc_one[:, lanes_of(number)] += dot(second_and_ones, kept[number][1])

    def add_two(number):
        acc_two[:, lanes_of(number)] += dot(out_turned, kept[number][0])

    def add_result(number):
        totals[0] = totals[0] + dot(kept[number][0], two[:, lanes_of(number)], NT)

    def add_second(number):
        totals[1] = totals[1] + dot(kept[number][1], one[:, lanes_of(number)], NT)

    make_hidden(0)
    make_slope(0)
    for number in range(count):
        between = []
        if number + 1 < count:
            between += [functools.partial(f, number + 1) for f in (make_hidden, make_slope)]
        if number > 0:
            between += [
                functools.partial(f, number - 1)
                for f in (add_result, add_second, add_one, add_two)
            ]
        kept[number] = gelu_rows(
            hiddens.pop(number), bias[0:1, lanes_of(number)], slopes.pop(number), between
        )
    for f in (add_result, add_second, add_one, add_two):
        f(count - 1)
    result, grad_second = totals
    output[...] = result.astype(LOW)
    add_row(5, grad_second * normed)
    add_row(6, grad_second)
    grad_res = grad_out + norm_back(grad_second, normed, rate, gain)
    grad_residual[...] = grad_res
    branch = grad_res.astype(LOW)
    add_row(4, branch.astype(F32))
    acc_proj[...] += dot(branch.T, own)
    grad_own = dot(branch, proj[...]).astype(LOW)
    grad_mixed[...] = grad_own
    high, rest = halves(grad_own.astype(F32) * own.astype(F32))
    head = lax.broadcasted_iota(jnp.int32, (16, width), 0)
    chosen = (lane_numbers((16, width)) // (width // HEADS) == head).astype(F32).astype(LOW)
    inner[...] = (dot(chosen, high, NT) + dot(chosen, rest, NT))[:8]

    @pl.when(step == pl.num_programs(0) - 1)
    def finish():
        total = acc_proj[...]
        for number in range(parts):
            turned = pltpu.roll(total, (width - block * number) % width, 1) if number else total
            proj_parts[numbers[PLACES + number]] = turned[:, :SUB].astype(LOW)
        for part in range(parts):
            ref, at = (grads_near, part) if part < mid else (grads_far, part - mid)
            lanes = pl.ds(part * width, width)
            for group in range(ref.shape[0]):
                here = pl.ds(group * ref.shape[2], ref.shape[2])
                ref[group, at, :, :width] = acc_one[here, lanes].astype(LOW)
                ref[group, at, :, width:last_at] = acc_two[here, lanes].astype(LOW)
                ref[group, at, :, last_at:] = proj_parts[part, here, :]
            sums[pl.ds(8 + numbers[OWNERS + part], 1), :] = acc_one[width : width + 1, lanes]


def mlp_both(numbers, near, far, vectors, mixed, tokens, cotangent, out_turned, out_sums):
    rows, width = tokens.shape
    parts = near.shape[1] + far.shape[1]
    hidden_width = parts * width
    tile = pl.BlockSpec((MLP_TILE, width), lambda s, *_: (s, 0))
    whole = lambda *dims: pl.BlockSpec(dims, lambda s, *_: (0,) * len(dims))
    return pl.pallas_call(
        mlp_kernel,
        grid_spec=pltpu.PrefetchScalarGridSpec(
            num_scalar_prefetch=1,
            grid=(rows // MLP_TILE,),
            in_specs=[
                whole(*near.shape), whole(*far.shape), whole(*vectors.shape), tile, tile, tile,
                pl.BlockSpec((width, MLP_TILE), lambda s, *_: (0, s)), whole(*out_sums.shape),
            ],
            out_specs=[
                tile,
                tile,
                tile,
                pl.BlockSpec((8, MLP_TILE), lambda s, *_: (0, s)),
                whole(*near.shape),
                whole(*far.shape),
                whole(*vectors.shape),
            ],
            scratch_shapes=[
                pltpu.VMEM((width, hidden_width), LOW),
                pltpu.VMEM((width, hidden_width), LOW),
                pltpu.VMEM((parts, width, SUB), LOW),
                pltpu.VMEM((width, width), LOW),
                pltpu.VMEM((width + 16, hidden_width), F32),
                pltpu.VMEM((width, hidden_width), F32),
                pltpu.VMEM((width, width), F32),
                pltpu.VMEM((8, hidden_width), F32),
            ],
        ),
        out_shape=[
            jax.ShapeDtypeStruct((rows, width), LOW),
            jax.ShapeDtypeStruct((rows, width), F32),
            jax.ShapeDtypeStruct((rows, width), LOW),
            jax.ShapeDtypeStruct((8, rows), F32),
            jax.ShapeDtypeStruct(near.shape, LOW),
            jax.ShapeDtypeStruct(far.shape, LOW),
            jax.ShapeDtypeStruct(vectors.shape, F32),
        ],
        compiler_params=pltpu.CompilerParams(vmem_limit_bytes=VMEM_LIMIT),
        cost_estimate=pl.CostEstimate(
            flops=34_000_000_000, bytes_accessed=20_000_000, transcendentals=6_000_000
        ),
        name="mlp_both",
    )(numbers, near, far, vectors, mixed, tokens, cotangent, out_turned, out_sums)


def attend_back_kernel(
    numbers,
    query,
    key_turned,
    value,
    probs,
    inner,
    grad_mixed,
    normed_turned,
    weight,
    vectors,
    sums,
    grad_qkv,
    near,
    far,
    grad_query,
    acc_key,
    acc_value,
    acc_sums,
    normed_sums,
    blocks,
    rows,
):
    step = pl.program_id(0)
    chunks = pl.num_programs(0) - 1
    pairs = range(PAIRS)
    count = len(pairs)
    scale = (SUB // 2) ** (-0.5)

    @pl.when(step == 0)
    def clear():
        acc_key[...] = jnp.zeros(acc_key.shape, F32)
        acc_value[...] = jnp.zeros(acc_value.shape, F32)
        normed_sums[...] = jnp.zeros(normed_sums.shape, F32)
        acc_sums[...] = jnp.zeros(acc_sums.shape, F32)

    @pl.when(step < chunks)
    def attend():
        def place(number):
            sub, at = number // count, number % count
            start = pl.multiple_of((step * (TILE // SUB) + sub) * SUB, SUB)
            return sub, at, start, pl.ds(start, SPAN), pl.ds(at * SUB, SUB)

        def slope(number):
            sub, _, _, near_rows, heads = place(number)
            grad = both_heads(grad_mixed[pl.ds(sub * SUB, SUB), heads])
            return dot(value[near_rows, heads], grad, NT)

        def soften(number, slopes):
            sub, at, _, _, _ = place(number)
            pair = pairs[at]
            cols = pl.ds(sub * SUB, SUB)
            both = []
            for head in range(2):
                lanes = slice(head * SUB, (head + 1) * SUB)
                less = slopes[:, lanes] - inner[2 * pair + head : 2 * pair + head + 1, cols]
                both.append((probs[at, sub, :, lanes].astype(F32) * less).astype(LOW))
            return jnp.concatenate(both, axis=1)

        def collect(number, scores):
            sub, at, start, near_rows, heads = place(number)
            first, second = halves_of(dot(key_turned[heads, near_rows], scores))
            turned = (jnp.concatenate([first, second], axis=0) * scale).astype(LOW)
            grad_query[pl.ds(start, SUB), heads] = turned.T
            wanted = both_heads(query[pl.ds(start + MARGIN, SUB), heads])
            acc_key[near_rows, heads] += dot(scores, wanted)
            grad = both_heads(grad_mixed[pl.ds(sub * SUB, SUB), heads])
            acc_value[near_rows, heads] += dot(probs[at, sub], grad)

        staged(TILE // SUB * count, slope, soften, collect)

    @pl.when(step > 0)
    def collect():
        here = pl.ds(pl.multiple_of((step - 1) * TILE, SUB), TILE)
        there = pl.ds(pl.multiple_of((step - 1) * TILE + MARGIN, SUB), TILE)
        parts = (
            grad_query[here, :],
            acc_key[there, :].astype(LOW),
            acc_value[there, :].astype(LOW),
        )
        joined = jnp.concatenate(parts, axis=1)
        grad_qkv[...] = joined
        normed_sums[...] += dot(normed_turned[...], joined)
        acc_sums[0:1, :] += jnp.sum(joined.astype(F32), axis=0, keepdims=True)

    @pl.when(step == chunks)
    def finish():
        weight_grad(
            numbers, normed_sums[...], acc_sums[0:1, :], weight, vectors, sums, near, far, blocks, rows
        )


def weight_grad(numbers, total, columns, weight, vectors, sums, near, far, blocks, rows):
    width = weight.shape[0]
    parts, mid = blocks.shape[0], near.shape[0]
    block = 3 * width // parts
    rows_each = 12 // parts
    wide = weight[...].astype(F32)
    grad_gain = jnp.sum(total * wide, axis=1, keepdims=True)
    grad_shift = jnp.sum(wide * columns, axis=1, keepdims=True)
    rows[...] = jnp.zeros(rows.shape, F32)
    rows[0:VEC_LANES, :] = sums[...]
    rows[2:3, :] = columns[:, :width]
    rows[3:4, :] = columns[:, 2 * width :]
    rows[VEC_LANES : 2 * VEC_LANES, :] = vectors[...]
    turned = rows[...].T
    gain = turned[:, VEC_LANES : VEC_LANES + 1]
    shift = turned[:, VEC_LANES + 1 : VEC_LANES + 2]
    lane = lane_numbers(turned.shape)
    turned = jnp.where(lane == 0, grad_gain, jnp.where(lane == 1, grad_shift, turned))
    total = total * gain + shift * columns
    at = block - 2 * SUB
    for number in range(parts):
        first, over = block * number // SUB * SUB, block * number % SUB
        piece = total[:, first : first + width + SUB]
        if over:
            missing = width + SUB - piece.shape[1]
            if missing:
                piece = jnp.concatenate([piece, jnp.zeros((width, missing), F32)], axis=1)
            piece = pltpu.roll(piece, width + SUB - over, 1)
        piece = piece[:, :width]
        vec = pltpu.roll(turned, (at - rows_each * number) % SUB, 1)
        last = jnp.where(lane < at, piece[:, 2 * SUB :], 0.0)
        last = jnp.where((lane >= at) & (lane < at + rows_each), vec, last)
        at_place = numbers[PLACES + number]
        blocks[at_place, :, : 2 * SUB] = piece[:, : 2 * SUB].astype(LOW)
        blocks[at_place, :, 2 * SUB :] = last.astype(LOW)
    near[...] = blocks[:mid]
    far[...] = blocks[mid:]


def attend_backward(
    numbers, parts, query, key_turned, value, probs, inner, grad_mixed, normed_turned, weight,
    vectors, sums,
):
    width, rows = normed_turned.shape
    padded = query.shape[0]
    chunks = rows // TILE
    tiles = TILE // SUB
    now = lambda s: jnp.minimum(s, chunks - 1)
    before = lambda s: jnp.maximum(s - 1, 0)
    whole = lambda *dims: pl.BlockSpec(dims, lambda s, *_: (0,) * len(dims))
    half = (parts // 2, width, width)
    return pl.pallas_call(
        attend_back_kernel,
        grid_spec=pltpu.PrefetchScalarGridSpec(
            num_scalar_prefetch=1,
            grid=(chunks + 1,),
            in_specs=[
                whole(padded, width),
                whole(width, padded),
                whole(padded, width),
                pl.BlockSpec((PAIRS, tiles, SPAN, 2 * SUB), lambda s, *_: (0, now(s), 0, 0)),
                pl.BlockSpec((8, TILE), lambda s, *_: (0, now(s))),
                pl.BlockSpec((TILE, width), lambda s, *_: (now(s), 0)),
                pl.BlockSpec((width, TILE), lambda s, *_: (0, before(s))),
                whole(*weight.shape),
                whole(*vectors.shape),
                whole(*sums.shape),
            ],
            out_specs=[
                pl.BlockSpec((TILE, 3 * width), lambda s, *_: (before(s), 0)),
                whole(*half),
                whole(*half),
            ],
            scratch_shapes=[
                pltpu.VMEM((rows, width), LOW),
                pltpu.VMEM((padded, width), F32),
                pltpu.VMEM((padded, width), F32),
                pltpu.VMEM((8, 3 * width), F32),
                pltpu.VMEM((width, 3 * width), F32),
                pltpu.VMEM((parts, width, width), LOW),
                pltpu.VMEM((SUB, width), F32),
            ],
        ),
        out_shape=[
            jax.ShapeDtypeStruct((rows, 3 * width), LOW),
            jax.ShapeDtypeStruct(half, LOW),
            jax.ShapeDtypeStruct(half, LOW),
        ],
        compiler_params=pltpu.CompilerParams(vmem_limit_bytes=VMEM_LIMIT),
        cost_estimate=pl.CostEstimate(
            flops=16_000_000_000, bytes_accessed=24_000_000, transcendentals=0
        ),
        name="attend_backward",
    )(
        numbers, query, key_turned, value, probs, inner, grad_mixed, normed_turned, weight, vectors,
        sums,
    )


def input_grad_kernel(weight, vectors, tokens, grad_residual, grad_qkv, input_grad):
    normed, rate = norm_parts(tokens[...].astype(F32))
    grad_first = dot(grad_qkv[...], weight[...], NT)
    back = norm_back(grad_first, normed, rate, vectors[0:1, :])
    input_grad[...] = (grad_residual[...] + back).astype(LOW)


def input_gradient(weight, vectors, tokens, grad_residual, grad_qkv):
    rows, width = tokens.shape
    size = TILE
    tile = pl.BlockSpec((size, width), lambda s: (s, 0))
    whole = lambda ref: pl.BlockSpec(ref.shape, lambda s: (0, 0))
    return pl.pallas_call(
        input_grad_kernel,
        grid=(rows // size,),
        in_specs=[
            whole(weight), whole(vectors), tile, tile,
            pl.BlockSpec((size, 3 * width), lambda s: (s, 0)),
        ],
        out_specs=tile,
        out_shape=jax.ShapeDtypeStruct((rows, width), LOW),
        compiler_params=pltpu.CompilerParams(vmem_limit_bytes=VMEM_LIMIT),
        cost_estimate=pl.CostEstimate(
            flops=4_000_000_000, bytes_accessed=13_000_000, transcendentals=2048
        ),
        name="input_gradient",
    )(weight, vectors, tokens, grad_residual, grad_qkv)


def halves(value):
    high = value.astype(LOW)
    return high, (value - high.astype(F32)).astype(LOW)


def dot_three(left, right):
    tall = jnp.concatenate([right[0], right[0], right[1]], axis=0)
    return dot(jnp.concatenate([left[0], left[1], left[0]], axis=1), tall)


def newton_rows(blocks, offset, rows, store):
    gram = dot(blocks[0], blocks[0], NT)
    for part in blocks[1:]:
        gram = gram + dot(part, part, NT)
    depth = gram.shape[0]
    down = lax.broadcasted_iota(jnp.int32, (depth, depth), 0)
    eye = (down == lane_numbers((depth, depth))).astype(F32)
    norm = 1.0 / (jnp.sqrt(jnp.sum(gram * eye, keepdims=True)) + 1e-07)
    gram = gram * (norm * norm)
    place = lax.broadcasted_iota(jnp.int32, (rows, depth), 0) + offset
    left = jnp.where(place == lane_numbers((rows, depth)), norm, 0.0)
    store[0:depth, :] = gram
    store[depth:, :] = left

    @pl.loop(0, NS_STEPS - 1)
    def advance(_):
        both = halves(store[...])
        pair = [part[:depth] for part in both]
        down = lax.broadcasted_iota(jnp.int32, (depth, depth), 0)
        eye = (down == lane_numbers((depth, depth))).astype(F32)
        square = dot_three(pair, pair)
        poly = halves(NEWTON_A * eye + NEWTON_B * store[0:depth, :] + NEWTON_C * square)
        made = dot_three(both, poly)
        store[depth:, :] = made[depth:]
        store[0:depth, :] = dot_three(halves(made[:depth]), poly)

    left = store[depth:, :]
    pair = halves(store[0:depth, :])
    once = dot_three(halves(left), pair)
    return NEWTON_A * left + NEWTON_B * once + NEWTON_C * dot_three(halves(once), pair)


def newton_store(depth, rows):
    return pltpu.VMEM((depth + tall_of(rows), depth), F32)


def stepped(left, own, height, old):
    high, rest = halves(left)
    ortho = (dot(high, own) + dot(rest, own))[: old.shape[0], : old.shape[1]]
    return old * (1.0 - MUON_RATE * MUON_DECAY) - (MUON_RATE * 0.2 * math.sqrt(height)) * ortho


def kept_lanes(value, low, high):
    lane = lane_numbers(value.shape)
    return jnp.where((lane >= low) & (lane < high), value.astype(F32), 0.0).astype(LOW)


def tall_of(rows):
    return -(-rows // 16) * 16


def muon_kernel(height, numbers, *refs):
    old, new, copy, store = refs[-4:]
    count = old.shape[1]
    blocks = [kept_lanes(ref[...], 0, count) for ref in refs[:-4]]
    left = newton_rows(blocks, numbers[OFFSET], tall_of(old.shape[0]), store)
    result = stepped(left, blocks[0], height, old[...])
    new[...] = result
    copy[...] = result.astype(LOW)


def muon(height, numbers, blocks, old):
    vmem = pl.BlockSpec(memory_space=pltpu.VMEM)

    def kernel(*refs):
        muon_kernel(height, *refs)

    return pl.pallas_call(
        kernel,
        in_specs=[pl.BlockSpec(memory_space=pltpu.SMEM)] + [vmem] * (len(blocks) + 1),
        out_specs=[vmem, vmem],
        out_shape=[
            jax.ShapeDtypeStruct(old.shape, F32),
            jax.ShapeDtypeStruct(old.shape, LOW),
        ],
        scratch_shapes=[newton_store(blocks[0].shape[0], old.shape[0])],
        compiler_params=pltpu.CompilerParams(vmem_limit_bytes=VMEM_LIMIT),
        cost_estimate=pl.CostEstimate(
            flops=9_000_000_000, bytes_accessed=2_000_000, transcendentals=10
        ),
        name="muon",
    )(numbers, *blocks, old)


def pick_kernel(count, numbers, *refs):
    pieces, columns, outs = refs[:count], refs[count], refs[count + 1 :]
    share = pieces[0].shape[0]
    for k, piece in enumerate(pieces):
        columns[k * share : (k + 1) * share, :] = piece[...]
        for n, out in enumerate(outs):
            at = pl.multiple_of(numbers[STARTS + n] * SUB, SUB)
            out[k * share : (k + 1) * share, :] = piece[:, pl.ds(at, out.shape[1])]


def pick(numbers, pieces, count):
    depth = len(pieces) * pieces[0].shape[0]
    vmem = pl.BlockSpec(memory_space=pltpu.VMEM)

    def kernel(*refs):
        pick_kernel(len(pieces), *refs)

    return pl.pallas_call(
        kernel,
        in_specs=[pl.BlockSpec(memory_space=pltpu.SMEM)] + [vmem] * len(pieces),
        out_specs=[vmem] * (count + 1),
        out_shape=[jax.ShapeDtypeStruct((depth, pieces[0].shape[1]), LOW)]
        + [jax.ShapeDtypeStruct((depth, depth), LOW)] * count,
        name="pick",
    )(numbers, *pieces)


def newton_kernel(at, numbers, *refs):
    left, store = refs[-2:]
    bounds = numbers[LOW_LANE], numbers[HIGH_LANE]
    blocks = [kept_lanes(ref[...], *bounds) for ref in refs[:-2]]
    start = numbers[OFFSET] if at is None else at
    left[...] = newton_rows(blocks, start, left.shape[0], store)


def newton(at, numbers, blocks, rows):
    vmem = pl.BlockSpec(memory_space=pltpu.VMEM)

    def kernel(*refs):
        newton_kernel(at, *refs)

    return pl.pallas_call(
        kernel,
        in_specs=[pl.BlockSpec(memory_space=pltpu.SMEM)] + [vmem] * len(blocks),
        out_specs=vmem,
        out_shape=jax.ShapeDtypeStruct((tall_of(rows), blocks[0].shape[0]), F32),
        scratch_shapes=[newton_store(blocks[0].shape[0], rows)],
        compiler_params=pltpu.CompilerParams(vmem_limit_bytes=VMEM_LIMIT),
        cost_estimate=pl.CostEstimate(
            flops=9_000_000_000, bytes_accessed=2_000_000, transcendentals=10
        ),
        name="newton",
    )(numbers, *blocks)


def finish_kernel(heights, lanes, numbers, columns, *refs):
    count = len(heights)
    store = refs[-1]
    news = refs[-1 - 2 * count : -1]
    olds = refs[-1 - 3 * count : -1 - 2 * count]
    lefts = refs[: -1 - 3 * count]
    for n, left in enumerate(lefts):
        store[n] = left[...]
    for n in range(count):
        wide = -(-olds[n].shape[1] // SUB) * SUB
        own = columns[:, lanes[n] : lanes[n] + wide]
        result = stepped(store[numbers[WHICH + n]], own, heights[n], olds[n][...])
        news[2 * n][...] = result
        news[2 * n + 1][...] = result.astype(LOW)


def finish(heights, lanes, numbers, columns, lefts, olds):
    vmem = pl.BlockSpec(memory_space=pltpu.VMEM)
    count = len(olds)

    def kernel(*refs):
        finish_kernel(heights, lanes, *refs)

    outs = pl.pallas_call(
        kernel,
        in_specs=[pl.BlockSpec(memory_space=pltpu.SMEM)] + [vmem] * (1 + len(lefts) + count),
        out_specs=[vmem] * (2 * count),
        out_shape=[
            jax.ShapeDtypeStruct(old.shape, kind) for old in olds for kind in (F32, LOW)
        ],
        scratch_shapes=[pltpu.VMEM((len(lefts), *lefts[0].shape), F32)],
        compiler_params=pltpu.CompilerParams(vmem_limit_bytes=VMEM_LIMIT),
        cost_estimate=pl.CostEstimate(
            flops=200_000_000, bytes_accessed=2_000_000, transcendentals=0
        ),
        name="finish",
    )(numbers, columns, *lefts, *olds)
    return [(outs[2 * n], outs[2 * n + 1]) for n in range(count)]


def exchange(x, axis, mask):
    size = lax.axis_size(axis)
    return lax.ppermute(x, axis, [(i, i ^ mask) for i in range(size)])


def place_masks(size):
    masks = [0]
    bit = size // 2
    while bit >= 1:
        masks = masks + [m ^ bit for m in masks]
        bit //= 2
    return masks


def from_columns(own):
    size = lax.axis_size("dp")
    sent = jnp.broadcast_to(own[None], (size, *own.shape))
    return lax.all_to_all(sent, "dp", split_axis=0, concat_axis=0, tiled=True)


def over_columns(own):
    return from_columns(own).reshape(-1, own.shape[1])


def device_numbers(dp, ns, share, width, proj_rows):
    masks = place_masks(ns)
    tasks = [(0, 0, width), (width // SUB, 0, width)]
    tasks += [(width // SUB + 1, 2 * SUB, 2 * SUB + proj_rows)] * (ns - 2)
    table = np.zeros((dp * ns, 24), np.int32)
    for device in range(dp * ns):
        column, index = device // ns, device % ns
        row = table[device]
        for n in range(ns):
            row[OWNERS + n] = index ^ masks[n]
            row[PLACES + (index ^ masks[n])] = n
            row[STARTS + n] = tasks[index ^ n][0]
        for n in range(3):
            row[WHICH + n] = index ^ n
        row[OFFSET] = column * share
        row[COLUMN] = column
        row[LOW_LANE], row[HIGH_LANE] = tasks[index][1:]
    return table


def half_rows(own):
    held = [own]
    bit = lax.axis_size("ns") // 2
    while bit > 1:
        held = held + [exchange(block, "ns", bit) for block in held]
        bit //= 2
    return held


def added(keep, got):
    return (keep.astype(F32) + got.astype(F32)).astype(LOW)


def sum_columns(pieces):
    return summed(lax.all_to_all(pieces, "dp", split_axis=0, concat_axis=0, tiled=True))


def summed(pieces):
    return jnp.sum(pieces.astype(F32), axis=0)


def columns_direct(own):
    devices = lax.axis_size("dp")
    if devices > 8 or own.shape[0] % 16:
        return [over_columns(own)], None
    return [own] + [exchange(own, "dp", mask) for mask in range(1, devices)], 0


def widened(arrays, lanes):
    joined = jnp.concatenate(arrays, axis=1)
    return jnp.pad(joined, ((0, 0), (0, lanes - joined.shape[1])))


def per_device(
    tokens,
    cotangent,
    segment,
    valid_rows,
    qkv_weight,
    proj_weight,
    fc1_weight,
    fc2_weight,
    qkv_moment,
    proj_moment,
    fc1_moment,
    fc2_moment,
    vectors,
    vector_moment,
    vector_square,
):
    rows, width = tokens.shape
    ns = lax.axis_size("ns")
    qkv_w, proj_w, fc1_w, fc2_w = (w.T for w in (qkv_weight, proj_weight, fc1_weight, fc2_weight))
    qkv_m, proj_m, fc1_m, fc2_m = (w.T for w in (qkv_moment, proj_moment, fc1_moment, fc2_moment))
    share, count = qkv_w.shape
    vec_rows = vectors.shape[0]
    first_lanes = width
    later_lanes = 2 * width + SUB

    table = device_numbers(lax.axis_size("dp"), ns, share, width, proj_w.shape[1])
    device = lax.axis_index("dp") * ns + lax.axis_index("ns")
    numbers = lax.dynamic_slice(jnp.asarray(table), (device, 0), (1, table.shape[1]))[0]

    row_ids = jnp.where(
        valid_rows > 0, segment, rows + jnp.arange(rows, dtype=jnp.int32)
    ).astype(F32)
    ids = jnp.pad(row_ids, (MARGIN, MARGIN), constant_values=-1.0).reshape(-1, SUB)
    ids = jnp.pad(ids, ((0, -ids.shape[0] % 8), (0, 0)), constant_values=-1.0)

    later_own = widened([fc1_w, fc2_w, proj_w], later_lanes).astype(LOW)
    later_pair = jnp.stack([later_own, exchange(later_own, "ns", ns // 2)])
    first_own = widened([qkv_w, vectors.T], first_lanes).astype(LOW)
    prepared = prepare(tokens, cotangent, ids)
    first_pieces = half_rows(over_columns(first_own))
    first_pieces, prepared, numbers = lax.optimization_barrier((first_pieces, prepared, numbers))
    normed, normed_turned, out_turned, columns, out_sums = prepared
    first_pieces = first_pieces + [exchange(piece, "ns", 1) for piece in first_pieces]
    later_near = from_columns(later_pair)
    if share % 16:
        later_near = jnp.moveaxis(later_near, 0, 1).reshape(1, ns // 2, width, later_lanes)

    query, _, value, key_turned, mixed, probs, weight, vector_full = attend_forward(
        numbers, first_pieces, normed, ids, columns
    )
    later_near, mixed = lax.optimization_barrier((later_near, mixed))
    later_far = exchange(later_near, "ns", 1)
    output, grad_residual, grad_mixed, inner, grads_near, grads_far, sums = mlp_both(
        numbers, later_near, later_far, vector_full, mixed, tokens, cotangent, out_turned, out_sums
    )
    held = added(grads_near, exchange(grads_far, "ns", 1))
    held, grad_mixed = lax.optimization_barrier((held, grad_mixed))
    if share % 16:
        held = jnp.moveaxis(held.reshape(ns // 2, -1, share, later_lanes), 1, 0)
    later_got = lax.all_to_all(held, "dp", split_axis=0, concat_axis=0, tiled=True)

    grad_qkv, grads_near, grads_far = attend_backward(
        numbers, ns, query, key_turned, value, probs, inner, grad_mixed, normed_turned, weight,
        vector_full, sums,
    )
    held = added(grads_near, exchange(grads_far, "ns", 1))
    got = exchange(held[1], "ns", ns // 2)
    input_grad = input_gradient(weight, vector_full, tokens, grad_residual, grad_qkv)
    got, input_grad, later_got = lax.optimization_barrier((got, input_grad, later_got))
    first_held = added(held[0], got).reshape(lax.axis_size("dp"), share, first_lanes)
    first_got = lax.all_to_all(first_held, "dp", split_axis=0, concat_axis=0, tiled=True)
    later_sums = summed(later_got)
    later_owned = later_sums[0] + exchange(later_sums[1].astype(LOW), "ns", ns // 2).astype(F32)
    later_moment = later_owned + 0.5 * widened([fc1_m, fc2_m, proj_m], later_lanes)
    pieces, at = columns_direct(later_moment.astype(LOW))
    first_got, pieces = lax.optimization_barrier((first_got, pieces))
    columns, *chosen = pick(numbers, pieces, ns)
    blocks = [chosen[0]] + [exchange(chosen[mask], "ns", mask) for mask in range(1, ns)]

    first_owned = summed(first_got)
    first_moment = first_owned + 0.5 * widened([qkv_m], first_lanes)
    first_pieces = half_rows(over_columns(first_moment.astype(LOW)))
    moments_new = (
        first_moment[:, :count],
        later_moment[:, 2 * width : 2 * width + proj_w.shape[1]],
        later_moment[:, :width],
        later_moment[:, width : 2 * width],
    )

    vector_grad = first_owned[:, count : count + vec_rows].T
    first_new = BETA_ONE * vector_moment + (1.0 - BETA_ONE) * vector_grad
    second_new = BETA_TWO * vector_square + (1.0 - BETA_TWO) * vector_grad * vector_grad
    first_hat = first_new / (1.0 - BETA_ONE**STEP)
    second_hat = second_new / (1.0 - BETA_TWO**STEP)
    vectors_new = vectors - ADAM_RATE * first_hat / (jnp.sqrt(second_hat) + ADAM_EPS)
    small = (*(m.T for m in moments_new), first_new, second_new, vectors_new)
    blocks, small = lax.optimization_barrier((blocks, small))
    left = newton(at, numbers, blocks, share)
    left, first_pieces = lax.optimization_barrier((left, first_pieces))
    first_pieces = first_pieces + [exchange(piece, "ns", 1) for piece in first_pieces]
    qkv_new = muon(count * ns, numbers, first_pieces, qkv_w)
    lefts = [left] + [exchange(left, "ns", mask) for mask in range(1, ns)]
    lefts, qkv_new = lax.optimization_barrier((lefts, qkv_new))
    fc1_new, fc2_new, proj_new = finish(
        [w.shape[1] * ns for w in (fc1_w, fc2_w, proj_w)],
        (0, width, 2 * width),
        numbers,
        columns,
        lefts,
        (fc1_w, fc2_w, proj_w),
    )

    news = (qkv_new, proj_new, fc1_new, fc2_new)
    return (
        output,
        input_grad,
        *(new[0].T for new in news),
        *small,
        *(new[1].T for new in news),
    )


def solution(mesh):
    rows = P(("dp", "ns"), None)
    flat = P(("dp", "ns"))
    block = P("ns", "dp")
    return jax.shard_map(
        per_device,
        mesh=mesh,
        in_specs=(rows, rows, flat, flat) + (block,) * 11,
        out_specs=(rows, rows) + (block,) * 15,
        check_vma=False,
    )
```

```python
import functools
import math

import jax
import jax.numpy as jnp
import numpy as np
from jax import lax
from jax.experimental import pallas as pl
from jax.experimental.pallas import tpu as pltpu
from jax.sharding import PartitionSpec as P

HEADS = 6
PAIRS = 3
MARGIN = 128
NS_STEPS = 5
STEP = 10
TILE = 512
MLP_TILE = 512
FF_CHUNK = 256
SUB = 128
SPAN = 384
VEC_LANES = 16
GROUP = 2


EPS_NORM = 1e-06
NEWTON_A = 3.4445
NEWTON_B = -4.775
NEWTON_C = 2.0315
MUON_RATE = 0.2
MUON_DECAY = 0.1
ADAM_RATE = 0.4
BETA_ONE = 0.9
BETA_TWO = 0.999
ADAM_EPS = 1e-08
LOW = jnp.bfloat16
F32 = jnp.float32
TN = (((0,), (0,)), ((), ()))
NT = (((1,), (1,)), ((), ()))
NN = (((1,), (0,)), ((), ()))
VMEM_LIMIT = 56 * 1024 * 1024
ERF_P = 0.3275911
ERF_COEFS = (0.254829592, -0.284496736, 1.421413741, -1.453152027, 1.061405429)


def dot(left, right, dims=NN):
    return lax.dot_general(left, right, dims, preferred_element_type=F32)


PLACES, OWNERS, STARTS, WHICH, OFFSET, LOW_LANE, HIGH_LANE, COLUMN = 0, 4, 8, 12, 16, 17, 18, 19


def lane_numbers(shape):
    return lax.broadcasted_iota(jnp.int32, shape, len(shape) - 1)


def norm_parts(value):
    center = value - jnp.mean(value, axis=-1, keepdims=True)
    rate = lax.rsqrt(jnp.mean(center * center, axis=-1, keepdims=True) + EPS_NORM)
    return center * rate, rate


def norm_back(grad, normed, rate, gain):
    scaled = grad * gain
    first = jnp.mean(scaled, axis=-1, keepdims=True)
    second = jnp.mean(scaled * normed, axis=-1, keepdims=True)
    return rate * (scaled - first - normed * second)


def gelu_both(value):
    below = 1.0 + (ERF_P * 0.5**0.5) * jnp.abs(value)
    ratio = pl.reciprocal(below, approx=True)
    ratio = ratio * (2.0 - below * ratio)
    decay = jnp.exp2((value * value) * (-0.5 * math.log2(math.e)))
    poly = 0.5 * ERF_COEFS[4]
    for coef in ERF_COEFS[3::-1]:
        poly = poly * ratio + 0.5 * coef
    tail = poly * ratio * decay
    phi = jnp.where(value >= 0, 1.0 - tail, tail)
    return value * phi, phi + (value * (1.0 / math.sqrt(2.0 * math.pi))) * decay


def gelu_rows(hidden, bias, grad, between):
    active, back = [], []
    rows = hidden.shape[0]
    pieces = rows // 16
    for n in range(pieces):
        if n * len(between) // pieces != (n - 1) * len(between) // pieces:
            between[n * len(between) // pieces]()
        here = slice(n * 16, (n + 1) * 16)
        value, slope = gelu_both(hidden[here] + bias)
        active.append(value.astype(LOW))
        back.append((grad[here] * slope).astype(LOW))
    return jnp.concatenate(active, axis=0), jnp.concatenate(back, axis=0)


def halves_of(lanes):
    half = lanes.shape[0] // 2
    return lanes[:half, :SUB], lanes[half:, SUB:]


def staged(count, first, second, third):
    made = first(0)
    kept = None
    for n in range(count):
        coming = first(n + 1) if n + 1 < count else None
        if kept is not None:
            third(n - 1, kept)
        kept = second(n, made)
        made = coming
    third(count - 1, kept)


def both_heads(pair):
    first = (lane_numbers((1, SUB)) < SUB // 2).astype(F32).astype(pair.dtype)
    second = (lane_numbers((1, SUB)) >= SUB // 2).astype(F32).astype(pair.dtype)
    return jnp.concatenate([pair * first, pair * second], axis=0)


def fetch(pairs, sems):
    copies = [
        pltpu.make_async_copy(source, target, sems.at[n])
        for n, (source, target) in enumerate(pairs)
    ]
    for copy in copies:
        copy.start()
    for copy in copies:
        copy.wait()


def prepare_kernel(tokens, cotangent, ids, normed, normed_turned, out_turned, columns, sums):
    step = pl.program_id(0)
    parts = columns.shape[0] // SUB

    @pl.when(step == 0)
    def clear():
        sums[...] = jnp.zeros(sums.shape, F32)
        for number in range(parts):
            row = jnp.broadcast_to(ids[number : number + 1, :], (SUB, SUB))
            columns[number * SUB : (number + 1) * SUB, :] = row.T

    value, _ = norm_parts(tokens[...].astype(F32))
    normed[...] = value
    normed_turned[...] = value.astype(LOW).T
    out_low = cotangent[...]
    out_turned[...] = out_low.T
    sums[0:1, :] += jnp.sum(out_low.astype(F32), axis=0, keepdims=True)


def prepare(tokens, cotangent, ids):
    rows, width = tokens.shape
    padded = rows + 2 * MARGIN
    tile = pl.BlockSpec((TILE, width), lambda s: (s, 0))
    turned = pl.BlockSpec((width, TILE), lambda s: (0, s))
    whole = lambda *dims: pl.BlockSpec(dims, lambda s: (0,) * len(dims))
    return pl.pallas_call(
        prepare_kernel,
        grid=(rows // TILE,),
        in_specs=[tile, tile, whole(*ids.shape)],
        out_specs=[tile, turned, turned, whole(padded, SUB), whole(8, width)],
        out_shape=[
            jax.ShapeDtypeStruct((rows, width), F32),
            jax.ShapeDtypeStruct((width, rows), LOW),
            jax.ShapeDtypeStruct((width, rows), LOW),
            jax.ShapeDtypeStruct((padded, SUB), F32),
            jax.ShapeDtypeStruct((8, width), F32),
        ],
        compiler_params=pltpu.CompilerParams(vmem_limit_bytes=VMEM_LIMIT),
        cost_estimate=pl.CostEstimate(
            flops=20_000_000, bytes_accessed=12_000_000, transcendentals=2048
        ),
        name="prepare",
    )(tokens, cotangent, ids)


def attend_kernel(numbers, *refs):
    (normed, ids, columns, query, key, value, key_turned, mixed, probs, weight, vectors,
     gathered, pair_weight, value_turned, shifts, sems) = refs[-16:]
    pieces = refs[:-16]
    step = pl.program_id(0)
    chunks = pl.num_programs(0) - 1
    width = normed.shape[1]
    parts = len(pieces)
    block = 3 * width // parts
    rows_each = 12 // parts

    @pl.when(step == 0)
    def assemble():
        fetch([(piece, gathered.at[n]) for n, piece in enumerate(pieces)], sems)
        tiles = [jnp.zeros((width, SUB), F32)] * (3 * width // SUB + 1)
        turned = jnp.zeros((width, SUB), F32)
        for number in range(parts):
            piece = gathered[numbers[PLACES + number]].astype(F32)
            kept = jnp.where(lane_numbers(piece.shape) < block, piece, 0.0)
            wide = jnp.concatenate([kept, jnp.zeros((width, SUB), F32)], axis=1)
            over = block * number % SUB
            wide = pltpu.roll(wide, over, 1) if over else wide
            for n in range(wide.shape[1] // SUB):
                at = block * number // SUB + n
                if at < len(tiles):
                    tiles[at] = tiles[at] + wide[:, n * SUB : (n + 1) * SUB]
            last = piece[:, 2 * SUB :]
            at = block - 2 * SUB
            lane = lane_numbers(last.shape)
            vec = jnp.where((lane >= at) & (lane < at + rows_each), last, 0.0)
            turned = turned + pltpu.roll(vec, (rows_each * number - at) % SUB, 1)
        total = jnp.concatenate(tiles[:-1], axis=1).astype(LOW)
        weight[...] = total
        pair_weight[...] = total[:, width:].T
        vectors[...] = turned.T[:VEC_LANES]
        shifts[...] = turned
        edges = (pl.ds(0, MARGIN), pl.ds(MARGIN + chunks * TILE, MARGIN))
        for edge in edges:
            for ref in (query, key, value):
                ref[edge, :] = jnp.zeros((MARGIN, width), LOW)
            for ref in (key_turned, value_turned):
                ref[:, edge] = jnp.zeros((width, MARGIN), LOW)

    @pl.when(step < chunks)
    def project():
        first_in = (normed[...] * vectors[0:1, :] + vectors[1:2, :]).astype(LOW)
        result = dot(first_in, weight[...])
        turned = dot(pair_weight[...], first_in, NT)
        here = pl.ds(pl.multiple_of(MARGIN + step * TILE, SUB), TILE)
        scale = (width // HEADS) ** (-0.5)
        made = (result[:, :width] + vectors[2:3, :]).astype(LOW) * jnp.asarray(scale, LOW)
        query[here, :] = made
        key[here, :] = result[:, width : 2 * width].astype(LOW)
        value[here, :] = (result[:, 2 * width :] + vectors[3:4, :]).astype(LOW)
        key_turned[:, here] = turned[:width].astype(LOW)
        value_turned[:, here] = (turned[width:] + shifts[:, 3:4]).astype(LOW)

    @pl.when(step > 0)
    def attend():
        def place(number):
            sub, pair = number // PAIRS, number % PAIRS
            tile = (step - 1) * (TILE // SUB) + sub
            start = pl.multiple_of(tile * SUB, SUB)
            return sub, pair, tile, start, pl.ds(start, SPAN), pl.ds(pair * SUB, SUB)

        def of_group(group):
            return range(group * GROUP, (group + 1) * GROUP)

        def score(group):
            made = []
            for number in of_group(group):
                _, _, _, start, near_rows, heads = place(number)
                wanted = both_heads(query[pl.ds(start + MARGIN, SUB), heads])
                made.append(dot(key[near_rows, heads], wanted, NT))
            return made

        def soften(group, made):
            own = []
            for number, scores in zip(of_group(group), made):
                _, _, tile, _, near_rows, _ = place(number)
                same = columns[near_rows, :] == ids[pl.ds(tile + 1, 1), :]
                own += [
                    jnp.where(same, scores[:, head * SUB : (head + 1) * SUB], -1e30)
                    for head in range(2)
                ]
            largest = [jnp.max(part, axis=0, keepdims=True) for part in own]
            expo = [jnp.exp(part - most) for part, most in zip(own, largest)]
            share = [1.0 / jnp.sum(part, axis=0, keepdims=True) for part in expo]
            scaled = [(part * by).astype(LOW) for part, by in zip(expo, share)]
            result = []
            for n, number in enumerate(of_group(group)):
                sub, pair, _, _, _, _ = place(number)
                result.append(jnp.concatenate(scaled[2 * n : 2 * n + 2], axis=1))
                probs[pair, sub] = result[-1]
            return result

        def mix(group, kept):
            for number, prob in zip(of_group(group), kept):
                sub, _, _, _, near_rows, heads = place(number)
                first, second = halves_of(dot(value_turned[heads, near_rows], prob))
                turned = jnp.concatenate([first, second], axis=0).astype(LOW)
                mixed[pl.ds(sub * SUB, SUB), heads] = turned.T

        staged(TILE // SUB * PAIRS // GROUP, score, soften, mix)


def attend_forward(numbers, pieces, normed, ids, columns):
    rows, width = normed.shape
    chunks = rows // TILE
    tiles = TILE // SUB
    parts = len(pieces)
    now = lambda s: jnp.minimum(s, chunks - 1)
    before = lambda s: jnp.maximum(s - 1, 0)
    whole = lambda *dims: pl.BlockSpec(dims, lambda s, *_: (0,) * len(dims))
    padded = rows + 2 * MARGIN
    return pl.pallas_call(
        attend_kernel,
        grid_spec=pltpu.PrefetchScalarGridSpec(
            num_scalar_prefetch=1,
            grid=(chunks + 1,),
            in_specs=[pl.BlockSpec(memory_space=pl.ANY)] * parts
            + [
                pl.BlockSpec((TILE, width), lambda s, *_: (now(s), 0)),
                whole(*ids.shape),
                whole(*columns.shape),
            ],
            out_specs=[
                whole(padded, width),
                whole(padded, width),
                whole(padded, width),
                whole(width, padded),
                pl.BlockSpec((TILE, width), lambda s, *_: (before(s), 0)),
                pl.BlockSpec((PAIRS, tiles, SPAN, 2 * SUB), lambda s, *_: (0, before(s), 0, 0)),
                whole(width, 3 * width),
                whole(VEC_LANES, width),
            ],
            scratch_shapes=[
                pltpu.VMEM((parts, *pieces[0].shape), LOW),
                pltpu.VMEM((2 * width, width), LOW),
                pltpu.VMEM((width, padded), LOW),
                pltpu.VMEM((width, SUB), F32),
                pltpu.SemaphoreType.DMA((parts,)),
            ],
        ),
        out_shape=[
            jax.ShapeDtypeStruct((padded, width), LOW),
            jax.ShapeDtypeStruct((padded, width), LOW),
            jax.ShapeDtypeStruct((padded, width), LOW),
            jax.ShapeDtypeStruct((width, padded), LOW),
            jax.ShapeDtypeStruct((rows, width), LOW),
            jax.ShapeDtypeStruct((PAIRS, rows // SUB, SPAN, 2 * SUB), LOW),
            jax.ShapeDtypeStruct((width, 3 * width), LOW),
            jax.ShapeDtypeStruct((VEC_LANES, width), F32),
        ],
        compiler_params=pltpu.CompilerParams(vmem_limit_bytes=VMEM_LIMIT),
        cost_estimate=pl.CostEstimate(
            flops=12_000_000_000, bytes_accessed=22_000_000, transcendentals=5_000_000
        ),
        name="attend_forward",
    )(numbers, *pieces, normed, ids, columns)


def mlp_kernel(numbers, near, far, *refs):
    (vectors, mixed, tokens, cotangent, out_turned, out_sums, output, grad_residual, grad_mixed, inner, grads_near,
     grads_far, sums, one, two, proj_parts, proj, acc_one, acc_two, acc_proj, bias
    ) = refs
    step = pl.program_id(0)
    width = tokens.shape[1]
    mid = near.shape[1]
    parts = mid + far.shape[1]
    block = width // parts
    last_at = 2 * width
    hidden_width = one.shape[1]

    @pl.when(step == 0)
    def assemble():
        for part in range(parts):
            ref, at = (near, part) if part < mid else (far, part - mid)
            lanes = pl.ds(part * width, width)
            for group in range(near.shape[0]):
                here = pl.ds(group * near.shape[2], near.shape[2])
                one[here, lanes] = ref[group, at, :, :width]
                two[here, lanes] = ref[group, at, :, width:last_at]
                proj_parts[part, here, :] = ref[group, at, :, last_at:]
        total = jnp.zeros((width, width), F32)
        for number in range(parts):
            piece = proj_parts[numbers[PLACES + number]].astype(F32)
            kept = jnp.where(lane_numbers(piece.shape) < block, piece, 0.0)
            wide = jnp.concatenate([kept, jnp.zeros((width, width - SUB), F32)], axis=1)
            total = total + (pltpu.roll(wide, block * number, 1) if number else wide)
        proj[...] = total.astype(LOW)
        for part in range(parts):
            row = vectors[pl.ds(8 + numbers[OWNERS + part], 1), :]
            bias[0:1, part * width : (part + 1) * width] = row
        acc_one[...] = jnp.zeros(acc_one.shape, F32)
        acc_two[...] = jnp.zeros(acc_two.shape, F32)
        acc_proj[...] = jnp.zeros(acc_proj.shape, F32)
        sums[...] = jnp.zeros(sums.shape, F32)
        sums[7:8, :] = out_sums[0:1, :]

    def add_row(row, values):
        sums[pl.ds(row, 1), :] += jnp.sum(values, axis=0, keepdims=True)

    own = mixed[...]
    residual = tokens[...].astype(F32) + dot(own, proj[...], NT) + vectors[4:5, :]
    normed, rate = norm_parts(residual)
    gain = vectors[5:6, :]
    second_in = (normed * gain + vectors[6:7, :]).astype(LOW)
    out_low = cotangent[...]
    grad_out = out_low.astype(F32)
    second_turned = second_in.T
    out_turned = out_turned[...]
    totals = [residual + vectors[7:8, :], jnp.zeros(residual.shape, F32)]

    count = hidden_width // FF_CHUNK
    ones = jnp.ones((16, MLP_TILE), LOW)
    second_and_ones = jnp.concatenate([second_turned, ones], axis=0)
    hiddens, slopes, kept = {}, {}, {}

    def lanes_of(number):
        return pl.ds(number * FF_CHUNK, FF_CHUNK)

    def make_hidden(number):
        hiddens[number] = dot(second_in, one[:, lanes_of(number)])

    def make_slope(number):
        slopes[number] = dot(out_low, two[:, lanes_of(number)])

    def add_one(number):
        acc_one[:, lanes_of(number)] += dot(second_and_ones, kept[number][1])

    def add_two(number):
        acc_two[:, lanes_of(number)] += dot(out_turned, kept[number][0])

    def add_result(number):
        totals[0] = totals[0] + dot(kept[number][0], two[:, lanes_of(number)], NT)

    def add_second(number):
        totals[1] = totals[1] + dot(kept[number][1], one[:, lanes_of(number)], NT)

    make_hidden(0)
    make_slope(0)
    for number in range(count):
        between = []
        if number + 1 < count:
            between += [functools.partial(f, number + 1) for f in (make_hidden, make_slope)]
        if number > 0:
            between += [
                functools.partial(f, number - 1)
                for f in (add_result, add_second, add_one, add_two)
            ]
        kept[number] = gelu_rows(
            hiddens.pop(number), bias[0:1, lanes_of(number)], slopes.pop(number), between
        )
    for f in (add_result, add_second, add_one, add_two):
        f(count - 1)
    result, grad_second = totals
    output[...] = result.astype(LOW)
    add_row(5, grad_second * normed)
    add_row(6, grad_second)
    grad_res = grad_out + norm_back(grad_second, normed, rate, gain)
    grad_residual[...] = grad_res
    branch = grad_res.astype(LOW)
    add_row(4, branch.astype(F32))
    acc_proj[...] += dot(branch.T, own)
    grad_own = dot(branch, proj[...]).astype(LOW)
    grad_mixed[...] = grad_own
    high, rest = halves(grad_own.astype(F32) * own.astype(F32))
    head = lax.broadcasted_iota(jnp.int32, (16, width), 0)
    chosen = (lane_numbers((16, width)) // (width // HEADS) == head).astype(F32).astype(LOW)
    inner[...] = (dot(chosen, high, NT) + dot(chosen, rest, NT))[:8]

    @pl.when(step == pl.num_programs(0) - 1)
    def finish():
        total = acc_proj[...]
        for number in range(parts):
            turned = pltpu.roll(total, (width - block * number) % width, 1) if number else total
            proj_parts[numbers[PLACES + number]] = turned[:, :SUB].astype(LOW)
        for part in range(parts):
            ref, at = (grads_near, part) if part < mid else (grads_far, part - mid)
            lanes = pl.ds(part * width, width)
            for group in range(ref.shape[0]):
                here = pl.ds(group * ref.shape[2], ref.shape[2])
                ref[group, at, :, :width] = acc_one[here, lanes].astype(LOW)
                ref[group, at, :, width:last_at] = acc_two[here, lanes].astype(LOW)
                ref[group, at, :, last_at:] = proj_parts[part, here, :]
            sums[pl.ds(8 + numbers[OWNERS + part], 1), :] = acc_one[width : width + 1, lanes]


def mlp_both(numbers, near, far, vectors, mixed, tokens, cotangent, out_turned, out_sums):
    rows, width = tokens.shape
    parts = near.shape[1] + far.shape[1]
    hidden_width = parts * width
    tile = pl.BlockSpec((MLP_TILE, width), lambda s, *_: (s, 0))
    whole = lambda *dims: pl.BlockSpec(dims, lambda s, *_: (0,) * len(dims))
    return pl.pallas_call(
        mlp_kernel,
        grid_spec=pltpu.PrefetchScalarGridSpec(
            num_scalar_prefetch=1,
            grid=(rows // MLP_TILE,),
            in_specs=[
                whole(*near.shape), whole(*far.shape), whole(*vectors.shape), tile, tile, tile,
                pl.BlockSpec((width, MLP_TILE), lambda s, *_: (0, s)), whole(*out_sums.shape),
            ],
            out_specs=[
                tile,
                tile,
                tile,
                pl.BlockSpec((8, MLP_TILE), lambda s, *_: (0, s)),
                whole(*near.shape),
                whole(*far.shape),
                whole(*vectors.shape),
            ],
            scratch_shapes=[
                pltpu.VMEM((width, hidden_width), LOW),
                pltpu.VMEM((width, hidden_width), LOW),
                pltpu.VMEM((parts, width, SUB), LOW),
                pltpu.VMEM((width, width), LOW),
                pltpu.VMEM((width + 16, hidden_width), F32),
                pltpu.VMEM((width, hidden_width), F32),
                pltpu.VMEM((width, width), F32),
                pltpu.VMEM((8, hidden_width), F32),
            ],
        ),
        out_shape=[
            jax.ShapeDtypeStruct((rows, width), LOW),
            jax.ShapeDtypeStruct((rows, width), F32),
            jax.ShapeDtypeStruct((rows, width), LOW),
            jax.ShapeDtypeStruct((8, rows), F32),
            jax.ShapeDtypeStruct(near.shape, LOW),
            jax.ShapeDtypeStruct(far.shape, LOW),
            jax.ShapeDtypeStruct(vectors.shape, F32),
        ],
        compiler_params=pltpu.CompilerParams(vmem_limit_bytes=VMEM_LIMIT),
        cost_estimate=pl.CostEstimate(
            flops=34_000_000_000, bytes_accessed=20_000_000, transcendentals=6_000_000
        ),
        name="mlp_both",
    )(numbers, near, far, vectors, mixed, tokens, cotangent, out_turned, out_sums)


def attend_back_kernel(
    numbers,
    query,
    key_turned,
    value,
    probs,
    inner,
    grad_mixed,
    normed_turned,
    weight,
    vectors,
    sums,
    grad_qkv,
    near,
    far,
    grad_query,
    acc_key,
    acc_value,
    acc_sums,
    normed_sums,
    blocks,
    rows,
):
    step = pl.program_id(0)
    chunks = pl.num_programs(0) - 1
    pairs = range(PAIRS)
    count = len(pairs)
    scale = (SUB // 2) ** (-0.5)

    @pl.when(step == 0)
    def clear():
        acc_key[...] = jnp.zeros(acc_key.shape, F32)
        acc_value[...] = jnp.zeros(acc_value.shape, F32)
        normed_sums[...] = jnp.zeros(normed_sums.shape, F32)
        acc_sums[...] = jnp.zeros(acc_sums.shape, F32)

    @pl.when(step < chunks)
    def attend():
        def place(number):
            sub, at = number // count, number % count
            start = pl.multiple_of((step * (TILE // SUB) + sub) * SUB, SUB)
            return sub, at, start, pl.ds(start, SPAN), pl.ds(at * SUB, SUB)

        def slope(number):
            sub, _, _, near_rows, heads = place(number)
            grad = both_heads(grad_mixed[pl.ds(sub * SUB, SUB), heads])
            return dot(value[near_rows, heads], grad, NT)

        def soften(number, slopes):
            sub, at, _, _, _ = place(number)
            pair = pairs[at]
            cols = pl.ds(sub * SUB, SUB)
            both = []
            for head in range(2):
                lanes = slice(head * SUB, (head + 1) * SUB)
                less = slopes[:, lanes] - inner[2 * pair + head : 2 * pair + head + 1, cols]
                both.append((probs[at, sub, :, lanes].astype(F32) * less).astype(LOW))
            return jnp.concatenate(both, axis=1)

        def collect(number, scores):
            sub, at, start, near_rows, heads = place(number)
            first, second = halves_of(dot(key_turned[heads, near_rows], scores))
            turned = (jnp.concatenate([first, second], axis=0) * scale).astype(LOW)
            grad_query[pl.ds(start, SUB), heads] = turned.T
            wanted = both_heads(query[pl.ds(start + MARGIN, SUB), heads])
            acc_key[near_rows, heads] += dot(scores, wanted)
            grad = both_heads(grad_mixed[pl.ds(sub * SUB, SUB), heads])
            acc_value[near_rows, heads] += dot(probs[at, sub], grad)

        staged(TILE // SUB * count, slope, soften, collect)

    @pl.when(step > 0)
    def collect():
        here = pl.ds(pl.multiple_of((step - 1) * TILE, SUB), TILE)
        there = pl.ds(pl.multiple_of((step - 1) * TILE + MARGIN, SUB), TILE)
        parts = (
            grad_query[here, :],
            acc_key[there, :].astype(LOW),
            acc_value[there, :].astype(LOW),
        )
        joined = jnp.concatenate(parts, axis=1)
        grad_qkv[...] = joined
        normed_sums[...] += dot(normed_turned[...], joined)
        acc_sums[0:1, :] += jnp.sum(joined.astype(F32), axis=0, keepdims=True)

    @pl.when(step == chunks)
    def finish():
        weight_grad(
            numbers, normed_sums[...], acc_sums[0:1, :], weight, vectors, sums, near, far, blocks, rows
        )


def weight_grad(numbers, total, columns, weight, vectors, sums, near, far, blocks, rows):
    width = weight.shape[0]
    parts, mid = blocks.shape[0], near.shape[0]
    block = 3 * width // parts
    rows_each = 12 // parts
    wide = weight[...].astype(F32)
    grad_gain = jnp.sum(total * wide, axis=1, keepdims=True)
    grad_shift = jnp.sum(wide * columns, axis=1, keepdims=True)
    rows[...] = jnp.zeros(rows.shape, F32)
    rows[0:VEC_LANES, :] = sums[...]
    rows[2:3, :] = columns[:, :width]
    rows[3:4, :] = columns[:, 2 * width :]
    rows[VEC_LANES : 2 * VEC_LANES, :] = vectors[...]
    turned = rows[...].T
    gain = turned[:, VEC_LANES : VEC_LANES + 1]
    shift = turned[:, VEC_LANES + 1 : VEC_LANES + 2]
    lane = lane_numbers(turned.shape)
    turned = jnp.where(lane == 0, grad_gain, jnp.where(lane == 1, grad_shift, turned))
    total = total * gain + shift * columns
    at = block - 2 * SUB
    for number in range(parts):
        first, over = block * number // SUB * SUB, block * number % SUB
        piece = total[:, first : first + width + SUB]
        if over:
            missing = width + SUB - piece.shape[1]
            if missing:
                piece = jnp.concatenate([piece, jnp.zeros((width, missing), F32)], axis=1)
            piece = pltpu.roll(piece, width + SUB - over, 1)
        piece = piece[:, :width]
        vec = pltpu.roll(turned, (at - rows_each * number) % SUB, 1)
        last = jnp.where(lane < at, piece[:, 2 * SUB :], 0.0)
        last = jnp.where((lane >= at) & (lane < at + rows_each), vec, last)
        at_place = numbers[PLACES + number]
        blocks[at_place, :, : 2 * SUB] = piece[:, : 2 * SUB].astype(LOW)
        blocks[at_place, :, 2 * SUB :] = last.astype(LOW)
    near[...] = blocks[:mid]
    far[...] = blocks[mid:]


def attend_backward(
    numbers, parts, query, key_turned, value, probs, inner, grad_mixed, normed_turned, weight,
    vectors, sums,
):
    width, rows = normed_turned.shape
    padded = query.shape[0]
    chunks = rows // TILE
    tiles = TILE // SUB
    now = lambda s: jnp.minimum(s, chunks - 1)
    before = lambda s: jnp.maximum(s - 1, 0)
    whole = lambda *dims: pl.BlockSpec(dims, lambda s, *_: (0,) * len(dims))
    half = (parts // 2, width, width)
    return pl.pallas_call(
        attend_back_kernel,
        grid_spec=pltpu.PrefetchScalarGridSpec(
            num_scalar_prefetch=1,
            grid=(chunks + 1,),
            in_specs=[
                whole(padded, width),
                whole(width, padded),
                whole(padded, width),
                pl.BlockSpec((PAIRS, tiles, SPAN, 2 * SUB), lambda s, *_: (0, now(s), 0, 0)),
                pl.BlockSpec((8, TILE), lambda s, *_: (0, now(s))),
                pl.BlockSpec((TILE, width), lambda s, *_: (now(s), 0)),
                pl.BlockSpec((width, TILE), lambda s, *_: (0, before(s))),
                whole(*weight.shape),
                whole(*vectors.shape),
                whole(*sums.shape),
            ],
            out_specs=[
                pl.BlockSpec((TILE, 3 * width), lambda s, *_: (before(s), 0)),
                whole(*half),
                whole(*half),
            ],
            scratch_shapes=[
                pltpu.VMEM((rows, width), LOW),
                pltpu.VMEM((padded, width), F32),
                pltpu.VMEM((padded, width), F32),
                pltpu.VMEM((8, 3 * width), F32),
                pltpu.VMEM((width, 3 * width), F32),
                pltpu.VMEM((parts, width, width), LOW),
                pltpu.VMEM((SUB, width), F32),
            ],
        ),
        out_shape=[
            jax.ShapeDtypeStruct((rows, 3 * width), LOW),
            jax.ShapeDtypeStruct(half, LOW),
            jax.ShapeDtypeStruct(half, LOW),
        ],
        compiler_params=pltpu.CompilerParams(vmem_limit_bytes=VMEM_LIMIT),
        cost_estimate=pl.CostEstimate(
            flops=16_000_000_000, bytes_accessed=24_000_000, transcendentals=0
        ),
        name="attend_backward",
    )(
        numbers, query, key_turned, value, probs, inner, grad_mixed, normed_turned, weight, vectors,
        sums,
    )


def input_grad_kernel(weight, vectors, tokens, grad_residual, grad_qkv, input_grad):
    normed, rate = norm_parts(tokens[...].astype(F32))
    grad_first = dot(grad_qkv[...], weight[...], NT)
    back = norm_back(grad_first, normed, rate, vectors[0:1, :])
    input_grad[...] = (grad_residual[...] + back).astype(LOW)


def input_gradient(weight, vectors, tokens, grad_residual, grad_qkv):
    rows, width = tokens.shape
    size = TILE
    tile = pl.BlockSpec((size, width), lambda s: (s, 0))
    whole = lambda ref: pl.BlockSpec(ref.shape, lambda s: (0, 0))
    return pl.pallas_call(
        input_grad_kernel,
        grid=(rows // size,),
        in_specs=[
            whole(weight), whole(vectors), tile, tile,
            pl.BlockSpec((size, 3 * width), lambda s: (s, 0)),
        ],
        out_specs=tile,
        out_shape=jax.ShapeDtypeStruct((rows, width), LOW),
        compiler_params=pltpu.CompilerParams(vmem_limit_bytes=VMEM_LIMIT),
        cost_estimate=pl.CostEstimate(
            flops=4_000_000_000, bytes_accessed=13_000_000, transcendentals=2048
        ),
        name="input_gradient",
    )(weight, vectors, tokens, grad_residual, grad_qkv)


def halves(value):
    high = value.astype(LOW)
    return high, (value - high.astype(F32)).astype(LOW)


def dot_three(left, right):
    tall = jnp.concatenate([right[0], right[0], right[1]], axis=0)
    return dot(jnp.concatenate([left[0], left[1], left[0]], axis=1), tall)


def newton_rows(blocks, offset, rows, store):
    gram = dot(blocks[0], blocks[0], NT)
    for part in blocks[1:]:
        gram = gram + dot(part, part, NT)
    depth = gram.shape[0]
    down = lax.broadcasted_iota(jnp.int32, (depth, depth), 0)
    eye = (down == lane_numbers((depth, depth))).astype(F32)
    norm = 1.0 / (jnp.sqrt(jnp.sum(gram * eye, keepdims=True)) + 1e-07)
    gram = gram * (norm * norm)
    place = lax.broadcasted_iota(jnp.int32, (rows, depth), 0) + offset
    left = jnp.where(place == lane_numbers((rows, depth)), norm, 0.0)
    store[0:depth, :] = gram
    store[depth:, :] = left

    @pl.loop(0, NS_STEPS - 1)
    def advance(_):
        both = halves(store[...])
        pair = [part[:depth] for part in both]
        down = lax.broadcasted_iota(jnp.int32, (depth, depth), 0)
        eye = (down == lane_numbers((depth, depth))).astype(F32)
        square = dot_three(pair, pair)
        poly = halves(NEWTON_A * eye + NEWTON_B * store[0:depth, :] + NEWTON_C * square)
        made = dot_three(both, poly)
        store[depth:, :] = made[depth:]
        store[0:depth, :] = dot_three(halves(made[:depth]), poly)

    left = store[depth:, :]
    pair = halves(store[0:depth, :])
    once = dot_three(halves(left), pair)
    return NEWTON_A * left + NEWTON_B * once + NEWTON_C * dot_three(halves(once), pair)


def newton_store(depth, rows):
    return pltpu.VMEM((depth + tall_of(rows), depth), F32)


def stepped(left, own, height, old):
    high, rest = halves(left)
    ortho = (dot(high, own) + dot(rest, own))[: old.shape[0], : old.shape[1]]
    return old * (1.0 - MUON_RATE * MUON_DECAY) - (MUON_RATE * 0.2 * math.sqrt(height)) * ortho


def kept_lanes(value, low, high):
    lane = lane_numbers(value.shape)
    return jnp.where((lane >= low) & (lane < high), value.astype(F32), 0.0).astype(LOW)


def tall_of(rows):
    return -(-rows // 16) * 16


def muon_kernel(height, numbers, *refs):
    old, new, copy, store = refs[-4:]
    count = old.shape[1]
    blocks = [kept_lanes(ref[...], 0, count) for ref in refs[:-4]]
    left = newton_rows(blocks, numbers[OFFSET], tall_of(old.shape[0]), store)
    result = stepped(left, blocks[0], height, old[...])
    new[...] = result
    copy[...] = result.astype(LOW)


def muon(height, numbers, blocks, old):
    vmem = pl.BlockSpec(memory_space=pltpu.VMEM)

    def kernel(*refs):
        muon_kernel(height, *refs)

    return pl.pallas_call(
        kernel,
        in_specs=[pl.BlockSpec(memory_space=pltpu.SMEM)] + [vmem] * (len(blocks) + 1),
        out_specs=[vmem, vmem],
        out_shape=[
            jax.ShapeDtypeStruct(old.shape, F32),
            jax.ShapeDtypeStruct(old.shape, LOW),
        ],
        scratch_shapes=[newton_store(blocks[0].shape[0], old.shape[0])],
        compiler_params=pltpu.CompilerParams(vmem_limit_bytes=VMEM_LIMIT),
        cost_estimate=pl.CostEstimate(
            flops=9_000_000_000, bytes_accessed=2_000_000, transcendentals=10
        ),
        name="muon",
    )(numbers, *blocks, old)


def pick_kernel(count, numbers, *refs):
    pieces, columns, outs = refs[:count], refs[count], refs[count + 1 :]
    share = pieces[0].shape[0]
    for k, piece in enumerate(pieces):
        columns[k * share : (k + 1) * share, :] = piece[...]
        for n, out in enumerate(outs):
            at = pl.multiple_of(numbers[STARTS + n] * SUB, SUB)
            out[k * share : (k + 1) * share, :] = piece[:, pl.ds(at, out.shape[1])]


def pick(numbers, pieces, count):
    depth = len(pieces) * pieces[0].shape[0]
    vmem = pl.BlockSpec(memory_space=pltpu.VMEM)

    def kernel(*refs):
        pick_kernel(len(pieces), *refs)

    return pl.pallas_call(
        kernel,
        in_specs=[pl.BlockSpec(memory_space=pltpu.SMEM)] + [vmem] * len(pieces),
        out_specs=[vmem] * (count + 1),
        out_shape=[jax.ShapeDtypeStruct((depth, pieces[0].shape[1]), LOW)]
        + [jax.ShapeDtypeStruct((depth, depth), LOW)] * count,
        name="pick",
    )(numbers, *pieces)


def newton_kernel(numbers, *refs):
    left, store = refs[-2:]
    bounds = numbers[LOW_LANE], numbers[HIGH_LANE]
    blocks = [kept_lanes(ref[...], *bounds) for ref in refs[:-2]]
    left[...] = newton_rows(blocks, numbers[OFFSET], left.shape[0], store)


def newton(numbers, blocks, rows):
    vmem = pl.BlockSpec(memory_space=pltpu.VMEM)
    return pl.pallas_call(
        newton_kernel,
        in_specs=[pl.BlockSpec(memory_space=pltpu.SMEM)] + [vmem] * len(blocks),
        out_specs=vmem,
        out_shape=jax.ShapeDtypeStruct((tall_of(rows), blocks[0].shape[0]), F32),
        scratch_shapes=[newton_store(blocks[0].shape[0], rows)],
        compiler_params=pltpu.CompilerParams(vmem_limit_bytes=VMEM_LIMIT),
        cost_estimate=pl.CostEstimate(
            flops=9_000_000_000, bytes_accessed=2_000_000, transcendentals=10
        ),
        name="newton",
    )(numbers, *blocks)


def finish_kernel(heights, lanes, numbers, columns, *refs):
    count = len(heights)
    store = refs[-1]
    news = refs[-1 - 2 * count : -1]
    olds = refs[-1 - 3 * count : -1 - 2 * count]
    lefts = refs[: -1 - 3 * count]
    for n, left in enumerate(lefts):
        store[n] = left[...]
    for n in range(count):
        wide = -(-olds[n].shape[1] // SUB) * SUB
        own = columns[:, lanes[n] : lanes[n] + wide]
        result = stepped(store[numbers[WHICH + n]], own, heights[n], olds[n][...])
        news[2 * n][...] = result
        news[2 * n + 1][...] = result.astype(LOW)


def finish(heights, lanes, numbers, columns, lefts, olds):
    vmem = pl.BlockSpec(memory_space=pltpu.VMEM)
    count = len(olds)

    def kernel(*refs):
        finish_kernel(heights, lanes, *refs)

    outs = pl.pallas_call(
        kernel,
        in_specs=[pl.BlockSpec(memory_space=pltpu.SMEM)] + [vmem] * (1 + len(lefts) + count),
        out_specs=[vmem] * (2 * count),
        out_shape=[
            jax.ShapeDtypeStruct(old.shape, kind) for old in olds for kind in (F32, LOW)
        ],
        scratch_shapes=[pltpu.VMEM((len(lefts), *lefts[0].shape), F32)],
        compiler_params=pltpu.CompilerParams(vmem_limit_bytes=VMEM_LIMIT),
        cost_estimate=pl.CostEstimate(
            flops=200_000_000, bytes_accessed=2_000_000, transcendentals=0
        ),
        name="finish",
    )(numbers, columns, *lefts, *olds)
    return [(outs[2 * n], outs[2 * n + 1]) for n in range(count)]


def exchange(x, axis, mask):
    size = lax.axis_size(axis)
    return lax.ppermute(x, axis, [(i, i ^ mask) for i in range(size)])


def place_masks(size):
    masks = [0]
    bit = size // 2
    while bit >= 1:
        masks = masks + [m ^ bit for m in masks]
        bit //= 2
    return masks


def from_columns(own):
    size = lax.axis_size("dp")
    sent = jnp.broadcast_to(own[None], (size, *own.shape))
    return lax.all_to_all(sent, "dp", split_axis=0, concat_axis=0, tiled=True)


def over_columns(own):
    return from_columns(own).reshape(-1, own.shape[1])


def device_numbers(dp, ns, share, width, proj_rows):
    masks = place_masks(ns)
    tasks = [(0, 0, width), (width // SUB, 0, width)]
    tasks += [(width // SUB + 1, 2 * SUB, 2 * SUB + proj_rows)] * (ns - 2)
    table = np.zeros((dp * ns, 24), np.int32)
    for device in range(dp * ns):
        column, index = device // ns, device % ns
        row = table[device]
        for n in range(ns):
            row[OWNERS + n] = index ^ masks[n]
            row[PLACES + (index ^ masks[n])] = n
            row[STARTS + n] = tasks[index ^ n][0]
        for n in range(3):
            row[WHICH + n] = index ^ n
        row[OFFSET] = column * share
        row[COLUMN] = column
        row[LOW_LANE], row[HIGH_LANE] = tasks[index][1:]
    return table


def half_rows(own):
    held = [own]
    bit = lax.axis_size("ns") // 2
    while bit > 1:
        held = held + [exchange(block, "ns", bit) for block in held]
        bit //= 2
    return held


def added(keep, got):
    return (keep.astype(F32) + got.astype(F32)).astype(LOW)


def sum_columns(pieces):
    return summed(lax.all_to_all(pieces, "dp", split_axis=0, concat_axis=0, tiled=True))


def summed(pieces):
    return jnp.sum(pieces.astype(F32), axis=0)


def split_kernel(numbers, keep, got, *outs):
    share = outs[0].shape[0]
    for mask, out in enumerate(outs):
        at = pl.ds(pl.multiple_of((numbers[COLUMN] ^ mask) * share, 16), share)
        out[...] = added(keep[at, :], got[at, :])


def split_sum(numbers, keep, got, devices):
    vmem = pl.BlockSpec(memory_space=pltpu.VMEM)
    shape = jax.ShapeDtypeStruct((keep.shape[0] // devices, keep.shape[1]), LOW)
    return pl.pallas_call(
        split_kernel,
        in_specs=[pl.BlockSpec(memory_space=pltpu.SMEM), vmem, vmem],
        out_specs=[vmem] * devices,
        out_shape=[shape] * devices,
        cost_estimate=pl.CostEstimate(
            flops=200_000, bytes_accessed=1_000_000, transcendentals=0
        ),
        name="split_sum",
    )(numbers, keep, got)


def widened(arrays, lanes):
    joined = jnp.concatenate(arrays, axis=1)
    return jnp.pad(joined, ((0, 0), (0, lanes - joined.shape[1])))


def per_device(
    tokens,
    cotangent,
    segment,
    valid_rows,
    qkv_weight,
    proj_weight,
    fc1_weight,
    fc2_weight,
    qkv_moment,
    proj_moment,
    fc1_moment,
    fc2_moment,
    vectors,
    vector_moment,
    vector_square,
):
    rows, width = tokens.shape
    ns = lax.axis_size("ns")
    qkv_w, proj_w, fc1_w, fc2_w = (w.T for w in (qkv_weight, proj_weight, fc1_weight, fc2_weight))
    qkv_m, proj_m, fc1_m, fc2_m = (w.T for w in (qkv_moment, proj_moment, fc1_moment, fc2_moment))
    share, count = qkv_w.shape
    vec_rows = vectors.shape[0]
    first_lanes = width
    later_lanes = 2 * width + SUB

    table = device_numbers(lax.axis_size("dp"), ns, share, width, proj_w.shape[1])
    device = lax.axis_index("dp") * ns + lax.axis_index("ns")
    numbers = lax.dynamic_slice(jnp.asarray(table), (device, 0), (1, table.shape[1]))[0]

    row_ids = jnp.where(
        valid_rows > 0, segment, rows + jnp.arange(rows, dtype=jnp.int32)
    ).astype(F32)
    ids = jnp.pad(row_ids, (MARGIN, MARGIN), constant_values=-1.0).reshape(-1, SUB)
    ids = jnp.pad(ids, ((0, -ids.shape[0] % 8), (0, 0)), constant_values=-1.0)

    later_own = widened([fc1_w, fc2_w, proj_w], later_lanes).astype(LOW)
    later_own, numbers = lax.optimization_barrier((later_own, numbers))
    later_pair = jnp.stack([later_own, exchange(later_own, "ns", ns // 2)])
    first_own = widened([qkv_w, vectors.T], first_lanes).astype(LOW)
    prepared = prepare(tokens, cotangent, ids)
    first_pieces = half_rows(over_columns(first_own))
    first_pieces, prepared = lax.optimization_barrier((first_pieces, prepared))
    normed, normed_turned, out_turned, columns, out_sums = prepared
    first_pieces = first_pieces + [exchange(piece, "ns", 1) for piece in first_pieces]
    later_near = from_columns(later_pair)
    if share % 16:
        later_near = jnp.moveaxis(later_near, 0, 1).reshape(1, ns // 2, width, later_lanes)

    query, _, value, key_turned, mixed, probs, weight, vector_full = attend_forward(
        numbers, first_pieces, normed, ids, columns
    )
    later_near, mixed = lax.optimization_barrier((later_near, mixed))
    later_far = exchange(later_near, "ns", 1)
    output, grad_residual, grad_mixed, inner, grads_near, grads_far, sums = mlp_both(
        numbers, later_near, later_far, vector_full, mixed, tokens, cotangent, out_turned, out_sums
    )
    held = added(grads_near, exchange(grads_far, "ns", 1))
    held, grad_mixed = lax.optimization_barrier((held, grad_mixed))
    if share % 16:
        held = jnp.moveaxis(held.reshape(ns // 2, -1, share, later_lanes), 1, 0)
    later_got = lax.all_to_all(held, "dp", split_axis=0, concat_axis=0, tiled=True)

    grad_qkv, grads_near, grads_far = attend_backward(
        numbers, ns, query, key_turned, value, probs, inner, grad_mixed, normed_turned, weight,
        vector_full, sums,
    )
    held = added(grads_near, exchange(grads_far, "ns", 1))
    got = exchange(held[1], "ns", ns // 2)
    input_grad = input_gradient(weight, vector_full, tokens, grad_residual, grad_qkv)
    got, input_grad, later_got = lax.optimization_barrier((got, input_grad, later_got))
    devices = lax.axis_size("dp")
    direct = devices <= 8 and share % 16 == 0
    if direct:
        first_held = split_sum(numbers, held[0], got, devices)
    else:
        first_held = [added(held[0], got)]
    later_sums = summed(later_got)
    later_owned = later_sums[0] + exchange(later_sums[1].astype(LOW), "ns", ns // 2).astype(F32)
    later_moment = later_owned + 0.5 * widened([fc1_m, fc2_m, proj_m], later_lanes)
    later_low, first_held = lax.optimization_barrier((later_moment.astype(LOW), first_held))
    pieces = [over_columns(later_low)]
    if direct:
        first_owned = first_held[0].astype(F32)
        for mask in range(1, devices):
            first_owned = first_owned + exchange(first_held[mask], "dp", mask).astype(F32)
    else:
        first_owned = sum_columns(first_held[0].reshape(devices, share, first_lanes))
    columns, *chosen = pick(numbers, pieces, ns)
    blocks = [chosen[0]] + [exchange(chosen[mask], "ns", mask) for mask in range(1, ns)]

    first_moment = first_owned + 0.5 * widened([qkv_m], first_lanes)
    first_pieces = half_rows(over_columns(first_moment.astype(LOW)))
    moments_new = (
        first_moment[:, :count],
        later_moment[:, 2 * width : 2 * width + proj_w.shape[1]],
        later_moment[:, :width],
        later_moment[:, width : 2 * width],
    )

    vector_grad = first_owned[:, count : count + vec_rows].T
    first_new = BETA_ONE * vector_moment + (1.0 - BETA_ONE) * vector_grad
    second_new = BETA_TWO * vector_square + (1.0 - BETA_TWO) * vector_grad * vector_grad
    first_hat = first_new / (1.0 - BETA_ONE**STEP)
    second_hat = second_new / (1.0 - BETA_TWO**STEP)
    vectors_new = vectors - ADAM_RATE * first_hat / (jnp.sqrt(second_hat) + ADAM_EPS)
    small = (*(m.T for m in moments_new), first_new, second_new, vectors_new)
    blocks, small = lax.optimization_barrier((blocks, small))
    left = newton(numbers, blocks, share)
    left, first_pieces = lax.optimization_barrier((left, first_pieces))
    first_pieces = first_pieces + [exchange(piece, "ns", 1) for piece in first_pieces]
    qkv_new = muon(count * ns, numbers, first_pieces, qkv_w)
    lefts = [left] + [exchange(left, "ns", mask) for mask in range(1, ns)]
    lefts, qkv_new = lax.optimization_barrier((lefts, qkv_new))
    fc1_new, fc2_new, proj_new = finish(
        [w.shape[1] * ns for w in (fc1_w, fc2_w, proj_w)],
        (0, width, 2 * width),
        numbers,
        columns,
        lefts,
        (fc1_w, fc2_w, proj_w),
    )

    news = (qkv_new, proj_new, fc1_new, fc2_new)
    return (
        output,
        input_grad,
        *(new[0].T for new in news),
        *small,
        *(new[1].T for new in news),
    )


def solution(mesh):
    rows = P(("dp", "ns"), None)
    flat = P(("dp", "ns"))
    block = P("ns", "dp")
    return jax.shard_map(
        per_device,
        mesh=mesh,
        in_specs=(rows, rows, flat, flat) + (block,) * 11,
        out_specs=(rows, rows) + (block,) * 15,
        check_vma=False,
    )
```

```python
import functools
import math

import jax
import jax.numpy as jnp
import numpy as np
from jax import lax
from jax.experimental import pallas as pl
from jax.experimental.pallas import tpu as pltpu
from jax.sharding import PartitionSpec as P

HEADS = 6
PAIRS = 3
MARGIN = 128
NS_STEPS = 5
STEP = 10
TILE = 512
MLP_TILE = 512
FF_CHUNK = 256
SUB = 128
SPAN = 384
VEC_LANES = 16
GROUP = 2


EPS_NORM = 1e-06
NEWTON_A = 3.4445
NEWTON_B = -4.775
NEWTON_C = 2.0315
MUON_RATE = 0.2
MUON_DECAY = 0.1
ADAM_RATE = 0.4
BETA_ONE = 0.9
BETA_TWO = 0.999
ADAM_EPS = 1e-08
LOW = jnp.bfloat16
F32 = jnp.float32
TN = (((0,), (0,)), ((), ()))
NT = (((1,), (1,)), ((), ()))
NN = (((1,), (0,)), ((), ()))
VMEM_LIMIT = 56 * 1024 * 1024
ERF_P = 0.3275911
ERF_COEFS = (0.254829592, -0.284496736, 1.421413741, -1.453152027, 1.061405429)


def dot(left, right, dims=NN):
    return lax.dot_general(left, right, dims, preferred_element_type=F32)


PLACES, OWNERS, STARTS, WHICH, OFFSET, LOW_LANE, HIGH_LANE, COLUMN = 0, 4, 8, 12, 16, 17, 18, 19


def lane_numbers(shape):
    return lax.broadcasted_iota(jnp.int32, shape, len(shape) - 1)


def norm_parts(value):
    center = value - jnp.mean(value, axis=-1, keepdims=True)
    rate = lax.rsqrt(jnp.mean(center * center, axis=-1, keepdims=True) + EPS_NORM)
    return center * rate, rate


def norm_back(grad, normed, rate, gain):
    scaled = grad * gain
    first = jnp.mean(scaled, axis=-1, keepdims=True)
    second = jnp.mean(scaled * normed, axis=-1, keepdims=True)
    return rate * (scaled - first - normed * second)


def gelu_both(value):
    below = 1.0 + (ERF_P * 0.5**0.5) * jnp.abs(value)
    ratio = pl.reciprocal(below, approx=True)
    ratio = ratio * (2.0 - below * ratio)
    decay = jnp.exp2((value * value) * (-0.5 * math.log2(math.e)))
    poly = 0.5 * ERF_COEFS[4]
    for coef in ERF_COEFS[3::-1]:
        poly = poly * ratio + 0.5 * coef
    tail = poly * ratio * decay
    phi = jnp.where(value >= 0, 1.0 - tail, tail)
    return value * phi, phi + (value * (1.0 / math.sqrt(2.0 * math.pi))) * decay


def gelu_rows(hidden, bias, grad, between):
    active, back = [], []
    rows = hidden.shape[0]
    pieces = rows // 16
    for n in range(pieces):
        if n * len(between) // pieces != (n - 1) * len(between) // pieces:
            between[n * len(between) // pieces]()
        here = slice(n * 16, (n + 1) * 16)
        value, slope = gelu_both(hidden[here] + bias)
        active.append(value.astype(LOW))
        back.append((grad[here] * slope).astype(LOW))
    return jnp.concatenate(active, axis=0), jnp.concatenate(back, axis=0)


def halves_of(lanes):
    half = lanes.shape[0] // 2
    return lanes[:half, :SUB], lanes[half:, SUB:]


def staged(count, first, second, third):
    made = first(0)
    kept = None
    for n in range(count):
        coming = first(n + 1) if n + 1 < count else None
        if kept is not None:
            third(n - 1, kept)
        kept = second(n, made)
        made = coming
    third(count - 1, kept)


def both_heads(pair):
    first = (lane_numbers((1, SUB)) < SUB // 2).astype(F32).astype(pair.dtype)
    second = (lane_numbers((1, SUB)) >= SUB // 2).astype(F32).astype(pair.dtype)
    return jnp.concatenate([pair * first, pair * second], axis=0)


def fetch(pairs, sems):
    copies = [
        pltpu.make_async_copy(source, target, sems.at[n])
        for n, (source, target) in enumerate(pairs)
    ]
    for copy in copies:
        copy.start()
    for copy in copies:
        copy.wait()


def prepare_kernel(tokens, cotangent, ids, normed, normed_turned, out_turned, columns, sums):
    step = pl.program_id(0)
    parts = columns.shape[0] // SUB

    @pl.when(step == 0)
    def clear():
        sums[...] = jnp.zeros(sums.shape, F32)
        for number in range(parts):
            row = jnp.broadcast_to(ids[number : number + 1, :], (SUB, SUB))
            columns[number * SUB : (number + 1) * SUB, :] = row.T

    value, _ = norm_parts(tokens[...].astype(F32))
    normed[...] = value
    normed_turned[...] = value.astype(LOW).T
    out_low = cotangent[...]
    out_turned[...] = out_low.T
    sums[0:1, :] += jnp.sum(out_low.astype(F32), axis=0, keepdims=True)


def prepare(tokens, cotangent, ids):
    rows, width = tokens.shape
    padded = rows + 2 * MARGIN
    tile = pl.BlockSpec((TILE, width), lambda s: (s, 0))
    turned = pl.BlockSpec((width, TILE), lambda s: (0, s))
    whole = lambda *dims: pl.BlockSpec(dims, lambda s: (0,) * len(dims))
    return pl.pallas_call(
        prepare_kernel,
        grid=(rows // TILE,),
        in_specs=[tile, tile, whole(*ids.shape)],
        out_specs=[tile, turned, turned, whole(padded, SUB), whole(8, width)],
        out_shape=[
            jax.ShapeDtypeStruct((rows, width), F32),
            jax.ShapeDtypeStruct((width, rows), LOW),
            jax.ShapeDtypeStruct((width, rows), LOW),
            jax.ShapeDtypeStruct((padded, SUB), F32),
            jax.ShapeDtypeStruct((8, width), F32),
        ],
        compiler_params=pltpu.CompilerParams(vmem_limit_bytes=VMEM_LIMIT),
        cost_estimate=pl.CostEstimate(
            flops=20_000_000, bytes_accessed=12_000_000, transcendentals=2048
        ),
        name="prepare",
    )(tokens, cotangent, ids)


def attend_kernel(numbers, *refs):
    (normed, ids, columns, query, key, value, key_turned, mixed, probs, weight, vectors,
     gathered, pair_weight, value_turned, shifts, sems) = refs[-16:]
    pieces = refs[:-16]
    step = pl.program_id(0)
    chunks = pl.num_programs(0) - 1
    width = normed.shape[1]
    parts = len(pieces)
    block = 3 * width // parts
    rows_each = 12 // parts

    @pl.when(step == 0)
    def assemble():
        fetch([(piece, gathered.at[n]) for n, piece in enumerate(pieces)], sems)
        tiles = [jnp.zeros((width, SUB), F32)] * (3 * width // SUB + 1)
        turned = jnp.zeros((width, SUB), F32)
        for number in range(parts):
            piece = gathered[numbers[PLACES + number]].astype(F32)
            kept = jnp.where(lane_numbers(piece.shape) < block, piece, 0.0)
            wide = jnp.concatenate([kept, jnp.zeros((width, SUB), F32)], axis=1)
            over = block * number % SUB
            wide = pltpu.roll(wide, over, 1) if over else wide
            for n in range(wide.shape[1] // SUB):
                at = block * number // SUB + n
                if at < len(tiles):
                    tiles[at] = tiles[at] + wide[:, n * SUB : (n + 1) * SUB]
            last = piece[:, 2 * SUB :]
            at = block - 2 * SUB
            lane = lane_numbers(last.shape)
            vec = jnp.where((lane >= at) & (lane < at + rows_each), last, 0.0)
            turned = turned + pltpu.roll(vec, (rows_each * number - at) % SUB, 1)
        total = jnp.concatenate(tiles[:-1], axis=1).astype(LOW)
        weight[...] = total
        pair_weight[...] = total[:, width:].T
        vectors[...] = turned.T[:VEC_LANES]
        shifts[...] = turned
        edges = (pl.ds(0, MARGIN), pl.ds(MARGIN + chunks * TILE, MARGIN))
        for edge in edges:
            for ref in (query, key, value):
                ref[edge, :] = jnp.zeros((MARGIN, width), LOW)
            for ref in (key_turned, value_turned):
                ref[:, edge] = jnp.zeros((width, MARGIN), LOW)

    @pl.when(step < chunks)
    def project():
        first_in = (normed[...] * vectors[0:1, :] + vectors[1:2, :]).astype(LOW)
        result = dot(first_in, weight[...])
        turned = dot(pair_weight[...], first_in, NT)
        here = pl.ds(pl.multiple_of(MARGIN + step * TILE, SUB), TILE)
        scale = (width // HEADS) ** (-0.5)
        made = (result[:, :width] + vectors[2:3, :]).astype(LOW) * jnp.asarray(scale, LOW)
        query[here, :] = made
        key[here, :] = result[:, width : 2 * width].astype(LOW)
        value[here, :] = (result[:, 2 * width :] + vectors[3:4, :]).astype(LOW)
        key_turned[:, here] = turned[:width].astype(LOW)
        value_turned[:, here] = (turned[width:] + shifts[:, 3:4]).astype(LOW)

    @pl.when(step > 0)
    def attend():
        def place(number):
            sub, pair = number // PAIRS, number % PAIRS
            tile = (step - 1) * (TILE // SUB) + sub
            start = pl.multiple_of(tile * SUB, SUB)
            return sub, pair, tile, start, pl.ds(start, SPAN), pl.ds(pair * SUB, SUB)

        def of_group(group):
            return range(group * GROUP, (group + 1) * GROUP)

        def score(group):
            made = []
            for number in of_group(group):
                _, _, _, start, near_rows, heads = place(number)
                wanted = both_heads(query[pl.ds(start + MARGIN, SUB), heads])
                made.append(dot(key[near_rows, heads], wanted, NT))
            return made

        def soften(group, made):
            own = []
            for number, scores in zip(of_group(group), made):
                _, _, tile, _, near_rows, _ = place(number)
                same = columns[near_rows, :] == ids[pl.ds(tile + 1, 1), :]
                own += [
                    jnp.where(same, scores[:, head * SUB : (head + 1) * SUB], -1e30)
                    for head in range(2)
                ]
            largest = [jnp.max(part, axis=0, keepdims=True) for part in own]
            expo = [jnp.exp(part - most) for part, most in zip(own, largest)]
            share = [1.0 / jnp.sum(part, axis=0, keepdims=True) for part in expo]
            scaled = [(part * by).astype(LOW) for part, by in zip(expo, share)]
            result = []
            for n, number in enumerate(of_group(group)):
                sub, pair, _, _, _, _ = place(number)
                result.append(jnp.concatenate(scaled[2 * n : 2 * n + 2], axis=1))
                probs[pair, sub] = result[-1]
            return result

        def mix(group, kept):
            for number, prob in zip(of_group(group), kept):
                sub, _, _, _, near_rows, heads = place(number)
                first, second = halves_of(dot(value_turned[heads, near_rows], prob))
                turned = jnp.concatenate([first, second], axis=0).astype(LOW)
                mixed[pl.ds(sub * SUB, SUB), heads] = turned.T

        staged(TILE // SUB * PAIRS // GROUP, score, soften, mix)


def attend_forward(numbers, pieces, normed, ids, columns):
    rows, width = normed.shape
    chunks = rows // TILE
    tiles = TILE // SUB
    parts = len(pieces)
    now = lambda s: jnp.minimum(s, chunks - 1)
    before = lambda s: jnp.maximum(s - 1, 0)
    whole = lambda *dims: pl.BlockSpec(dims, lambda s, *_: (0,) * len(dims))
    padded = rows + 2 * MARGIN
    return pl.pallas_call(
        attend_kernel,
        grid_spec=pltpu.PrefetchScalarGridSpec(
            num_scalar_prefetch=1,
            grid=(chunks + 1,),
            in_specs=[pl.BlockSpec(memory_space=pl.ANY)] * parts
            + [
                pl.BlockSpec((TILE, width), lambda s, *_: (now(s), 0)),
                whole(*ids.shape),
                whole(*columns.shape),
            ],
            out_specs=[
                whole(padded, width),
                whole(padded, width),
                whole(padded, width),
                whole(width, padded),
                pl.BlockSpec((TILE, width), lambda s, *_: (before(s), 0)),
                pl.BlockSpec((PAIRS, tiles, SPAN, 2 * SUB), lambda s, *_: (0, before(s), 0, 0)),
                whole(width, 3 * width),
                whole(VEC_LANES, width),
            ],
            scratch_shapes=[
                pltpu.VMEM((parts, *pieces[0].shape), LOW),
                pltpu.VMEM((2 * width, width), LOW),
                pltpu.VMEM((width, padded), LOW),
                pltpu.VMEM((width, SUB), F32),
                pltpu.SemaphoreType.DMA((parts,)),
            ],
        ),
        out_shape=[
            jax.ShapeDtypeStruct((padded, width), LOW),
            jax.ShapeDtypeStruct((padded, width), LOW),
            jax.ShapeDtypeStruct((padded, width), LOW),
            jax.ShapeDtypeStruct((width, padded), LOW),
            jax.ShapeDtypeStruct((rows, width), LOW),
            jax.ShapeDtypeStruct((PAIRS, rows // SUB, SPAN, 2 * SUB), LOW),
            jax.ShapeDtypeStruct((width, 3 * width), LOW),
            jax.ShapeDtypeStruct((VEC_LANES, width), F32),
        ],
        compiler_params=pltpu.CompilerParams(vmem_limit_bytes=VMEM_LIMIT),
        cost_estimate=pl.CostEstimate(
            flops=12_000_000_000, bytes_accessed=22_000_000, transcendentals=5_000_000
        ),
        name="attend_forward",
    )(numbers, *pieces, normed, ids, columns)


def mlp_kernel(numbers, near, far, *refs):
    (vectors, mixed, tokens, cotangent, out_turned, out_sums, output, grad_residual, grad_mixed, inner, grads_near,
     grads_far, sums, one, two, proj_parts, proj, acc_one, acc_two, acc_proj, bias
    ) = refs
    step = pl.program_id(0)
    width = tokens.shape[1]
    mid = near.shape[1]
    parts = mid + far.shape[1]
    block = width // parts
    last_at = 2 * width
    hidden_width = one.shape[1]

    @pl.when(step == 0)
    def assemble():
        for part in range(parts):
            ref, at = (near, part) if part < mid else (far, part - mid)
            lanes = pl.ds(part * width, width)
            for group in range(near.shape[0]):
                here = pl.ds(group * near.shape[2], near.shape[2])
                one[here, lanes] = ref[group, at, :, :width]
                two[here, lanes] = ref[group, at, :, width:last_at]
                proj_parts[part, here, :] = ref[group, at, :, last_at:]
        total = jnp.zeros((width, width), F32)
        for number in range(parts):
            piece = proj_parts[numbers[PLACES + number]].astype(F32)
            kept = jnp.where(lane_numbers(piece.shape) < block, piece, 0.0)
            wide = jnp.concatenate([kept, jnp.zeros((width, width - SUB), F32)], axis=1)
            total = total + (pltpu.roll(wide, block * number, 1) if number else wide)
        proj[...] = total.astype(LOW)
        for part in range(parts):
            row = vectors[pl.ds(8 + numbers[OWNERS + part], 1), :]
            bias[0:1, part * width : (part + 1) * width] = row
        acc_one[...] = jnp.zeros(acc_one.shape, F32)
        acc_two[...] = jnp.zeros(acc_two.shape, F32)
        acc_proj[...] = jnp.zeros(acc_proj.shape, F32)
        sums[...] = jnp.zeros(sums.shape, F32)
        sums[7:8, :] = out_sums[0:1, :]

    def add_row(row, values):
        sums[pl.ds(row, 1), :] += jnp.sum(values, axis=0, keepdims=True)

    own = mixed[...]
    residual = tokens[...].astype(F32) + dot(own, proj[...], NT) + vectors[4:5, :]
    normed, rate = norm_parts(residual)
    gain = vectors[5:6, :]
    second_in = (normed * gain + vectors[6:7, :]).astype(LOW)
    out_low = cotangent[...]
    grad_out = out_low.astype(F32)
    second_turned = second_in.T
    out_turned = out_turned[...]
    totals = [residual + vectors[7:8, :], jnp.zeros(residual.shape, F32)]

    count = hidden_width // FF_CHUNK
    ones = jnp.ones((16, MLP_TILE), LOW)
    second_and_ones = jnp.concatenate([second_turned, ones], axis=0)
    hiddens, slopes, kept = {}, {}, {}

    def lanes_of(number):
        return pl.ds(number * FF_CHUNK, FF_CHUNK)

    def make_hidden(number):
        hiddens[number] = dot(second_in, one[:, lanes_of(number)])

    def make_slope(number):
        slopes[number] = dot(out_low, two[:, lanes_of(number)])

    def add_one(number):
        acc_one[:, lanes_of(number)] += dot(second_and_ones, kept[number][1])

    def add_two(number):
        acc_two[:, lanes_of(number)] += dot(out_turned, kept[number][0])

    def add_result(number):
        totals[0] = totals[0] + dot(kept[number][0], two[:, lanes_of(number)], NT)

    def add_second(number):
        totals[1] = totals[1] + dot(kept[number][1], one[:, lanes_of(number)], NT)

    make_hidden(0)
    make_slope(0)
    for number in range(count):
        between = []
        if number + 1 < count:
            between += [functools.partial(f, number + 1) for f in (make_hidden, make_slope)]
        if number > 0:
            between += [
                functools.partial(f, number - 1)
                for f in (add_result, add_second, add_one, add_two)
            ]
        kept[number] = gelu_rows(
            hiddens.pop(number), bias[0:1, lanes_of(number)], slopes.pop(number), between
        )
    for f in (add_result, add_second, add_one, add_two):
        f(count - 1)
    result, grad_second = totals
    output[...] = result.astype(LOW)
    add_row(5, grad_second * normed)
    add_row(6, grad_second)
    grad_res = grad_out + norm_back(grad_second, normed, rate, gain)
    grad_residual[...] = grad_res
    branch = grad_res.astype(LOW)
    add_row(4, branch.astype(F32))
    acc_proj[...] += dot(branch.T, own)
    grad_own = dot(branch, proj[...]).astype(LOW)
    grad_mixed[...] = grad_own
    high, rest = halves(grad_own.astype(F32) * own.astype(F32))
    head = lax.broadcasted_iota(jnp.int32, (16, width), 0)
    chosen = (lane_numbers((16, width)) // (width // HEADS) == head).astype(F32).astype(LOW)
    inner[...] = (dot(chosen, high, NT) + dot(chosen, rest, NT))[:8]

    @pl.when(step == pl.num_programs(0) - 1)
    def finish():
        total = acc_proj[...]
        for number in range(parts):
            turned = pltpu.roll(total, (width - block * number) % width, 1) if number else total
            proj_parts[numbers[PLACES + number]] = turned[:, :SUB].astype(LOW)
        for part in range(parts):
            ref, at = (grads_near, part) if part < mid else (grads_far, part - mid)
            lanes = pl.ds(part * width, width)
            for group in range(ref.shape[0]):
                here = pl.ds(group * ref.shape[2], ref.shape[2])
                ref[group, at, :, :width] = acc_one[here, lanes].astype(LOW)
                ref[group, at, :, width:last_at] = acc_two[here, lanes].astype(LOW)
                ref[group, at, :, last_at:] = proj_parts[part, here, :]
            sums[pl.ds(8 + numbers[OWNERS + part], 1), :] = acc_one[width : width + 1, lanes]


def mlp_both(numbers, near, far, vectors, mixed, tokens, cotangent, out_turned, out_sums):
    rows, width = tokens.shape
    parts = near.shape[1] + far.shape[1]
    hidden_width = parts * width
    tile = pl.BlockSpec((MLP_TILE, width), lambda s, *_: (s, 0))
    whole = lambda *dims: pl.BlockSpec(dims, lambda s, *_: (0,) * len(dims))
    return pl.pallas_call(
        mlp_kernel,
        grid_spec=pltpu.PrefetchScalarGridSpec(
            num_scalar_prefetch=1,
            grid=(rows // MLP_TILE,),
            in_specs=[
                whole(*near.shape), whole(*far.shape), whole(*vectors.shape), tile, tile, tile,
                pl.BlockSpec((width, MLP_TILE), lambda s, *_: (0, s)), whole(*out_sums.shape),
            ],
            out_specs=[
                tile,
                tile,
                tile,
                pl.BlockSpec((8, MLP_TILE), lambda s, *_: (0, s)),
                whole(*near.shape),
                whole(*far.shape),
                whole(*vectors.shape),
            ],
            scratch_shapes=[
                pltpu.VMEM((width, hidden_width), LOW),
                pltpu.VMEM((width, hidden_width), LOW),
                pltpu.VMEM((parts, width, SUB), LOW),
                pltpu.VMEM((width, width), LOW),
                pltpu.VMEM((width + 16, hidden_width), F32),
                pltpu.VMEM((width, hidden_width), F32),
                pltpu.VMEM((width, width), F32),
                pltpu.VMEM((8, hidden_width), F32),
            ],
        ),
        out_shape=[
            jax.ShapeDtypeStruct((rows, width), LOW),
            jax.ShapeDtypeStruct((rows, width), F32),
            jax.ShapeDtypeStruct((rows, width), LOW),
            jax.ShapeDtypeStruct((8, rows), F32),
            jax.ShapeDtypeStruct(near.shape, LOW),
            jax.ShapeDtypeStruct(far.shape, LOW),
            jax.ShapeDtypeStruct(vectors.shape, F32),
        ],
        compiler_params=pltpu.CompilerParams(vmem_limit_bytes=VMEM_LIMIT),
        cost_estimate=pl.CostEstimate(
            flops=34_000_000_000, bytes_accessed=20_000_000, transcendentals=6_000_000
        ),
        name="mlp_both",
    )(numbers, near, far, vectors, mixed, tokens, cotangent, out_turned, out_sums)


def attend_back_kernel(
    numbers,
    query,
    key_turned,
    value,
    probs,
    inner,
    grad_mixed,
    normed_turned,
    weight,
    vectors,
    sums,
    grad_qkv,
    near,
    far,
    grad_query,
    acc_key,
    acc_value,
    acc_sums,
    normed_sums,
    blocks,
    rows,
):
    step = pl.program_id(0)
    chunks = pl.num_programs(0) - 1
    pairs = range(PAIRS)
    count = len(pairs)
    scale = (SUB // 2) ** (-0.5)

    @pl.when(step == 0)
    def clear():
        acc_key[...] = jnp.zeros(acc_key.shape, F32)
        acc_value[...] = jnp.zeros(acc_value.shape, F32)
        normed_sums[...] = jnp.zeros(normed_sums.shape, F32)
        acc_sums[...] = jnp.zeros(acc_sums.shape, F32)

    @pl.when(step < chunks)
    def attend():
        def place(number):
            sub, at = number // count, number % count
            start = pl.multiple_of((step * (TILE // SUB) + sub) * SUB, SUB)
            return sub, at, start, pl.ds(start, SPAN), pl.ds(at * SUB, SUB)

        def slope(number):
            sub, _, _, near_rows, heads = place(number)
            grad = both_heads(grad_mixed[pl.ds(sub * SUB, SUB), heads])
            return dot(value[near_rows, heads], grad, NT)

        def soften(number, slopes):
            sub, at, _, _, _ = place(number)
            pair = pairs[at]
            cols = pl.ds(sub * SUB, SUB)
            both = []
            for head in range(2):
                lanes = slice(head * SUB, (head + 1) * SUB)
                less = slopes[:, lanes] - inner[2 * pair + head : 2 * pair + head + 1, cols]
                both.append((probs[at, sub, :, lanes].astype(F32) * less).astype(LOW))
            return jnp.concatenate(both, axis=1)

        def collect(number, scores):
            sub, at, start, near_rows, heads = place(number)
            first, second = halves_of(dot(key_turned[heads, near_rows], scores))
            turned = (jnp.concatenate([first, second], axis=0) * scale).astype(LOW)
            grad_query[pl.ds(start, SUB), heads] = turned.T
            wanted = both_heads(query[pl.ds(start + MARGIN, SUB), heads])
            acc_key[near_rows, heads] += dot(scores, wanted)
            grad = both_heads(grad_mixed[pl.ds(sub * SUB, SUB), heads])
            acc_value[near_rows, heads] += dot(probs[at, sub], grad)

        staged(TILE // SUB * count, slope, soften, collect)

    @pl.when(step > 0)
    def collect():
        here = pl.ds(pl.multiple_of((step - 1) * TILE, SUB), TILE)
        there = pl.ds(pl.multiple_of((step - 1) * TILE + MARGIN, SUB), TILE)
        parts = (
            grad_query[here, :],
            acc_key[there, :].astype(LOW),
            acc_value[there, :].astype(LOW),
        )
        joined = jnp.concatenate(parts, axis=1)
        grad_qkv[...] = joined
        normed_sums[...] += dot(normed_turned[...], joined)
        acc_sums[0:1, :] += jnp.sum(joined.astype(F32), axis=0, keepdims=True)

    @pl.when(step == chunks)
    def finish():
        weight_grad(
            numbers, normed_sums[...], acc_sums[0:1, :], weight, vectors, sums, near, far, blocks, rows
        )


def weight_grad(numbers, total, columns, weight, vectors, sums, near, far, blocks, rows):
    width = weight.shape[0]
    parts, mid = blocks.shape[0], near.shape[0]
    block = 3 * width // parts
    rows_each = 12 // parts
    wide = weight[...].astype(F32)
    grad_gain = jnp.sum(total * wide, axis=1, keepdims=True)
    grad_shift = jnp.sum(wide * columns, axis=1, keepdims=True)
    rows[...] = jnp.zeros(rows.shape, F32)
    rows[0:VEC_LANES, :] = sums[...]
    rows[2:3, :] = columns[:, :width]
    rows[3:4, :] = columns[:, 2 * width :]
    rows[VEC_LANES : 2 * VEC_LANES, :] = vectors[...]
    turned = rows[...].T
    gain = turned[:, VEC_LANES : VEC_LANES + 1]
    shift = turned[:, VEC_LANES + 1 : VEC_LANES + 2]
    lane = lane_numbers(turned.shape)
    turned = jnp.where(lane == 0, grad_gain, jnp.where(lane == 1, grad_shift, turned))
    total = total * gain + shift * columns
    at = block - 2 * SUB
    for number in range(parts):
        first, over = block * number // SUB * SUB, block * number % SUB
        piece = total[:, first : first + width + SUB]
        if over:
            missing = width + SUB - piece.shape[1]
            if missing:
                piece = jnp.concatenate([piece, jnp.zeros((width, missing), F32)], axis=1)
            piece = pltpu.roll(piece, width + SUB - over, 1)
        piece = piece[:, :width]
        vec = pltpu.roll(turned, (at - rows_each * number) % SUB, 1)
        last = jnp.where(lane < at, piece[:, 2 * SUB :], 0.0)
        last = jnp.where((lane >= at) & (lane < at + rows_each), vec, last)
        at_place = numbers[PLACES + number]
        blocks[at_place, :, : 2 * SUB] = piece[:, : 2 * SUB].astype(LOW)
        blocks[at_place, :, 2 * SUB :] = last.astype(LOW)
    near[...] = blocks[:mid]
    far[...] = blocks[mid:]


def attend_backward(
    numbers, parts, query, key_turned, value, probs, inner, grad_mixed, normed_turned, weight,
    vectors, sums,
):
    width, rows = normed_turned.shape
    padded = query.shape[0]
    chunks = rows // TILE
    tiles = TILE // SUB
    now = lambda s: jnp.minimum(s, chunks - 1)
    before = lambda s: jnp.maximum(s - 1, 0)
    whole = lambda *dims: pl.BlockSpec(dims, lambda s, *_: (0,) * len(dims))
    half = (parts // 2, width, width)
    return pl.pallas_call(
        attend_back_kernel,
        grid_spec=pltpu.PrefetchScalarGridSpec(
            num_scalar_prefetch=1,
            grid=(chunks + 1,),
            in_specs=[
                whole(padded, width),
                whole(width, padded),
                whole(padded, width),
                pl.BlockSpec((PAIRS, tiles, SPAN, 2 * SUB), lambda s, *_: (0, now(s), 0, 0)),
                pl.BlockSpec((8, TILE), lambda s, *_: (0, now(s))),
                pl.BlockSpec((TILE, width), lambda s, *_: (now(s), 0)),
                pl.BlockSpec((width, TILE), lambda s, *_: (0, before(s))),
                whole(*weight.shape),
                whole(*vectors.shape),
                whole(*sums.shape),
            ],
            out_specs=[
                pl.BlockSpec((TILE, 3 * width), lambda s, *_: (before(s), 0)),
                whole(*half),
                whole(*half),
            ],
            scratch_shapes=[
                pltpu.VMEM((rows, width), LOW),
                pltpu.VMEM((padded, width), F32),
                pltpu.VMEM((padded, width), F32),
                pltpu.VMEM((8, 3 * width), F32),
                pltpu.VMEM((width, 3 * width), F32),
                pltpu.VMEM((parts, width, width), LOW),
                pltpu.VMEM((SUB, width), F32),
            ],
        ),
        out_shape=[
            jax.ShapeDtypeStruct((rows, 3 * width), LOW),
            jax.ShapeDtypeStruct(half, LOW),
            jax.ShapeDtypeStruct(half, LOW),
        ],
        compiler_params=pltpu.CompilerParams(vmem_limit_bytes=VMEM_LIMIT),
        cost_estimate=pl.CostEstimate(
            flops=16_000_000_000, bytes_accessed=24_000_000, transcendentals=0
        ),
        name="attend_backward",
    )(
        numbers, query, key_turned, value, probs, inner, grad_mixed, normed_turned, weight, vectors,
        sums,
    )


def input_grad_kernel(weight, vectors, tokens, grad_residual, grad_qkv, input_grad):
    normed, rate = norm_parts(tokens[...].astype(F32))
    grad_first = dot(grad_qkv[...], weight[...], NT)
    back = norm_back(grad_first, normed, rate, vectors[0:1, :])
    input_grad[...] = (grad_residual[...] + back).astype(LOW)


def input_gradient(weight, vectors, tokens, grad_residual, grad_qkv):
    rows, width = tokens.shape
    size = TILE
    tile = pl.BlockSpec((size, width), lambda s: (s, 0))
    whole = lambda ref: pl.BlockSpec(ref.shape, lambda s: (0, 0))
    return pl.pallas_call(
        input_grad_kernel,
        grid=(rows // size,),
        in_specs=[
            whole(weight), whole(vectors), tile, tile,
            pl.BlockSpec((size, 3 * width), lambda s: (s, 0)),
        ],
        out_specs=tile,
        out_shape=jax.ShapeDtypeStruct((rows, width), LOW),
        compiler_params=pltpu.CompilerParams(vmem_limit_bytes=VMEM_LIMIT),
        cost_estimate=pl.CostEstimate(
            flops=4_000_000_000, bytes_accessed=13_000_000, transcendentals=2048
        ),
        name="input_gradient",
    )(weight, vectors, tokens, grad_residual, grad_qkv)


def halves(value):
    high = value.astype(LOW)
    return high, (value - high.astype(F32)).astype(LOW)


def dot_three(left, right):
    tall = jnp.concatenate([right[0], right[0], right[1]], axis=0)
    return dot(jnp.concatenate([left[0], left[1], left[0]], axis=1), tall)


def newton_rows(blocks, offset, rows, store):
    gram = dot(blocks[0], blocks[0], NT)
    for part in blocks[1:]:
        gram = gram + dot(part, part, NT)
    depth = gram.shape[0]
    down = lax.broadcasted_iota(jnp.int32, (depth, depth), 0)
    eye = (down == lane_numbers((depth, depth))).astype(F32)
    norm = 1.0 / (jnp.sqrt(jnp.sum(gram * eye, keepdims=True)) + 1e-07)
    gram = gram * (norm * norm)
    place = lax.broadcasted_iota(jnp.int32, (rows, depth), 0) + offset
    left = jnp.where(place == lane_numbers((rows, depth)), norm, 0.0)
    store[0:depth, :] = gram
    store[depth:, :] = left

    @pl.loop(0, NS_STEPS - 1)
    def advance(_):
        both = halves(store[...])
        pair = [part[:depth] for part in both]
        down = lax.broadcasted_iota(jnp.int32, (depth, depth), 0)
        eye = (down == lane_numbers((depth, depth))).astype(F32)
        square = dot_three(pair, pair)
        poly = halves(NEWTON_A * eye + NEWTON_B * store[0:depth, :] + NEWTON_C * square)
        made = dot_three(both, poly)
        store[depth:, :] = made[depth:]
        store[0:depth, :] = dot_three(halves(made[:depth]), poly)

    left = store[depth:, :]
    pair = halves(store[0:depth, :])
    once = dot_three(halves(left), pair)
    return NEWTON_A * left + NEWTON_B * once + NEWTON_C * dot_three(halves(once), pair)


def newton_store(depth, rows):
    return pltpu.VMEM((depth + tall_of(rows), depth), F32)


def stepped(left, own, height, old):
    high, rest = halves(left)
    ortho = (dot(high, own) + dot(rest, own))[: old.shape[0], : old.shape[1]]
    return old * (1.0 - MUON_RATE * MUON_DECAY) - (MUON_RATE * 0.2 * math.sqrt(height)) * ortho


def kept_lanes(value, low, high):
    lane = lane_numbers(value.shape)
    return jnp.where((lane >= low) & (lane < high), value.astype(F32), 0.0).astype(LOW)


def tall_of(rows):
    return -(-rows // 16) * 16


def muon_kernel(height, numbers, *refs):
    old, new, copy, store = refs[-4:]
    count = old.shape[1]
    blocks = [kept_lanes(ref[...], 0, count) for ref in refs[:-4]]
    left = newton_rows(blocks, numbers[OFFSET], tall_of(old.shape[0]), store)
    result = stepped(left, blocks[0], height, old[...])
    new[...] = result
    copy[...] = result.astype(LOW)


def muon(height, numbers, blocks, old):
    vmem = pl.BlockSpec(memory_space=pltpu.VMEM)

    def kernel(*refs):
        muon_kernel(height, *refs)

    return pl.pallas_call(
        kernel,
        in_specs=[pl.BlockSpec(memory_space=pltpu.SMEM)] + [vmem] * (len(blocks) + 1),
        out_specs=[vmem, vmem],
        out_shape=[
            jax.ShapeDtypeStruct(old.shape, F32),
            jax.ShapeDtypeStruct(old.shape, LOW),
        ],
        scratch_shapes=[newton_store(blocks[0].shape[0], old.shape[0])],
        compiler_params=pltpu.CompilerParams(vmem_limit_bytes=VMEM_LIMIT),
        cost_estimate=pl.CostEstimate(
            flops=9_000_000_000, bytes_accessed=2_000_000, transcendentals=10
        ),
        name="muon",
    )(numbers, *blocks, old)


def pick_kernel(count, numbers, *refs):
    pieces, columns, outs = refs[:count], refs[count], refs[count + 1 :]
    share = pieces[0].shape[0]
    for k, piece in enumerate(pieces):
        columns[k * share : (k + 1) * share, :] = piece[...]
        for n, out in enumerate(outs):
            at = pl.multiple_of(numbers[STARTS + n] * SUB, SUB)
            out[k * share : (k + 1) * share, :] = piece[:, pl.ds(at, out.shape[1])]


def pick(numbers, pieces, count):
    depth = len(pieces) * pieces[0].shape[0]
    vmem = pl.BlockSpec(memory_space=pltpu.VMEM)

    def kernel(*refs):
        pick_kernel(len(pieces), *refs)

    return pl.pallas_call(
        kernel,
        in_specs=[pl.BlockSpec(memory_space=pltpu.SMEM)] + [vmem] * len(pieces),
        out_specs=[vmem] * (count + 1),
        out_shape=[jax.ShapeDtypeStruct((depth, pieces[0].shape[1]), LOW)]
        + [jax.ShapeDtypeStruct((depth, depth), LOW)] * count,
        name="pick",
    )(numbers, *pieces)


def newton_kernel(at, numbers, *refs):
    left, store = refs[-2:]
    bounds = numbers[LOW_LANE], numbers[HIGH_LANE]
    blocks = [kept_lanes(ref[...], *bounds) for ref in refs[:-2]]
    start = numbers[OFFSET] if at is None else at
    left[...] = newton_rows(blocks, start, left.shape[0], store)


def newton(at, numbers, blocks, rows):
    vmem = pl.BlockSpec(memory_space=pltpu.VMEM)

    def kernel(*refs):
        newton_kernel(at, *refs)

    return pl.pallas_call(
        kernel,
        in_specs=[pl.BlockSpec(memory_space=pltpu.SMEM)] + [vmem] * len(blocks),
        out_specs=vmem,
        out_shape=jax.ShapeDtypeStruct((tall_of(rows), blocks[0].shape[0]), F32),
        scratch_shapes=[newton_store(blocks[0].shape[0], rows)],
        compiler_params=pltpu.CompilerParams(vmem_limit_bytes=VMEM_LIMIT),
        cost_estimate=pl.CostEstimate(
            flops=9_000_000_000, bytes_accessed=2_000_000, transcendentals=10
        ),
        name="newton",
    )(numbers, *blocks)


def finish_kernel(heights, lanes, numbers, columns, *refs):
    count = len(heights)
    store = refs[-1]
    news = refs[-1 - 2 * count : -1]
    olds = refs[-1 - 3 * count : -1 - 2 * count]
    lefts = refs[: -1 - 3 * count]
    for n, left in enumerate(lefts):
        store[n] = left[...]
    for n in range(count):
        wide = -(-olds[n].shape[1] // SUB) * SUB
        own = columns[:, lanes[n] : lanes[n] + wide]
        result = stepped(store[numbers[WHICH + n]], own, heights[n], olds[n][...])
        news[2 * n][...] = result
        news[2 * n + 1][...] = result.astype(LOW)


def finish(heights, lanes, numbers, columns, lefts, olds):
    vmem = pl.BlockSpec(memory_space=pltpu.VMEM)
    count = len(olds)

    def kernel(*refs):
        finish_kernel(heights, lanes, *refs)

    outs = pl.pallas_call(
        kernel,
        in_specs=[pl.BlockSpec(memory_space=pltpu.SMEM)] + [vmem] * (1 + len(lefts) + count),
        out_specs=[vmem] * (2 * count),
        out_shape=[
            jax.ShapeDtypeStruct(old.shape, kind) for old in olds for kind in (F32, LOW)
        ],
        scratch_shapes=[pltpu.VMEM((len(lefts), *lefts[0].shape), F32)],
        compiler_params=pltpu.CompilerParams(vmem_limit_bytes=VMEM_LIMIT),
        cost_estimate=pl.CostEstimate(
            flops=200_000_000, bytes_accessed=2_000_000, transcendentals=0
        ),
        name="finish",
    )(numbers, columns, *lefts, *olds)
    return [(outs[2 * n], outs[2 * n + 1]) for n in range(count)]


def exchange(x, axis, mask):
    size = lax.axis_size(axis)
    return lax.ppermute(x, axis, [(i, i ^ mask) for i in range(size)])


def place_masks(size):
    masks = [0]
    bit = size // 2
    while bit >= 1:
        masks = masks + [m ^ bit for m in masks]
        bit //= 2
    return masks


def from_columns(own):
    size = lax.axis_size("dp")
    sent = jnp.broadcast_to(own[None], (size, *own.shape))
    return lax.all_to_all(sent, "dp", split_axis=0, concat_axis=0, tiled=True)


def over_columns(own):
    return from_columns(own).reshape(-1, own.shape[1])


def device_numbers(dp, ns, share, width, proj_rows):
    masks = place_masks(ns)
    tasks = [(0, 0, width), (width // SUB, 0, width)]
    tasks += [(width // SUB + 1, 2 * SUB, 2 * SUB + proj_rows)] * (ns - 2)
    table = np.zeros((dp * ns, 24), np.int32)
    for device in range(dp * ns):
        column, index = device // ns, device % ns
        row = table[device]
        for n in range(ns):
            row[OWNERS + n] = index ^ masks[n]
            row[PLACES + (index ^ masks[n])] = n
            row[STARTS + n] = tasks[index ^ n][0]
        for n in range(3):
            row[WHICH + n] = index ^ n
        row[OFFSET] = column * share
        row[COLUMN] = column
        row[LOW_LANE], row[HIGH_LANE] = tasks[index][1:]
    return table


def half_rows(own):
    held = [own]
    bit = lax.axis_size("ns") // 2
    while bit > 1:
        held = held + [exchange(block, "ns", bit) for block in held]
        bit //= 2
    return held


def added(keep, got):
    return (keep.astype(F32) + got.astype(F32)).astype(LOW)


def sum_columns(pieces):
    return summed(lax.all_to_all(pieces, "dp", split_axis=0, concat_axis=0, tiled=True))


def summed(pieces):
    return jnp.sum(pieces.astype(F32), axis=0)


def columns_direct(own):
    devices = lax.axis_size("dp")
    if devices > 8 or own.shape[0] % 16:
        return [over_columns(own)], None
    return [own] + [exchange(own, "dp", mask) for mask in range(1, devices)], 0


def widened(arrays, lanes):
    joined = jnp.concatenate(arrays, axis=1)
    return jnp.pad(joined, ((0, 0), (0, lanes - joined.shape[1])))


def per_device(
    tokens,
    cotangent,
    segment,
    valid_rows,
    qkv_weight,
    proj_weight,
    fc1_weight,
    fc2_weight,
    qkv_moment,
    proj_moment,
    fc1_moment,
    fc2_moment,
    vectors,
    vector_moment,
    vector_square,
):
    rows, width = tokens.shape
    ns = lax.axis_size("ns")
    qkv_w, proj_w, fc1_w, fc2_w = (w.T for w in (qkv_weight, proj_weight, fc1_weight, fc2_weight))
    qkv_m, proj_m, fc1_m, fc2_m = (w.T for w in (qkv_moment, proj_moment, fc1_moment, fc2_moment))
    share, count = qkv_w.shape
    vec_rows = vectors.shape[0]
    first_lanes = width
    later_lanes = 2 * width + SUB

    table = device_numbers(lax.axis_size("dp"), ns, share, width, proj_w.shape[1])
    device = lax.axis_index("dp") * ns + lax.axis_index("ns")
    numbers = lax.dynamic_slice(jnp.asarray(table), (device, 0), (1, table.shape[1]))[0]

    row_ids = jnp.where(
        valid_rows > 0, segment, rows + jnp.arange(rows, dtype=jnp.int32)
    ).astype(F32)
    ids = jnp.pad(row_ids, (MARGIN, MARGIN), constant_values=-1.0).reshape(-1, SUB)
    ids = jnp.pad(ids, ((0, -ids.shape[0] % 8), (0, 0)), constant_values=-1.0)

    later_own = widened([fc1_w, fc2_w, proj_w], later_lanes).astype(LOW)
    later_own, numbers = lax.optimization_barrier((later_own, numbers))
    later_pair = jnp.stack([later_own, exchange(later_own, "ns", ns // 2)])
    first_own = widened([qkv_w, vectors.T], first_lanes).astype(LOW)
    prepared = prepare(tokens, cotangent, ids)
    first_pieces = half_rows(over_columns(first_own))
    first_pieces, prepared = lax.optimization_barrier((first_pieces, prepared))
    normed, normed_turned, out_turned, columns, out_sums = prepared
    first_pieces = first_pieces + [exchange(piece, "ns", 1) for piece in first_pieces]
    later_near = from_columns(later_pair)
    if share % 16:
        later_near = jnp.moveaxis(later_near, 0, 1).reshape(1, ns // 2, width, later_lanes)

    query, _, value, key_turned, mixed, probs, weight, vector_full = attend_forward(
        numbers, first_pieces, normed, ids, columns
    )
    later_near, mixed = lax.optimization_barrier((later_near, mixed))
    later_far = exchange(later_near, "ns", 1)
    output, grad_residual, grad_mixed, inner, grads_near, grads_far, sums = mlp_both(
        numbers, later_near, later_far, vector_full, mixed, tokens, cotangent, out_turned, out_sums
    )
    held = added(grads_near, exchange(grads_far, "ns", 1))
    held, grad_mixed = lax.optimization_barrier((held, grad_mixed))
    if share % 16:
        held = jnp.moveaxis(held.reshape(ns // 2, -1, share, later_lanes), 1, 0)
    later_got = lax.all_to_all(held, "dp", split_axis=0, concat_axis=0, tiled=True)

    grad_qkv, grads_near, grads_far = attend_backward(
        numbers, ns, query, key_turned, value, probs, inner, grad_mixed, normed_turned, weight,
        vector_full, sums,
    )
    held = added(grads_near, exchange(grads_far, "ns", 1))
    got = exchange(held[1], "ns", ns // 2)
    input_grad = input_gradient(weight, vector_full, tokens, grad_residual, grad_qkv)
    got, input_grad, later_got = lax.optimization_barrier((got, input_grad, later_got))
    first_held = added(held[0], got).reshape(lax.axis_size("dp"), share, first_lanes)
    first_got = lax.all_to_all(first_held, "dp", split_axis=0, concat_axis=0, tiled=True)
    later_sums = summed(later_got)
    later_owned = later_sums[0] + exchange(later_sums[1].astype(LOW), "ns", ns // 2).astype(F32)
    later_moment = later_owned + 0.5 * widened([fc1_m, fc2_m, proj_m], later_lanes)
    pieces, at = columns_direct(later_moment.astype(LOW))
    columns, *chosen = pick(numbers, pieces, ns)
    first_got, chosen = lax.optimization_barrier((first_got, chosen))
    blocks = [chosen[0]] + [exchange(chosen[mask], "ns", mask) for mask in range(1, ns)]

    first_owned = summed(first_got)
    first_moment = first_owned + 0.5 * widened([qkv_m], first_lanes)
    first_pieces = half_rows(over_columns(first_moment.astype(LOW)))
    moments_new = (
        first_moment[:, :count],
        later_moment[:, 2 * width : 2 * width + proj_w.shape[1]],
        later_moment[:, :width],
        later_moment[:, width : 2 * width],
    )

    vector_grad = first_owned[:, count : count + vec_rows].T
    first_new = BETA_ONE * vector_moment + (1.0 - BETA_ONE) * vector_grad
    second_new = BETA_TWO * vector_square + (1.0 - BETA_TWO) * vector_grad * vector_grad
    first_hat = first_new / (1.0 - BETA_ONE**STEP)
    second_hat = second_new / (1.0 - BETA_TWO**STEP)
    vectors_new = vectors - ADAM_RATE * first_hat / (jnp.sqrt(second_hat) + ADAM_EPS)
    small = (*(m.T for m in moments_new), first_new, second_new, vectors_new)
    blocks, small = lax.optimization_barrier((blocks, small))
    left = newton(at, numbers, blocks, share)
    left, first_pieces = lax.optimization_barrier((left, first_pieces))
    first_pieces = first_pieces + [exchange(piece, "ns", 1) for piece in first_pieces]
    qkv_new = muon(count * ns, numbers, first_pieces, qkv_w)
    lefts = [left] + [exchange(left, "ns", mask) for mask in range(1, ns)]
    lefts, qkv_new = lax.optimization_barrier((lefts, qkv_new))
    fc1_new, fc2_new, proj_new = finish(
        [w.shape[1] * ns for w in (fc1_w, fc2_w, proj_w)],
        (0, width, 2 * width),
        numbers,
        columns,
        lefts,
        (fc1_w, fc2_w, proj_w),
    )

    news = (qkv_new, proj_new, fc1_new, fc2_new)
    return (
        output,
        input_grad,
        *(new[0].T for new in news),
        *small,
        *(new[1].T for new in news),
    )


def solution(mesh):
    rows = P(("dp", "ns"), None)
    flat = P(("dp", "ns"))
    block = P("ns", "dp")
    return jax.shard_map(
        per_device,
        mesh=mesh,
        in_specs=(rows, rows, flat, flat) + (block,) * 11,
        out_specs=(rows, rows) + (block,) * 15,
        check_vma=False,
    )
```

```python
import functools
import math

import jax
import jax.numpy as jnp
import numpy as np
from jax import lax
from jax.experimental import pallas as pl
from jax.experimental.pallas import tpu as pltpu
from jax.sharding import PartitionSpec as P

HEADS = 6
PAIRS = 3
MARGIN = 128
NS_STEPS = 5
STEP = 10
TILE = 512
MLP_TILE = 512
FF_CHUNK = 256
SUB = 128
SPAN = 384
VEC_LANES = 16
GROUP = 2


EPS_NORM = 1e-06
NEWTON_A = 3.4445
NEWTON_B = -4.775
NEWTON_C = 2.0315
MUON_RATE = 0.2
MUON_DECAY = 0.1
ADAM_RATE = 0.4
BETA_ONE = 0.9
BETA_TWO = 0.999
ADAM_EPS = 1e-08
LOW = jnp.bfloat16
F32 = jnp.float32
TN = (((0,), (0,)), ((), ()))
NT = (((1,), (1,)), ((), ()))
NN = (((1,), (0,)), ((), ()))
VMEM_LIMIT = 56 * 1024 * 1024
ERF_P = 0.3275911
ERF_COEFS = (0.254829592, -0.284496736, 1.421413741, -1.453152027, 1.061405429)


def dot(left, right, dims=NN):
    return lax.dot_general(left, right, dims, preferred_element_type=F32)


PLACES, OWNERS, STARTS, WHICH, OFFSET, LOW_LANE, HIGH_LANE, COLUMN = 0, 4, 8, 12, 16, 17, 18, 19


def lane_numbers(shape):
    return lax.broadcasted_iota(jnp.int32, shape, len(shape) - 1)


def norm_parts(value):
    center = value - jnp.mean(value, axis=-1, keepdims=True)
    rate = lax.rsqrt(jnp.mean(center * center, axis=-1, keepdims=True) + EPS_NORM)
    return center * rate, rate


def norm_back(grad, normed, rate, gain):
    scaled = grad * gain
    first = jnp.mean(scaled, axis=-1, keepdims=True)
    second = jnp.mean(scaled * normed, axis=-1, keepdims=True)
    return rate * (scaled - first - normed * second)


def gelu_both(value):
    below = 1.0 + (ERF_P * 0.5**0.5) * jnp.abs(value)
    ratio = pl.reciprocal(below, approx=True)
    ratio = ratio * (2.0 - below * ratio)
    decay = jnp.exp2((value * value) * (-0.5 * math.log2(math.e)))
    poly = 0.5 * ERF_COEFS[4]
    for coef in ERF_COEFS[3::-1]:
        poly = poly * ratio + 0.5 * coef
    tail = poly * ratio * decay
    phi = jnp.where(value >= 0, 1.0 - tail, tail)
    return value * phi, phi + (value * (1.0 / math.sqrt(2.0 * math.pi))) * decay


def gelu_rows(hidden, bias, grad, between):
    active, back = [], []
    rows = hidden.shape[0]
    pieces = rows // 16
    for n in range(pieces):
        if n * len(between) // pieces != (n - 1) * len(between) // pieces:
            between[n * len(between) // pieces]()
        here = slice(n * 16, (n + 1) * 16)
        value, slope = gelu_both(hidden[here] + bias)
        active.append(value.astype(LOW))
        back.append((grad[here] * slope).astype(LOW))
    return jnp.concatenate(active, axis=0), jnp.concatenate(back, axis=0)


def halves_of(lanes):
    half = lanes.shape[0] // 2
    return lanes[:half, :SUB], lanes[half:, SUB:]


def staged(count, first, second, third):
    made = first(0)
    kept = None
    for n in range(count):
        coming = first(n + 1) if n + 1 < count else None
        if kept is not None:
            third(n - 1, kept)
        kept = second(n, made)
        made = coming
    third(count - 1, kept)


def both_heads(pair):
    first = (lane_numbers((1, SUB)) < SUB // 2).astype(F32).astype(pair.dtype)
    second = (lane_numbers((1, SUB)) >= SUB // 2).astype(F32).astype(pair.dtype)
    return jnp.concatenate([pair * first, pair * second], axis=0)


def fetch(pairs, sems):
    copies = [
        pltpu.make_async_copy(source, target, sems.at[n])
        for n, (source, target) in enumerate(pairs)
    ]
    for copy in copies:
        copy.start()
    for copy in copies:
        copy.wait()


def prepare_kernel(tokens, cotangent, ids, normed, normed_turned, out_turned, columns, sums):
    step = pl.program_id(0)
    parts = columns.shape[0] // SUB

    @pl.when(step == 0)
    def clear():
        sums[...] = jnp.zeros(sums.shape, F32)
        for number in range(parts):
            row = jnp.broadcast_to(ids[number : number + 1, :], (SUB, SUB))
            columns[number * SUB : (number + 1) * SUB, :] = row.T

    value, _ = norm_parts(tokens[...].astype(F32))
    normed[...] = value
    normed_turned[...] = value.astype(LOW).T
    out_low = cotangent[...]
    out_turned[...] = out_low.T
    sums[0:1, :] += jnp.sum(out_low.astype(F32), axis=0, keepdims=True)


def prepare(tokens, cotangent, ids):
    rows, width = tokens.shape
    padded = rows + 2 * MARGIN
    tile = pl.BlockSpec((TILE, width), lambda s: (s, 0))
    turned = pl.BlockSpec((width, TILE), lambda s: (0, s))
    whole = lambda *dims: pl.BlockSpec(dims, lambda s: (0,) * len(dims))
    return pl.pallas_call(
        prepare_kernel,
        grid=(rows // TILE,),
        in_specs=[tile, tile, whole(*ids.shape)],
        out_specs=[tile, turned, turned, whole(padded, SUB), whole(8, width)],
        out_shape=[
            jax.ShapeDtypeStruct((rows, width), F32),
            jax.ShapeDtypeStruct((width, rows), LOW),
            jax.ShapeDtypeStruct((width, rows), LOW),
            jax.ShapeDtypeStruct((padded, SUB), F32),
            jax.ShapeDtypeStruct((8, width), F32),
        ],
        compiler_params=pltpu.CompilerParams(vmem_limit_bytes=VMEM_LIMIT),
        cost_estimate=pl.CostEstimate(
            flops=20_000_000, bytes_accessed=12_000_000, transcendentals=2048
        ),
        name="prepare",
    )(tokens, cotangent, ids)


def attend_kernel(numbers, *refs):
    (normed, ids, columns, query, key, value, key_turned, mixed, probs, weight, vectors,
     gathered, pair_weight, value_turned, shifts, sems) = refs[-16:]
    pieces = refs[:-16]
    step = pl.program_id(0)
    chunks = pl.num_programs(0) - 1
    width = normed.shape[1]
    parts = len(pieces)
    block = 3 * width // parts
    rows_each = 12 // parts

    @pl.when(step == 0)
    def assemble():
        fetch([(piece, gathered.at[n]) for n, piece in enumerate(pieces)], sems)
        tiles = [jnp.zeros((width, SUB), F32)] * (3 * width // SUB + 1)
        turned = jnp.zeros((width, SUB), F32)
        for number in range(parts):
            piece = gathered[numbers[PLACES + number]].astype(F32)
            kept = jnp.where(lane_numbers(piece.shape) < block, piece, 0.0)
            wide = jnp.concatenate([kept, jnp.zeros((width, SUB), F32)], axis=1)
            over = block * number % SUB
            wide = pltpu.roll(wide, over, 1) if over else wide
            for n in range(wide.shape[1] // SUB):
                at = block * number // SUB + n
                if at < len(tiles):
                    tiles[at] = tiles[at] + wide[:, n * SUB : (n + 1) * SUB]
            last = piece[:, 2 * SUB :]
            at = block - 2 * SUB
            lane = lane_numbers(last.shape)
            vec = jnp.where((lane >= at) & (lane < at + rows_each), last, 0.0)
            turned = turned + pltpu.roll(vec, (rows_each * number - at) % SUB, 1)
        total = jnp.concatenate(tiles[:-1], axis=1).astype(LOW)
        weight[...] = total
        pair_weight[...] = total[:, width:].T
        vectors[...] = turned.T[:VEC_LANES]
        shifts[...] = turned
        edges = (pl.ds(0, MARGIN), pl.ds(MARGIN + chunks * TILE, MARGIN))
        for edge in edges:
            for ref in (query, key, value):
                ref[edge, :] = jnp.zeros((MARGIN, width), LOW)
            for ref in (key_turned, value_turned):
                ref[:, edge] = jnp.zeros((width, MARGIN), LOW)

    @pl.when(step < chunks)
    def project():
        first_in = (normed[...] * vectors[0:1, :] + vectors[1:2, :]).astype(LOW)
        result = dot(first_in, weight[...])
        turned = dot(pair_weight[...], first_in, NT)
        here = pl.ds(pl.multiple_of(MARGIN + step * TILE, SUB), TILE)
        scale = (width // HEADS) ** (-0.5)
        made = (result[:, :width] + vectors[2:3, :]).astype(LOW) * jnp.asarray(scale, LOW)
        query[here, :] = made
        key[here, :] = result[:, width : 2 * width].astype(LOW)
        value[here, :] = (result[:, 2 * width :] + vectors[3:4, :]).astype(LOW)
        key_turned[:, here] = turned[:width].astype(LOW)
        value_turned[:, here] = (turned[width:] + shifts[:, 3:4]).astype(LOW)

    @pl.when(step > 0)
    def attend():
        def place(number):
            sub, pair = number // PAIRS, number % PAIRS
            tile = (step - 1) * (TILE // SUB) + sub
            start = pl.multiple_of(tile * SUB, SUB)
            return sub, pair, tile, start, pl.ds(start, SPAN), pl.ds(pair * SUB, SUB)

        def of_group(group):
            return range(group * GROUP, (group + 1) * GROUP)

        def score(group):
            made = []
            for number in of_group(group):
                _, _, _, start, near_rows, heads = place(number)
                wanted = both_heads(query[pl.ds(start + MARGIN, SUB), heads])
                made.append(dot(key[near_rows, heads], wanted, NT))
            return made

        def soften(group, made):
            own = []
            for number, scores in zip(of_group(group), made):
                _, _, tile, _, near_rows, _ = place(number)
                same = columns[near_rows, :] == ids[pl.ds(tile + 1, 1), :]
                own += [
                    jnp.where(same, scores[:, head * SUB : (head + 1) * SUB], -1e30)
                    for head in range(2)
                ]
            largest = [jnp.max(part, axis=0, keepdims=True) for part in own]
            expo = [jnp.exp(part - most) for part, most in zip(own, largest)]
            share = [1.0 / jnp.sum(part, axis=0, keepdims=True) for part in expo]
            scaled = [(part * by).astype(LOW) for part, by in zip(expo, share)]
            result = []
            for n, number in enumerate(of_group(group)):
                sub, pair, _, _, _, _ = place(number)
                result.append(jnp.concatenate(scaled[2 * n : 2 * n + 2], axis=1))
                probs[pair, sub] = result[-1]
            return result

        def mix(group, kept):
            for number, prob in zip(of_group(group), kept):
                sub, _, _, _, near_rows, heads = place(number)
                first, second = halves_of(dot(value_turned[heads, near_rows], prob))
                turned = jnp.concatenate([first, second], axis=0).astype(LOW)
                mixed[pl.ds(sub * SUB, SUB), heads] = turned.T

        staged(TILE // SUB * PAIRS // GROUP, score, soften, mix)


def attend_forward(numbers, pieces, normed, ids, columns):
    rows, width = normed.shape
    chunks = rows // TILE
    tiles = TILE // SUB
    parts = len(pieces)
    now = lambda s: jnp.minimum(s, chunks - 1)
    before = lambda s: jnp.maximum(s - 1, 0)
    whole = lambda *dims: pl.BlockSpec(dims, lambda s, *_: (0,) * len(dims))
    padded = rows + 2 * MARGIN
    return pl.pallas_call(
        attend_kernel,
        grid_spec=pltpu.PrefetchScalarGridSpec(
            num_scalar_prefetch=1,
            grid=(chunks + 1,),
            in_specs=[pl.BlockSpec(memory_space=pl.ANY)] * parts
            + [
                pl.BlockSpec((TILE, width), lambda s, *_: (now(s), 0)),
                whole(*ids.shape),
                whole(*columns.shape),
            ],
            out_specs=[
                whole(padded, width),
                whole(padded, width),
                whole(padded, width),
                whole(width, padded),
                pl.BlockSpec((TILE, width), lambda s, *_: (before(s), 0)),
                pl.BlockSpec((PAIRS, tiles, SPAN, 2 * SUB), lambda s, *_: (0, before(s), 0, 0)),
                whole(width, 3 * width),
                whole(VEC_LANES, width),
            ],
            scratch_shapes=[
                pltpu.VMEM((parts, *pieces[0].shape), LOW),
                pltpu.VMEM((2 * width, width), LOW),
                pltpu.VMEM((width, padded), LOW),
                pltpu.VMEM((width, SUB), F32),
                pltpu.SemaphoreType.DMA((parts,)),
            ],
        ),
        out_shape=[
            jax.ShapeDtypeStruct((padded, width), LOW),
            jax.ShapeDtypeStruct((padded, width), LOW),
            jax.ShapeDtypeStruct((padded, width), LOW),
            jax.ShapeDtypeStruct((width, padded), LOW),
            jax.ShapeDtypeStruct((rows, width), LOW),
            jax.ShapeDtypeStruct((PAIRS, rows // SUB, SPAN, 2 * SUB), LOW),
            jax.ShapeDtypeStruct((width, 3 * width), LOW),
            jax.ShapeDtypeStruct((VEC_LANES, width), F32),
        ],
        compiler_params=pltpu.CompilerParams(vmem_limit_bytes=VMEM_LIMIT),
        cost_estimate=pl.CostEstimate(
            flops=12_000_000_000, bytes_accessed=22_000_000, transcendentals=5_000_000
        ),
        name="attend_forward",
    )(numbers, *pieces, normed, ids, columns)


def mlp_kernel(numbers, near, far, *refs):
    (vectors, mixed, tokens, cotangent, out_turned, out_sums, output, grad_residual, grad_mixed, inner, grads_near,
     grads_far, sums, one, two, proj_parts, proj, acc_one, acc_two, acc_proj, bias
    ) = refs
    step = pl.program_id(0)
    width = tokens.shape[1]
    mid = near.shape[1]
    parts = mid + far.shape[1]
    block = width // parts
    last_at = 2 * width
    hidden_width = one.shape[1]

    @pl.when(step == 0)
    def assemble():
        for part in range(parts):
            ref, at = (near, part) if part < mid else (far, part - mid)
            lanes = pl.ds(part * width, width)
            for group in range(near.shape[0]):
                here = pl.ds(group * near.shape[2], near.shape[2])
                one[here, lanes] = ref[group, at, :, :width]
                two[here, lanes] = ref[group, at, :, width:last_at]
                proj_parts[part, here, :] = ref[group, at, :, last_at:]
        total = jnp.zeros((width, width), F32)
        for number in range(parts):
            piece = proj_parts[numbers[PLACES + number]].astype(F32)
            kept = jnp.where(lane_numbers(piece.shape) < block, piece, 0.0)
            wide = jnp.concatenate([kept, jnp.zeros((width, width - SUB), F32)], axis=1)
            total = total + (pltpu.roll(wide, block * number, 1) if number else wide)
        proj[...] = total.astype(LOW)
        for part in range(parts):
            row = vectors[pl.ds(8 + numbers[OWNERS + part], 1), :]
            bias[0:1, part * width : (part + 1) * width] = row
        acc_one[...] = jnp.zeros(acc_one.shape, F32)
        acc_two[...] = jnp.zeros(acc_two.shape, F32)
        acc_proj[...] = jnp.zeros(acc_proj.shape, F32)
        sums[...] = jnp.zeros(sums.shape, F32)
        sums[7:8, :] = out_sums[0:1, :]

    def add_row(row, values):
        sums[pl.ds(row, 1), :] += jnp.sum(values, axis=0, keepdims=True)

    own = mixed[...]
    residual = tokens[...].astype(F32) + dot(own, proj[...], NT) + vectors[4:5, :]
    normed, rate = norm_parts(residual)
    gain = vectors[5:6, :]
    second_in = (normed * gain + vectors[6:7, :]).astype(LOW)
    out_low = cotangent[...]
    grad_out = out_low.astype(F32)
    second_turned = second_in.T
    out_turned = out_turned[...]
    totals = [residual + vectors[7:8, :], jnp.zeros(residual.shape, F32)]

    count = hidden_width // FF_CHUNK
    ones = jnp.ones((16, MLP_TILE), LOW)
    second_and_ones = jnp.concatenate([second_turned, ones], axis=0)
    hiddens, slopes, kept = {}, {}, {}

    def lanes_of(number):
        return pl.ds(number * FF_CHUNK, FF_CHUNK)

    def make_hidden(number):
        hiddens[number] = dot(second_in, one[:, lanes_of(number)])

    def make_slope(number):
        slopes[number] = dot(out_low, two[:, lanes_of(number)])

    def add_one(number):
        acc_one[:, lanes_of(number)] += dot(second_and_ones, kept[number][1])

    def add_two(number):
        acc_two[:, lanes_of(number)] += dot(out_turned, kept[number][0])

    def add_result(number):
        totals[0] = totals[0] + dot(kept[number][0], two[:, lanes_of(number)], NT)

    def add_second(number):
        totals[1] = totals[1] + dot(kept[number][1], one[:, lanes_of(number)], NT)

    make_hidden(0)
    make_slope(0)
    for number in range(count):
        between = []
        if number + 1 < count:
            between += [functools.partial(f, number + 1) for f in (make_hidden, make_slope)]
        if number > 0:
            between += [
                functools.partial(f, number - 1)
                for f in (add_result, add_second, add_one, add_two)
            ]
        kept[number] = gelu_rows(
            hiddens.pop(number), bias[0:1, lanes_of(number)], slopes.pop(number), between
        )
    for f in (add_result, add_second, add_one, add_two):
        f(count - 1)
    result, grad_second = totals
    output[...] = result.astype(LOW)
    add_row(5, grad_second * normed)
    add_row(6, grad_second)
    grad_res = grad_out + norm_back(grad_second, normed, rate, gain)
    grad_residual[...] = grad_res
    branch = grad_res.astype(LOW)
    add_row(4, branch.astype(F32))
    acc_proj[...] += dot(branch.T, own)
    grad_own = dot(branch, proj[...]).astype(LOW)
    grad_mixed[...] = grad_own
    high, rest = halves(grad_own.astype(F32) * own.astype(F32))
    head = lax.broadcasted_iota(jnp.int32, (16, width), 0)
    chosen = (lane_numbers((16, width)) // (width // HEADS) == head).astype(F32).astype(LOW)
    inner[...] = (dot(chosen, high, NT) + dot(chosen, rest, NT))[:8]

    @pl.when(step == pl.num_programs(0) - 1)
    def finish():
        total = acc_proj[...]
        for number in range(parts):
            turned = pltpu.roll(total, (width - block * number) % width, 1) if number else total
            proj_parts[numbers[PLACES + number]] = turned[:, :SUB].astype(LOW)
        for part in range(parts):
            ref, at = (grads_near, part) if part < mid else (grads_far, part - mid)
            lanes = pl.ds(part * width, width)
            for group in range(ref.shape[0]):
                here = pl.ds(group * ref.shape[2], ref.shape[2])
                ref[group, at, :, :width] = acc_one[here, lanes].astype(LOW)
                ref[group, at, :, width:last_at] = acc_two[here, lanes].astype(LOW)
                ref[group, at, :, last_at:] = proj_parts[part, here, :]
            sums[pl.ds(8 + numbers[OWNERS + part], 1), :] = acc_one[width : width + 1, lanes]


def mlp_both(numbers, near, far, vectors, mixed, tokens, cotangent, out_turned, out_sums):
    rows, width = tokens.shape
    parts = near.shape[1] + far.shape[1]
    hidden_width = parts * width
    tile = pl.BlockSpec((MLP_TILE, width), lambda s, *_: (s, 0))
    whole = lambda *dims: pl.BlockSpec(dims, lambda s, *_: (0,) * len(dims))
    return pl.pallas_call(
        mlp_kernel,
        grid_spec=pltpu.PrefetchScalarGridSpec(
            num_scalar_prefetch=1,
            grid=(rows // MLP_TILE,),
            in_specs=[
                whole(*near.shape), whole(*far.shape), whole(*vectors.shape), tile, tile, tile,
                pl.BlockSpec((width, MLP_TILE), lambda s, *_: (0, s)), whole(*out_sums.shape),
            ],
            out_specs=[
                tile,
                tile,
                tile,
                pl.BlockSpec((8, MLP_TILE), lambda s, *_: (0, s)),
                whole(*near.shape),
                whole(*far.shape),
                whole(*vectors.shape),
            ],
            scratch_shapes=[
                pltpu.VMEM((width, hidden_width), LOW),
                pltpu.VMEM((width, hidden_width), LOW),
                pltpu.VMEM((parts, width, SUB), LOW),
                pltpu.VMEM((width, width), LOW),
                pltpu.VMEM((width + 16, hidden_width), F32),
                pltpu.VMEM((width, hidden_width), F32),
                pltpu.VMEM((width, width), F32),
                pltpu.VMEM((8, hidden_width), F32),
            ],
        ),
        out_shape=[
            jax.ShapeDtypeStruct((rows, width), LOW),
            jax.ShapeDtypeStruct((rows, width), F32),
            jax.ShapeDtypeStruct((rows, width), LOW),
            jax.ShapeDtypeStruct((8, rows), F32),
            jax.ShapeDtypeStruct(near.shape, LOW),
            jax.ShapeDtypeStruct(far.shape, LOW),
            jax.ShapeDtypeStruct(vectors.shape, F32),
        ],
        compiler_params=pltpu.CompilerParams(vmem_limit_bytes=VMEM_LIMIT),
        cost_estimate=pl.CostEstimate(
            flops=34_000_000_000, bytes_accessed=20_000_000, transcendentals=6_000_000
        ),
        name="mlp_both",
    )(numbers, near, far, vectors, mixed, tokens, cotangent, out_turned, out_sums)


def attend_back_kernel(
    numbers,
    query,
    key_turned,
    value,
    probs,
    inner,
    grad_mixed,
    normed_turned,
    weight,
    vectors,
    sums,
    grad_qkv,
    near,
    far,
    grad_query,
    acc_key,
    acc_value,
    acc_sums,
    normed_sums,
    blocks,
    rows,
):
    step = pl.program_id(0)
    chunks = pl.num_programs(0) - 1
    pairs = range(PAIRS)
    count = len(pairs)
    scale = (SUB // 2) ** (-0.5)

    @pl.when(step == 0)
    def clear():
        acc_key[...] = jnp.zeros(acc_key.shape, F32)
        acc_value[...] = jnp.zeros(acc_value.shape, F32)
        normed_sums[...] = jnp.zeros(normed_sums.shape, F32)
        acc_sums[...] = jnp.zeros(acc_sums.shape, F32)

    @pl.when(step < chunks)
    def attend():
        def place(number):
            sub, at = number // count, number % count
            start = pl.multiple_of((step * (TILE // SUB) + sub) * SUB, SUB)
            return sub, at, start, pl.ds(start, SPAN), pl.ds(at * SUB, SUB)

        def slope(number):
            sub, _, _, near_rows, heads = place(number)
            grad = both_heads(grad_mixed[pl.ds(sub * SUB, SUB), heads])
            return dot(value[near_rows, heads], grad, NT)

        def soften(number, slopes):
            sub, at, _, _, _ = place(number)
            pair = pairs[at]
            cols = pl.ds(sub * SUB, SUB)
            both = []
            for head in range(2):
                lanes = slice(head * SUB, (head + 1) * SUB)
                less = slopes[:, lanes] - inner[2 * pair + head : 2 * pair + head + 1, cols]
                both.append((probs[at, sub, :, lanes].astype(F32) * less).astype(LOW))
            return jnp.concatenate(both, axis=1)

        def collect(number, scores):
            sub, at, start, near_rows, heads = place(number)
            first, second = halves_of(dot(key_turned[heads, near_rows], scores))
            turned = (jnp.concatenate([first, second], axis=0) * scale).astype(LOW)
            grad_query[pl.ds(start, SUB), heads] = turned.T
            wanted = both_heads(query[pl.ds(start + MARGIN, SUB), heads])
            acc_key[near_rows, heads] += dot(scores, wanted)
            grad = both_heads(grad_mixed[pl.ds(sub * SUB, SUB), heads])
            acc_value[near_rows, heads] += dot(probs[at, sub], grad)

        staged(TILE // SUB * count, slope, soften, collect)

    @pl.when(step > 0)
    def collect():
        here = pl.ds(pl.multiple_of((step - 1) * TILE, SUB), TILE)
        there = pl.ds(pl.multiple_of((step - 1) * TILE + MARGIN, SUB), TILE)
        parts = (
            grad_query[here, :],
            acc_key[there, :].astype(LOW),
            acc_value[there, :].astype(LOW),
        )
        joined = jnp.concatenate(parts, axis=1)
        grad_qkv[...] = joined
        normed_sums[...] += dot(normed_turned[...], joined)
        acc_sums[0:1, :] += jnp.sum(joined.astype(F32), axis=0, keepdims=True)

    @pl.when(step == chunks)
    def finish():
        weight_grad(
            numbers, normed_sums[...], acc_sums[0:1, :], weight, vectors, sums, near, far, blocks, rows
        )


def weight_grad(numbers, total, columns, weight, vectors, sums, near, far, blocks, rows):
    width = weight.shape[0]
    parts, mid = blocks.shape[0], near.shape[0]
    block = 3 * width // parts
    rows_each = 12 // parts
    wide = weight[...].astype(F32)
    grad_gain = jnp.sum(total * wide, axis=1, keepdims=True)
    grad_shift = jnp.sum(wide * columns, axis=1, keepdims=True)
    rows[...] = jnp.zeros(rows.shape, F32)
    rows[0:VEC_LANES, :] = sums[...]
    rows[2:3, :] = columns[:, :width]
    rows[3:4, :] = columns[:, 2 * width :]
    rows[VEC_LANES : 2 * VEC_LANES, :] = vectors[...]
    turned = rows[...].T
    gain = turned[:, VEC_LANES : VEC_LANES + 1]
    shift = turned[:, VEC_LANES + 1 : VEC_LANES + 2]
    lane = lane_numbers(turned.shape)
    turned = jnp.where(lane == 0, grad_gain, jnp.where(lane == 1, grad_shift, turned))
    total = total * gain + shift * columns
    at = block - 2 * SUB
    for number in range(parts):
        first, over = block * number // SUB * SUB, block * number % SUB
        piece = total[:, first : first + width + SUB]
        if over:
            missing = width + SUB - piece.shape[1]
            if missing:
                piece = jnp.concatenate([piece, jnp.zeros((width, missing), F32)], axis=1)
            piece = pltpu.roll(piece, width + SUB - over, 1)
        piece = piece[:, :width]
        vec = pltpu.roll(turned, (at - rows_each * number) % SUB, 1)
        last = jnp.where(lane < at, piece[:, 2 * SUB :], 0.0)
        last = jnp.where((lane >= at) & (lane < at + rows_each), vec, last)
        at_place = numbers[PLACES + number]
        blocks[at_place, :, : 2 * SUB] = piece[:, : 2 * SUB].astype(LOW)
        blocks[at_place, :, 2 * SUB :] = last.astype(LOW)
    near[...] = blocks[:mid]
    far[...] = blocks[mid:]


def attend_backward(
    numbers, parts, query, key_turned, value, probs, inner, grad_mixed, normed_turned, weight,
    vectors, sums,
):
    width, rows = normed_turned.shape
    padded = query.shape[0]
    chunks = rows // TILE
    tiles = TILE // SUB
    now = lambda s: jnp.minimum(s, chunks - 1)
    before = lambda s: jnp.maximum(s - 1, 0)
    whole = lambda *dims: pl.BlockSpec(dims, lambda s, *_: (0,) * len(dims))
    half = (parts // 2, width, width)
    return pl.pallas_call(
        attend_back_kernel,
        grid_spec=pltpu.PrefetchScalarGridSpec(
            num_scalar_prefetch=1,
            grid=(chunks + 1,),
            in_specs=[
                whole(padded, width),
                whole(width, padded),
                whole(padded, width),
                pl.BlockSpec((PAIRS, tiles, SPAN, 2 * SUB), lambda s, *_: (0, now(s), 0, 0)),
                pl.BlockSpec((8, TILE), lambda s, *_: (0, now(s))),
                pl.BlockSpec((TILE, width), lambda s, *_: (now(s), 0)),
                pl.BlockSpec((width, TILE), lambda s, *_: (0, before(s))),
                whole(*weight.shape),
                whole(*vectors.shape),
                whole(*sums.shape),
            ],
            out_specs=[
                pl.BlockSpec((TILE, 3 * width), lambda s, *_: (before(s), 0)),
                whole(*half),
                whole(*half),
            ],
            scratch_shapes=[
                pltpu.VMEM((rows, width), LOW),
                pltpu.VMEM((padded, width), F32),
                pltpu.VMEM((padded, width), F32),
                pltpu.VMEM((8, 3 * width), F32),
                pltpu.VMEM((width, 3 * width), F32),
                pltpu.VMEM((parts, width, width), LOW),
                pltpu.VMEM((SUB, width), F32),
            ],
        ),
        out_shape=[
            jax.ShapeDtypeStruct((rows, 3 * width), LOW),
            jax.ShapeDtypeStruct(half, LOW),
            jax.ShapeDtypeStruct(half, LOW),
        ],
        compiler_params=pltpu.CompilerParams(vmem_limit_bytes=VMEM_LIMIT),
        cost_estimate=pl.CostEstimate(
            flops=16_000_000_000, bytes_accessed=24_000_000, transcendentals=0
        ),
        name="attend_backward",
    )(
        numbers, query, key_turned, value, probs, inner, grad_mixed, normed_turned, weight, vectors,
        sums,
    )


def input_grad_kernel(weight, vectors, tokens, grad_residual, grad_qkv, input_grad):
    normed, rate = norm_parts(tokens[...].astype(F32))
    grad_first = dot(grad_qkv[...], weight[...], NT)
    back = norm_back(grad_first, normed, rate, vectors[0:1, :])
    input_grad[...] = (grad_residual[...] + back).astype(LOW)


def input_gradient(weight, vectors, tokens, grad_residual, grad_qkv):
    rows, width = tokens.shape
    size = TILE
    tile = pl.BlockSpec((size, width), lambda s: (s, 0))
    whole = lambda ref: pl.BlockSpec(ref.shape, lambda s: (0, 0))
    return pl.pallas_call(
        input_grad_kernel,
        grid=(rows // size,),
        in_specs=[
            whole(weight), whole(vectors), tile, tile,
            pl.BlockSpec((size, 3 * width), lambda s: (s, 0)),
        ],
        out_specs=tile,
        out_shape=jax.ShapeDtypeStruct((rows, width), LOW),
        compiler_params=pltpu.CompilerParams(vmem_limit_bytes=VMEM_LIMIT),
        cost_estimate=pl.CostEstimate(
            flops=4_000_000_000, bytes_accessed=13_000_000, transcendentals=2048
        ),
        name="input_gradient",
    )(weight, vectors, tokens, grad_residual, grad_qkv)


def halves(value):
    high = value.astype(LOW)
    return high, (value - high.astype(F32)).astype(LOW)


def dot_three(left, right):
    tall = jnp.concatenate([right[0], right[0], right[1]], axis=0)
    return dot(jnp.concatenate([left[0], left[1], left[0]], axis=1), tall)


def newton_rows(blocks, offset, rows, store):
    gram = dot(blocks[0], blocks[0], NT)
    for part in blocks[1:]:
        gram = gram + dot(part, part, NT)
    depth = gram.shape[0]
    down = lax.broadcasted_iota(jnp.int32, (depth, depth), 0)
    eye = (down == lane_numbers((depth, depth))).astype(F32)
    norm = 1.0 / (jnp.sqrt(jnp.sum(gram * eye, keepdims=True)) + 1e-07)
    gram = gram * (norm * norm)
    place = lax.broadcasted_iota(jnp.int32, (rows, depth), 0) + offset
    left = jnp.where(place == lane_numbers((rows, depth)), norm, 0.0)
    store[0:depth, :] = gram
    store[depth:, :] = left

    @pl.loop(0, NS_STEPS - 1)
    def advance(_):
        both = halves(store[...])
        pair = [part[:depth] for part in both]
        down = lax.broadcasted_iota(jnp.int32, (depth, depth), 0)
        eye = (down == lane_numbers((depth, depth))).astype(F32)
        square = dot_three(pair, pair)
        poly = halves(NEWTON_A * eye + NEWTON_B * store[0:depth, :] + NEWTON_C * square)
        made = dot_three(both, poly)
        store[depth:, :] = made[depth:]
        store[0:depth, :] = dot_three(halves(made[:depth]), poly)

    left = store[depth:, :]
    pair = halves(store[0:depth, :])
    once = dot_three(halves(left), pair)
    return NEWTON_A * left + NEWTON_B * once + NEWTON_C * dot_three(halves(once), pair)


def newton_store(depth, rows):
    return pltpu.VMEM((depth + tall_of(rows), depth), F32)


def stepped(left, own, height, old):
    high, rest = halves(left)
    ortho = (dot(high, own) + dot(rest, own))[: old.shape[0], : old.shape[1]]
    return old * (1.0 - MUON_RATE * MUON_DECAY) - (MUON_RATE * 0.2 * math.sqrt(height)) * ortho


def kept_lanes(value, low, high):
    lane = lane_numbers(value.shape)
    return jnp.where((lane >= low) & (lane < high), value.astype(F32), 0.0).astype(LOW)


def tall_of(rows):
    return -(-rows // 16) * 16


def muon_kernel(height, numbers, *refs):
    old, new, copy, store = refs[-4:]
    count = old.shape[1]
    blocks = [kept_lanes(ref[...], 0, count) for ref in refs[:-4]]
    left = newton_rows(blocks, numbers[OFFSET], tall_of(old.shape[0]), store)
    result = stepped(left, blocks[0], height, old[...])
    new[...] = result
    copy[...] = result.astype(LOW)


def muon(height, numbers, blocks, old):
    vmem = pl.BlockSpec(memory_space=pltpu.VMEM)

    def kernel(*refs):
        muon_kernel(height, *refs)

    return pl.pallas_call(
        kernel,
        in_specs=[pl.BlockSpec(memory_space=pltpu.SMEM)] + [vmem] * (len(blocks) + 1),
        out_specs=[vmem, vmem],
        out_shape=[
            jax.ShapeDtypeStruct(old.shape, F32),
            jax.ShapeDtypeStruct(old.shape, LOW),
        ],
        scratch_shapes=[newton_store(blocks[0].shape[0], old.shape[0])],
        compiler_params=pltpu.CompilerParams(vmem_limit_bytes=VMEM_LIMIT),
        cost_estimate=pl.CostEstimate(
            flops=9_000_000_000, bytes_accessed=2_000_000, transcendentals=10
        ),
        name="muon",
    )(numbers, *blocks, old)


def pick_kernel(count, numbers, *refs):
    pieces, columns, outs = refs[:count], refs[count], refs[count + 1 :]
    share = pieces[0].shape[0]
    for k, piece in enumerate(pieces):
        columns[k * share : (k + 1) * share, :] = piece[...]
        for n, out in enumerate(outs):
            at = pl.multiple_of(numbers[STARTS + n] * SUB, SUB)
            out[k * share : (k + 1) * share, :] = piece[:, pl.ds(at, out.shape[1])]


def pick(numbers, pieces, count):
    depth = len(pieces) * pieces[0].shape[0]
    vmem = pl.BlockSpec(memory_space=pltpu.VMEM)

    def kernel(*refs):
        pick_kernel(len(pieces), *refs)

    return pl.pallas_call(
        kernel,
        in_specs=[pl.BlockSpec(memory_space=pltpu.SMEM)] + [vmem] * len(pieces),
        out_specs=[vmem] * (count + 1),
        out_shape=[jax.ShapeDtypeStruct((depth, pieces[0].shape[1]), LOW)]
        + [jax.ShapeDtypeStruct((depth, depth), LOW)] * count,
        name="pick",
    )(numbers, *pieces)


def newton_kernel(at, numbers, *refs):
    left, store = refs[-2:]
    bounds = numbers[LOW_LANE], numbers[HIGH_LANE]
    blocks = [kept_lanes(ref[...], *bounds) for ref in refs[:-2]]
    start = numbers[OFFSET] if at is None else at
    left[...] = newton_rows(blocks, start, left.shape[0], store)


def newton(at, numbers, blocks, rows):
    vmem = pl.BlockSpec(memory_space=pltpu.VMEM)

    def kernel(*refs):
        newton_kernel(at, *refs)

    return pl.pallas_call(
        kernel,
        in_specs=[pl.BlockSpec(memory_space=pltpu.SMEM)] + [vmem] * len(blocks),
        out_specs=vmem,
        out_shape=jax.ShapeDtypeStruct((tall_of(rows), blocks[0].shape[0]), F32),
        scratch_shapes=[newton_store(blocks[0].shape[0], rows)],
        compiler_params=pltpu.CompilerParams(vmem_limit_bytes=VMEM_LIMIT),
        cost_estimate=pl.CostEstimate(
            flops=9_000_000_000, bytes_accessed=2_000_000, transcendentals=10
        ),
        name="newton",
    )(numbers, *blocks)


def finish_kernel(heights, lanes, numbers, columns, *refs):
    count = len(heights)
    store = refs[-1]
    news = refs[-1 - 2 * count : -1]
    olds = refs[-1 - 3 * count : -1 - 2 * count]
    lefts = refs[: -1 - 3 * count]
    for n, left in enumerate(lefts):
        store[n] = left[...]
    for n in range(count):
        wide = -(-olds[n].shape[1] // SUB) * SUB
        own = columns[:, lanes[n] : lanes[n] + wide]
        result = stepped(store[numbers[WHICH + n]], own, heights[n], olds[n][...])
        news[2 * n][...] = result
        news[2 * n + 1][...] = result.astype(LOW)


def finish(heights, lanes, numbers, columns, lefts, olds):
    vmem = pl.BlockSpec(memory_space=pltpu.VMEM)
    count = len(olds)

    def kernel(*refs):
        finish_kernel(heights, lanes, *refs)

    outs = pl.pallas_call(
        kernel,
        in_specs=[pl.BlockSpec(memory_space=pltpu.SMEM)] + [vmem] * (1 + len(lefts) + count),
        out_specs=[vmem] * (2 * count),
        out_shape=[
            jax.ShapeDtypeStruct(old.shape, kind) for old in olds for kind in (F32, LOW)
        ],
        scratch_shapes=[pltpu.VMEM((len(lefts), *lefts[0].shape), F32)],
        compiler_params=pltpu.CompilerParams(vmem_limit_bytes=VMEM_LIMIT),
        cost_estimate=pl.CostEstimate(
            flops=200_000_000, bytes_accessed=2_000_000, transcendentals=0
        ),
        name="finish",
    )(numbers, columns, *lefts, *olds)
    return [(outs[2 * n], outs[2 * n + 1]) for n in range(count)]


def exchange(x, axis, mask):
    size = lax.axis_size(axis)
    return lax.ppermute(x, axis, [(i, i ^ mask) for i in range(size)])


def place_masks(size):
    masks = [0]
    bit = size // 2
    while bit >= 1:
        masks = masks + [m ^ bit for m in masks]
        bit //= 2
    return masks


def from_columns(own):
    size = lax.axis_size("dp")
    sent = jnp.broadcast_to(own[None], (size, *own.shape))
    return lax.all_to_all(sent, "dp", split_axis=0, concat_axis=0, tiled=True)


def over_columns(own):
    return from_columns(own).reshape(-1, own.shape[1])


def device_numbers(dp, ns, share, width, proj_rows):
    masks = place_masks(ns)
    tasks = [(0, 0, width), (width // SUB, 0, width)]
    tasks += [(width // SUB + 1, 2 * SUB, 2 * SUB + proj_rows)] * (ns - 2)
    table = np.zeros((dp * ns, 24), np.int32)
    for device in range(dp * ns):
        column, index = device // ns, device % ns
        row = table[device]
        for n in range(ns):
            row[OWNERS + n] = index ^ masks[n]
            row[PLACES + (index ^ masks[n])] = n
            row[STARTS + n] = tasks[index ^ n][0]
        for n in range(3):
            row[WHICH + n] = index ^ n
        row[OFFSET] = column * share
        row[COLUMN] = column
        row[LOW_LANE], row[HIGH_LANE] = tasks[index][1:]
    return table


def half_rows(own):
    held = [own]
    bit = lax.axis_size("ns") // 2
    while bit > 1:
        held = held + [exchange(block, "ns", bit) for block in held]
        bit //= 2
    return held


def added(keep, got):
    return (keep.astype(F32) + got.astype(F32)).astype(LOW)


def sum_columns(pieces):
    return summed(lax.all_to_all(pieces, "dp", split_axis=0, concat_axis=0, tiled=True))


def summed(pieces):
    return jnp.sum(pieces.astype(F32), axis=0)


def columns_direct(own):
    devices = lax.axis_size("dp")
    if devices > 8 or own.shape[0] % 16:
        return [over_columns(own)], None
    even = [own] + [exchange(own, "dp", mask) for mask in range(2, devices, 2)]
    return [part for piece in even for part in (piece, exchange(piece, "dp", 1))], 0


def widened(arrays, lanes):
    joined = jnp.concatenate(arrays, axis=1)
    return jnp.pad(joined, ((0, 0), (0, lanes - joined.shape[1])))


def per_device(
    tokens,
    cotangent,
    segment,
    valid_rows,
    qkv_weight,
    proj_weight,
    fc1_weight,
    fc2_weight,
    qkv_moment,
    proj_moment,
    fc1_moment,
    fc2_moment,
    vectors,
    vector_moment,
    vector_square,
):
    rows, width = tokens.shape
    ns = lax.axis_size("ns")
    qkv_w, proj_w, fc1_w, fc2_w = (w.T for w in (qkv_weight, proj_weight, fc1_weight, fc2_weight))
    qkv_m, proj_m, fc1_m, fc2_m = (w.T for w in (qkv_moment, proj_moment, fc1_moment, fc2_moment))
    share, count = qkv_w.shape
    vec_rows = vectors.shape[0]
    first_lanes = width
    later_lanes = 2 * width + SUB

    table = device_numbers(lax.axis_size("dp"), ns, share, width, proj_w.shape[1])
    device = lax.axis_index("dp") * ns + lax.axis_index("ns")
    numbers = lax.dynamic_slice(jnp.asarray(table), (device, 0), (1, table.shape[1]))[0]

    row_ids = jnp.where(
        valid_rows > 0, segment, rows + jnp.arange(rows, dtype=jnp.int32)
    ).astype(F32)
    ids = jnp.pad(row_ids, (MARGIN, MARGIN), constant_values=-1.0).reshape(-1, SUB)
    ids = jnp.pad(ids, ((0, -ids.shape[0] % 8), (0, 0)), constant_values=-1.0)

    later_own = widened([fc1_w, fc2_w, proj_w], later_lanes).astype(LOW)
    later_own, numbers = lax.optimization_barrier((later_own, numbers))
    later_pair = jnp.stack([later_own, exchange(later_own, "ns", ns // 2)])
    first_own = widened([qkv_w, vectors.T], first_lanes).astype(LOW)
    prepared = prepare(tokens, cotangent, ids)
    first_pieces = half_rows(over_columns(first_own))
    first_pieces, prepared = lax.optimization_barrier((first_pieces, prepared))
    normed, normed_turned, out_turned, columns, out_sums = prepared
    first_pieces = first_pieces + [exchange(piece, "ns", 1) for piece in first_pieces]
    later_near = from_columns(later_pair)
    if share % 16:
        later_near = jnp.moveaxis(later_near, 0, 1).reshape(1, ns // 2, width, later_lanes)

    query, _, value, key_turned, mixed, probs, weight, vector_full = attend_forward(
        numbers, first_pieces, normed, ids, columns
    )
    later_near, mixed = lax.optimization_barrier((later_near, mixed))
    later_far = exchange(later_near, "ns", 1)
    output, grad_residual, grad_mixed, inner, grads_near, grads_far, sums = mlp_both(
        numbers, later_near, later_far, vector_full, mixed, tokens, cotangent, out_turned, out_sums
    )
    held = added(grads_near, exchange(grads_far, "ns", 1))
    held, grad_mixed = lax.optimization_barrier((held, grad_mixed))
    if share % 16:
        held = jnp.moveaxis(held.reshape(ns // 2, -1, share, later_lanes), 1, 0)
    later_got = lax.all_to_all(held, "dp", split_axis=0, concat_axis=0, tiled=True)

    grad_qkv, grads_near, grads_far = attend_backward(
        numbers, ns, query, key_turned, value, probs, inner, grad_mixed, normed_turned, weight,
        vector_full, sums,
    )
    held = added(grads_near, exchange(grads_far, "ns", 1))
    got = exchange(held[1], "ns", ns // 2)
    input_grad = input_gradient(weight, vector_full, tokens, grad_residual, grad_qkv)
    got, input_grad, later_got = lax.optimization_barrier((got, input_grad, later_got))
    first_held = added(held[0], got).reshape(lax.axis_size("dp"), share, first_lanes)
    first_got = lax.all_to_all(first_held, "dp", split_axis=0, concat_axis=0, tiled=True)
    later_sums = summed(later_got)
    later_owned = later_sums[0] + exchange(later_sums[1].astype(LOW), "ns", ns // 2).astype(F32)
    later_moment = later_owned + 0.5 * widened([fc1_m, fc2_m, proj_m], later_lanes)
    pieces, at = columns_direct(later_moment.astype(LOW))
    columns, *chosen = pick(numbers, pieces, ns)
    first_got, chosen = lax.optimization_barrier((first_got, chosen))
    blocks = [chosen[0]] + [exchange(chosen[mask], "ns", mask) for mask in range(1, ns)]

    first_owned = summed(first_got)
    first_moment = first_owned + 0.5 * widened([qkv_m], first_lanes)
    first_pieces = half_rows(over_columns(first_moment.astype(LOW)))
    moments_new = (
        first_moment[:, :count],
        later_moment[:, 2 * width : 2 * width + proj_w.shape[1]],
        later_moment[:, :width],
        later_moment[:, width : 2 * width],
    )

    vector_grad = first_owned[:, count : count + vec_rows].T
    first_new = BETA_ONE * vector_moment + (1.0 - BETA_ONE) * vector_grad
    second_new = BETA_TWO * vector_square + (1.0 - BETA_TWO) * vector_grad * vector_grad
    first_hat = first_new / (1.0 - BETA_ONE**STEP)
    second_hat = second_new / (1.0 - BETA_TWO**STEP)
    vectors_new = vectors - ADAM_RATE * first_hat / (jnp.sqrt(second_hat) + ADAM_EPS)
    small = (*(m.T for m in moments_new), first_new, second_new, vectors_new)
    blocks, small = lax.optimization_barrier((blocks, small))
    left = newton(at, numbers, blocks, share)
    left, first_pieces = lax.optimization_barrier((left, first_pieces))
    first_pieces = first_pieces + [exchange(piece, "ns", 1) for piece in first_pieces]
    qkv_new = muon(count * ns, numbers, first_pieces, qkv_w)
    lefts = [left] + [exchange(left, "ns", mask) for mask in range(1, ns)]
    lefts, qkv_new = lax.optimization_barrier((lefts, qkv_new))
    fc1_new, fc2_new, proj_new = finish(
        [w.shape[1] * ns for w in (fc1_w, fc2_w, proj_w)],
        (0, width, 2 * width),
        numbers,
        columns,
        lefts,
        (fc1_w, fc2_w, proj_w),
    )

    news = (qkv_new, proj_new, fc1_new, fc2_new)
    return (
        output,
        input_grad,
        *(new[0].T for new in news),
        *small,
        *(new[1].T for new in news),
    )


def solution(mesh):
    rows = P(("dp", "ns"), None)
    flat = P(("dp", "ns"))
    block = P("ns", "dp")
    return jax.shard_map(
        per_device,
        mesh=mesh,
        in_specs=(rows, rows, flat, flat) + (block,) * 11,
        out_specs=(rows, rows) + (block,) * 15,
        check_vma=False,
    )
```

```python
import functools
import math

import jax
import jax.numpy as jnp
import numpy as np
from jax import lax
from jax.experimental import pallas as pl
from jax.experimental.pallas import tpu as pltpu
from jax.sharding import PartitionSpec as P

HEADS = 6
PAIRS = 3
MARGIN = 128
NS_STEPS = 5
STEP = 10
TILE = 512
MLP_TILE = 512
FF_CHUNK = 256
SUB = 128
SPAN = 384
VEC_LANES = 16
GROUP = 2


EPS_NORM = 1e-06
NEWTON_A = 3.4445
NEWTON_B = -4.775
NEWTON_C = 2.0315
MUON_RATE = 0.2
MUON_DECAY = 0.1
ADAM_RATE = 0.4
BETA_ONE = 0.9
BETA_TWO = 0.999
ADAM_EPS = 1e-08
LOW = jnp.bfloat16
F32 = jnp.float32
TN = (((0,), (0,)), ((), ()))
NT = (((1,), (1,)), ((), ()))
NN = (((1,), (0,)), ((), ()))
VMEM_LIMIT = 56 * 1024 * 1024
ERF_P = 0.3275911
ERF_COEFS = (0.254829592, -0.284496736, 1.421413741, -1.453152027, 1.061405429)


def dot(left, right, dims=NN):
    return lax.dot_general(left, right, dims, preferred_element_type=F32)


PLACES, OWNERS, STARTS, WHICH, OFFSET, LOW_LANE, HIGH_LANE, COLUMN = 0, 4, 8, 12, 16, 17, 18, 19


def lane_numbers(shape):
    return lax.broadcasted_iota(jnp.int32, shape, len(shape) - 1)


def norm_parts(value):
    center = value - jnp.mean(value, axis=-1, keepdims=True)
    rate = lax.rsqrt(jnp.mean(center * center, axis=-1, keepdims=True) + EPS_NORM)
    return center * rate, rate


def norm_back(grad, normed, rate, gain):
    scaled = grad * gain
    first = jnp.mean(scaled, axis=-1, keepdims=True)
    second = jnp.mean(scaled * normed, axis=-1, keepdims=True)
    return rate * (scaled - first - normed * second)


def gelu_both(value):
    below = 1.0 + (ERF_P * 0.5**0.5) * jnp.abs(value)
    ratio = pl.reciprocal(below, approx=True)
    ratio = ratio * (2.0 - below * ratio)
    decay = jnp.exp2((value * value) * (-0.5 * math.log2(math.e)))
    poly = 0.5 * ERF_COEFS[4]
    for coef in ERF_COEFS[3::-1]:
        poly = poly * ratio + 0.5 * coef
    tail = poly * ratio * decay
    phi = jnp.where(value >= 0, 1.0 - tail, tail)
    return value * phi, phi + (value * (1.0 / math.sqrt(2.0 * math.pi))) * decay


def gelu_rows(hidden, bias, grad, between):
    active, back = [], []
    rows = hidden.shape[0]
    pieces = rows // 16
    for n in range(pieces):
        if n * len(between) // pieces != (n - 1) * len(between) // pieces:
            between[n * len(between) // pieces]()
        here = slice(n * 16, (n + 1) * 16)
        value, slope = gelu_both(hidden[here] + bias)
        active.append(value.astype(LOW))
        back.append((grad[here] * slope).astype(LOW))
    return jnp.concatenate(active, axis=0), jnp.concatenate(back, axis=0)


def halves_of(lanes):
    half = lanes.shape[0] // 2
    return lanes[:half, :SUB], lanes[half:, SUB:]


def staged(count, first, second, third):
    made = first(0)
    kept = None
    for n in range(count):
        coming = first(n + 1) if n + 1 < count else None
        if kept is not None:
            third(n - 1, kept)
        kept = second(n, made)
        made = coming
    third(count - 1, kept)


def both_heads(pair):
    first = (lane_numbers((1, SUB)) < SUB // 2).astype(F32).astype(pair.dtype)
    second = (lane_numbers((1, SUB)) >= SUB // 2).astype(F32).astype(pair.dtype)
    return jnp.concatenate([pair * first, pair * second], axis=0)


def fetch(pairs, sems):
    copies = [
        pltpu.make_async_copy(source, target, sems.at[n])
        for n, (source, target) in enumerate(pairs)
    ]
    for copy in copies:
        copy.start()
    for copy in copies:
        copy.wait()


def prepare_kernel(tokens, cotangent, ids, normed, normed_turned, out_turned, columns, sums):
    step = pl.program_id(0)
    parts = columns.shape[0] // SUB

    @pl.when(step == 0)
    def clear():
        sums[...] = jnp.zeros(sums.shape, F32)
        for number in range(parts):
            row = jnp.broadcast_to(ids[number : number + 1, :], (SUB, SUB))
            columns[number * SUB : (number + 1) * SUB, :] = row.T

    value, _ = norm_parts(tokens[...].astype(F32))
    normed[...] = value
    normed_turned[...] = value.astype(LOW).T
    out_low = cotangent[...]
    out_turned[...] = out_low.T
    sums[0:1, :] += jnp.sum(out_low.astype(F32), axis=0, keepdims=True)


def prepare(tokens, cotangent, ids):
    rows, width = tokens.shape
    padded = rows + 2 * MARGIN
    tile = pl.BlockSpec((TILE, width), lambda s: (s, 0))
    turned = pl.BlockSpec((width, TILE), lambda s: (0, s))
    whole = lambda *dims: pl.BlockSpec(dims, lambda s: (0,) * len(dims))
    return pl.pallas_call(
        prepare_kernel,
        grid=(rows // TILE,),
        in_specs=[tile, tile, whole(*ids.shape)],
        out_specs=[tile, turned, turned, whole(padded, SUB), whole(8, width)],
        out_shape=[
            jax.ShapeDtypeStruct((rows, width), F32),
            jax.ShapeDtypeStruct((width, rows), LOW),
            jax.ShapeDtypeStruct((width, rows), LOW),
            jax.ShapeDtypeStruct((padded, SUB), F32),
            jax.ShapeDtypeStruct((8, width), F32),
        ],
        compiler_params=pltpu.CompilerParams(vmem_limit_bytes=VMEM_LIMIT),
        cost_estimate=pl.CostEstimate(
            flops=20_000_000, bytes_accessed=12_000_000, transcendentals=2048
        ),
        name="prepare",
    )(tokens, cotangent, ids)


def attend_kernel(numbers, *refs):
    (normed, ids, columns, query, key, value, key_turned, mixed, probs, weight, vectors,
     gathered, pair_weight, value_turned, shifts, sems) = refs[-16:]
    pieces = refs[:-16]
    step = pl.program_id(0)
    chunks = pl.num_programs(0) - 1
    width = normed.shape[1]
    parts = len(pieces)
    block = 3 * width // parts
    rows_each = 12 // parts

    @pl.when(step == 0)
    def assemble():
        fetch([(piece, gathered.at[n]) for n, piece in enumerate(pieces)], sems)
        tiles = [jnp.zeros((width, SUB), F32)] * (3 * width // SUB + 1)
        turned = jnp.zeros((width, SUB), F32)
        for number in range(parts):
            piece = gathered[numbers[PLACES + number]].astype(F32)
            kept = jnp.where(lane_numbers(piece.shape) < block, piece, 0.0)
            wide = jnp.concatenate([kept, jnp.zeros((width, SUB), F32)], axis=1)
            over = block * number % SUB
            wide = pltpu.roll(wide, over, 1) if over else wide
            for n in range(wide.shape[1] // SUB):
                at = block * number // SUB + n
                if at < len(tiles):
                    tiles[at] = tiles[at] + wide[:, n * SUB : (n + 1) * SUB]
            last = piece[:, 2 * SUB :]
            at = block - 2 * SUB
            lane = lane_numbers(last.shape)
            vec = jnp.where((lane >= at) & (lane < at + rows_each), last, 0.0)
            turned = turned + pltpu.roll(vec, (rows_each * number - at) % SUB, 1)
        total = jnp.concatenate(tiles[:-1], axis=1).astype(LOW)
        weight[...] = total
        pair_weight[...] = total[:, width:].T
        vectors[...] = turned.T[:VEC_LANES]
        shifts[...] = turned
        edges = (pl.ds(0, MARGIN), pl.ds(MARGIN + chunks * TILE, MARGIN))
        for edge in edges:
            for ref in (query, key, value):
                ref[edge, :] = jnp.zeros((MARGIN, width), LOW)
            for ref in (key_turned, value_turned):
                ref[:, edge] = jnp.zeros((width, MARGIN), LOW)

    @pl.when(step < chunks)
    def project():
        first_in = (normed[...] * vectors[0:1, :] + vectors[1:2, :]).astype(LOW)
        result = dot(first_in, weight[...])
        turned = dot(pair_weight[...], first_in, NT)
        here = pl.ds(pl.multiple_of(MARGIN + step * TILE, SUB), TILE)
        scale = (width // HEADS) ** (-0.5)
        made = (result[:, :width] + vectors[2:3, :]).astype(LOW) * jnp.asarray(scale, LOW)
        query[here, :] = made
        key[here, :] = result[:, width : 2 * width].astype(LOW)
        value[here, :] = (result[:, 2 * width :] + vectors[3:4, :]).astype(LOW)
        key_turned[:, here] = turned[:width].astype(LOW)
        value_turned[:, here] = (turned[width:] + shifts[:, 3:4]).astype(LOW)

    @pl.when(step > 0)
    def attend():
        def place(number):
            sub, pair = number // PAIRS, number % PAIRS
            tile = (step - 1) * (TILE // SUB) + sub
            start = pl.multiple_of(tile * SUB, SUB)
            return sub, pair, tile, start, pl.ds(start, SPAN), pl.ds(pair * SUB, SUB)

        def of_group(group):
            return range(group * GROUP, (group + 1) * GROUP)

        def score(group):
            made = []
            for number in of_group(group):
                _, _, _, start, near_rows, heads = place(number)
                wanted = both_heads(query[pl.ds(start + MARGIN, SUB), heads])
                made.append(dot(key[near_rows, heads], wanted, NT))
            return made

        def soften(group, made):
            own = []
            for number, scores in zip(of_group(group), made):
                _, _, tile, _, near_rows, _ = place(number)
                same = columns[near_rows, :] == ids[pl.ds(tile + 1, 1), :]
                own += [
                    jnp.where(same, scores[:, head * SUB : (head + 1) * SUB], -1e30)
                    for head in range(2)
                ]
            largest = [jnp.max(part, axis=0, keepdims=True) for part in own]
            expo = [jnp.exp(part - most) for part, most in zip(own, largest)]
            share = [1.0 / jnp.sum(part, axis=0, keepdims=True) for part in expo]
            scaled = [(part * by).astype(LOW) for part, by in zip(expo, share)]
            result = []
            for n, number in enumerate(of_group(group)):
                sub, pair, _, _, _, _ = place(number)
                result.append(jnp.concatenate(scaled[2 * n : 2 * n + 2], axis=1))
                probs[pair, sub] = result[-1]
            return result

        def mix(group, kept):
            for number, prob in zip(of_group(group), kept):
                sub, _, _, _, near_rows, heads = place(number)
                first, second = halves_of(dot(value_turned[heads, near_rows], prob))
                turned = jnp.concatenate([first, second], axis=0).astype(LOW)
                mixed[pl.ds(sub * SUB, SUB), heads] = turned.T

        staged(TILE // SUB * PAIRS // GROUP, score, soften, mix)


def attend_forward(numbers, pieces, normed, ids, columns):
    rows, width = normed.shape
    chunks = rows // TILE
    tiles = TILE // SUB
    parts = len(pieces)
    now = lambda s: jnp.minimum(s, chunks - 1)
    before = lambda s: jnp.maximum(s - 1, 0)
    whole = lambda *dims: pl.BlockSpec(dims, lambda s, *_: (0,) * len(dims))
    padded = rows + 2 * MARGIN
    return pl.pallas_call(
        attend_kernel,
        grid_spec=pltpu.PrefetchScalarGridSpec(
            num_scalar_prefetch=1,
            grid=(chunks + 1,),
            in_specs=[pl.BlockSpec(memory_space=pl.ANY)] * parts
            + [
                pl.BlockSpec((TILE, width), lambda s, *_: (now(s), 0)),
                whole(*ids.shape),
                whole(*columns.shape),
            ],
            out_specs=[
                whole(padded, width),
                whole(padded, width),
                whole(padded, width),
                whole(width, padded),
                pl.BlockSpec((TILE, width), lambda s, *_: (before(s), 0)),
                pl.BlockSpec((PAIRS, tiles, SPAN, 2 * SUB), lambda s, *_: (0, before(s), 0, 0)),
                whole(width, 3 * width),
                whole(VEC_LANES, width),
            ],
            scratch_shapes=[
                pltpu.VMEM((parts, *pieces[0].shape), LOW),
                pltpu.VMEM((2 * width, width), LOW),
                pltpu.VMEM((width, padded), LOW),
                pltpu.VMEM((width, SUB), F32),
                pltpu.SemaphoreType.DMA((parts,)),
            ],
        ),
        out_shape=[
            jax.ShapeDtypeStruct((padded, width), LOW),
            jax.ShapeDtypeStruct((padded, width), LOW),
            jax.ShapeDtypeStruct((padded, width), LOW),
            jax.ShapeDtypeStruct((width, padded), LOW),
            jax.ShapeDtypeStruct((rows, width), LOW),
            jax.ShapeDtypeStruct((PAIRS, rows // SUB, SPAN, 2 * SUB), LOW),
            jax.ShapeDtypeStruct((width, 3 * width), LOW),
            jax.ShapeDtypeStruct((VEC_LANES, width), F32),
        ],
        compiler_params=pltpu.CompilerParams(vmem_limit_bytes=VMEM_LIMIT),
        cost_estimate=pl.CostEstimate(
            flops=12_000_000_000, bytes_accessed=22_000_000, transcendentals=5_000_000
        ),
        name="attend_forward",
    )(numbers, *pieces, normed, ids, columns)


def mlp_kernel(numbers, near, far, *refs):
    (vectors, mixed, tokens, cotangent, out_turned, out_sums, output, grad_residual, grad_mixed, inner, grads_near,
     grads_far, sums, one, two, proj_parts, proj, acc_one, acc_two, acc_proj, bias
    ) = refs
    step = pl.program_id(0)
    width = tokens.shape[1]
    mid = near.shape[1]
    parts = mid + far.shape[1]
    block = width // parts
    last_at = 2 * width
    hidden_width = one.shape[1]

    @pl.when(step == 0)
    def assemble():
        for part in range(parts):
            ref, at = (near, part) if part < mid else (far, part - mid)
            lanes = pl.ds(part * width, width)
            for group in range(near.shape[0]):
                here = pl.ds(group * near.shape[2], near.shape[2])
                one[here, lanes] = ref[group, at, :, :width]
                two[here, lanes] = ref[group, at, :, width:last_at]
                proj_parts[part, here, :] = ref[group, at, :, last_at:]
        total = jnp.zeros((width, width), F32)
        for number in range(parts):
            piece = proj_parts[numbers[PLACES + number]].astype(F32)
            kept = jnp.where(lane_numbers(piece.shape) < block, piece, 0.0)
            wide = jnp.concatenate([kept, jnp.zeros((width, width - SUB), F32)], axis=1)
            total = total + (pltpu.roll(wide, block * number, 1) if number else wide)
        proj[...] = total.astype(LOW)
        for part in range(parts):
            row = vectors[pl.ds(8 + numbers[OWNERS + part], 1), :]
            bias[0:1, part * width : (part + 1) * width] = row
        acc_one[...] = jnp.zeros(acc_one.shape, F32)
        acc_two[...] = jnp.zeros(acc_two.shape, F32)
        acc_proj[...] = jnp.zeros(acc_proj.shape, F32)
        sums[...] = jnp.zeros(sums.shape, F32)
        sums[7:8, :] = out_sums[0:1, :]

    def add_row(row, values):
        sums[pl.ds(row, 1), :] += jnp.sum(values, axis=0, keepdims=True)

    own = mixed[...]
    residual = tokens[...].astype(F32) + dot(own, proj[...], NT) + vectors[4:5, :]
    normed, rate = norm_parts(residual)
    gain = vectors[5:6, :]
    second_in = (normed * gain + vectors[6:7, :]).astype(LOW)
    out_low = cotangent[...]
    grad_out = out_low.astype(F32)
    second_turned = second_in.T
    out_turned = out_turned[...]
    totals = [residual + vectors[7:8, :], jnp.zeros(residual.shape, F32)]

    count = hidden_width // FF_CHUNK
    ones = jnp.ones((16, MLP_TILE), LOW)
    second_and_ones = jnp.concatenate([second_turned, ones], axis=0)
    hiddens, slopes, kept = {}, {}, {}

    def lanes_of(number):
        return pl.ds(number * FF_CHUNK, FF_CHUNK)

    def make_hidden(number):
        hiddens[number] = dot(second_in, one[:, lanes_of(number)])

    def make_slope(number):
        slopes[number] = dot(out_low, two[:, lanes_of(number)])

    def add_one(number):
        acc_one[:, lanes_of(number)] += dot(second_and_ones, kept[number][1])

    def add_two(number):
        acc_two[:, lanes_of(number)] += dot(out_turned, kept[number][0])

    def add_result(number):
        totals[0] = totals[0] + dot(kept[number][0], two[:, lanes_of(number)], NT)

    def add_second(number):
        totals[1] = totals[1] + dot(kept[number][1], one[:, lanes_of(number)], NT)

    make_hidden(0)
    make_slope(0)
    for number in range(count):
        between = []
        if number + 1 < count:
            between += [functools.partial(f, number + 1) for f in (make_hidden, make_slope)]
        if number > 0:
            between += [
                functools.partial(f, number - 1)
                for f in (add_result, add_second, add_one, add_two)
            ]
        kept[number] = gelu_rows(
            hiddens.pop(number), bias[0:1, lanes_of(number)], slopes.pop(number), between
        )
    for f in (add_result, add_second, add_one, add_two):
        f(count - 1)
    result, grad_second = totals
    output[...] = result.astype(LOW)
    add_row(5, grad_second * normed)
    add_row(6, grad_second)
    grad_res = grad_out + norm_back(grad_second, normed, rate, gain)
    grad_residual[...] = grad_res
    branch = grad_res.astype(LOW)
    add_row(4, branch.astype(F32))
    acc_proj[...] += dot(branch.T, own)
    grad_own = dot(branch, proj[...]).astype(LOW)
    grad_mixed[...] = grad_own
    high, rest = halves(grad_own.astype(F32) * own.astype(F32))
    head = lax.broadcasted_iota(jnp.int32, (16, width), 0)
    chosen = (lane_numbers((16, width)) // (width // HEADS) == head).astype(F32).astype(LOW)
    inner[...] = (dot(chosen, high, NT) + dot(chosen, rest, NT))[:8]

    @pl.when(step == pl.num_programs(0) - 1)
    def finish():
        total = acc_proj[...]
        for number in range(parts):
            turned = pltpu.roll(total, (width - block * number) % width, 1) if number else total
            proj_parts[numbers[PLACES + number]] = turned[:, :SUB].astype(LOW)
        for part in range(parts):
            ref, at = (grads_near, part) if part < mid else (grads_far, part - mid)
            lanes = pl.ds(part * width, width)
            for group in range(ref.shape[0]):
                here = pl.ds(group * ref.shape[2], ref.shape[2])
                ref[group, at, :, :width] = acc_one[here, lanes].astype(LOW)
                ref[group, at, :, width:last_at] = acc_two[here, lanes].astype(LOW)
                ref[group, at, :, last_at:] = proj_parts[part, here, :]
            sums[pl.ds(8 + numbers[OWNERS + part], 1), :] = acc_one[width : width + 1, lanes]


def mlp_both(numbers, near, far, vectors, mixed, tokens, cotangent, out_turned, out_sums):
    rows, width = tokens.shape
    parts = near.shape[1] + far.shape[1]
    hidden_width = parts * width
    tile = pl.BlockSpec((MLP_TILE, width), lambda s, *_: (s, 0))
    whole = lambda *dims: pl.BlockSpec(dims, lambda s, *_: (0,) * len(dims))
    return pl.pallas_call(
        mlp_kernel,
        grid_spec=pltpu.PrefetchScalarGridSpec(
            num_scalar_prefetch=1,
            grid=(rows // MLP_TILE,),
            in_specs=[
                whole(*near.shape), whole(*far.shape), whole(*vectors.shape), tile, tile, tile,
                pl.BlockSpec((width, MLP_TILE), lambda s, *_: (0, s)), whole(*out_sums.shape),
            ],
            out_specs=[
                tile,
                tile,
                tile,
                pl.BlockSpec((8, MLP_TILE), lambda s, *_: (0, s)),
                whole(*near.shape),
                whole(*far.shape),
                whole(*vectors.shape),
            ],
            scratch_shapes=[
                pltpu.VMEM((width, hidden_width), LOW),
                pltpu.VMEM((width, hidden_width), LOW),
                pltpu.VMEM((parts, width, SUB), LOW),
                pltpu.VMEM((width, width), LOW),
                pltpu.VMEM((width + 16, hidden_width), F32),
                pltpu.VMEM((width, hidden_width), F32),
                pltpu.VMEM((width, width), F32),
                pltpu.VMEM((8, hidden_width), F32),
            ],
        ),
        out_shape=[
            jax.ShapeDtypeStruct((rows, width), LOW),
            jax.ShapeDtypeStruct((rows, width), F32),
            jax.ShapeDtypeStruct((rows, width), LOW),
            jax.ShapeDtypeStruct((8, rows), F32),
            jax.ShapeDtypeStruct(near.shape, LOW),
            jax.ShapeDtypeStruct(far.shape, LOW),
            jax.ShapeDtypeStruct(vectors.shape, F32),
        ],
        compiler_params=pltpu.CompilerParams(vmem_limit_bytes=VMEM_LIMIT),
        cost_estimate=pl.CostEstimate(
            flops=34_000_000_000, bytes_accessed=20_000_000, transcendentals=6_000_000
        ),
        name="mlp_both",
    )(numbers, near, far, vectors, mixed, tokens, cotangent, out_turned, out_sums)


def attend_back_kernel(
    numbers,
    query,
    key_turned,
    value,
    probs,
    inner,
    grad_mixed,
    normed_turned,
    weight,
    vectors,
    sums,
    grad_qkv,
    near,
    far,
    grad_query,
    acc_key,
    acc_value,
    acc_sums,
    normed_sums,
    blocks,
    rows,
):
    step = pl.program_id(0)
    chunks = pl.num_programs(0) - 1
    pairs = range(PAIRS)
    count = len(pairs)
    scale = (SUB // 2) ** (-0.5)

    @pl.when(step == 0)
    def clear():
        acc_key[...] = jnp.zeros(acc_key.shape, F32)
        acc_value[...] = jnp.zeros(acc_value.shape, F32)
        normed_sums[...] = jnp.zeros(normed_sums.shape, F32)
        acc_sums[...] = jnp.zeros(acc_sums.shape, F32)

    @pl.when(step < chunks)
    def attend():
        def place(number):
            sub, at = number // count, number % count
            start = pl.multiple_of((step * (TILE // SUB) + sub) * SUB, SUB)
            return sub, at, start, pl.ds(start, SPAN), pl.ds(at * SUB, SUB)

        def slope(number):
            sub, _, _, near_rows, heads = place(number)
            grad = both_heads(grad_mixed[pl.ds(sub * SUB, SUB), heads])
            return dot(value[near_rows, heads], grad, NT)

        def soften(number, slopes):
            sub, at, _, _, _ = place(number)
            pair = pairs[at]
            cols = pl.ds(sub * SUB, SUB)
            both = []
            for head in range(2):
                lanes = slice(head * SUB, (head + 1) * SUB)
                less = slopes[:, lanes] - inner[2 * pair + head : 2 * pair + head + 1, cols]
                both.append((probs[at, sub, :, lanes].astype(F32) * less).astype(LOW))
            return jnp.concatenate(both, axis=1)

        def collect(number, scores):
            sub, at, start, near_rows, heads = place(number)
            first, second = halves_of(dot(key_turned[heads, near_rows], scores))
            turned = (jnp.concatenate([first, second], axis=0) * scale).astype(LOW)
            grad_query[pl.ds(start, SUB), heads] = turned.T
            wanted = both_heads(query[pl.ds(start + MARGIN, SUB), heads])
            acc_key[near_rows, heads] += dot(scores, wanted)
            grad = both_heads(grad_mixed[pl.ds(sub * SUB, SUB), heads])
            acc_value[near_rows, heads] += dot(probs[at, sub], grad)

        staged(TILE // SUB * count, slope, soften, collect)

    @pl.when(step > 0)
    def collect():
        here = pl.ds(pl.multiple_of((step - 1) * TILE, SUB), TILE)
        there = pl.ds(pl.multiple_of((step - 1) * TILE + MARGIN, SUB), TILE)
        parts = (
            grad_query[here, :],
            acc_key[there, :].astype(LOW),
            acc_value[there, :].astype(LOW),
        )
        joined = jnp.concatenate(parts, axis=1)
        grad_qkv[...] = joined
        normed_sums[...] += dot(normed_turned[...], joined)
        acc_sums[0:1, :] += jnp.sum(joined.astype(F32), axis=0, keepdims=True)

    @pl.when(step == chunks)
    def finish():
        weight_grad(
            numbers, normed_sums[...], acc_sums[0:1, :], weight, vectors, sums, near, far, blocks, rows
        )


def weight_grad(numbers, total, columns, weight, vectors, sums, near, far, blocks, rows):
    width = weight.shape[0]
    parts, mid = blocks.shape[0], near.shape[0]
    block = 3 * width // parts
    rows_each = 12 // parts
    wide = weight[...].astype(F32)
    grad_gain = jnp.sum(total * wide, axis=1, keepdims=True)
    grad_shift = jnp.sum(wide * columns, axis=1, keepdims=True)
    rows[...] = jnp.zeros(rows.shape, F32)
    rows[0:VEC_LANES, :] = sums[...]
    rows[2:3, :] = columns[:, :width]
    rows[3:4, :] = columns[:, 2 * width :]
    rows[VEC_LANES : 2 * VEC_LANES, :] = vectors[...]
    turned = rows[...].T
    gain = turned[:, VEC_LANES : VEC_LANES + 1]
    shift = turned[:, VEC_LANES + 1 : VEC_LANES + 2]
    lane = lane_numbers(turned.shape)
    turned = jnp.where(lane == 0, grad_gain, jnp.where(lane == 1, grad_shift, turned))
    total = total * gain + shift * columns
    at = block - 2 * SUB
    for number in range(parts):
        first, over = block * number // SUB * SUB, block * number % SUB
        piece = total[:, first : first + width + SUB]
        if over:
            missing = width + SUB - piece.shape[1]
            if missing:
                piece = jnp.concatenate([piece, jnp.zeros((width, missing), F32)], axis=1)
            piece = pltpu.roll(piece, width + SUB - over, 1)
        piece = piece[:, :width]
        vec = pltpu.roll(turned, (at - rows_each * number) % SUB, 1)
        last = jnp.where(lane < at, piece[:, 2 * SUB :], 0.0)
        last = jnp.where((lane >= at) & (lane < at + rows_each), vec, last)
        at_place = numbers[PLACES + number]
        blocks[at_place, :, : 2 * SUB] = piece[:, : 2 * SUB].astype(LOW)
        blocks[at_place, :, 2 * SUB :] = last.astype(LOW)
    near[...] = blocks[:mid]
    far[...] = blocks[mid:]


def attend_backward(
    numbers, parts, query, key_turned, value, probs, inner, grad_mixed, normed_turned, weight,
    vectors, sums,
):
    width, rows = normed_turned.shape
    padded = query.shape[0]
    chunks = rows // TILE
    tiles = TILE // SUB
    now = lambda s: jnp.minimum(s, chunks - 1)
    before = lambda s: jnp.maximum(s - 1, 0)
    whole = lambda *dims: pl.BlockSpec(dims, lambda s, *_: (0,) * len(dims))
    half = (parts // 2, width, width)
    return pl.pallas_call(
        attend_back_kernel,
        grid_spec=pltpu.PrefetchScalarGridSpec(
            num_scalar_prefetch=1,
            grid=(chunks + 1,),
            in_specs=[
                whole(padded, width),
                whole(width, padded),
                whole(padded, width),
                pl.BlockSpec((PAIRS, tiles, SPAN, 2 * SUB), lambda s, *_: (0, now(s), 0, 0)),
                pl.BlockSpec((8, TILE), lambda s, *_: (0, now(s))),
                pl.BlockSpec((TILE, width), lambda s, *_: (now(s), 0)),
                pl.BlockSpec((width, TILE), lambda s, *_: (0, before(s))),
                whole(*weight.shape),
                whole(*vectors.shape),
                whole(*sums.shape),
            ],
            out_specs=[
                pl.BlockSpec((TILE, 3 * width), lambda s, *_: (before(s), 0)),
                whole(*half),
                whole(*half),
            ],
            scratch_shapes=[
                pltpu.VMEM((rows, width), LOW),
                pltpu.VMEM((padded, width), F32),
                pltpu.VMEM((padded, width), F32),
                pltpu.VMEM((8, 3 * width), F32),
                pltpu.VMEM((width, 3 * width), F32),
                pltpu.VMEM((parts, width, width), LOW),
                pltpu.VMEM((SUB, width), F32),
            ],
        ),
        out_shape=[
            jax.ShapeDtypeStruct((rows, 3 * width), LOW),
            jax.ShapeDtypeStruct(half, LOW),
            jax.ShapeDtypeStruct(half, LOW),
        ],
        compiler_params=pltpu.CompilerParams(vmem_limit_bytes=VMEM_LIMIT),
        cost_estimate=pl.CostEstimate(
            flops=16_000_000_000, bytes_accessed=24_000_000, transcendentals=0
        ),
        name="attend_backward",
    )(
        numbers, query, key_turned, value, probs, inner, grad_mixed, normed_turned, weight, vectors,
        sums,
    )


def input_grad_kernel(weight, vectors, tokens, grad_residual, grad_qkv, input_grad):
    normed, rate = norm_parts(tokens[...].astype(F32))
    grad_first = dot(grad_qkv[...], weight[...], NT)
    back = norm_back(grad_first, normed, rate, vectors[0:1, :])
    input_grad[...] = (grad_residual[...] + back).astype(LOW)


def input_gradient(weight, vectors, tokens, grad_residual, grad_qkv):
    rows, width = tokens.shape
    size = TILE
    tile = pl.BlockSpec((size, width), lambda s: (s, 0))
    whole = lambda ref: pl.BlockSpec(ref.shape, lambda s: (0, 0))
    return pl.pallas_call(
        input_grad_kernel,
        grid=(rows // size,),
        in_specs=[
            whole(weight), whole(vectors), tile, tile,
            pl.BlockSpec((size, 3 * width), lambda s: (s, 0)),
        ],
        out_specs=tile,
        out_shape=jax.ShapeDtypeStruct((rows, width), LOW),
        compiler_params=pltpu.CompilerParams(vmem_limit_bytes=VMEM_LIMIT),
        cost_estimate=pl.CostEstimate(
            flops=4_000_000_000, bytes_accessed=13_000_000, transcendentals=2048
        ),
        name="input_gradient",
    )(weight, vectors, tokens, grad_residual, grad_qkv)


def halves(value):
    high = value.astype(LOW)
    return high, (value - high.astype(F32)).astype(LOW)


def dot_three(left, right):
    tall = jnp.concatenate([right[0], right[0], right[1]], axis=0)
    return dot(jnp.concatenate([left[0], left[1], left[0]], axis=1), tall)


def newton_rows(blocks, offset, rows, store):
    gram = dot(blocks[0], blocks[0], NT)
    for part in blocks[1:]:
        gram = gram + dot(part, part, NT)
    depth = gram.shape[0]
    down = lax.broadcasted_iota(jnp.int32, (depth, depth), 0)
    eye = (down == lane_numbers((depth, depth))).astype(F32)
    norm = 1.0 / (jnp.sqrt(jnp.sum(gram * eye, keepdims=True)) + 1e-07)
    gram = gram * (norm * norm)
    place = lax.broadcasted_iota(jnp.int32, (rows, depth), 0) + offset
    left = jnp.where(place == lane_numbers((rows, depth)), norm, 0.0)
    store[0:depth, :] = gram
    store[depth:, :] = left

    @pl.loop(0, NS_STEPS - 1)
    def advance(_):
        both = halves(store[...])
        pair = [part[:depth] for part in both]
        down = lax.broadcasted_iota(jnp.int32, (depth, depth), 0)
        eye = (down == lane_numbers((depth, depth))).astype(F32)
        square = dot_three(pair, pair)
        poly = halves(NEWTON_A * eye + NEWTON_B * store[0:depth, :] + NEWTON_C * square)
        made = dot_three(both, poly)
        store[depth:, :] = made[depth:]
        store[0:depth, :] = dot_three(halves(made[:depth]), poly)

    left = store[depth:, :]
    pair = halves(store[0:depth, :])
    once = dot_three(halves(left), pair)
    return NEWTON_A * left + NEWTON_B * once + NEWTON_C * dot_three(halves(once), pair)


def newton_store(depth, rows):
    return pltpu.VMEM((depth + tall_of(rows), depth), F32)


def stepped(left, own, height, old):
    high, rest = halves(left)
    ortho = (dot(high, own) + dot(rest, own))[: old.shape[0], : old.shape[1]]
    return old * (1.0 - MUON_RATE * MUON_DECAY) - (MUON_RATE * 0.2 * math.sqrt(height)) * ortho


def kept_lanes(value, low, high):
    lane = lane_numbers(value.shape)
    return jnp.where((lane >= low) & (lane < high), value.astype(F32), 0.0).astype(LOW)


def tall_of(rows):
    return -(-rows // 16) * 16


def muon_kernel(height, numbers, *refs):
    old, new, copy, store = refs[-4:]
    count = old.shape[1]
    blocks = [kept_lanes(ref[...], 0, count) for ref in refs[:-4]]
    left = newton_rows(blocks, numbers[OFFSET], tall_of(old.shape[0]), store)
    result = stepped(left, blocks[0], height, old[...])
    new[...] = result
    copy[...] = result.astype(LOW)


def muon(height, numbers, blocks, old):
    vmem = pl.BlockSpec(memory_space=pltpu.VMEM)

    def kernel(*refs):
        muon_kernel(height, *refs)

    return pl.pallas_call(
        kernel,
        in_specs=[pl.BlockSpec(memory_space=pltpu.SMEM)] + [vmem] * (len(blocks) + 1),
        out_specs=[vmem, vmem],
        out_shape=[
            jax.ShapeDtypeStruct(old.shape, F32),
            jax.ShapeDtypeStruct(old.shape, LOW),
        ],
        scratch_shapes=[newton_store(blocks[0].shape[0], old.shape[0])],
        compiler_params=pltpu.CompilerParams(vmem_limit_bytes=VMEM_LIMIT),
        cost_estimate=pl.CostEstimate(
            flops=9_000_000_000, bytes_accessed=2_000_000, transcendentals=10
        ),
        name="muon",
    )(numbers, *blocks, old)


def pick_kernel(count, numbers, *refs):
    pieces, columns, outs = refs[:count], refs[count], refs[count + 1 :]
    share = pieces[0].shape[0]
    for k, piece in enumerate(pieces):
        columns[k * share : (k + 1) * share, :] = piece[...]
        for n, out in enumerate(outs):
            at = pl.multiple_of(numbers[STARTS + n] * SUB, SUB)
            out[k * share : (k + 1) * share, :] = piece[:, pl.ds(at, out.shape[1])]


def pick(numbers, pieces, count):
    depth = len(pieces) * pieces[0].shape[0]
    vmem = pl.BlockSpec(memory_space=pltpu.VMEM)

    def kernel(*refs):
        pick_kernel(len(pieces), *refs)

    return pl.pallas_call(
        kernel,
        in_specs=[pl.BlockSpec(memory_space=pltpu.SMEM)] + [vmem] * len(pieces),
        out_specs=[vmem] * (count + 1),
        out_shape=[jax.ShapeDtypeStruct((depth, pieces[0].shape[1]), LOW)]
        + [jax.ShapeDtypeStruct((depth, depth), LOW)] * count,
        name="pick",
    )(numbers, *pieces)


def newton_kernel(at, numbers, *refs):
    left, store = refs[-2:]
    bounds = numbers[LOW_LANE], numbers[HIGH_LANE]
    blocks = [kept_lanes(ref[...], *bounds) for ref in refs[:-2]]
    start = numbers[OFFSET] if at is None else at
    left[...] = newton_rows(blocks, start, left.shape[0], store)


def newton(at, numbers, blocks, rows):
    vmem = pl.BlockSpec(memory_space=pltpu.VMEM)

    def kernel(*refs):
        newton_kernel(at, *refs)

    return pl.pallas_call(
        kernel,
        in_specs=[pl.BlockSpec(memory_space=pltpu.SMEM)] + [vmem] * len(blocks),
        out_specs=vmem,
        out_shape=jax.ShapeDtypeStruct((tall_of(rows), blocks[0].shape[0]), F32),
        scratch_shapes=[newton_store(blocks[0].shape[0], rows)],
        compiler_params=pltpu.CompilerParams(vmem_limit_bytes=VMEM_LIMIT),
        cost_estimate=pl.CostEstimate(
            flops=9_000_000_000, bytes_accessed=2_000_000, transcendentals=10
        ),
        name="newton",
    )(numbers, *blocks)


def finish_kernel(heights, lanes, numbers, columns, *refs):
    count = len(heights)
    store = refs[-1]
    news = refs[-1 - 2 * count : -1]
    olds = refs[-1 - 3 * count : -1 - 2 * count]
    lefts = refs[: -1 - 3 * count]
    for n, left in enumerate(lefts):
        store[n] = left[...]
    for n in range(count):
        wide = -(-olds[n].shape[1] // SUB) * SUB
        own = columns[:, lanes[n] : lanes[n] + wide]
        result = stepped(store[numbers[WHICH + n]], own, heights[n], olds[n][...])
        news[2 * n][...] = result
        news[2 * n + 1][...] = result.astype(LOW)


def finish(heights, lanes, numbers, columns, lefts, olds):
    vmem = pl.BlockSpec(memory_space=pltpu.VMEM)
    count = len(olds)

    def kernel(*refs):
        finish_kernel(heights, lanes, *refs)

    outs = pl.pallas_call(
        kernel,
        in_specs=[pl.BlockSpec(memory_space=pltpu.SMEM)] + [vmem] * (1 + len(lefts) + count),
        out_specs=[vmem] * (2 * count),
        out_shape=[
            jax.ShapeDtypeStruct(old.shape, kind) for old in olds for kind in (F32, LOW)
        ],
        scratch_shapes=[pltpu.VMEM((len(lefts), *lefts[0].shape), F32)],
        compiler_params=pltpu.CompilerParams(vmem_limit_bytes=VMEM_LIMIT),
        cost_estimate=pl.CostEstimate(
            flops=200_000_000, bytes_accessed=2_000_000, transcendentals=0
        ),
        name="finish",
    )(numbers, columns, *lefts, *olds)
    return [(outs[2 * n], outs[2 * n + 1]) for n in range(count)]


def exchange(x, axis, mask):
    size = lax.axis_size(axis)
    return lax.ppermute(x, axis, [(i, i ^ mask) for i in range(size)])


def place_masks(size):
    masks = [0]
    bit = size // 2
    while bit >= 1:
        masks = masks + [m ^ bit for m in masks]
        bit //= 2
    return masks


def from_columns(own):
    size = lax.axis_size("dp")
    sent = jnp.broadcast_to(own[None], (size, *own.shape))
    return lax.all_to_all(sent, "dp", split_axis=0, concat_axis=0, tiled=True)


def over_columns(own):
    return from_columns(own).reshape(-1, own.shape[1])


def device_numbers(dp, ns, share, width, proj_rows):
    masks = place_masks(ns)
    tasks = [(0, 0, width), (width // SUB, 0, width)]
    tasks += [(width // SUB + 1, 2 * SUB, 2 * SUB + proj_rows)] * (ns - 2)
    table = np.zeros((dp * ns, 24), np.int32)
    for device in range(dp * ns):
        column, index = device // ns, device % ns
        row = table[device]
        for n in range(ns):
            row[OWNERS + n] = index ^ masks[n]
            row[PLACES + (index ^ masks[n])] = n
            row[STARTS + n] = tasks[index ^ n][0]
        for n in range(3):
            row[WHICH + n] = index ^ n
        row[OFFSET] = column * share
        row[COLUMN] = column
        row[LOW_LANE], row[HIGH_LANE] = tasks[index][1:]
    return table


def half_rows(own):
    held = [own]
    bit = lax.axis_size("ns") // 2
    while bit > 1:
        held = held + [exchange(block, "ns", bit) for block in held]
        bit //= 2
    return held


def added(keep, got):
    return (keep.astype(F32) + got.astype(F32)).astype(LOW)


def sum_columns(pieces):
    return summed(lax.all_to_all(pieces, "dp", split_axis=0, concat_axis=0, tiled=True))


def summed(pieces):
    return jnp.sum(pieces.astype(F32), axis=0)


def columns_direct(own, other):
    devices = lax.axis_size("dp")
    if devices > 8 or own.shape[0] % 16:
        return [over_columns(own)], None
    parts = [own, exchange(own, "dp", 1)]
    for mask in range(2, devices, 2):
        piece, _ = lax.optimization_barrier((exchange(own, "dp", mask), other))
        parts += [piece, exchange(piece, "dp", 1)]
    return parts, 0


def widened(arrays, lanes):
    joined = jnp.concatenate(arrays, axis=1)
    return jnp.pad(joined, ((0, 0), (0, lanes - joined.shape[1])))


def per_device(
    tokens,
    cotangent,
    segment,
    valid_rows,
    qkv_weight,
    proj_weight,
    fc1_weight,
    fc2_weight,
    qkv_moment,
    proj_moment,
    fc1_moment,
    fc2_moment,
    vectors,
    vector_moment,
    vector_square,
):
    rows, width = tokens.shape
    ns = lax.axis_size("ns")
    qkv_w, proj_w, fc1_w, fc2_w = (w.T for w in (qkv_weight, proj_weight, fc1_weight, fc2_weight))
    qkv_m, proj_m, fc1_m, fc2_m = (w.T for w in (qkv_moment, proj_moment, fc1_moment, fc2_moment))
    share, count = qkv_w.shape
    vec_rows = vectors.shape[0]
    first_lanes = width
    later_lanes = 2 * width + SUB

    table = device_numbers(lax.axis_size("dp"), ns, share, width, proj_w.shape[1])
    device = lax.axis_index("dp") * ns + lax.axis_index("ns")
    numbers = lax.dynamic_slice(jnp.asarray(table), (device, 0), (1, table.shape[1]))[0]

    row_ids = jnp.where(
        valid_rows > 0, segment, rows + jnp.arange(rows, dtype=jnp.int32)
    ).astype(F32)
    ids = jnp.pad(row_ids, (MARGIN, MARGIN), constant_values=-1.0).reshape(-1, SUB)
    ids = jnp.pad(ids, ((0, -ids.shape[0] % 8), (0, 0)), constant_values=-1.0)

    later_own = widened([fc1_w, fc2_w, proj_w], later_lanes).astype(LOW)
    later_own, numbers = lax.optimization_barrier((later_own, numbers))
    later_pair = jnp.stack([later_own, exchange(later_own, "ns", ns // 2)])
    first_own = widened([qkv_w, vectors.T], first_lanes).astype(LOW)
    prepared = prepare(tokens, cotangent, ids)
    first_pieces = half_rows(over_columns(first_own))
    first_pieces, prepared = lax.optimization_barrier((first_pieces, prepared))
    normed, normed_turned, out_turned, columns, out_sums = prepared
    first_pieces = first_pieces + [exchange(piece, "ns", 1) for piece in first_pieces]
    later_near = from_columns(later_pair)
    if share % 16:
        later_near = jnp.moveaxis(later_near, 0, 1).reshape(1, ns // 2, width, later_lanes)

    query, _, value, key_turned, mixed, probs, weight, vector_full = attend_forward(
        numbers, first_pieces, normed, ids, columns
    )
    later_near, mixed = lax.optimization_barrier((later_near, mixed))
    later_far = exchange(later_near, "ns", 1)
    output, grad_residual, grad_mixed, inner, grads_near, grads_far, sums = mlp_both(
        numbers, later_near, later_far, vector_full, mixed, tokens, cotangent, out_turned, out_sums
    )
    held = added(grads_near, exchange(grads_far, "ns", 1))
    held, grad_mixed = lax.optimization_barrier((held, grad_mixed))
    if share % 16:
        held = jnp.moveaxis(held.reshape(ns // 2, -1, share, later_lanes), 1, 0)
    later_got = lax.all_to_all(held, "dp", split_axis=0, concat_axis=0, tiled=True)

    grad_qkv, grads_near, grads_far = attend_backward(
        numbers, ns, query, key_turned, value, probs, inner, grad_mixed, normed_turned, weight,
        vector_full, sums,
    )
    held = added(grads_near, exchange(grads_far, "ns", 1))
    got = exchange(held[1], "ns", ns // 2)
    input_grad = input_gradient(weight, vector_full, tokens, grad_residual, grad_qkv)
    got, input_grad, later_got = lax.optimization_barrier((got, input_grad, later_got))
    first_held = added(held[0], got).reshape(lax.axis_size("dp"), share, first_lanes)
    first_got = lax.all_to_all(first_held, "dp", split_axis=0, concat_axis=0, tiled=True)
    later_sums = summed(later_got)
    later_owned = later_sums[0] + exchange(later_sums[1].astype(LOW), "ns", ns // 2).astype(F32)
    later_moment = later_owned + 0.5 * widened([fc1_m, fc2_m, proj_m], later_lanes)
    first_owned = summed(first_got)
    first_moment = first_owned + 0.5 * widened([qkv_m], first_lanes)
    first_low = first_moment.astype(LOW)
    pieces, at = columns_direct(later_moment.astype(LOW), first_low)
    first_pieces = half_rows(over_columns(first_low))
    columns, *chosen = pick(numbers, pieces, ns)
    blocks = [chosen[0]] + [exchange(chosen[mask], "ns", mask) for mask in range(1, ns)]
    moments_new = (
        first_moment[:, :count],
        later_moment[:, 2 * width : 2 * width + proj_w.shape[1]],
        later_moment[:, :width],
        later_moment[:, width : 2 * width],
    )

    vector_grad = first_owned[:, count : count + vec_rows].T
    first_new = BETA_ONE * vector_moment + (1.0 - BETA_ONE) * vector_grad
    second_new = BETA_TWO * vector_square + (1.0 - BETA_TWO) * vector_grad * vector_grad
    first_hat = first_new / (1.0 - BETA_ONE**STEP)
    second_hat = second_new / (1.0 - BETA_TWO**STEP)
    vectors_new = vectors - ADAM_RATE * first_hat / (jnp.sqrt(second_hat) + ADAM_EPS)
    small = (*(m.T for m in moments_new), first_new, second_new, vectors_new)
    blocks, small = lax.optimization_barrier((blocks, small))
    left = newton(at, numbers, blocks, share)
    left, first_pieces = lax.optimization_barrier((left, first_pieces))
    first_pieces = first_pieces + [exchange(piece, "ns", 1) for piece in first_pieces]
    qkv_new = muon(count * ns, numbers, first_pieces, qkv_w)
    lefts = [left] + [exchange(left, "ns", mask) for mask in range(1, ns)]
    lefts, qkv_new = lax.optimization_barrier((lefts, qkv_new))
    fc1_new, fc2_new, proj_new = finish(
        [w.shape[1] * ns for w in (fc1_w, fc2_w, proj_w)],
        (0, width, 2 * width),
        numbers,
        columns,
        lefts,
        (fc1_w, fc2_w, proj_w),
    )

    news = (qkv_new, proj_new, fc1_new, fc2_new)
    return (
        output,
        input_grad,
        *(new[0].T for new in news),
        *small,
        *(new[1].T for new in news),
    )


def solution(mesh):
    rows = P(("dp", "ns"), None)
    flat = P(("dp", "ns"))
    block = P("ns", "dp")
    return jax.shard_map(
        per_device,
        mesh=mesh,
        in_specs=(rows, rows, flat, flat) + (block,) * 11,
        out_specs=(rows, rows) + (block,) * 15,
        check_vma=False,
    )
```
